32 devices in a mesh: wide: 16 (over z, y, core), narrow: 2 (over x).
Axes of the slice: x: 2, y: 2, z: 4, core: 2. Of those that a mesh axis runs over, the one named last changes fastest.
Arguments:
- tokens: bfloat16 [64, 336, 768], P(('wide', 'narrow')), may hold values from -6 to 6
- skip: bfloat16 [64, 336, 768], P(('wide', 'narrow')), may hold values from -6 to 6
- flags: int32 [64], P(('wide', 'narrow')), may hold values from 0 to 1
- cotangent: bfloat16 [64, 336, 768], P(('wide', 'narrow')), may hold values from -6 to 6
- norm_gains: bfloat16 [2, 2, 768], P(None, None, 'narrow'), may hold values from 0.5 to 1.5
- norm_biases: bfloat16 [2, 2, 768], P(None, None, 'narrow'), may hold values from -2 to 2
- qkv_weight: bfloat16 [2, 768, 2304], P(None, 'narrow'), may hold values from -0.21875 to 0.21875
- out_weight: bfloat16 [2, 768, 768], P(None, 'narrow'), may hold values from -1.25 to 1.25
- out_bias: bfloat16 [2, 768], P(None, 'narrow'), may hold values from -2 to 2
- up_weight: bfloat16 [2, 768, 3072], P(None, 'narrow'), may hold values from -0.21875 to 0.21875
- up_bias: bfloat16 [2, 3072], P(None, 'narrow'), may hold values from -2 to 2
- down_weight: bfloat16 [2, 3072, 768], P(None, 'narrow'), may hold values from -0.109375 to 0.109375
- down_bias: bfloat16 [2, 768], P(None, 'narrow'), may hold values from -2 to 2
- skip_weight: bfloat16 [1536, 768], P('narrow'), may hold values from -0.15625 to 0.15625
- skip_bias: bfloat16 [768], P('narrow'), may hold values from -2 to 2
Outputs:
- output: bfloat16 [64, 336, 768], P(('wide', 'narrow'))
- tokens_grad: float32 [64, 336, 768], P(('wide', 'narrow'))
- skip_grad: float32 [64, 336, 768], P(('wide', 'narrow'))
- norm_gains_grad: float32 [2, 2, 768], P(None, None, 'narrow')
- norm_biases_grad: float32 [2, 2, 768], P(None, None, 'narrow')
- qkv_weight_grad: float32 [2, 768, 2304], P(None, 'narrow')
- out_weight_grad: float32 [2, 768, 768], P(None, 'narrow')
- out_bias_grad: float32 [2, 768], P(None, 'narrow')
- up_weight_grad: float32 [2, 768, 3072], P(None, 'narrow')
- up_bias_grad: float32 [2, 3072], P(None, 'narrow')
- down_weight_grad: float32 [2, 3072, 768], P(None, 'narrow')
- down_bias_grad: float32 [2, 768], P(None, 'narrow')
- skip_weight_grad: float32 [1536, 768], P('narrow')
- skip_bias_grad: float32 [768], P('narrow')
The draws below stay inside these ranges and needn't reach their ends.
Inputs may be any that keep to these rules, and one draw needn't show every extreme that they name: `flags`: 1 where the item holds 77 caption tokens, 0 where it holds none.
All inputs are finite; a program needn't handle non-finite values.
Results may differ from the reference program's by a relative error of at most 0.02.
Values may be sent and summed in bfloat16 or wider, within the bound.
No kernel may reach another device: no remote copies, remote signals or barrier semaphores. Data moves between devices by JAX's collectives and lax.ppermute only.
A program may use at most 256 MiB of HBM per device.

```python
import math
import jax
import jax.numpy as jnp
from jax import lax

D = 768
HEAD_DIM = 64
FF = 3072
PATCHES = 256
CAPTION = 77
SEQ = 336
LAYERS = 2
ITEMS = 64
N_WIDE = 16


def place_ends(entries, stream_key, smallest, high):
    longest = entries.shape.index(max(entries.shape))
    spots = []
    for shift in (0, 1):
        where = [jax.random.randint(jax.random.fold_in(stream_key, axis), (), 0, length) for axis, length in enumerate(entries.shape)]
        where[longest] = (where[longest] + shift) % entries.shape[longest]
        spots.append(tuple(where))
    return entries.at[spots[0]].set(smallest).at[spots[1]].set(high)


def shard_levels(rng, shape, cuts, least, high):
    level, own = 1.0, jax.random.fold_in(rng, 6)
    for dim, blocks in cuts:
        draws = jnp.exp(jax.random.uniform(jax.random.fold_in(own, dim), (blocks,), jnp.float32, least / len(cuts), high / len(cuts)))
        level = level * jnp.repeat(draws, shape[dim] // blocks).reshape([-1 if axis == dim else 1 for axis in range(len(shape))])
    return level


def normal_values(rng, dims, scale, limit, split=(), kind=jnp.bfloat16):
    loudness = shard_levels(rng, dims, split, -0.22, 0.18) if split else 1.0
    values = jax.random.normal(rng, dims, jnp.float32) * scale * loudness
    return jnp.minimum(jnp.maximum(values, -limit), limit).astype(kind)


def setup_inputs(seed: int = 0) -> dict:
    seeds = jax.random.split(jax.random.key(seed), 16)
    tokens = normal_values(seeds[0], (ITEMS, SEQ, D), 1.0, 6.0, ((0, 32),))
    skip = normal_values(seeds[1], (ITEMS, SEQ, D), 1.0, 6.0, ((0, 32),))
    flags = place_ends(jax.random.randint(seeds[2], (ITEMS,), 0, 2), jax.random.fold_in(seeds[2], 1), 0, 1).astype(jnp.int32)
    cotangent = normal_values(seeds[3], (ITEMS, SEQ, D), 1.0, 6.0, ((0, 32),))
    norm_gains = jnp.clip(1.0 + 0.1 * jax.random.normal(seeds[4], (LAYERS, 2, D), jnp.float32), 0.5, 1.5).astype(jnp.bfloat16)
    norm_biases = normal_values(seeds[5], (LAYERS, 2, D), 0.3, 2.0, ((2, 2),))
    qkv_weight = normal_values(seeds[6], (LAYERS, D, 3 * D), D ** -0.5, 0.21875, ((1, 2),))
    out_weight = normal_values(seeds[7], (LAYERS, D, D), (D // 32) ** -0.5, 1.25, ((1, 2),))
    out_bias = normal_values(seeds[8], (LAYERS, D), 0.3, 2.0, ((1, 2),))
    up_weight = normal_values(seeds[9], (LAYERS, D, FF), D ** -0.5, 0.21875, ((1, 2),))
    up_bias = normal_values(seeds[10], (LAYERS, FF), 0.3, 2.0, ((1, 2),))
    down_weight = normal_values(seeds[11], (LAYERS, FF, D), FF ** -0.5, 0.109375, ((1, 2),))
    down_bias = normal_values(seeds[12], (LAYERS, D), 0.3, 2.0, ((1, 2),))
    skip_weight = normal_values(seeds[13], (2 * D, D), (2 * D) ** -0.5, 0.15625, ((0, 2),))
    skip_bias = normal_values(seeds[14], (D,), 0.3, 2.0, ((0, 2),))
    return dict(tokens=tokens, skip=skip, flags=flags, cotangent=cotangent, norm_gains=norm_gains, norm_biases=norm_biases, qkv_weight=qkv_weight, out_weight=out_weight, out_bias=out_bias, up_weight=up_weight, up_bias=up_bias, down_weight=down_weight, down_bias=down_bias, skip_weight=skip_weight, skip_bias=skip_bias)


@jax.custom_vjp
def low(v):
    return lax.optimization_barrier(v.astype(jnp.bfloat16)).astype(jnp.float32)

@jax.custom_vjp
def low_back(v):
    return v

def low_keep(v):
    return (low(v), None)

def low_pass(kept, grad):
    return (grad,)

def back_keep(v):
    return (v, None)

def back_low(kept, grad):
    return (low(grad),)
low.defvjp(low_keep, low_pass)
low_back.defvjp(back_keep, back_low)
epsilon = 1e-05
masked_score = -1e+30
highest = lax.Precision.HIGHEST

def layer_norm(values, gain, shift):
    centred = values - lax.optimization_barrier(jnp.mean(values, axis=-1, keepdims=True))
    spread = lax.optimization_barrier(jnp.mean(centred * centred, axis=-1, keepdims=True))
    return centred * lax.rsqrt(spread + epsilon) * gain + shift

def project(values, weight):
    return jnp.einsum('nsd,de->nse', values, weight, precision=highest)

def residual_block(inputs, gains, shifts, qkv_weight, out_weight, out_bias, up_weight, up_bias, down_weight, down_bias, valid):
    batch_items, seq_rows, model_width = inputs.shape
    head_count = model_width // HEAD_DIM
    first = low(layer_norm(inputs, gains[0], shifts[0]))
    packed = low(low_back(project(first, qkv_weight)))
    packed = packed.reshape(batch_items, seq_rows, 3, head_count, HEAD_DIM)
    queries = packed[:, :, 0]
    keys = packed[:, :, 1]
    values = packed[:, :, 2]
    raw = low_back(jnp.einsum('nqhd,nkhd->nhqk', queries, keys, precision=highest) * HEAD_DIM ** (-0.5))
    scores = jnp.where(valid[:, None, None, :], raw, masked_score)
    probs = low(jax.nn.softmax(scores, axis=-1))
    mixed = jnp.einsum('nhqk,nkhd->nqhd', probs, values, precision=highest)
    mixed = low(low_back(mixed.reshape(batch_items, seq_rows, model_width)))
    middle = inputs + low_back(project(mixed, out_weight) + out_bias)
    second = low(layer_norm(middle, gains[1], shifts[1]))
    hidden_pre = low_back(project(second, up_weight) + up_bias)
    hidden = low(jax.nn.gelu(hidden_pre, approximate=False))
    return middle + low_back(project(hidden, down_weight) + down_bias)

def forward(weights, tokens, skip, valid):
    gains, shifts, qkv_weight, out_weight, out_bias, up_weight, up_bias, down_weight, down_bias, skip_weight, skip_bias = weights
    middle = residual_block(tokens, gains[0], shifts[0], qkv_weight[0], out_weight[0], out_bias[0], up_weight[0], up_bias[0], down_weight[0], down_bias[0], valid)
    joined = low(jnp.concatenate([middle, skip], axis=-1))
    entry = low_back(project(joined, skip_weight) + skip_bias)
    final = residual_block(entry, gains[1], shifts[1], qkv_weight[1], out_weight[1], out_bias[1], up_weight[1], up_bias[1], down_weight[1], down_bias[1], valid)
    return jnp.where(valid[:, :, None], final, 0.0)

def reference(tokens, skip, flags, cotangent, norm_gains, norm_biases, qkv_weight, out_weight, out_bias, up_weight, up_bias, down_weight, down_bias, skip_weight, skip_bias):
    weights = tuple((weight.astype(jnp.float32) for weight in (norm_gains, norm_biases, qkv_weight, out_weight, out_bias, up_weight, up_bias, down_weight, down_bias, skip_weight, skip_bias)))
    batch_items, seq_rows, model_width = tokens.shape
    lengths = PATCHES + 1 + CAPTION * flags
    valid = jnp.arange(seq_rows, dtype=jnp.int32)[None, :] < lengths[:, None]
    group_size = math.gcd(batch_items, max(1, 4096 // seq_rows))
    group_count = batch_items // group_size

    def grouped(array):
        return array.reshape((group_count, group_size) + array.shape[1:])

    def group_step(totals, pieces):
        group_tokens, group_skip, group_cotangent, group_valid = pieces
        result, pullback = jax.vjp(lambda weight_set, inputs, joined_skip: forward(weight_set, inputs, joined_skip, group_valid), weights, group_tokens.astype(jnp.float32), group_skip.astype(jnp.float32))
        weight_grads, inputs_grad, skip_part = pullback(group_cotangent.astype(jnp.float32))
        totals = jax.tree.map(lambda total, term: total + term, totals, weight_grads)
        return (totals, (result.astype(jnp.bfloat16), inputs_grad, skip_part))
    zeros = jax.tree.map(jnp.zeros_like, weights)
    totals, (results, inputs_grads, skip_parts) = lax.scan(group_step, zeros, (grouped(tokens), grouped(skip), grouped(cotangent), grouped(valid)))
    output = results.reshape(batch_items, seq_rows, model_width)
    tokens_grad = inputs_grads.reshape(batch_items, seq_rows, model_width)
    skip_grad = skip_parts.reshape(batch_items, seq_rows, model_width)
    scaled = tuple((total / N_WIDE for total in totals))
    return (output, tokens_grad, skip_grad, scaled[0], scaled[1], scaled[2], scaled[3], scaled[4], scaled[5], scaled[6], scaled[7], scaled[8], scaled[9], scaled[10])
```

```python
import jax
import jax.numpy as jnp
from jax import lax
from jax.sharding import PartitionSpec as P

HEAD_DIM = 64
PATCHES = 256
CAPTION = 77


epsilon = 1e-05
masked_score = -1e30


def row_dot(left, right):
    return lax.dot_general(
        left, right, (((0,), (0,)), ((), ())), preferred_element_type=jnp.float32
    )


def back_dot(left, weight):
    return lax.dot_general(
        left, weight, (((1,), (1,)), ((), ())), preferred_element_type=jnp.float32
    )


def normalize(values):
    centred = values - jnp.mean(values, axis=-1, keepdims=True)
    factor = lax.rsqrt(jnp.mean(centred * centred, axis=-1, keepdims=True) + epsilon)
    return (centred * factor, factor)


def normalize_back(upstream, normed, factor):
    return factor * (
        upstream
        - jnp.mean(upstream, axis=-1, keepdims=True)
        - normed * jnp.mean(upstream * normed, axis=-1, keepdims=True)
    )


def score_block(queries, keys, valid):
    raw = jnp.einsum(
        "nqhd,nkhd->nhqk", queries, keys, preferred_element_type=jnp.float32
    ) * HEAD_DIM ** (-0.5)
    return jnp.where(valid[:, None, None, :], raw, masked_score)


def block_forward(inputs, params, valid):
    gains, shifts, qkv_weight, out_weight, out_bias, up_weight, up_bias, down_weight, down_bias = (
        params[:9]
    )
    batch_items, seq_rows, model_width = inputs.shape
    head_count = model_width // HEAD_DIM
    flat = inputs.reshape(batch_items * seq_rows, model_width)
    normed_one, factor_one = normalize(flat)
    first = (normed_one * gains[0] + shifts[0]).astype(jnp.bfloat16)
    packed = jnp.dot(first, qkv_weight, preferred_element_type=jnp.float32).astype(jnp.bfloat16)
    packed = packed.reshape(batch_items, seq_rows, 3, head_count, HEAD_DIM)
    queries = packed[:, :, 0]
    keys = packed[:, :, 1]
    values = packed[:, :, 2]
    scores = score_block(queries, keys, valid)
    largest = jnp.max(scores, axis=-1, keepdims=True)
    log_total = largest + jnp.log(jnp.sum(jnp.exp(scores - largest), axis=-1, keepdims=True))
    rounded_probs = jnp.exp(scores - log_total).astype(jnp.bfloat16)
    mixed = jnp.einsum("nhqk,nkhd->nqhd", rounded_probs, values, preferred_element_type=jnp.float32)
    mixed = mixed.reshape(batch_items * seq_rows, model_width).astype(jnp.bfloat16)
    middle = flat + jnp.dot(mixed, out_weight, preferred_element_type=jnp.float32) + out_bias
    normed_two, factor_two = normalize(middle)
    second = (normed_two * gains[1] + shifts[1]).astype(jnp.bfloat16)
    hidden_pre = jnp.dot(second, up_weight, preferred_element_type=jnp.float32) + up_bias
    hidden = jax.nn.gelu(hidden_pre, approximate=False).astype(jnp.bfloat16)
    result = middle + jnp.dot(hidden, down_weight, preferred_element_type=jnp.float32) + down_bias
    kept = (
        normed_one,
        factor_one,
        first,
        queries,
        keys,
        values,
        log_total,
        mixed,
        normed_two,
        factor_two,
        second,
        hidden_pre,
        hidden,
    )
    return (result.reshape(inputs.shape), kept)


def block_backward(upstream, params, kept, valid):
    gains, shifts, qkv_weight, out_weight, out_bias, up_weight, up_bias, down_weight, down_bias = (
        params[:9]
    )
    (
        normed_one,
        factor_one,
        first,
        queries,
        keys,
        values,
        log_total,
        mixed,
        normed_two,
        factor_two,
        second,
        hidden_pre,
        hidden,
    ) = kept
    batch_items, seq_rows, head_count, head_size = queries.shape
    model_width = head_count * head_size
    incoming = upstream.reshape(batch_items * seq_rows, model_width)
    rounded_out = incoming.astype(jnp.bfloat16)
    grad_down_weight = row_dot(hidden, rounded_out)
    grad_down_bias = jnp.sum(rounded_out.astype(jnp.float32), axis=0)
    grad_hidden = back_dot(rounded_out, down_weight)
    unused, gelu_back = jax.vjp(lambda before: jax.nn.gelu(before, approximate=False), hidden_pre)
    grad_pre = gelu_back(grad_hidden)[0].astype(jnp.bfloat16)
    grad_up_weight = row_dot(second, grad_pre)
    grad_up_bias = jnp.sum(grad_pre.astype(jnp.float32), axis=0)
    grad_second = back_dot(grad_pre, up_weight)
    gain_two = jnp.sum(grad_second * normed_two, axis=0)
    shift_two = jnp.sum(grad_second, axis=0)
    grad_middle = incoming + normalize_back(grad_second * gains[1], normed_two, factor_two)
    grad_branch = grad_middle.astype(jnp.bfloat16)
    grad_out_weight = row_dot(mixed, grad_branch)
    grad_out_bias = jnp.sum(grad_branch.astype(jnp.float32), axis=0)
    grad_mixed = back_dot(grad_branch, out_weight).astype(jnp.bfloat16)
    grad_mixed = grad_mixed.reshape(batch_items, seq_rows, head_count, head_size)
    scores = score_block(queries, keys, valid)
    probs = jnp.exp(scores - log_total)
    rounded_probs = probs.astype(jnp.bfloat16)
    grad_values = jnp.einsum(
        "nhqk,nqhd->nkhd", rounded_probs, grad_mixed, preferred_element_type=jnp.float32
    )
    grad_probs = jnp.einsum(
        "nqhd,nkhd->nhqk", grad_mixed, values, preferred_element_type=jnp.float32
    )
    grad_scores = probs * (grad_probs - jnp.sum(grad_probs * probs, axis=-1, keepdims=True))
    grad_scores = grad_scores.astype(jnp.bfloat16)
    grad_queries = jnp.einsum(
        "nhqk,nkhd->nqhd", grad_scores, keys, preferred_element_type=jnp.float32
    ) * HEAD_DIM ** (-0.5)
    grad_keys = jnp.einsum(
        "nhqk,nqhd->nkhd", grad_scores, queries, preferred_element_type=jnp.float32
    ) * HEAD_DIM ** (-0.5)
    grad_packed = jnp.stack([grad_queries, grad_keys, grad_values], axis=2)
    grad_packed = grad_packed.reshape(batch_items * seq_rows, 3 * model_width).astype(jnp.bfloat16)
    grad_qkv_weight = row_dot(first, grad_packed)
    grad_first = back_dot(grad_packed, qkv_weight)
    gain_one = jnp.sum(grad_first * normed_one, axis=0)
    shift_one = jnp.sum(grad_first, axis=0)
    grad_inputs = grad_middle + normalize_back(grad_first * gains[0], normed_one, factor_one)
    grads = (
        jnp.stack([gain_one, gain_two]),
        jnp.stack([shift_one, shift_two]),
        grad_qkv_weight,
        grad_out_weight,
        grad_out_bias,
        grad_up_weight,
        grad_up_bias,
        grad_down_weight,
        grad_down_bias,
    )
    return (grad_inputs.reshape(batch_items, seq_rows, model_width), grads)


def swap(values, axis, mask):
    size = lax.axis_size(axis)
    return lax.ppermute(values, axis, [(source, source ^ mask) for source in range(size)])


def masks(axis, skipped=0):
    size = lax.axis_size(axis)
    return [1 << bit for bit in range(skipped, size.bit_length() - 1)]


def gather_rows(shard):
    rows = shard.shape[0]
    me, place = lax.axis_index("narrow"), lax.axis_index("wide")
    sharing = [mask for mask in masks("wide")[:2]]
    count = 1 << len(sharing)
    quarter = place & (count - 1)
    length = rows // count
    held = lax.dynamic_slice_in_dim(shard, quarter * length, length)[None]
    for mask in masks("narrow"):
        held = jnp.concatenate([held, swap(held, "narrow", mask)])
    pieces = {0: held[1:]}
    for mask in reversed(sharing):
        pieces.update({key ^ mask: swap(piece, "wide", mask) for key, piece in pieces.items()})
    full = jnp.zeros((lax.axis_size("narrow") * rows,) + shard.shape[1:], shard.dtype)
    full = lax.dynamic_update_slice_in_dim(full, shard, me * rows, 0)
    for key, piece in pieces.items():
        for offset in range(1, lax.axis_size("narrow")):
            start = (me ^ offset) * rows + (quarter ^ key) * length
            full = lax.dynamic_update_slice_in_dim(full, piece[offset - 1], start, 0)
    return full


def halve(values, axis, mask):
    bit = (lax.axis_index(axis) & mask) // mask
    sent = lax.dynamic_index_in_dim(values, 1 - bit, 0, keepdims=False)
    kept = lax.dynamic_index_in_dim(values, bit, 0, keepdims=False)
    return kept + swap(sent, axis, mask)


def double(values, axis, mask):
    bit = (lax.axis_index(axis) & mask) // mask
    got = swap(values, axis, mask)
    both = jnp.stack([values, values])
    return lax.dynamic_update_index_in_dim(both, got, 1 - bit, 0)


def reduce_rows(term):
    rows, columns = term.shape
    narrow_size, wide_size = lax.axis_size("narrow"), lax.axis_size("wide")
    order = [("wide", mask) for mask in masks("wide")[:1]]
    order += [("narrow", mask) for mask in reversed(masks("narrow"))]
    order += [("wide", mask) for mask in masks("wide")[1:]]
    length = rows // (narrow_size * wide_size)
    values = term.reshape(narrow_size, 2, wide_size // 2, length, columns)
    values = values.swapaxes(0, 1)
    for axis, mask in order:
        values = values.reshape((2, -1, length, columns))
        values = halve(values, axis, mask)
    for axis, mask in reversed(order):
        if axis == "wide":
            values = double(values, axis, mask).reshape(-1, length, columns)
    return values.reshape(rows // narrow_size, columns)


def sum_all(values):
    for axis in ("wide", "narrow"):
        for mask in masks(axis):
            values = values + swap(values, axis, mask)
    return values


def on_device(
    tokens,
    skip,
    flags,
    cotangent,
    norm_gains,
    norm_biases,
    qkv_weight,
    out_weight,
    out_bias,
    up_weight,
    up_bias,
    down_weight,
    down_bias,
    skip_weight,
    skip_bias,
):
    batch_items, seq_rows, model_width = tokens.shape
    lengths = PATCHES + 1 + CAPTION * flags
    valid = lax.broadcasted_iota(jnp.int32, (batch_items, seq_rows), 1) < lengths[:, None]
    small = (norm_gains, norm_biases, out_bias, up_bias, down_bias, skip_bias)
    packed_small = jnp.concatenate([piece.reshape(-1) for piece in small])
    held = packed_small[None]
    for mask in masks("narrow"):
        held = jnp.concatenate([held, swap(held, "narrow", mask)])
    me = lax.axis_index("narrow")
    every = [lax.dynamic_index_in_dim(held, me ^ place, 0, keepdims=False) for place in range(lax.axis_size("narrow"))]
    whole, start = [], 0
    for piece in small:
        stop = start + piece.size
        whole.append(jnp.concatenate([part[start:stop].reshape(piece.shape) for part in every], axis=-1))
        start = stop
    gains, shifts, out_biases, up_biases, down_biases, skip_shift = whole

    def layer_params(layer):
        return (
            gains[layer],
            shifts[layer],
            gather_rows(qkv_weight[layer]),
            gather_rows(out_weight[layer]),
            out_biases[layer],
            gather_rows(up_weight[layer]),
            up_biases[layer],
            gather_rows(down_weight[layer]),
            down_biases[layer],
        )

    first_params = layer_params(0)
    inputs = tokens.astype(jnp.float32)
    middle, first_kept = block_forward(inputs, first_params, valid)
    join_weight = gather_rows(skip_weight)
    second_params = layer_params(1)
    joined = jnp.concatenate([middle.astype(jnp.bfloat16), skip], axis=-1)
    joined = joined.reshape(batch_items * seq_rows, 2 * model_width)
    entry = jnp.dot(joined, join_weight, preferred_element_type=jnp.float32) + skip_shift
    entry = entry.reshape(batch_items, seq_rows, model_width)
    final, second_kept = block_forward(entry, second_params, valid)
    row_valid = valid[:, :, None]
    output = jnp.where(row_valid, final, 0.0).astype(jnp.bfloat16)
    grad_final = jnp.where(row_valid, cotangent.astype(jnp.float32), 0.0)
    grad_entry, second_terms = block_backward(grad_final, second_params, second_kept, valid)
    rounded_entry = grad_entry.reshape(batch_items * seq_rows, model_width).astype(jnp.bfloat16)
    grad_skip_weight = row_dot(joined, rounded_entry)
    grad_skip_bias = jnp.sum(rounded_entry.astype(jnp.float32), axis=0)
    grad_joined = back_dot(rounded_entry, join_weight).reshape(
        batch_items, seq_rows, 2 * model_width
    )
    grad_middle = grad_joined[:, :, :model_width]
    skip_grad = grad_joined[:, :, model_width:]
    tokens_grad, first_terms = block_backward(grad_middle, first_params, first_kept, valid)
    inverse = 1.0 / lax.axis_size("wide")

    def summed(term):
        return reduce_rows(term.astype(jnp.bfloat16)).astype(jnp.float32) * inverse

    second_sums = [summed(second_terms[place]) for place in (7, 5, 3, 2)]
    join_sum = summed(grad_skip_weight)
    first_sums = [summed(first_terms[place]) for place in (7, 5, 3, 2)]
    large = [jnp.stack([lower, upper]) for lower, upper in zip(first_sums, second_sums)]
    shares = lax.axis_size("narrow")
    minor = [jnp.stack([first_terms[place], second_terms[place]]) for place in (0, 1, 4, 6, 8)]
    minor.append(grad_skip_bias)
    split = [jnp.moveaxis(piece.reshape(piece.shape[:-1] + (shares, -1)), -2, 0) for piece in minor]
    packed_minor = jnp.concatenate([piece.reshape(shares, -1) for piece in split], axis=1)
    owned = lax.dynamic_index_in_dim(sum_all(packed_minor), me, 0, keepdims=False) * inverse
    results, start = [], 0
    for piece in split:
        stop = start + piece.size // shares
        results.append(owned[start:stop].reshape(piece.shape[1:]))
        start = stop
    return (
        output,
        tokens_grad,
        skip_grad,
        results[0],
        results[1],
        large[3],
        large[2],
        results[2],
        large[1],
        results[3],
        large[0],
        results[4],
        join_sum,
        results[5],
    )


def solution(mesh):
    placed = (
        P(("wide", "narrow"), None, None),
        P(("wide", "narrow"), None, None),
        P(("wide", "narrow")),
        P(("wide", "narrow"), None, None),
        P(None, None, "narrow"),
        P(None, None, "narrow"),
        P(None, "narrow", None),
        P(None, "narrow", None),
        P(None, "narrow"),
        P(None, "narrow", None),
        P(None, "narrow"),
        P(None, "narrow", None),
        P(None, "narrow"),
        P("narrow", None),
        P("narrow"),
    )
    return jax.shard_map(
        on_device,
        mesh=mesh,
        in_specs=placed,
        out_specs=(
            P(("wide", "narrow"), None, None),
            P(("wide", "narrow"), None, None),
            P(("wide", "narrow"), None, None),
            P(None, None, "narrow"),
            P(None, None, "narrow"),
            P(None, "narrow", None),
            P(None, "narrow", None),
            P(None, "narrow"),
            P(None, "narrow", None),
            P(None, "narrow"),
            P(None, "narrow", None),
            P(None, "narrow"),
            P("narrow", None),
            P("narrow"),
        ),
        check_vma=False,
    )
```

```python
import jax
import jax.numpy as jnp
from jax import lax
from jax.experimental import pallas as pl
from jax.experimental.pallas import tpu as pltpu
from jax.sharding import PartitionSpec as P

HEAD_DIM = 64
PATCHES = 256
CAPTION = 77
PAIR = 2 * HEAD_DIM


epsilon = 1e-05
masked_score = -1e30
low = jnp.bfloat16
full = jnp.float32
ANY = pl.BlockSpec(memory_space=pl.ANY)
SCALARS = pl.BlockSpec(memory_space=pltpu.SMEM)


def dot(left, right, contract=(1, 0)):
    dims = (((contract[0],), (contract[1],)), ((), ()))
    return lax.dot_general(left, right, dims, preferred_element_type=full)


def normalize(values):
    centred = values - jnp.mean(values, axis=-1, keepdims=True)
    factor = lax.rsqrt(jnp.mean(centred * centred, axis=-1, keepdims=True) + epsilon)
    return centred * factor, factor


def normalize_back(upstream, normed, factor):
    return factor * (
        upstream
        - jnp.mean(upstream, axis=-1, keepdims=True)
        - normed * jnp.mean(upstream * normed, axis=-1, keepdims=True)
    )


def column_sum(values):
    return jnp.sum(values.astype(full), axis=0, keepdims=True)


def whole(shape):
    return pl.BlockSpec(shape, lambda *grid: (0,) * len(shape))


def call(body, grid, ins, outs, name, scratch=(), aliases=None, limit=56):
    return pl.pallas_call(
        body,
        grid=grid,
        in_specs=[spec for _, spec in ins],
        out_specs=[spec for _, _, spec in outs],
        out_shape=[jax.ShapeDtypeStruct(shape, kind) for shape, kind, _ in outs],
        scratch_shapes=list(scratch),
        name=name,
        input_output_aliases=aliases or {},
        cost_estimate=pl.CostEstimate(flops=10**6, bytes_accessed=10**6, transcendentals=0),
        compiler_params=pltpu.CompilerParams(vmem_limit_bytes=limit * 2**20),
    )(*[array for array, _ in ins])


class Weight:
    def __init__(self, array, layer, width, spots):
        self.array, self.layer, self.width, self.spots = array, layer, width, spots
        shard = array if layer is None else array[layer]
        self.rows, self.columns = shard.shape
        self.shares = lax.axis_size("narrow")
        self.blocks = self.columns // width
        self.total = self.rows * self.shares
        self.sharing = masks("wide")[:2]
        while self.rows % (16 << len(self.sharing)):
            self.sharing.pop()
        self.count = 1 << len(self.sharing)
        self.length = self.rows // self.count
        place = lax.axis_index("wide") & (self.count - 1)
        self.piece = lax.dynamic_slice_in_dim(shard, place * self.length, self.length)

    def fetch(self, *earlier):
        held = after(self.piece, *earlier)[None]
        for mask in masks("narrow"):
            held = jnp.concatenate([held, swap(held, "narrow", mask)])
        self.pieces = {0: held[1:]}

    def share(self, which, *earlier):
        if which < len(self.sharing):
            mask = self.sharing[which]
            got = {key ^ mask: swap(after(piece, *earlier), "wide", mask) for key, piece in self.pieces.items()}
            self.pieces.update(got)

    def arrays(self):
        return [self.array] + list(self.pieces.values())

    def scratch(self):
        copies = 1 + len(self.pieces) * (self.shares - 1)
        return [pltpu.VMEM((self.blocks, self.total, self.width), low), pltpu.SemaphoreType.DMA((self.blocks, copies))]

    def copies(self, spots, refs, held, signals, block):
        own, pieces = refs[0], refs[1:]
        columns = pl.ds(block * self.width, self.width)
        me = spots[0]
        own = own if self.layer is None else own.at[self.layer]
        begin = pl.multiple_of(me * self.rows, 16)
        found = [(own.at[:, columns], begin, self.rows)]
        for key, piece in zip(self.pieces, pieces):
            for offset in range(1, self.shares):
                begin = (me ^ offset) * self.rows + ((spots[1] & (self.count - 1)) ^ key) * self.length
                found.append((piece.at[offset - 1, :, columns], pl.multiple_of(begin, 16), self.length))
        return [
            pltpu.make_async_copy(source, held.at[block, pl.ds(begin, length)], signals.at[block, place])
            for place, (source, begin, length) in enumerate(found)
        ]

    def start(self, *refs):
        for block in range(self.blocks):
            for copy in self.copies(*refs, block):
                copy.start()

    def wait(self, *refs, block=0):
        for copy in self.copies(*refs, block):
            copy.wait()


def weighted(body, weights, grid, ins, outs, name, scratch=()):
    spots = weights[0].spots
    operands = [(spots, SCALARS)] + [(array, ANY) for weight in weights for array in weight.arrays()]
    counts = [len(weight.arrays()) for weight in weights]
    extra = [piece for weight in weights for piece in weight.scratch()]

    def wrapped(*refs):
        spots_ref, rest = refs[0], list(refs[1:])
        sources = []
        for count in counts:
            sources.append(rest[:count])
            rest = rest[count:]
        spare = rest[len(rest) - len(extra) :]
        rest = rest[: len(rest) - len(extra)]
        handles = []
        for place, weight in enumerate(weights):
            held, signals = spare[2 * place : 2 * place + 2]
            refs_of = (spots_ref, sources[place], held, signals)
            handles.append((weight, refs_of, held))

        @pl.when(pl.program_id(0) == 0)
        def _():
            for weight, refs_of, _ in handles:
                weight.start(*refs_of)

        def ready(place, block=0):
            weight, refs_of, held = handles[place]
            weight.wait(*refs_of, block=block)

        body(ready, [held for _, _, held in handles], *rest)

    return call(wrapped, grid, operands + ins, outs, name, list(scratch) + extra)


def project_qkv(inputs, gain, shift, weight):
    rows, width = inputs.shape

    def body(ready, held, x_ref, gain_ref, shift_ref, a_ref, out_ref):
        step = pl.program_id(0)

        @pl.when(step == 0)
        def _():
            normed, _ = normalize(x_ref[...].astype(full))
            a_ref[...] = (normed * gain_ref[...] + shift_ref[...]).astype(low)

        ready(0, step)
        scale = jnp.where(step == 0, HEAD_DIM ** (-0.5), 1.0)
        out_ref[0] = (dot(a_ref[...], held[0][step]).astype(low).astype(full) * scale).astype(low)

    return weighted(
        body,
        [weight],
        (3,),
        [
            (inputs, whole((rows, width))),
            (gain, whole((1, width))),
            (shift, whole((1, width))),
        ],
        [
            ((rows, width), low, whole((rows, width))),
            ((3, rows, width), low, pl.BlockSpec((1, rows, width), lambda j: (j, 0, 0))),
        ],
        "project_qkv",
    )


def join_qkv(middle, skip, join_weight, join_shift, gain, shift, weight):
    rows, width = middle.shape

    def body(ready, held, m_ref, s_ref, jb_ref, gain_ref, shift_ref, e_ref, a_ref, out_ref):
        step = pl.program_id(0)

        @pl.when(step == 0)
        def _():
            ready(0)
            entry = dot(m_ref[...], held[0][0, :width]) + dot(s_ref[...], held[0][0, width:]) + jb_ref[...]
            e_ref[...] = entry
            normed, _ = normalize(entry)
            a_ref[...] = (normed * gain_ref[...] + shift_ref[...]).astype(low)

        ready(1, step)
        scale = jnp.where(step == 0, HEAD_DIM ** (-0.5), 1.0)
        out_ref[0] = (dot(a_ref[...], held[1][step]).astype(low).astype(full) * scale).astype(low)

    return weighted(
        body,
        [join_weight, weight],
        (3,),
        [
            (middle, whole((rows, width))),
            (skip, whole((rows, width))),
            (join_shift, whole((1, width))),
            (gain, whole((1, width))),
            (shift, whole((1, width))),
        ],
        [
            ((rows, width), full, whole((rows, width))),
            ((rows, width), low, whole((rows, width))),
            ((3, rows, width), low, pl.BlockSpec((1, rows, width), lambda j: (j, 0, 0))),
        ],
        "join_qkv",
    )


def head_masks(seq_rows):
    lane = lax.broadcasted_iota(jnp.int32, (seq_rows, PAIR), 1)
    return [lane < HEAD_DIM, lane >= HEAD_DIM]


def attend(packed, lengths, items, seq_rows):
    width = packed.shape[-1]
    pairs = width // PAIR

    def body(length_ref, q_ref, k_ref, v_ref, out_ref, total_ref):
        length = length_ref[pl.program_id(0)]
        queries, keys, values = q_ref[0, 0], k_ref[0, 0], v_ref[0, 0]
        counts = lax.broadcasted_iota(jnp.int32, (seq_rows, seq_rows), 0) < length
        mixed = jnp.zeros((PAIR, seq_rows), full)
        for head, lanes in enumerate(head_masks(seq_rows)):
            scores = dot(keys, jnp.where(lanes, queries, 0), (1, 1))
            scores = jnp.where(counts, scores, masked_score)
            largest = jnp.max(scores, axis=0, keepdims=True)
            weights = jnp.exp(scores - largest)
            total = jnp.sum(weights, axis=0, keepdims=True)
            part = dot(jnp.where(lanes, values, 0), weights.astype(low), (0, 0))
            mixed += part * (1.0 / total)
            total_ref[0, 0, head : head + 1] = largest + jnp.log(total)
        out_ref[0] = mixed.T.astype(low)

    def block(which):
        return pl.BlockSpec((1, 1, seq_rows, PAIR), lambda n, h: (which, n, 0, h))

    return call(
        body,
        (items, pairs),
        [
            (lengths, SCALARS),
            (packed, block(0)),
            (packed, block(1)),
            (packed, block(2)),
        ],
        [
            ((items, seq_rows, width), low, pl.BlockSpec((1, seq_rows, PAIR), lambda n, h: (n, 0, h))),
            ((items, pairs, 8, seq_rows), full, pl.BlockSpec((1, 1, 8, seq_rows), lambda n, h: (n, h, 0, 0))),
        ],
        "attend",
    )


def attend_back(packed, grad_mixed, totals, lengths, items, seq_rows):
    width = packed.shape[-1]
    pairs = width // PAIR

    def body(length_ref, q_ref, k_ref, v_ref, g_ref, total_ref, out_ref):
        length = length_ref[pl.program_id(0)]
        queries, keys, values, upstream = q_ref[0, 0], k_ref[0, 0], v_ref[0, 0], g_ref[0]
        counts = lax.broadcasted_iota(jnp.int32, (seq_rows, seq_rows), 0) < length
        grad_queries = jnp.zeros((PAIR, seq_rows), full)
        grad_keys = jnp.zeros((seq_rows, PAIR), full)
        grad_values = jnp.zeros((seq_rows, PAIR), full)
        for head, lanes in enumerate(head_masks(seq_rows)):
            own_queries = jnp.where(lanes, queries, 0)
            own_upstream = jnp.where(lanes, upstream, 0)
            scores = dot(keys, own_queries, (1, 1))
            shifted = jnp.where(counts, scores, masked_score) - total_ref[0, 0, head : head + 1]
            probs = jnp.exp(shifted)
            grad_probs = dot(values, own_upstream, (1, 1))
            centre = jnp.sum(grad_probs * probs, axis=0, keepdims=True)
            grad_scores = (probs * (grad_probs - centre)).astype(low)
            grad_values += dot(probs.astype(low), own_upstream)
            grad_keys += dot(grad_scores, own_queries)
            grad_queries += dot(jnp.where(lanes, keys, 0), grad_scores, (0, 0))
        out_ref[0, 0] = (grad_queries.T * HEAD_DIM ** (-0.5)).astype(low)
        out_ref[1, 0] = grad_keys.astype(low)
        out_ref[2, 0] = grad_values.astype(low)

    def block(which):
        return pl.BlockSpec((1, 1, seq_rows, PAIR), lambda n, h: (which, n, 0, h))

    return call(
        body,
        (items, pairs),
        [
            (lengths, SCALARS),
            (packed, block(0)),
            (packed, block(1)),
            (packed, block(2)),
            (grad_mixed, pl.BlockSpec((1, seq_rows, PAIR), lambda n, h: (n, 0, h))),
            (totals, pl.BlockSpec((1, 1, 8, seq_rows), lambda n, h: (n, h, 0, 0))),
        ],
        [
            ((3, items, seq_rows, width), low, pl.BlockSpec((3, 1, seq_rows, PAIR), lambda n, h: (0, n, 0, h))),
        ],
        "attend_back",
    )[0]


def gelu_parts(before):
    decay = jnp.exp(before * before * -0.5)
    inverse = pl.reciprocal(1.0 + (0.3275911 * 0.5**0.5) * jnp.abs(before), approx=False)
    series = 1.061405429 * 0.5
    for term in (-1.453152027, 1.421413741, -0.284496736, 0.254829592):
        series = series * inverse + term * 0.5
    below = series * inverse * decay
    share = jnp.where(before >= 0, 1.0 - below, below)
    return before * share, share + before * decay * 0.3989422804014327


def feed_forward(inputs, mixed, out_weight, out_bias, gain, shift, up_weight, up_bias, down_weight, down_bias, keep):
    rows, width = inputs.shape
    steps = up_weight.blocks
    hidden = steps * width

    def body(ready, held, x_ref, o_ref, ob_ref, gain_ref, shift_ref, ub_ref, db_ref, keep_ref, m_ref, a_ref, g_ref, s_ref, y_ref, total):
        step = pl.program_id(0)

        @pl.when(step == 0)
        def _():
            ready(0)
            middle = x_ref[...].astype(full) + dot(o_ref[...], held[0][0]) + ob_ref[...]
            m_ref[...] = middle
            normed, _ = normalize(middle)
            a_ref[...] = (normed * gain_ref[...] + shift_ref[...]).astype(low)
            total[...] = middle + db_ref[...]

        ready(1, step)
        before = dot(a_ref[...], held[1][step]) + ub_ref[...]
        value, slope = gelu_parts(before)
        g_ref[...] = value.astype(low)
        s_ref[...] = slope.astype(low)

        @pl.when(step == 0)
        def _():
            ready(2)

        total[...] += dot(g_ref[...], held[2][0, pl.ds(pl.multiple_of(step * width, width), width)])

        @pl.when(step == steps - 1)
        def _():
            y_ref[...] = jnp.where(keep_ref[...] > 0, total[...], 0.0).astype(low)

    return weighted(
        body,
        [out_weight, up_weight, down_weight],
        (steps,),
        [
            (inputs, whole((rows, width))),
            (mixed, whole((rows, width))),
            (out_bias, whole((1, width))),
            (gain, whole((1, width))),
            (shift, whole((1, width))),
            (up_bias, pl.BlockSpec((1, width), lambda j: (0, j))),
            (down_bias, whole((1, width))),
            (keep, whole((rows, 1))),
        ],
        [
            ((rows, width), full, whole((rows, width))),
            ((rows, width), low, whole((rows, width))),
            ((rows, hidden), low, pl.BlockSpec((rows, width), lambda j: (0, j))),
            ((rows, hidden), low, pl.BlockSpec((rows, width), lambda j: (0, j))),
            ((rows, width), low, whole((rows, width))),
        ],
        "feed_forward",
        scratch=[pltpu.VMEM((rows, width), full)],
    )


def feed_forward_back(upstream, slope, down_weight, up_weight, middle, gain, out_weight, keep):
    rows, width = upstream.shape
    steps = up_weight.blocks
    hidden = steps * width

    def body(ready, held, y_ref, keep_ref, s_ref, m_ref, gain_ref, du_ref, dm_ref, db_ref, do_ref, dz_ref, sums_ref, usum_ref, total):
        step = pl.program_id(0)

        @pl.when(step == 0)
        def _():
            rounded = jnp.where(keep_ref[...] > 0, y_ref[...].astype(full), 0.0).astype(low)
            dz_ref[...] = rounded
            sums_ref[0:1] = column_sum(rounded)
            total[...] = jnp.zeros_like(total)
            ready(0)

        down = held[0][0, pl.ds(pl.multiple_of(step * width, width), width)]
        grad = (dot(dz_ref[...], down, (1, 1)) * s_ref[...].astype(full)).astype(low)
        du_ref[...] = grad
        usum_ref[...] = column_sum(grad)
        ready(1, step)
        total[...] += dot(grad, held[1][step], (1, 1))

        @pl.when(step == steps - 1)
        def _():
            grad_second = total[...]
            normed, factor = normalize(m_ref[...])
            sums_ref[1:2] = column_sum(grad_second * normed)
            sums_ref[2:3] = column_sum(grad_second)
            incoming = jnp.where(keep_ref[...] > 0, y_ref[...].astype(full), 0.0)
            grad_middle = incoming + normalize_back(grad_second * gain_ref[...], normed, factor)
            dm_ref[...] = grad_middle
            branch = grad_middle.astype(low)
            db_ref[...] = branch
            sums_ref[3:4] = column_sum(branch)
            ready(2)
            do_ref[...] = dot(branch, held[2][0], (1, 1)).astype(low)

    return weighted(
        body,
        [down_weight, up_weight, out_weight],
        (steps,),
        [
            (upstream, whole((rows, width))),
            (keep, whole((rows, 1))),
            (slope, pl.BlockSpec((rows, width), lambda j: (0, j))),
            (middle, whole((rows, width))),
            (gain, whole((1, width))),
        ],
        [
            ((rows, hidden), low, pl.BlockSpec((rows, width), lambda j: (0, j))),
            ((rows, width), full, whole((rows, width))),
            ((rows, width), low, whole((rows, width))),
            ((rows, width), low, whole((rows, width))),
            ((rows, width), low, whole((rows, width))),
            ((8, width), full, whole((8, width))),
            ((1, hidden), full, pl.BlockSpec((1, width), lambda j: (0, j))),
        ],
        "feed_forward_back",
        scratch=[pltpu.VMEM((rows, width), full)],
    )


def project_back(grad_packed, weight, inputs, gain, grad_middle, join_weight=None):
    rows, width = inputs.shape
    joined = join_weight is not None

    def body(ready, held, g_ref, x_ref, gain_ref, dm_ref, *rest):
        if joined:
            de_ref, dx_ref, skip_ref, sums_ref, total = rest
        else:
            dx_ref, sums_ref, total = rest
        step = pl.program_id(0)

        @pl.when(step == 0)
        def _():
            total[...] = jnp.zeros_like(total)

        ready(0, step)
        total[...] += dot(g_ref[0], held[0][step], (1, 1))

        @pl.when(step == 2)
        def _():
            grad_first = total[...]
            normed, factor = normalize(x_ref[...].astype(full))
            sums_ref[0:1] = column_sum(grad_first * normed)
            sums_ref[1:2] = column_sum(grad_first)
            grad = dm_ref[...] + normalize_back(grad_first * gain_ref[...], normed, factor)
            if joined:
                entry = grad.astype(low)
                de_ref[...] = entry
                sums_ref[2:3] = column_sum(entry)
                ready(1)
                dx_ref[...] = dot(entry, held[1][0, :width], (1, 1))
                skip_ref[...] = dot(entry, held[1][0, width:], (1, 1))
            else:
                dx_ref[...] = grad

    ins = [
        (grad_packed, pl.BlockSpec((1, rows, width), lambda j: (j, 0, 0))),
        (inputs, whole((rows, width))),
        (gain, whole((1, width))),
        (grad_middle, whole((rows, width))),
    ]
    outs = [((rows, width), full, whole((rows, width))), ((8, width), full, whole((8, width)))]
    if joined:
        outs = [((rows, width), low, whole((rows, width))), outs[0], outs[0], outs[1]]
    return weighted(
        body,
        [weight] + ([join_weight] if joined else []),
        (3,),
        ins,
        outs,
        "project_back",
        scratch=[pltpu.VMEM((rows, width), full)],
    )


def picked(body, which, grid, ins, outs, name, aliases=None):
    return pl.pallas_call(
        body,
        grid_spec=pltpu.PrefetchScalarGridSpec(
            num_scalar_prefetch=1,
            grid=grid,
            in_specs=[spec for _, spec in ins],
            out_specs=[spec for _, _, spec in outs],
        ),
        out_shape=[jax.ShapeDtypeStruct(shape, kind) for shape, kind, _ in outs],
        name=name,
        input_output_aliases={place + 1: out for place, out in (aliases or {}).items()},
        cost_estimate=pl.CostEstimate(flops=10**6, bytes_accessed=10**6, transcendentals=0),
        compiler_params=pltpu.CompilerParams(vmem_limit_bytes=48 * 2**20),
    )(which, *[array for array, _ in ins])


def up_term(left, right, core):
    rows, width = left.shape
    shares = lax.axis_size("narrow")
    part = width // shares

    def body(core_ref, l_ref, r_ref, out_ref):
        out_ref[...] = dot(l_ref[...], r_ref[...], (0, 0)).astype(low).reshape(shares, 1, part, width)

    return picked(
        body,
        core,
        (2,),
        [
            (left, pl.BlockSpec((rows, width), lambda g, core: (0, 0))),
            (right, pl.BlockSpec((rows, width), lambda g, core: (0, core[0] * 2 + g))),
        ],
        [((shares, 2, part, width), low, pl.BlockSpec((shares, 1, part, width), lambda g, core: (0, g, 0, 0)))],
        "up_term",
    )[0].reshape(shares, 2 * part, width)


def qkv_out_term(first, packed, mixed, branch, core):
    rows, width = first.shape
    shares = lax.axis_size("narrow")
    part = width // shares

    def body(core_ref, l_ref, r_ref, o_ref, b_ref, out_ref):
        last = core_ref[0] * 2 + pl.program_id(0) == 3

        @pl.when(last)
        def _():
            out_ref[...] = dot(o_ref[...], b_ref[...], (0, 0)).astype(low).reshape(shares, 1, part, width)

        @pl.when(jnp.logical_not(last))
        def _():
            out_ref[...] = dot(l_ref[...], r_ref[0], (0, 0)).astype(low).reshape(shares, 1, part, width)

    flat = pl.BlockSpec((rows, width), lambda g, core: (0, 0))
    return picked(
        body,
        core,
        (2,),
        [
            (first, flat),
            (packed, pl.BlockSpec((1, rows, width), lambda g, core: (jnp.minimum(core[0] * 2 + g, 2), 0, 0))),
            (mixed, flat),
            (branch, flat),
        ],
        [((shares, 2, part, width), low, pl.BlockSpec((shares, 1, part, width), lambda g, core: (0, g, 0, 0)))],
        "qkv_out_term",
    )[0].reshape(shares, 2 * part, width)


def down_term(left, right, core):
    rows, width = right.shape
    shares = lax.axis_size("narrow")
    part = left.shape[1] // (2 * shares)
    direct = part == width
    if not direct:
        left = left.reshape(rows, shares, 2, part)
        left = lax.dynamic_index_in_dim(left, core[0], 2, keepdims=False).reshape(rows, shares * part)
    steps = shares * part // width

    def body(core_ref, l_ref, r_ref, out_ref):
        out_ref[...] = dot(l_ref[...], r_ref[...], (0, 0)).astype(low)

    return picked(
        body,
        core,
        (steps,),
        [
            (left, pl.BlockSpec((rows, width), lambda g, core: (0, g * 2 + core[0] if direct else g))),
            (right, pl.BlockSpec((rows, width), lambda g, core: (0, 0))),
        ],
        [((shares * part, width), low, pl.BlockSpec((width, width), lambda g, core: (g, 0)))],
        "down_term",
    )[0].reshape(shares, part, width)


def join_term(middle, skip, right, core):
    rows, width = right.shape
    shares = lax.axis_size("narrow")
    half = width // 2

    def body(core_ref, m_ref, s_ref, r_ref, out_ref):
        out_ref[:width] = dot(m_ref[...], r_ref[...], (0, 0)).astype(low)
        out_ref[width:] = dot(s_ref[...], r_ref[...], (0, 0)).astype(low)

    flat = pl.BlockSpec((rows, width), lambda g, core: (0, 0))
    return picked(
        body,
        core,
        (1,),
        [(middle, flat), (skip, flat), (right, pl.BlockSpec((rows, half), lambda g, core: (0, core[0])))],
        [((2 * width, half), low, pl.BlockSpec((2 * width, half), lambda g, core: (0, 0)))],
        "join_term",
    )[0].reshape(shares, 2 * width // shares, half)


def add_halve(kept, got, bit):
    _, rows, columns = kept.shape
    steps = 2 if rows % 32 == 0 and rows >= 256 else 1
    block = pl.BlockSpec((2, rows // steps, columns), lambda g, bit: (0, g, 0))
    out = ((rows, columns), low, pl.BlockSpec((rows // steps, columns), lambda g, bit: (g, 0)))

    def body(bit_ref, kept_ref, got_ref, sent_ref, left_ref):
        mine = bit_ref[0]
        for target, place in ((sent_ref, 1 - mine), (left_ref, mine)):
            target[...] = (kept_ref[place].astype(full) + got_ref[place].astype(full)).astype(low)

    return picked(body, bit, (steps,), [(kept, block), (got, block)], [out, out], "add_halve")


def pair_up(own, got, bit):
    rows, columns = own.shape

    def body(bit_ref, own_ref, got_ref, out_ref):
        mine = bit_ref[0]
        out_ref[mine] = own_ref[...]
        out_ref[1 - mine] = got_ref[...]

    flat = pl.BlockSpec((rows, columns), lambda g, bit: (0, 0))
    out = ((2, rows, columns), low, pl.BlockSpec((2, rows, columns), lambda g, bit: (0, 0, 0)))
    return picked(body, bit, (1,), [(own, flat), (got, flat)], [out], "pair_up")[0]


def finish(kind, own, got, core, scale, layer, targets):
    shares = lax.axis_size("narrow")
    columns = own.shape[-1]
    aliases = {place + 2: place for place in range(len(targets))}

    def chosen(core_ref, half, own_ref, got_ref):
        return jnp.where(core_ref[0] == half, own_ref[...], got_ref[...]).astype(full) * scale

    if kind == "join":
        rows = own.shape[0]

        def body(core_ref, own_ref, got_ref, out_ref):
            out_ref[:, :columns] = chosen(core_ref, 0, own_ref, got_ref)
            out_ref[:, columns:] = chosen(core_ref, 1, own_ref, got_ref)

        flat = pl.BlockSpec((rows, columns), lambda g, core: (0, 0))
        out = ((rows, 2 * columns), full, pl.BlockSpec((rows, 2 * columns), lambda g, core: (0, 0)))
        return picked(body, core, (1,), [(own, flat), (got, flat)], [out], "finish_join")
    if kind == "down":
        rows = own.shape[0]

        def body(core_ref, own_ref, got_ref, *rest):
            rest[-1][0] = chosen(core_ref, pl.program_id(0), own_ref, got_ref)

        flat = pl.BlockSpec((rows, columns), lambda g, core: (0, 0))
        ins = [(own, flat), (got, flat)] + [(target, ANY) for target in targets]
        out = ((2, 2 * rows, columns), full, pl.BlockSpec((1, rows, columns), lambda g, core: (layer, g, 0)))
        return picked(body, core, (2,), ins, [out], "finish_down", aliases)
    rows = own.shape[0] // 2
    block = pl.BlockSpec((rows, columns), lambda g, core: (g % 2, 0))
    ins = [(own, block), (got, block)] + [(target, ANY) for target in targets]
    if kind == "up":

        def body(core_ref, own_ref, got_ref, *rest):
            rest[-1][0] = chosen(core_ref, pl.program_id(0) // 2, own_ref, got_ref)

        out = ((2, rows, 4 * columns), full, pl.BlockSpec((1, rows, columns), lambda g, core: (layer, 0, g)))
        return picked(body, core, (4,), ins, [out], "finish_up", aliases)

    def body(core_ref, own_ref, got_ref, *rest):
        qkv_ref, out_ref = rest[-2:]
        values = chosen(core_ref, pl.program_id(0) // 2, own_ref, got_ref)

        @pl.when(pl.program_id(0) < 3)
        def _():
            qkv_ref[0] = values

        @pl.when(pl.program_id(0) == 3)
        def _():
            out_ref[0] = values

    outs = [
        ((2, rows, 3 * columns), full, pl.BlockSpec((1, rows, columns), lambda g, core: (layer, 0, jnp.minimum(g, 2)))),
        ((2, rows, columns), full, pl.BlockSpec((1, rows, columns), lambda g, core: (layer, 0, 0))),
    ]
    return picked(body, core, (4,), ins, outs, "finish_qkv_out", aliases)


def after(value, *earlier):
    return lax.optimization_barrier((value,) + earlier)[0] if earlier else value


def swap(values, axis, mask):
    size = lax.axis_size(axis)
    return lax.ppermute(values, axis, [(source, source ^ mask) for source in range(size)])


def masks(axis):
    return [1 << bit for bit in range(lax.axis_size(axis).bit_length() - 1)]


class Order:
    def __init__(self):
        self.last = ()

    def run(self, function, *arrays, **named):
        held = lax.optimization_barrier(tuple(arrays) + self.last)[: len(arrays)]
        out = function(*held, **named)
        self.last = (jax.tree.leaves(out)[0],)
        return out


class Reduce:
    def __init__(self, order, kind, term, *arrays):
        self.order, self.kind = order, kind
        place = lax.axis_index("wide")
        self.core = (place & 1).astype(jnp.int32).reshape(1)
        self.sent = order.run(term, *arrays, 1 - self.core)
        self.got = swap(self.sent, "wide", 1)
        self.kept = order.run(term, *arrays, self.core)
        self.columns = self.kept.shape[-1]
        stages = [("narrow", mask) for mask in reversed(masks("narrow"))]
        stages += [("wide", mask) for mask in masks("wide")[1:]]
        self.down = list(stages)
        self.up = [stage for stage in reversed(stages) if stage[0] == "wide"]
        self.joining = None

    def bit(self, axis, mask):
        return ((lax.axis_index(axis) & mask) // mask).astype(jnp.int32).reshape(1)

    def step(self):
        if self.down:
            axis, mask = self.down.pop(0)
            shape = (2, -1, self.columns)
            kept, got = self.kept.reshape(shape), self.got.reshape(shape)
            self.sent, self.kept = self.order.run(add_halve, kept, got, self.bit(axis, mask))
            self.got = swap(self.sent, axis, mask)
            return
        if self.joining is None:
            total = self.order.run(lambda one, two: (one.astype(full) + two.astype(full)).astype(low), self.kept, self.got)
        else:
            total = self.order.run(pair_up, self.kept, self.got, self.bit(*self.joining))
            total = total.reshape(-1, self.columns)
        self.kept = total
        if self.up:
            self.joining = self.up.pop(0)
            self.got = swap(total, *self.joining)
        else:
            self.got = swap(total, "wide", 1)

    def steps_left(self):
        return len(self.down) + 1 + len([1 for _ in self.up])

    def finish(self, layer, targets=()):
        scale = 1.0 / lax.axis_size("wide")

        def last(own, got, core, *targets):
            return finish(self.kind, own, got, core, scale, layer, targets)

        return self.order.run(last, self.kept, self.got, self.core, *targets)


def sum_all(values):
    for axis in ("wide", "narrow"):
        for mask in masks(axis):
            values = values + swap(values, axis, mask)
    return values


def on_device(
    tokens,
    skip,
    flags,
    cotangent,
    norm_gains,
    norm_biases,
    qkv_weight,
    out_weight,
    out_bias,
    up_weight,
    up_bias,
    down_weight,
    down_bias,
    skip_weight,
    skip_bias,
):
    items, seq_rows, width = tokens.shape
    rows = items * seq_rows
    lengths = PATCHES + 1 + CAPTION * flags
    valid = lax.broadcasted_iota(jnp.int32, (items, seq_rows), 1) < lengths[:, None]
    keep = valid.reshape(rows, 1).astype(full)
    every = jnp.ones((rows, 1), full)
    me = lax.axis_index("narrow")
    shares = lax.axis_size("narrow")
    spots = jnp.stack([me, lax.axis_index("wide")]).astype(jnp.int32)
    order = Order()

    weights = (qkv_weight, out_weight, up_weight, down_weight)
    qkv0, out0, up0, down0 = [Weight(weight, 0, width, spots) for weight in weights]
    qkv1, out1, up1, down1 = [Weight(weight, 1, width, spots) for weight in weights]
    join = Weight(skip_weight, None, width, spots)

    small = (norm_gains, norm_biases, out_bias, up_bias, down_bias, skip_bias)
    held = jnp.concatenate([piece.reshape(-1) for piece in small])[None]
    for mask in masks("narrow"):
        held = jnp.concatenate([held, swap(held, "narrow", mask)])
    parts = [lax.dynamic_index_in_dim(held, me ^ place, 0, keepdims=False) for place in range(shares)]
    wide_small, begin = [], 0
    for piece in small:
        end = begin + piece.size
        both = [part[begin:end].reshape(piece.shape) for part in parts]
        wide_small.append(jnp.concatenate(both, axis=-1).astype(full))
        begin = end
    gains, shifts, out_biases, up_biases, down_biases, join_shift = wide_small

    def line(values):
        return values.reshape(1, -1)

    tokens_flat, skip_flat, cotangent_flat = [array.reshape(rows, width) for array in (tokens, skip, cotangent)]

    qkv0.fetch()
    out0.fetch()
    up0.fetch()
    down0.fetch()
    qkv0.share(1)
    out0.share(1)
    qkv0.share(0)
    out0.share(0)
    up0.share(1)
    a0, packed0 = order.run(lambda *x: project_qkv(*x, qkv0), tokens_flat, line(gains[0, 0]), line(shifts[0, 0]))
    down0.share(1, a0)
    up0.share(0, a0)
    join.fetch(a0)
    qkv1.fetch(a0)
    packed0 = packed0.reshape(3, items, seq_rows, width)
    mixed0, totals0 = order.run(lambda *x: attend(*x, items, seq_rows), packed0, lengths)
    down0.share(0, mixed0)
    join.share(1, mixed0)
    qkv1.share(1, mixed0)
    out1.fetch(mixed0)
    up1.fetch(mixed0)
    mixed0 = mixed0.reshape(rows, width)
    m0, second0, hidden0, slope0, middle = order.run(
        lambda x, o, ob, g, s, ub, db: feed_forward(x, o, out0, ob, g, s, up0, ub, down0, db, every),
        tokens_flat, mixed0, line(out_biases[0]), line(gains[0, 1]), line(shifts[0, 1]), line(up_biases[0]),
        line(down_biases[0]),
    )
    join.share(0, middle)
    qkv1.share(0, middle)
    out1.share(1, middle)
    up1.share(1, middle)
    down1.fetch(middle)
    entry, a1, packed1 = order.run(
        lambda m, s, jb, g, sh: join_qkv(m, s, join, jb, g, sh, qkv1),
        middle, skip_flat, line(join_shift), line(gains[1, 0]), line(shifts[1, 0]),
    )
    out1.share(0, a1)
    up1.share(0, a1)
    down1.share(1, a1)
    packed1 = packed1.reshape(3, items, seq_rows, width)
    mixed1, totals1 = order.run(lambda *x: attend(*x, items, seq_rows), packed1, lengths)
    mixed1 = mixed1.reshape(rows, width)
    down1.share(0, mixed1)
    m1, second1, hidden1, slope1, output = order.run(
        lambda x, o, ob, g, s, ub, db: feed_forward(x, o, out1, ob, g, s, up1, ub, down1, db, keep),
        entry, mixed1, line(out_biases[1]), line(gains[1, 1]), line(shifts[1, 1]), line(up_biases[1]),
        line(down_biases[1]),
    )

    dz1 = jnp.where(keep > 0, cotangent_flat, 0)
    reduce_down1 = Reduce(order, "down", down_term, hidden1, dz1)
    reduce_down1.step()
    du, dm, db, do, dz, sums1, usum1 = order.run(
        lambda y, s, m, g: feed_forward_back(y, s, down1, up1, m, g, out1, keep),
        cotangent_flat, slope1, m1, line(gains[1, 1]),
    )
    reduce_up1 = Reduce(order, "up", up_term, second1, du)
    reduce_up1.step()
    reduce_down1.step()
    dpacked = order.run(
        lambda *x: attend_back(*x, items, seq_rows), packed1, do.reshape(items, seq_rows, width), totals1, lengths
    )
    flat_packed = dpacked.reshape(3, rows, width)
    reduce_qkv1 = Reduce(order, "qkv", qkv_out_term, a1, flat_packed, mixed1, db)
    reduce_qkv1.step()
    reduce_down1.step()
    reduce_up1.step()
    dentry, dmiddle, skip_grad, sums3 = order.run(
        lambda gp, x, g, dm: project_back(gp, qkv1, x, g, dm, join), flat_packed, entry, line(gains[1, 0]), dm
    )
    reduce_join = Reduce(order, "join", join_term, middle, skip_flat, dentry)
    reduce_down1.step()
    reduce_up1.step()
    reduce_join.step()
    reduce_qkv1.step()

    dz0 = dmiddle.astype(low)
    reduce_down0 = Reduce(order, "down", down_term, hidden0, dz0)
    reduce_down0.step()
    reduce_down1.step()
    reduce_up1.step()
    reduce_qkv1.step()
    reduce_join.step()
    du, dm, db, do, dz, sums0, usum0 = order.run(
        lambda y, s, m, g: feed_forward_back(y, s, down0, up0, m, g, out0, every),
        dmiddle, slope0, m0, line(gains[0, 1]),
    )
    reduce_up0 = Reduce(order, "up", up_term, second0, du)
    reduce_up0.step()
    reduce_down1.step()
    reduce_up1.step()
    reduce_qkv1.step()
    reduce_join.step()
    reduce_down0.step()
    dpacked = order.run(
        lambda *x: attend_back(*x, items, seq_rows), packed0, do.reshape(items, seq_rows, width), totals0, lengths
    )
    flat_packed = dpacked.reshape(3, rows, width)
    reduce_qkv0 = Reduce(order, "qkv", qkv_out_term, a0, flat_packed, mixed0, db)
    reduce_qkv0.step()
    reduce_down1.step()
    reduce_up1.step()
    reduce_qkv1.step()
    reduce_join.step()
    reduce_down0.step()
    reduce_up0.step()
    tokens_grad, sums2 = order.run(
        lambda gp, x, g, dm: project_back(gp, qkv0, x, g, dm), flat_packed, tokens_flat, line(gains[0, 0]), dm
    )

    def norm_terms(place):
        return jnp.stack([jnp.stack([sums2[place], sums0[1 + place]]), jnp.stack([sums3[place], sums1[1 + place]])])

    minor = [
        norm_terms(0),
        norm_terms(1),
        jnp.stack([sums0[3], sums1[3]]),
        jnp.concatenate([usum0, usum1]),
        jnp.stack([sums0[0], sums1[0]]),
        sums3[2],
    ]
    split = [jnp.moveaxis(piece.reshape(piece.shape[:-1] + (shares, -1)), -2, 0) for piece in minor]
    packed_minor = jnp.concatenate([piece.reshape(shares, -1) for piece in split], axis=1)
    owned = lax.dynamic_index_in_dim(sum_all(packed_minor), me, 0, keepdims=False) * (1.0 / lax.axis_size("wide"))

    running = [reduce_down1, reduce_up1, reduce_qkv1, reduce_join, reduce_down0, reduce_up0, reduce_qkv0]
    done = {}
    while running:
        for each in list(running):
            if each.up or each.down or (each.joining is None):
                each.step()
            elif not getattr(each, "closed", False):
                each.step()
                each.closed = True
            else:
                running.remove(each)
                layer = 0 if each in (reduce_down0, reduce_up0, reduce_qkv0) else 1
                done[each.kind] = each.finish(layer, done.get(each.kind, ()))

    minor_sums, begin = [], 0
    for piece in split:
        end = begin + piece.size // shares
        minor_sums.append(owned[begin:end].reshape(piece.shape[1:]))
        begin = end
    return (
        output.reshape(tokens.shape),
        tokens_grad.reshape(tokens.shape),
        skip_grad.reshape(tokens.shape),
        minor_sums[0],
        minor_sums[1],
        done["qkv"][0],
        done["qkv"][1],
        minor_sums[2],
        done["up"][0],
        minor_sums[3],
        done["down"][0],
        minor_sums[4],
        done["join"][0],
        minor_sums[5],
    )


def solution(mesh):
    placed = (
        P(("wide", "narrow"), None, None),
        P(("wide", "narrow"), None, None),
        P(("wide", "narrow")),
        P(("wide", "narrow"), None, None),
        P(None, None, "narrow"),
        P(None, None, "narrow"),
        P(None, "narrow", None),
        P(None, "narrow", None),
        P(None, "narrow"),
        P(None, "narrow", None),
        P(None, "narrow"),
        P(None, "narrow", None),
        P(None, "narrow"),
        P("narrow", None),
        P("narrow"),
    )
    return jax.shard_map(
        on_device,
        mesh=mesh,
        in_specs=placed,
        out_specs=(
            P(("wide", "narrow"), None, None),
            P(("wide", "narrow"), None, None),
            P(("wide", "narrow"), None, None),
            P(None, None, "narrow"),
            P(None, None, "narrow"),
            P(None, "narrow", None),
            P(None, "narrow", None),
            P(None, "narrow"),
            P(None, "narrow", None),
            P(None, "narrow"),
            P(None, "narrow", None),
            P(None, "narrow"),
            P("narrow", None),
            P("narrow"),
        ),
        check_vma=False,
    )
```

```python
import jax
import jax.numpy as jnp
from jax import lax
from jax.experimental import pallas as pl
from jax.experimental.pallas import tpu as pltpu
from jax.sharding import PartitionSpec as P

HEAD_DIM = 64
PATCHES = 256
CAPTION = 77
PAIR = 2 * HEAD_DIM


epsilon = 1e-05
masked_score = -1e30
low = jnp.bfloat16
full = jnp.float32
ANY = pl.BlockSpec(memory_space=pl.ANY)
SCALARS = pl.BlockSpec(memory_space=pltpu.SMEM)


def dot(left, right, contract=(1, 0)):
    dims = (((contract[0],), (contract[1],)), ((), ()))
    return lax.dot_general(left, right, dims, preferred_element_type=full)


def normalize(values):
    centred = values - jnp.mean(values, axis=-1, keepdims=True)
    factor = lax.rsqrt(jnp.mean(centred * centred, axis=-1, keepdims=True) + epsilon)
    return centred * factor, factor


def normalize_back(upstream, normed, factor):
    return factor * (
        upstream
        - jnp.mean(upstream, axis=-1, keepdims=True)
        - normed * jnp.mean(upstream * normed, axis=-1, keepdims=True)
    )


def column_sum(values):
    return jnp.sum(values.astype(full), axis=0, keepdims=True)


def whole(shape):
    return pl.BlockSpec(shape, lambda *grid: (0,) * len(shape))


def cost(micros):
    return pl.CostEstimate(flops=int(micros * 10**9), bytes_accessed=10**5, transcendentals=0)


def call(body, grid, ins, outs, name, micros, scratch=(), limit=56):
    return pl.pallas_call(
        body,
        grid=grid,
        in_specs=[spec for _, spec in ins],
        out_specs=[spec for _, _, spec in outs],
        out_shape=[jax.ShapeDtypeStruct(shape, kind) for shape, kind, _ in outs],
        scratch_shapes=list(scratch),
        name=name,
        cost_estimate=cost(micros),
        compiler_params=pltpu.CompilerParams(vmem_limit_bytes=limit * 2**20),
    )(*[array for array, _ in ins])


class Weight:
    def __init__(self, array, layer, width, spots):
        self.array, self.layer, self.width, self.spots = array, layer, width, spots
        self.rows, self.columns = array.shape[-2:]
        self.shares = lax.axis_size("narrow")
        self.blocks = self.columns // width
        self.total = self.rows * self.shares
        self.sharing = masks("wide")[:2]
        while self.rows % (16 << len(self.sharing)):
            self.sharing.pop()
        self.count = 1 << len(self.sharing)
        self.length = self.rows // self.count

    def fetch(self, *earlier):
        array = after(self.array, *earlier)
        place = (lax.axis_index("wide") & (self.count - 1)) * self.length
        lead = () if self.layer is None else (self.layer,)
        sizes = (1,) * len(lead) + (self.length, self.columns)
        self.sent = lax.dynamic_slice(array, lead + (place, 0), sizes).reshape(1, self.length, self.columns)
        held = self.sent
        for mask in masks("narrow"):
            held = jnp.concatenate([held, swap(held, "narrow", mask)])
        self.pieces = {0: held[1:]}

    def share(self, which, *earlier):
        if which < len(self.sharing):
            mask = self.sharing[which]
            got = {key ^ mask: swap(after(piece, *earlier), "wide", mask) for key, piece in self.pieces.items()}
            self.pieces.update(got)

    def arrays(self):
        return [self.array] + list(self.pieces.values())

    def scratch(self):
        copies = 1 + len(self.pieces) * (self.shares - 1)
        return [pltpu.VMEM((self.blocks, self.total, self.width), low), pltpu.SemaphoreType.DMA((self.blocks, copies))]

    def copies(self, spots, refs, held, signals, block):
        own, pieces = refs[0], refs[1:]
        columns = pl.ds(block * self.width, self.width)
        me = spots[0]
        own = own if self.layer is None else own.at[self.layer]
        begin = pl.multiple_of(me * self.rows, 16)
        found = [(own.at[:, columns], begin, self.rows)]
        for key, piece in zip(self.pieces, pieces):
            for offset in range(1, self.shares):
                begin = (me ^ offset) * self.rows + ((spots[1] & (self.count - 1)) ^ key) * self.length
                found.append((piece.at[offset - 1, :, columns], pl.multiple_of(begin, 16), self.length))
        return [
            pltpu.make_async_copy(source, held.at[block, pl.ds(begin, length)], signals.at[block, place])
            for place, (source, begin, length) in enumerate(found)
        ]

    def start(self, *refs):
        for block in range(self.blocks):
            for copy in self.copies(*refs, block):
                copy.start()

    def wait(self, *refs, block=0):
        for copy in self.copies(*refs, block):
            copy.wait()


def weighted(body, weights, grid, ins, outs, name, micros, scratch=()):
    spots = weights[0].spots
    operands = [(spots, SCALARS)] + [(array, ANY) for weight in weights for array in weight.arrays()]
    counts = [len(weight.arrays()) for weight in weights]
    extra = [piece for weight in weights for piece in weight.scratch()]

    def wrapped(*refs):
        spots_ref, rest = refs[0], list(refs[1:])
        sources = []
        for count in counts:
            sources.append(rest[:count])
            rest = rest[count:]
        spare = rest[len(rest) - len(extra) :]
        rest = rest[: len(rest) - len(extra)]
        handles = []
        for place, weight in enumerate(weights):
            held, signals = spare[2 * place : 2 * place + 2]
            refs_of = (spots_ref, sources[place], held, signals)
            handles.append((weight, refs_of, held))

        @pl.when(pl.program_id(0) == 0)
        def _():
            for weight, refs_of, _ in handles:
                weight.start(*refs_of)

        def ready(place, block=0):
            weight, refs_of, held = handles[place]
            weight.wait(*refs_of, block=block)

        body(ready, [held for _, _, held in handles], *rest)

    return call(wrapped, grid, operands + ins, outs, name, micros, list(scratch) + extra)


def project_qkv(inputs, gain, shift, weight):
    rows, width = inputs.shape

    def body(ready, held, x_ref, gain_ref, shift_ref, a_ref, out_ref):
        step = pl.program_id(0)

        @pl.when(step == 0)
        def _():
            normed, _ = normalize(x_ref[...].astype(full))
            a_ref[...] = (normed * gain_ref[...] + shift_ref[...]).astype(low)

        ready(0, step)
        scale = jnp.where(step == 0, HEAD_DIM ** (-0.5), 1.0)
        out_ref[0] = (dot(a_ref[...], held[0][step]).astype(low).astype(full) * scale).astype(low)

    return weighted(
        body,
        [weight],
        (3,),
        [
            (inputs, whole((rows, width))),
            (gain, whole((1, width))),
            (shift, whole((1, width))),
        ],
        [
            ((rows, width), low, whole((rows, width))),
            ((3, rows, width), low, pl.BlockSpec((1, rows, width), lambda j: (j, 0, 0))),
        ],
        "project_qkv",
        7,
    )


def join_qkv(middle, skip, join_weight, join_shift, gain, shift, weight):
    rows, width = middle.shape

    def body(ready, held, m_ref, s_ref, jb_ref, gain_ref, shift_ref, e_ref, a_ref, out_ref):
        step = pl.program_id(0)

        @pl.when(step == 0)
        def _():
            ready(0)
            entry = dot(m_ref[...], held[0][0, :width]) + dot(s_ref[...], held[0][0, width:]) + jb_ref[...]
            e_ref[...] = entry
            normed, _ = normalize(entry)
            a_ref[...] = (normed * gain_ref[...] + shift_ref[...]).astype(low)

        ready(1, step)
        scale = jnp.where(step == 0, HEAD_DIM ** (-0.5), 1.0)
        out_ref[0] = (dot(a_ref[...], held[1][step]).astype(low).astype(full) * scale).astype(low)

    return weighted(
        body,
        [join_weight, weight],
        (3,),
        [
            (middle, whole((rows, width))),
            (skip, whole((rows, width))),
            (join_shift, whole((1, width))),
            (gain, whole((1, width))),
            (shift, whole((1, width))),
        ],
        [
            ((rows, width), full, whole((rows, width))),
            ((rows, width), low, whole((rows, width))),
            ((3, rows, width), low, pl.BlockSpec((1, rows, width), lambda j: (j, 0, 0))),
        ],
        "join_qkv",
        11,
    )


def head_masks(seq_rows):
    lane = lax.broadcasted_iota(jnp.int32, (seq_rows, PAIR), 1)
    return [lane < HEAD_DIM, lane >= HEAD_DIM]


def attend(packed, lengths, items, seq_rows):
    width = packed.shape[-1]
    pairs = width // PAIR

    def body(length_ref, q_ref, k_ref, v_ref, out_ref, total_ref):
        length = length_ref[pl.program_id(0)]
        queries, keys, values = q_ref[0, 0], k_ref[0, 0], v_ref[0, 0]
        counts = lax.broadcasted_iota(jnp.int32, (seq_rows, seq_rows), 0) < length
        mixed = jnp.zeros((PAIR, seq_rows), full)
        for head, lanes in enumerate(head_masks(seq_rows)):
            scores = dot(keys, jnp.where(lanes, queries, 0), (1, 1))
            scores = jnp.where(counts, scores, masked_score)
            largest = jnp.max(scores, axis=0, keepdims=True)
            weights = jnp.exp(scores - largest)
            total = jnp.sum(weights, axis=0, keepdims=True)
            part = dot(jnp.where(lanes, values, 0), weights.astype(low), (0, 0))
            mixed += part * (1.0 / total)
            total_ref[0, 0, head : head + 1] = largest + jnp.log(total)
        out_ref[0] = mixed.T.astype(low)

    def block(which):
        return pl.BlockSpec((1, 1, seq_rows, PAIR), lambda n, h: (which, n, 0, h))

    return call(
        body,
        (items, pairs),
        [
            (lengths, SCALARS),
            (packed, block(0)),
            (packed, block(1)),
            (packed, block(2)),
        ],
        [
            ((items, seq_rows, width), low, pl.BlockSpec((1, seq_rows, PAIR), lambda n, h: (n, 0, h))),
            ((items, pairs, 8, seq_rows), full, pl.BlockSpec((1, 1, 8, seq_rows), lambda n, h: (n, h, 0, 0))),
        ],
        "attend",
        13,
    )


def attend_back(packed, grad_mixed, totals, lengths, items, seq_rows):
    width = packed.shape[-1]
    pairs = width // PAIR

    def body(length_ref, q_ref, k_ref, v_ref, g_ref, total_ref, out_ref):
        length = length_ref[pl.program_id(0)]
        queries, keys, values, upstream = q_ref[0, 0], k_ref[0, 0], v_ref[0, 0], g_ref[0]
        counts = lax.broadcasted_iota(jnp.int32, (seq_rows, seq_rows), 0) < length
        grad_queries = jnp.zeros((PAIR, seq_rows), full)
        grad_keys = jnp.zeros((seq_rows, PAIR), full)
        grad_values = jnp.zeros((seq_rows, PAIR), full)
        for head, lanes in enumerate(head_masks(seq_rows)):
            own_queries = jnp.where(lanes, queries, 0)
            own_upstream = jnp.where(lanes, upstream, 0)
            scores = dot(keys, own_queries, (1, 1))
            shifted = jnp.where(counts, scores, masked_score) - total_ref[0, 0, head : head + 1]
            probs = jnp.exp(shifted)
            grad_probs = dot(values, own_upstream, (1, 1))
            centre = jnp.sum(grad_probs * probs, axis=0, keepdims=True)
            grad_scores = (probs * (grad_probs - centre)).astype(low)
            grad_values += dot(probs.astype(low), own_upstream)
            grad_keys += dot(grad_scores, own_queries)
            grad_queries += dot(jnp.where(lanes, keys, 0), grad_scores, (0, 0))
        out_ref[0, 0] = (grad_queries.T * HEAD_DIM ** (-0.5)).astype(low)
        out_ref[1, 0] = grad_keys.astype(low)
        out_ref[2, 0] = grad_values.astype(low)

    def block(which):
        return pl.BlockSpec((1, 1, seq_rows, PAIR), lambda n, h: (which, n, 0, h))

    return call(
        body,
        (items, pairs),
        [
            (lengths, SCALARS),
            (packed, block(0)),
            (packed, block(1)),
            (packed, block(2)),
            (grad_mixed, pl.BlockSpec((1, seq_rows, PAIR), lambda n, h: (n, 0, h))),
            (totals, pl.BlockSpec((1, 1, 8, seq_rows), lambda n, h: (n, h, 0, 0))),
        ],
        [
            ((3, items, seq_rows, width), low, pl.BlockSpec((3, 1, seq_rows, PAIR), lambda n, h: (0, n, 0, h))),
        ],
        "attend_back",
        17,
    )[0]


def gelu_parts(before):
    decay = jnp.exp(before * before * -0.5)
    inverse = pl.reciprocal(1.0 + (0.3275911 * 0.5**0.5) * jnp.abs(before), approx=False)
    series = 1.061405429 * 0.5
    for term in (-1.453152027, 1.421413741, -0.284496736, 0.254829592):
        series = series * inverse + term * 0.5
    below = series * inverse * decay
    share = jnp.where(before >= 0, 1.0 - below, below)
    return before * share, share + before * decay * 0.3989422804014327


def feed_forward(inputs, mixed, out_weight, out_bias, gain, shift, up_weight, up_bias, down_weight, down_bias, keep=None):
    rows, width = inputs.shape
    steps = up_weight.blocks
    hidden = steps * width

    def body(ready, held, x_ref, o_ref, ob_ref, gain_ref, shift_ref, ub_ref, db_ref, *rest):
        m_ref, a_ref, g_ref, s_ref, y_ref, total = rest[-6:]
        step = pl.program_id(0)

        @pl.when(step == 0)
        def _():
            ready(0)
            middle = x_ref[...].astype(full) + dot(o_ref[...], held[0][0]) + ob_ref[...]
            m_ref[...] = middle
            normed, _ = normalize(middle)
            a_ref[...] = (normed * gain_ref[...] + shift_ref[...]).astype(low)
            total[...] = middle + db_ref[...]

        ready(1, step)
        before = dot(a_ref[...], held[1][step]) + ub_ref[...]
        value, slope = gelu_parts(before)
        g_ref[...] = value.astype(low)
        s_ref[...] = slope.astype(low)

        @pl.when(step == 0)
        def _():
            ready(2)

        total[...] += dot(g_ref[...], held[2][0, pl.ds(pl.multiple_of(step * width, width), width)])

        @pl.when(step == steps - 1)
        def _():
            value = total[...]
            if keep is not None:
                value = jnp.where(rest[0][...] > 0, value, 0.0)
            y_ref[...] = value.astype(low)

    return weighted(
        body,
        [out_weight, up_weight, down_weight],
        (steps,),
        [
            (inputs, whole((rows, width))),
            (mixed, whole((rows, width))),
            (out_bias, whole((1, width))),
            (gain, whole((1, width))),
            (shift, whole((1, width))),
            (up_bias, pl.BlockSpec((1, width), lambda j: (0, j))),
            (down_bias, whole((1, width))),
        ]
        + ([] if keep is None else [(keep, whole((rows, 1)))]),
        [
            ((rows, width), full, whole((rows, width))),
            ((rows, width), low, whole((rows, width))),
            ((rows, hidden), low, pl.BlockSpec((rows, width), lambda j: (0, j))),
            ((rows, hidden), low, pl.BlockSpec((rows, width), lambda j: (0, j))),
            ((rows, width), low, whole((rows, width))),
        ],
        "feed_forward",
        23,
        scratch=[pltpu.VMEM((rows, width), full)],
    )


def feed_forward_back(upstream, rounded, slope, down_weight, up_weight, middle, gain, out_weight):
    rows, width = upstream.shape
    steps = up_weight.blocks
    hidden = steps * width

    def body(ready, held, y_ref, dz_ref, s_ref, m_ref, gain_ref, du_ref, dm_ref, db_ref, do_ref, sums_ref, usum_ref, total):
        step = pl.program_id(0)

        @pl.when(step == 0)
        def _():
            sums_ref[0:1] = column_sum(dz_ref[...])
            total[...] = jnp.zeros_like(total)
            ready(0)

        down = held[0][0, pl.ds(pl.multiple_of(step * width, width), width)]
        grad = (dot(dz_ref[...], down, (1, 1)) * s_ref[...].astype(full)).astype(low)
        du_ref[...] = grad
        usum_ref[...] = column_sum(grad)
        ready(1, step)
        total[...] += dot(grad, held[1][step], (1, 1))

        @pl.when(step == steps - 1)
        def _():
            grad_second = total[...]
            normed, factor = normalize(m_ref[...])
            sums_ref[1:2] = column_sum(grad_second * normed)
            sums_ref[2:3] = column_sum(grad_second)
            grad_middle = y_ref[...].astype(full) + normalize_back(grad_second * gain_ref[...], normed, factor)
            dm_ref[...] = grad_middle
            branch = grad_middle.astype(low)
            db_ref[...] = branch
            sums_ref[3:4] = column_sum(branch)
            ready(2)
            do_ref[...] = dot(branch, held[2][0], (1, 1)).astype(low)

    return weighted(
        body,
        [down_weight, up_weight, out_weight],
        (steps,),
        [
            (upstream, whole((rows, width))),
            (rounded, whole((rows, width))),
            (slope, pl.BlockSpec((rows, width), lambda j: (0, j))),
            (middle, whole((rows, width))),
            (gain, whole((1, width))),
        ],
        [
            ((rows, hidden), low, pl.BlockSpec((rows, width), lambda j: (0, j))),
            ((rows, width), full, whole((rows, width))),
            ((rows, width), low, whole((rows, width))),
            ((rows, width), low, whole((rows, width))),
            ((8, width), full, whole((8, width))),
            ((1, hidden), full, pl.BlockSpec((1, width), lambda j: (0, j))),
        ],
        "feed_forward_back",
        21,
        scratch=[pltpu.VMEM((rows, width), full)],
    )


def project_back(grad_packed, weight, inputs, gain, grad_middle, join_weight=None):
    rows, width = inputs.shape
    joined = join_weight is not None

    def body(ready, held, g_ref, x_ref, gain_ref, dm_ref, *rest):
        if joined:
            de_ref, dx_ref, dz_ref, skip_ref, sums_ref, total = rest
        else:
            dx_ref, sums_ref, total = rest
        step = pl.program_id(0)

        @pl.when(step == 0)
        def _():
            total[...] = jnp.zeros_like(total)

        ready(0, step)
        total[...] += dot(g_ref[0], held[0][step], (1, 1))

        @pl.when(step == 2)
        def _():
            grad_first = total[...]
            normed, factor = normalize(x_ref[...].astype(full))
            sums_ref[0:1] = column_sum(grad_first * normed)
            sums_ref[1:2] = column_sum(grad_first)
            grad = dm_ref[...] + normalize_back(grad_first * gain_ref[...], normed, factor)
            if joined:
                entry = grad.astype(low)
                de_ref[...] = entry
                sums_ref[2:3] = column_sum(entry)
                ready(1)
                grad = dot(entry, held[1][0, :width], (1, 1))
                dx_ref[...] = grad
                dz_ref[...] = grad.astype(low)
                skip_ref[...] = dot(entry, held[1][0, width:], (1, 1))
            else:
                dx_ref[...] = grad

    ins = [
        (grad_packed, pl.BlockSpec((1, rows, width), lambda j: (j, 0, 0))),
        (inputs, whole((rows, width))),
        (gain, whole((1, width))),
        (grad_middle, whole((rows, width))),
    ]
    outs = [((rows, width), full, whole((rows, width))), ((8, width), full, whole((8, width)))]
    if joined:
        rounded = ((rows, width), low, whole((rows, width)))
        outs = [rounded, outs[0], rounded, outs[0], outs[1]]
    return weighted(
        body,
        [weight] + ([join_weight] if joined else []),
        (3,),
        ins,
        outs,
        "project_back",
        13 if joined else 9,
        scratch=[pltpu.VMEM((rows, width), full)],
    )


def picked(body, which, grid, ins, outs, name, micros, aliases=None):
    return pl.pallas_call(
        body,
        grid_spec=pltpu.PrefetchScalarGridSpec(
            num_scalar_prefetch=1,
            grid=grid,
            in_specs=[spec for _, spec in ins],
            out_specs=[spec for _, _, spec in outs],
        ),
        out_shape=[jax.ShapeDtypeStruct(shape, kind) for shape, kind, _ in outs],
        name=name,
        input_output_aliases={place + 1: out for place, out in (aliases or {}).items()},
        cost_estimate=cost(micros),
        compiler_params=pltpu.CompilerParams(vmem_limit_bytes=48 * 2**20),
    )(which, *[array for array, _ in ins])


def up_term(left, right, core):
    rows, width = left.shape
    shares = lax.axis_size("narrow")
    part = width // shares

    def body(core_ref, l_ref, r_ref, out_ref):
        out_ref[...] = dot(l_ref[...], r_ref[...], (0, 0)).astype(low).reshape(shares, 1, part, width)

    return picked(
        body,
        core,
        (2,),
        [
            (left, pl.BlockSpec((rows, width), lambda g, core: (0, 0))),
            (right, pl.BlockSpec((rows, width), lambda g, core: (0, core[0] * 2 + g))),
        ],
        [((shares, 2, part, width), low, pl.BlockSpec((shares, 1, part, width), lambda g, core: (0, g, 0, 0)))],
        "up_term",
        3.5,
    )[0].reshape(shares, 2 * part, width)


def qkv_out_term(first, packed, mixed, branch, core):
    rows, width = first.shape
    shares = lax.axis_size("narrow")
    part = width // shares

    def body(core_ref, l_ref, r_ref, o_ref, b_ref, one_ref, two_ref):
        step = pl.program_id(0)
        last = core_ref[0] * 2 + step == 3

        @pl.when(last)
        def _():
            two_ref[...] = dot(o_ref[...], b_ref[...], (0, 0)).astype(low).reshape(shares, part, width)

        @pl.when(jnp.logical_not(last))
        def _():
            value = dot(l_ref[...], r_ref[0], (0, 0)).astype(low).reshape(shares, part, width)

            @pl.when(step == 0)
            def _():
                one_ref[...] = value

            @pl.when(step == 1)
            def _():
                two_ref[...] = value

    flat = pl.BlockSpec((rows, width), lambda g, core: (0, 0))
    out = ((shares, part, width), low, pl.BlockSpec((shares, part, width), lambda g, core: (0, 0, 0)))
    return picked(
        body,
        core,
        (2,),
        [
            (first, flat),
            (packed, pl.BlockSpec((1, rows, width), lambda g, core: (jnp.minimum(core[0] * 2 + g, 2), 0, 0))),
            (mixed, flat),
            (branch, flat),
        ],
        [out, out],
        "qkv_out_term",
        3.5,
    )


def down_term(left, right, core):
    rows, width = right.shape
    shares = lax.axis_size("narrow")
    part = left.shape[1] // (2 * shares)
    direct = part == width
    if not direct:
        left = left.reshape(rows, shares, 2, part)
        left = lax.dynamic_index_in_dim(left, core[0], 2, keepdims=False).reshape(rows, shares * part)
    steps = shares * part // width

    def body(core_ref, l_ref, r_ref, out_ref):
        out_ref[...] = dot(l_ref[...], r_ref[...], (0, 0)).astype(low)

    return picked(
        body,
        core,
        (steps,),
        [
            (left, pl.BlockSpec((rows, width), lambda g, core: (0, g * 2 + core[0] if direct else g))),
            (right, pl.BlockSpec((rows, width), lambda g, core: (0, 0))),
        ],
        [((shares * part, width), low, pl.BlockSpec((width, width), lambda g, core: (g, 0)))],
        "down_term",
        3.5,
    )[0].reshape(shares, part, width)


def join_term(middle, skip, right, core):
    rows, width = right.shape
    shares = lax.axis_size("narrow")
    part = width // shares
    half = width // 2
    if part != half:
        left = jnp.concatenate([middle, skip], axis=1).reshape(rows, shares, 2, part)
        left = lax.dynamic_index_in_dim(left, core[0], 2, keepdims=False).reshape(rows, shares * part)
        middle, skip = left[:, :half], left[:, half:]

    def body(core_ref, m_ref, s_ref, r_ref, out_ref):
        out_ref[:half] = dot(m_ref[...], r_ref[...], (0, 0)).astype(low)
        out_ref[half:] = dot(s_ref[...], r_ref[...], (0, 0)).astype(low)

    side = pl.BlockSpec((rows, half), lambda g, core: (0, core[0] if part == half else 0))
    return picked(
        body,
        core,
        (1,),
        [(middle, side), (skip, side), (right, pl.BlockSpec((rows, width), lambda g, core: (0, 0)))],
        [((width, width), low, pl.BlockSpec((width, width), lambda g, core: (0, 0)))],
        "join_term",
        2,
    )[0].reshape(shares, part, width)


def add_halve(bit, *pairs):
    lead, columns = pairs[0].shape[0], pairs[0].shape[-1]
    sizes = [pair.shape[2] for pair in pairs[::2]]
    total = sum(sizes)
    steps = 2 if len(sizes) == 1 and total % 32 == 0 and total >= 256 else 1

    def body(bit_ref, *refs):
        mine = bit_ref[0]
        for target, place in ((refs[-2], 1 - mine), (refs[-1], mine)):
            begin = 0
            for kept_ref, got_ref in zip(refs[:-2:2], refs[1:-2:2]):
                length = kept_ref.shape[2]
                for each in range(lead):
                    value = kept_ref[each, place].astype(full) + got_ref[each, place].astype(full)
                    target[each, begin : begin + length] = value.astype(low)
                begin += length

    ins = [
        (pair, pl.BlockSpec((lead, 2, pair.shape[2] // steps, columns), lambda g, bit: (0, 0, g, 0)))
        for pair in pairs
    ]
    out = (
        (lead, total, columns),
        low,
        pl.BlockSpec((lead, total // steps, columns), lambda g, bit: (0, g, 0)),
    )
    return picked(body, bit, (steps,), ins, [out, out], "add_halve", 2)


def add(one, two):
    return (one.astype(full) + two.astype(full)).astype(low)


def pair_up(own, got, bit):
    rows, columns = own.shape

    def body(bit_ref, own_ref, got_ref, out_ref):
        mine = bit_ref[0]
        out_ref[mine] = own_ref[...]
        out_ref[1 - mine] = got_ref[...]

    flat = pl.BlockSpec((rows, columns), lambda g, bit: (0, 0))
    out = ((2, rows, columns), low, pl.BlockSpec((2, rows, columns), lambda g, bit: (0, 0, 0)))
    return picked(body, bit, (1,), [(own, flat), (got, flat)], [out], "pair_up", 1)[0]


def finish(kind, half, own, got, begin, length, core, layer, targets):
    pieces, _, columns = own.shape
    scale = 1.0 / lax.axis_size("wide")
    aliases = {place + 2: place for place in range(len(targets))}
    source = pl.BlockSpec((pieces, length, columns), lambda g, core: (0, begin // length, 0))
    ins = [(own, source), (got, source)] + [(target, ANY) for target in targets]
    rows = pieces * length

    def chosen(core_ref, which, own_ref, got_ref, place=None):
        sides = [own_ref, got_ref]
        if place is None:
            values = [side[...].reshape(pieces * length, columns) for side in sides]
        else:
            near = pl.ds(place * (pieces // 2), pieces // 2)
            values = [side[near].reshape(pieces * length // 2, columns) for side in sides]
        return jnp.where(core_ref[0] == which, values[0], values[1]).astype(full) * scale

    if kind in ("down", "join"):

        def body(core_ref, own_ref, got_ref, *rest):
            rest[-1][0] = chosen(core_ref, pl.program_id(0), own_ref, got_ref)

        place = layer if kind == "down" else 0
        shape = (2 if kind == "down" else 1, 2 * rows, columns)
        out = (shape, full, pl.BlockSpec((1, rows, columns), lambda g, core: (place, g, 0)))
        return picked(body, core, (2,), ins, [out], "finish_rows", 3, aliases)
    steps = 4 if half is None else 2
    rows = rows // 2 if half is None else rows

    def block(step):
        return step if half is None else 2 * step + half

    def values_of(core_ref, own_ref, got_ref):
        step = pl.program_id(0)
        if half is None:
            return chosen(core_ref, step // 2, own_ref, got_ref, step % 2)
        return chosen(core_ref, step, own_ref, got_ref)

    def body(core_ref, own_ref, got_ref, *rest):
        values = values_of(core_ref, own_ref, got_ref)
        if kind == "up":
            rest[-1][0] = values
            return
        last = block(pl.program_id(0)) == 3

        @pl.when(jnp.logical_not(last))
        def _():
            rest[-2][0] = values

        @pl.when(last)
        def _():
            rest[-1][0] = values

    if kind == "up":
        outs = [((2, rows, 4 * columns), full, pl.BlockSpec((1, rows, columns), lambda g, core: (layer, 0, block(g))))]
        return picked(body, core, (steps,), ins, outs, "finish_columns", 3, aliases)
    outs = [
        (
            (2, rows, 3 * columns),
            full,
            pl.BlockSpec((1, rows, columns), lambda g, core: (layer, 0, jnp.minimum(block(g), 2))),
        ),
        ((2, rows, columns), full, pl.BlockSpec((1, rows, columns), lambda g, core: (layer, 0, 0))),
    ]
    return picked(body, core, (steps,), ins, outs, "finish_qkv_out", 3, aliases)


def after(value, *earlier):
    return lax.optimization_barrier((value,) + earlier)[0] if earlier else value


def swap(values, axis, mask):
    size = lax.axis_size(axis)
    return lax.ppermute(values, axis, [(source, source ^ mask) for source in range(size)])


def masks(axis):
    return [1 << bit for bit in range(lax.axis_size(axis).bit_length() - 1)]


class Order:
    def __init__(self):
        self.last = ()

    def run(self, function, *arrays):
        held = lax.optimization_barrier(tuple(arrays) + self.last)[: len(arrays)]
        out = function(*held)
        self.last = (jax.tree.leaves(out)[0],)
        return out


def place_bit(axis, mask):
    return ((lax.axis_index(axis) & mask) // mask).astype(jnp.int32).reshape(1)


class Term:
    def __init__(self, kind, layer, half, kept, got, core):
        self.kind, self.layer, self.half, self.kept, self.got, self.core = kind, layer, half, kept, got, core


def terms_of(order, kind, layer, function, *arrays):
    core = place_bit("wide", 1)
    sent = order.run(lambda *x: function(*x, 1 - core), *arrays)
    got = jax.tree.map(lambda each: swap(each, "wide", 1), sent)
    kept = order.run(lambda *x: function(*x, core), *arrays)
    if isinstance(kept, (tuple, list)):
        return [Term(kind, layer, place, kept[place], got[place], core) for place in range(len(kept))]
    return [Term(kind, layer, None, kept, got, core)]


class Reduce:
    def __init__(self, order, terms, first=()):
        self.order, self.terms = order, terms
        wide = [("wide", mask) for mask in masks("wide")[1:]]
        narrow = [("narrow", mask) for mask in reversed(masks("narrow"))]
        early = [stage for stage in wide if stage[1] in first]
        late = [stage for stage in wide if stage[1] not in first]
        self.early, self.down, self.up = early + narrow, late, list(reversed(early))
        self.pieces = 2 ** len(early)
        self.columns = terms[0].kept.shape[-1]
        self.passed = [0] * len(terms)
        self.parts = [(term.kept, term.got) for term in terms]
        self.joining, self.lengths, self.closed = None, None, False

    def halve(self, axis, mask, lead, pairs):
        shaped = [array.reshape(lead, 2, -1, self.columns) for pair in pairs for array in pair]
        bit = place_bit(axis, mask)
        sent, kept = self.order.run(lambda *x: add_halve(bit, *x), *shaped)
        return kept, swap(sent, axis, mask)

    def apart(self, place=0):
        axis, mask = self.early[self.passed[place]]
        self.passed[place] += 1
        lead = lax.axis_size("narrow") if axis == "wide" else 1
        self.parts[place] = self.halve(axis, mask, lead, [self.parts[place]])
        if axis == "narrow" and self.passed[place] < len(self.early):
            self.apart(place)

    def step(self):
        if self.down:
            axis, mask = self.down.pop(0)
            rows = [kept.size // self.columns for kept, _ in self.parts]
            even = all(each % 32 == 0 for each in rows)
            if self.lengths is None:
                self.lengths = [each // 2 for each in rows] if even else rows
                self.pieces *= 2 if even else 1
                if not even:
                    flat = [[side.reshape(-1, self.columns) for side in pair] for pair in self.parts]
                    self.parts = [tuple(jnp.concatenate(sides) for sides in zip(*flat))]
            if even:
                self.up.insert(0, (axis, mask))
                self.parts = [self.halve(axis, mask, 1, self.parts)]
            else:
                total = self.order.run(add, *self.parts[0])
                self.parts = [(total, swap(total, axis, mask))]
            return
        kept, got = [array.reshape(-1, self.columns) for array in self.parts[0]]
        if self.joining is None:
            total = self.order.run(add, kept, got)
        else:
            bit = place_bit(*self.joining)
            total = self.order.run(lambda *x: pair_up(*x, bit), kept, got).reshape(-1, self.columns)
        if self.up:
            self.joining = self.up.pop(0)
            self.parts = [(total, swap(total, *self.joining))]
        else:
            self.parts = [(total, swap(total, "wide", 1))]
            self.closed = True

    def finish(self, done):
        own, got = [array.reshape(self.pieces, -1, self.columns) for array in self.parts[0]]
        begin = 0
        for term, length in zip(self.terms, self.lengths):
            targets = done.get(term.kind, ())

            def last(own, got, core, *targets, term=term, begin=begin, length=length):
                return finish(term.kind, term.half, own, got, begin, length, core, term.layer, targets)

            done[term.kind] = self.order.run(last, own, got, term.core, *targets)
            begin += length


def on_device(
    tokens,
    skip,
    flags,
    cotangent,
    norm_gains,
    norm_biases,
    qkv_weight,
    out_weight,
    out_bias,
    up_weight,
    up_bias,
    down_weight,
    down_bias,
    skip_weight,
    skip_bias,
):
    items, seq_rows, width = tokens.shape
    rows = items * seq_rows
    me = lax.axis_index("narrow")
    shares = lax.axis_size("narrow")
    spots = jnp.stack([me, lax.axis_index("wide")]).astype(jnp.int32)
    order = Order()

    weights = (qkv_weight, out_weight, up_weight, down_weight)
    qkv0, out0, up0, down0 = [Weight(weight, 0, width, spots) for weight in weights]
    qkv1, out1, up1, down1 = [Weight(weight, 1, width, spots) for weight in weights]
    join = Weight(skip_weight, None, width, spots)

    qkv0.fetch()
    out0.fetch(qkv0.sent)
    up0.fetch(out0.sent)
    down0.fetch(up0.sent)
    small = (norm_gains, norm_biases, out_bias, up_bias, down_bias, skip_bias)
    held = after(jnp.concatenate([piece.reshape(-1) for piece in small]), down0.sent)[None]
    for mask in masks("narrow"):
        held = jnp.concatenate([held, swap(held, "narrow", mask)])
    parts = [lax.dynamic_index_in_dim(held, me ^ place, 0, keepdims=False) for place in range(shares)]
    wide_small, begin = [], 0
    for piece in small:
        end = begin + piece.size
        both = [part[begin:end].reshape(piece.shape) for part in parts]
        wide_small.append(jnp.concatenate(both, axis=-1).astype(full))
        begin = end
    gains, shifts, out_biases, up_biases, down_biases, join_shift = wide_small

    def line(values):
        return values.reshape(1, -1)

    tokens_flat, skip_flat, cotangent_flat = [array.reshape(rows, width) for array in (tokens, skip, cotangent)]
    lengths = PATCHES + 1 + CAPTION * flags
    valid = lax.broadcasted_iota(jnp.int32, (items, seq_rows), 1) < lengths[:, None]
    keep = valid.reshape(rows, 1).astype(full)
    dz1 = jnp.where(keep > 0, cotangent_flat, 0)

    qkv0.share(1)
    qkv0.share(0)
    a0, packed0 = order.run(lambda *x: project_qkv(*x, qkv0), tokens_flat, line(gains[0, 0]), line(shifts[0, 0]))
    out0.share(1, a0)
    up0.share(1, a0)
    down0.share(1, a0)
    join.fetch(a0)
    qkv1.fetch(a0)
    packed0 = packed0.reshape(3, items, seq_rows, width)
    mixed0, totals0 = order.run(lambda *x: attend(*x, items, seq_rows), packed0, lengths)
    out0.share(0, mixed0)
    up0.share(0, mixed0)
    down0.share(0, mixed0)
    join.share(1, mixed0)
    qkv1.share(1, mixed0)
    out1.fetch(mixed0)
    up1.fetch(mixed0)
    mixed0 = mixed0.reshape(rows, width)
    m0, second0, hidden0, slope0, middle = order.run(
        lambda x, o, ob, g, s, ub, db: feed_forward(x, o, out0, ob, g, s, up0, ub, down0, db),
        tokens_flat, mixed0, line(out_biases[0]), line(gains[0, 1]), line(shifts[0, 1]), line(up_biases[0]),
        line(down_biases[0]),
    )
    join.share(0, middle)
    qkv1.share(0, middle)
    out1.share(1, middle)
    up1.share(1, middle)
    down1.fetch(middle)
    entry, a1, packed1 = order.run(
        lambda m, s, jb, g, sh: join_qkv(m, s, join, jb, g, sh, qkv1),
        middle, skip_flat, line(join_shift), line(gains[1, 0]), line(shifts[1, 0]),
    )
    out1.share(0, a1)
    up1.share(0, a1)
    down1.share(1, a1)
    packed1 = packed1.reshape(3, items, seq_rows, width)
    mixed1, totals1 = order.run(lambda *x: attend(*x, items, seq_rows), packed1, lengths)
    mixed1 = mixed1.reshape(rows, width)
    down1.share(0, mixed1)
    m1, second1, hidden1, slope1, output = order.run(
        lambda x, o, ob, g, s, ub, db, k: feed_forward(x, o, out1, ob, g, s, up1, ub, down1, db, k),
        entry, mixed1, line(out_biases[1]), line(gains[1, 1]), line(shifts[1, 1]), line(up_biases[1]),
        line(down_biases[1]), keep,
    )

    down1_term = terms_of(order, "down", 1, down_term, hidden1, dz1)
    pending = Reduce(order, down1_term)
    pending.apart()
    du, dm, db, do, sums1, usum1 = order.run(
        lambda y, z, s, m, g: feed_forward_back(y, z, s, down1, up1, m, g, out1),
        dz1, dz1, slope1, m1, line(gains[1, 1]),
    )
    up1_term = terms_of(order, "up", 1, up_term, second1, du)
    first = Reduce(order, down1_term + up1_term)
    first.parts[0], first.passed[0] = pending.parts[0], pending.passed[0]
    first.apart(1)
    dpacked = order.run(
        lambda *x: attend_back(*x, items, seq_rows), packed1, do.reshape(items, seq_rows, width), totals1, lengths
    )
    flat_packed = dpacked.reshape(3, rows, width)
    qkv1_terms = terms_of(order, "qkv", 1, qkv_out_term, a1, flat_packed, mixed1, db)
    pending = Reduce(order, qkv1_terms)
    pending.apart(0)
    pending.apart(1)
    dentry, dmiddle, dz0, skip_grad, sums3 = order.run(
        lambda gp, x, g, dm: project_back(gp, qkv1, x, g, dm, join), flat_packed, entry, line(gains[1, 0]), dm
    )
    join_terms = terms_of(order, "join", 1, join_term, middle, skip_flat, dentry)
    first.step()
    second = Reduce(order, qkv1_terms + join_terms)
    second.parts[:2], second.passed[:2] = pending.parts, pending.passed
    second.apart(2)

    down0_term = terms_of(order, "down", 0, down_term, hidden0, dz0)
    pending = Reduce(order, down0_term, (4,))
    pending.apart()
    du, dm, db, do, sums0, usum0 = order.run(
        lambda y, z, s, m, g: feed_forward_back(y, z, s, down0, up0, m, g, out0),
        dmiddle, dz0, slope0, m0, line(gains[0, 1]),
    )
    up0_term = terms_of(order, "up", 0, up_term, second0, du)
    third = Reduce(order, down0_term + up0_term, (4,))
    third.parts[0], third.passed[0] = pending.parts[0], pending.passed[0]
    first.step()
    third.apart(1)
    third.apart(0)
    second.step()
    dpacked = order.run(
        lambda *x: attend_back(*x, items, seq_rows), packed0, do.reshape(items, seq_rows, width), totals0, lengths
    )
    flat_packed = dpacked.reshape(3, rows, width)
    qkv0_terms = terms_of(order, "qkv", 0, qkv_out_term, a0, flat_packed, mixed0, db)
    first.step()
    second.step()
    third.apart(1)
    fourth = Reduce(order, qkv0_terms[:1])
    fifth = Reduce(order, qkv0_terms[1:], (4,))
    fourth.apart()
    fifth.apart()
    first.step()
    tokens_grad, sums2 = order.run(
        lambda gp, x, g, dm: project_back(gp, qkv0, x, g, dm), flat_packed, tokens_flat, line(gains[0, 0]), dm
    )

    def norm_terms(place):
        return jnp.stack([jnp.stack([sums2[place], sums0[1 + place]]), jnp.stack([sums3[place], sums1[1 + place]])])

    minor = [
        norm_terms(0),
        norm_terms(1),
        jnp.stack([sums0[3], sums1[3]]),
        jnp.concatenate([usum0, usum1]),
        jnp.stack([sums0[0], sums1[0]]),
        sums3[2],
    ]
    split = [jnp.moveaxis(piece.reshape(piece.shape[:-1] + (shares, -1)), -2, 0) for piece in minor]
    minor_sum = jnp.concatenate([piece.reshape(shares, -1) for piece in split], axis=1)
    minor_stages = [("wide", mask) for mask in masks("wide")] + [("narrow", mask) for mask in masks("narrow")]
    minor_got = swap(minor_sum, *minor_stages[0])

    def minor_step():
        nonlocal minor_sum, minor_got
        if minor_stages:
            minor_stages.pop(0)
            minor_sum = order.run(lambda one, two: one + two, minor_sum, minor_got)
            if minor_stages:
                minor_got = swap(minor_sum, *minor_stages[0])

    done = {}
    first.step()
    second.step()
    third.step()
    minor_step()
    fifth.apart()
    first.step()
    second.step()
    fourth.step()
    minor_step()
    third.step()
    fifth.step()
    second.step()
    first.step()
    fourth.step()
    minor_step()
    third.step()
    fifth.step()
    first.finish(done)
    second.step()
    fourth.step()
    minor_step()
    third.step()
    fifth.step()
    second.step()
    fourth.step()
    minor_step()
    third.step()
    fifth.step()
    second.finish(done)
    for stage in range(9):
        minor_step()
        for each in (fourth, third, fifth):
            if not each.closed:
                each.step()
            elif each.parts:
                each.finish(done)
                each.parts = None

    owned = lax.dynamic_index_in_dim(minor_sum, me, 0, keepdims=False) * (1.0 / lax.axis_size("wide"))
    minor_sums, begin = [], 0
    for piece in split:
        end = begin + piece.size // shares
        minor_sums.append(owned[begin:end].reshape(piece.shape[1:]))
        begin = end
    return (
        output.reshape(tokens.shape),
        tokens_grad.reshape(tokens.shape),
        skip_grad.reshape(tokens.shape),
        minor_sums[0],
        minor_sums[1],
        done["qkv"][0],
        done["qkv"][1],
        minor_sums[2],
        done["up"][0],
        minor_sums[3],
        done["down"][0],
        minor_sums[4],
        done["join"][0][0],
        minor_sums[5],
    )


def solution(mesh):
    placed = (
        P(("wide", "narrow"), None, None),
        P(("wide", "narrow"), None, None),
        P(("wide", "narrow")),
        P(("wide", "narrow"), None, None),
        P(None, None, "narrow"),
        P(None, None, "narrow"),
        P(None, "narrow", None),
        P(None, "narrow", None),
        P(None, "narrow"),
        P(None, "narrow", None),
        P(None, "narrow"),
        P(None, "narrow", None),
        P(None, "narrow"),
        P("narrow", None),
        P("narrow"),
    )
    return jax.shard_map(
        on_device,
        mesh=mesh,
        in_specs=placed,
        out_specs=(
            P(("wide", "narrow"), None, None),
            P(("wide", "narrow"), None, None),
            P(("wide", "narrow"), None, None),
            P(None, None, "narrow"),
            P(None, None, "narrow"),
            P(None, "narrow", None),
            P(None, "narrow", None),
            P(None, "narrow"),
            P(None, "narrow", None),
            P(None, "narrow"),
            P(None, "narrow", None),
            P(None, "narrow"),
            P("narrow", None),
            P("narrow"),
        ),
        check_vma=False,
    )
```

```python
import jax
import jax.numpy as jnp
from jax import lax
from jax.experimental import pallas as pl
from jax.experimental.pallas import tpu as pltpu
from jax.sharding import PartitionSpec as P

HEAD_DIM = 64
PATCHES = 256
CAPTION = 77
PAIR = 2 * HEAD_DIM


epsilon = 1e-05
masked_score = -1e30
low = jnp.bfloat16
full = jnp.float32
ANY = pl.BlockSpec(memory_space=pl.ANY)
SCALARS = pl.BlockSpec(memory_space=pltpu.SMEM)


def dot(left, right, contract=(1, 0)):
    dims = (((contract[0],), (contract[1],)), ((), ()))
    return lax.dot_general(left, right, dims, preferred_element_type=full)


def normalize(values):
    centred = values - jnp.mean(values, axis=-1, keepdims=True)
    factor = lax.rsqrt(jnp.mean(centred * centred, axis=-1, keepdims=True) + epsilon)
    return centred * factor, factor


def normalize_back(upstream, normed, factor):
    return factor * (
        upstream
        - jnp.mean(upstream, axis=-1, keepdims=True)
        - normed * jnp.mean(upstream * normed, axis=-1, keepdims=True)
    )


def column_sum(values):
    return jnp.sum(values.astype(full), axis=0, keepdims=True)


def whole(shape):
    return pl.BlockSpec(shape, lambda *grid: (0,) * len(shape))


def cost(micros):
    return pl.CostEstimate(flops=int(micros * 3 * 10**8), bytes_accessed=0, transcendentals=0)


def call(body, grid, ins, outs, name, micros, scratch=(), limit=56):
    return pl.pallas_call(
        body,
        grid=grid,
        in_specs=[spec for _, spec in ins],
        out_specs=[spec for _, _, spec in outs],
        out_shape=[jax.ShapeDtypeStruct(shape, kind) for shape, kind, _ in outs],
        scratch_shapes=list(scratch),
        name=name,
        cost_estimate=cost(micros),
        compiler_params=pltpu.CompilerParams(vmem_limit_bytes=limit * 2**20),
    )(*[array for array, _ in ins])


class Weight:
    def __init__(self, array, layer, width, spots):
        self.array, self.layer, self.width, self.spots = array, layer, width, spots
        self.rows, self.columns = array.shape[-2:]
        self.shares = lax.axis_size("narrow")
        self.blocks = self.columns // width
        self.total = self.rows * self.shares
        self.sharing = masks("wide")[:2]
        while self.rows % (16 << len(self.sharing)):
            self.sharing.pop()
        self.count = 1 << len(self.sharing)
        self.length = self.rows // self.count

    def fetch(self, *earlier):
        array = after(self.array, *earlier)
        place = (lax.axis_index("wide") & (self.count - 1)) * self.length
        lead = () if self.layer is None else (self.layer,)
        sizes = (1,) * len(lead) + (self.length, self.columns)
        self.sent = lax.dynamic_slice(array, lead + (place, 0), sizes).reshape(1, self.length, self.columns)
        held = self.sent
        for mask in masks("narrow"):
            held = jnp.concatenate([held, swap(held, "narrow", mask)])
        self.pieces = {0: held[1:]}

    def share(self, which, *earlier):
        if which < len(self.sharing):
            mask = self.sharing[which]
            got = {key ^ mask: swap(after(piece, *earlier), "wide", mask) for key, piece in self.pieces.items()}
            self.pieces.update(got)

    def arrays(self):
        return [self.array] + list(self.pieces.values())

    def scratch(self):
        copies = 1 + len(self.pieces) * (self.shares - 1)
        return [pltpu.VMEM((self.blocks, self.total, self.width), low), pltpu.SemaphoreType.DMA((self.blocks, copies))]

    def copies(self, spots, refs, held, signals, block):
        own, pieces = refs[0], refs[1:]
        columns = pl.ds(block * self.width, self.width)
        me = spots[0]
        own = own if self.layer is None else own.at[self.layer]
        begin = pl.multiple_of(me * self.rows, 16)
        found = [(own.at[:, columns], begin, self.rows)]
        for key, piece in zip(self.pieces, pieces):
            for offset in range(1, self.shares):
                begin = (me ^ offset) * self.rows + ((spots[1] & (self.count - 1)) ^ key) * self.length
                found.append((piece.at[offset - 1, :, columns], pl.multiple_of(begin, 16), self.length))
        return [
            pltpu.make_async_copy(source, held.at[block, pl.ds(begin, length)], signals.at[block, place])
            for place, (source, begin, length) in enumerate(found)
        ]

    def start(self, *refs):
        for block in range(self.blocks):
            for copy in self.copies(*refs, block):
                copy.start()

    def wait(self, *refs, block=0):
        for copy in self.copies(*refs, block):
            copy.wait()


def weighted(body, weights, grid, ins, outs, name, micros, scratch=()):
    spots = weights[0].spots
    operands = [(spots, SCALARS)] + [(array, ANY) for weight in weights for array in weight.arrays()]
    counts = [len(weight.arrays()) for weight in weights]
    extra = [piece for weight in weights for piece in weight.scratch()]

    def wrapped(*refs):
        spots_ref, rest = refs[0], list(refs[1:])
        sources = []
        for count in counts:
            sources.append(rest[:count])
            rest = rest[count:]
        spare = rest[len(rest) - len(extra) :]
        rest = rest[: len(rest) - len(extra)]
        handles = []
        for place, weight in enumerate(weights):
            held, signals = spare[2 * place : 2 * place + 2]
            refs_of = (spots_ref, sources[place], held, signals)
            handles.append((weight, refs_of, held))

        @pl.when(pl.program_id(0) == 0)
        def _():
            for weight, refs_of, _ in handles:
                weight.start(*refs_of)

        def ready(place, block=0):
            weight, refs_of, held = handles[place]
            weight.wait(*refs_of, block=block)

        body(ready, [held for _, _, held in handles], *rest)

    return call(wrapped, grid, operands + ins, outs, name, micros, list(scratch) + extra)


def project_qkv(inputs, gain, shift, weight):
    rows, width = inputs.shape

    def body(ready, held, x_ref, gain_ref, shift_ref, a_ref, out_ref):
        step = pl.program_id(0)

        @pl.when(step == 0)
        def _():
            normed, _ = normalize(x_ref[...].astype(full))
            a_ref[...] = (normed * gain_ref[...] + shift_ref[...]).astype(low)

        ready(0, step)
        scale = jnp.where(step == 0, HEAD_DIM ** (-0.5), 1.0)
        out_ref[0] = (dot(a_ref[...], held[0][step]).astype(low).astype(full) * scale).astype(low)

    return weighted(
        body,
        [weight],
        (3,),
        [
            (inputs, whole((rows, width))),
            (gain, whole((1, width))),
            (shift, whole((1, width))),
        ],
        [
            ((rows, width), low, whole((rows, width))),
            ((3, rows, width), low, pl.BlockSpec((1, rows, width), lambda j: (j, 0, 0))),
        ],
        "project_qkv",
        7,
    )


def join_qkv(middle, skip, join_weight, join_shift, gain, shift, weight):
    rows, width = middle.shape

    def body(ready, held, m_ref, s_ref, jb_ref, gain_ref, shift_ref, e_ref, a_ref, out_ref):
        step = pl.program_id(0)

        @pl.when(step == 0)
        def _():
            ready(0)
            entry = dot(m_ref[...], held[0][0, :width]) + dot(s_ref[...], held[0][0, width:]) + jb_ref[...]
            e_ref[...] = entry
            normed, _ = normalize(entry)
            a_ref[...] = (normed * gain_ref[...] + shift_ref[...]).astype(low)

        ready(1, step)
        scale = jnp.where(step == 0, HEAD_DIM ** (-0.5), 1.0)
        out_ref[0] = (dot(a_ref[...], held[1][step]).astype(low).astype(full) * scale).astype(low)

    return weighted(
        body,
        [join_weight, weight],
        (3,),
        [
            (middle, whole((rows, width))),
            (skip, whole((rows, width))),
            (join_shift, whole((1, width))),
            (gain, whole((1, width))),
            (shift, whole((1, width))),
        ],
        [
            ((rows, width), full, whole((rows, width))),
            ((rows, width), low, whole((rows, width))),
            ((3, rows, width), low, pl.BlockSpec((1, rows, width), lambda j: (j, 0, 0))),
        ],
        "join_qkv",
        11,
    )


def head_masks(seq_rows):
    lane = lax.broadcasted_iota(jnp.int32, (seq_rows, PAIR), 1)
    return [lane < HEAD_DIM, lane >= HEAD_DIM]


def attend(packed, lengths, items, seq_rows):
    width = packed.shape[-1]
    pairs = width // PAIR

    def body(length_ref, q_ref, k_ref, v_ref, out_ref, total_ref):
        length = length_ref[pl.program_id(0)]
        queries, keys, values = q_ref[0, 0], k_ref[0, 0], v_ref[0, 0]
        counts = lax.broadcasted_iota(jnp.int32, (seq_rows, seq_rows), 0) < length
        mixed = jnp.zeros((PAIR, seq_rows), full)
        for head, lanes in enumerate(head_masks(seq_rows)):
            scores = dot(keys, jnp.where(lanes, queries, 0), (1, 1))
            scores = jnp.where(counts, scores, masked_score)
            largest = jnp.max(scores, axis=0, keepdims=True)
            weights = jnp.exp(scores - largest)
            total = jnp.sum(weights, axis=0, keepdims=True)
            part = dot(jnp.where(lanes, values, 0), weights.astype(low), (0, 0))
            mixed += part * (1.0 / total)
            total_ref[0, 0, head : head + 1] = largest + jnp.log(total)
        out_ref[0] = mixed.T.astype(low)

    def block(which):
        return pl.BlockSpec((1, 1, seq_rows, PAIR), lambda n, h: (which, n, 0, h))

    return call(
        body,
        (items, pairs),
        [
            (lengths, SCALARS),
            (packed, block(0)),
            (packed, block(1)),
            (packed, block(2)),
        ],
        [
            ((items, seq_rows, width), low, pl.BlockSpec((1, seq_rows, PAIR), lambda n, h: (n, 0, h))),
            ((items, pairs, 8, seq_rows), full, pl.BlockSpec((1, 1, 8, seq_rows), lambda n, h: (n, h, 0, 0))),
        ],
        "attend",
        13,
    )


def attend_back(packed, grad_mixed, totals, lengths, items, seq_rows):
    width = packed.shape[-1]
    pairs = width // PAIR

    def body(length_ref, q_ref, k_ref, v_ref, g_ref, total_ref, out_ref):
        length = length_ref[pl.program_id(0)]
        queries, keys, values, upstream = q_ref[0, 0], k_ref[0, 0], v_ref[0, 0], g_ref[0]
        counts = lax.broadcasted_iota(jnp.int32, (seq_rows, seq_rows), 0) < length
        grad_queries = jnp.zeros((PAIR, seq_rows), full)
        grad_keys = jnp.zeros((seq_rows, PAIR), full)
        grad_values = jnp.zeros((seq_rows, PAIR), full)
        for head, lanes in enumerate(head_masks(seq_rows)):
            own_queries = jnp.where(lanes, queries, 0)
            own_upstream = jnp.where(lanes, upstream, 0)
            scores = dot(keys, own_queries, (1, 1))
            shifted = jnp.where(counts, scores, masked_score) - total_ref[0, 0, head : head + 1]
            probs = jnp.exp(shifted)
            grad_probs = dot(values, own_upstream, (1, 1))
            centre = jnp.sum(grad_probs * probs, axis=0, keepdims=True)
            grad_scores = (probs * (grad_probs - centre)).astype(low)
            grad_values += dot(probs.astype(low), own_upstream)
            grad_keys += dot(grad_scores, own_queries)
            grad_queries += dot(jnp.where(lanes, keys, 0), grad_scores, (0, 0))
        out_ref[0, 0] = (grad_queries.T * HEAD_DIM ** (-0.5)).astype(low)
        out_ref[1, 0] = grad_keys.astype(low)
        out_ref[2, 0] = grad_values.astype(low)

    def block(which):
        return pl.BlockSpec((1, 1, seq_rows, PAIR), lambda n, h: (which, n, 0, h))

    return call(
        body,
        (items, pairs),
        [
            (lengths, SCALARS),
            (packed, block(0)),
            (packed, block(1)),
            (packed, block(2)),
            (grad_mixed, pl.BlockSpec((1, seq_rows, PAIR), lambda n, h: (n, 0, h))),
            (totals, pl.BlockSpec((1, 1, 8, seq_rows), lambda n, h: (n, h, 0, 0))),
        ],
        [
            ((3, items, seq_rows, width), low, pl.BlockSpec((3, 1, seq_rows, PAIR), lambda n, h: (0, n, 0, h))),
        ],
        "attend_back",
        17,
    )[0]


def gelu_parts(before):
    decay = jnp.exp(before * before * -0.5)
    inverse = pl.reciprocal(1.0 + (0.3275911 * 0.5**0.5) * jnp.abs(before), approx=False)
    series = 1.061405429 * 0.5
    for term in (-1.453152027, 1.421413741, -0.284496736, 0.254829592):
        series = series * inverse + term * 0.5
    below = series * inverse * decay
    share = jnp.where(before >= 0, 1.0 - below, below)
    return before * share, share + before * decay * 0.3989422804014327


def feed_forward(inputs, mixed, out_weight, out_bias, gain, shift, up_weight, up_bias, down_weight, down_bias, keep=None):
    rows, width = inputs.shape
    steps = up_weight.blocks
    hidden = steps * width

    def body(ready, held, x_ref, o_ref, ob_ref, gain_ref, shift_ref, ub_ref, db_ref, *rest):
        m_ref, a_ref, g_ref, s_ref, y_ref, total = rest[-6:]
        step = pl.program_id(0)

        @pl.when(step == 0)
        def _():
            ready(0)
            middle = x_ref[...].astype(full) + dot(o_ref[...], held[0][0]) + ob_ref[...]
            m_ref[...] = middle
            normed, _ = normalize(middle)
            a_ref[...] = (normed * gain_ref[...] + shift_ref[...]).astype(low)
            total[...] = middle + db_ref[...]

        ready(1, step)
        before = dot(a_ref[...], held[1][step]) + ub_ref[...]
        value, slope = gelu_parts(before)
        g_ref[...] = value.astype(low)
        s_ref[...] = slope.astype(low)

        @pl.when(step == 0)
        def _():
            ready(2)

        total[...] += dot(g_ref[...], held[2][0, pl.ds(pl.multiple_of(step * width, width), width)])

        @pl.when(step == steps - 1)
        def _():
            value = total[...]
            if keep is not None:
                value = jnp.where(rest[0][...] > 0, value, 0.0)
            y_ref[...] = value.astype(low)

    return weighted(
        body,
        [out_weight, up_weight, down_weight],
        (steps,),
        [
            (inputs, whole((rows, width))),
            (mixed, whole((rows, width))),
            (out_bias, whole((1, width))),
            (gain, whole((1, width))),
            (shift, whole((1, width))),
            (up_bias, pl.BlockSpec((1, width), lambda j: (0, j))),
            (down_bias, whole((1, width))),
        ]
        + ([] if keep is None else [(keep, whole((rows, 1)))]),
        [
            ((rows, width), full, whole((rows, width))),
            ((rows, width), low, whole((rows, width))),
            ((rows, hidden), low, pl.BlockSpec((rows, width), lambda j: (0, j))),
            ((rows, hidden), low, pl.BlockSpec((rows, width), lambda j: (0, j))),
            ((rows, width), low, whole((rows, width))),
        ],
        "feed_forward",
        23,
        scratch=[pltpu.VMEM((rows, width), full)],
    )


def feed_forward_back(upstream, rounded, slope, down_weight, up_weight, middle, gain, out_weight):
    rows, width = upstream.shape
    steps = up_weight.blocks
    hidden = steps * width

    def body(ready, held, y_ref, dz_ref, s_ref, m_ref, gain_ref, du_ref, dm_ref, db_ref, do_ref, sums_ref, usum_ref, total):
        step = pl.program_id(0)

        @pl.when(step == 0)
        def _():
            sums_ref[0:1] = column_sum(dz_ref[...])
            total[...] = jnp.zeros_like(total)
            ready(0)

        down = held[0][0, pl.ds(pl.multiple_of(step * width, width), width)]
        grad = (dot(dz_ref[...], down, (1, 1)) * s_ref[...].astype(full)).astype(low)
        du_ref[...] = grad
        usum_ref[...] = column_sum(grad)
        ready(1, step)
        total[...] += dot(grad, held[1][step], (1, 1))

        @pl.when(step == steps - 1)
        def _():
            grad_second = total[...]
            normed, factor = normalize(m_ref[...])
            sums_ref[1:2] = column_sum(grad_second * normed)
            sums_ref[2:3] = column_sum(grad_second)
            grad_middle = y_ref[...].astype(full) + normalize_back(grad_second * gain_ref[...], normed, factor)
            dm_ref[...] = grad_middle
            branch = grad_middle.astype(low)
            db_ref[...] = branch
            sums_ref[3:4] = column_sum(branch)
            ready(2)
            do_ref[...] = dot(branch, held[2][0], (1, 1)).astype(low)

    return weighted(
        body,
        [down_weight, up_weight, out_weight],
        (steps,),
        [
            (upstream, whole((rows, width))),
            (rounded, whole((rows, width))),
            (slope, pl.BlockSpec((rows, width), lambda j: (0, j))),
            (middle, whole((rows, width))),
            (gain, whole((1, width))),
        ],
        [
            ((rows, hidden), low, pl.BlockSpec((rows, width), lambda j: (0, j))),
            ((rows, width), full, whole((rows, width))),
            ((rows, width), low, whole((rows, width))),
            ((rows, width), low, whole((rows, width))),
            ((8, width), full, whole((8, width))),
            ((1, hidden), full, pl.BlockSpec((1, width), lambda j: (0, j))),
        ],
        "feed_forward_back",
        21,
        scratch=[pltpu.VMEM((rows, width), full)],
    )


def project_back(grad_packed, weight, inputs, gain, grad_middle, join_weight=None):
    rows, width = inputs.shape
    joined = join_weight is not None

    def body(ready, held, g_ref, x_ref, gain_ref, dm_ref, *rest):
        if joined:
            de_ref, dx_ref, dz_ref, skip_ref, sums_ref, total = rest
        else:
            dx_ref, sums_ref, total = rest
        step = pl.program_id(0)

        @pl.when(step == 0)
        def _():
            total[...] = jnp.zeros_like(total)

        ready(0, step)
        total[...] += dot(g_ref[0], held[0][step], (1, 1))

        @pl.when(step == 2)
        def _():
            grad_first = total[...]
            normed, factor = normalize(x_ref[...].astype(full))
            sums_ref[0:1] = column_sum(grad_first * normed)
            sums_ref[1:2] = column_sum(grad_first)
            grad = dm_ref[...] + normalize_back(grad_first * gain_ref[...], normed, factor)
            if joined:
                entry = grad.astype(low)
                de_ref[...] = entry
                sums_ref[2:3] = column_sum(entry)
                ready(1)
                grad = dot(entry, held[1][0, :width], (1, 1))
                dx_ref[...] = grad
                dz_ref[...] = grad.astype(low)
                skip_ref[...] = dot(entry, held[1][0, width:], (1, 1))
            else:
                dx_ref[...] = grad

    ins = [
        (grad_packed, pl.BlockSpec((1, rows, width), lambda j: (j, 0, 0))),
        (inputs, whole((rows, width))),
        (gain, whole((1, width))),
        (grad_middle, whole((rows, width))),
    ]
    outs = [((rows, width), full, whole((rows, width))), ((8, width), full, whole((8, width)))]
    if joined:
        rounded = ((rows, width), low, whole((rows, width)))
        outs = [rounded, outs[0], rounded, outs[0], outs[1]]
    return weighted(
        body,
        [weight] + ([join_weight] if joined else []),
        (3,),
        ins,
        outs,
        "project_back",
        13 if joined else 9,
        scratch=[pltpu.VMEM((rows, width), full)],
    )


def picked(body, which, grid, ins, outs, name, micros, aliases=None):
    return pl.pallas_call(
        body,
        grid_spec=pltpu.PrefetchScalarGridSpec(
            num_scalar_prefetch=1,
            grid=grid,
            in_specs=[spec for _, spec in ins],
            out_specs=[spec for _, _, spec in outs],
        ),
        out_shape=[jax.ShapeDtypeStruct(shape, kind) for shape, kind, _ in outs],
        name=name,
        input_output_aliases={place + 1: out for place, out in (aliases or {}).items()},
        cost_estimate=cost(micros),
        compiler_params=pltpu.CompilerParams(vmem_limit_bytes=48 * 2**20),
    )(which, *[array for array, _ in ins])


def quarters(rows, width, narrow_rows):
    shape = (lax.axis_size("narrow") // 2 * narrow_rows, width)
    return [(shape, low, pl.BlockSpec(shape, lambda g, core: (0, 0)))] * 4


def up_term(left, right, core):
    rows, width = left.shape
    part = width // lax.axis_size("narrow")
    half = width // 2

    def body(core_ref, l_ref, r_ref, *outs):
        value = dot(l_ref[...], r_ref[...], (0, 0)).astype(low)
        for block in range(2):

            @pl.when(pl.program_id(0) == block)
            def _():
                outs[block][...] = value[:half]
                outs[2 + block][...] = value[half:]

    return picked(
        body,
        core,
        (2,),
        [
            (left, pl.BlockSpec((rows, width), lambda g, core: (0, 0))),
            (right, pl.BlockSpec((rows, width), lambda g, core: (0, core[0] * 2 + g))),
        ],
        quarters(rows, width, part),
        "up_term",
        3.5,
    )


def qkv_out_term(first, packed, mixed, branch, core):
    rows, width = first.shape
    part = width // lax.axis_size("narrow")
    half = width // 2

    def body(core_ref, l_ref, r_ref, o_ref, b_ref, *outs):
        step = pl.program_id(0)
        last = core_ref[0] * 2 + step == 3

        def put(block, value):
            outs[block][...] = value[:half]
            outs[2 + block][...] = value[half:]

        @pl.when(last)
        def _():
            put(1, dot(o_ref[...], b_ref[...], (0, 0)).astype(low))

        @pl.when(jnp.logical_not(last))
        def _():
            value = dot(l_ref[...], r_ref[0], (0, 0)).astype(low)
            for block in range(2):

                @pl.when(step == block)
                def _():
                    put(block, value)

    flat = pl.BlockSpec((rows, width), lambda g, core: (0, 0))
    return picked(
        body,
        core,
        (2,),
        [
            (first, flat),
            (packed, pl.BlockSpec((1, rows, width), lambda g, core: (jnp.minimum(core[0] * 2 + g, 2), 0, 0))),
            (mixed, flat),
            (branch, flat),
        ],
        quarters(rows, width, part),
        "qkv_out_term",
        3.5,
    )


def down_term(left, right, core):
    rows, width = right.shape
    shares = lax.axis_size("narrow")
    part = left.shape[1] // (2 * shares)
    direct = part == width
    if not direct:
        left = left.reshape(rows, shares, 2, 2, part // 2)
        left = lax.dynamic_index_in_dim(left, core[0], 2, keepdims=False)
        left = left.reshape(rows, 2, shares // 2, 2, part // 2).swapaxes(2, 3).reshape(rows, 2 * width)
    half = width // 2

    def body(core_ref, l_ref, r_ref, *outs):
        value = dot(l_ref[...], r_ref[...], (0, 0)).astype(low)
        for owner in range(2):

            @pl.when(pl.program_id(0) == owner)
            def _():
                outs[2 * owner][...] = value[:half]
                outs[2 * owner + 1][...] = value[half:]

    return picked(
        body,
        core,
        (2,),
        [
            (left, pl.BlockSpec((rows, width), lambda g, core: (0, g * 2 + core[0] if direct else g))),
            (right, pl.BlockSpec((rows, width), lambda g, core: (0, 0))),
        ],
        quarters(rows, width, part // 2),
        "down_term",
        3.5,
    )


def join_term(middle, skip, right, core):
    rows, width = right.shape
    shares = lax.axis_size("narrow")
    part = width // shares
    half = width // 2
    if part != half:
        left = jnp.concatenate([middle, skip], axis=1).reshape(rows, shares, 2, 2, part // 2)
        left = lax.dynamic_index_in_dim(left, core[0], 2, keepdims=False)
        left = left.reshape(rows, 2, shares // 2, 2, part // 2).swapaxes(2, 3).reshape(rows, width)
        middle, skip = left[:, :half], left[:, half:]

    def body(core_ref, m_ref, s_ref, r_ref, *outs):
        for owner, left_ref in enumerate((m_ref, s_ref)):
            value = dot(left_ref[...], r_ref[...], (0, 0)).astype(low)
            outs[2 * owner][...] = value[: half // 2]
            outs[2 * owner + 1][...] = value[half // 2 :]

    side = pl.BlockSpec((rows, half), lambda g, core: (0, core[0] if part == half else 0))
    return picked(
        body,
        core,
        (1,),
        [(middle, side), (skip, side), (right, pl.BlockSpec((rows, width), lambda g, core: (0, 0)))],
        quarters(rows, width, part // 2),
        "join_term",
        2,
    )


def cross(bit, *pieces):
    kept, got = pieces[:4], pieces[4:]
    rows, columns = kept[0].shape
    steps = 2 if rows % 32 == 0 else 1

    def body(bit_ref, *refs):
        sent_ref, left_ref = refs[8:]

        def put(target, owner):
            for block in range(2):
                one, two = refs[2 * owner + block], refs[4 + 2 * owner + block]
                target[block] = (one[...].astype(full) + two[...].astype(full)).astype(low)

        for mine in range(2):

            @pl.when(bit_ref[0] == mine)
            def _():
                put(sent_ref, 1 - mine)
                put(left_ref, mine)

    ins = [(piece, pl.BlockSpec((rows // steps, columns), lambda g, bit: (g, 0))) for piece in kept + got]
    out = ((2, rows, columns), low, pl.BlockSpec((2, rows // steps, columns), lambda g, bit: (0, g, 0)))
    return picked(body, bit, (steps,), ins, [out, out], "cross", 2.5)


def add_halve(bit, *pairs):
    lead, columns = pairs[0].shape[0], pairs[0].shape[-1]
    sizes = [pair.shape[2] for pair in pairs[::2]]
    total = sum(sizes)
    steps = 2 if len(sizes) == 1 and total % 32 == 0 and total >= 256 else 1

    def body(bit_ref, *refs):
        mine = bit_ref[0]
        for target, place in ((refs[-2], 1 - mine), (refs[-1], mine)):
            begin = 0
            for kept_ref, got_ref in zip(refs[:-2:2], refs[1:-2:2]):
                length = kept_ref.shape[2]
                for each in range(lead):
                    value = kept_ref[each, place].astype(full) + got_ref[each, place].astype(full)
                    target[each, begin : begin + length] = value.astype(low)
                begin += length

    ins = [
        (pair, pl.BlockSpec((lead, 2, pair.shape[2] // steps, columns), lambda g, bit: (0, 0, g, 0)))
        for pair in pairs
    ]
    out = (
        (lead, total, columns),
        low,
        pl.BlockSpec((lead, total // steps, columns), lambda g, bit: (0, g, 0)),
    )
    return picked(body, bit, (steps,), ins, [out, out], "add_halve", 2)


def add(one, two):
    return (one.astype(full) + two.astype(full)).astype(low)


def pair_up(own, got, bit):
    rows, columns = own.shape

    def body(bit_ref, own_ref, got_ref, out_ref):
        mine = bit_ref[0]
        out_ref[mine] = own_ref[...]
        out_ref[1 - mine] = got_ref[...]

    flat = pl.BlockSpec((rows, columns), lambda g, bit: (0, 0))
    out = ((2, rows, columns), low, pl.BlockSpec((2, rows, columns), lambda g, bit: (0, 0, 0)))
    return picked(body, bit, (1,), [(own, flat), (got, flat)], [out], "pair_up", 1)[0]


def finish(kind, half, own, got, begin, length, core, layer, targets):
    pieces, _, columns = own.shape
    scale = 1.0 / lax.axis_size("wide")
    aliases = {place + 2: place for place in range(len(targets))}
    source = pl.BlockSpec((pieces, length, columns), lambda g, core: (0, begin // length, 0))
    ins = [(own, source), (got, source)] + [(target, ANY) for target in targets]
    rows = pieces * length

    def chosen(core_ref, which, own_ref, got_ref, place=None):
        sides = [own_ref, got_ref]
        if place is None:
            values = [side[...].reshape(pieces * length, columns) for side in sides]
        else:
            near = pl.ds(place * (pieces // 2), pieces // 2)
            values = [side[near].reshape(pieces * length // 2, columns) for side in sides]
        return jnp.where(core_ref[0] == which, values[0], values[1]).astype(full) * scale

    if kind in ("down", "join"):

        def body(core_ref, own_ref, got_ref, *rest):
            rest[-1][0] = chosen(core_ref, pl.program_id(0), own_ref, got_ref)

        place = layer if kind == "down" else 0
        shape = (2 if kind == "down" else 1, 2 * rows, columns)
        out = (shape, full, pl.BlockSpec((1, rows, columns), lambda g, core: (place, g, 0)))
        return picked(body, core, (2,), ins, [out], "finish_rows", 3, aliases)
    steps = 4 if half is None else 2
    rows = rows // 2 if half is None else rows

    def block(step):
        return step if half is None else 2 * step + half

    def values_of(core_ref, own_ref, got_ref):
        step = pl.program_id(0)
        if half is None:
            return chosen(core_ref, step // 2, own_ref, got_ref, step % 2)
        return chosen(core_ref, step, own_ref, got_ref)

    def body(core_ref, own_ref, got_ref, *rest):
        values = values_of(core_ref, own_ref, got_ref)
        if kind == "up":
            rest[-1][0] = values
            return
        last = block(pl.program_id(0)) == 3

        @pl.when(jnp.logical_not(last))
        def _():
            rest[-2][0] = values

        @pl.when(last)
        def _():
            rest[-1][0] = values

    if kind == "up":
        outs = [((2, rows, 4 * columns), full, pl.BlockSpec((1, rows, columns), lambda g, core: (layer, 0, block(g))))]
        return picked(body, core, (steps,), ins, outs, "finish_columns", 3, aliases)
    outs = [
        (
            (2, rows, 3 * columns),
            full,
            pl.BlockSpec((1, rows, columns), lambda g, core: (layer, 0, jnp.minimum(block(g), 2))),
        ),
        ((2, rows, columns), full, pl.BlockSpec((1, rows, columns), lambda g, core: (layer, 0, 0))),
    ]
    return picked(body, core, (steps,), ins, outs, "finish_qkv_out", 3, aliases)


def after(value, *earlier):
    return lax.optimization_barrier((value,) + earlier)[0] if earlier else value


def swap(values, axis, mask):
    size = lax.axis_size(axis)
    return lax.ppermute(values, axis, [(source, source ^ mask) for source in range(size)])


def masks(axis):
    return [1 << bit for bit in range(lax.axis_size(axis).bit_length() - 1)]


class Order:
    def __init__(self):
        self.last = ()

    def run(self, function, *arrays):
        held = lax.optimization_barrier(tuple(arrays) + self.last)[: len(arrays)]
        out = function(*held)
        self.last = (jax.tree.leaves(out)[0],)
        return out

    def hold(self, *arrays):
        self.last += arrays


def place_bit(axis, mask):
    return ((lax.axis_index(axis) & mask) // mask).astype(jnp.int32).reshape(1)


class Term:
    def __init__(self, order, kind, layer, function, *arrays):
        self.order, self.kind, self.layer = order, kind, layer
        self.core = place_bit("wide", 1)
        sent = order.run(lambda *x: function(*x, 1 - self.core), *arrays)
        self.got = [swap(each, "wide", 1) for each in sent]
        self.columns = sent[0].shape[-1]
        self.keep = lambda: order.run(lambda *x: function(*x, self.core), *arrays)

    def stay(self):
        self.kept, self.keep = self.keep(), None

    def pass_narrow(self):
        stages = list(reversed(masks("narrow")))
        if self.keep:
            self.stay()
        bit = place_bit("narrow", stages[0])
        sent, self.kept = self.order.run(lambda *x: cross(bit, *x), *self.kept, *self.got)
        self.got = swap(sent, "narrow", stages[0])
        for mask in stages[1:]:
            self.kept, self.got = halve(self.order, "narrow", mask, 2, [(self.kept, self.got)], self.columns)


    def pass_wide(self, mask):
        self.kept, self.got = halve(self.order, "wide", mask, 1, [(self.kept, self.got)], self.columns)


def halve(order, axis, mask, lead, pairs, columns):
    shaped = [array.reshape(lead, 2, -1, columns) for pair in pairs for array in pair]
    bit = place_bit(axis, mask)
    sent, kept = order.run(lambda *x: add_halve(bit, *x), *shaped)
    return kept, swap(sent, axis, mask)


class Reduce:
    def __init__(self, order, terms, passed=()):
        self.order, self.terms = order, terms
        self.down = [mask for mask in masks("wide")[1:] if mask not in passed]
        self.up = list(reversed(passed))
        self.pieces, self.columns = 2 ** len(passed), terms[0].columns
        self.parts = [(term.kept, term.got) for term in terms]
        self.lengths, self.first = [each.size // self.columns for each, _ in self.parts], True
        self.joining, self.closed = None, False

    def step(self):
        if self.closed:
            return
        if self.down:
            mask = self.down.pop(0)
            rows = [kept.size // self.columns for kept, _ in self.parts]
            even = all(each % 32 == 0 for each in rows)
            if self.first and even:
                self.pieces, self.lengths = 2 * self.pieces, [each // 2 for each in rows]
            self.first = False
            if even:
                self.up.insert(0, mask)
                self.parts = [halve(self.order, "wide", mask, 1, self.parts, self.columns)]
            else:
                flat = [[side.reshape(-1, self.columns) for side in pair] for pair in self.parts]
                pair = [jnp.concatenate(sides) for sides in zip(*flat)]
                total = self.order.run(add, *pair)
                self.parts = [(total, swap(total, "wide", mask))]
            return
        kept, got = [array.reshape(-1, self.columns) for array in self.parts[0]]
        if self.joining is None:
            total = self.order.run(add, kept, got)
        else:
            bit = place_bit("wide", self.joining)
            total = self.order.run(lambda *x: pair_up(*x, bit), kept, got).reshape(-1, self.columns)
        if self.up:
            self.joining = self.up.pop(0)
            self.parts = [(total, swap(total, "wide", self.joining))]
        else:
            self.parts = [(total, swap(total, "wide", 1))]
            self.closed = True

    def sum_rest(self):
        rows = [kept.size // self.columns for kept, _ in self.parts]
        flat = [[side.reshape(-1, self.columns) for side in pair] for pair in self.parts]
        self.lengths, self.pieces = [each // 2 for each in rows], 2
        flat = [[side.reshape(2, -1, self.columns) for side in pair] for pair in self.parts]
        pair = [jnp.concatenate(sides, axis=1) for sides in zip(*flat)]
        total = self.order.run(add, *pair)
        size = lax.axis_size("wide")
        groups = [[device + core for device in range(0, size, 2)] for core in range(2)]
        total = lax.psum(total, "wide", axis_index_groups=groups)
        self.parts, self.down, self.up, self.joining = [(total,)], [], [], 0

    def close(self):
        total = self.parts[0][0].reshape(-1, self.columns)
        total = self.order.run(lambda x: x, total) if False else total
        self.parts = [(total, swap(total, "wide", 1))]
        self.closed = True

    def finish(self, done):
        own, got = [array.reshape(self.pieces, -1, self.columns) for array in self.parts[0]]
        begin = 0
        for term, length in zip(self.terms, self.lengths):
            targets = done.get(term.kind, ())

            def last(own, got, core, *targets, term=term, begin=begin, length=length):
                return finish(term.kind, None, own, got, begin, length, core, term.layer, targets)

            done[term.kind] = self.order.run(last, own, got, term.core, *targets)
            begin += length


def on_device(
    tokens,
    skip,
    flags,
    cotangent,
    norm_gains,
    norm_biases,
    qkv_weight,
    out_weight,
    out_bias,
    up_weight,
    up_bias,
    down_weight,
    down_bias,
    skip_weight,
    skip_bias,
):
    items, seq_rows, width = tokens.shape
    rows = items * seq_rows
    me = lax.axis_index("narrow")
    shares = lax.axis_size("narrow")
    spots = jnp.stack([me, lax.axis_index("wide")]).astype(jnp.int32)
    order = Order()

    weights = (qkv_weight, out_weight, up_weight, down_weight)
    qkv0, out0, up0, down0 = [Weight(weight, 0, width, spots) for weight in weights]
    qkv1, out1, up1, down1 = [Weight(weight, 1, width, spots) for weight in weights]
    join = Weight(skip_weight, None, width, spots)

    qkv0.fetch()
    out0.fetch(qkv0.sent)
    up0.fetch(out0.sent)
    down0.fetch(up0.sent)
    small = (norm_gains, norm_biases, out_bias, up_bias, down_bias, skip_bias)
    held = after(jnp.concatenate([piece.reshape(-1) for piece in small]), down0.sent)[None]
    for mask in masks("narrow"):
        held = jnp.concatenate([held, swap(held, "narrow", mask)])
    parts = [lax.dynamic_index_in_dim(held, me ^ place, 0, keepdims=False) for place in range(shares)]
    wide_small, begin = [], 0
    for piece in small:
        end = begin + piece.size
        both = [part[begin:end].reshape(piece.shape) for part in parts]
        wide_small.append(jnp.concatenate(both, axis=-1).astype(full))
        begin = end
    gains, shifts, out_biases, up_biases, down_biases, join_shift = wide_small

    def line(values):
        return values.reshape(1, -1)

    tokens_flat, skip_flat, cotangent_flat = [array.reshape(rows, width) for array in (tokens, skip, cotangent)]
    lengths = PATCHES + 1 + CAPTION * flags
    valid = lax.broadcasted_iota(jnp.int32, (items, seq_rows), 1) < lengths[:, None]
    keep = valid.reshape(rows, 1).astype(full)
    dz1 = jnp.where(keep > 0, cotangent_flat, 0)

    qkv0.share(1)
    qkv0.share(0)
    a0, packed0 = order.run(lambda *x: project_qkv(*x, qkv0), tokens_flat, line(gains[0, 0]), line(shifts[0, 0]))
    out0.share(1, a0)
    up0.share(1, a0)
    down0.share(1, a0)
    join.fetch(a0)
    qkv1.fetch(a0)
    packed0 = packed0.reshape(3, items, seq_rows, width)
    mixed0, totals0 = order.run(lambda *x: attend(*x, items, seq_rows), packed0, lengths)
    out0.share(0, mixed0)
    up0.share(0, mixed0)
    down0.share(0, mixed0)
    join.share(1, mixed0)
    qkv1.share(1, mixed0)
    out1.fetch(mixed0)
    up1.fetch(mixed0)
    mixed0 = mixed0.reshape(rows, width)
    m0, second0, hidden0, slope0, middle = order.run(
        lambda x, o, ob, g, s, ub, db: feed_forward(x, o, out0, ob, g, s, up0, ub, down0, db),
        tokens_flat, mixed0, line(out_biases[0]), line(gains[0, 1]), line(shifts[0, 1]), line(up_biases[0]),
        line(down_biases[0]),
    )
    join.share(0, middle)
    qkv1.share(0, middle)
    out1.share(1, middle)
    up1.share(1, middle)
    down1.fetch(middle)
    entry, a1, packed1 = order.run(
        lambda m, s, jb, g, sh: join_qkv(m, s, join, jb, g, sh, qkv1),
        middle, skip_flat, line(join_shift), line(gains[1, 0]), line(shifts[1, 0]),
    )
    out1.share(0, a1)
    up1.share(0, a1)
    down1.share(1, a1)
    packed1 = packed1.reshape(3, items, seq_rows, width)
    mixed1, totals1 = order.run(lambda *x: attend(*x, items, seq_rows), packed1, lengths)
    mixed1 = mixed1.reshape(rows, width)
    down1.share(0, mixed1)
    m1, second1, hidden1, slope1, output = order.run(
        lambda x, o, ob, g, s, ub, db, k: feed_forward(x, o, out1, ob, g, s, up1, ub, down1, db, k),
        entry, mixed1, line(out_biases[1]), line(gains[1, 1]), line(shifts[1, 1]), line(up_biases[1]),
        line(down_biases[1]), keep,
    )

    term_down1 = Term(order, "down", 1, down_term, hidden1, dz1)
    term_down1.pass_narrow()
    du, dm, db, do, sums1, usum1 = order.run(
        lambda y, z, s, m, g: feed_forward_back(y, z, s, down1, up1, m, g, out1),
        dz1, dz1, slope1, m1, line(gains[1, 1]),
    )
    term_up1 = Term(order, "up", 1, up_term, second1, du)
    term_up1.pass_narrow()
    order.hold(term_down1.got)
    dpacked = order.run(
        lambda *x: attend_back(*x, items, seq_rows), packed1, do.reshape(items, seq_rows, width), totals1, lengths
    )
    flat_packed = dpacked.reshape(3, rows, width)
    term_qkv1 = Term(order, "qkv", 1, qkv_out_term, a1, flat_packed, mixed1, db)
    term_qkv1.pass_narrow()
    first = Reduce(order, [term_down1, term_up1])
    first.sum_rest()
    dentry, dmiddle, dz0, skip_grad, sums3 = order.run(
        lambda gp, x, g, dm: project_back(gp, qkv1, x, g, dm, join), flat_packed, entry, line(gains[1, 0]), dm
    )
    term_down0 = Term(order, "down", 0, down_term, hidden0, dz0)
    term_down0.stay()
    term_qkv1.pass_wide(2)
    term_down0.pass_narrow()
    term_join = Term(order, "join", 1, join_term, middle, skip_flat, dentry)
    term_join.pass_narrow()

    du, dm, db, do, sums0, usum0 = order.run(
        lambda y, z, s, m, g: feed_forward_back(y, z, s, down0, up0, m, g, out0),
        dmiddle, dz0, slope0, m0, line(gains[0, 1]),
    )
    term_up0 = Term(order, "up", 0, up_term, second0, du)
    term_up0.stay()
    term_down0.pass_wide(2)
    term_up0.pass_narrow()
    term_join.pass_wide(2)
    dpacked = order.run(
        lambda *x: attend_back(*x, items, seq_rows), packed0, do.reshape(items, seq_rows, width), totals0, lengths
    )
    second = Reduce(order, [term_qkv1, term_join], (2,))
    second.step()
    flat_packed = dpacked.reshape(3, rows, width)
    term_qkv0 = Term(order, "qkv", 0, qkv_out_term, a0, flat_packed, mixed0, db)
    term_qkv0.stay()
    term_up0.pass_wide(2)
    second.step()
    term_qkv0.pass_narrow()
    tokens_grad, sums2 = order.run(
        lambda gp, x, g, dm: project_back(gp, qkv0, x, g, dm), flat_packed, tokens_flat, line(gains[0, 0]), dm
    )
    fourth = Reduce(order, [term_qkv0])
    third = Reduce(order, [term_down0, term_up0], (2,))

    def norm_terms(place):
        return jnp.stack([jnp.stack([sums2[place], sums0[1 + place]]), jnp.stack([sums3[place], sums1[1 + place]])])

    minor = [
        norm_terms(0),
        norm_terms(1),
        jnp.stack([sums0[3], sums1[3]]),
        jnp.concatenate([usum0, usum1]),
        jnp.stack([sums0[0], sums1[0]]),
        sums3[2],
    ]
    split = [jnp.moveaxis(piece.reshape(piece.shape[:-1] + (shares, -1)), -2, 0) for piece in minor]
    minor_sum = jnp.concatenate([piece.reshape(shares, -1) for piece in split], axis=1)
    minor_stages = [("wide", mask) for mask in masks("wide")] + [("narrow", mask) for mask in masks("narrow")]
    minor_got = swap(minor_sum, *minor_stages[0])

    def minor_step():
        nonlocal minor_sum, minor_got
        if minor_stages:
            minor_stages.pop(0)
            minor_sum = order.run(lambda one, two: one + two, minor_sum, minor_got)
            if minor_stages:
                minor_got = swap(minor_sum, *minor_stages[0])

    done = {}
    second.step()
    third.step()
    minor_step()
    fourth.step()
    second.step()
    minor_step()
    third.step()
    second.step()
    fourth.step()
    minor_step()
    third.step()
    first.close()
    second.step()
    fourth.step()
    minor_step()
    third.step()
    first.finish(done)
    fourth.step()
    second.finish(done)
    minor_step()
    third.step()
    fourth.step()
    third.step()
    fourth.step()
    third.finish(done)
    fourth.step()
    for each in (second, third, fourth):
        while not each.closed:
            each.step()
    while minor_stages:
        minor_step()
    fourth.finish(done)

    owned = lax.dynamic_index_in_dim(minor_sum, me, 0, keepdims=False) * (1.0 / lax.axis_size("wide"))
    minor_sums, begin = [], 0
    for piece in split:
        end = begin + piece.size // shares
        minor_sums.append(owned[begin:end].reshape(piece.shape[1:]))
        begin = end
    return (
        output.reshape(tokens.shape),
        tokens_grad.reshape(tokens.shape),
        skip_grad.reshape(tokens.shape),
        minor_sums[0],
        minor_sums[1],
        done["qkv"][0],
        done["qkv"][1],
        minor_sums[2],
        done["up"][0],
        minor_sums[3],
        done["down"][0],
        minor_sums[4],
        done["join"][0][0],
        minor_sums[5],
    )


def solution(mesh):
    placed = (
        P(("wide", "narrow"), None, None),
        P(("wide", "narrow"), None, None),
        P(("wide", "narrow")),
        P(("wide", "narrow"), None, None),
        P(None, None, "narrow"),
        P(None, None, "narrow"),
        P(None, "narrow", None),
        P(None, "narrow", None),
        P(None, "narrow"),
        P(None, "narrow", None),
        P(None, "narrow"),
        P(None, "narrow", None),
        P(None, "narrow"),
        P("narrow", None),
        P("narrow"),
    )
    return jax.shard_map(
        on_device,
        mesh=mesh,
        in_specs=placed,
        out_specs=(
            P(("wide", "narrow"), None, None),
            P(("wide", "narrow"), None, None),
            P(("wide", "narrow"), None, None),
            P(None, None, "narrow"),
            P(None, None, "narrow"),
            P(None, "narrow", None),
            P(None, "narrow", None),
            P(None, "narrow"),
            P(None, "narrow", None),
            P(None, "narrow"),
            P(None, "narrow", None),
            P(None, "narrow"),
            P("narrow", None),
            P("narrow"),
        ),
        check_vma=False,
    )
```

```python
import copy

import jax
import jax.numpy as jnp
from jax import lax
from jax.experimental import pallas as pl
from jax.experimental.pallas import tpu as pltpu
from jax.sharding import PartitionSpec as P

HEAD_DIM = 64
PATCHES = 256
CAPTION = 77
PAIR = 2 * HEAD_DIM


epsilon = 1e-05
masked_score = -1e30
low = jnp.bfloat16
full = jnp.float32
ANY = pl.BlockSpec(memory_space=pl.ANY)
SCALARS = pl.BlockSpec(memory_space=pltpu.SMEM)


def dot(left, right, contract=(1, 0)):
    dims = (((contract[0],), (contract[1],)), ((), ()))
    return lax.dot_general(left, right, dims, preferred_element_type=full)


def normalize(values):
    centred = values - jnp.mean(values, axis=-1, keepdims=True)
    factor = lax.rsqrt(jnp.mean(centred * centred, axis=-1, keepdims=True) + epsilon)
    return centred * factor, factor


def normalize_back(upstream, normed, factor):
    return factor * (
        upstream
        - jnp.mean(upstream, axis=-1, keepdims=True)
        - normed * jnp.mean(upstream * normed, axis=-1, keepdims=True)
    )


def column_sum(values):
    return jnp.sum(values.astype(full), axis=0, keepdims=True)


def whole(shape):
    return pl.BlockSpec(shape, lambda *grid: (0,) * len(shape))


def cost(micros):
    return pl.CostEstimate(flops=int(micros * 3 * 10**8), bytes_accessed=0, transcendentals=0)


def call(body, grid, ins, outs, name, micros, scratch=(), limit=56):
    return pl.pallas_call(
        body,
        grid=grid,
        in_specs=[spec for _, spec in ins],
        out_specs=[spec for _, _, spec in outs],
        out_shape=[jax.ShapeDtypeStruct(shape, kind) for shape, kind, _ in outs],
        scratch_shapes=list(scratch),
        name=name,
        cost_estimate=cost(micros),
        compiler_params=pltpu.CompilerParams(vmem_limit_bytes=limit * 2**20),
    )(*[array for array, _ in ins])


class Weight:
    def __init__(self, array, layer, width, spots):
        self.array, self.layer, self.width, self.spots = array, layer, width, spots
        self.rows, self.columns = array.shape[-2:]
        self.shares = lax.axis_size("narrow")
        self.blocks = self.columns // width
        self.total = self.rows * self.shares
        self.sharing = masks("wide")[:2]
        while self.rows % (16 << len(self.sharing)):
            self.sharing.pop()
        self.count = 1 << len(self.sharing)
        self.length = self.rows // self.count

    def fetch(self, *earlier):
        array = after(self.array, *earlier)
        place = (lax.axis_index("wide") & (self.count - 1)) * self.length
        lead = () if self.layer is None else (self.layer,)
        sizes = (1,) * len(lead) + (self.length, self.columns)
        self.sent = lax.dynamic_slice(array, lead + (place, 0), sizes).reshape(1, self.length, self.columns)
        held = self.sent
        for mask in masks("narrow"):
            held = jnp.concatenate([held, swap(held, "narrow", mask)])
        self.pieces = {0: held[1:]}

    def share(self, which, *earlier):
        if which < len(self.sharing):
            mask = self.sharing[which]
            got = {key ^ mask: swap(after(piece, *earlier), "wide", mask) for key, piece in self.pieces.items()}
            self.pieces.update(got)

    def got(self):
        return list(self.pieces.values())

    def arrays(self):
        return [self.array] + list(self.pieces.values())

    def scratch(self):
        copies = 1 + len(self.pieces) * (self.shares - 1)
        return [pltpu.VMEM((self.blocks, self.total, self.width), low), pltpu.SemaphoreType.DMA((self.blocks, copies))]

    def copies(self, spots, refs, held, signals, block):
        own, pieces = refs[0], refs[1:]
        columns = pl.ds(block * self.width, self.width)
        me = spots[0]
        own = own if self.layer is None else own.at[self.layer]
        begin = pl.multiple_of(me * self.rows, 16)
        found = [(own.at[:, columns], begin, self.rows)]
        for key, piece in zip(self.pieces, pieces):
            for offset in range(1, self.shares):
                begin = (me ^ offset) * self.rows + ((spots[1] & (self.count - 1)) ^ key) * self.length
                found.append((piece.at[offset - 1, :, columns], pl.multiple_of(begin, 16), self.length))
        return [
            pltpu.make_async_copy(source, held.at[block, pl.ds(begin, length)], signals.at[block, place])
            for place, (source, begin, length) in enumerate(found)
        ]

    def start(self, *refs):
        for block in range(self.blocks):
            for copy in self.copies(*refs, block):
                copy.start()

    def wait(self, *refs, block=0):
        for copy in self.copies(*refs, block):
            copy.wait()


def weighted(body, weights, grid, ins, outs, name, micros, scratch=()):
    spots = weights[0].spots
    operands = [(spots, SCALARS)] + [(array, ANY) for weight in weights for array in weight.arrays()]
    counts = [len(weight.arrays()) for weight in weights]
    extra = [piece for weight in weights for piece in weight.scratch()]

    def wrapped(*refs):
        spots_ref, rest = refs[0], list(refs[1:])
        sources = []
        for count in counts:
            sources.append(rest[:count])
            rest = rest[count:]
        spare = rest[len(rest) - len(extra) :]
        rest = rest[: len(rest) - len(extra)]
        handles = []
        for place, weight in enumerate(weights):
            held, signals = spare[2 * place : 2 * place + 2]
            refs_of = (spots_ref, sources[place], held, signals)
            handles.append((weight, refs_of, held))

        @pl.when(pl.program_id(0) == 0)
        def _():
            for weight, refs_of, _ in handles:
                weight.start(*refs_of)

        def ready(place, block=0):
            weight, refs_of, held = handles[place]
            weight.wait(*refs_of, block=block)

        body(ready, [held for _, _, held in handles], *rest)

    return call(wrapped, grid, operands + ins, outs, name, micros, list(scratch) + extra)


def pack_small(*small):
    part = small[0].shape[-1]
    counts = [piece.size // part for piece in small]

    def body(*refs):
        row = 0
        for ref in refs[:-1]:
            values = ref[...].reshape(-1, ref.shape[-1])
            for each in range(values.shape[0]):
                for begin in range(0, values.shape[1], part):
                    refs[-1][row : row + 1] = values[each : each + 1, begin : begin + part].astype(full)
                    row += 1
        refs[-1][row:] = jnp.zeros((refs[-1].shape[0] - row, part), full)

    flat = [piece.reshape((1,) * (2 - piece.ndim) + piece.shape) for piece in small]
    rows = -(-sum(counts) // 16) * 16
    out = ((rows, part), full, whole((rows, part)))
    return call(body, (1,), [(piece, whole(piece.shape)) for piece in flat], [out], "pack_small", 1)[0].astype(low)


def unpack_small(parts, me, small, width):
    shares, _, part = parts.shape
    lines = [(piece.size // piece.shape[-1], piece.shape[-1] // part) for piece in small]
    total = sum(count * many for count, many in lines)
    rows = -(-total // 8) * 8

    def body(me_ref, parts_ref, out_ref):
        values = parts_ref[...].astype(full)
        for mine in range(shares):

            @pl.when(me_ref[0] == mine)
            def _():
                for owner in range(shares):
                    source, target = 0, 0
                    for count, many in lines:
                        for each in range(count):
                            for piece in range(many):
                                at = owner * many * part + piece * part
                                row, column = target + at // width, at % width
                                line = values[owner ^ mine, source : source + 1]
                                out_ref[row : row + 1, column : column + part] = line
                                source += 1
                            target += many
        if rows > total:
            out_ref[total:] = jnp.zeros((rows - total, width), full)

    ins = [(parts, pl.BlockSpec(parts.shape, lambda g, me: (0, 0, 0)))]
    out = ((rows, width), full, pl.BlockSpec((rows, width), lambda g, me: (0, 0)))
    return picked(body, me, (1,), ins, [out], "unpack_small", 1)[0]


def project_qkv(inputs, gain, shift, weight):
    rows, width = inputs.shape

    def body(ready, held, x_ref, gain_ref, shift_ref, a_ref, out_ref):
        step = pl.program_id(0)

        @pl.when(step == 0)
        def _():
            normed, _ = normalize(x_ref[...].astype(full))
            a_ref[...] = (normed * gain_ref[...] + shift_ref[...]).astype(low)

        ready(0, step)
        scale = jnp.where(step == 0, HEAD_DIM ** (-0.5), 1.0)
        out_ref[0] = (dot(a_ref[...], held[0][step]).astype(low).astype(full) * scale).astype(low)

    return weighted(
        body,
        [weight],
        (3,),
        [
            (inputs, whole((rows, width))),
            (gain, whole((1, width))),
            (shift, whole((1, width))),
        ],
        [
            ((rows, width), low, whole((rows, width))),
            ((3, rows, width), low, pl.BlockSpec((1, rows, width), lambda j: (j, 0, 0))),
        ],
        "project_qkv",
        7,
    )


def join_qkv(middle, skip, join_weight, join_shift, gain, shift, weight):
    rows, width = middle.shape

    def body(ready, held, m_ref, s_ref, jb_ref, gain_ref, shift_ref, e_ref, a_ref, out_ref):
        step = pl.program_id(0)

        @pl.when(step == 0)
        def _():
            ready(0)
            entry = dot(m_ref[...], held[0][0, :width]) + dot(s_ref[...], held[0][0, width:]) + jb_ref[...]
            e_ref[...] = entry
            normed, _ = normalize(entry)
            a_ref[...] = (normed * gain_ref[...] + shift_ref[...]).astype(low)

        ready(1, step)
        scale = jnp.where(step == 0, HEAD_DIM ** (-0.5), 1.0)
        out_ref[0] = (dot(a_ref[...], held[1][step]).astype(low).astype(full) * scale).astype(low)

    return weighted(
        body,
        [join_weight, weight],
        (3,),
        [
            (middle, whole((rows, width))),
            (skip, whole((rows, width))),
            (join_shift, whole((1, width))),
            (gain, whole((1, width))),
            (shift, whole((1, width))),
        ],
        [
            ((rows, width), full, whole((rows, width))),
            ((rows, width), low, whole((rows, width))),
            ((3, rows, width), low, pl.BlockSpec((1, rows, width), lambda j: (j, 0, 0))),
        ],
        "join_qkv",
        11,
    )


def head_masks(seq_rows):
    lane = lax.broadcasted_iota(jnp.int32, (seq_rows, PAIR), 1)
    return [lane < HEAD_DIM, lane >= HEAD_DIM]


def attend(packed, lengths, items, seq_rows):
    width = packed.shape[-1]
    pairs = width // PAIR

    def body(length_ref, q_ref, k_ref, v_ref, out_ref, total_ref):
        length = length_ref[pl.program_id(0)]
        queries, keys, values = q_ref[0, 0], k_ref[0, 0], v_ref[0, 0]
        counts = lax.broadcasted_iota(jnp.int32, (seq_rows, seq_rows), 0) < length
        mixed = jnp.zeros((PAIR, seq_rows), full)
        for head, lanes in enumerate(head_masks(seq_rows)):
            scores = dot(keys, jnp.where(lanes, queries, 0), (1, 1))
            scores = jnp.where(counts, scores, masked_score)
            largest = jnp.max(scores, axis=0, keepdims=True)
            weights = jnp.exp(scores - largest)
            total = jnp.sum(weights, axis=0, keepdims=True)
            part = dot(jnp.where(lanes, values, 0), weights.astype(low), (0, 0))
            mixed += part * (1.0 / total)
            total_ref[0, 0, head : head + 1] = largest + jnp.log(total)
        out_ref[0] = mixed.T.astype(low)

    def block(which):
        return pl.BlockSpec((1, 1, seq_rows, PAIR), lambda n, h: (which, n, 0, h))

    return call(
        body,
        (items, pairs),
        [
            (lengths, SCALARS),
            (packed, block(0)),
            (packed, block(1)),
            (packed, block(2)),
        ],
        [
            ((items, seq_rows, width), low, pl.BlockSpec((1, seq_rows, PAIR), lambda n, h: (n, 0, h))),
            ((items, pairs, 8, seq_rows), full, pl.BlockSpec((1, 1, 8, seq_rows), lambda n, h: (n, h, 0, 0))),
        ],
        "attend",
        13,
    )


def attend_back(packed, grad_mixed, totals, lengths, items, seq_rows):
    width = packed.shape[-1]
    pairs = width // PAIR

    def body(length_ref, q_ref, k_ref, v_ref, g_ref, total_ref, out_ref):
        length = length_ref[pl.program_id(0)]
        queries, keys, values, upstream = q_ref[0, 0], k_ref[0, 0], v_ref[0, 0], g_ref[0]
        counts = lax.broadcasted_iota(jnp.int32, (seq_rows, seq_rows), 0) < length
        grad_queries = jnp.zeros((PAIR, seq_rows), full)
        grad_keys = jnp.zeros((seq_rows, PAIR), full)
        grad_values = jnp.zeros((seq_rows, PAIR), full)
        for head, lanes in enumerate(head_masks(seq_rows)):
            own_queries = jnp.where(lanes, queries, 0)
            own_upstream = jnp.where(lanes, upstream, 0)
            scores = dot(keys, own_queries, (1, 1))
            shifted = jnp.where(counts, scores, masked_score) - total_ref[0, 0, head : head + 1]
            probs = jnp.exp(shifted)
            grad_probs = dot(values, own_upstream, (1, 1))
            centre = jnp.sum(grad_probs * probs, axis=0, keepdims=True)
            grad_scores = (probs * (grad_probs - centre)).astype(low)
            grad_values += dot(probs.astype(low), own_upstream)
            grad_keys += dot(grad_scores, own_queries)
            grad_queries += dot(jnp.where(lanes, keys, 0), grad_scores, (0, 0))
        out_ref[0, 0] = (grad_queries.T * HEAD_DIM ** (-0.5)).astype(low)
        out_ref[1, 0] = grad_keys.astype(low)
        out_ref[2, 0] = grad_values.astype(low)

    def block(which):
        return pl.BlockSpec((1, 1, seq_rows, PAIR), lambda n, h: (which, n, 0, h))

    return call(
        body,
        (items, pairs),
        [
            (lengths, SCALARS),
            (packed, block(0)),
            (packed, block(1)),
            (packed, block(2)),
            (grad_mixed, pl.BlockSpec((1, seq_rows, PAIR), lambda n, h: (n, 0, h))),
            (totals, pl.BlockSpec((1, 1, 8, seq_rows), lambda n, h: (n, h, 0, 0))),
        ],
        [
            ((3, items, seq_rows, width), low, pl.BlockSpec((3, 1, seq_rows, PAIR), lambda n, h: (0, n, 0, h))),
        ],
        "attend_back",
        17,
    )[0]


def gelu_parts(before):
    decay = jnp.exp(before * before * -0.5)
    inverse = pl.reciprocal(1.0 + (0.3275911 * 0.5**0.5) * jnp.abs(before), approx=False)
    series = 1.061405429 * 0.5
    for term in (-1.453152027, 1.421413741, -0.284496736, 0.254829592):
        series = series * inverse + term * 0.5
    below = series * inverse * decay
    share = jnp.where(before >= 0, 1.0 - below, below)
    return before * share, share + before * decay * 0.3989422804014327


def feed_forward(inputs, mixed, out_weight, out_bias, gain, shift, up_weight, up_bias, down_weight, down_bias, keep=None):
    rows, width = inputs.shape
    steps = up_weight.blocks
    hidden = steps * width

    def body(ready, held, x_ref, o_ref, ob_ref, gain_ref, shift_ref, ub_ref, db_ref, *rest):
        m_ref, a_ref, g_ref, s_ref, y_ref, total = rest[-6:]
        step = pl.program_id(0)

        @pl.when(step == 0)
        def _():
            ready(0)
            middle = x_ref[...].astype(full) + dot(o_ref[...], held[0][0]) + ob_ref[...]
            m_ref[...] = middle
            normed, _ = normalize(middle)
            a_ref[...] = (normed * gain_ref[...] + shift_ref[...]).astype(low)
            total[...] = middle + db_ref[...]

        ready(1, step)
        before = dot(a_ref[...], held[1][step]) + ub_ref[...]
        value, slope = gelu_parts(before)
        g_ref[...] = value.astype(low)
        s_ref[...] = slope.astype(low)

        @pl.when(step == 0)
        def _():
            ready(2)

        total[...] += dot(g_ref[...], held[2][0, pl.ds(pl.multiple_of(step * width, width), width)])

        @pl.when(step == steps - 1)
        def _():
            value = total[...]
            if keep is not None:
                value = jnp.where(rest[0][...] > 0, value, 0.0)
            y_ref[...] = value.astype(low)

    return weighted(
        body,
        [out_weight, up_weight, down_weight],
        (steps,),
        [
            (inputs, whole((rows, width))),
            (mixed, whole((rows, width))),
            (out_bias, whole((1, width))),
            (gain, whole((1, width))),
            (shift, whole((1, width))),
            (up_bias, pl.BlockSpec((1, width), lambda j: (0, j))),
            (down_bias, whole((1, width))),
        ]
        + ([] if keep is None else [(keep, whole((rows, 1)))]),
        [
            ((rows, width), full, whole((rows, width))),
            ((rows, width), low, whole((rows, width))),
            ((rows, hidden), low, pl.BlockSpec((rows, width), lambda j: (0, j))),
            ((rows, hidden), low, pl.BlockSpec((rows, width), lambda j: (0, j))),
            ((rows, width), low, whole((rows, width))),
        ],
        "feed_forward",
        23,
        scratch=[pltpu.VMEM((rows, width), full)],
    )


def feed_forward_back(upstream, rounded, slope, down_weight, up_weight, middle, gain, out_weight):
    rows, width = upstream.shape
    steps = up_weight.blocks
    hidden = steps * width

    def body(ready, held, y_ref, dz_ref, s_ref, m_ref, gain_ref, du_ref, dm_ref, db_ref, do_ref, sums_ref, total):
        step = pl.program_id(0)

        @pl.when(step == 0)
        def _():
            sums_ref[0:1] = column_sum(dz_ref[...])
            total[...] = jnp.zeros_like(total)
            ready(0)

        down = held[0][0, pl.ds(pl.multiple_of(step * width, width), width)]
        grad = (dot(dz_ref[...], down, (1, 1)) * s_ref[...].astype(full)).astype(low)
        du_ref[...] = grad
        sums_ref[pl.ds(4 + step, 1)] = column_sum(grad)
        ready(1, step)
        total[...] += dot(grad, held[1][step], (1, 1))

        @pl.when(step == steps - 1)
        def _():
            grad_second = total[...]
            normed, factor = normalize(m_ref[...])
            sums_ref[1:2] = column_sum(grad_second * normed)
            sums_ref[2:3] = column_sum(grad_second)
            grad_middle = y_ref[...].astype(full) + normalize_back(grad_second * gain_ref[...], normed, factor)
            dm_ref[...] = grad_middle
            branch = grad_middle.astype(low)
            db_ref[...] = branch
            sums_ref[3:4] = column_sum(branch)
            ready(2)
            do_ref[...] = dot(branch, held[2][0], (1, 1)).astype(low)

    return weighted(
        body,
        [down_weight, up_weight, out_weight],
        (steps,),
        [
            (upstream, whole((rows, width))),
            (rounded, whole((rows, width))),
            (slope, pl.BlockSpec((rows, width), lambda j: (0, j))),
            (middle, whole((rows, width))),
            (gain, whole((1, width))),
        ],
        [
            ((rows, hidden), low, pl.BlockSpec((rows, width), lambda j: (0, j))),
            ((rows, width), full, whole((rows, width))),
            ((rows, width), low, whole((rows, width))),
            ((rows, width), low, whole((rows, width))),
            ((4 + steps, width), full, whole((4 + steps, width))),
        ],
        "feed_forward_back",
        21,
        scratch=[pltpu.VMEM((rows, width), full)],
    )


def project_back(grad_packed, weight, inputs, gain, grad_middle, join_weight=None):
    rows, width = inputs.shape
    joined = join_weight is not None

    def body(ready, held, g_ref, x_ref, gain_ref, dm_ref, *rest):
        if joined:
            de_ref, dx_ref, dz_ref, skip_ref, sums_ref, total = rest
        else:
            dx_ref, sums_ref, total = rest
        step = pl.program_id(0)

        @pl.when(step == 0)
        def _():
            total[...] = jnp.zeros_like(total)

        ready(0, step)
        total[...] += dot(g_ref[0], held[0][step], (1, 1))

        @pl.when(step == 2)
        def _():
            grad_first = total[...]
            normed, factor = normalize(x_ref[...].astype(full))
            sums_ref[0:1] = column_sum(grad_first * normed)
            sums_ref[1:2] = column_sum(grad_first)
            grad = dm_ref[...] + normalize_back(grad_first * gain_ref[...], normed, factor)
            if joined:
                entry = grad.astype(low)
                de_ref[...] = entry
                sums_ref[2:3] = column_sum(entry)
                ready(1)
                grad = dot(entry, held[1][0, :width], (1, 1))
                dx_ref[...] = grad
                dz_ref[...] = grad.astype(low)
                skip_ref[...] = dot(entry, held[1][0, width:], (1, 1))
            else:
                dx_ref[...] = grad

    ins = [
        (grad_packed, pl.BlockSpec((1, rows, width), lambda j: (j, 0, 0))),
        (inputs, whole((rows, width))),
        (gain, whole((1, width))),
        (grad_middle, whole((rows, width))),
    ]
    outs = [((rows, width), full, whole((rows, width))), ((8, width), full, whole((8, width)))]
    if joined:
        rounded = ((rows, width), low, whole((rows, width)))
        outs = [rounded, outs[0], rounded, outs[0], outs[1]]
    return weighted(
        body,
        [weight] + ([join_weight] if joined else []),
        (3,),
        ins,
        outs,
        "project_back",
        13 if joined else 9,
        scratch=[pltpu.VMEM((rows, width), full)],
    )


def picked(body, which, grid, ins, outs, name, micros, aliases=None):
    return pl.pallas_call(
        body,
        grid_spec=pltpu.PrefetchScalarGridSpec(
            num_scalar_prefetch=1,
            grid=grid,
            in_specs=[spec for _, spec in ins],
            out_specs=[spec for _, _, spec in outs],
        ),
        out_shape=[jax.ShapeDtypeStruct(shape, kind) for shape, kind, _ in outs],
        name=name,
        input_output_aliases={place + 1: out for place, out in (aliases or {}).items()},
        cost_estimate=cost(micros),
        compiler_params=pltpu.CompilerParams(vmem_limit_bytes=48 * 2**20),
    )(which, *[array for array, _ in ins])


def quarters(rows, width, narrow_rows):
    shape = (lax.axis_size("narrow") // 2 * narrow_rows, width)
    return [(shape, low, pl.BlockSpec(shape, lambda g, core: (0, 0)))] * 4


def up_term(left, right, core):
    rows, width = left.shape
    part = width // lax.axis_size("narrow")
    half = width // 2

    def body(core_ref, l_ref, r_ref, *outs):
        value = dot(l_ref[...], r_ref[...], (0, 0)).astype(low)
        for block in range(2):

            @pl.when(pl.program_id(0) == block)
            def _():
                outs[block][...] = value[:half]
                outs[2 + block][...] = value[half:]

    return picked(
        body,
        core,
        (2,),
        [
            (left, pl.BlockSpec((rows, width), lambda g, core: (0, 0))),
            (right, pl.BlockSpec((rows, width), lambda g, core: (0, core[0] * 2 + g))),
        ],
        quarters(rows, width, part),
        "up_term",
        3.5,
    )


def qkv_out_term(first, packed, mixed, branch, core):
    rows, width = first.shape
    part = width // lax.axis_size("narrow")
    half = width // 2

    def body(core_ref, l_ref, r_ref, o_ref, b_ref, *outs):
        step = pl.program_id(0)
        last = core_ref[0] * 2 + step == 3

        def put(block, value):
            outs[block][...] = value[:half]
            outs[2 + block][...] = value[half:]

        @pl.when(last)
        def _():
            put(1, dot(o_ref[...], b_ref[...], (0, 0)).astype(low))

        @pl.when(jnp.logical_not(last))
        def _():
            value = dot(l_ref[...], r_ref[0], (0, 0)).astype(low)
            for block in range(2):

                @pl.when(step == block)
                def _():
                    put(block, value)

    flat = pl.BlockSpec((rows, width), lambda g, core: (0, 0))
    return picked(
        body,
        core,
        (2,),
        [
            (first, flat),
            (packed, pl.BlockSpec((1, rows, width), lambda g, core: (jnp.minimum(core[0] * 2 + g, 2), 0, 0))),
            (mixed, flat),
            (branch, flat),
        ],
        quarters(rows, width, part),
        "qkv_out_term",
        3.5,
    )


def down_term(left, right, core):
    rows, width = right.shape
    shares = lax.axis_size("narrow")
    part = left.shape[1] // (2 * shares)
    direct = part == width
    if not direct:
        left = left.reshape(rows, shares, 2, 2, part // 2)
        left = lax.dynamic_index_in_dim(left, core[0], 2, keepdims=False)
        left = left.reshape(rows, 2, shares // 2, 2, part // 2).swapaxes(2, 3).reshape(rows, 2 * width)
    half = width // 2

    def body(core_ref, l_ref, r_ref, *outs):
        value = dot(l_ref[...], r_ref[...], (0, 0)).astype(low)
        for owner in range(2):

            @pl.when(pl.program_id(0) == owner)
            def _():
                outs[2 * owner][...] = value[:half]
                outs[2 * owner + 1][...] = value[half:]

    return picked(
        body,
        core,
        (2,),
        [
            (left, pl.BlockSpec((rows, width), lambda g, core: (0, g * 2 + core[0] if direct else g))),
            (right, pl.BlockSpec((rows, width), lambda g, core: (0, 0))),
        ],
        quarters(rows, width, part // 2),
        "down_term",
        3.5,
    )


def join_term(middle, skip, right, core):
    rows, width = right.shape
    shares = lax.axis_size("narrow")
    part = width // shares
    half = width // 2
    if part != half:
        left = jnp.concatenate([middle, skip], axis=1).reshape(rows, shares, 2, 2, part // 2)
        left = lax.dynamic_index_in_dim(left, core[0], 2, keepdims=False)
        left = left.reshape(rows, 2, shares // 2, 2, part // 2).swapaxes(2, 3).reshape(rows, width)
        middle, skip = left[:, :half], left[:, half:]

    def body(core_ref, m_ref, s_ref, r_ref, *outs):
        for owner, left_ref in enumerate((m_ref, s_ref)):
            value = dot(left_ref[...], r_ref[...], (0, 0)).astype(low)
            outs[2 * owner][...] = value[: half // 2]
            outs[2 * owner + 1][...] = value[half // 2 :]

    side = pl.BlockSpec((rows, half), lambda g, core: (0, core[0] if part == half else 0))
    return picked(
        body,
        core,
        (1,),
        [(middle, side), (skip, side), (right, pl.BlockSpec((rows, width), lambda g, core: (0, 0)))],
        quarters(rows, width, part // 2),
        "join_term",
        2,
    )


def cross(bit, *pieces):
    kept, got = pieces[: len(pieces) // 2], pieces[len(pieces) // 2 :]
    rows, columns = kept[0].shape
    blocks = len(kept) // 2
    steps = 2 if rows % 32 == 0 else 1

    def body(bit_ref, *refs):
        sent_ref, left_ref = refs[-2:]

        def put(target, owner):
            for block in range(blocks):
                place = owner * blocks + block
                one, two = refs[place], refs[2 * blocks + place]
                target[block] = (one[...].astype(full) + two[...].astype(full)).astype(low)

        for mine in range(2):

            @pl.when(bit_ref[0] == mine)
            def _():
                put(sent_ref, 1 - mine)
                put(left_ref, mine)

    ins = [(piece, pl.BlockSpec((rows // steps, columns), lambda g, bit: (g, 0))) for piece in kept + got]
    out = ((blocks, rows, columns), low, pl.BlockSpec((blocks, rows // steps, columns), lambda g, bit: (0, g, 0)))
    return picked(body, bit, (steps,), ins, [out, out], "cross", 2)


def add_halve(bit, *pairs):
    lead, columns = pairs[0].shape[0], pairs[0].shape[-1]
    sizes = [pair.shape[2] for pair in pairs[::2]]
    total = sum(sizes)
    steps = 2 if len(sizes) == 1 and total % 32 == 0 and total >= 256 else 1

    def body(bit_ref, *refs):
        mine = bit_ref[0]
        for target, place in ((refs[-2], 1 - mine), (refs[-1], mine)):
            begin = 0
            for kept_ref, got_ref in zip(refs[:-2:2], refs[1:-2:2]):
                length = kept_ref.shape[2]
                for each in range(lead):
                    value = kept_ref[each, place].astype(full) + got_ref[each, place].astype(full)
                    target[each, begin : begin + length] = value.astype(low)
                begin += length

    ins = [
        (pair, pl.BlockSpec((lead, 2, pair.shape[2] // steps, columns), lambda g, bit: (0, 0, g, 0)))
        for pair in pairs
    ]
    out = (
        (lead, total, columns),
        low,
        pl.BlockSpec((lead, total // steps, columns), lambda g, bit: (0, g, 0)),
    )
    return picked(body, bit, (steps,), ins, [out, out], "add_halve", 2)


def add(one, two):
    return (one.astype(full) + two.astype(full)).astype(low)


def pair_up(own, got, bit):
    rows, columns = own.shape

    def body(bit_ref, own_ref, got_ref, out_ref):
        mine = bit_ref[0]
        out_ref[mine] = own_ref[...]
        out_ref[1 - mine] = got_ref[...]

    flat = pl.BlockSpec((rows, columns), lambda g, bit: (0, 0))
    out = ((2, rows, columns), low, pl.BlockSpec((2, rows, columns), lambda g, bit: (0, 0, 0)))
    return picked(body, bit, (1,), [(own, flat), (got, flat)], [out], "pair_up", 1)[0]


def finish(kind, half, own, got, begin, length, core, layer, targets):
    pieces, _, columns = own.shape
    scale = 1.0 / lax.axis_size("wide")
    aliases = {place + 2: place for place in range(len(targets))}
    source = pl.BlockSpec((pieces, length, columns), lambda g, core: (0, begin // length, 0))
    ins = [(own, source), (got, source)] + [(target, ANY) for target in targets]
    rows = pieces * length

    def chosen(core_ref, which, own_ref, got_ref, place=None):
        sides = [own_ref, got_ref]
        if place is None:
            values = [side[...].reshape(pieces * length, columns) for side in sides]
        else:
            if pieces == 1:
                near = (0, pl.ds(place * (length // 2), length // 2))
            else:
                near = (pl.ds(place * (pieces // 2), pieces // 2),)
            values = [side[near].reshape(pieces * length // 2, columns) for side in sides]
        return jnp.where(core_ref[0] == which, values[0], values[1]).astype(full) * scale

    if kind in ("down", "join"):

        def body(core_ref, own_ref, got_ref, *rest):
            rest[-1][0] = chosen(core_ref, pl.program_id(0), own_ref, got_ref)

        place = layer if kind == "down" else 0
        shape = (2 if kind == "down" else 1, 2 * rows, columns)
        out = (shape, full, pl.BlockSpec((1, rows, columns), lambda g, core: (place, g, 0)))
        return picked(body, core, (2,), ins, [out], "finish_rows", 3, aliases)
    steps = 4 if half is None else 2
    rows = rows // 2 if half is None else rows

    def block(step):
        return step if half is None else 2 * step + half

    def values_of(core_ref, own_ref, got_ref):
        step = pl.program_id(0)
        if half is None:
            return chosen(core_ref, step // 2, own_ref, got_ref, step % 2)
        return chosen(core_ref, step, own_ref, got_ref)

    def body(core_ref, own_ref, got_ref, *rest):
        values = values_of(core_ref, own_ref, got_ref)
        if kind == "up":
            rest[-1][0] = values
            return
        last = block(pl.program_id(0)) == 3

        @pl.when(jnp.logical_not(last))
        def _():
            rest[-2][0] = values

        @pl.when(last)
        def _():
            rest[-1][0] = values

    if kind == "up":
        outs = [((2, rows, 4 * columns), full, pl.BlockSpec((1, rows, columns), lambda g, core: (layer, 0, block(g))))]
        return picked(body, core, (steps,), ins, outs, "finish_columns", 3, aliases)
    outs = [
        (
            (2, rows, 3 * columns),
            full,
            pl.BlockSpec((1, rows, columns), lambda g, core: (layer, 0, jnp.minimum(block(g), 2))),
        ),
        ((2, rows, columns), full, pl.BlockSpec((1, rows, columns), lambda g, core: (layer, 0, 0))),
    ]
    return picked(body, core, (steps,), ins, outs, "finish_qkv_out", 3, aliases)


def small_gradients(total, me, width, shares, blocks):
    part = width // shares
    scale = 1.0 / lax.axis_size("wide")

    def body(me_ref, total_ref, gains_ref, shifts_ref, out_ref, up_ref, down_ref, join_ref):
        values = total_ref[...] * scale
        back = [values[0:8], values[8:16]]
        ahead = [values[16 : 20 + blocks], values[20 + blocks : 24 + 2 * blocks]]
        for place in range(shares):

            @pl.when(me_ref[0] == place)
            def _():
                columns = slice(place * part, place * part + part)
                for layer in range(2):
                    for row, target in ((0, gains_ref), (1, shifts_ref)):
                        target[layer, 0:1] = back[layer][row : row + 1, columns]
                        target[layer, 1:2] = ahead[layer][row + 1 : row + 2, columns]
                    out_ref[layer : layer + 1] = ahead[layer][3:4, columns]
                    down_ref[layer : layer + 1] = ahead[layer][0:1, columns]
                    begin = place * part * blocks
                    while begin < (place + 1) * part * blocks:
                        row, column = begin // width, begin % width
                        length = min(width - column, (place + 1) * part * blocks - begin)
                        at = begin - place * part * blocks
                        piece = ahead[layer][4 + row : 5 + row, column : column + length]
                        up_ref[layer : layer + 1, at : at + length] = piece
                        begin += length
                join_ref[...] = back[1][2:3, columns]

    shapes = [(2, 2, part), (2, 2, part), (2, part), (2, part * blocks), (2, part), (1, part)]
    outs = [(shape, full, pl.BlockSpec(shape, lambda g, me, n=len(shape): (0,) * n)) for shape in shapes]
    ins = [(total, pl.BlockSpec(total.shape, lambda g, me: (0, 0)))]
    return picked(body, me, (1,), ins, outs, "small_gradients", 1)


def after(value, *earlier):
    return lax.optimization_barrier((value,) + earlier)[0] if earlier else value


def swap(values, axis, mask):
    size = lax.axis_size(axis)
    return lax.ppermute(values, axis, [(source, source ^ mask) for source in range(size)])


def masks(axis):
    return [1 << bit for bit in range(lax.axis_size(axis).bit_length() - 1)]


class Order:
    def __init__(self):
        self.last = ()

    def run(self, function, *arrays):
        held = lax.optimization_barrier(tuple(arrays) + self.last)[: len(arrays)]
        out = function(*held)
        self.last = (jax.tree.leaves(out)[0],)
        return out

    def hold(self, *arrays):
        self.last += arrays


def place_bit(axis, mask):
    return ((lax.axis_index(axis) & mask) // mask).astype(jnp.int32).reshape(1)


class Term:
    def __init__(self, order, kind, layer, function, *arrays):
        self.order, self.kind, self.layer, self.half = order, kind, layer, None
        self.core = place_bit("wide", 1)
        sent = order.run(lambda *x: function(*x, 1 - self.core), *arrays)
        self.got = [swap(each, "wide", 1) for each in sent]
        self.columns = sent[0].shape[-1]
        self.keep = lambda: order.run(lambda *x: function(*x, self.core), *arrays)

    def stay(self):
        self.kept, self.keep = self.keep(), None

    def part(self, half):
        other = copy.copy(self)
        other.kept, other.got, other.half = self.kept[half::2], self.got[half::2], half
        return other

    def pass_narrow(self):
        stages = list(reversed(masks("narrow")))
        if isinstance(self.kept, (list, tuple)):
            bit = place_bit("narrow", stages[0])
            blocks = len(self.kept) // 2
            sent, self.kept = self.order.run(lambda *x: cross(bit, *x), *self.kept, *self.got)
            self.got = swap(sent, "narrow", stages.pop(0))
        else:
            blocks = 1
        for mask in stages:
            pairs = [(self.kept, self.got)]
            self.kept, self.got = halve(self.order, "narrow", mask, blocks, pairs, self.columns)

    def pass_wide(self, mask):
        pairs = list(zip(self.kept, self.got)) if isinstance(self.kept, (list, tuple)) else [(self.kept, self.got)]
        self.kept, self.got = halve(self.order, "wide", mask, 1, pairs, self.columns)

    def add_up(self):
        return self.order.run(add, self.kept, self.got).reshape(1, -1, self.columns)

    def finish(self, done, own, got, begin, length):
        targets = done.get(self.kind, ())

        def last(own, got, core, *targets):
            return finish(self.kind, self.half, own, got, begin, length, core, self.layer, targets)

        done[self.kind] = self.order.run(last, own, got, self.core, *targets)


def halve(order, axis, mask, lead, pairs, columns):
    shaped = [array.reshape(lead, 2, -1, columns) for pair in pairs for array in pair]
    bit = place_bit(axis, mask)
    sent, kept = order.run(lambda *x: add_halve(bit, *x), *shaped)
    return kept, swap(sent, axis, mask)


class Reduce:
    def __init__(self, order, terms, passed=()):
        self.order, self.terms = order, terms
        self.down = [mask for mask in masks("wide")[1:] if mask not in passed]
        self.up = list(reversed(passed))
        self.pieces, self.columns = 2 ** len(passed), terms[0].columns
        self.parts = [(term.kept, term.got) for term in terms]
        self.lengths, self.first = [each.size // self.columns for each, _ in self.parts], True
        self.joining, self.closed = None, False

    def step(self):
        if self.closed:
            return
        if self.down:
            mask = self.down.pop(0)
            rows = [kept.size // self.columns for kept, _ in self.parts]
            even = all(each % 32 == 0 for each in rows)
            if self.first and even:
                self.pieces, self.lengths = 2 * self.pieces, [each // 2 for each in rows]
            self.first = False
            if even:
                self.up.insert(0, mask)
                self.parts = [halve(self.order, "wide", mask, 1, self.parts, self.columns)]
            else:
                flat = [[side.reshape(-1, self.columns) for side in pair] for pair in self.parts]
                pair = [jnp.concatenate(sides) for sides in zip(*flat)]
                total = self.order.run(add, *pair)
                self.parts = [(total, swap(total, "wide", mask))]
            return
        kept, got = [array.reshape(-1, self.columns) for array in self.parts[0]]
        if self.joining is None:
            total = self.order.run(add, kept, got)
        else:
            bit = place_bit("wide", self.joining)
            total = self.order.run(lambda *x: pair_up(*x, bit), kept, got).reshape(-1, self.columns)
        if self.up:
            self.joining = self.up.pop(0)
            self.parts = [(total, swap(total, "wide", self.joining))]
        else:
            self.parts = [(total, swap(total, "wide", 1))]
            self.closed = True

    def finish(self, done):
        own, got = [array.reshape(self.pieces, -1, self.columns) for array in self.parts[0]]
        begin = 0
        for term, length in zip(self.terms, self.lengths):
            term.finish(done, own, got, begin, length)
            begin += length


def on_device(
    tokens,
    skip,
    flags,
    cotangent,
    norm_gains,
    norm_biases,
    qkv_weight,
    out_weight,
    out_bias,
    up_weight,
    up_bias,
    down_weight,
    down_bias,
    skip_weight,
    skip_bias,
):
    items, seq_rows, width = tokens.shape
    rows = items * seq_rows
    me = lax.axis_index("narrow")
    shares = lax.axis_size("narrow")
    spots = jnp.stack([me, lax.axis_index("wide")]).astype(jnp.int32)
    order = Order()

    weights = (qkv_weight, out_weight, up_weight, down_weight)
    qkv0, out0, up0, down0 = [Weight(weight, 0, width, spots) for weight in weights]
    qkv1, out1, up1, down1 = [Weight(weight, 1, width, spots) for weight in weights]
    join = Weight(skip_weight, None, width, spots)

    small = (norm_gains, norm_biases, out_bias, down_bias, skip_bias, up_bias)
    held = order.run(pack_small, *small)[None]
    for mask in masks("narrow"):
        held = jnp.concatenate([held, swap(held, "narrow", mask)])
    qkv0.fetch(*order.last)
    out0.fetch(held)
    up0.fetch(out0.sent)
    down0.fetch(up0.sent)
    place = me.astype(jnp.int32).reshape(1)
    lines = order.run(lambda x: unpack_small(x, place, small, width), held)

    def line(row):
        return lines[row : row + 1]

    gains, shifts = [[line(2 * layer + each) for each in range(2)] for layer in range(2)], None
    shifts = [[line(4 + 2 * layer + each) for each in range(2)] for layer in range(2)]
    out_biases, down_biases, join_shift = [line(8), line(9)], [line(10), line(11)], line(12)
    blocks = up0.blocks
    up_biases = [lines[13 + layer * blocks : 13 + (layer + 1) * blocks].reshape(1, -1) for layer in range(2)]

    tokens_flat, skip_flat, cotangent_flat = [array.reshape(rows, width) for array in (tokens, skip, cotangent)]
    lengths = PATCHES + 1 + CAPTION * flags
    valid = lax.broadcasted_iota(jnp.int32, (items, seq_rows), 1) < lengths[:, None]
    keep = valid.reshape(rows, 1).astype(full)
    dz1 = jnp.where(keep > 0, cotangent_flat, 0)

    qkv0.share(1)
    qkv0.share(0)
    order.hold(*out0.got(), *up0.got())
    out0.share(1)
    up0.share(1)
    a0, packed0 = order.run(lambda *x: project_qkv(*x, qkv0), tokens_flat, gains[0][0], shifts[0][0])
    order.hold(*down0.got())
    down0.share(1)
    join.fetch(a0)
    qkv1.fetch(join.sent)
    packed0 = packed0.reshape(3, items, seq_rows, width)
    mixed0, totals0 = order.run(lambda *x: attend(*x, items, seq_rows), packed0, lengths)
    out0.share(0, mixed0)
    up0.share(0, mixed0)
    down0.share(0, mixed0)
    out1.fetch(mixed0)
    up1.fetch(out1.sent)
    down1.fetch(up1.sent)
    order.hold(*join.got(), *qkv1.got())
    join.share(1)
    qkv1.share(1)
    mixed0 = mixed0.reshape(rows, width)
    m0, second0, hidden0, slope0, middle = order.run(
        lambda x, o, ob, g, s, ub, db: feed_forward(x, o, out0, ob, g, s, up0, ub, down0, db),
        tokens_flat, mixed0, out_biases[0], gains[0][1], shifts[0][1], up_biases[0], down_biases[0],
    )
    join.share(0, middle)
    qkv1.share(0, middle)
    order.hold(*out1.got(), *up1.got(), *down1.got())
    out1.share(1)
    up1.share(1)
    down1.share(1)
    entry, a1, packed1 = order.run(
        lambda m, s, jb, g, sh: join_qkv(m, s, join, jb, g, sh, qkv1),
        middle, skip_flat, join_shift, gains[1][0], shifts[1][0],
    )
    packed1 = packed1.reshape(3, items, seq_rows, width)
    mixed1, totals1 = order.run(lambda *x: attend(*x, items, seq_rows), packed1, lengths)
    out1.share(0, mixed1)
    up1.share(0, mixed1)
    down1.share(0, mixed1)
    mixed1 = mixed1.reshape(rows, width)
    m1, second1, hidden1, slope1, output = order.run(
        lambda x, o, ob, g, s, ub, db, k: feed_forward(x, o, out1, ob, g, s, up1, ub, down1, db, k),
        entry, mixed1, out_biases[1], gains[1][1], shifts[1][1], up_biases[1], down_biases[1], keep,
    )

    done = {}
    term_down1 = Term(order, "down", 1, down_term, hidden1, dz1)
    term_down1.stay()
    term_down1.pass_narrow()
    du, dm, db, do, sums1 = order.run(
        lambda y, z, s, m, g: feed_forward_back(y, z, s, down1, up1, m, g, out1),
        dz1, dz1, slope1, m1, gains[1][1],
    )
    term_up1 = Term(order, "up", 1, up_term, second1, du)
    term_up1.stay()
    term_up1.pass_narrow()
    total_down1 = term_down1.add_up()
    dpacked = order.run(
        lambda *x: attend_back(*x, items, seq_rows), packed1, do.reshape(items, seq_rows, width), totals1, lengths
    )
    flat_packed = dpacked.reshape(3, rows, width)
    term_qkv1 = Term(order, "qkv", 1, qkv_out_term, a1, flat_packed, mixed1, db)
    term_qkv1.stay()
    term_qkv1.pass_narrow()
    total_up1 = term_up1.add_up()
    size = lax.axis_size("wide")
    groups = [[device + core for device in range(0, size, 2)] for core in range(2)]
    totals = lax.psum((total_down1, total_up1), "wide", axis_index_groups=groups)
    dentry, dmiddle, dz0, skip_grad, sums3 = order.run(
        lambda gp, x, g, dm: project_back(gp, qkv1, x, g, dm, join), flat_packed, entry, gains[1][0], dm
    )
    term_down0 = Term(order, "down", 0, down_term, hidden0, dz0)
    term_down0.stay()
    term_down0.pass_narrow()
    term_qkv1.pass_wide(2)
    term_join = Term(order, "join", 1, join_term, middle, skip_flat, dentry)
    term_join.stay()
    term_join.pass_narrow()

    du, dm, db, do, sums0 = order.run(
        lambda y, z, s, m, g: feed_forward_back(y, z, s, down0, up0, m, g, out0),
        dmiddle, dz0, slope0, m0, gains[0][1],
    )
    term_down0.pass_wide(2)
    term_up0 = Term(order, "up", 0, up_term, second0, du)
    term_up0.stay()
    term_up0.pass_narrow()
    term_join.pass_wide(2)
    dpacked = order.run(
        lambda *x: attend_back(*x, items, seq_rows), packed0, do.reshape(items, seq_rows, width), totals0, lengths
    )
    first = Reduce(order, [term_qkv1, term_join], (2,))
    first.step()
    second = Reduce(order, [term_down0], (2,))
    second.step()
    flat_packed = dpacked.reshape(3, rows, width)
    term_qkv0 = Term(order, "qkv", 0, qkv_out_term, a0, flat_packed, mixed0, db)
    term_qkv0.stay()
    one, two = term_qkv0.part(0), term_qkv0.part(1)
    early = 4 if shares == 2 else None
    if early:
        two.pass_wide(early)
    third = Reduce(order, [term_up0])
    third.step()
    one.pass_narrow()
    second.step()
    first.step()
    tokens_grad, sums2 = order.run(
        lambda gp, x, g, dm: project_back(gp, qkv0, x, g, dm), flat_packed, tokens_flat, gains[0][0], dm
    )
    minor = jnp.concatenate([sums2, sums3, sums0, sums1])
    minor_stages = [("narrow", mask) for mask in masks("narrow")] + [("wide", mask) for mask in masks("wide")]
    minor_got = swap(minor, *minor_stages[0])

    def minor_step():
        nonlocal minor, minor_got
        if minor_stages:
            minor_stages.pop(0)
            minor = order.run(lambda one, two: one + two, minor, minor_got)
            if minor_stages:
                minor_got = swap(minor, *minor_stages[0])

    two.pass_narrow()
    third.step()
    fourth = Reduce(order, [one])
    fourth.step()
    second.step()
    first.step()
    fifth = Reduce(order, [two], (early,) if early else ())
    fifth.step()
    order.hold(*totals)
    other = [swap(after(total, *order.last), "wide", 1) for total in totals]
    third.step()
    fourth.step()
    second.step()
    fifth.step()
    minor_step()
    first.step()
    third.step()
    fourth.step()
    minor_step()
    second.step()
    fifth.step()
    minor_step()
    for term, own, got in zip((term_down1, term_up1), totals, other):
        term.finish(done, own, got, 0, own.shape[1])
    first.step()
    third.step()
    fourth.step()
    fifth.step()
    second.step()
    minor_step()
    third.step()
    fourth.step()
    second.finish(done)
    first.step()
    fifth.step()
    fourth.step()
    minor_step()
    first.finish(done)
    third.step()
    fifth.step()
    fourth.step()
    for each in (first, second, third, fourth, fifth):
        while not each.closed:
            each.step()
    while minor_stages:
        minor_step()
    third.finish(done)
    fifth.finish(done)
    fourth.finish(done)
    small = order.run(lambda x: small_gradients(x, place, width, shares, up1.blocks), minor)

    return (
        output.reshape(tokens.shape),
        tokens_grad.reshape(tokens.shape),
        skip_grad.reshape(tokens.shape),
        small[0],
        small[1],
        done["qkv"][0],
        done["qkv"][1],
        small[2],
        done["up"][0],
        small[3],
        done["down"][0],
        small[4],
        done["join"][0][0],
        small[5].reshape(-1),
    )


def solution(mesh):
    placed = (
        P(("wide", "narrow"), None, None),
        P(("wide", "narrow"), None, None),
        P(("wide", "narrow")),
        P(("wide", "narrow"), None, None),
        P(None, None, "narrow"),
        P(None, None, "narrow"),
        P(None, "narrow", None),
        P(None, "narrow", None),
        P(None, "narrow"),
        P(None, "narrow", None),
        P(None, "narrow"),
        P(None, "narrow", None),
        P(None, "narrow"),
        P("narrow", None),
        P("narrow"),
    )
    return jax.shard_map(
        on_device,
        mesh=mesh,
        in_specs=placed,
        out_specs=(
            P(("wide", "narrow"), None, None),
            P(("wide", "narrow"), None, None),
            P(("wide", "narrow"), None, None),
            P(None, None, "narrow"),
            P(None, None, "narrow"),
            P(None, "narrow", None),
            P(None, "narrow", None),
            P(None, "narrow"),
            P(None, "narrow", None),
            P(None, "narrow"),
            P(None, "narrow", None),
            P(None, "narrow"),
            P("narrow", None),
            P("narrow"),
        ),
        check_vma=False,
    )
```

```python
import copy

import jax
import jax.numpy as jnp
from jax import lax
from jax.experimental import pallas as pl
from jax.experimental.pallas import tpu as pltpu
from jax.sharding import PartitionSpec as P

HEAD_DIM = 64
PATCHES = 256
CAPTION = 77
PAIR = 2 * HEAD_DIM


epsilon = 1e-05
masked_score = -1e30
low = jnp.bfloat16
full = jnp.float32
ANY = pl.BlockSpec(memory_space=pl.ANY)
SCALARS = pl.BlockSpec(memory_space=pltpu.SMEM)


def dot(left, right, contract=(1, 0)):
    dims = (((contract[0],), (contract[1],)), ((), ()))
    return lax.dot_general(left, right, dims, preferred_element_type=full)


def normalize(values):
    centred = values - jnp.mean(values, axis=-1, keepdims=True)
    factor = lax.rsqrt(jnp.mean(centred * centred, axis=-1, keepdims=True) + epsilon)
    return centred * factor, factor


def normalize_back(upstream, normed, factor):
    return factor * (
        upstream
        - jnp.mean(upstream, axis=-1, keepdims=True)
        - normed * jnp.mean(upstream * normed, axis=-1, keepdims=True)
    )


def column_sum(values):
    return jnp.sum(values.astype(full), axis=0, keepdims=True)


def whole(shape):
    return pl.BlockSpec(shape, lambda *grid: (0,) * len(shape))


def cost(micros):
    return pl.CostEstimate(flops=int(micros * 3 * 10**8), bytes_accessed=0, transcendentals=0)


def call(body, grid, ins, outs, name, micros, scratch=(), limit=56):
    return pl.pallas_call(
        body,
        grid=grid,
        in_specs=[spec for _, spec in ins],
        out_specs=[spec for _, _, spec in outs],
        out_shape=[jax.ShapeDtypeStruct(shape, kind) for shape, kind, _ in outs],
        scratch_shapes=list(scratch),
        name=name,
        cost_estimate=cost(micros),
        compiler_params=pltpu.CompilerParams(vmem_limit_bytes=limit * 2**20),
    )(*[array for array, _ in ins])


class Fetch:
    def __init__(self, arrays, sharing):
        self.arrays, self.sharing = arrays, list(sharing)
        self.rows = arrays[0][0].shape[-2]
        while self.rows % (16 << len(self.sharing)):
            self.sharing.pop()
        self.length = self.rows >> len(self.sharing)

    def quarter(self, place):
        return sum(((place // mask) & 1) << bit for bit, mask in enumerate(self.sharing))

    def fetch(self, *earlier):
        found = []
        for array, layer in self.arrays:
            array = after(array, *earlier)
            lead = () if layer is None else (layer,)
            begin = self.quarter(lax.axis_index("wide")) * self.length
            sizes = (1,) * len(lead) + (self.length, array.shape[-1])
            found.append(lax.dynamic_slice(array, lead + (begin, 0), sizes).reshape(self.length, -1))
        self.sent = (jnp.concatenate(found, axis=1) if len(found) > 1 else found[0])[None]
        held = self.sent
        for mask in masks("narrow"):
            held = jnp.concatenate([held, swap(held, "narrow", mask)])
        self.pieces = {0: held[1:]}

    def share(self, which, *earlier):
        if which < len(self.sharing):
            mask = self.sharing[which]
            got = {key ^ (1 << which): swap(after(piece, *earlier), "wide", mask) for key, piece in self.pieces.items()}
            self.pieces.update(got)

    def got(self):
        return list(self.pieces.values())


class Weight:
    def __init__(self, fetched, which, width, spots):
        self.fetched, self.spots, self.width = fetched, spots, width
        self.array, self.layer = fetched.arrays[which]
        self.begin = sum(array.shape[-1] for array, _ in fetched.arrays[:which])
        self.rows, columns = self.array.shape[-2:]
        self.shares = lax.axis_size("narrow")
        self.blocks = columns // width
        self.total = self.rows * self.shares

    def arrays(self):
        return [self.array] + self.fetched.got()

    def scratch(self):
        copies = 1 + len(self.fetched.pieces) * (self.shares - 1)
        return [pltpu.VMEM((self.blocks, self.total, self.width), low), pltpu.SemaphoreType.DMA((self.blocks, copies))]

    def copies(self, spots, refs, held, signals, block):
        own, pieces = refs[0], refs[1:]
        me, length = spots[0], self.fetched.length
        own = own if self.layer is None else own.at[self.layer]
        columns = pl.ds(block * self.width, self.width)
        begin = pl.multiple_of(me * self.rows, 16)
        found = [(own.at[:, columns], begin, self.rows)]
        columns = pl.ds(self.begin + block * self.width, self.width)
        for key, piece in zip(self.fetched.pieces, pieces):
            for offset in range(1, self.shares):
                begin = (me ^ offset) * self.rows + (self.fetched.quarter(spots[1]) ^ key) * length
                found.append((piece.at[offset - 1, :, columns], pl.multiple_of(begin, 16), length))
        return [
            pltpu.make_async_copy(source, held.at[block, pl.ds(begin, length)], signals.at[block, place])
            for place, (source, begin, length) in enumerate(found)
        ]

    def start(self, *refs):
        for block in range(self.blocks):
            for copy in self.copies(*refs, block):
                copy.start()

    def wait(self, *refs, block=0):
        for copy in self.copies(*refs, block):
            copy.wait()


def weighted(body, weights, grid, ins, outs, name, micros, scratch=()):
    spots = weights[0].spots
    operands = [(spots, SCALARS)] + [(array, ANY) for weight in weights for array in weight.arrays()]
    counts = [len(weight.arrays()) for weight in weights]
    extra = [piece for weight in weights for piece in weight.scratch()]

    def wrapped(*refs):
        spots_ref, rest = refs[0], list(refs[1:])
        sources = []
        for count in counts:
            sources.append(rest[:count])
            rest = rest[count:]
        spare = rest[len(rest) - len(extra) :]
        rest = rest[: len(rest) - len(extra)]
        handles = []
        for place, weight in enumerate(weights):
            held, signals = spare[2 * place : 2 * place + 2]
            refs_of = (spots_ref, sources[place], held, signals)
            handles.append((weight, refs_of, held))

        @pl.when(pl.program_id(0) == 0)
        def _():
            for weight, refs_of, _ in handles:
                weight.start(*refs_of)

        def ready(place, block=0):
            weight, refs_of, held = handles[place]
            weight.wait(*refs_of, block=block)

        body(ready, [held for _, _, held in handles], *rest)

    return call(wrapped, grid, operands + ins, outs, name, micros, list(scratch) + extra)


def pack_small(*small):
    part = small[0].shape[-1]
    counts = [piece.size // part for piece in small]

    def body(*refs):
        row = 0
        for ref in refs[:-1]:
            values = ref[...].reshape(-1, ref.shape[-1])
            for each in range(values.shape[0]):
                for begin in range(0, values.shape[1], part):
                    refs[-1][row : row + 1] = values[each : each + 1, begin : begin + part].astype(full)
                    row += 1
        refs[-1][row:] = jnp.zeros((refs[-1].shape[0] - row, part), full)

    flat = [piece.reshape((1,) * (2 - piece.ndim) + piece.shape) for piece in small]
    rows = -(-sum(counts) // 16) * 16
    out = ((rows, part), full, whole((rows, part)))
    return call(body, (1,), [(piece, whole(piece.shape)) for piece in flat], [out], "pack_small", 1)[0].astype(low)


def unpack_small(parts, me, small, width):
    shares, _, part = parts.shape
    lines = [(piece.size // piece.shape[-1], piece.shape[-1] // part) for piece in small]
    total = sum(count * many for count, many in lines)
    rows = -(-total // 8) * 8

    def body(me_ref, parts_ref, out_ref):
        values = parts_ref[...].astype(full)
        for mine in range(shares):

            @pl.when(me_ref[0] == mine)
            def _():
                for owner in range(shares):
                    source, target = 0, 0
                    for count, many in lines:
                        for each in range(count):
                            for piece in range(many):
                                at = owner * many * part + piece * part
                                row, column = target + at // width, at % width
                                line = values[owner ^ mine, source : source + 1]
                                out_ref[row : row + 1, column : column + part] = line
                                source += 1
                            target += many
        if rows > total:
            out_ref[total:] = jnp.zeros((rows - total, width), full)

    ins = [(parts, pl.BlockSpec(parts.shape, lambda g, me: (0, 0, 0)))]
    out = ((rows, width), full, pl.BlockSpec((rows, width), lambda g, me: (0, 0)))
    return picked(body, me, (1,), ins, [out], "unpack_small", 1)[0]


def project_qkv(inputs, gain, shift, weight):
    rows, width = inputs.shape

    def body(ready, held, x_ref, gain_ref, shift_ref, a_ref, out_ref):
        step = pl.program_id(0)

        @pl.when(step == 0)
        def _():
            normed, _ = normalize(x_ref[...].astype(full))
            a_ref[...] = (normed * gain_ref[...] + shift_ref[...]).astype(low)

        ready(0, step)
        scale = jnp.where(step == 0, HEAD_DIM ** (-0.5), 1.0)
        out_ref[0] = (dot(a_ref[...], held[0][step]).astype(low).astype(full) * scale).astype(low)

    return weighted(
        body,
        [weight],
        (3,),
        [
            (inputs, whole((rows, width))),
            (gain, whole((1, width))),
            (shift, whole((1, width))),
        ],
        [
            ((rows, width), low, whole((rows, width))),
            ((3, rows, width), low, pl.BlockSpec((1, rows, width), lambda j: (j, 0, 0))),
        ],
        "project_qkv",
        7,
    )


def join_qkv(middle, skip, join_weight, join_shift, gain, shift, weight):
    rows, width = middle.shape

    def body(ready, held, m_ref, s_ref, jb_ref, gain_ref, shift_ref, e_ref, a_ref, out_ref):
        step = pl.program_id(0)

        @pl.when(step == 0)
        def _():
            ready(0)
            entry = dot(m_ref[...], held[0][0, :width]) + dot(s_ref[...], held[0][0, width:]) + jb_ref[...]
            e_ref[...] = entry
            normed, _ = normalize(entry)
            a_ref[...] = (normed * gain_ref[...] + shift_ref[...]).astype(low)

        ready(1, step)
        scale = jnp.where(step == 0, HEAD_DIM ** (-0.5), 1.0)
        out_ref[0] = (dot(a_ref[...], held[1][step]).astype(low).astype(full) * scale).astype(low)

    return weighted(
        body,
        [join_weight, weight],
        (3,),
        [
            (middle, whole((rows, width))),
            (skip, whole((rows, width))),
            (join_shift, whole((1, width))),
            (gain, whole((1, width))),
            (shift, whole((1, width))),
        ],
        [
            ((rows, width), full, whole((rows, width))),
            ((rows, width), low, whole((rows, width))),
            ((3, rows, width), low, pl.BlockSpec((1, rows, width), lambda j: (j, 0, 0))),
        ],
        "join_qkv",
        11,
    )


def head_masks(seq_rows):
    lane = lax.broadcasted_iota(jnp.int32, (seq_rows, PAIR), 1)
    return [lane < HEAD_DIM, lane >= HEAD_DIM]


def attend(packed, lengths, items, seq_rows):
    width = packed.shape[-1]
    pairs = width // PAIR

    def body(length_ref, q_ref, k_ref, v_ref, out_ref, total_ref):
        length = length_ref[pl.program_id(0)]
        queries, keys, values = q_ref[0, 0], k_ref[0, 0], v_ref[0, 0]
        counts = lax.broadcasted_iota(jnp.int32, (seq_rows, seq_rows), 0) < length
        mixed = jnp.zeros((PAIR, seq_rows), full)
        for head, lanes in enumerate(head_masks(seq_rows)):
            scores = dot(keys, jnp.where(lanes, queries, 0), (1, 1))
            scores = jnp.where(counts, scores, masked_score)
            largest = jnp.max(scores, axis=0, keepdims=True)
            weights = jnp.exp(scores - largest)
            total = jnp.sum(weights, axis=0, keepdims=True)
            part = dot(jnp.where(lanes, values, 0), weights.astype(low), (0, 0))
            mixed += part * (1.0 / total)
            total_ref[0, 0, head : head + 1] = largest + jnp.log(total)
        out_ref[0] = mixed.T.astype(low)

    def block(which):
        return pl.BlockSpec((1, 1, seq_rows, PAIR), lambda n, h: (which, n, 0, h))

    return call(
        body,
        (items, pairs),
        [
            (lengths, SCALARS),
            (packed, block(0)),
            (packed, block(1)),
            (packed, block(2)),
        ],
        [
            ((items, seq_rows, width), low, pl.BlockSpec((1, seq_rows, PAIR), lambda n, h: (n, 0, h))),
            ((items, pairs, 8, seq_rows), full, pl.BlockSpec((1, 1, 8, seq_rows), lambda n, h: (n, h, 0, 0))),
        ],
        "attend",
        13,
    )


def attend_back(packed, grad_mixed, totals, lengths, items, seq_rows):
    width = packed.shape[-1]
    pairs = width // PAIR

    def body(length_ref, q_ref, k_ref, v_ref, g_ref, total_ref, out_ref):
        length = length_ref[pl.program_id(0)]
        queries, keys, values, upstream = q_ref[0, 0], k_ref[0, 0], v_ref[0, 0], g_ref[0]
        counts = lax.broadcasted_iota(jnp.int32, (seq_rows, seq_rows), 0) < length
        grad_queries = jnp.zeros((PAIR, seq_rows), full)
        grad_keys = jnp.zeros((seq_rows, PAIR), full)
        grad_values = jnp.zeros((seq_rows, PAIR), full)
        for head, lanes in enumerate(head_masks(seq_rows)):
            own_queries = jnp.where(lanes, queries, 0)
            own_upstream = jnp.where(lanes, upstream, 0)
            scores = dot(keys, own_queries, (1, 1))
            shifted = jnp.where(counts, scores, masked_score) - total_ref[0, 0, head : head + 1]
            probs = jnp.exp(shifted)
            grad_probs = dot(values, own_upstream, (1, 1))
            centre = jnp.sum(grad_probs * probs, axis=0, keepdims=True)
            grad_scores = (probs * (grad_probs - centre)).astype(low)
            grad_values += dot(probs.astype(low), own_upstream)
            grad_keys += dot(grad_scores, own_queries)
            grad_queries += dot(jnp.where(lanes, keys, 0), grad_scores, (0, 0))
        out_ref[0, 0] = (grad_queries.T * HEAD_DIM ** (-0.5)).astype(low)
        out_ref[1, 0] = grad_keys.astype(low)
        out_ref[2, 0] = grad_values.astype(low)

    def block(which):
        return pl.BlockSpec((1, 1, seq_rows, PAIR), lambda n, h: (which, n, 0, h))

    return call(
        body,
        (items, pairs),
        [
            (lengths, SCALARS),
            (packed, block(0)),
            (packed, block(1)),
            (packed, block(2)),
            (grad_mixed, pl.BlockSpec((1, seq_rows, PAIR), lambda n, h: (n, 0, h))),
            (totals, pl.BlockSpec((1, 1, 8, seq_rows), lambda n, h: (n, h, 0, 0))),
        ],
        [
            ((3, items, seq_rows, width), low, pl.BlockSpec((3, 1, seq_rows, PAIR), lambda n, h: (0, n, 0, h))),
        ],
        "attend_back",
        17,
    )[0]


def gelu_parts(before):
    decay = jnp.exp(before * before * -0.5)
    inverse = pl.reciprocal(1.0 + (0.3275911 * 0.5**0.5) * jnp.abs(before), approx=False)
    series = 1.061405429 * 0.5
    for term in (-1.453152027, 1.421413741, -0.284496736, 0.254829592):
        series = series * inverse + term * 0.5
    below = series * inverse * decay
    share = jnp.where(before >= 0, 1.0 - below, below)
    return before * share, share + before * decay * 0.3989422804014327


def feed_forward(inputs, mixed, out_weight, out_bias, gain, shift, up_weight, up_bias, down_weight, down_bias, keep=None):
    rows, width = inputs.shape
    steps = up_weight.blocks
    hidden = steps * width

    def body(ready, held, x_ref, o_ref, ob_ref, gain_ref, shift_ref, ub_ref, db_ref, *rest):
        m_ref, a_ref, g_ref, s_ref, y_ref, total = rest[-6:]
        step = pl.program_id(0)

        @pl.when(step == 0)
        def _():
            ready(0)
            middle = x_ref[...].astype(full) + dot(o_ref[...], held[0][0]) + ob_ref[...]
            m_ref[...] = middle
            normed, _ = normalize(middle)
            a_ref[...] = (normed * gain_ref[...] + shift_ref[...]).astype(low)
            total[...] = middle + db_ref[...]

        ready(1, step)
        before = dot(a_ref[...], held[1][step]) + ub_ref[...]
        value, slope = gelu_parts(before)
        g_ref[...] = value.astype(low)
        s_ref[...] = slope.astype(low)

        @pl.when(step == 0)
        def _():
            ready(2)

        total[...] += dot(g_ref[...], held[2][0, pl.ds(pl.multiple_of(step * width, width), width)])

        @pl.when(step == steps - 1)
        def _():
            value = total[...]
            if keep is not None:
                value = jnp.where(rest[0][...] > 0, value, 0.0)
            y_ref[...] = value.astype(low)

    return weighted(
        body,
        [out_weight, up_weight, down_weight],
        (steps,),
        [
            (inputs, whole((rows, width))),
            (mixed, whole((rows, width))),
            (out_bias, whole((1, width))),
            (gain, whole((1, width))),
            (shift, whole((1, width))),
            (up_bias, pl.BlockSpec((1, width), lambda j: (0, j))),
            (down_bias, whole((1, width))),
        ]
        + ([] if keep is None else [(keep, whole((rows, 1)))]),
        [
            ((rows, width), full, whole((rows, width))),
            ((rows, width), low, whole((rows, width))),
            ((rows, hidden), low, pl.BlockSpec((rows, width), lambda j: (0, j))),
            ((rows, hidden), low, pl.BlockSpec((rows, width), lambda j: (0, j))),
            ((rows, width), low, whole((rows, width))),
        ],
        "feed_forward",
        23,
        scratch=[pltpu.VMEM((rows, width), full)],
    )


def feed_forward_back(upstream, rounded, slope, down_weight, up_weight, middle, gain, out_weight):
    rows, width = upstream.shape
    steps = up_weight.blocks
    hidden = steps * width

    def body(ready, held, y_ref, dz_ref, s_ref, m_ref, gain_ref, du_ref, dm_ref, db_ref, do_ref, sums_ref, total):
        step = pl.program_id(0)

        @pl.when(step == 0)
        def _():
            sums_ref[0:1] = column_sum(dz_ref[...])
            total[...] = jnp.zeros_like(total)
            ready(0)

        down = held[0][0, pl.ds(pl.multiple_of(step * width, width), width)]
        grad = (dot(dz_ref[...], down, (1, 1)) * s_ref[...].astype(full)).astype(low)
        du_ref[...] = grad
        sums_ref[pl.ds(4 + step, 1)] = column_sum(grad)
        ready(1, step)
        total[...] += dot(grad, held[1][step], (1, 1))

        @pl.when(step == steps - 1)
        def _():
            grad_second = total[...]
            normed, factor = normalize(m_ref[...])
            sums_ref[1:2] = column_sum(grad_second * normed)
            sums_ref[2:3] = column_sum(grad_second)
            grad_middle = y_ref[...].astype(full) + normalize_back(grad_second * gain_ref[...], normed, factor)
            dm_ref[...] = grad_middle
            branch = grad_middle.astype(low)
            db_ref[...] = branch
            sums_ref[3:4] = column_sum(branch)
            ready(2)
            do_ref[...] = dot(branch, held[2][0], (1, 1)).astype(low)

    return weighted(
        body,
        [down_weight, up_weight, out_weight],
        (steps,),
        [
            (upstream, whole((rows, width))),
            (rounded, whole((rows, width))),
            (slope, pl.BlockSpec((rows, width), lambda j: (0, j))),
            (middle, whole((rows, width))),
            (gain, whole((1, width))),
        ],
        [
            ((rows, hidden), low, pl.BlockSpec((rows, width), lambda j: (0, j))),
            ((rows, width), full, whole((rows, width))),
            ((rows, width), low, whole((rows, width))),
            ((rows, width), low, whole((rows, width))),
            ((4 + steps, width), full, whole((4 + steps, width))),
        ],
        "feed_forward_back",
        21,
        scratch=[pltpu.VMEM((rows, width), full)],
    )


def project_back(grad_packed, weight, inputs, gain, grad_middle, join_weight=None):
    rows, width = inputs.shape
    joined = join_weight is not None

    def body(ready, held, g_ref, x_ref, gain_ref, dm_ref, *rest):
        if joined:
            de_ref, dx_ref, dz_ref, skip_ref, sums_ref, total = rest
        else:
            dx_ref, sums_ref, total = rest
        step = pl.program_id(0)

        @pl.when(step == 0)
        def _():
            total[...] = jnp.zeros_like(total)

        ready(0, step)
        total[...] += dot(g_ref[0], held[0][step], (1, 1))

        @pl.when(step == 2)
        def _():
            grad_first = total[...]
            normed, factor = normalize(x_ref[...].astype(full))
            sums_ref[0:1] = column_sum(grad_first * normed)
            sums_ref[1:2] = column_sum(grad_first)
            grad = dm_ref[...] + normalize_back(grad_first * gain_ref[...], normed, factor)
            if joined:
                entry = grad.astype(low)
                de_ref[...] = entry
                sums_ref[2:3] = column_sum(entry)
                ready(1)
                grad = dot(entry, held[1][0, :width], (1, 1))
                dx_ref[...] = grad
                dz_ref[...] = grad.astype(low)
                skip_ref[...] = dot(entry, held[1][0, width:], (1, 1))
            else:
                dx_ref[...] = grad

    ins = [
        (grad_packed, pl.BlockSpec((1, rows, width), lambda j: (j, 0, 0))),
        (inputs, whole((rows, width))),
        (gain, whole((1, width))),
        (grad_middle, whole((rows, width))),
    ]
    outs = [((rows, width), full, whole((rows, width))), ((8, width), full, whole((8, width)))]
    if joined:
        rounded = ((rows, width), low, whole((rows, width)))
        outs = [rounded, outs[0], rounded, outs[0], outs[1]]
    return weighted(
        body,
        [weight] + ([join_weight] if joined else []),
        (3,),
        ins,
        outs,
        "project_back",
        13 if joined else 9,
        scratch=[pltpu.VMEM((rows, width), full)],
    )


def picked(body, which, grid, ins, outs, name, micros, aliases=None):
    return pl.pallas_call(
        body,
        grid_spec=pltpu.PrefetchScalarGridSpec(
            num_scalar_prefetch=1,
            grid=grid,
            in_specs=[spec for _, spec in ins],
            out_specs=[spec for _, _, spec in outs],
        ),
        out_shape=[jax.ShapeDtypeStruct(shape, kind) for shape, kind, _ in outs],
        name=name,
        input_output_aliases={place + 1: out for place, out in (aliases or {}).items()},
        cost_estimate=cost(micros),
        compiler_params=pltpu.CompilerParams(vmem_limit_bytes=48 * 2**20),
    )(which, *[array for array, _ in ins])


def quarters(rows, width, narrow_rows):
    shape = (lax.axis_size("narrow") // 2 * narrow_rows, width)
    return [(shape, low, pl.BlockSpec(shape, lambda g, core: (0, 0)))] * 4


def up_term(left, right, core):
    rows, width = left.shape
    part = width // lax.axis_size("narrow")
    half = width // 2

    def body(core_ref, l_ref, r_ref, *outs):
        value = dot(l_ref[...], r_ref[...], (0, 0)).astype(low)
        for block in range(2):

            @pl.when(pl.program_id(0) == block)
            def _():
                outs[block][...] = value[:half]
                outs[2 + block][...] = value[half:]

    return picked(
        body,
        core,
        (2,),
        [
            (left, pl.BlockSpec((rows, width), lambda g, core: (0, 0))),
            (right, pl.BlockSpec((rows, width), lambda g, core: (0, core[0] * 2 + g))),
        ],
        quarters(rows, width, part),
        "up_term",
        3.5,
    )


def qkv_out_term(first, packed, mixed, branch, core):
    rows, width = first.shape
    part = width // lax.axis_size("narrow")
    half = width // 2

    def body(core_ref, l_ref, r_ref, o_ref, b_ref, *outs):
        step = pl.program_id(0)
        last = core_ref[0] * 2 + step == 3

        def put(block, value):
            outs[block][...] = value[:half]
            outs[2 + block][...] = value[half:]

        @pl.when(last)
        def _():
            put(1, dot(o_ref[...], b_ref[...], (0, 0)).astype(low))

        @pl.when(jnp.logical_not(last))
        def _():
            value = dot(l_ref[...], r_ref[0], (0, 0)).astype(low)
            for block in range(2):

                @pl.when(step == block)
                def _():
                    put(block, value)

    flat = pl.BlockSpec((rows, width), lambda g, core: (0, 0))
    return picked(
        body,
        core,
        (2,),
        [
            (first, flat),
            (packed, pl.BlockSpec((1, rows, width), lambda g, core: (jnp.minimum(core[0] * 2 + g, 2), 0, 0))),
            (mixed, flat),
            (branch, flat),
        ],
        quarters(rows, width, part),
        "qkv_out_term",
        3.5,
    )


def down_term(left, right, core):
    rows, width = right.shape
    shares = lax.axis_size("narrow")
    part = left.shape[1] // (2 * shares)
    direct = part == width
    if not direct:
        left = left.reshape(rows, shares, 2, 2, part // 2)
        left = lax.dynamic_index_in_dim(left, core[0], 2, keepdims=False)
        left = left.reshape(rows, 2, shares // 2, 2, part // 2).swapaxes(2, 3).reshape(rows, 2 * width)
    half = width // 2

    def body(core_ref, l_ref, r_ref, *outs):
        value = dot(l_ref[...], r_ref[...], (0, 0)).astype(low)
        for owner in range(2):

            @pl.when(pl.program_id(0) == owner)
            def _():
                outs[2 * owner][...] = value[:half]
                outs[2 * owner + 1][...] = value[half:]

    return picked(
        body,
        core,
        (2,),
        [
            (left, pl.BlockSpec((rows, width), lambda g, core: (0, g * 2 + core[0] if direct else g))),
            (right, pl.BlockSpec((rows, width), lambda g, core: (0, 0))),
        ],
        quarters(rows, width, part // 2),
        "down_term",
        3.5,
    )


def join_term(middle, skip, right, core):
    rows, width = right.shape
    shares = lax.axis_size("narrow")
    part = width // shares
    half = width // 2
    if part != half:
        left = jnp.concatenate([middle, skip], axis=1).reshape(rows, shares, 2, 2, part // 2)
        left = lax.dynamic_index_in_dim(left, core[0], 2, keepdims=False)
        left = left.reshape(rows, 2, shares // 2, 2, part // 2).swapaxes(2, 3).reshape(rows, width)
        middle, skip = left[:, :half], left[:, half:]

    def body(core_ref, m_ref, s_ref, r_ref, *outs):
        for owner, left_ref in enumerate((m_ref, s_ref)):
            value = dot(left_ref[...], r_ref[...], (0, 0)).astype(low)
            outs[2 * owner][...] = value[: half // 2]
            outs[2 * owner + 1][...] = value[half // 2 :]

    side = pl.BlockSpec((rows, half), lambda g, core: (0, core[0] if part == half else 0))
    return picked(
        body,
        core,
        (1,),
        [(middle, side), (skip, side), (right, pl.BlockSpec((rows, width), lambda g, core: (0, 0)))],
        quarters(rows, width, part // 2),
        "join_term",
        2,
    )


def cross(bit, *pieces):
    kept, got = pieces[: len(pieces) // 2], pieces[len(pieces) // 2 :]
    rows, columns = kept[0].shape
    blocks = len(kept) // 2
    steps = 2 if rows % 32 == 0 else 1

    def body(bit_ref, *refs):
        sent_ref, left_ref = refs[-2:]

        def put(target, owner):
            for block in range(blocks):
                place = owner * blocks + block
                one, two = refs[place], refs[2 * blocks + place]
                target[block] = (one[...].astype(full) + two[...].astype(full)).astype(low)

        for mine in range(2):

            @pl.when(bit_ref[0] == mine)
            def _():
                put(sent_ref, 1 - mine)
                put(left_ref, mine)

    ins = [(piece, pl.BlockSpec((rows // steps, columns), lambda g, bit: (g, 0))) for piece in kept + got]
    out = ((blocks, rows, columns), low, pl.BlockSpec((blocks, rows // steps, columns), lambda g, bit: (0, g, 0)))
    return picked(body, bit, (steps,), ins, [out, out], "cross", 2)


def add_halve(bit, *pairs):
    lead, columns = pairs[0].shape[0], pairs[0].shape[-1]
    sizes = [pair.shape[2] for pair in pairs[::2]]
    total = sum(sizes)
    steps = 2 if len(sizes) == 1 and total % 32 == 0 and total >= 256 else 1

    def body(bit_ref, *refs):
        mine = bit_ref[0]
        for target, place in ((refs[-2], 1 - mine), (refs[-1], mine)):
            begin = 0
            for kept_ref, got_ref in zip(refs[:-2:2], refs[1:-2:2]):
                length = kept_ref.shape[2]
                for each in range(lead):
                    value = kept_ref[each, place].astype(full) + got_ref[each, place].astype(full)
                    target[each, begin : begin + length] = value.astype(low)
                begin += length

    ins = [
        (pair, pl.BlockSpec((lead, 2, pair.shape[2] // steps, columns), lambda g, bit: (0, 0, g, 0)))
        for pair in pairs
    ]
    out = (
        (lead, total, columns),
        low,
        pl.BlockSpec((lead, total // steps, columns), lambda g, bit: (0, g, 0)),
    )
    return picked(body, bit, (steps,), ins, [out, out], "add_halve", 2)


def add_into(target, place, count, one, two):
    rows, columns = one.shape[-2:]
    steps = 2 if rows % 32 == 0 else 1
    block = pl.BlockSpec((1, rows // steps, columns), lambda g: (0, g, 0))

    def body(one_ref, two_ref, *rest):
        rest[-1][...] = (one_ref[...].astype(full) + two_ref[...].astype(full)).astype(low)

    ins = [one.reshape(1, rows, columns), two.reshape(1, rows, columns)]
    return pl.pallas_call(
        body,
        grid=(steps,),
        in_specs=[block, block] + ([] if target is None else [ANY]),
        out_specs=pl.BlockSpec((1, rows // steps, columns), lambda g: (place, g, 0)),
        out_shape=jax.ShapeDtypeStruct((count, rows, columns), low),
        name="add_into",
        input_output_aliases={} if target is None else {2: 0},
        cost_estimate=cost(1.3),
    )(*ins, *([] if target is None else [target]))


def add(one, two):
    return (one.astype(full) + two.astype(full)).astype(low)


def pair_up(own, got, bit):
    rows, columns = own.shape

    def body(bit_ref, own_ref, got_ref, out_ref):
        mine = bit_ref[0]
        out_ref[mine] = own_ref[...]
        out_ref[1 - mine] = got_ref[...]

    flat = pl.BlockSpec((rows, columns), lambda g, bit: (0, 0))
    out = ((2, rows, columns), low, pl.BlockSpec((2, rows, columns), lambda g, bit: (0, 0, 0)))
    return picked(body, bit, (1,), [(own, flat), (got, flat)], [out], "pair_up", 1)[0]


def finish(kind, half, own, got, begin, length, core, layer, targets):
    pieces, _, columns = own.shape
    scale = 1.0 / lax.axis_size("wide")
    aliases = {place + 2: place for place in range(len(targets))}
    source = pl.BlockSpec((pieces, length, columns), lambda g, core: (0, begin // length, 0))
    ins = [(own, source), (got, source)] + [(target, ANY) for target in targets]
    rows = pieces * length

    def chosen(core_ref, which, own_ref, got_ref, place=None):
        sides = [own_ref, got_ref]
        if place is None:
            values = [side[...].reshape(pieces * length, columns) for side in sides]
        else:
            if pieces == 1:
                near = (0, pl.ds(place * (length // 2), length // 2))
            else:
                near = (pl.ds(place * (pieces // 2), pieces // 2),)
            values = [side[near].reshape(pieces * length // 2, columns) for side in sides]
        return jnp.where(core_ref[0] == which, values[0], values[1]).astype(full) * scale

    if kind in ("down", "join"):

        def body(core_ref, own_ref, got_ref, *rest):
            rest[-1][0] = chosen(core_ref, pl.program_id(0), own_ref, got_ref)

        place = layer if kind == "down" else 0
        shape = (2 if kind == "down" else 1, 2 * rows, columns)
        out = (shape, full, pl.BlockSpec((1, rows, columns), lambda g, core: (place, g, 0)))
        return picked(body, core, (2,), ins, [out], "finish_rows", 3, aliases)
    steps = 4 if half is None else 2
    rows = rows // 2 if half is None else rows

    def block(step):
        return step if half is None else 2 * step + half

    def values_of(core_ref, own_ref, got_ref):
        step = pl.program_id(0)
        if half is None:
            return chosen(core_ref, step // 2, own_ref, got_ref, step % 2)
        return chosen(core_ref, step, own_ref, got_ref)

    def body(core_ref, own_ref, got_ref, *rest):
        values = values_of(core_ref, own_ref, got_ref)
        if kind == "up":
            rest[-1][0] = values
            return
        if half == 0:
            rest[-1][0] = values
            return
        last = block(pl.program_id(0)) == 3

        @pl.when(jnp.logical_not(last))
        def _():
            rest[-2][0] = values

        @pl.when(last)
        def _():
            rest[-1][0] = values

    if kind == "up":
        outs = [((2, rows, 4 * columns), full, pl.BlockSpec((1, rows, columns), lambda g, core: (layer, 0, block(g))))]
        return picked(body, core, (steps,), ins, outs, "finish_columns", 3, aliases)

    def spot(step):
        return block(step if half == 0 else jnp.minimum(step, steps - 2))

    outs = [
        ((2, rows, 3 * columns), full, pl.BlockSpec((1, rows, columns), lambda g, core: (layer, 0, spot(g)))),
        ((2, rows, columns), full, pl.BlockSpec((1, rows, columns), lambda g, core: (layer, 0, 0))),
    ]
    if half == 0:
        kept = targets[1:]
        ins, outs, aliases = ins[:3] if targets else ins, outs[:1], {2: 0} if targets else {}
        return (picked(body, core, (steps,), ins, outs, "finish_qkv", 3, aliases)[0], *kept)
    return picked(body, core, (steps,), ins, outs, "finish_qkv_out", 3, aliases)


def small_gradients(total, me, width, shares, blocks):
    part = width // shares
    scale = 1.0 / lax.axis_size("wide")

    def body(me_ref, total_ref, gains_ref, shifts_ref, out_ref, up_ref, down_ref, join_ref):
        values = total_ref[...] * scale
        back = [values[0:8], values[8:16]]
        ahead = [values[16 : 20 + blocks], values[20 + blocks : 24 + 2 * blocks]]
        for place in range(shares):

            @pl.when(me_ref[0] == place)
            def _():
                columns = slice(place * part, place * part + part)
                for layer in range(2):
                    for row, target in ((0, gains_ref), (1, shifts_ref)):
                        target[layer, 0:1] = back[layer][row : row + 1, columns]
                        target[layer, 1:2] = ahead[layer][row + 1 : row + 2, columns]
                    out_ref[layer : layer + 1] = ahead[layer][3:4, columns]
                    down_ref[layer : layer + 1] = ahead[layer][0:1, columns]
                    begin = place * part * blocks
                    while begin < (place + 1) * part * blocks:
                        row, column = begin // width, begin % width
                        length = min(width - column, (place + 1) * part * blocks - begin)
                        at = begin - place * part * blocks
                        piece = ahead[layer][4 + row : 5 + row, column : column + length]
                        up_ref[layer : layer + 1, at : at + length] = piece
                        begin += length
                join_ref[...] = back[1][2:3, columns]

    shapes = [(2, 2, part), (2, 2, part), (2, part), (2, part * blocks), (2, part), (1, part)]
    outs = [(shape, full, pl.BlockSpec(shape, lambda g, me, n=len(shape): (0,) * n)) for shape in shapes]
    ins = [(total, pl.BlockSpec(total.shape, lambda g, me: (0, 0)))]
    return picked(body, me, (1,), ins, outs, "small_gradients", 1)


def after(value, *earlier):
    return lax.optimization_barrier((value,) + earlier)[0] if earlier else value


def swap(values, axis, mask):
    size = lax.axis_size(axis)
    return lax.ppermute(values, axis, [(source, source ^ mask) for source in range(size)])


def masks(axis):
    return [1 << bit for bit in range(lax.axis_size(axis).bit_length() - 1)]


class Order:
    def __init__(self):
        self.last = ()

    def run(self, function, *arrays):
        held = lax.optimization_barrier(tuple(arrays) + self.last)[: len(arrays)]
        out = function(*held)
        self.last = (jax.tree.leaves(out)[0],)
        return out

    def hold(self, *arrays):
        self.last += arrays


def place_bit(axis, mask):
    return ((lax.axis_index(axis) & mask) // mask).astype(jnp.int32).reshape(1)


class Term:
    def __init__(self, order, kind, layer, function, *arrays):
        self.order, self.kind, self.layer, self.half = order, kind, layer, None
        self.core = place_bit("wide", 1)
        sent = order.run(lambda *x: function(*x, 1 - self.core), *arrays)
        self.got = [swap(each, "wide", 1) for each in sent]
        self.columns = sent[0].shape[-1]
        self.keep = lambda: order.run(lambda *x: function(*x, self.core), *arrays)

    def stay(self):
        self.kept, self.keep = self.keep(), None

    def part(self, half):
        other = copy.copy(self)
        other.kept, other.got, other.half = self.kept[half::2], self.got[half::2], half
        return other

    def pass_narrow(self):
        stages = list(reversed(masks("narrow")))
        if isinstance(self.kept, (list, tuple)):
            bit = place_bit("narrow", stages[0])
            blocks = len(self.kept) // 2
            sent, self.kept = self.order.run(lambda *x: cross(bit, *x), *self.kept, *self.got)
            self.got = swap(sent, "narrow", stages.pop(0))
        else:
            blocks = 1
        for mask in stages:
            pairs = [(self.kept, self.got)]
            self.kept, self.got = halve(self.order, "narrow", mask, blocks, pairs, self.columns)

    def pass_wide(self, mask):
        pairs = list(zip(self.kept, self.got)) if isinstance(self.kept, (list, tuple)) else [(self.kept, self.got)]
        self.kept, self.got = halve(self.order, "wide", mask, 1, pairs, self.columns)

    def add_into(self, target, place, count):
        kept, got = [side.reshape(-1, self.columns) for side in (self.kept, self.got)]
        if target is None:
            return self.order.run(lambda one, two: add_into(None, place, count, one, two), kept, got)
        return self.order.run(lambda target, one, two: add_into(target, place, count, one, two), target, kept, got)

    def finish(self, done, own, got, begin, length):
        targets = done.get(self.kind, ())

        def last(own, got, core, *targets):
            return finish(self.kind, self.half, own, got, begin, length, core, self.layer, targets)

        done[self.kind] = self.order.run(last, own, got, self.core, *targets)


def halve(order, axis, mask, lead, pairs, columns):
    shaped = [array.reshape(lead, 2, -1, columns) for pair in pairs for array in pair]
    bit = place_bit(axis, mask)
    sent, kept = order.run(lambda *x: add_halve(bit, *x), *shaped)
    return kept, swap(sent, axis, mask)


class Reduce:
    def __init__(self, order, terms, passed=()):
        self.order, self.terms = order, terms
        self.down = [mask for mask in masks("wide")[1:] if mask not in passed]
        self.up = list(reversed(passed))
        self.pieces, self.columns = 2 ** len(passed), terms[0].columns
        self.parts = [(term.kept, term.got) for term in terms]
        self.lengths, self.first = [each.size // self.columns for each, _ in self.parts], True
        self.joining, self.closed = None, False

    def step(self):
        if self.closed:
            return
        if self.down:
            mask = self.down.pop(0)
            rows = [kept.size // self.columns for kept, _ in self.parts]
            even = all(each % 32 == 0 for each in rows)
            if self.first and even:
                self.pieces, self.lengths = 2 * self.pieces, [each // 2 for each in rows]
            self.first = False
            if even:
                self.up.insert(0, mask)
                self.parts = [halve(self.order, "wide", mask, 1, self.parts, self.columns)]
            else:
                flat = [[side.reshape(-1, self.columns) for side in pair] for pair in self.parts]
                pair = [jnp.concatenate(sides) for sides in zip(*flat)]
                total = self.order.run(add, *pair)
                self.parts = [(total, swap(total, "wide", mask))]
            return
        kept, got = [array.reshape(-1, self.columns) for array in self.parts[0]]
        if self.joining is None:
            total = self.order.run(add, kept, got)
        else:
            bit = place_bit("wide", self.joining)
            total = self.order.run(lambda *x: pair_up(*x, bit), kept, got).reshape(-1, self.columns)
        if self.up:
            self.joining = self.up.pop(0)
            self.parts = [(total, swap(total, "wide", self.joining))]
        else:
            self.parts = [(total, swap(total, "wide", 1))]
            self.closed = True

    def finish(self, done):
        own, got = [array.reshape(self.pieces, -1, self.columns) for array in self.parts[0]]
        begin = 0
        for term, length in zip(self.terms, self.lengths):
            term.finish(done, own, got, begin, length)
            begin += length


def on_device(
    tokens,
    skip,
    flags,
    cotangent,
    norm_gains,
    norm_biases,
    qkv_weight,
    out_weight,
    out_bias,
    up_weight,
    up_bias,
    down_weight,
    down_bias,
    skip_weight,
    skip_bias,
):
    items, seq_rows, width = tokens.shape
    rows = items * seq_rows
    me = lax.axis_index("narrow")
    shares = lax.axis_size("narrow")
    spots = jnp.stack([me, lax.axis_index("wide")]).astype(jnp.int32)
    order = Order()

    def fetches(layer):
        return (
            Fetch([(qkv_weight, layer)], (1, 2)),
            Fetch([(out_weight, layer), (up_weight, layer)], (1, 2)),
            Fetch([(down_weight, layer)], (1, 4)),
        )

    fetch_qkv0, fetch_up0, fetch_down0 = fetches(0)
    fetch_qkv1, fetch_up1, fetch_down1 = fetches(1)
    fetch_join = Fetch([(skip_weight, None)], (1, 4))
    qkv0, qkv1 = [Weight(each, 0, width, spots) for each in (fetch_qkv0, fetch_qkv1)]
    out0, out1 = [Weight(each, 0, width, spots) for each in (fetch_up0, fetch_up1)]
    up0, up1 = [Weight(each, 1, width, spots) for each in (fetch_up0, fetch_up1)]
    down0, down1 = [Weight(each, 0, width, spots) for each in (fetch_down0, fetch_down1)]
    join = Weight(fetch_join, 0, width, spots)

    small = (norm_gains, norm_biases, out_bias, down_bias, skip_bias, up_bias)
    held = order.run(pack_small, *small)[None]
    for mask in masks("narrow"):
        held = jnp.concatenate([held, swap(held, "narrow", mask)])
    fetch_qkv0.fetch(*order.last)
    fetch_up0.fetch(held)
    fetch_down0.fetch(fetch_up0.sent)
    place = me.astype(jnp.int32).reshape(1)
    lines = order.run(lambda x: unpack_small(x, place, small, width), held)

    def line(row):
        return lines[row : row + 1]

    gains, shifts = [[line(2 * layer + each) for each in range(2)] for layer in range(2)], None
    shifts = [[line(4 + 2 * layer + each) for each in range(2)] for layer in range(2)]
    out_biases, down_biases, join_shift = [line(8), line(9)], [line(10), line(11)], line(12)
    blocks = up0.blocks
    up_biases = [lines[13 + layer * blocks : 13 + (layer + 1) * blocks].reshape(1, -1) for layer in range(2)]

    tokens_flat, skip_flat, cotangent_flat = [array.reshape(rows, width) for array in (tokens, skip, cotangent)]
    lengths = PATCHES + 1 + CAPTION * flags
    valid = lax.broadcasted_iota(jnp.int32, (items, seq_rows), 1) < lengths[:, None]
    keep = valid.reshape(rows, 1).astype(full)
    dz1 = jnp.where(keep > 0, cotangent_flat, 0)

    fetch_qkv0.share(1)
    fetch_qkv0.share(0)
    order.hold(*fetch_up0.got())
    fetch_up0.share(1)
    a0, packed0 = order.run(lambda *x: project_qkv(*x, qkv0), tokens_flat, gains[0][0], shifts[0][0])
    order.hold(*fetch_down0.got())
    fetch_down0.share(1)
    fetch_join.fetch(a0)
    fetch_qkv1.fetch(fetch_join.sent)
    packed0 = packed0.reshape(3, items, seq_rows, width)
    mixed0, totals0 = order.run(lambda *x: attend(*x, items, seq_rows), packed0, lengths)
    fetch_up0.share(0, mixed0)
    fetch_down0.share(0, mixed0)
    fetch_up1.fetch(mixed0)
    fetch_down1.fetch(fetch_up1.sent)
    order.hold(*fetch_join.got(), *fetch_qkv1.got())
    fetch_join.share(1)
    fetch_qkv1.share(1)
    mixed0 = mixed0.reshape(rows, width)
    m0, second0, hidden0, slope0, middle = order.run(
        lambda x, o, ob, g, s, ub, db: feed_forward(x, o, out0, ob, g, s, up0, ub, down0, db),
        tokens_flat, mixed0, out_biases[0], gains[0][1], shifts[0][1], up_biases[0], down_biases[0],
    )
    fetch_join.share(0, middle)
    fetch_qkv1.share(0, middle)
    order.hold(*fetch_up1.got(), *fetch_down1.got())
    fetch_up1.share(1)
    fetch_down1.share(1)
    entry, a1, packed1 = order.run(
        lambda m, s, jb, g, sh: join_qkv(m, s, join, jb, g, sh, qkv1),
        middle, skip_flat, join_shift, gains[1][0], shifts[1][0],
    )
    packed1 = packed1.reshape(3, items, seq_rows, width)
    mixed1, totals1 = order.run(lambda *x: attend(*x, items, seq_rows), packed1, lengths)
    fetch_up1.share(0, mixed1)
    fetch_down1.share(0, mixed1)
    mixed1 = mixed1.reshape(rows, width)
    m1, second1, hidden1, slope1, output = order.run(
        lambda x, o, ob, g, s, ub, db, k: feed_forward(x, o, out1, ob, g, s, up1, ub, down1, db, k),
        entry, mixed1, out_biases[1], gains[1][1], shifts[1][1], up_biases[1], down_biases[1], keep,
    )

    done = {}
    term_down1 = Term(order, "down", 1, down_term, hidden1, dz1)
    term_down1.stay()
    term_down1.pass_narrow()
    du, dm, db, do, sums1 = order.run(
        lambda y, z, s, m, g: feed_forward_back(y, z, s, down1, up1, m, g, out1),
        dz1, dz1, slope1, m1, gains[1][1],
    )
    term_up1 = Term(order, "up", 1, up_term, second1, du)
    term_up1.stay()
    term_up1.pass_narrow()
    total = term_down1.add_into(None, 0, 3)
    dpacked = order.run(
        lambda *x: attend_back(*x, items, seq_rows), packed1, do.reshape(items, seq_rows, width), totals1, lengths
    )
    flat_packed = dpacked.reshape(3, rows, width)
    term_qkv1 = Term(order, "qkv", 1, qkv_out_term, a1, flat_packed, mixed1, db)
    term_qkv1.stay()
    term_qkv1.pass_narrow()
    total = term_up1.add_into(total, 1, 3)
    dentry, dmiddle, dz0, skip_grad, sums3 = order.run(
        lambda gp, x, g, dm: project_back(gp, qkv1, x, g, dm, join), flat_packed, entry, gains[1][0], dm
    )
    term_down0 = Term(order, "down", 0, down_term, hidden0, dz0)
    term_down0.stay()
    term_down0.pass_narrow()
    total = term_qkv1.add_into(total, 2, 3)
    size = lax.axis_size("wide")
    groups = [[device + core for device in range(0, size, 2)] for core in range(2)]
    flat_total = total.reshape(-1, width)
    part = lax.psum_scatter(flat_total, "wide", axis_index_groups=groups, scatter_dimension=0, tiled=True)
    term_join = Term(order, "join", 1, join_term, middle, skip_flat, dentry)
    term_join.stay()
    term_join.pass_narrow()

    du, dm, db, do, sums0 = order.run(
        lambda y, z, s, m, g: feed_forward_back(y, z, s, down0, up0, m, g, out0),
        dmiddle, dz0, slope0, m0, gains[0][1],
    )
    term_down0.pass_wide(2)
    term_up0 = Term(order, "up", 0, up_term, second0, du)
    term_up0.stay()
    term_up0.pass_narrow()
    dpacked = order.run(
        lambda *x: attend_back(*x, items, seq_rows), packed0, do.reshape(items, seq_rows, width), totals0, lengths
    )
    first = Reduce(order, [term_down0], (2,))
    first.step()
    flat_packed = dpacked.reshape(3, rows, width)
    term_qkv0 = Term(order, "qkv", 0, qkv_out_term, a0, flat_packed, mixed0, db)
    term_qkv0.stay()
    one, two = term_qkv0.part(0), term_qkv0.part(1)
    early = 4 if shares == 2 else None
    order.hold(part)
    gathered = lax.all_gather(part, "wide", axis_index_groups=groups, tiled=True)
    first.step()
    second = Reduce(order, [term_up0, term_join])
    second.step()
    if early:
        two.pass_wide(early)
    one.pass_narrow()
    first.step()
    tokens_grad, sums2 = order.run(
        lambda gp, x, g, dm: project_back(gp, qkv0, x, g, dm), flat_packed, tokens_flat, gains[0][0], dm
    )
    minor = jnp.concatenate([sums2, sums3, sums0, sums1])
    minor_stages = [("narrow", mask) for mask in masks("narrow")] + [("wide", mask) for mask in masks("wide")]
    minor_got = swap(minor, *minor_stages[0])

    def minor_step():
        nonlocal minor, minor_got
        if minor_stages:
            minor_stages.pop(0)
            minor = order.run(lambda one, two: one + two, minor, minor_got)
            if minor_stages:
                minor_got = swap(minor, *minor_stages[0])

    two.pass_narrow()
    second.step()
    first.step()
    third = Reduce(order, [one])
    third.step()
    fourth = Reduce(order, [two], (early,) if early else ())
    fourth.step()
    second.step()
    third.step()
    first.step()
    fourth.step()
    minor_step()
    second.step()
    third.step()
    fourth.step()
    first.step()
    minor_step()
    second.step()
    first.finish(done)
    fourth.step()
    third.step()
    order.hold(gathered)
    other = swap(after(gathered, *order.last), "wide", 1)
    minor_step()
    second.step()
    fourth.step()
    third.step()
    minor_step()
    own, got = gathered.reshape(1, -1, width), other.reshape(1, -1, width)
    for which, term in enumerate((term_down1, term_up1, term_qkv1)):
        term.finish(done, own, got, which * (own.shape[1] // 3), own.shape[1] // 3)
    fourth.step()
    third.step()
    second.step()
    fourth.finish(done)
    minor_step()
    third.step()
    second.finish(done)
    for each in (first, second, third, fourth):
        while not each.closed:
            each.step()
    while minor_stages:
        minor_step()
    third.finish(done)
    small = order.run(lambda x: small_gradients(x, place, width, shares, up1.blocks), minor)

    return (
        output.reshape(tokens.shape),
        tokens_grad.reshape(tokens.shape),
        skip_grad.reshape(tokens.shape),
        small[0],
        small[1],
        done["qkv"][0],
        done["qkv"][1],
        small[2],
        done["up"][0],
        small[3],
        done["down"][0],
        small[4],
        done["join"][0][0],
        small[5].reshape(-1),
    )


def solution(mesh):
    placed = (
        P(("wide", "narrow"), None, None),
        P(("wide", "narrow"), None, None),
        P(("wide", "narrow")),
        P(("wide", "narrow"), None, None),
        P(None, None, "narrow"),
        P(None, None, "narrow"),
        P(None, "narrow", None),
        P(None, "narrow", None),
        P(None, "narrow"),
        P(None, "narrow", None),
        P(None, "narrow"),
        P(None, "narrow", None),
        P(None, "narrow"),
        P("narrow", None),
        P("narrow"),
    )
    return jax.shard_map(
        on_device,
        mesh=mesh,
        in_specs=placed,
        out_specs=(
            P(("wide", "narrow"), None, None),
            P(("wide", "narrow"), None, None),
            P(("wide", "narrow"), None, None),
            P(None, None, "narrow"),
            P(None, None, "narrow"),
            P(None, "narrow", None),
            P(None, "narrow", None),
            P(None, "narrow"),
            P(None, "narrow", None),
            P(None, "narrow"),
            P(None, "narrow", None),
            P(None, "narrow"),
            P("narrow", None),
            P("narrow"),
        ),
        check_vma=False,
    )
```

```python
import copy

import jax
import jax.numpy as jnp
from jax import lax
from jax.experimental import pallas as pl
from jax.experimental.pallas import tpu as pltpu
from jax.sharding import PartitionSpec as P

HEAD_DIM = 64
PATCHES = 256
CAPTION = 77
PAIR = 2 * HEAD_DIM


epsilon = 1e-05
masked_score = -1e30
low = jnp.bfloat16
full = jnp.float32
ANY = pl.BlockSpec(memory_space=pl.ANY)
SCALARS = pl.BlockSpec(memory_space=pltpu.SMEM)


def dot(left, right, contract=(1, 0)):
    dims = (((contract[0],), (contract[1],)), ((), ()))
    return lax.dot_general(left, right, dims, preferred_element_type=full)


def normalize(values):
    centred = values - jnp.mean(values, axis=-1, keepdims=True)
    factor = lax.rsqrt(jnp.mean(centred * centred, axis=-1, keepdims=True) + epsilon)
    return centred * factor, factor


def normalize_back(upstream, normed, factor):
    return factor * (
        upstream
        - jnp.mean(upstream, axis=-1, keepdims=True)
        - normed * jnp.mean(upstream * normed, axis=-1, keepdims=True)
    )


def column_sum(values):
    return jnp.sum(values.astype(full), axis=0, keepdims=True)


def whole(shape):
    return pl.BlockSpec(shape, lambda *grid: (0,) * len(shape))


def cost(micros):
    return pl.CostEstimate(flops=int(micros * 3 * 10**8), bytes_accessed=0, transcendentals=0)


def call(body, grid, ins, outs, name, micros, scratch=(), limit=56):
    return pl.pallas_call(
        body,
        grid=grid,
        in_specs=[spec for _, spec in ins],
        out_specs=[spec for _, _, spec in outs],
        out_shape=[jax.ShapeDtypeStruct(shape, kind) for shape, kind, _ in outs],
        scratch_shapes=list(scratch),
        name=name,
        cost_estimate=cost(micros),
        compiler_params=pltpu.CompilerParams(vmem_limit_bytes=limit * 2**20),
    )(*[array for array, _ in ins])


class Fetch:
    def __init__(self, arrays, sharing):
        self.arrays, self.sharing = arrays, list(sharing)
        self.rows = arrays[0][0].shape[-2]
        while self.rows % (16 << len(self.sharing)):
            self.sharing.pop()
        self.length = self.rows >> len(self.sharing)

    def quarter(self, place):
        return sum(((place // mask) & 1) << bit for bit, mask in enumerate(self.sharing))

    def fetch(self, *earlier):
        found = []
        for array, layer in self.arrays:
            array = after(array, *earlier)
            lead = () if layer is None else (layer,)
            begin = self.quarter(lax.axis_index("wide")) * self.length
            sizes = (1,) * len(lead) + (self.length, array.shape[-1])
            found.append(lax.dynamic_slice(array, lead + (begin, 0), sizes).reshape(self.length, -1))
        self.sent = (jnp.concatenate(found, axis=1) if len(found) > 1 else found[0])[None]
        held = self.sent
        for mask in masks("narrow"):
            held = jnp.concatenate([held, swap(held, "narrow", mask)])
        self.pieces = {0: held[1:]}

    def share(self, which, *earlier):
        if which < len(self.sharing):
            mask = self.sharing[which]
            got = {key ^ (1 << which): swap(after(piece, *earlier), "wide", mask) for key, piece in self.pieces.items()}
            self.pieces.update(got)

    def got(self):
        return list(self.pieces.values())


class Weight:
    def __init__(self, fetched, which, width, spots):
        self.fetched, self.spots, self.width = fetched, spots, width
        self.array, self.layer = fetched.arrays[which]
        self.begin = sum(array.shape[-1] for array, _ in fetched.arrays[:which])
        self.rows, columns = self.array.shape[-2:]
        self.shares = lax.axis_size("narrow")
        self.blocks = columns // width
        self.total = self.rows * self.shares

    def arrays(self):
        return [self.array] + self.fetched.got()

    def scratch(self):
        copies = 1 + len(self.fetched.pieces) * (self.shares - 1)
        return [pltpu.VMEM((self.blocks, self.total, self.width), low), pltpu.SemaphoreType.DMA((self.blocks, copies))]

    def copies(self, spots, refs, held, signals, block):
        own, pieces = refs[0], refs[1:]
        me, length = spots[0], self.fetched.length
        own = own if self.layer is None else own.at[self.layer]
        columns = pl.ds(block * self.width, self.width)
        begin = pl.multiple_of(me * self.rows, 16)
        found = [(own.at[:, columns], begin, self.rows)]
        columns = pl.ds(self.begin + block * self.width, self.width)
        for key, piece in zip(self.fetched.pieces, pieces):
            for offset in range(1, self.shares):
                begin = (me ^ offset) * self.rows + (self.fetched.quarter(spots[1]) ^ key) * length
                found.append((piece.at[offset - 1, :, columns], pl.multiple_of(begin, 16), length))
        return [
            pltpu.make_async_copy(source, held.at[block, pl.ds(begin, length)], signals.at[block, place])
            for place, (source, begin, length) in enumerate(found)
        ]

    def wait(self, *refs, block=0):
        for copy in self.copies(*refs, block):
            copy.wait()


def weighted(body, weights, grid, ins, outs, name, micros, scratch=(), first=((0, 0),)):
    spots = weights[0].spots
    operands = [(spots, SCALARS)] + [(array, ANY) for weight in weights for array in weight.arrays()]
    counts = [len(weight.arrays()) for weight in weights]
    extra = [piece for weight in weights for piece in weight.scratch()]

    def wrapped(*refs):
        spots_ref, rest = refs[0], list(refs[1:])
        sources = []
        for count in counts:
            sources.append(rest[:count])
            rest = rest[count:]
        spare = rest[len(rest) - len(extra) :]
        rest = rest[: len(rest) - len(extra)]
        handles = []
        for place, weight in enumerate(weights):
            held, signals = spare[2 * place : 2 * place + 2]
            refs_of = (spots_ref, sources[place], held, signals)
            handles.append((weight, refs_of, held))

        everything = [(place, block) for place, weight in enumerate(weights) for block in range(weight.blocks)]

        def begin(wanted):
            for place, block in wanted:
                weight, refs_of, _ = handles[place]
                for copy in weight.copies(*refs_of, block):
                    copy.start()

        @pl.when(pl.program_id(0) == 0)
        def _():
            begin(first)

        def ready(place, block=0, then=False):
            weight, refs_of, held = handles[place]
            weight.wait(*refs_of, block=block)
            if then:
                begin([each for each in everything if each not in first])

        body(ready, [held for _, _, held in handles], *rest)

    return call(wrapped, grid, operands + ins, outs, name, micros, list(scratch) + extra)


def pack_small(*small):
    part = small[0].shape[-1]
    counts = [piece.size // part for piece in small]

    def body(*refs):
        row = 0
        for ref in refs[:-1]:
            values = ref[...].reshape(-1, ref.shape[-1])
            for each in range(values.shape[0]):
                for begin in range(0, values.shape[1], part):
                    refs[-1][row : row + 1] = values[each : each + 1, begin : begin + part].astype(full)
                    row += 1
        refs[-1][row:] = jnp.zeros((refs[-1].shape[0] - row, part), full)

    flat = [piece.reshape((1,) * (2 - piece.ndim) + piece.shape) for piece in small]
    rows = -(-sum(counts) // 16) * 16
    out = ((rows, part), full, whole((rows, part)))
    return call(body, (1,), [(piece, whole(piece.shape)) for piece in flat], [out], "pack_small", 1)[0].astype(low)


def unpack_small(parts, me, small, width):
    shares, _, part = parts.shape
    lines = [(piece.size // piece.shape[-1], piece.shape[-1] // part) for piece in small]
    total = sum(count * many for count, many in lines)
    rows = -(-total // 8) * 8

    def body(me_ref, parts_ref, out_ref):
        values = parts_ref[...].astype(full)
        for mine in range(shares):

            @pl.when(me_ref[0] == mine)
            def _():
                for owner in range(shares):
                    source, target = 0, 0
                    for count, many in lines:
                        for each in range(count):
                            for piece in range(many):
                                at = owner * many * part + piece * part
                                row, column = target + at // width, at % width
                                line = values[owner ^ mine, source : source + 1]
                                out_ref[row : row + 1, column : column + part] = line
                                source += 1
                            target += many
        if rows > total:
            out_ref[total:] = jnp.zeros((rows - total, width), full)

    ins = [(parts, pl.BlockSpec(parts.shape, lambda g, me: (0, 0, 0)))]
    out = ((rows, width), full, pl.BlockSpec((rows, width), lambda g, me: (0, 0)))
    return picked(body, me, (1,), ins, [out], "unpack_small", 1)[0]


def project_qkv(inputs, gain, shift, weight):
    rows, width = inputs.shape

    def body(ready, held, x_ref, gain_ref, shift_ref, a_ref, out_ref):
        step = pl.program_id(0)

        @pl.when(step == 0)
        def _():
            normed, _ = normalize(x_ref[...].astype(full))
            a_ref[...] = (normed * gain_ref[...] + shift_ref[...]).astype(low)
            ready(0, 0, then=True)

        @pl.when(step > 0)
        def _():
            ready(0, step)

        scale = jnp.where(step == 0, HEAD_DIM ** (-0.5), 1.0)
        out_ref[0] = (dot(a_ref[...], held[0][step]).astype(low).astype(full) * scale).astype(low)

    return weighted(
        body,
        [weight],
        (3,),
        [
            (inputs, whole((rows, width))),
            (gain, whole((1, width))),
            (shift, whole((1, width))),
        ],
        [
            ((rows, width), low, whole((rows, width))),
            ((3, rows, width), low, pl.BlockSpec((1, rows, width), lambda j: (j, 0, 0))),
        ],
        "project_qkv",
        7,
    )


def join_qkv(middle, skip, join_weight, join_shift, gain, shift, weight):
    rows, width = middle.shape

    def body(ready, held, m_ref, s_ref, jb_ref, gain_ref, shift_ref, e_ref, a_ref, out_ref):
        step = pl.program_id(0)

        @pl.when(step == 0)
        def _():
            ready(0, then=True)
            entry = dot(m_ref[...], held[0][0, :width]) + dot(s_ref[...], held[0][0, width:]) + jb_ref[...]
            e_ref[...] = entry
            normed, _ = normalize(entry)
            a_ref[...] = (normed * gain_ref[...] + shift_ref[...]).astype(low)

        ready(1, step)
        scale = jnp.where(step == 0, HEAD_DIM ** (-0.5), 1.0)
        out_ref[0] = (dot(a_ref[...], held[1][step]).astype(low).astype(full) * scale).astype(low)

    return weighted(
        body,
        [join_weight, weight],
        (3,),
        [
            (middle, whole((rows, width))),
            (skip, whole((rows, width))),
            (join_shift, whole((1, width))),
            (gain, whole((1, width))),
            (shift, whole((1, width))),
        ],
        [
            ((rows, width), full, whole((rows, width))),
            ((rows, width), low, whole((rows, width))),
            ((3, rows, width), low, pl.BlockSpec((1, rows, width), lambda j: (j, 0, 0))),
        ],
        "join_qkv",
        11,
        first=((0, 0), (1, 0)),
    )


def head_masks(seq_rows):
    lane = lax.broadcasted_iota(jnp.int32, (seq_rows, PAIR), 1)
    return [lane < HEAD_DIM, lane >= HEAD_DIM]


def attend(packed, lengths, items, seq_rows):
    width = packed.shape[-1]
    pairs = width // PAIR

    def body(length_ref, q_ref, k_ref, v_ref, out_ref, total_ref):
        length = length_ref[pl.program_id(0)]
        queries, keys, values = q_ref[0, 0], k_ref[0, 0], v_ref[0, 0]
        counts = lax.broadcasted_iota(jnp.int32, (seq_rows, seq_rows), 0) < length
        mixed = jnp.zeros((PAIR, seq_rows), full)
        for head, lanes in enumerate(head_masks(seq_rows)):
            scores = dot(keys, jnp.where(lanes, queries, 0), (1, 1))
            scores = jnp.where(counts, scores, masked_score)
            largest = jnp.max(scores, axis=0, keepdims=True)
            weights = jnp.exp(scores - largest)
            total = jnp.sum(weights, axis=0, keepdims=True)
            part = dot(jnp.where(lanes, values, 0), weights.astype(low), (0, 0))
            mixed += part * (1.0 / total)
            total_ref[0, 0, head : head + 1] = largest + jnp.log(total)
        out_ref[0] = mixed.T.astype(low)

    def block(which):
        return pl.BlockSpec((1, 1, seq_rows, PAIR), lambda n, h: (which, n, 0, h))

    return call(
        body,
        (items, pairs),
        [
            (lengths, SCALARS),
            (packed, block(0)),
            (packed, block(1)),
            (packed, block(2)),
        ],
        [
            ((items, seq_rows, width), low, pl.BlockSpec((1, seq_rows, PAIR), lambda n, h: (n, 0, h))),
            ((items, pairs, 8, seq_rows), full, pl.BlockSpec((1, 1, 8, seq_rows), lambda n, h: (n, h, 0, 0))),
        ],
        "attend",
        13,
    )


def attend_back(packed, grad_mixed, totals, lengths, items, seq_rows):
    width = packed.shape[-1]
    pairs = width // PAIR

    def body(length_ref, q_ref, k_ref, v_ref, g_ref, total_ref, out_ref):
        length = length_ref[pl.program_id(0)]
        queries, keys, values, upstream = q_ref[0, 0], k_ref[0, 0], v_ref[0, 0], g_ref[0]
        counts = lax.broadcasted_iota(jnp.int32, (seq_rows, seq_rows), 0) < length
        grad_queries = jnp.zeros((PAIR, seq_rows), full)
        grad_keys = jnp.zeros((seq_rows, PAIR), full)
        grad_values = jnp.zeros((seq_rows, PAIR), full)
        for head, lanes in enumerate(head_masks(seq_rows)):
            own_queries = jnp.where(lanes, queries, 0)
            own_upstream = jnp.where(lanes, upstream, 0)
            scores = dot(keys, own_queries, (1, 1))
            shifted = jnp.where(counts, scores, masked_score) - total_ref[0, 0, head : head + 1]
            probs = jnp.exp(shifted)
            grad_probs = dot(values, own_upstream, (1, 1))
            centre = jnp.sum(grad_probs * probs, axis=0, keepdims=True)
            grad_scores = (probs * (grad_probs - centre)).astype(low)
            grad_values += dot(probs.astype(low), own_upstream)
            grad_keys += dot(grad_scores, own_queries)
            grad_queries += dot(jnp.where(lanes, keys, 0), grad_scores, (0, 0))
        out_ref[0, 0] = (grad_queries.T * HEAD_DIM ** (-0.5)).astype(low)
        out_ref[1, 0] = grad_keys.astype(low)
        out_ref[2, 0] = grad_values.astype(low)

    def block(which):
        return pl.BlockSpec((1, 1, seq_rows, PAIR), lambda n, h: (which, n, 0, h))

    return call(
        body,
        (items, pairs),
        [
            (lengths, SCALARS),
            (packed, block(0)),
            (packed, block(1)),
            (packed, block(2)),
            (grad_mixed, pl.BlockSpec((1, seq_rows, PAIR), lambda n, h: (n, 0, h))),
            (totals, pl.BlockSpec((1, 1, 8, seq_rows), lambda n, h: (n, h, 0, 0))),
        ],
        [
            ((3, items, seq_rows, width), low, pl.BlockSpec((3, 1, seq_rows, PAIR), lambda n, h: (0, n, 0, h))),
        ],
        "attend_back",
        17,
    )[0]


def gelu_parts(before):
    decay = jnp.exp(before * before * -0.5)
    inverse = pl.reciprocal(1.0 + (0.3275911 * 0.5**0.5) * jnp.abs(before), approx=False)
    series = 1.061405429 * 0.5
    for term in (-1.453152027, 1.421413741, -0.284496736, 0.254829592):
        series = series * inverse + term * 0.5
    below = series * inverse * decay
    share = jnp.where(before >= 0, 1.0 - below, below)
    return before * share, share + before * decay * 0.3989422804014327


def feed_forward(inputs, mixed, out_weight, out_bias, gain, shift, up_weight, up_bias, down_weight, down_bias, keep=None):
    rows, width = inputs.shape
    steps = up_weight.blocks
    hidden = steps * width

    def body(ready, held, x_ref, o_ref, ob_ref, gain_ref, shift_ref, ub_ref, db_ref, *rest):
        m_ref, a_ref, g_ref, s_ref, y_ref, total = rest[-6:]
        step = pl.program_id(0)

        @pl.when(step == 0)
        def _():
            ready(0, then=True)
            middle = x_ref[...].astype(full) + dot(o_ref[...], held[0][0]) + ob_ref[...]
            m_ref[...] = middle
            normed, _ = normalize(middle)
            a_ref[...] = (normed * gain_ref[...] + shift_ref[...]).astype(low)
            total[...] = middle + db_ref[...]

        ready(1, step)
        before = dot(a_ref[...], held[1][step]) + ub_ref[...]
        value, slope = gelu_parts(before)
        g_ref[...] = value.astype(low)
        s_ref[...] = slope.astype(low)

        @pl.when(step == 0)
        def _():
            ready(2)

        total[...] += dot(g_ref[...], held[2][0, pl.ds(pl.multiple_of(step * width, width), width)])

        @pl.when(step == steps - 1)
        def _():
            value = total[...]
            if keep is not None:
                value = jnp.where(rest[0][...] > 0, value, 0.0)
            y_ref[...] = value.astype(low)

    return weighted(
        body,
        [out_weight, up_weight, down_weight],
        (steps,),
        [
            (inputs, whole((rows, width))),
            (mixed, whole((rows, width))),
            (out_bias, whole((1, width))),
            (gain, whole((1, width))),
            (shift, whole((1, width))),
            (up_bias, pl.BlockSpec((1, width), lambda j: (0, j))),
            (down_bias, whole((1, width))),
        ]
        + ([] if keep is None else [(keep, whole((rows, 1)))]),
        [
            ((rows, width), full, whole((rows, width))),
            ((rows, width), low, whole((rows, width))),
            ((rows, hidden), low, pl.BlockSpec((rows, width), lambda j: (0, j))),
            ((rows, hidden), low, pl.BlockSpec((rows, width), lambda j: (0, j))),
            ((rows, width), low, whole((rows, width))),
        ],
        "feed_forward",
        23,
        scratch=[pltpu.VMEM((rows, width), full)],
        first=((0, 0), (1, 0)),
    )


def feed_forward_back(upstream, rounded, slope, down_weight, up_weight, middle, gain, out_weight):
    rows, width = upstream.shape
    steps = up_weight.blocks
    hidden = steps * width

    def body(ready, held, y_ref, dz_ref, s_ref, m_ref, gain_ref, du_ref, dm_ref, db_ref, do_ref, sums_ref, total):
        step = pl.program_id(0)

        @pl.when(step == 0)
        def _():
            sums_ref[0:1] = column_sum(dz_ref[...])
            total[...] = jnp.zeros_like(total)
            ready(0, then=True)

        down = held[0][0, pl.ds(pl.multiple_of(step * width, width), width)]
        grad = (dot(dz_ref[...], down, (1, 1)) * s_ref[...].astype(full)).astype(low)
        du_ref[...] = grad
        sums_ref[pl.ds(4 + step, 1)] = column_sum(grad)
        ready(1, step)
        total[...] += dot(grad, held[1][step], (1, 1))

        @pl.when(step == steps - 1)
        def _():
            grad_second = total[...]
            normed, factor = normalize(m_ref[...])
            sums_ref[1:2] = column_sum(grad_second * normed)
            sums_ref[2:3] = column_sum(grad_second)
            grad_middle = y_ref[...].astype(full) + normalize_back(grad_second * gain_ref[...], normed, factor)
            dm_ref[...] = grad_middle
            branch = grad_middle.astype(low)
            db_ref[...] = branch
            sums_ref[3:4] = column_sum(branch)
            ready(2)
            do_ref[...] = dot(branch, held[2][0], (1, 1)).astype(low)

    return weighted(
        body,
        [down_weight, up_weight, out_weight],
        (steps,),
        [
            (upstream, whole((rows, width))),
            (rounded, whole((rows, width))),
            (slope, pl.BlockSpec((rows, width), lambda j: (0, j))),
            (middle, whole((rows, width))),
            (gain, whole((1, width))),
        ],
        [
            ((rows, hidden), low, pl.BlockSpec((rows, width), lambda j: (0, j))),
            ((rows, width), full, whole((rows, width))),
            ((rows, width), low, whole((rows, width))),
            ((rows, width), low, whole((rows, width))),
            ((4 + steps, width), full, whole((4 + steps, width))),
        ],
        "feed_forward_back",
        21,
        scratch=[pltpu.VMEM((rows, width), full)],
        first=((0, 0), (1, 0)),
    )


def project_back(grad_packed, weight, inputs, gain, grad_middle, join_weight=None):
    rows, width = inputs.shape
    joined = join_weight is not None

    def body(ready, held, g_ref, x_ref, gain_ref, dm_ref, *rest):
        if joined:
            de_ref, dx_ref, dz_ref, skip_ref, sums_ref, total = rest
        else:
            dx_ref, sums_ref, total = rest
        step = pl.program_id(0)

        @pl.when(step == 0)
        def _():
            total[...] = jnp.zeros_like(total)
            ready(0, 0, then=True)

        @pl.when(step > 0)
        def _():
            ready(0, step)

        total[...] += dot(g_ref[0], held[0][step], (1, 1))

        @pl.when(step == 2)
        def _():
            grad_first = total[...]
            normed, factor = normalize(x_ref[...].astype(full))
            sums_ref[0:1] = column_sum(grad_first * normed)
            sums_ref[1:2] = column_sum(grad_first)
            grad = dm_ref[...] + normalize_back(grad_first * gain_ref[...], normed, factor)
            if joined:
                entry = grad.astype(low)
                de_ref[...] = entry
                sums_ref[2:3] = column_sum(entry)
                ready(1)
                grad = dot(entry, held[1][0, :width], (1, 1))
                dx_ref[...] = grad
                dz_ref[...] = grad.astype(low)
                skip_ref[...] = dot(entry, held[1][0, width:], (1, 1))
            else:
                dx_ref[...] = grad

    ins = [
        (grad_packed, pl.BlockSpec((1, rows, width), lambda j: (j, 0, 0))),
        (inputs, whole((rows, width))),
        (gain, whole((1, width))),
        (grad_middle, whole((rows, width))),
    ]
    outs = [((rows, width), full, whole((rows, width))), ((8, width), full, whole((8, width)))]
    if joined:
        rounded = ((rows, width), low, whole((rows, width)))
        outs = [rounded, outs[0], rounded, outs[0], outs[1]]
    return weighted(
        body,
        [weight] + ([join_weight] if joined else []),
        (3,),
        ins,
        outs,
        "project_back",
        13 if joined else 9,
        scratch=[pltpu.VMEM((rows, width), full)],
    )


def picked(body, which, grid, ins, outs, name, micros, aliases=None):
    return pl.pallas_call(
        body,
        grid_spec=pltpu.PrefetchScalarGridSpec(
            num_scalar_prefetch=1,
            grid=grid,
            in_specs=[spec for _, spec in ins],
            out_specs=[spec for _, _, spec in outs],
        ),
        out_shape=[jax.ShapeDtypeStruct(shape, kind) for shape, kind, _ in outs],
        name=name,
        input_output_aliases={place + 1: out for place, out in (aliases or {}).items()},
        cost_estimate=cost(micros),
        compiler_params=pltpu.CompilerParams(vmem_limit_bytes=48 * 2**20),
    )(which, *[array for array, _ in ins])


def quarters(rows, width, narrow_rows):
    shape = (lax.axis_size("narrow") // 2 * narrow_rows, width)
    return [(shape, low, pl.BlockSpec(shape, lambda g, core: (0, 0)))] * 4


def up_term(left, right, core):
    rows, width = left.shape
    part = width // lax.axis_size("narrow")
    half = width // 2

    def body(core_ref, l_ref, r_ref, *outs):
        value = dot(l_ref[...], r_ref[...], (0, 0)).astype(low)
        for block in range(2):

            @pl.when(pl.program_id(0) == block)
            def _():
                outs[block][...] = value[:half]
                outs[2 + block][...] = value[half:]

    return picked(
        body,
        core,
        (2,),
        [
            (left, pl.BlockSpec((rows, width), lambda g, core: (0, 0))),
            (right, pl.BlockSpec((rows, width), lambda g, core: (0, core[0] * 2 + g))),
        ],
        quarters(rows, width, part),
        "up_term",
        3.5,
    )


def qkv_out_term(first, packed, mixed, branch, core):
    rows, width = first.shape
    part = width // lax.axis_size("narrow")
    half = width // 2

    def body(core_ref, l_ref, r_ref, o_ref, b_ref, *outs):
        step = pl.program_id(0)
        last = core_ref[0] * 2 + step == 3

        def put(block, value):
            outs[block][...] = value[:half]
            outs[2 + block][...] = value[half:]

        @pl.when(last)
        def _():
            put(1, dot(o_ref[...], b_ref[...], (0, 0)).astype(low))

        @pl.when(jnp.logical_not(last))
        def _():
            value = dot(l_ref[...], r_ref[0], (0, 0)).astype(low)
            for block in range(2):

                @pl.when(step == block)
                def _():
                    put(block, value)

    flat = pl.BlockSpec((rows, width), lambda g, core: (0, 0))
    return picked(
        body,
        core,
        (2,),
        [
            (first, flat),
            (packed, pl.BlockSpec((1, rows, width), lambda g, core: (jnp.minimum(core[0] * 2 + g, 2), 0, 0))),
            (mixed, flat),
            (branch, flat),
        ],
        quarters(rows, width, part),
        "qkv_out_term",
        3.5,
    )


def down_term(left, right, core):
    rows, width = right.shape
    shares = lax.axis_size("narrow")
    part = left.shape[1] // (2 * shares)
    direct = part == width
    if not direct:
        left = left.reshape(rows, shares, 2, 2, part // 2)
        left = lax.dynamic_index_in_dim(left, core[0], 2, keepdims=False)
        left = left.reshape(rows, 2, shares // 2, 2, part // 2).swapaxes(2, 3).reshape(rows, 2 * width)
    half = width // 2

    def body(core_ref, l_ref, r_ref, *outs):
        value = dot(l_ref[...], r_ref[...], (0, 0)).astype(low)
        for owner in range(2):

            @pl.when(pl.program_id(0) == owner)
            def _():
                outs[2 * owner][...] = value[:half]
                outs[2 * owner + 1][...] = value[half:]

    return picked(
        body,
        core,
        (2,),
        [
            (left, pl.BlockSpec((rows, width), lambda g, core: (0, g * 2 + core[0] if direct else g))),
            (right, pl.BlockSpec((rows, width), lambda g, core: (0, 0))),
        ],
        quarters(rows, width, part // 2),
        "down_term",
        3.5,
    )


def join_term(middle, skip, right, core):
    rows, width = right.shape
    shares = lax.axis_size("narrow")
    part = width // shares
    half = width // 2
    if part != half:
        left = jnp.concatenate([middle, skip], axis=1).reshape(rows, shares, 2, 2, part // 2)
        left = lax.dynamic_index_in_dim(left, core[0], 2, keepdims=False)
        left = left.reshape(rows, 2, shares // 2, 2, part // 2).swapaxes(2, 3).reshape(rows, width)
        middle, skip = left[:, :half], left[:, half:]

    def body(core_ref, m_ref, s_ref, r_ref, *outs):
        for owner, left_ref in enumerate((m_ref, s_ref)):
            value = dot(left_ref[...], r_ref[...], (0, 0)).astype(low)
            outs[2 * owner][...] = value[: half // 2]
            outs[2 * owner + 1][...] = value[half // 2 :]

    side = pl.BlockSpec((rows, half), lambda g, core: (0, core[0] if part == half else 0))
    return picked(
        body,
        core,
        (1,),
        [(middle, side), (skip, side), (right, pl.BlockSpec((rows, width), lambda g, core: (0, 0)))],
        quarters(rows, width, part // 2),
        "join_term",
        2,
    )


def cross(bit, *pieces):
    kept, got = pieces[: len(pieces) // 2], pieces[len(pieces) // 2 :]
    rows, columns = kept[0].shape
    blocks = len(kept) // 2
    steps = 2 if rows % 32 == 0 else 1

    def body(bit_ref, *refs):
        sent_ref, left_ref = refs[-2:]

        def put(target, owner):
            for block in range(blocks):
                place = owner * blocks + block
                one, two = refs[place], refs[2 * blocks + place]
                target[block] = (one[...].astype(full) + two[...].astype(full)).astype(low)

        for mine in range(2):

            @pl.when(bit_ref[0] == mine)
            def _():
                put(sent_ref, 1 - mine)
                put(left_ref, mine)

    ins = [(piece, pl.BlockSpec((rows // steps, columns), lambda g, bit: (g, 0))) for piece in kept + got]
    out = ((blocks, rows, columns), low, pl.BlockSpec((blocks, rows // steps, columns), lambda g, bit: (0, g, 0)))
    return picked(body, bit, (steps,), ins, [out, out], "cross", 2)


def add_halve(bit, *pairs):
    lead, columns = pairs[0].shape[0], pairs[0].shape[-1]
    sizes = [pair.shape[2] for pair in pairs[::2]]
    total = sum(sizes)
    steps = 2 if len(sizes) == 1 and total % 32 == 0 and total >= 256 else 1

    def body(bit_ref, *refs):
        mine = bit_ref[0]
        for target, place in ((refs[-2], 1 - mine), (refs[-1], mine)):
            begin = 0
            for kept_ref, got_ref in zip(refs[:-2:2], refs[1:-2:2]):
                length = kept_ref.shape[2]
                for each in range(lead):
                    value = kept_ref[each, place].astype(full) + got_ref[each, place].astype(full)
                    target[each, begin : begin + length] = value.astype(low)
                begin += length

    ins = [
        (pair, pl.BlockSpec((lead, 2, pair.shape[2] // steps, columns), lambda g, bit: (0, 0, g, 0)))
        for pair in pairs
    ]
    out = (
        (lead, total, columns),
        low,
        pl.BlockSpec((lead, total // steps, columns), lambda g, bit: (0, g, 0)),
    )
    return picked(body, bit, (steps,), ins, [out, out], "add_halve", 2)


def add_into(target, place, count, one, two):
    rows, columns = one.shape[-2:]
    steps = 2 if rows % 32 == 0 else 1
    block = pl.BlockSpec((1, rows // steps, columns), lambda g: (0, g, 0))

    def body(one_ref, two_ref, *rest):
        rest[-1][...] = (one_ref[...].astype(full) + two_ref[...].astype(full)).astype(low)

    ins = [one.reshape(1, rows, columns), two.reshape(1, rows, columns)]
    return pl.pallas_call(
        body,
        grid=(steps,),
        in_specs=[block, block] + ([] if target is None else [ANY]),
        out_specs=pl.BlockSpec((1, rows // steps, columns), lambda g: (place, g, 0)),
        out_shape=jax.ShapeDtypeStruct((count, rows, columns), low),
        name="add_into",
        input_output_aliases={} if target is None else {2: 0},
        cost_estimate=cost(1.3),
    )(*ins, *([] if target is None else [target]))


def add(one, two):
    return (one.astype(full) + two.astype(full)).astype(low)


def pair_up(own, got, bit):
    rows, columns = own.shape

    def body(bit_ref, own_ref, got_ref, out_ref):
        mine = bit_ref[0]
        out_ref[mine] = own_ref[...]
        out_ref[1 - mine] = got_ref[...]

    flat = pl.BlockSpec((rows, columns), lambda g, bit: (0, 0))
    out = ((2, rows, columns), low, pl.BlockSpec((2, rows, columns), lambda g, bit: (0, 0, 0)))
    return picked(body, bit, (1,), [(own, flat), (got, flat)], [out], "pair_up", 1)[0]


def finish(kind, half, own, got, begin, length, core, layer, targets):
    pieces, _, columns = own.shape
    scale = 1.0 / lax.axis_size("wide")
    aliases = {place + 2: place for place in range(len(targets))}
    source = pl.BlockSpec((pieces, length, columns), lambda g, core: (0, begin // length, 0))
    ins = [(own, source), (got, source)] + [(target, ANY) for target in targets]
    rows = pieces * length

    def chosen(core_ref, which, own_ref, got_ref, place=None):
        sides = [own_ref, got_ref]
        if place is None:
            values = [side[...].reshape(pieces * length, columns) for side in sides]
        else:
            if pieces == 1:
                near = (0, pl.ds(place * (length // 2), length // 2))
            else:
                near = (pl.ds(place * (pieces // 2), pieces // 2),)
            values = [side[near].reshape(pieces * length // 2, columns) for side in sides]
        return jnp.where(core_ref[0] == which, values[0], values[1]).astype(full) * scale

    if kind in ("down", "join"):

        def body(core_ref, own_ref, got_ref, *rest):
            rest[-1][0] = chosen(core_ref, pl.program_id(0), own_ref, got_ref)

        place = layer if kind == "down" else 0
        shape = (2 if kind == "down" else 1, 2 * rows, columns)
        out = (shape, full, pl.BlockSpec((1, rows, columns), lambda g, core: (place, g, 0)))
        return picked(body, core, (2,), ins, [out], "finish_rows", 3, aliases)
    steps = 4 if half is None else 2
    rows = rows // 2 if half is None else rows

    def block(step):
        return step if half is None else 2 * step + half

    def values_of(core_ref, own_ref, got_ref):
        step = pl.program_id(0)
        if half is None:
            return chosen(core_ref, step // 2, own_ref, got_ref, step % 2)
        return chosen(core_ref, step, own_ref, got_ref)

    def body(core_ref, own_ref, got_ref, *rest):
        values = values_of(core_ref, own_ref, got_ref)
        if kind == "up":
            rest[-1][0] = values
            return
        if half == 0:
            rest[-1][0] = values
            return
        last = block(pl.program_id(0)) == 3

        @pl.when(jnp.logical_not(last))
        def _():
            rest[-2][0] = values

        @pl.when(last)
        def _():
            rest[-1][0] = values

    if kind == "up":
        outs = [((2, rows, 4 * columns), full, pl.BlockSpec((1, rows, columns), lambda g, core: (layer, 0, block(g))))]
        return picked(body, core, (steps,), ins, outs, "finish_columns", 3, aliases)

    def spot(step):
        return block(step if half == 0 else jnp.minimum(step, steps - 2))

    outs = [
        ((2, rows, 3 * columns), full, pl.BlockSpec((1, rows, columns), lambda g, core: (layer, 0, spot(g)))),
        ((2, rows, columns), full, pl.BlockSpec((1, rows, columns), lambda g, core: (layer, 0, 0))),
    ]
    if half == 0:
        kept = targets[1:]
        ins, outs, aliases = ins[:3] if targets else ins, outs[:1], {2: 0} if targets else {}
        return (picked(body, core, (steps,), ins, outs, "finish_qkv", 3, aliases)[0], *kept)
    return picked(body, core, (steps,), ins, outs, "finish_qkv_out", 3, aliases)


def small_gradients(total, me, width, shares, blocks):
    part = width // shares
    scale = 1.0 / lax.axis_size("wide")

    def body(me_ref, total_ref, gains_ref, shifts_ref, out_ref, up_ref, down_ref, join_ref):
        values = total_ref[...] * scale
        back = [values[0:8], values[8:16]]
        ahead = [values[16 : 20 + blocks], values[20 + blocks : 24 + 2 * blocks]]
        for place in range(shares):

            @pl.when(me_ref[0] == place)
            def _():
                columns = slice(place * part, place * part + part)
                for layer in range(2):
                    for row, target in ((0, gains_ref), (1, shifts_ref)):
                        target[layer, 0:1] = back[layer][row : row + 1, columns]
                        target[layer, 1:2] = ahead[layer][row + 1 : row + 2, columns]
                    out_ref[layer : layer + 1] = ahead[layer][3:4, columns]
                    down_ref[layer : layer + 1] = ahead[layer][0:1, columns]
                    begin = place * part * blocks
                    while begin < (place + 1) * part * blocks:
                        row, column = begin // width, begin % width
                        length = min(width - column, (place + 1) * part * blocks - begin)
                        at = begin - place * part * blocks
                        piece = ahead[layer][4 + row : 5 + row, column : column + length]
                        up_ref[layer : layer + 1, at : at + length] = piece
                        begin += length
                join_ref[...] = back[1][2:3, columns]

    shapes = [(2, 2, part), (2, 2, part), (2, part), (2, part * blocks), (2, part), (1, part)]
    outs = [(shape, full, pl.BlockSpec(shape, lambda g, me, n=len(shape): (0,) * n)) for shape in shapes]
    ins = [(total, pl.BlockSpec(total.shape, lambda g, me: (0, 0)))]
    return picked(body, me, (1,), ins, outs, "small_gradients", 1)


def after(value, *earlier):
    return lax.optimization_barrier((value,) + earlier)[0] if earlier else value


def swap(values, axis, mask):
    size = lax.axis_size(axis)
    return lax.ppermute(values, axis, [(source, source ^ mask) for source in range(size)])


def masks(axis):
    return [1 << bit for bit in range(lax.axis_size(axis).bit_length() - 1)]


class Order:
    def __init__(self):
        self.last = ()

    def run(self, function, *arrays):
        held = lax.optimization_barrier(tuple(arrays) + self.last)[: len(arrays)]
        out = function(*held)
        self.last = (jax.tree.leaves(out)[0],)
        return out

    def hold(self, *arrays):
        self.last += arrays


def place_bit(axis, mask):
    return ((lax.axis_index(axis) & mask) // mask).astype(jnp.int32).reshape(1)


class Term:
    def __init__(self, order, kind, layer, function, *arrays):
        self.order, self.kind, self.layer, self.half = order, kind, layer, None
        self.core = place_bit("wide", 1)
        sent = order.run(lambda *x: function(*x, 1 - self.core), *arrays)
        self.got = [swap(each, "wide", 1) for each in sent]
        self.columns = sent[0].shape[-1]
        self.keep = lambda: order.run(lambda *x: function(*x, self.core), *arrays)

    def stay(self):
        self.kept, self.keep = self.keep(), None

    def part(self, half):
        other = copy.copy(self)
        other.kept, other.got, other.half = self.kept[half::2], self.got[half::2], half
        return other

    def pass_narrow(self):
        stages = list(reversed(masks("narrow")))
        if isinstance(self.kept, (list, tuple)):
            bit = place_bit("narrow", stages[0])
            blocks = len(self.kept) // 2
            sent, self.kept = self.order.run(lambda *x: cross(bit, *x), *self.kept, *self.got)
            self.got = swap(sent, "narrow", stages.pop(0))
        else:
            blocks = 1
        for mask in stages:
            pairs = [(self.kept, self.got)]
            self.kept, self.got = halve(self.order, "narrow", mask, blocks, pairs, self.columns)

    def pass_wide(self, mask):
        pairs = list(zip(self.kept, self.got)) if isinstance(self.kept, (list, tuple)) else [(self.kept, self.got)]
        self.kept, self.got = halve(self.order, "wide", mask, 1, pairs, self.columns)

    def add_into(self, target, place, count):
        kept, got = [side.reshape(-1, self.columns) for side in (self.kept, self.got)]
        if target is None:
            return self.order.run(lambda one, two: add_into(None, place, count, one, two), kept, got)
        return self.order.run(lambda target, one, two: add_into(target, place, count, one, two), target, kept, got)

    def finish(self, done, own, got, begin, length):
        targets = done.get(self.kind, ())

        def last(own, got, core, *targets):
            return finish(self.kind, self.half, own, got, begin, length, core, self.layer, targets)

        done[self.kind] = self.order.run(last, own, got, self.core, *targets)


def halve(order, axis, mask, lead, pairs, columns):
    shaped = [array.reshape(lead, 2, -1, columns) for pair in pairs for array in pair]
    bit = place_bit(axis, mask)
    sent, kept = order.run(lambda *x: add_halve(bit, *x), *shaped)
    return kept, swap(sent, axis, mask)


class Reduce:
    def __init__(self, order, terms, passed=()):
        self.order, self.terms = order, terms
        self.down = [mask for mask in masks("wide")[1:] if mask not in passed]
        self.up = list(reversed(passed))
        self.pieces, self.columns = 2 ** len(passed), terms[0].columns
        self.parts = [(term.kept, term.got) for term in terms]
        self.lengths, self.first = [each.size // self.columns for each, _ in self.parts], True
        self.joining, self.closed = None, False

    def step(self):
        if self.closed:
            return
        if self.down:
            mask = self.down.pop(0)
            rows = [kept.size // self.columns for kept, _ in self.parts]
            even = all(each % 32 == 0 for each in rows)
            if self.first and even:
                self.pieces, self.lengths = 2 * self.pieces, [each // 2 for each in rows]
            self.first = False
            if even:
                self.up.insert(0, mask)
                self.parts = [halve(self.order, "wide", mask, 1, self.parts, self.columns)]
            else:
                flat = [[side.reshape(-1, self.columns) for side in pair] for pair in self.parts]
                pair = [jnp.concatenate(sides) for sides in zip(*flat)]
                total = self.order.run(add, *pair)
                self.parts = [(total, swap(total, "wide", mask))]
            return
        kept, got = [array.reshape(-1, self.columns) for array in self.parts[0]]
        if self.joining is None:
            total = self.order.run(add, kept, got)
        else:
            bit = place_bit("wide", self.joining)
            total = self.order.run(lambda *x: pair_up(*x, bit), kept, got).reshape(-1, self.columns)
        if self.up:
            self.joining = self.up.pop(0)
            self.parts = [(total, swap(total, "wide", self.joining))]
        else:
            self.parts = [(total, swap(total, "wide", 1))]
            self.closed = True

    def finish(self, done):
        own, got = [array.reshape(self.pieces, -1, self.columns) for array in self.parts[0]]
        begin = 0
        for term, length in zip(self.terms, self.lengths):
            term.finish(done, own, got, begin, length)
            begin += length


def on_device(
    tokens,
    skip,
    flags,
    cotangent,
    norm_gains,
    norm_biases,
    qkv_weight,
    out_weight,
    out_bias,
    up_weight,
    up_bias,
    down_weight,
    down_bias,
    skip_weight,
    skip_bias,
):
    items, seq_rows, width = tokens.shape
    rows = items * seq_rows
    me = lax.axis_index("narrow")
    shares = lax.axis_size("narrow")
    spots = jnp.stack([me, lax.axis_index("wide")]).astype(jnp.int32)
    order = Order()

    def fetches(layer):
        return (
            Fetch([(qkv_weight, layer)], (1, 2)),
            Fetch([(out_weight, layer), (up_weight, layer)], (1, 2)),
            Fetch([(down_weight, layer)], (1, 4)),
        )

    fetch_qkv0, fetch_up0, fetch_down0 = fetches(0)
    fetch_qkv1, fetch_up1, fetch_down1 = fetches(1)
    fetch_join = Fetch([(skip_weight, None)], (1, 4))
    qkv0, qkv1 = [Weight(each, 0, width, spots) for each in (fetch_qkv0, fetch_qkv1)]
    out0, out1 = [Weight(each, 0, width, spots) for each in (fetch_up0, fetch_up1)]
    up0, up1 = [Weight(each, 1, width, spots) for each in (fetch_up0, fetch_up1)]
    down0, down1 = [Weight(each, 0, width, spots) for each in (fetch_down0, fetch_down1)]
    join = Weight(fetch_join, 0, width, spots)

    small = (norm_gains, norm_biases, out_bias, down_bias, skip_bias, up_bias)
    held = order.run(pack_small, *small)[None]
    for mask in masks("narrow"):
        held = jnp.concatenate([held, swap(held, "narrow", mask)])
    fetch_qkv0.fetch(*order.last)
    fetch_up0.fetch(held)
    fetch_down0.fetch(fetch_up0.sent)
    fetch_join.fetch(fetch_down0.sent)
    fetch_qkv1.fetch(fetch_join.sent)
    place = me.astype(jnp.int32).reshape(1)
    lines = order.run(lambda x: unpack_small(x, place, small, width), held)

    def line(row):
        return lines[row : row + 1]

    gains, shifts = [[line(2 * layer + each) for each in range(2)] for layer in range(2)], None
    shifts = [[line(4 + 2 * layer + each) for each in range(2)] for layer in range(2)]
    out_biases, down_biases, join_shift = [line(8), line(9)], [line(10), line(11)], line(12)
    blocks = up0.blocks
    up_biases = [lines[13 + layer * blocks : 13 + (layer + 1) * blocks].reshape(1, -1) for layer in range(2)]

    tokens_flat, skip_flat, cotangent_flat = [array.reshape(rows, width) for array in (tokens, skip, cotangent)]
    lengths = PATCHES + 1 + CAPTION * flags
    valid = lax.broadcasted_iota(jnp.int32, (items, seq_rows), 1) < lengths[:, None]
    keep = valid.reshape(rows, 1).astype(full)
    dz1 = jnp.where(keep > 0, cotangent_flat, 0)

    fetch_qkv0.share(1)
    fetch_qkv0.share(0)
    order.hold(*fetch_up0.got())
    fetch_up0.share(1)
    a0, packed0 = order.run(lambda *x: project_qkv(*x, qkv0), tokens_flat, gains[0][0], shifts[0][0])
    order.hold(*fetch_down0.got())
    fetch_down0.share(1, a0)
    packed0 = packed0.reshape(3, items, seq_rows, width)
    mixed0, totals0 = order.run(lambda *x: attend(*x, items, seq_rows), packed0, lengths)
    fetch_up0.share(0, mixed0)
    fetch_down0.share(0, mixed0)
    fetch_up1.fetch(mixed0)
    fetch_down1.fetch(fetch_up1.sent)
    order.hold(*fetch_join.got(), *fetch_qkv1.got())
    fetch_join.share(1)
    fetch_qkv1.share(1)
    mixed0 = mixed0.reshape(rows, width)
    m0, second0, hidden0, slope0, middle = order.run(
        lambda x, o, ob, g, s, ub, db: feed_forward(x, o, out0, ob, g, s, up0, ub, down0, db),
        tokens_flat, mixed0, out_biases[0], gains[0][1], shifts[0][1], up_biases[0], down_biases[0],
    )
    fetch_join.share(0, middle)
    fetch_qkv1.share(0, middle)
    order.hold(*fetch_up1.got(), *fetch_down1.got())
    fetch_up1.share(1)
    fetch_down1.share(1)
    entry, a1, packed1 = order.run(
        lambda m, s, jb, g, sh: join_qkv(m, s, join, jb, g, sh, qkv1),
        middle, skip_flat, join_shift, gains[1][0], shifts[1][0],
    )
    packed1 = packed1.reshape(3, items, seq_rows, width)
    mixed1, totals1 = order.run(lambda *x: attend(*x, items, seq_rows), packed1, lengths)
    fetch_up1.share(0, mixed1)
    fetch_down1.share(0, mixed1)
    mixed1 = mixed1.reshape(rows, width)
    m1, second1, hidden1, slope1, output = order.run(
        lambda x, o, ob, g, s, ub, db, k: feed_forward(x, o, out1, ob, g, s, up1, ub, down1, db, k),
        entry, mixed1, out_biases[1], gains[1][1], shifts[1][1], up_biases[1], down_biases[1], keep,
    )

    done = {}
    term_down1 = Term(order, "down", 1, down_term, hidden1, dz1)
    term_down1.stay()
    term_down1.pass_narrow()
    du, dm, db, do, sums1 = order.run(
        lambda y, z, s, m, g: feed_forward_back(y, z, s, down1, up1, m, g, out1),
        dz1, dz1, slope1, m1, gains[1][1],
    )
    term_up1 = Term(order, "up", 1, up_term, second1, du)
    term_up1.stay()
    term_up1.pass_narrow()
    total = term_down1.add_into(None, 0, 3)
    dpacked = order.run(
        lambda *x: attend_back(*x, items, seq_rows), packed1, do.reshape(items, seq_rows, width), totals1, lengths
    )
    flat_packed = dpacked.reshape(3, rows, width)
    term_qkv1 = Term(order, "qkv", 1, qkv_out_term, a1, flat_packed, mixed1, db)
    term_qkv1.stay()
    term_qkv1.pass_narrow()
    total = term_up1.add_into(total, 1, 3)
    dentry, dmiddle, dz0, skip_grad, sums3 = order.run(
        lambda gp, x, g, dm: project_back(gp, qkv1, x, g, dm, join), flat_packed, entry, gains[1][0], dm
    )
    term_join = Term(order, "join", 1, join_term, middle, skip_flat, dentry)
    term_join.stay()
    term_join.pass_narrow()
    term_down0 = Term(order, "down", 0, down_term, hidden0, dz0)
    term_down0.stay()
    total = term_qkv1.add_into(total, 2, 3)
    size = lax.axis_size("wide")
    groups = [[device + core for device in range(0, size, 2)] for core in range(2)]
    flat_total = total.reshape(-1, width)
    part = lax.psum_scatter(flat_total, "wide", axis_index_groups=groups, scatter_dimension=0, tiled=True)
    term_down0.pass_narrow()

    du, dm, db, do, sums0 = order.run(
        lambda y, z, s, m, g: feed_forward_back(y, z, s, down0, up0, m, g, out0),
        dmiddle, dz0, slope0, m0, gains[0][1],
    )
    term_join.pass_wide(2)
    term_up0 = Term(order, "up", 0, up_term, second0, du)
    term_up0.stay()
    term_up0.pass_narrow()
    dpacked = order.run(
        lambda *x: attend_back(*x, items, seq_rows), packed0, do.reshape(items, seq_rows, width), totals0, lengths
    )
    term_down0.pass_wide(2)
    flat_packed = dpacked.reshape(3, rows, width)
    term_qkv0 = Term(order, "qkv", 0, qkv_out_term, a0, flat_packed, mixed0, db)
    term_qkv0.stay()
    one, two = term_qkv0.part(0), term_qkv0.part(1)
    early = 4 if shares == 2 else None
    if early:
        two.pass_wide(early)
    one.pass_narrow()
    order.hold(part, term_up0.got)
    first = Reduce(order, [term_down0, term_join], (2,))
    first.step()
    gathered = lax.all_gather(after(part, *order.last), "wide", axis_index_groups=groups, tiled=True)
    second = Reduce(order, [term_up0])
    second.step()
    tokens_grad, sums2 = order.run(
        lambda gp, x, g, dm: project_back(gp, qkv0, x, g, dm), flat_packed, tokens_flat, gains[0][0], dm
    )
    minor = jnp.concatenate([sums2, sums3, sums0, sums1])
    minor_stages = [("narrow", mask) for mask in masks("narrow")] + [("wide", mask) for mask in masks("wide")]
    minor_got = swap(minor, *minor_stages[0])

    def minor_step():
        nonlocal minor, minor_got
        if minor_stages:
            minor_stages.pop(0)
            minor = order.run(lambda one, two: one + two, minor, minor_got)
            if minor_stages:
                minor_got = swap(minor, *minor_stages[0])

    two.pass_narrow()
    third = Reduce(order, [one])
    third.step()
    first.step()
    second.step()
    minor_step()
    fourth = Reduce(order, [two], (early,) if early else ())
    fourth.step()
    third.step()
    minor_step()
    first.step()
    fourth.step()
    second.step()
    third.step()
    minor_step()
    first.step()
    fourth.step()
    second.step()
    third.step()
    order.hold(gathered)
    other = swap(after(gathered, *order.last), "wide", 1)
    minor_step()
    first.step()
    fourth.step()
    second.step()
    third.step()
    own, got = gathered.reshape(1, -1, width), other.reshape(1, -1, width)
    for which, term in enumerate((term_down1, term_up1, term_qkv1)):
        term.finish(done, own, got, which * (own.shape[1] // 3), own.shape[1] // 3)
    second.step()
    first.step()
    fourth.step()
    third.step()
    minor_step()
    first.finish(done)
    second.step()
    fourth.step()
    third.step()
    for each in (first, second, third, fourth):
        while not each.closed:
            each.step()
    while minor_stages:
        minor_step()
    second.finish(done)
    fourth.finish(done)
    third.finish(done)
    small = order.run(lambda x: small_gradients(x, place, width, shares, up1.blocks), minor)

    return (
        output.reshape(tokens.shape),
        tokens_grad.reshape(tokens.shape),
        skip_grad.reshape(tokens.shape),
        small[0],
        small[1],
        done["qkv"][0],
        done["qkv"][1],
        small[2],
        done["up"][0],
        small[3],
        done["down"][0],
        small[4],
        done["join"][0][0],
        small[5].reshape(-1),
    )


def solution(mesh):
    placed = (
        P(("wide", "narrow"), None, None),
        P(("wide", "narrow"), None, None),
        P(("wide", "narrow")),
        P(("wide", "narrow"), None, None),
        P(None, None, "narrow"),
        P(None, None, "narrow"),
        P(None, "narrow", None),
        P(None, "narrow", None),
        P(None, "narrow"),
        P(None, "narrow", None),
        P(None, "narrow"),
        P(None, "narrow", None),
        P(None, "narrow"),
        P("narrow", None),
        P("narrow"),
    )
    return jax.shard_map(
        on_device,
        mesh=mesh,
        in_specs=placed,
        out_specs=(
            P(("wide", "narrow"), None, None),
            P(("wide", "narrow"), None, None),
            P(("wide", "narrow"), None, None),
            P(None, None, "narrow"),
            P(None, None, "narrow"),
            P(None, "narrow", None),
            P(None, "narrow", None),
            P(None, "narrow"),
            P(None, "narrow", None),
            P(None, "narrow"),
            P(None, "narrow", None),
            P(None, "narrow"),
            P("narrow", None),
            P("narrow"),
        ),
        check_vma=False,
    )
```

```python
import copy

import jax
import jax.numpy as jnp
from jax import lax
from jax.experimental import pallas as pl
from jax.experimental.pallas import tpu as pltpu
from jax.sharding import PartitionSpec as P

HEAD_DIM = 64
PATCHES = 256
CAPTION = 77
PAIR = 2 * HEAD_DIM


epsilon = 1e-05
masked_score = -1e30
low = jnp.bfloat16
full = jnp.float32
ANY = pl.BlockSpec(memory_space=pl.ANY)
SCALARS = pl.BlockSpec(memory_space=pltpu.SMEM)


def dot(left, right, contract=(1, 0)):
    dims = (((contract[0],), (contract[1],)), ((), ()))
    return lax.dot_general(left, right, dims, preferred_element_type=full)


def normalize(values):
    centred = values - jnp.mean(values, axis=-1, keepdims=True)
    factor = lax.rsqrt(jnp.mean(centred * centred, axis=-1, keepdims=True) + epsilon)
    return centred * factor, factor


def normalize_back(upstream, normed, factor):
    return factor * (
        upstream
        - jnp.mean(upstream, axis=-1, keepdims=True)
        - normed * jnp.mean(upstream * normed, axis=-1, keepdims=True)
    )


def column_sum(values):
    return jnp.sum(values.astype(full), axis=0, keepdims=True)


def whole(shape):
    return pl.BlockSpec(shape, lambda *grid: (0,) * len(shape))


def cost(micros):
    return pl.CostEstimate(flops=int(micros * 3 * 10**8), bytes_accessed=0, transcendentals=0)


def call(body, grid, ins, outs, name, micros, scratch=(), limit=56):
    return pl.pallas_call(
        body,
        grid=grid,
        in_specs=[spec for _, spec in ins],
        out_specs=[spec for _, _, spec in outs],
        out_shape=[jax.ShapeDtypeStruct(shape, kind) for shape, kind, _ in outs],
        scratch_shapes=list(scratch),
        name=name,
        cost_estimate=cost(micros),
        compiler_params=pltpu.CompilerParams(vmem_limit_bytes=limit * 2**20),
    )(*[array for array, _ in ins])


class Fetch:
    def __init__(self, arrays, sharing):
        self.arrays, self.sharing = arrays, list(sharing)
        self.rows = arrays[0][0].shape[-2]
        while self.rows % (16 << len(self.sharing)):
            self.sharing.pop()
        self.length = self.rows >> len(self.sharing)

    def quarter(self, place):
        return sum(((place // mask) & 1) << bit for bit, mask in enumerate(self.sharing))

    def fetch(self, *earlier):
        found = []
        for array, layer in self.arrays:
            array = after(array, *earlier)
            lead = () if layer is None else (layer,)
            begin = self.quarter(lax.axis_index("wide")) * self.length
            sizes = (1,) * len(lead) + (self.length, array.shape[-1])
            found.append(lax.dynamic_slice(array, lead + (begin, 0), sizes).reshape(self.length, -1))
        self.sent = (jnp.concatenate(found, axis=1) if len(found) > 1 else found[0])[None]
        held = self.sent
        for mask in masks("narrow"):
            held = jnp.concatenate([held, swap(held, "narrow", mask)])
        self.pieces = {0: held[1:]}

    def share(self, which, *earlier):
        if which < len(self.sharing):
            mask = self.sharing[which]
            got = {key ^ (1 << which): swap(after(piece, *earlier), "wide", mask) for key, piece in self.pieces.items()}
            self.pieces.update(got)

    def got(self):
        return list(self.pieces.values())


class Weight:
    def __init__(self, fetched, which, width, spots):
        self.fetched, self.spots, self.width = fetched, spots, width
        self.array, self.layer = fetched.arrays[which]
        self.begin = sum(array.shape[-1] for array, _ in fetched.arrays[:which])
        self.rows, columns = self.array.shape[-2:]
        self.shares = lax.axis_size("narrow")
        self.blocks = columns // width
        self.total = self.rows * self.shares

    def arrays(self):
        return [self.array] + self.fetched.got()

    def scratch(self):
        copies = 1 + len(self.fetched.pieces) * (self.shares - 1)
        return [pltpu.VMEM((self.blocks, self.total, self.width), low), pltpu.SemaphoreType.DMA((self.blocks, copies))]

    def copies(self, spots, refs, held, signals, block):
        own, pieces = refs[0], refs[1:]
        me, length = spots[0], self.fetched.length
        own = own if self.layer is None else own.at[self.layer]
        columns = pl.ds(block * self.width, self.width)
        begin = pl.multiple_of(me * self.rows, 16)
        found = [(own.at[:, columns], begin, self.rows)]
        columns = pl.ds(self.begin + block * self.width, self.width)
        for key, piece in zip(self.fetched.pieces, pieces):
            for offset in range(1, self.shares):
                begin = (me ^ offset) * self.rows + (self.fetched.quarter(spots[1]) ^ key) * length
                found.append((piece.at[offset - 1, :, columns], pl.multiple_of(begin, 16), length))
        return [
            pltpu.make_async_copy(source, held.at[block, pl.ds(begin, length)], signals.at[block, place])
            for place, (source, begin, length) in enumerate(found)
        ]

    def wait(self, *refs, block=0):
        for copy in self.copies(*refs, block):
            copy.wait()


def weighted(body, weights, grid, ins, outs, name, micros, scratch=(), first=((0, 0),)):
    spots = weights[0].spots
    operands = [(spots, SCALARS)] + [(array, ANY) for weight in weights for array in weight.arrays()]
    counts = [len(weight.arrays()) for weight in weights]
    extra = [piece for weight in weights for piece in weight.scratch()]

    def wrapped(*refs):
        spots_ref, rest = refs[0], list(refs[1:])
        sources = []
        for count in counts:
            sources.append(rest[:count])
            rest = rest[count:]
        spare = rest[len(rest) - len(extra) :]
        rest = rest[: len(rest) - len(extra)]
        handles = []
        for place, weight in enumerate(weights):
            held, signals = spare[2 * place : 2 * place + 2]
            refs_of = (spots_ref, sources[place], held, signals)
            handles.append((weight, refs_of, held))

        everything = [(place, block) for place, weight in enumerate(weights) for block in range(weight.blocks)]

        def begin(wanted):
            for place, block in wanted:
                weight, refs_of, _ = handles[place]
                for copy in weight.copies(*refs_of, block):
                    copy.start()

        @pl.when(pl.program_id(0) == 0)
        def _():
            begin(first)

        def ready(place, block=0, then=False):
            weight, refs_of, held = handles[place]
            weight.wait(*refs_of, block=block)
            if then:
                begin([each for each in everything if each not in first])

        body(ready, [held for _, _, held in handles], *rest)

    return call(wrapped, grid, operands + ins, outs, name, micros, list(scratch) + extra)


def pack_small(*small):
    part = small[0].shape[-1]
    counts = [piece.size // part for piece in small]

    def body(*refs):
        row = 0
        for ref in refs[:-1]:
            values = ref[...].reshape(-1, ref.shape[-1])
            for each in range(values.shape[0]):
                for begin in range(0, values.shape[1], part):
                    refs[-1][row : row + 1] = values[each : each + 1, begin : begin + part].astype(full)
                    row += 1
        refs[-1][row:] = jnp.zeros((refs[-1].shape[0] - row, part), full)

    flat = [piece.reshape((1,) * (2 - piece.ndim) + piece.shape) for piece in small]
    rows = -(-sum(counts) // 16) * 16
    out = ((rows, part), full, whole((rows, part)))
    return call(body, (1,), [(piece, whole(piece.shape)) for piece in flat], [out], "pack_small", 1)[0].astype(low)


def unpack_small(parts, me, small, width):
    shares, _, part = parts.shape
    lines = [(piece.size // piece.shape[-1], piece.shape[-1] // part) for piece in small]
    total = sum(count * many for count, many in lines)
    rows = -(-total // 8) * 8

    def body(me_ref, parts_ref, out_ref):
        values = parts_ref[...].astype(full)
        for mine in range(shares):

            @pl.when(me_ref[0] == mine)
            def _():
                for owner in range(shares):
                    source, target = 0, 0
                    for count, many in lines:
                        for each in range(count):
                            for piece in range(many):
                                at = owner * many * part + piece * part
                                row, column = target + at // width, at % width
                                line = values[owner ^ mine, source : source + 1]
                                out_ref[row : row + 1, column : column + part] = line
                                source += 1
                            target += many
        if rows > total:
            out_ref[total:] = jnp.zeros((rows - total, width), full)

    ins = [(parts, pl.BlockSpec(parts.shape, lambda g, me: (0, 0, 0)))]
    out = ((rows, width), full, pl.BlockSpec((rows, width), lambda g, me: (0, 0)))
    return picked(body, me, (1,), ins, [out], "unpack_small", 1)[0]


def project_qkv(inputs, gain, shift, weight):
    rows, width = inputs.shape

    def body(ready, held, x_ref, gain_ref, shift_ref, a_ref, out_ref):
        step = pl.program_id(0)

        @pl.when(step == 0)
        def _():
            normed, _ = normalize(x_ref[...].astype(full))
            a_ref[...] = (normed * gain_ref[...] + shift_ref[...]).astype(low)
            ready(0, 0, then=True)

        @pl.when(step > 0)
        def _():
            ready(0, step)

        scale = jnp.where(step == 0, HEAD_DIM ** (-0.5), 1.0)
        out_ref[0] = (dot(a_ref[...], held[0][step]).astype(low).astype(full) * scale).astype(low)

    return weighted(
        body,
        [weight],
        (3,),
        [
            (inputs, whole((rows, width))),
            (gain, whole((1, width))),
            (shift, whole((1, width))),
        ],
        [
            ((rows, width), low, whole((rows, width))),
            ((3, rows, width), low, pl.BlockSpec((1, rows, width), lambda j: (j, 0, 0))),
        ],
        "project_qkv",
        7,
    )


def join_qkv(middle, skip, join_weight, join_shift, gain, shift, weight):
    rows, width = middle.shape

    def body(ready, held, m_ref, s_ref, jb_ref, gain_ref, shift_ref, e_ref, a_ref, out_ref):
        step = pl.program_id(0)

        @pl.when(step == 0)
        def _():
            ready(0, then=True)
            entry = dot(m_ref[...], held[0][0, :width]) + dot(s_ref[...], held[0][0, width:]) + jb_ref[...]
            e_ref[...] = entry
            normed, _ = normalize(entry)
            a_ref[...] = (normed * gain_ref[...] + shift_ref[...]).astype(low)

        ready(1, step)
        scale = jnp.where(step == 0, HEAD_DIM ** (-0.5), 1.0)
        out_ref[0] = (dot(a_ref[...], held[1][step]).astype(low).astype(full) * scale).astype(low)

    return weighted(
        body,
        [join_weight, weight],
        (3,),
        [
            (middle, whole((rows, width))),
            (skip, whole((rows, width))),
            (join_shift, whole((1, width))),
            (gain, whole((1, width))),
            (shift, whole((1, width))),
        ],
        [
            ((rows, width), full, whole((rows, width))),
            ((rows, width), low, whole((rows, width))),
            ((3, rows, width), low, pl.BlockSpec((1, rows, width), lambda j: (j, 0, 0))),
        ],
        "join_qkv",
        11,
        first=((0, 0), (1, 0)),
    )


def head_masks(seq_rows):
    lane = lax.broadcasted_iota(jnp.int32, (seq_rows, PAIR), 1)
    return [lane < HEAD_DIM, lane >= HEAD_DIM]


def attend(packed, lengths, items, seq_rows):
    width = packed.shape[-1]
    pairs = width // PAIR

    def body(length_ref, q_ref, k_ref, v_ref, out_ref, total_ref):
        length = length_ref[pl.program_id(0)]
        queries, keys, values = q_ref[0, 0], k_ref[0, 0], v_ref[0, 0]
        counts = lax.broadcasted_iota(jnp.int32, (seq_rows, seq_rows), 0) < length
        mixed = jnp.zeros((PAIR, seq_rows), full)
        for head, lanes in enumerate(head_masks(seq_rows)):
            scores = dot(keys, jnp.where(lanes, queries, 0), (1, 1))
            scores = jnp.where(counts, scores, masked_score)
            largest = jnp.max(scores, axis=0, keepdims=True)
            weights = jnp.exp(scores - largest)
            total = jnp.sum(weights, axis=0, keepdims=True)
            part = dot(jnp.where(lanes, values, 0), weights.astype(low), (0, 0))
            mixed += part * (1.0 / total)
            total_ref[0, 0, head : head + 1] = largest + jnp.log(total)
        out_ref[0] = mixed.T.astype(low)

    def block(which):
        return pl.BlockSpec((1, 1, seq_rows, PAIR), lambda n, h: (which, n, 0, h))

    return call(
        body,
        (items, pairs),
        [
            (lengths, SCALARS),
            (packed, block(0)),
            (packed, block(1)),
            (packed, block(2)),
        ],
        [
            ((items, seq_rows, width), low, pl.BlockSpec((1, seq_rows, PAIR), lambda n, h: (n, 0, h))),
            ((items, pairs, 8, seq_rows), full, pl.BlockSpec((1, 1, 8, seq_rows), lambda n, h: (n, h, 0, 0))),
        ],
        "attend",
        13,
    )


def attend_back(packed, grad_mixed, totals, lengths, items, seq_rows):
    width = packed.shape[-1]
    pairs = width // PAIR

    def body(length_ref, q_ref, k_ref, v_ref, g_ref, total_ref, out_ref):
        length = length_ref[pl.program_id(0)]
        queries, keys, values, upstream = q_ref[0, 0], k_ref[0, 0], v_ref[0, 0], g_ref[0]
        counts = lax.broadcasted_iota(jnp.int32, (seq_rows, seq_rows), 0) < length
        grad_queries = jnp.zeros((PAIR, seq_rows), full)
        grad_keys = jnp.zeros((seq_rows, PAIR), full)
        grad_values = jnp.zeros((seq_rows, PAIR), full)
        for head, lanes in enumerate(head_masks(seq_rows)):
            own_queries = jnp.where(lanes, queries, 0)
            own_upstream = jnp.where(lanes, upstream, 0)
            scores = dot(keys, own_queries, (1, 1))
            shifted = jnp.where(counts, scores, masked_score) - total_ref[0, 0, head : head + 1]
            probs = jnp.exp(shifted)
            grad_probs = dot(values, own_upstream, (1, 1))
            centre = jnp.sum(grad_probs * probs, axis=0, keepdims=True)
            grad_scores = (probs * (grad_probs - centre)).astype(low)
            grad_values += dot(probs.astype(low), own_upstream)
            grad_keys += dot(grad_scores, own_queries)
            grad_queries += dot(jnp.where(lanes, keys, 0), grad_scores, (0, 0))
        out_ref[0, 0] = (grad_queries.T * HEAD_DIM ** (-0.5)).astype(low)
        out_ref[1, 0] = grad_keys.astype(low)
        out_ref[2, 0] = grad_values.astype(low)

    def block(which):
        return pl.BlockSpec((1, 1, seq_rows, PAIR), lambda n, h: (which, n, 0, h))

    return call(
        body,
        (items, pairs),
        [
            (lengths, SCALARS),
            (packed, block(0)),
            (packed, block(1)),
            (packed, block(2)),
            (grad_mixed, pl.BlockSpec((1, seq_rows, PAIR), lambda n, h: (n, 0, h))),
            (totals, pl.BlockSpec((1, 1, 8, seq_rows), lambda n, h: (n, h, 0, 0))),
        ],
        [
            ((3, items, seq_rows, width), low, pl.BlockSpec((3, 1, seq_rows, PAIR), lambda n, h: (0, n, 0, h))),
        ],
        "attend_back",
        17,
    )[0]


def gelu_parts(before):
    decay = jnp.exp(before * before * -0.5)
    inverse = pl.reciprocal(1.0 + (0.3275911 * 0.5**0.5) * jnp.abs(before), approx=False)
    series = 1.061405429 * 0.5
    for term in (-1.453152027, 1.421413741, -0.284496736, 0.254829592):
        series = series * inverse + term * 0.5
    below = series * inverse * decay
    share = jnp.where(before >= 0, 1.0 - below, below)
    return before * share, share + before * decay * 0.3989422804014327


def feed_forward(inputs, mixed, out_weight, out_bias, gain, shift, up_weight, up_bias, down_weight, down_bias, keep=None):
    rows, width = inputs.shape
    steps = up_weight.blocks
    hidden = steps * width

    def body(ready, held, x_ref, o_ref, ob_ref, gain_ref, shift_ref, ub_ref, db_ref, *rest):
        m_ref, a_ref, g_ref, s_ref, y_ref, total = rest[-6:]
        step = pl.program_id(0)

        @pl.when(step == 0)
        def _():
            ready(0, then=True)
            middle = x_ref[...].astype(full) + dot(o_ref[...], held[0][0]) + ob_ref[...]
            m_ref[...] = middle
            normed, _ = normalize(middle)
            a_ref[...] = (normed * gain_ref[...] + shift_ref[...]).astype(low)
            total[...] = middle + db_ref[...]

        ready(1, step)
        before = dot(a_ref[...], held[1][step]) + ub_ref[...]
        value, slope = gelu_parts(before)
        g_ref[...] = value.astype(low)
        s_ref[...] = slope.astype(low)

        @pl.when(step == 0)
        def _():
            ready(2)

        total[...] += dot(g_ref[...], held[2][0, pl.ds(pl.multiple_of(step * width, width), width)])

        @pl.when(step == steps - 1)
        def _():
            value = total[...]
            if keep is not None:
                value = jnp.where(rest[0][...] > 0, value, 0.0)
            y_ref[...] = value.astype(low)

    return weighted(
        body,
        [out_weight, up_weight, down_weight],
        (steps,),
        [
            (inputs, whole((rows, width))),
            (mixed, whole((rows, width))),
            (out_bias, whole((1, width))),
            (gain, whole((1, width))),
            (shift, whole((1, width))),
            (up_bias, pl.BlockSpec((1, width), lambda j: (0, j))),
            (down_bias, whole((1, width))),
        ]
        + ([] if keep is None else [(keep, whole((rows, 1)))]),
        [
            ((rows, width), full, whole((rows, width))),
            ((rows, width), low, whole((rows, width))),
            ((rows, hidden), low, pl.BlockSpec((rows, width), lambda j: (0, j))),
            ((rows, hidden), low, pl.BlockSpec((rows, width), lambda j: (0, j))),
            ((rows, width), low, whole((rows, width))),
        ],
        "feed_forward",
        23,
        scratch=[pltpu.VMEM((rows, width), full)],
        first=((0, 0), (1, 0)),
    )


def feed_forward_back(upstream, rounded, slope, down_weight, up_weight, middle, gain, out_weight):
    rows, width = upstream.shape
    steps = up_weight.blocks
    hidden = steps * width

    def body(ready, held, y_ref, dz_ref, s_ref, m_ref, gain_ref, du_ref, dm_ref, db_ref, do_ref, sums_ref, total):
        step = pl.program_id(0)

        @pl.when(step == 0)
        def _():
            sums_ref[0:1] = column_sum(dz_ref[...])
            total[...] = jnp.zeros_like(total)
            ready(0, then=True)

        down = held[0][0, pl.ds(pl.multiple_of(step * width, width), width)]
        grad = (dot(dz_ref[...], down, (1, 1)) * s_ref[...].astype(full)).astype(low)
        du_ref[...] = grad
        sums_ref[pl.ds(4 + step, 1)] = column_sum(grad)
        ready(1, step)
        total[...] += dot(grad, held[1][step], (1, 1))

        @pl.when(step == steps - 1)
        def _():
            grad_second = total[...]
            normed, factor = normalize(m_ref[...])
            sums_ref[1:2] = column_sum(grad_second * normed)
            sums_ref[2:3] = column_sum(grad_second)
            grad_middle = y_ref[...].astype(full) + normalize_back(grad_second * gain_ref[...], normed, factor)
            dm_ref[...] = grad_middle
            branch = grad_middle.astype(low)
            db_ref[...] = branch
            sums_ref[3:4] = column_sum(branch)
            ready(2)
            do_ref[...] = dot(branch, held[2][0], (1, 1)).astype(low)

    return weighted(
        body,
        [down_weight, up_weight, out_weight],
        (steps,),
        [
            (upstream, whole((rows, width))),
            (rounded, whole((rows, width))),
            (slope, pl.BlockSpec((rows, width), lambda j: (0, j))),
            (middle, whole((rows, width))),
            (gain, whole((1, width))),
        ],
        [
            ((rows, hidden), low, pl.BlockSpec((rows, width), lambda j: (0, j))),
            ((rows, width), full, whole((rows, width))),
            ((rows, width), low, whole((rows, width))),
            ((rows, width), low, whole((rows, width))),
            ((4 + steps, width), full, whole((4 + steps, width))),
        ],
        "feed_forward_back",
        21,
        scratch=[pltpu.VMEM((rows, width), full)],
        first=((0, 0), (1, 0)),
    )


def project_back(grad_packed, weight, inputs, gain, grad_middle, join_weight=None):
    rows, width = inputs.shape
    joined = join_weight is not None

    def body(ready, held, g_ref, x_ref, gain_ref, dm_ref, *rest):
        if joined:
            de_ref, dx_ref, dz_ref, skip_ref, sums_ref, total = rest
        else:
            dx_ref, sums_ref, total = rest
        step = pl.program_id(0)

        @pl.when(step == 0)
        def _():
            total[...] = jnp.zeros_like(total)
            ready(0, 0, then=True)

        @pl.when(step > 0)
        def _():
            ready(0, step)

        total[...] += dot(g_ref[0], held[0][step], (1, 1))

        @pl.when(step == 2)
        def _():
            grad_first = total[...]
            normed, factor = normalize(x_ref[...].astype(full))
            sums_ref[0:1] = column_sum(grad_first * normed)
            sums_ref[1:2] = column_sum(grad_first)
            grad = dm_ref[...] + normalize_back(grad_first * gain_ref[...], normed, factor)
            if joined:
                entry = grad.astype(low)
                de_ref[...] = entry
                sums_ref[2:3] = column_sum(entry)
                ready(1)
                grad = dot(entry, held[1][0, :width], (1, 1))
                dx_ref[...] = grad
                dz_ref[...] = grad.astype(low)
                skip_ref[...] = dot(entry, held[1][0, width:], (1, 1))
            else:
                dx_ref[...] = grad

    ins = [
        (grad_packed, pl.BlockSpec((1, rows, width), lambda j: (j, 0, 0))),
        (inputs, whole((rows, width))),
        (gain, whole((1, width))),
        (grad_middle, whole((rows, width))),
    ]
    outs = [((rows, width), full, whole((rows, width))), ((8, width), full, whole((8, width)))]
    if joined:
        rounded = ((rows, width), low, whole((rows, width)))
        outs = [rounded, outs[0], rounded, outs[0], outs[1]]
    return weighted(
        body,
        [weight] + ([join_weight] if joined else []),
        (3,),
        ins,
        outs,
        "project_back",
        13 if joined else 9,
        scratch=[pltpu.VMEM((rows, width), full)],
    )


def picked(body, which, grid, ins, outs, name, micros, aliases=None):
    return pl.pallas_call(
        body,
        grid_spec=pltpu.PrefetchScalarGridSpec(
            num_scalar_prefetch=1,
            grid=grid,
            in_specs=[spec for _, spec in ins],
            out_specs=[spec for _, _, spec in outs],
        ),
        out_shape=[jax.ShapeDtypeStruct(shape, kind) for shape, kind, _ in outs],
        name=name,
        input_output_aliases={place + 1: out for place, out in (aliases or {}).items()},
        cost_estimate=cost(micros),
        compiler_params=pltpu.CompilerParams(vmem_limit_bytes=48 * 2**20),
    )(which, *[array for array, _ in ins])


def quarters(rows, width, narrow_rows):
    shape = (lax.axis_size("narrow") // 2 * narrow_rows, width)
    return [(shape, low, pl.BlockSpec(shape, lambda g, core: (0, 0)))] * 4


def up_term(left, right, core):
    rows, width = left.shape
    part = width // lax.axis_size("narrow")
    half = width // 2

    def body(core_ref, l_ref, r_ref, *outs):
        value = dot(l_ref[...], r_ref[...], (0, 0)).astype(low)
        for block in range(2):

            @pl.when(pl.program_id(0) == block)
            def _():
                outs[block][...] = value[:half]
                outs[2 + block][...] = value[half:]

    return picked(
        body,
        core,
        (2,),
        [
            (left, pl.BlockSpec((rows, width), lambda g, core: (0, 0))),
            (right, pl.BlockSpec((rows, width), lambda g, core: (0, core[0] * 2 + g))),
        ],
        quarters(rows, width, part),
        "up_term",
        3.5,
    )


def qkv_out_term(first, packed, mixed, branch, core):
    rows, width = first.shape
    part = width // lax.axis_size("narrow")
    half = width // 2

    def body(core_ref, l_ref, r_ref, o_ref, b_ref, *outs):
        step = pl.program_id(0)
        last = core_ref[0] * 2 + step == 3

        def put(block, value):
            outs[block][...] = value[:half]
            outs[2 + block][...] = value[half:]

        @pl.when(last)
        def _():
            put(1, dot(o_ref[...], b_ref[...], (0, 0)).astype(low))

        @pl.when(jnp.logical_not(last))
        def _():
            value = dot(l_ref[...], r_ref[0], (0, 0)).astype(low)
            for block in range(2):

                @pl.when(step == block)
                def _():
                    put(block, value)

    flat = pl.BlockSpec((rows, width), lambda g, core: (0, 0))
    return picked(
        body,
        core,
        (2,),
        [
            (first, flat),
            (packed, pl.BlockSpec((1, rows, width), lambda g, core: (jnp.minimum(core[0] * 2 + g, 2), 0, 0))),
            (mixed, flat),
            (branch, flat),
        ],
        quarters(rows, width, part),
        "qkv_out_term",
        3.5,
    )


def down_term(left, right, core):
    rows, width = right.shape
    shares = lax.axis_size("narrow")
    part = left.shape[1] // (2 * shares)
    direct = part == width
    if not direct:
        left = left.reshape(rows, shares, 2, 2, part // 2)
        left = lax.dynamic_index_in_dim(left, core[0], 2, keepdims=False)
        left = left.reshape(rows, 2, shares // 2, 2, part // 2).swapaxes(2, 3).reshape(rows, 2 * width)
    half = width // 2

    def body(core_ref, l_ref, r_ref, *outs):
        value = dot(l_ref[...], r_ref[...], (0, 0)).astype(low)
        for owner in range(2):

            @pl.when(pl.program_id(0) == owner)
            def _():
                outs[2 * owner][...] = value[:half]
                outs[2 * owner + 1][...] = value[half:]

    return picked(
        body,
        core,
        (2,),
        [
            (left, pl.BlockSpec((rows, width), lambda g, core: (0, g * 2 + core[0] if direct else g))),
            (right, pl.BlockSpec((rows, width), lambda g, core: (0, 0))),
        ],
        quarters(rows, width, part // 2),
        "down_term",
        3.5,
    )


def join_term(middle, skip, right, core):
    rows, width = right.shape
    shares = lax.axis_size("narrow")
    part = width // shares
    half = width // 2
    if part != half:
        left = jnp.concatenate([middle, skip], axis=1).reshape(rows, shares, 2, 2, part // 2)
        left = lax.dynamic_index_in_dim(left, core[0], 2, keepdims=False)
        left = left.reshape(rows, 2, shares // 2, 2, part // 2).swapaxes(2, 3).reshape(rows, width)
        middle, skip = left[:, :half], left[:, half:]

    def body(core_ref, m_ref, s_ref, r_ref, *outs):
        for owner, left_ref in enumerate((m_ref, s_ref)):
            value = dot(left_ref[...], r_ref[...], (0, 0)).astype(low)
            outs[2 * owner][...] = value[: half // 2]
            outs[2 * owner + 1][...] = value[half // 2 :]

    side = pl.BlockSpec((rows, half), lambda g, core: (0, core[0] if part == half else 0))
    return picked(
        body,
        core,
        (1,),
        [(middle, side), (skip, side), (right, pl.BlockSpec((rows, width), lambda g, core: (0, 0)))],
        quarters(rows, width, part // 2),
        "join_term",
        2,
    )


def cross(bit, *pieces):
    kept, got = pieces[: len(pieces) // 2], pieces[len(pieces) // 2 :]
    rows, columns = kept[0].shape
    blocks = len(kept) // 2
    steps = 2 if rows % 32 == 0 else 1

    def body(bit_ref, *refs):
        sent_ref, left_ref = refs[-2:]

        def put(target, owner):
            for block in range(blocks):
                place = owner * blocks + block
                one, two = refs[place], refs[2 * blocks + place]
                target[block] = (one[...].astype(full) + two[...].astype(full)).astype(low)

        for mine in range(2):

            @pl.when(bit_ref[0] == mine)
            def _():
                put(sent_ref, 1 - mine)
                put(left_ref, mine)

    ins = [(piece, pl.BlockSpec((rows // steps, columns), lambda g, bit: (g, 0))) for piece in kept + got]
    out = ((blocks, rows, columns), low, pl.BlockSpec((blocks, rows // steps, columns), lambda g, bit: (0, g, 0)))
    return picked(body, bit, (steps,), ins, [out, out], "cross", 2)


def add_halve(bit, *pairs):
    lead, columns = pairs[0].shape[0], pairs[0].shape[-1]
    sizes = [pair.shape[2] for pair in pairs[::2]]
    total = sum(sizes)
    steps = 2 if len(sizes) == 1 and total % 32 == 0 and total >= 256 else 1

    def body(bit_ref, *refs):
        mine = bit_ref[0]
        for target, place in ((refs[-2], 1 - mine), (refs[-1], mine)):
            begin = 0
            for kept_ref, got_ref in zip(refs[:-2:2], refs[1:-2:2]):
                length = kept_ref.shape[2]
                for each in range(lead):
                    value = kept_ref[each, place].astype(full) + got_ref[each, place].astype(full)
                    target[each, begin : begin + length] = value.astype(low)
                begin += length

    ins = [
        (pair, pl.BlockSpec((lead, 2, pair.shape[2] // steps, columns), lambda g, bit: (0, 0, g, 0)))
        for pair in pairs
    ]
    out = (
        (lead, total, columns),
        low,
        pl.BlockSpec((lead, total // steps, columns), lambda g, bit: (0, g, 0)),
    )
    return picked(body, bit, (steps,), ins, [out, out], "add_halve", 2)


def add_into(target, place, count, one, two):
    rows, columns = one.shape[-2:]
    steps = 2 if rows % 32 == 0 else 1
    block = pl.BlockSpec((1, rows // steps, columns), lambda g: (0, g, 0))

    def body(one_ref, two_ref, *rest):
        rest[-1][...] = (one_ref[...].astype(full) + two_ref[...].astype(full)).astype(low)

    ins = [one.reshape(1, rows, columns), two.reshape(1, rows, columns)]
    return pl.pallas_call(
        body,
        grid=(steps,),
        in_specs=[block, block] + ([] if target is None else [ANY]),
        out_specs=pl.BlockSpec((1, rows // steps, columns), lambda g: (place, g, 0)),
        out_shape=jax.ShapeDtypeStruct((count, rows, columns), low),
        name="add_into",
        input_output_aliases={} if target is None else {2: 0},
        cost_estimate=cost(1.3),
    )(*ins, *([] if target is None else [target]))


def add(one, two):
    return (one.astype(full) + two.astype(full)).astype(low)


def pair_up(own, got, bit):
    rows, columns = own.shape

    def body(bit_ref, own_ref, got_ref, out_ref):
        mine = bit_ref[0]
        out_ref[mine] = own_ref[...]
        out_ref[1 - mine] = got_ref[...]

    flat = pl.BlockSpec((rows, columns), lambda g, bit: (0, 0))
    out = ((2, rows, columns), low, pl.BlockSpec((2, rows, columns), lambda g, bit: (0, 0, 0)))
    return picked(body, bit, (1,), [(own, flat), (got, flat)], [out], "pair_up", 1)[0]


def finish(kind, half, own, got, begin, length, core, layer, targets):
    pieces, _, columns = own.shape
    scale = 1.0 / lax.axis_size("wide")
    aliases = {place + 2: place for place in range(len(targets))}
    source = pl.BlockSpec((pieces, length, columns), lambda g, core: (0, begin // length, 0))
    ins = [(own, source), (got, source)] + [(target, ANY) for target in targets]
    rows = pieces * length

    def chosen(core_ref, which, own_ref, got_ref, place=None):
        sides = [own_ref, got_ref]
        if place is None:
            values = [side[...].reshape(pieces * length, columns) for side in sides]
        else:
            if pieces == 1:
                near = (0, pl.ds(place * (length // 2), length // 2))
            else:
                near = (pl.ds(place * (pieces // 2), pieces // 2),)
            values = [side[near].reshape(pieces * length // 2, columns) for side in sides]
        return jnp.where(core_ref[0] == which, values[0], values[1]).astype(full) * scale

    if kind in ("down", "join"):

        def body(core_ref, own_ref, got_ref, *rest):
            rest[-1][0] = chosen(core_ref, pl.program_id(0), own_ref, got_ref)

        place = layer if kind == "down" else 0
        shape = (2 if kind == "down" else 1, 2 * rows, columns)
        out = (shape, full, pl.BlockSpec((1, rows, columns), lambda g, core: (place, g, 0)))
        return picked(body, core, (2,), ins, [out], "finish_rows", 3, aliases)
    steps = 4 if half is None else 2
    rows = rows // 2 if half is None else rows

    def block(step):
        return step if half is None else 2 * step + half

    def values_of(core_ref, own_ref, got_ref):
        step = pl.program_id(0)
        if half is None:
            return chosen(core_ref, step // 2, own_ref, got_ref, step % 2)
        return chosen(core_ref, step, own_ref, got_ref)

    def body(core_ref, own_ref, got_ref, *rest):
        values = values_of(core_ref, own_ref, got_ref)
        if kind == "up":
            rest[-1][0] = values
            return
        if half == 0:
            rest[-1][0] = values
            return
        last = block(pl.program_id(0)) == 3

        @pl.when(jnp.logical_not(last))
        def _():
            rest[-2][0] = values

        @pl.when(last)
        def _():
            rest[-1][0] = values

    if kind == "up":
        outs = [((2, rows, 4 * columns), full, pl.BlockSpec((1, rows, columns), lambda g, core: (layer, 0, block(g))))]
        return picked(body, core, (steps,), ins, outs, "finish_columns", 3, aliases)

    def spot(step):
        return block(step if half == 0 else jnp.minimum(step, steps - 2))

    outs = [
        ((2, rows, 3 * columns), full, pl.BlockSpec((1, rows, columns), lambda g, core: (layer, 0, spot(g)))),
        ((2, rows, columns), full, pl.BlockSpec((1, rows, columns), lambda g, core: (layer, 0, 0))),
    ]
    if half == 0:
        kept = targets[1:]
        ins, outs, aliases = ins[:3] if targets else ins, outs[:1], {2: 0} if targets else {}
        return (picked(body, core, (steps,), ins, outs, "finish_qkv", 3, aliases)[0], *kept)
    return picked(body, core, (steps,), ins, outs, "finish_qkv_out", 3, aliases)


def small_gradients(total, me, width, shares, blocks):
    part = width // shares
    scale = 1.0 / lax.axis_size("wide")

    def body(me_ref, total_ref, gains_ref, shifts_ref, out_ref, up_ref, down_ref, join_ref):
        values = total_ref[...] * scale
        back = [values[0:8], values[8:16]]
        ahead = [values[16 : 20 + blocks], values[20 + blocks : 24 + 2 * blocks]]
        for place in range(shares):

            @pl.when(me_ref[0] == place)
            def _():
                columns = slice(place * part, place * part + part)
                for layer in range(2):
                    for row, target in ((0, gains_ref), (1, shifts_ref)):
                        target[layer, 0:1] = back[layer][row : row + 1, columns]
                        target[layer, 1:2] = ahead[layer][row + 1 : row + 2, columns]
                    out_ref[layer : layer + 1] = ahead[layer][3:4, columns]
                    down_ref[layer : layer + 1] = ahead[layer][0:1, columns]
                    begin = place * part * blocks
                    while begin < (place + 1) * part * blocks:
                        row, column = begin // width, begin % width
                        length = min(width - column, (place + 1) * part * blocks - begin)
                        at = begin - place * part * blocks
                        piece = ahead[layer][4 + row : 5 + row, column : column + length]
                        up_ref[layer : layer + 1, at : at + length] = piece
                        begin += length
                join_ref[...] = back[1][2:3, columns]

    shapes = [(2, 2, part), (2, 2, part), (2, part), (2, part * blocks), (2, part), (1, part)]
    outs = [(shape, full, pl.BlockSpec(shape, lambda g, me, n=len(shape): (0,) * n)) for shape in shapes]
    ins = [(total, pl.BlockSpec(total.shape, lambda g, me: (0, 0)))]
    return picked(body, me, (1,), ins, outs, "small_gradients", 1)


def after(value, *earlier):
    return lax.optimization_barrier((value,) + earlier)[0] if earlier else value


def swap(values, axis, mask):
    size = lax.axis_size(axis)
    return lax.ppermute(values, axis, [(source, source ^ mask) for source in range(size)])


def masks(axis):
    return [1 << bit for bit in range(lax.axis_size(axis).bit_length() - 1)]


class Order:
    def __init__(self):
        self.last = ()

    def run(self, function, *arrays):
        held = lax.optimization_barrier(tuple(arrays) + self.last)[: len(arrays)]
        out = function(*held)
        self.last = (jax.tree.leaves(out)[0],)
        return out

    def hold(self, *arrays):
        self.last += arrays


def place_bit(axis, mask):
    return ((lax.axis_index(axis) & mask) // mask).astype(jnp.int32).reshape(1)


class Term:
    def __init__(self, order, kind, layer, function, *arrays):
        self.order, self.kind, self.layer, self.half = order, kind, layer, None
        self.core = place_bit("wide", 1)
        sent = order.run(lambda *x: function(*x, 1 - self.core), *arrays)
        self.got = [swap(each, "wide", 1) for each in sent]
        self.columns = sent[0].shape[-1]
        self.keep = lambda: order.run(lambda *x: function(*x, self.core), *arrays)

    def stay(self):
        self.kept, self.keep = self.keep(), None

    def part(self, half):
        other = copy.copy(self)
        other.kept, other.got, other.half = self.kept[half::2], self.got[half::2], half
        return other

    def pass_narrow(self):
        stages = list(reversed(masks("narrow")))
        if isinstance(self.kept, (list, tuple)):
            bit = place_bit("narrow", stages[0])
            blocks = len(self.kept) // 2
            sent, self.kept = self.order.run(lambda *x: cross(bit, *x), *self.kept, *self.got)
            self.got = swap(sent, "narrow", stages.pop(0))
        else:
            blocks = 1
        for mask in stages:
            pairs = [(self.kept, self.got)]
            self.kept, self.got = halve(self.order, "narrow", mask, blocks, pairs, self.columns)

    def pass_first(self, mask):
        swapped = [self.kept[owner * 2 + block] for block in range(2) for owner in range(2)]
        brought = [self.got[owner * 2 + block] for block in range(2) for owner in range(2)]
        bit = place_bit("wide", mask)
        sent, self.kept = self.order.run(lambda *x: cross(bit, *x), *swapped, *brought)
        self.got = swap(sent, "wide", mask)

    def pass_wide(self, mask):
        pairs = list(zip(self.kept, self.got)) if isinstance(self.kept, (list, tuple)) else [(self.kept, self.got)]
        self.kept, self.got = halve(self.order, "wide", mask, 1, pairs, self.columns)

    def add_into(self, target, place, count):
        kept, got = [side.reshape(-1, self.columns) for side in (self.kept, self.got)]
        if target is None:
            return self.order.run(lambda one, two: add_into(None, place, count, one, two), kept, got)
        return self.order.run(lambda target, one, two: add_into(target, place, count, one, two), target, kept, got)

    def finish(self, done, own, got, begin, length):
        targets = done.get(self.kind, ())

        def last(own, got, core, *targets):
            return finish(self.kind, self.half, own, got, begin, length, core, self.layer, targets)

        done[self.kind] = self.order.run(last, own, got, self.core, *targets)


def halve(order, axis, mask, lead, pairs, columns):
    shaped = [array.reshape(lead, 2, -1, columns) for pair in pairs for array in pair]
    bit = place_bit(axis, mask)
    sent, kept = order.run(lambda *x: add_halve(bit, *x), *shaped)
    return kept, swap(sent, axis, mask)


class Reduce:
    def __init__(self, order, terms, passed=()):
        self.order, self.terms = order, terms
        self.down = [mask for mask in masks("wide")[1:] if mask not in passed]
        self.up = list(reversed(passed))
        self.pieces, self.columns = 2 ** len(passed), terms[0].columns
        self.parts = [(term.kept, term.got) for term in terms]
        self.lengths, self.first = [each.size // self.columns for each, _ in self.parts], True
        self.joining, self.closed = None, False

    def step(self):
        if self.closed:
            return
        if self.down:
            mask = self.down.pop(0)
            rows = [kept.size // self.columns for kept, _ in self.parts]
            even = all(each % 32 == 0 for each in rows)
            if self.first and even:
                self.pieces, self.lengths = 2 * self.pieces, [each // 2 for each in rows]
            self.first = False
            if even:
                self.up.insert(0, mask)
                self.parts = [halve(self.order, "wide", mask, 1, self.parts, self.columns)]
            else:
                flat = [[side.reshape(-1, self.columns) for side in pair] for pair in self.parts]
                pair = [jnp.concatenate(sides) for sides in zip(*flat)]
                total = self.order.run(add, *pair)
                self.parts = [(total, swap(total, "wide", mask))]
            return
        kept, got = [array.reshape(-1, self.columns) for array in self.parts[0]]
        if self.joining is None:
            total = self.order.run(add, kept, got)
        else:
            bit = place_bit("wide", self.joining)
            total = self.order.run(lambda *x: pair_up(*x, bit), kept, got).reshape(-1, self.columns)
        if self.up:
            self.joining = self.up.pop(0)
            self.parts = [(total, swap(total, "wide", self.joining))]
        else:
            self.parts = [(total, swap(total, "wide", 1))]
            self.closed = True

    def finish(self, done):
        own, got = [array.reshape(self.pieces, -1, self.columns) for array in self.parts[0]]
        begin = 0
        for term, length in zip(self.terms, self.lengths):
            term.finish(done, own, got, begin, length)
            begin += length


def on_device(
    tokens,
    skip,
    flags,
    cotangent,
    norm_gains,
    norm_biases,
    qkv_weight,
    out_weight,
    out_bias,
    up_weight,
    up_bias,
    down_weight,
    down_bias,
    skip_weight,
    skip_bias,
):
    items, seq_rows, width = tokens.shape
    rows = items * seq_rows
    me = lax.axis_index("narrow")
    shares = lax.axis_size("narrow")
    spots = jnp.stack([me, lax.axis_index("wide")]).astype(jnp.int32)
    order = Order()

    def fetches(layer):
        return (
            Fetch([(qkv_weight, layer)], (1, 2)),
            Fetch([(out_weight, layer), (up_weight, layer)], (1, 2)),
            Fetch([(down_weight, layer)], (1, 4)),
        )

    fetch_qkv0, fetch_up0, fetch_down0 = fetches(0)
    fetch_qkv1, fetch_up1, fetch_down1 = fetches(1)
    fetch_join = Fetch([(skip_weight, None)], (1, 4))
    qkv0, qkv1 = [Weight(each, 0, width, spots) for each in (fetch_qkv0, fetch_qkv1)]
    out0, out1 = [Weight(each, 0, width, spots) for each in (fetch_up0, fetch_up1)]
    up0, up1 = [Weight(each, 1, width, spots) for each in (fetch_up0, fetch_up1)]
    down0, down1 = [Weight(each, 0, width, spots) for each in (fetch_down0, fetch_down1)]
    join = Weight(fetch_join, 0, width, spots)

    small = (norm_gains, norm_biases, out_bias, down_bias, skip_bias, up_bias)
    held = order.run(pack_small, *small)[None]
    for mask in masks("narrow"):
        held = jnp.concatenate([held, swap(held, "narrow", mask)])
    fetch_qkv0.fetch(*order.last)
    fetch_up0.fetch(held)
    fetch_down0.fetch(fetch_up0.sent)
    fetch_join.fetch(fetch_down0.sent)
    fetch_qkv1.fetch(fetch_join.sent)
    place = me.astype(jnp.int32).reshape(1)
    lines = order.run(lambda x: unpack_small(x, place, small, width), held)

    def line(row):
        return lines[row : row + 1]

    gains, shifts = [[line(2 * layer + each) for each in range(2)] for layer in range(2)], None
    shifts = [[line(4 + 2 * layer + each) for each in range(2)] for layer in range(2)]
    out_biases, down_biases, join_shift = [line(8), line(9)], [line(10), line(11)], line(12)
    blocks = up0.blocks
    up_biases = [lines[13 + layer * blocks : 13 + (layer + 1) * blocks].reshape(1, -1) for layer in range(2)]

    tokens_flat, skip_flat, cotangent_flat = [array.reshape(rows, width) for array in (tokens, skip, cotangent)]
    lengths = PATCHES + 1 + CAPTION * flags
    valid = lax.broadcasted_iota(jnp.int32, (items, seq_rows), 1) < lengths[:, None]
    keep = valid.reshape(rows, 1).astype(full)
    dz1 = jnp.where(keep > 0, cotangent_flat, 0)

    fetch_qkv0.share(1)
    fetch_qkv0.share(0)
    order.hold(*fetch_up0.got())
    fetch_up0.share(1)
    a0, packed0 = order.run(lambda *x: project_qkv(*x, qkv0), tokens_flat, gains[0][0], shifts[0][0])
    order.hold(*fetch_down0.got())
    fetch_down0.share(1, a0)
    fetch_up1.fetch(a0)
    fetch_down1.fetch(fetch_up1.sent)
    packed0 = packed0.reshape(3, items, seq_rows, width)
    mixed0, totals0 = order.run(lambda *x: attend(*x, items, seq_rows), packed0, lengths)
    fetch_up0.share(0, mixed0)
    fetch_down0.share(0, mixed0)
    order.hold(*fetch_join.got(), *fetch_qkv1.got())
    fetch_join.share(1, mixed0)
    fetch_qkv1.share(1, mixed0)
    mixed0 = mixed0.reshape(rows, width)
    m0, second0, hidden0, slope0, middle = order.run(
        lambda x, o, ob, g, s, ub, db: feed_forward(x, o, out0, ob, g, s, up0, ub, down0, db),
        tokens_flat, mixed0, out_biases[0], gains[0][1], shifts[0][1], up_biases[0], down_biases[0],
    )
    fetch_join.share(0, middle)
    fetch_qkv1.share(0, middle)
    order.hold(*fetch_up1.got(), *fetch_down1.got())
    fetch_up1.share(1, middle)
    fetch_down1.share(1, middle)
    entry, a1, packed1 = order.run(
        lambda m, s, jb, g, sh: join_qkv(m, s, join, jb, g, sh, qkv1),
        middle, skip_flat, join_shift, gains[1][0], shifts[1][0],
    )
    packed1 = packed1.reshape(3, items, seq_rows, width)
    mixed1, totals1 = order.run(lambda *x: attend(*x, items, seq_rows), packed1, lengths)
    fetch_up1.share(0, mixed1)
    fetch_down1.share(0, mixed1)
    mixed1 = mixed1.reshape(rows, width)
    m1, second1, hidden1, slope1, output = order.run(
        lambda x, o, ob, g, s, ub, db, k: feed_forward(x, o, out1, ob, g, s, up1, ub, down1, db, k),
        entry, mixed1, out_biases[1], gains[1][1], shifts[1][1], up_biases[1], down_biases[1], keep,
    )

    done = {}
    term_down1 = Term(order, "down", 1, down_term, hidden1, dz1)
    term_down1.stay()
    term_down1.pass_narrow()
    du, dm, db, do, sums1 = order.run(
        lambda y, z, s, m, g: feed_forward_back(y, z, s, down1, up1, m, g, out1),
        dz1, dz1, slope1, m1, gains[1][1],
    )
    term_up1 = Term(order, "up", 1, up_term, second1, du)
    term_up1.stay()
    term_up1.pass_narrow()
    total = term_down1.add_into(None, 0, 3)
    dpacked = order.run(
        lambda *x: attend_back(*x, items, seq_rows), packed1, do.reshape(items, seq_rows, width), totals1, lengths
    )
    flat_packed = dpacked.reshape(3, rows, width)
    term_qkv1 = Term(order, "qkv", 1, qkv_out_term, a1, flat_packed, mixed1, db)
    term_qkv1.stay()
    term_qkv1.pass_narrow()
    total = term_up1.add_into(total, 1, 3)
    dentry, dmiddle, dz0, skip_grad, sums3 = order.run(
        lambda gp, x, g, dm: project_back(gp, qkv1, x, g, dm, join), flat_packed, entry, gains[1][0], dm
    )
    term_join = Term(order, "join", 1, join_term, middle, skip_flat, dentry)
    term_join.stay()
    term_join.pass_narrow()
    term_down0 = Term(order, "down", 0, down_term, hidden0, dz0)
    term_down0.stay()
    total = term_qkv1.add_into(total, 2, 3)
    size = lax.axis_size("wide")
    groups = [[device + core for device in range(0, size, 2)] for core in range(2)]
    flat_total = total.reshape(-1, width)
    part = lax.psum_scatter(flat_total, "wide", axis_index_groups=groups, scatter_dimension=0, tiled=True)
    term_down0.pass_first(2)

    du, dm, db, do, sums0 = order.run(
        lambda y, z, s, m, g: feed_forward_back(y, z, s, down0, up0, m, g, out0),
        dmiddle, dz0, slope0, m0, gains[0][1],
    )
    term_join.pass_wide(2)
    term_up0 = Term(order, "up", 0, up_term, second0, du)
    term_up0.stay()
    term_down0.pass_narrow()
    term_up0.pass_narrow()
    dpacked = order.run(
        lambda *x: attend_back(*x, items, seq_rows), packed0, do.reshape(items, seq_rows, width), totals0, lengths
    )
    order.hold(term_down0.got, term_join.got)
    flat_packed = dpacked.reshape(3, rows, width)
    term_qkv0 = Term(order, "qkv", 0, qkv_out_term, a0, flat_packed, mixed0, db)
    term_qkv0.stay()
    one, two = term_qkv0.part(0), term_qkv0.part(1)
    early = 4 if shares == 2 else None
    if early:
        two.pass_wide(early)
    one.pass_narrow()
    order.hold(term_up0.got, part)
    first = Reduce(order, [term_down0, term_join], (2,))
    first.step()
    gathered = lax.all_gather(after(part, *order.last), "wide", axis_index_groups=groups, tiled=True)
    second = Reduce(order, [term_up0])
    second.step()
    tokens_grad, sums2 = order.run(
        lambda gp, x, g, dm: project_back(gp, qkv0, x, g, dm), flat_packed, tokens_flat, gains[0][0], dm
    )
    minor = jnp.concatenate([sums2, sums3, sums0, sums1])
    minor_stages = [("narrow", mask) for mask in masks("narrow")] + [("wide", mask) for mask in masks("wide")]
    minor_got = swap(minor, *minor_stages[0])

    def minor_step():
        nonlocal minor, minor_got
        if minor_stages:
            minor_stages.pop(0)
            minor = order.run(lambda one, two: one + two, minor, minor_got)
            if minor_stages:
                minor_got = swap(minor, *minor_stages[0])

    two.pass_narrow()
    third = Reduce(order, [one])
    third.step()
    first.step()
    second.step()
    minor_step()
    fourth = Reduce(order, [two], (early,) if early else ())
    fourth.step()
    third.step()
    minor_step()
    first.step()
    fourth.step()
    second.step()
    third.step()
    minor_step()
    first.step()
    fourth.step()
    second.step()
    third.step()
    order.hold(gathered)
    other = swap(after(gathered, *order.last), "wide", 1)
    minor_step()
    first.step()
    fourth.step()
    second.step()
    third.step()
    own, got = gathered.reshape(1, -1, width), other.reshape(1, -1, width)
    for which, term in enumerate((term_down1, term_up1, term_qkv1)):
        term.finish(done, own, got, which * (own.shape[1] // 3), own.shape[1] // 3)
    second.step()
    first.step()
    fourth.step()
    third.step()
    minor_step()
    first.finish(done)
    second.step()
    fourth.step()
    third.step()
    for each in (first, second, third, fourth):
        while not each.closed:
            each.step()
    while minor_stages:
        minor_step()
    second.finish(done)
    fourth.finish(done)
    third.finish(done)
    small = order.run(lambda x: small_gradients(x, place, width, shares, up1.blocks), minor)

    return (
        output.reshape(tokens.shape),
        tokens_grad.reshape(tokens.shape),
        skip_grad.reshape(tokens.shape),
        small[0],
        small[1],
        done["qkv"][0],
        done["qkv"][1],
        small[2],
        done["up"][0],
        small[3],
        done["down"][0],
        small[4],
        done["join"][0][0],
        small[5].reshape(-1),
    )


def solution(mesh):
    placed = (
        P(("wide", "narrow"), None, None),
        P(("wide", "narrow"), None, None),
        P(("wide", "narrow")),
        P(("wide", "narrow"), None, None),
        P(None, None, "narrow"),
        P(None, None, "narrow"),
        P(None, "narrow", None),
        P(None, "narrow", None),
        P(None, "narrow"),
        P(None, "narrow", None),
        P(None, "narrow"),
        P(None, "narrow", None),
        P(None, "narrow"),
        P("narrow", None),
        P("narrow"),
    )
    return jax.shard_map(
        on_device,
        mesh=mesh,
        in_specs=placed,
        out_specs=(
            P(("wide", "narrow"), None, None),
            P(("wide", "narrow"), None, None),
            P(("wide", "narrow"), None, None),
            P(None, None, "narrow"),
            P(None, None, "narrow"),
            P(None, "narrow", None),
            P(None, "narrow", None),
            P(None, "narrow"),
            P(None, "narrow", None),
            P(None, "narrow"),
            P(None, "narrow", None),
            P(None, "narrow"),
            P("narrow", None),
            P("narrow"),
        ),
        check_vma=False,
    )
```

```python
import copy
import math

import jax
import jax.numpy as jnp
from jax import lax
from jax.experimental import pallas as pl
from jax.experimental.pallas import tpu as pltpu
from jax.sharding import PartitionSpec as P

HEAD_DIM = 64
PATCHES = 256
CAPTION = 77
PAIR = 2 * HEAD_DIM


epsilon = 1e-05
masked_score = -1e30
low = jnp.bfloat16
full = jnp.float32
SPARE = 14
ANY = pl.BlockSpec(memory_space=pl.ANY)
SCALARS = pl.BlockSpec(memory_space=pltpu.SMEM)


def dot(left, right, contract=(1, 0)):
    dims = (((contract[0],), (contract[1],)), ((), ()))
    return lax.dot_general(left, right, dims, preferred_element_type=full)


def normalize(values):
    centred = values - jnp.mean(values, axis=-1, keepdims=True)
    factor = lax.rsqrt(jnp.mean(centred * centred, axis=-1, keepdims=True) + epsilon)
    return centred * factor, factor


def normalize_back(upstream, normed, factor):
    return factor * (
        upstream
        - jnp.mean(upstream, axis=-1, keepdims=True)
        - normed * jnp.mean(upstream * normed, axis=-1, keepdims=True)
    )


def column_sum(values):
    return jnp.sum(values.astype(full), axis=0, keepdims=True)


def whole(shape):
    return pl.BlockSpec(shape, lambda *grid: (0,) * len(shape))


def cost(micros):
    return pl.CostEstimate(flops=int(micros * 3 * 10**8), bytes_accessed=0, transcendentals=0)


def room(ins, outs, scratch, spare):
    total = spare * 2**20
    for shape, kind, spec in [(array.shape, array.dtype, spec) for array, spec in ins] + list(outs):
        if spec.block_shape is not None and spec.memory_space is None:
            total += 2 * math.prod(spec.block_shape) * jnp.dtype(kind).itemsize
    for piece in scratch:
        if piece.memory_space == pltpu.VMEM:
            total += math.prod(piece.shape) * jnp.dtype(piece.dtype).itemsize
    return total


def call(body, grid, ins, outs, name, micros, scratch=(), spare=6):
    return pl.pallas_call(
        body,
        grid=grid,
        in_specs=[spec for _, spec in ins],
        out_specs=[spec for _, _, spec in outs],
        out_shape=[jax.ShapeDtypeStruct(shape, kind) for shape, kind, _ in outs],
        scratch_shapes=list(scratch),
        name=name,
        cost_estimate=cost(micros),
        compiler_params=pltpu.CompilerParams(vmem_limit_bytes=room(ins, outs, scratch, spare)),
    )(*[array for array, _ in ins])


class Fetch:
    def __init__(self, arrays, sharing):
        self.arrays, self.sharing = arrays, list(sharing)
        self.rows = arrays[0][0].shape[-2]
        while self.rows % (16 << len(self.sharing)):
            self.sharing.pop()
        self.length = self.rows >> len(self.sharing)

    def quarter(self, place):
        return sum(((place // mask) & 1) << bit for bit, mask in enumerate(self.sharing))

    def fetch(self, *earlier):
        found = []
        for array, layer in self.arrays:
            array = after(array, *earlier)
            lead = () if layer is None else (layer,)
            begin = self.quarter(lax.axis_index("wide")) * self.length
            sizes = (1,) * len(lead) + (self.length, array.shape[-1])
            found.append(lax.dynamic_slice(array, lead + (begin, 0), sizes).reshape(self.length, -1))
        self.sent = (jnp.concatenate(found, axis=1) if len(found) > 1 else found[0])[None]
        held = self.sent
        for mask in masks("narrow"):
            held = jnp.concatenate([held, swap(held, "narrow", mask)])
        self.pieces = {0: held[1:]}

    def share(self, which, *earlier):
        if which < len(self.sharing):
            mask = self.sharing[which]
            got = {key ^ (1 << which): swap(after(piece, *earlier), "wide", mask) for key, piece in self.pieces.items()}
            self.pieces.update(got)

    def got(self):
        return list(self.pieces.values())


class Weight:
    def __init__(self, fetched, which, width, spots):
        self.fetched, self.spots, self.width = fetched, spots, width
        self.array, self.layer = fetched.arrays[which]
        self.begin = sum(array.shape[-1] for array, _ in fetched.arrays[:which])
        self.rows, columns = self.array.shape[-2:]
        self.shares = lax.axis_size("narrow")
        self.blocks = columns // width
        self.total = self.rows * self.shares

    def arrays(self):
        return [self.array] + self.fetched.got()

    def scratch(self):
        copies = 1 + len(self.fetched.pieces) * (self.shares - 1)
        return [pltpu.VMEM((self.blocks, self.total, self.width), low), pltpu.SemaphoreType.DMA((self.blocks, copies))]

    def copies(self, spots, refs, held, signals, block):
        own, pieces = refs[0], refs[1:]
        me, length = spots[0], self.fetched.length
        own = own if self.layer is None else own.at[self.layer]
        columns = pl.ds(block * self.width, self.width)
        begin = pl.multiple_of(me * self.rows, 16)
        found = [(own.at[:, columns], begin, self.rows)]
        columns = pl.ds(self.begin + block * self.width, self.width)
        for key, piece in zip(self.fetched.pieces, pieces):
            for offset in range(1, self.shares):
                begin = (me ^ offset) * self.rows + (self.fetched.quarter(spots[1]) ^ key) * length
                found.append((piece.at[offset - 1, :, columns], pl.multiple_of(begin, 16), length))
        return [
            pltpu.make_async_copy(source, held.at[block, pl.ds(begin, length)], signals.at[block, place])
            for place, (source, begin, length) in enumerate(found)
        ]

    def wait(self, *refs, block=0):
        for copy in self.copies(*refs, block):
            copy.wait()


def weighted(body, weights, grid, ins, outs, name, micros, scratch=(), first=((0, 0),), spare=SPARE):
    spots = weights[0].spots
    operands = [(spots, SCALARS)] + [(array, ANY) for weight in weights for array in weight.arrays()]
    counts = [len(weight.arrays()) for weight in weights]
    extra = [piece for weight in weights for piece in weight.scratch()]

    def wrapped(*refs):
        spots_ref, rest = refs[0], list(refs[1:])
        sources = []
        for count in counts:
            sources.append(rest[:count])
            rest = rest[count:]
        spare = rest[len(rest) - len(extra) :]
        rest = rest[: len(rest) - len(extra)]
        handles = []
        for place, weight in enumerate(weights):
            held, signals = spare[2 * place : 2 * place + 2]
            refs_of = (spots_ref, sources[place], held, signals)
            handles.append((weight, refs_of, held))

        everything = [(place, block) for place, weight in enumerate(weights) for block in range(weight.blocks)]

        def begin(wanted):
            for place, block in wanted:
                weight, refs_of, _ = handles[place]
                for copy in weight.copies(*refs_of, block):
                    copy.start()

        @pl.when(pl.program_id(0) == 0)
        def _():
            begin(first)

        def ready(place, block=0, then=False):
            weight, refs_of, held = handles[place]
            weight.wait(*refs_of, block=block)
            if then:
                begin([each for each in everything if each not in first])

        body(ready, [held for _, _, held in handles], *rest)

    return call(wrapped, grid, operands + ins, outs, name, micros, list(scratch) + extra, spare)


def pack_small(*small):
    part = small[0].shape[-1]
    counts = [piece.size // part for piece in small]

    def body(*refs):
        row = 0
        for ref in refs[:-1]:
            values = ref[...].reshape(-1, ref.shape[-1])
            for each in range(values.shape[0]):
                for begin in range(0, values.shape[1], part):
                    refs[-1][row : row + 1] = values[each : each + 1, begin : begin + part].astype(full)
                    row += 1
        refs[-1][row:] = jnp.zeros((refs[-1].shape[0] - row, part), full)

    flat = [piece.reshape((1,) * (2 - piece.ndim) + piece.shape) for piece in small]
    rows = -(-sum(counts) // 16) * 16
    out = ((rows, part), full, whole((rows, part)))
    return call(body, (1,), [(piece, whole(piece.shape)) for piece in flat], [out], "pack_small", 1)[0].astype(low)


def unpack_small(parts, me, small, width):
    shares, _, part = parts.shape
    lines = [(piece.size // piece.shape[-1], piece.shape[-1] // part) for piece in small]
    total = sum(count * many for count, many in lines)
    rows = -(-total // 8) * 8

    def body(me_ref, parts_ref, out_ref):
        values = parts_ref[...].astype(full)
        for mine in range(shares):

            @pl.when(me_ref[0] == mine)
            def _():
                for owner in range(shares):
                    source, target = 0, 0
                    for count, many in lines:
                        for each in range(count):
                            for piece in range(many):
                                at = owner * many * part + piece * part
                                row, column = target + at // width, at % width
                                line = values[owner ^ mine, source : source + 1]
                                out_ref[row : row + 1, column : column + part] = line
                                source += 1
                            target += many
        if rows > total:
            out_ref[total:] = jnp.zeros((rows - total, width), full)

    ins = [(parts, pl.BlockSpec(parts.shape, lambda g, me: (0, 0, 0)))]
    out = ((rows, width), full, pl.BlockSpec((rows, width), lambda g, me: (0, 0)))
    return picked(body, me, (1,), ins, [out], "unpack_small", 1)[0]


def project_qkv(inputs, gain, shift, weight):
    rows, width = inputs.shape

    def body(ready, held, x_ref, gain_ref, shift_ref, a_ref, out_ref):
        step = pl.program_id(0)

        @pl.when(step == 0)
        def _():
            normed, _ = normalize(x_ref[...].astype(full))
            a_ref[...] = (normed * gain_ref[...] + shift_ref[...]).astype(low)
            ready(0, 0, then=True)

        @pl.when(step > 0)
        def _():
            ready(0, step)

        scale = jnp.where(step == 0, HEAD_DIM ** (-0.5), 1.0)
        out_ref[0] = (dot(a_ref[...], held[0][step]).astype(low).astype(full) * scale).astype(low)

    return weighted(
        body,
        [weight],
        (3,),
        [
            (inputs, whole((rows, width))),
            (gain, whole((1, width))),
            (shift, whole((1, width))),
        ],
        [
            ((rows, width), low, whole((rows, width))),
            ((3, rows, width), low, pl.BlockSpec((1, rows, width), lambda j: (j, 0, 0))),
        ],
        "project_qkv",
        7,
    )


def join_qkv(middle, skip, join_weight, join_shift, gain, shift, weight):
    rows, width = middle.shape

    def body(ready, held, m_ref, s_ref, jb_ref, gain_ref, shift_ref, e_ref, a_ref, out_ref):
        step = pl.program_id(0)

        @pl.when(step == 0)
        def _():
            ready(0, then=True)
            entry = dot(m_ref[...], held[0][0, :width]) + dot(s_ref[...], held[0][0, width:]) + jb_ref[...]
            e_ref[...] = entry
            normed, _ = normalize(entry)
            a_ref[...] = (normed * gain_ref[...] + shift_ref[...]).astype(low)

        ready(1, step)
        scale = jnp.where(step == 0, HEAD_DIM ** (-0.5), 1.0)
        out_ref[0] = (dot(a_ref[...], held[1][step]).astype(low).astype(full) * scale).astype(low)

    return weighted(
        body,
        [join_weight, weight],
        (3,),
        [
            (middle, whole((rows, width))),
            (skip, whole((rows, width))),
            (join_shift, whole((1, width))),
            (gain, whole((1, width))),
            (shift, whole((1, width))),
        ],
        [
            ((rows, width), full, whole((rows, width))),
            ((rows, width), low, whole((rows, width))),
            ((3, rows, width), low, pl.BlockSpec((1, rows, width), lambda j: (j, 0, 0))),
        ],
        "join_qkv",
        11,
        first=((0, 0), (1, 0)),
    )


def head_masks(seq_rows):
    lane = lax.broadcasted_iota(jnp.int32, (seq_rows, PAIR), 1)
    return [lane < HEAD_DIM, lane >= HEAD_DIM]


def pairs_of(width):
    pairs = width // PAIR
    return pairs, max(group for group in (1, 2, 3) if pairs % group == 0)


def attend(packed, lengths, items, seq_rows):
    width = packed.shape[-1]
    pairs, group = pairs_of(width)

    def body(length_ref, q_ref, k_ref, v_ref, out_ref, total_ref):
        counts = lax.broadcasted_iota(jnp.int32, (seq_rows, seq_rows), 1) < length_ref[pl.program_id(0)]
        for pair in range(group):
            columns = slice(pair * PAIR, (pair + 1) * PAIR)
            queries, keys, values = q_ref[0, 0, :, columns], k_ref[0, 0, :, columns], v_ref[0, 0, :, columns]
            mixed = jnp.zeros((seq_rows, PAIR), full)
            for head, lanes in enumerate(head_masks(seq_rows)):
                scores = dot(jnp.where(lanes, queries, 0), keys, (1, 1))
                scores = jnp.where(counts, scores, masked_score)
                largest = jnp.max(scores, axis=1, keepdims=True)
                weights = jnp.exp(scores - largest)
                total = jnp.sum(weights, axis=1, keepdims=True)
                mixed += dot(weights.astype(low), jnp.where(lanes, values, 0)) * (1.0 / total)
                total_ref[0, pair, head : head + 1] = (largest + jnp.log(total)).T
            out_ref[0, :, columns] = mixed.astype(low)

    def block(which):
        return pl.BlockSpec((1, 1, seq_rows, group * PAIR), lambda n, h: (which, n, 0, h))

    return call(
        body,
        (items, pairs // group),
        [(lengths, SCALARS), (packed, block(0)), (packed, block(1)), (packed, block(2))],
        [
            (
                (items, seq_rows, width),
                low,
                pl.BlockSpec((1, seq_rows, group * PAIR), lambda n, h: (n, 0, h)),
            ),
            (
                (items, pairs, 8, seq_rows),
                full,
                pl.BlockSpec((1, group, 8, seq_rows), lambda n, h: (n, h, 0, 0)),
            ),
        ],
        "attend",
        10,
        spare=14,
    )


def attend_back(packed, grad_mixed, totals, lengths, items, seq_rows):
    width = packed.shape[-1]
    pairs, group = pairs_of(width)
    sides = [slice(0, PATCHES), slice(PATCHES, seq_rows)]

    def body(length_ref, q_ref, k_ref, v_ref, g_ref, total_ref, out_ref):
        row = PATCHES + lax.broadcasted_iota(jnp.int32, (seq_rows - PATCHES, seq_rows), 0)
        counts = row < length_ref[pl.program_id(0)]
        for pair in range(group):
            columns = slice(pair * PAIR, (pair + 1) * PAIR)
            queries, keys, values = q_ref[0, 0, :, columns], k_ref[0, 0, :, columns], v_ref[0, 0, :, columns]
            upstream = g_ref[0, :, columns]
            grad_queries = jnp.zeros((PAIR, seq_rows), full)
            grad_keys, grad_values = [0.0, 0.0], [0.0, 0.0]
            for head, lanes in enumerate(head_masks(seq_rows)):
                own_queries = jnp.where(lanes, queries, 0)
                own_upstream = jnp.where(lanes, upstream, 0)
                own_keys = jnp.where(lanes, keys, 0)
                parts, centre = [], 0.0
                for side, rows in enumerate(sides):
                    scores = dot(keys[rows], own_queries, (1, 1))
                    if side:
                        scores = jnp.where(counts, scores, masked_score)
                    probs = jnp.exp(scores - total_ref[0, pair, head : head + 1])
                    grad_probs = dot(values[rows], own_upstream, (1, 1))
                    centre += jnp.sum(grad_probs * probs, axis=0, keepdims=True)
                    parts.append((probs, grad_probs))
                for side, (probs, grad_probs) in enumerate(parts):
                    grad_scores = (probs * (grad_probs - centre)).astype(low)
                    grad_values[side] += dot(probs.astype(low), own_upstream)
                    grad_keys[side] += dot(grad_scores, own_queries)
                    grad_queries += dot(own_keys[sides[side]], grad_scores, (0, 0))
            out_ref[0, 0, :, columns] = (grad_queries.T * HEAD_DIM ** (-0.5)).astype(low)
            for side, rows in enumerate(sides):
                out_ref[1, 0, rows, columns] = grad_keys[side].astype(low)
                out_ref[2, 0, rows, columns] = grad_values[side].astype(low)

    def block(which):
        return pl.BlockSpec((1, 1, seq_rows, group * PAIR), lambda n, h: (which, n, 0, h))

    return call(
        body,
        (items, pairs // group),
        [
            (lengths, SCALARS),
            (packed, block(0)),
            (packed, block(1)),
            (packed, block(2)),
            (grad_mixed, pl.BlockSpec((1, seq_rows, group * PAIR), lambda n, h: (n, 0, h))),
            (totals, pl.BlockSpec((1, group, 8, seq_rows), lambda n, h: (n, h, 0, 0))),
        ],
        [
            (
                (3, items, seq_rows, width),
                low,
                pl.BlockSpec((3, 1, seq_rows, group * PAIR), lambda n, h: (0, n, 0, h)),
            ),
        ],
        "attend_back",
        15,
        spare=14,
    )[0]


def gelu_parts(before):
    decay = jnp.exp(before * before * -0.5)
    inverse = pl.reciprocal(1.0 + (0.3275911 * 0.5**0.5) * jnp.abs(before), approx=False)
    series = 1.061405429 * 0.5
    for term in (-1.453152027, 1.421413741, -0.284496736, 0.254829592):
        series = series * inverse + term * 0.5
    below = series * inverse * decay
    share = jnp.where(before >= 0, 1.0 - below, below)
    return before * share, share + before * decay * 0.3989422804014327


def feed_forward(inputs, mixed, out_weight, out_bias, gain, shift, up_weight, up_bias, down_weight, down_bias, keep=None):
    rows, width = inputs.shape
    steps = up_weight.blocks
    hidden = steps * width

    def body(ready, held, x_ref, o_ref, ob_ref, gain_ref, shift_ref, ub_ref, db_ref, *rest):
        m_ref, a_ref, g_ref, s_ref, y_ref, total = rest[-6:]
        step = pl.program_id(0)

        @pl.when(step == 0)
        def _():
            ready(0, then=True)
            middle = x_ref[...].astype(full) + dot(o_ref[...], held[0][0]) + ob_ref[...]
            m_ref[...] = middle
            normed, _ = normalize(middle)
            a_ref[...] = (normed * gain_ref[...] + shift_ref[...]).astype(low)
            total[...] = middle + db_ref[...]

        ready(1, step)
        before = dot(a_ref[...], held[1][step]) + ub_ref[...]
        value, slope = gelu_parts(before)
        g_ref[...] = value.astype(low)
        s_ref[...] = slope.astype(low)

        @pl.when(step == 0)
        def _():
            ready(2)

        total[...] += dot(g_ref[...], held[2][0, pl.ds(pl.multiple_of(step * width, width), width)])

        @pl.when(step == steps - 1)
        def _():
            value = total[...]
            if keep is not None:
                value = jnp.where(rest[0][...] > 0, value, 0.0)
            y_ref[...] = value.astype(low)

    return weighted(
        body,
        [out_weight, up_weight, down_weight],
        (steps,),
        [
            (inputs, whole((rows, width))),
            (mixed, whole((rows, width))),
            (out_bias, whole((1, width))),
            (gain, whole((1, width))),
            (shift, whole((1, width))),
            (up_bias, pl.BlockSpec((1, width), lambda j: (0, j))),
            (down_bias, whole((1, width))),
        ]
        + ([] if keep is None else [(keep, whole((rows, 1)))]),
        [
            ((rows, width), full, whole((rows, width))),
            ((rows, width), low, whole((rows, width))),
            ((rows, hidden), low, pl.BlockSpec((rows, width), lambda j: (0, j))),
            ((rows, hidden), low, pl.BlockSpec((rows, width), lambda j: (0, j))),
            ((rows, width), low, whole((rows, width))),
        ],
        "feed_forward",
        23,
        scratch=[pltpu.VMEM((rows, width), full)],
        first=((0, 0), (1, 0)),
    )


def feed_forward_back(upstream, rounded, slope, down_weight, up_weight, middle, gain, out_weight):
    rows, width = upstream.shape
    steps = up_weight.blocks
    hidden = steps * width

    def body(ready, held, y_ref, dz_ref, s_ref, m_ref, gain_ref, du_ref, dm_ref, db_ref, do_ref, sums_ref, total):
        step = pl.program_id(0)

        @pl.when(step == 0)
        def _():
            sums_ref[0:1] = column_sum(dz_ref[...])
            total[...] = jnp.zeros_like(total)
            ready(0, then=True)

        down = held[0][0, pl.ds(pl.multiple_of(step * width, width), width)]
        grad = (dot(dz_ref[...], down, (1, 1)) * s_ref[...].astype(full)).astype(low)
        du_ref[...] = grad
        sums_ref[pl.ds(4 + step, 1)] = column_sum(grad)
        ready(1, step)
        total[...] += dot(grad, held[1][step], (1, 1))

        @pl.when(step == steps - 1)
        def _():
            grad_second = total[...]
            normed, factor = normalize(m_ref[...])
            sums_ref[1:2] = column_sum(grad_second * normed)
            sums_ref[2:3] = column_sum(grad_second)
            grad_middle = y_ref[...].astype(full) + normalize_back(grad_second * gain_ref[...], normed, factor)
            dm_ref[...] = grad_middle
            branch = grad_middle.astype(low)
            db_ref[...] = branch
            sums_ref[3:4] = column_sum(branch)
            ready(2)
            do_ref[...] = dot(branch, held[2][0], (1, 1)).astype(low)

    return weighted(
        body,
        [down_weight, up_weight, out_weight],
        (steps,),
        [
            (upstream, whole((rows, width))),
            (rounded, whole((rows, width))),
            (slope, pl.BlockSpec((rows, width), lambda j: (0, j))),
            (middle, whole((rows, width))),
            (gain, whole((1, width))),
        ],
        [
            ((rows, hidden), low, pl.BlockSpec((rows, width), lambda j: (0, j))),
            ((rows, width), full, whole((rows, width))),
            ((rows, width), low, whole((rows, width))),
            ((rows, width), low, whole((rows, width))),
            ((4 + steps, width), full, whole((4 + steps, width))),
        ],
        "feed_forward_back",
        21,
        scratch=[pltpu.VMEM((rows, width), full)],
        first=((0, 0), (1, 0)),
    )


def project_back(grad_packed, weight, inputs, gain, grad_middle, join_weight=None):
    rows, width = inputs.shape
    joined = join_weight is not None

    def body(ready, held, g_ref, x_ref, gain_ref, dm_ref, *rest):
        if joined:
            de_ref, dx_ref, dz_ref, skip_ref, sums_ref, total = rest
        else:
            dx_ref, sums_ref, total = rest
        step = pl.program_id(0)

        @pl.when(step == 0)
        def _():
            total[...] = jnp.zeros_like(total)
            ready(0, 0, then=True)

        @pl.when(step > 0)
        def _():
            ready(0, step)

        total[...] += dot(g_ref[0], held[0][step], (1, 1))

        @pl.when(step == 2)
        def _():
            grad_first = total[...]
            normed, factor = normalize(x_ref[...].astype(full))
            sums_ref[0:1] = column_sum(grad_first * normed)
            sums_ref[1:2] = column_sum(grad_first)
            grad = dm_ref[...] + normalize_back(grad_first * gain_ref[...], normed, factor)
            if joined:
                entry = grad.astype(low)
                de_ref[...] = entry
                sums_ref[2:3] = column_sum(entry)
                ready(1)
                grad = dot(entry, held[1][0, :width], (1, 1))
                dx_ref[...] = grad
                dz_ref[...] = grad.astype(low)
                skip_ref[...] = dot(entry, held[1][0, width:], (1, 1))
            else:
                dx_ref[...] = grad

    ins = [
        (grad_packed, pl.BlockSpec((1, rows, width), lambda j: (j, 0, 0))),
        (inputs, whole((rows, width))),
        (gain, whole((1, width))),
        (grad_middle, whole((rows, width))),
    ]
    outs = [((rows, width), full, whole((rows, width))), ((8, width), full, whole((8, width)))]
    if joined:
        rounded = ((rows, width), low, whole((rows, width)))
        outs = [rounded, outs[0], rounded, outs[0], outs[1]]
    return weighted(
        body,
        [weight] + ([join_weight] if joined else []),
        (3,),
        ins,
        outs,
        "project_back",
        13 if joined else 9,
        scratch=[pltpu.VMEM((rows, width), full)],
    )


def picked(body, which, grid, ins, outs, name, micros, aliases=None, spare=4):
    return pl.pallas_call(
        body,
        grid_spec=pltpu.PrefetchScalarGridSpec(
            num_scalar_prefetch=1,
            grid=grid,
            in_specs=[spec for _, spec in ins],
            out_specs=[spec for _, _, spec in outs],
        ),
        out_shape=[jax.ShapeDtypeStruct(shape, kind) for shape, kind, _ in outs],
        name=name,
        input_output_aliases={place + 1: out for place, out in (aliases or {}).items()},
        cost_estimate=cost(micros),
        compiler_params=pltpu.CompilerParams(vmem_limit_bytes=room(ins, outs, (), spare)),
    )(which, *[array for array, _ in ins])


def quarters(rows, width, narrow_rows):
    shape = (lax.axis_size("narrow") // 2 * narrow_rows, width)
    return [(shape, low, pl.BlockSpec(shape, lambda g, core: (0, 0)))] * 4


def up_term(left, right, core):
    rows, width = left.shape
    part = width // lax.axis_size("narrow")
    half = width // 2

    def body(core_ref, l_ref, r_ref, *outs):
        value = dot(l_ref[...], r_ref[...], (0, 0)).astype(low)
        for block in range(2):

            @pl.when(pl.program_id(0) == block)
            def _():
                outs[block][...] = value[:half]
                outs[2 + block][...] = value[half:]

    return picked(
        body,
        core,
        (2,),
        [
            (left, pl.BlockSpec((rows, width), lambda g, core: (0, 0))),
            (right, pl.BlockSpec((rows, width), lambda g, core: (0, core[0] * 2 + g))),
        ],
        quarters(rows, width, part),
        "up_term",
        3.5,
    )


def qkv_out_term(first, packed, mixed, branch, core):
    rows, width = first.shape
    part = width // lax.axis_size("narrow")
    half = width // 2

    def body(core_ref, l_ref, r_ref, o_ref, b_ref, *outs):
        step = pl.program_id(0)
        last = core_ref[0] * 2 + step == 3

        def put(block, value):
            outs[block][...] = value[:half]
            outs[2 + block][...] = value[half:]

        @pl.when(last)
        def _():
            put(1, dot(o_ref[...], b_ref[...], (0, 0)).astype(low))

        @pl.when(jnp.logical_not(last))
        def _():
            value = dot(l_ref[...], r_ref[0], (0, 0)).astype(low)
            for block in range(2):

                @pl.when(step == block)
                def _():
                    put(block, value)

    flat = pl.BlockSpec((rows, width), lambda g, core: (0, 0))
    return picked(
        body,
        core,
        (2,),
        [
            (first, flat),
            (packed, pl.BlockSpec((1, rows, width), lambda g, core: (jnp.minimum(core[0] * 2 + g, 2), 0, 0))),
            (mixed, flat),
            (branch, flat),
        ],
        quarters(rows, width, part),
        "qkv_out_term",
        3.5,
    )


def down_term(left, right, core):
    rows, width = right.shape
    shares = lax.axis_size("narrow")
    part = left.shape[1] // (2 * shares)
    direct = part == width
    if not direct:
        left = left.reshape(rows, shares, 2, 2, part // 2)
        left = lax.dynamic_index_in_dim(left, core[0], 2, keepdims=False)
        left = left.reshape(rows, 2, shares // 2, 2, part // 2).swapaxes(2, 3).reshape(rows, 2 * width)
    half = width // 2

    def body(core_ref, l_ref, r_ref, *outs):
        value = dot(l_ref[...], r_ref[...], (0, 0)).astype(low)
        for owner in range(2):

            @pl.when(pl.program_id(0) == owner)
            def _():
                outs[2 * owner][...] = value[:half]
                outs[2 * owner + 1][...] = value[half:]

    return picked(
        body,
        core,
        (2,),
        [
            (left, pl.BlockSpec((rows, width), lambda g, core: (0, g * 2 + core[0] if direct else g))),
            (right, pl.BlockSpec((rows, width), lambda g, core: (0, 0))),
        ],
        quarters(rows, width, part // 2),
        "down_term",
        3.5,
    )


def join_term(middle, skip, right, core):
    rows, width = right.shape
    shares = lax.axis_size("narrow")
    part = width // shares
    half = width // 2
    if part != half:
        left = jnp.concatenate([middle, skip], axis=1).reshape(rows, shares, 2, 2, part // 2)
        left = lax.dynamic_index_in_dim(left, core[0], 2, keepdims=False)
        left = left.reshape(rows, 2, shares // 2, 2, part // 2).swapaxes(2, 3).reshape(rows, width)
        middle, skip = left[:, :half], left[:, half:]

    def body(core_ref, m_ref, s_ref, r_ref, *outs):
        for owner, left_ref in enumerate((m_ref, s_ref)):
            value = dot(left_ref[...], r_ref[...], (0, 0)).astype(low)
            outs[2 * owner][...] = value[: half // 2]
            outs[2 * owner + 1][...] = value[half // 2 :]

    side = pl.BlockSpec((rows, half), lambda g, core: (0, core[0] if part == half else 0))
    return picked(
        body,
        core,
        (1,),
        [(middle, side), (skip, side), (right, pl.BlockSpec((rows, width), lambda g, core: (0, 0)))],
        quarters(rows, width, part // 2),
        "join_term",
        2,
    )


def cross(bit, *pieces):
    kept, got = pieces[: len(pieces) // 2], pieces[len(pieces) // 2 :]
    rows, columns = kept[0].shape
    blocks = len(kept) // 2
    steps = 2 if rows % 32 == 0 else 1

    def body(bit_ref, *refs):
        sent_ref, left_ref = refs[-2:]

        def put(target, owner):
            for block in range(blocks):
                place = owner * blocks + block
                one, two = refs[place], refs[2 * blocks + place]
                target[block] = (one[...].astype(full) + two[...].astype(full)).astype(low)

        for mine in range(2):

            @pl.when(bit_ref[0] == mine)
            def _():
                put(sent_ref, 1 - mine)
                put(left_ref, mine)

    ins = [(piece, pl.BlockSpec((rows // steps, columns), lambda g, bit: (g, 0))) for piece in kept + got]
    out = ((blocks, rows, columns), low, pl.BlockSpec((blocks, rows // steps, columns), lambda g, bit: (0, g, 0)))
    return picked(body, bit, (steps,), ins, [out, out], "cross", 2)


def add_halve(bit, *pairs):
    lead, columns = pairs[0].shape[0], pairs[0].shape[-1]
    sizes = [pair.shape[2] for pair in pairs[::2]]
    total = sum(sizes)
    steps = 2 if len(sizes) == 1 and total % 32 == 0 and total >= 256 else 1

    def body(bit_ref, *refs):
        mine = bit_ref[0]
        for target, place in ((refs[-2], 1 - mine), (refs[-1], mine)):
            begin = 0
            for kept_ref, got_ref in zip(refs[:-2:2], refs[1:-2:2]):
                length = kept_ref.shape[2]
                for each in range(lead):
                    value = kept_ref[each, place].astype(full) + got_ref[each, place].astype(full)
                    target[each, begin : begin + length] = value.astype(low)
                begin += length

    ins = [
        (pair, pl.BlockSpec((lead, 2, pair.shape[2] // steps, columns), lambda g, bit: (0, 0, g, 0)))
        for pair in pairs
    ]
    out = (
        (lead, total, columns),
        low,
        pl.BlockSpec((lead, total // steps, columns), lambda g, bit: (0, g, 0)),
    )
    return picked(body, bit, (steps,), ins, [out, out], "add_halve", 2)


def add_into(target, place, count, one, two):
    rows, columns = one.shape[-2:]
    steps = 2 if rows % 32 == 0 else 1
    block = pl.BlockSpec((1, rows // steps, columns), lambda g: (0, g, 0))

    def body(one_ref, two_ref, *rest):
        rest[-1][...] = (one_ref[...].astype(full) + two_ref[...].astype(full)).astype(low)

    ins = [one.reshape(1, rows, columns), two.reshape(1, rows, columns)]
    return pl.pallas_call(
        body,
        grid=(steps,),
        in_specs=[block, block] + ([] if target is None else [ANY]),
        out_specs=pl.BlockSpec((1, rows // steps, columns), lambda g: (place, g, 0)),
        out_shape=jax.ShapeDtypeStruct((count, rows, columns), low),
        name="add_into",
        input_output_aliases={} if target is None else {2: 0},
        cost_estimate=cost(1.3),
    )(*ins, *([] if target is None else [target]))


def add(one, two):
    return (one.astype(full) + two.astype(full)).astype(low)


def pair_up(own, got, bit):
    rows, columns = own.shape

    def body(bit_ref, own_ref, got_ref, out_ref):
        mine = bit_ref[0]
        out_ref[mine] = own_ref[...]
        out_ref[1 - mine] = got_ref[...]

    flat = pl.BlockSpec((rows, columns), lambda g, bit: (0, 0))
    out = ((2, rows, columns), low, pl.BlockSpec((2, rows, columns), lambda g, bit: (0, 0, 0)))
    return picked(body, bit, (1,), [(own, flat), (got, flat)], [out], "pair_up", 1)[0]


def finish(kind, half, own, got, begin, length, core, layer, targets):
    pieces, _, columns = own.shape
    scale = 1.0 / lax.axis_size("wide")
    aliases = {place + 2: place for place in range(len(targets))}
    source = pl.BlockSpec((pieces, length, columns), lambda g, core: (0, begin // length, 0))
    ins = [(own, source), (got, source)] + [(target, ANY) for target in targets]
    rows = pieces * length

    def chosen(core_ref, which, own_ref, got_ref, place=None):
        sides = [own_ref, got_ref]
        if place is None:
            values = [side[...].reshape(pieces * length, columns) for side in sides]
        else:
            if pieces == 1:
                near = (0, pl.ds(place * (length // 2), length // 2))
            else:
                near = (pl.ds(place * (pieces // 2), pieces // 2),)
            values = [side[near].reshape(pieces * length // 2, columns) for side in sides]
        return jnp.where(core_ref[0] == which, values[0], values[1]).astype(full) * scale

    if kind in ("down", "join"):

        def body(core_ref, own_ref, got_ref, *rest):
            rest[-1][0] = chosen(core_ref, pl.program_id(0), own_ref, got_ref)

        place = layer if kind == "down" else 0
        shape = (2 if kind == "down" else 1, 2 * rows, columns)
        out = (shape, full, pl.BlockSpec((1, rows, columns), lambda g, core: (place, g, 0)))
        return picked(body, core, (2,), ins, [out], "finish_rows", 3, aliases)
    steps = 4 if half is None else 2
    rows = rows // 2 if half is None else rows

    def block(step):
        return step if half is None else 2 * step + half

    def values_of(core_ref, own_ref, got_ref):
        step = pl.program_id(0)
        if half is None:
            return chosen(core_ref, step // 2, own_ref, got_ref, step % 2)
        return chosen(core_ref, step, own_ref, got_ref)

    def body(core_ref, own_ref, got_ref, *rest):
        values = values_of(core_ref, own_ref, got_ref)
        if kind == "up":
            rest[-1][0] = values
            return
        if half == 0:
            rest[-1][0] = values
            return
        last = block(pl.program_id(0)) == 3

        @pl.when(jnp.logical_not(last))
        def _():
            rest[-2][0] = values

        @pl.when(last)
        def _():
            rest[-1][0] = values

    if kind == "up":
        outs = [((2, rows, 4 * columns), full, pl.BlockSpec((1, rows, columns), lambda g, core: (layer, 0, block(g))))]
        return picked(body, core, (steps,), ins, outs, "finish_columns", 3, aliases)

    def spot(step):
        return block(step if half == 0 else jnp.minimum(step, steps - 2))

    outs = [
        ((2, rows, 3 * columns), full, pl.BlockSpec((1, rows, columns), lambda g, core: (layer, 0, spot(g)))),
        ((2, rows, columns), full, pl.BlockSpec((1, rows, columns), lambda g, core: (layer, 0, 0))),
    ]
    if half == 0:
        kept = targets[1:]
        ins, outs, aliases = ins[:3] if targets else ins, outs[:1], {2: 0} if targets else {}
        return (picked(body, core, (steps,), ins, outs, "finish_qkv", 3, aliases)[0], *kept)
    return picked(body, core, (steps,), ins, outs, "finish_qkv_out", 3, aliases)


def small_gradients(total, me, width, shares, blocks):
    part = width // shares
    scale = 1.0 / lax.axis_size("wide")

    def body(me_ref, total_ref, gains_ref, shifts_ref, out_ref, up_ref, down_ref, join_ref):
        values = total_ref[...] * scale
        back = [values[0:8], values[8:16]]
        ahead = [values[16 : 20 + blocks], values[20 + blocks : 24 + 2 * blocks]]
        for place in range(shares):

            @pl.when(me_ref[0] == place)
            def _():
                columns = slice(place * part, place * part + part)
                for layer in range(2):
                    for row, target in ((0, gains_ref), (1, shifts_ref)):
                        target[layer, 0:1] = back[layer][row : row + 1, columns]
                        target[layer, 1:2] = ahead[layer][row + 1 : row + 2, columns]
                    out_ref[layer : layer + 1] = ahead[layer][3:4, columns]
                    down_ref[layer : layer + 1] = ahead[layer][0:1, columns]
                    begin = place * part * blocks
                    while begin < (place + 1) * part * blocks:
                        row, column = begin // width, begin % width
                        length = min(width - column, (place + 1) * part * blocks - begin)
                        at = begin - place * part * blocks
                        piece = ahead[layer][4 + row : 5 + row, column : column + length]
                        up_ref[layer : layer + 1, at : at + length] = piece
                        begin += length
                join_ref[...] = back[1][2:3, columns]

    shapes = [(2, 2, part), (2, 2, part), (2, part), (2, part * blocks), (2, part), (1, part)]
    outs = [(shape, full, pl.BlockSpec(shape, lambda g, me, n=len(shape): (0,) * n)) for shape in shapes]
    ins = [(total, pl.BlockSpec(total.shape, lambda g, me: (0, 0)))]
    return picked(body, me, (1,), ins, outs, "small_gradients", 1)


def after(value, *earlier):
    return lax.optimization_barrier((value,) + earlier)[0] if earlier else value


def swap(values, axis, mask):
    size = lax.axis_size(axis)
    return lax.ppermute(values, axis, [(source, source ^ mask) for source in range(size)])


def masks(axis):
    return [1 << bit for bit in range(lax.axis_size(axis).bit_length() - 1)]


class Order:
    def __init__(self):
        self.last = ()

    def run(self, function, *arrays):
        held = lax.optimization_barrier(tuple(arrays) + self.last)[: len(arrays)]
        out = function(*held)
        self.last = (jax.tree.leaves(out)[0],)
        return out

    def hold(self, *arrays):
        self.last += arrays


def place_bit(axis, mask):
    return ((lax.axis_index(axis) & mask) // mask).astype(jnp.int32).reshape(1)


class Term:
    def __init__(self, order, kind, layer, function, *arrays):
        self.order, self.kind, self.layer, self.half = order, kind, layer, None
        self.core = place_bit("wide", 1)
        sent = order.run(lambda *x: function(*x, 1 - self.core), *arrays)
        self.got = [swap(each, "wide", 1) for each in sent]
        self.columns = sent[0].shape[-1]
        self.keep = lambda: order.run(lambda *x: function(*x, self.core), *arrays)

    def stay(self):
        self.kept, self.keep = self.keep(), None

    def part(self, half):
        other = copy.copy(self)
        other.kept, other.got, other.half = self.kept[half::2], self.got[half::2], half
        return other

    def pass_narrow(self):
        stages = list(reversed(masks("narrow")))
        if isinstance(self.kept, (list, tuple)):
            bit = place_bit("narrow", stages[0])
            blocks = len(self.kept) // 2
            sent, self.kept = self.order.run(lambda *x: cross(bit, *x), *self.kept, *self.got)
            self.got = swap(sent, "narrow", stages.pop(0))
        else:
            blocks = 1
        for mask in stages:
            pairs = [(self.kept, self.got)]
            self.kept, self.got = halve(self.order, "narrow", mask, blocks, pairs, self.columns)

    def pass_first(self, mask):
        swapped = [self.kept[owner * 2 + block] for block in range(2) for owner in range(2)]
        brought = [self.got[owner * 2 + block] for block in range(2) for owner in range(2)]
        bit = place_bit("wide", mask)
        sent, self.kept = self.order.run(lambda *x: cross(bit, *x), *swapped, *brought)
        self.got = swap(sent, "wide", mask)

    def pass_wide(self, mask):
        pairs = list(zip(self.kept, self.got)) if isinstance(self.kept, (list, tuple)) else [(self.kept, self.got)]
        self.kept, self.got = halve(self.order, "wide", mask, 1, pairs, self.columns)

    def add_into(self, target, place, count):
        kept, got = [side.reshape(-1, self.columns) for side in (self.kept, self.got)]
        if target is None:
            return self.order.run(lambda one, two: add_into(None, place, count, one, two), kept, got)
        return self.order.run(lambda target, one, two: add_into(target, place, count, one, two), target, kept, got)

    def finish(self, done, own, got, begin, length):
        targets = done.get(self.kind, ())

        def last(own, got, core, *targets):
            return finish(self.kind, self.half, own, got, begin, length, core, self.layer, targets)

        done[self.kind] = self.order.run(last, own, got, self.core, *targets)


def halve(order, axis, mask, lead, pairs, columns):
    shaped = [array.reshape(lead, 2, -1, columns) for pair in pairs for array in pair]
    bit = place_bit(axis, mask)
    sent, kept = order.run(lambda *x: add_halve(bit, *x), *shaped)
    return kept, swap(sent, axis, mask)


class Reduce:
    def __init__(self, order, terms, passed=(), late=()):
        self.order, self.terms = order, terms
        rest = [mask for mask in masks("wide")[1:] if mask not in passed]
        self.down = [mask for mask in rest if mask not in late] + [mask for mask in rest if mask in late]
        self.up = list(reversed(passed))
        self.pieces, self.columns = 2 ** len(passed), terms[0].columns
        self.parts = [(term.kept, term.got) for term in terms]
        self.lengths, self.first = [each.size // self.columns for each, _ in self.parts], True
        self.joining, self.closed = None, False

    def step(self):
        if self.closed:
            return
        if self.down:
            mask = self.down.pop(0)
            rows = [kept.size // self.columns for kept, _ in self.parts]
            even = all(each % 32 == 0 for each in rows)
            if self.first and even:
                self.pieces, self.lengths = 2 * self.pieces, [each // 2 for each in rows]
            self.first = False
            if even:
                self.up.insert(0, mask)
                self.parts = [halve(self.order, "wide", mask, 1, self.parts, self.columns)]
            else:
                flat = [[side.reshape(-1, self.columns) for side in pair] for pair in self.parts]
                pair = [jnp.concatenate(sides) for sides in zip(*flat)]
                total = self.order.run(add, *pair)
                self.parts = [(total, swap(total, "wide", mask))]
            return
        kept, got = [array.reshape(-1, self.columns) for array in self.parts[0]]
        if self.joining is None:
            total = self.order.run(add, kept, got)
        else:
            bit = place_bit("wide", self.joining)
            total = self.order.run(lambda *x: pair_up(*x, bit), kept, got).reshape(-1, self.columns)
        if self.up:
            self.joining = self.up.pop(0)
            self.parts = [(total, swap(total, "wide", self.joining))]
        else:
            self.parts = [(total, swap(total, "wide", 1))]
            self.closed = True

    def finish(self, done):
        own, got = [array.reshape(self.pieces, -1, self.columns) for array in self.parts[0]]
        begin = 0
        for term, length in zip(self.terms, self.lengths):
            term.finish(done, own, got, begin, length)
            begin += length


def on_device(
    tokens,
    skip,
    flags,
    cotangent,
    norm_gains,
    norm_biases,
    qkv_weight,
    out_weight,
    out_bias,
    up_weight,
    up_bias,
    down_weight,
    down_bias,
    skip_weight,
    skip_bias,
):
    items, seq_rows, width = tokens.shape
    rows = items * seq_rows
    me = lax.axis_index("narrow")
    shares = lax.axis_size("narrow")
    spots = jnp.stack([me, lax.axis_index("wide")]).astype(jnp.int32)
    order = Order()

    def fetches(layer):
        return (
            Fetch([(qkv_weight, layer)], (1, 2)),
            Fetch([(out_weight, layer), (up_weight, layer)], (1, 2)),
            Fetch([(down_weight, layer)], (1, 4)),
        )

    fetch_qkv0, fetch_up0, fetch_down0 = fetches(0)
    fetch_qkv1, fetch_up1, fetch_down1 = fetches(1)
    fetch_join = Fetch([(skip_weight, None)], (1, 4))
    qkv0, qkv1 = [Weight(each, 0, width, spots) for each in (fetch_qkv0, fetch_qkv1)]
    out0, out1 = [Weight(each, 0, width, spots) for each in (fetch_up0, fetch_up1)]
    up0, up1 = [Weight(each, 1, width, spots) for each in (fetch_up0, fetch_up1)]
    down0, down1 = [Weight(each, 0, width, spots) for each in (fetch_down0, fetch_down1)]
    join = Weight(fetch_join, 0, width, spots)

    small = (norm_gains, norm_biases, out_bias, down_bias, skip_bias, up_bias)
    held = order.run(pack_small, *small)[None]
    for mask in masks("narrow"):
        held = jnp.concatenate([held, swap(held, "narrow", mask)])
    fetch_qkv0.fetch(*order.last)
    fetch_up0.fetch(held)
    fetch_down0.fetch(fetch_up0.sent)
    fetch_join.fetch(fetch_down0.sent)
    fetch_qkv1.fetch(fetch_join.sent)
    place = me.astype(jnp.int32).reshape(1)
    lines = order.run(lambda x: unpack_small(x, place, small, width), held)

    def line(row):
        return lines[row : row + 1]

    gains, shifts = [[line(2 * layer + each) for each in range(2)] for layer in range(2)], None
    shifts = [[line(4 + 2 * layer + each) for each in range(2)] for layer in range(2)]
    out_biases, down_biases, join_shift = [line(8), line(9)], [line(10), line(11)], line(12)
    blocks = up0.blocks
    up_biases = [lines[13 + layer * blocks : 13 + (layer + 1) * blocks].reshape(1, -1) for layer in range(2)]

    tokens_flat, skip_flat, cotangent_flat = [array.reshape(rows, width) for array in (tokens, skip, cotangent)]
    lengths = PATCHES + 1 + CAPTION * flags
    valid = lax.broadcasted_iota(jnp.int32, (items, seq_rows), 1) < lengths[:, None]
    keep = valid.reshape(rows, 1).astype(full)
    dz1 = jnp.where(keep > 0, cotangent_flat, 0)

    fetch_qkv0.share(1)
    fetch_qkv0.share(0)
    order.hold(*fetch_up0.got())
    fetch_up0.share(1)
    a0, packed0 = order.run(lambda *x: project_qkv(*x, qkv0), tokens_flat, gains[0][0], shifts[0][0])
    order.hold(*fetch_down0.got())
    fetch_down0.share(1, a0)
    fetch_up1.fetch(a0)
    fetch_down1.fetch(fetch_up1.sent)
    packed0 = packed0.reshape(3, items, seq_rows, width)
    mixed0, totals0 = order.run(lambda *x: attend(*x, items, seq_rows), packed0, lengths)
    fetch_up0.share(0, mixed0)
    fetch_down0.share(0, mixed0)
    order.hold(*fetch_join.got(), *fetch_qkv1.got())
    fetch_join.share(1, mixed0)
    fetch_qkv1.share(1, mixed0)
    mixed0 = mixed0.reshape(rows, width)
    m0, second0, hidden0, slope0, middle = order.run(
        lambda x, o, ob, g, s, ub, db: feed_forward(x, o, out0, ob, g, s, up0, ub, down0, db),
        tokens_flat, mixed0, out_biases[0], gains[0][1], shifts[0][1], up_biases[0], down_biases[0],
    )
    fetch_join.share(0, middle)
    fetch_qkv1.share(0, middle)
    order.hold(*fetch_up1.got(), *fetch_down1.got())
    fetch_up1.share(1, middle)
    fetch_down1.share(1, middle)
    entry, a1, packed1 = order.run(
        lambda m, s, jb, g, sh: join_qkv(m, s, join, jb, g, sh, qkv1),
        middle, skip_flat, join_shift, gains[1][0], shifts[1][0],
    )
    packed1 = packed1.reshape(3, items, seq_rows, width)
    mixed1, totals1 = order.run(lambda *x: attend(*x, items, seq_rows), packed1, lengths)
    fetch_up1.share(0, mixed1)
    fetch_down1.share(0, mixed1)
    mixed1 = mixed1.reshape(rows, width)
    m1, second1, hidden1, slope1, output = order.run(
        lambda x, o, ob, g, s, ub, db, k: feed_forward(x, o, out1, ob, g, s, up1, ub, down1, db, k),
        entry, mixed1, out_biases[1], gains[1][1], shifts[1][1], up_biases[1], down_biases[1], keep,
    )

    done = {}
    term_down1 = Term(order, "down", 1, down_term, hidden1, dz1)
    term_down1.stay()
    term_down1.pass_narrow()
    du, dm, db, do, sums1 = order.run(
        lambda y, z, s, m, g: feed_forward_back(y, z, s, down1, up1, m, g, out1),
        dz1, dz1, slope1, m1, gains[1][1],
    )
    term_up1 = Term(order, "up", 1, up_term, second1, du)
    term_up1.stay()
    term_up1.pass_narrow()
    total = term_down1.add_into(None, 0, 3)
    dpacked = order.run(
        lambda *x: attend_back(*x, items, seq_rows), packed1, do.reshape(items, seq_rows, width), totals1, lengths
    )
    flat_packed = dpacked.reshape(3, rows, width)
    term_qkv1 = Term(order, "qkv", 1, qkv_out_term, a1, flat_packed, mixed1, db)
    term_qkv1.stay()
    term_qkv1.pass_narrow()
    total = term_up1.add_into(total, 1, 3)
    dentry, dmiddle, dz0, skip_grad, sums3 = order.run(
        lambda gp, x, g, dm: project_back(gp, qkv1, x, g, dm, join), flat_packed, entry, gains[1][0], dm
    )
    term_join = Term(order, "join", 1, join_term, middle, skip_flat, dentry)
    term_join.stay()
    term_join.pass_narrow()
    term_down0 = Term(order, "down", 0, down_term, hidden0, dz0)
    term_down0.stay()
    total = term_qkv1.add_into(total, 2, 3)
    size = lax.axis_size("wide")
    groups = [[device + core for device in range(0, size, 2)] for core in range(2)]
    flat_total = total.reshape(-1, width)
    part = lax.psum_scatter(flat_total, "wide", axis_index_groups=groups, scatter_dimension=0, tiled=True)
    term_down0.pass_first(2)

    du, dm, db, do, sums0 = order.run(
        lambda y, z, s, m, g: feed_forward_back(y, z, s, down0, up0, m, g, out0),
        dmiddle, dz0, slope0, m0, gains[0][1],
    )
    term_join.pass_wide(2)
    term_up0 = Term(order, "up", 0, up_term, second0, du)
    term_up0.stay()
    term_down0.pass_narrow()
    term_up0.pass_narrow()
    dpacked = order.run(
        lambda *x: attend_back(*x, items, seq_rows), packed0, do.reshape(items, seq_rows, width), totals0, lengths
    )
    order.hold(term_down0.got, term_join.got)
    flat_packed = dpacked.reshape(3, rows, width)
    term_qkv0 = Term(order, "qkv", 0, qkv_out_term, a0, flat_packed, mixed0, db)
    term_qkv0.stay()
    one, two = term_qkv0.part(0), term_qkv0.part(1)
    one.pass_narrow()
    two.pass_narrow()
    order.hold(term_up0.got, part)
    first = Reduce(order, [term_down0, term_join], (2,))
    first.step()
    gathered = lax.all_gather(after(part, *order.last), "wide", axis_index_groups=groups, tiled=True)
    second = Reduce(order, [term_up0])
    second.step()
    tokens_grad, sums2 = order.run(
        lambda gp, x, g, dm: project_back(gp, qkv0, x, g, dm), flat_packed, tokens_flat, gains[0][0], dm
    )
    minor = jnp.concatenate([sums2, sums3, sums0, sums1])
    places = masks("wide")
    minor_stages = [("narrow", mask) for mask in masks("narrow")]
    minor_stages += [("wide", mask) for mask in places if mask != 2] + [("wide", mask) for mask in places if mask == 2]
    minor_got = swap(minor, *minor_stages[0])

    def minor_step():
        nonlocal minor, minor_got
        if minor_stages:
            minor_stages.pop(0)
            minor = order.run(lambda one, two: one + two, minor, minor_got)
            if minor_stages:
                minor_got = swap(minor, *minor_stages[0])

    first.step()
    third = Reduce(order, [one])
    third.step()
    second.step()
    fourth = Reduce(order, [two], late=(2,))
    fourth.step()
    first.step()
    third.step()
    minor_step()
    second.step()
    fourth.step()
    minor_step()
    fourth.step()
    first.step()
    third.step()
    minor_step()
    second.step()
    fourth.step()
    order.hold(gathered)
    other = swap(after(gathered, *order.last), "wide", 1)
    first.step()
    third.step()
    own, got = gathered.reshape(1, -1, width), other.reshape(1, -1, width)
    for which, term in enumerate((term_down1, term_up1, term_qkv1)):
        term.finish(done, own, got, which * (own.shape[1] // 3), own.shape[1] // 3)
    second.step()
    fourth.step()
    third.step()
    minor_step()
    first.step()
    fourth.step()
    second.step()
    third.step()
    first.finish(done)
    fourth.step()
    second.step()
    third.step()
    for each in (first, second, third, fourth):
        while not each.closed:
            each.step()
    while minor_stages:
        minor_step()
    fourth.finish(done)
    second.finish(done)
    third.finish(done)
    small = order.run(lambda x: small_gradients(x, place, width, shares, up1.blocks), minor)

    return (
        output.reshape(tokens.shape),
        tokens_grad.reshape(tokens.shape),
        skip_grad.reshape(tokens.shape),
        small[0],
        small[1],
        done["qkv"][0],
        done["qkv"][1],
        small[2],
        done["up"][0],
        small[3],
        done["down"][0],
        small[4],
        done["join"][0][0],
        small[5].reshape(-1),
    )


def solution(mesh):
    placed = (
        P(("wide", "narrow"), None, None),
        P(("wide", "narrow"), None, None),
        P(("wide", "narrow")),
        P(("wide", "narrow"), None, None),
        P(None, None, "narrow"),
        P(None, None, "narrow"),
        P(None, "narrow", None),
        P(None, "narrow", None),
        P(None, "narrow"),
        P(None, "narrow", None),
        P(None, "narrow"),
        P(None, "narrow", None),
        P(None, "narrow"),
        P("narrow", None),
        P("narrow"),
    )
    return jax.shard_map(
        on_device,
        mesh=mesh,
        in_specs=placed,
        out_specs=(
            P(("wide", "narrow"), None, None),
            P(("wide", "narrow"), None, None),
            P(("wide", "narrow"), None, None),
            P(None, None, "narrow"),
            P(None, None, "narrow"),
            P(None, "narrow", None),
            P(None, "narrow", None),
            P(None, "narrow"),
            P(None, "narrow", None),
            P(None, "narrow"),
            P(None, "narrow", None),
            P(None, "narrow"),
            P("narrow", None),
            P("narrow"),
        ),
        check_vma=False,
    )
```

```python
import copy
import math

import jax
import jax.numpy as jnp
from jax import lax
from jax.experimental import pallas as pl
from jax.experimental.pallas import tpu as pltpu
from jax.sharding import PartitionSpec as P

HEAD_DIM = 64
PATCHES = 256
CAPTION = 77
PAIR = 2 * HEAD_DIM


epsilon = 1e-05
masked_score = -1e30
low = jnp.bfloat16
full = jnp.float32
SPARE = 14
ANY = pl.BlockSpec(memory_space=pltpu.HBM)
SCALARS = pl.BlockSpec(memory_space=pltpu.SMEM)


def dot(left, right, contract=(1, 0)):
    dims = (((contract[0],), (contract[1],)), ((), ()))
    return lax.dot_general(left, right, dims, preferred_element_type=full)


def normalize(values):
    centred = values - jnp.mean(values, axis=-1, keepdims=True)
    factor = lax.rsqrt(jnp.mean(centred * centred, axis=-1, keepdims=True) + epsilon)
    return centred * factor, factor


def normalize_back(upstream, normed, factor):
    return factor * (
        upstream
        - jnp.mean(upstream, axis=-1, keepdims=True)
        - normed * jnp.mean(upstream * normed, axis=-1, keepdims=True)
    )


def column_sum(values):
    return jnp.sum(values.astype(full), axis=0, keepdims=True)


def whole(shape):
    return pl.BlockSpec(shape, lambda *grid: (0,) * len(shape))


def cost(micros):
    return pl.CostEstimate(flops=int(micros * 3 * 10**8), bytes_accessed=0, transcendentals=0)


def room(ins, outs, scratch, spare):
    total = spare * 2**20
    for shape, kind, spec in [(array.shape, array.dtype, spec) for array, spec in ins] + list(outs):
        if spec.block_shape is not None and spec.memory_space is None:
            total += 2 * math.prod(spec.block_shape) * jnp.dtype(kind).itemsize
    for piece in scratch:
        if piece.memory_space == pltpu.VMEM:
            total += math.prod(piece.shape) * jnp.dtype(piece.dtype).itemsize
    return total


def call(body, grid, ins, outs, name, micros, scratch=(), spare=6):
    return pl.pallas_call(
        body,
        grid=grid,
        in_specs=[spec for _, spec in ins],
        out_specs=[spec for _, _, spec in outs],
        out_shape=[jax.ShapeDtypeStruct(shape, kind) for shape, kind, _ in outs],
        scratch_shapes=list(scratch),
        name=name,
        cost_estimate=cost(micros),
        compiler_params=pltpu.CompilerParams(vmem_limit_bytes=room(ins, outs, scratch, spare)),
    )(*[array for array, _ in ins])


class Fetch:
    def __init__(self, arrays, sharing):
        self.arrays, self.sharing = arrays, list(sharing)
        self.rows = arrays[0][0].shape[-2]
        while self.rows % (16 << len(self.sharing)):
            self.sharing.pop()
        self.length = self.rows >> len(self.sharing)

    def quarter(self, place):
        return sum(((place // mask) & 1) << bit for bit, mask in enumerate(self.sharing))

    def fetch(self, *earlier):
        found = []
        for array, layer in self.arrays:
            array = after(array, *earlier)
            lead = () if layer is None else (layer,)
            begin = self.quarter(lax.axis_index("wide")) * self.length
            sizes = (1,) * len(lead) + (self.length, array.shape[-1])
            found.append(lax.dynamic_slice(array, lead + (begin, 0), sizes).reshape(self.length, -1))
        self.sent = (jnp.concatenate(found, axis=1) if len(found) > 1 else found[0])[None]
        held = self.sent
        for mask in masks("narrow"):
            held = jnp.concatenate([held, swap(held, "narrow", mask)])
        self.pieces = {0: held[1:]}

    def share(self, which, *earlier):
        if which < len(self.sharing):
            mask = self.sharing[which]
            got = {key ^ (1 << which): swap(after(piece, *earlier), "wide", mask) for key, piece in self.pieces.items()}
            self.pieces.update(got)

    def got(self):
        return list(self.pieces.values())


class Weight:
    def __init__(self, fetched, which, width, spots):
        self.fetched, self.spots, self.width = fetched, spots, width
        self.array, self.layer = fetched.arrays[which]
        self.begin = sum(array.shape[-1] for array, _ in fetched.arrays[:which])
        self.rows, columns = self.array.shape[-2:]
        self.shares = lax.axis_size("narrow")
        self.blocks = columns // width
        self.total = self.rows * self.shares

    def arrays(self):
        return [self.array] + self.fetched.got()

    def scratch(self):
        copies = 1 + len(self.fetched.pieces) * (self.shares - 1)
        return [pltpu.VMEM((self.blocks, self.total, self.width), low), pltpu.SemaphoreType.DMA((self.blocks, copies))]

    def copies(self, spots, refs, held, signals, block):
        own, pieces = refs[0], refs[1:]
        me, length = spots[0], self.fetched.length
        own = own if self.layer is None else own.at[self.layer]
        columns = pl.ds(block * self.width, self.width)
        begin = pl.multiple_of(me * self.rows, 16)
        found = [(own.at[:, columns], begin, self.rows)]
        columns = pl.ds(self.begin + block * self.width, self.width)
        for key, piece in zip(self.fetched.pieces, pieces):
            for offset in range(1, self.shares):
                begin = (me ^ offset) * self.rows + (self.fetched.quarter(spots[1]) ^ key) * length
                found.append((piece.at[offset - 1, :, columns], pl.multiple_of(begin, 16), length))
        return [
            pltpu.make_async_copy(source, held.at[block, pl.ds(begin, length)], signals.at[block, place])
            for place, (source, begin, length) in enumerate(found)
        ]

    def wait(self, *refs, block=0):
        for copy in self.copies(*refs, block):
            copy.wait()


def weighted(body, weights, grid, ins, outs, name, micros, scratch=(), first=((0, 0),), spare=SPARE):
    spots = weights[0].spots
    operands = [(spots, SCALARS)] + [(array, ANY) for weight in weights for array in weight.arrays()]
    counts = [len(weight.arrays()) for weight in weights]
    extra = [piece for weight in weights for piece in weight.scratch()]

    def wrapped(*refs):
        spots_ref, rest = refs[0], list(refs[1:])
        sources = []
        for count in counts:
            sources.append(rest[:count])
            rest = rest[count:]
        spare = rest[len(rest) - len(extra) :]
        rest = rest[: len(rest) - len(extra)]
        handles = []
        for place, weight in enumerate(weights):
            held, signals = spare[2 * place : 2 * place + 2]
            refs_of = (spots_ref, sources[place], held, signals)
            handles.append((weight, refs_of, held))

        everything = [(place, block) for place, weight in enumerate(weights) for block in range(weight.blocks)]

        def begin(wanted):
            for place, block in wanted:
                weight, refs_of, _ = handles[place]
                for copy in weight.copies(*refs_of, block):
                    copy.start()

        @pl.when(pl.program_id(0) == 0)
        def _():
            begin(first)

        def ready(place, block=0, then=False):
            weight, refs_of, held = handles[place]
            weight.wait(*refs_of, block=block)
            if then:
                begin([each for each in everything if each not in first])

        body(ready, [held for _, _, held in handles], *rest)

    return call(wrapped, grid, operands + ins, outs, name, micros, list(scratch) + extra, spare)


def pack_small(*small):
    part = small[0].shape[-1]
    counts = [piece.size // part for piece in small]

    def body(*refs):
        row = 0
        for ref in refs[:-1]:
            values = ref[...].reshape(-1, ref.shape[-1])
            for each in range(values.shape[0]):
                for begin in range(0, values.shape[1], part):
                    refs[-1][row : row + 1] = values[each : each + 1, begin : begin + part].astype(full)
                    row += 1
        refs[-1][row:] = jnp.zeros((refs[-1].shape[0] - row, part), full)

    flat = [piece.reshape((1,) * (2 - piece.ndim) + piece.shape) for piece in small]
    rows = -(-sum(counts) // 16) * 16
    out = ((rows, part), full, whole((rows, part)))
    return call(body, (1,), [(piece, whole(piece.shape)) for piece in flat], [out], "pack_small", 1)[0].astype(low)


def unpack_small(parts, me, small, width):
    shares, _, part = parts.shape
    lines = [(piece.size // piece.shape[-1], piece.shape[-1] // part) for piece in small]
    total = sum(count * many for count, many in lines)
    rows = -(-total // 8) * 8

    def body(me_ref, parts_ref, out_ref):
        values = parts_ref[...].astype(full)
        for mine in range(shares):

            @pl.when(me_ref[0] == mine)
            def _():
                for owner in range(shares):
                    source, target = 0, 0
                    for count, many in lines:
                        for each in range(count):
                            for piece in range(many):
                                at = owner * many * part + piece * part
                                row, column = target + at // width, at % width
                                line = values[owner ^ mine, source : source + 1]
                                out_ref[row : row + 1, column : column + part] = line
                                source += 1
                            target += many
        if rows > total:
            out_ref[total:] = jnp.zeros((rows - total, width), full)

    ins = [(parts, pl.BlockSpec(parts.shape, lambda g, me: (0, 0, 0)))]
    out = ((rows, width), full, pl.BlockSpec((rows, width), lambda g, me: (0, 0)))
    return picked(body, me, (1,), ins, [out], "unpack_small", 1)[0]


def project_qkv(inputs, gain, shift, weight):
    rows, width = inputs.shape

    def body(ready, held, x_ref, gain_ref, shift_ref, a_ref, out_ref):
        step = pl.program_id(0)

        @pl.when(step == 0)
        def _():
            normed, _ = normalize(x_ref[...].astype(full))
            a_ref[...] = (normed * gain_ref[...] + shift_ref[...]).astype(low)
            ready(0, 0, then=True)

        @pl.when(step > 0)
        def _():
            ready(0, step)

        scale = jnp.where(step == 0, HEAD_DIM ** (-0.5), 1.0)
        out_ref[0] = (dot(a_ref[...], held[0][step]).astype(low).astype(full) * scale).astype(low)

    return weighted(
        body,
        [weight],
        (3,),
        [
            (inputs, whole((rows, width))),
            (gain, whole((1, width))),
            (shift, whole((1, width))),
        ],
        [
            ((rows, width), low, whole((rows, width))),
            ((3, rows, width), low, pl.BlockSpec((1, rows, width), lambda j: (j, 0, 0))),
        ],
        "project_qkv",
        7,
    )


def join_qkv(middle, skip, join_weight, join_shift, gain, shift, weight):
    rows, width = middle.shape

    def body(ready, held, m_ref, s_ref, jb_ref, gain_ref, shift_ref, e_ref, a_ref, out_ref):
        step = pl.program_id(0)

        @pl.when(step == 0)
        def _():
            ready(0, then=True)
            entry = dot(m_ref[...], held[0][0, :width]) + dot(s_ref[...], held[0][0, width:]) + jb_ref[...]
            e_ref[...] = entry
            normed, _ = normalize(entry)
            a_ref[...] = (normed * gain_ref[...] + shift_ref[...]).astype(low)

        ready(1, step)
        scale = jnp.where(step == 0, HEAD_DIM ** (-0.5), 1.0)
        out_ref[0] = (dot(a_ref[...], held[1][step]).astype(low).astype(full) * scale).astype(low)

    return weighted(
        body,
        [join_weight, weight],
        (3,),
        [
            (middle, whole((rows, width))),
            (skip, whole((rows, width))),
            (join_shift, whole((1, width))),
            (gain, whole((1, width))),
            (shift, whole((1, width))),
        ],
        [
            ((rows, width), full, whole((rows, width))),
            ((rows, width), low, whole((rows, width))),
            ((3, rows, width), low, pl.BlockSpec((1, rows, width), lambda j: (j, 0, 0))),
        ],
        "join_qkv",
        11,
        first=((0, 0), (1, 0)),
    )


def head_masks(seq_rows):
    lane = lax.broadcasted_iota(jnp.int32, (seq_rows, PAIR), 1)
    return [lane < HEAD_DIM, lane >= HEAD_DIM]


def pairs_of(width):
    pairs = width // PAIR
    return pairs, max(group for group in (1, 2, 3) if pairs % group == 0)


def attend(packed, lengths, items, seq_rows):
    width = packed.shape[-1]
    pairs, group = pairs_of(width)

    def body(length_ref, q_ref, k_ref, v_ref, out_ref, total_ref):
        counts = lax.broadcasted_iota(jnp.int32, (seq_rows, seq_rows), 1) < length_ref[pl.program_id(0)]
        for pair in range(group):
            columns = slice(pair * PAIR, (pair + 1) * PAIR)
            queries, keys, values = q_ref[0, 0, :, columns], k_ref[0, 0, :, columns], v_ref[0, 0, :, columns]
            mixed = jnp.zeros((seq_rows, PAIR), full)
            for head, lanes in enumerate(head_masks(seq_rows)):
                scores = dot(jnp.where(lanes, queries, 0), keys, (1, 1))
                scores = jnp.where(counts, scores, masked_score)
                largest = jnp.max(scores, axis=1, keepdims=True)
                weights = jnp.exp(scores - largest)
                total = jnp.sum(weights, axis=1, keepdims=True)
                mixed += dot(weights.astype(low), jnp.where(lanes, values, 0)) * (1.0 / total)
                total_ref[0, pair, head : head + 1] = (largest + jnp.log(total)).T
            out_ref[0, :, columns] = mixed.astype(low)

    def block(which):
        return pl.BlockSpec((1, 1, seq_rows, group * PAIR), lambda n, h: (which, n, 0, h))

    return call(
        body,
        (items, pairs // group),
        [(lengths, SCALARS), (packed, block(0)), (packed, block(1)), (packed, block(2))],
        [
            (
                (items, seq_rows, width),
                low,
                pl.BlockSpec((1, seq_rows, group * PAIR), lambda n, h: (n, 0, h)),
            ),
            (
                (items, pairs, 8, seq_rows),
                full,
                pl.BlockSpec((1, group, 8, seq_rows), lambda n, h: (n, h, 0, 0)),
            ),
        ],
        "attend",
        10,
        spare=14,
    )


def attend_back(packed, grad_mixed, totals, lengths, items, seq_rows):
    width = packed.shape[-1]
    pairs, group = pairs_of(width)
    sides = [slice(0, PATCHES), slice(PATCHES, seq_rows)]

    def body(length_ref, q_ref, k_ref, v_ref, g_ref, total_ref, out_ref):
        row = PATCHES + lax.broadcasted_iota(jnp.int32, (seq_rows - PATCHES, seq_rows), 0)
        counts = row < length_ref[pl.program_id(0)]
        for pair in range(group):
            columns = slice(pair * PAIR, (pair + 1) * PAIR)
            queries, keys, values = q_ref[0, 0, :, columns], k_ref[0, 0, :, columns], v_ref[0, 0, :, columns]
            upstream = g_ref[0, :, columns]
            grad_queries = jnp.zeros((PAIR, seq_rows), full)
            grad_keys, grad_values = [0.0, 0.0], [0.0, 0.0]
            for head, lanes in enumerate(head_masks(seq_rows)):
                own_queries = jnp.where(lanes, queries, 0)
                own_upstream = jnp.where(lanes, upstream, 0)
                own_keys = jnp.where(lanes, keys, 0)
                parts, centre = [], 0.0
                for side, rows in enumerate(sides):
                    scores = dot(keys[rows], own_queries, (1, 1))
                    if side:
                        scores = jnp.where(counts, scores, masked_score)
                    probs = jnp.exp(scores - total_ref[0, pair, head : head + 1])
                    grad_probs = dot(values[rows], own_upstream, (1, 1))
                    centre += jnp.sum(grad_probs * probs, axis=0, keepdims=True)
                    parts.append((probs, grad_probs))
                for side, (probs, grad_probs) in enumerate(parts):
                    grad_scores = (probs * (grad_probs - centre)).astype(low)
                    grad_values[side] += dot(probs.astype(low), own_upstream)
                    grad_keys[side] += dot(grad_scores, own_queries)
                    grad_queries += dot(own_keys[sides[side]], grad_scores, (0, 0))
            out_ref[0, 0, :, columns] = (grad_queries.T * HEAD_DIM ** (-0.5)).astype(low)
            for side, rows in enumerate(sides):
                out_ref[1, 0, rows, columns] = grad_keys[side].astype(low)
                out_ref[2, 0, rows, columns] = grad_values[side].astype(low)

    def block(which):
        return pl.BlockSpec((1, 1, seq_rows, group * PAIR), lambda n, h: (which, n, 0, h))

    return call(
        body,
        (items, pairs // group),
        [
            (lengths, SCALARS),
            (packed, block(0)),
            (packed, block(1)),
            (packed, block(2)),
            (grad_mixed, pl.BlockSpec((1, seq_rows, group * PAIR), lambda n, h: (n, 0, h))),
            (totals, pl.BlockSpec((1, group, 8, seq_rows), lambda n, h: (n, h, 0, 0))),
        ],
        [
            (
                (3, items, seq_rows, width),
                low,
                pl.BlockSpec((3, 1, seq_rows, group * PAIR), lambda n, h: (0, n, 0, h)),
            ),
        ],
        "attend_back",
        15,
        spare=14,
    )[0]


def gelu_parts(before):
    decay = jnp.exp(before * before * -0.5)
    inverse = pl.reciprocal(1.0 + (0.3275911 * 0.5**0.5) * jnp.abs(before), approx=False)
    series = 1.061405429 * 0.5
    for term in (-1.453152027, 1.421413741, -0.284496736, 0.254829592):
        series = series * inverse + term * 0.5
    below = series * inverse * decay
    share = jnp.where(before >= 0, 1.0 - below, below)
    return before * share, share + before * decay * 0.3989422804014327


def feed_forward(inputs, mixed, out_weight, out_bias, gain, shift, up_weight, up_bias, down_weight, down_bias, keep=None):
    rows, width = inputs.shape
    steps = up_weight.blocks
    hidden = steps * width

    def body(ready, held, x_ref, o_ref, ob_ref, gain_ref, shift_ref, ub_ref, db_ref, *rest):
        m_ref, a_ref, g_ref, s_ref, y_ref, total = rest[-6:]
        step = pl.program_id(0)

        @pl.when(step == 0)
        def _():
            ready(0, then=True)
            middle = x_ref[...].astype(full) + dot(o_ref[...], held[0][0]) + ob_ref[...]
            m_ref[...] = middle
            normed, _ = normalize(middle)
            a_ref[...] = (normed * gain_ref[...] + shift_ref[...]).astype(low)
            total[...] = middle + db_ref[...]

        ready(1, step)
        before = dot(a_ref[...], held[1][step]) + ub_ref[...]
        value, slope = gelu_parts(before)
        g_ref[...] = value.astype(low)
        s_ref[...] = slope.astype(low)

        @pl.when(step == 0)
        def _():
            ready(2)

        total[...] += dot(g_ref[...], held[2][0, pl.ds(pl.multiple_of(step * width, width), width)])

        @pl.when(step == steps - 1)
        def _():
            value = total[...]
            if keep is not None:
                value = jnp.where(rest[0][...] > 0, value, 0.0)
            y_ref[...] = value.astype(low)

    return weighted(
        body,
        [out_weight, up_weight, down_weight],
        (steps,),
        [
            (inputs, whole((rows, width))),
            (mixed, whole((rows, width))),
            (out_bias, whole((1, width))),
            (gain, whole((1, width))),
            (shift, whole((1, width))),
            (up_bias, pl.BlockSpec((1, width), lambda j: (0, j))),
            (down_bias, whole((1, width))),
        ]
        + ([] if keep is None else [(keep, whole((rows, 1)))]),
        [
            ((rows, width), full, whole((rows, width))),
            ((rows, width), low, whole((rows, width))),
            ((rows, hidden), low, pl.BlockSpec((rows, width), lambda j: (0, j))),
            ((rows, hidden), low, pl.BlockSpec((rows, width), lambda j: (0, j))),
            ((rows, width), low, whole((rows, width))),
        ],
        "feed_forward",
        23,
        scratch=[pltpu.VMEM((rows, width), full)],
        first=((0, 0), (1, 0)),
    )


def feed_forward_back(upstream, rounded, slope, down_weight, up_weight, middle, gain, out_weight):
    rows, width = upstream.shape
    steps = up_weight.blocks
    hidden = steps * width

    def body(ready, held, y_ref, dz_ref, s_ref, m_ref, gain_ref, du_ref, dm_ref, db_ref, do_ref, sums_ref, total):
        step = pl.program_id(0)

        @pl.when(step == 0)
        def _():
            sums_ref[0:1] = column_sum(dz_ref[...])
            total[...] = jnp.zeros_like(total)
            ready(0, then=True)

        down = held[0][0, pl.ds(pl.multiple_of(step * width, width), width)]
        grad = (dot(dz_ref[...], down, (1, 1)) * s_ref[...].astype(full)).astype(low)
        du_ref[...] = grad
        sums_ref[pl.ds(4 + step, 1)] = column_sum(grad)
        ready(1, step)
        total[...] += dot(grad, held[1][step], (1, 1))

        @pl.when(step == steps - 1)
        def _():
            grad_second = total[...]
            normed, factor = normalize(m_ref[...])
            sums_ref[1:2] = column_sum(grad_second * normed)
            sums_ref[2:3] = column_sum(grad_second)
            grad_middle = y_ref[...].astype(full) + normalize_back(grad_second * gain_ref[...], normed, factor)
            dm_ref[...] = grad_middle
            branch = grad_middle.astype(low)
            db_ref[...] = branch
            sums_ref[3:4] = column_sum(branch)
            ready(2)
            do_ref[...] = dot(branch, held[2][0], (1, 1)).astype(low)

    return weighted(
        body,
        [down_weight, up_weight, out_weight],
        (steps,),
        [
            (upstream, whole((rows, width))),
            (rounded, whole((rows, width))),
            (slope, pl.BlockSpec((rows, width), lambda j: (0, j))),
            (middle, whole((rows, width))),
            (gain, whole((1, width))),
        ],
        [
            ((rows, hidden), low, pl.BlockSpec((rows, width), lambda j: (0, j))),
            ((rows, width), full, whole((rows, width))),
            ((rows, width), low, whole((rows, width))),
            ((rows, width), low, whole((rows, width))),
            ((4 + steps, width), full, whole((4 + steps, width))),
        ],
        "feed_forward_back",
        21,
        scratch=[pltpu.VMEM((rows, width), full)],
        first=((0, 0), (1, 0)),
    )


def project_back(grad_packed, weight, inputs, gain, grad_middle, join_weight=None):
    rows, width = inputs.shape
    joined = join_weight is not None

    def body(ready, held, g_ref, x_ref, gain_ref, dm_ref, *rest):
        if joined:
            de_ref, dx_ref, dz_ref, skip_ref, sums_ref, total = rest
        else:
            dx_ref, sums_ref, total = rest
        step = pl.program_id(0)

        @pl.when(step == 0)
        def _():
            total[...] = jnp.zeros_like(total)
            ready(0, 0, then=True)

        @pl.when(step > 0)
        def _():
            ready(0, step)

        total[...] += dot(g_ref[0], held[0][step], (1, 1))

        @pl.when(step == 2)
        def _():
            grad_first = total[...]
            normed, factor = normalize(x_ref[...].astype(full))
            sums_ref[0:1] = column_sum(grad_first * normed)
            sums_ref[1:2] = column_sum(grad_first)
            grad = dm_ref[...] + normalize_back(grad_first * gain_ref[...], normed, factor)
            if joined:
                entry = grad.astype(low)
                de_ref[...] = entry
                sums_ref[2:3] = column_sum(entry)
                ready(1)
                grad = dot(entry, held[1][0, :width], (1, 1))
                dx_ref[...] = grad
                dz_ref[...] = grad.astype(low)
                skip_ref[...] = dot(entry, held[1][0, width:], (1, 1))
            else:
                dx_ref[...] = grad

    ins = [
        (grad_packed, pl.BlockSpec((1, rows, width), lambda j: (j, 0, 0))),
        (inputs, whole((rows, width))),
        (gain, whole((1, width))),
        (grad_middle, whole((rows, width))),
    ]
    outs = [((rows, width), full, whole((rows, width))), ((8, width), full, whole((8, width)))]
    if joined:
        rounded = ((rows, width), low, whole((rows, width)))
        outs = [rounded, outs[0], rounded, outs[0], outs[1]]
    return weighted(
        body,
        [weight] + ([join_weight] if joined else []),
        (3,),
        ins,
        outs,
        "project_back",
        13 if joined else 9,
        scratch=[pltpu.VMEM((rows, width), full)],
    )


def picked(body, which, grid, ins, outs, name, micros, aliases=None, spare=4):
    return pl.pallas_call(
        body,
        grid_spec=pltpu.PrefetchScalarGridSpec(
            num_scalar_prefetch=1,
            grid=grid,
            in_specs=[spec for _, spec in ins],
            out_specs=[spec for _, _, spec in outs],
        ),
        out_shape=[jax.ShapeDtypeStruct(shape, kind) for shape, kind, _ in outs],
        name=name,
        input_output_aliases={place + 1: out for place, out in (aliases or {}).items()},
        cost_estimate=cost(micros),
        compiler_params=pltpu.CompilerParams(vmem_limit_bytes=room(ins, outs, (), spare)),
    )(which, *[array for array, _ in ins])


def quarters(rows, width, narrow_rows):
    shape = (lax.axis_size("narrow") // 2 * narrow_rows, width)
    return [(shape, low, pl.BlockSpec(shape, lambda g, core: (0, 0)))] * 4


def up_term(left, right, core):
    rows, width = left.shape
    part = width // lax.axis_size("narrow")
    half = width // 2

    def body(core_ref, l_ref, r_ref, *outs):
        value = dot(l_ref[...], r_ref[...], (0, 0)).astype(low)
        for block in range(2):

            @pl.when(pl.program_id(0) == block)
            def _():
                outs[block][...] = value[:half]
                outs[2 + block][...] = value[half:]

    return picked(
        body,
        core,
        (2,),
        [
            (left, pl.BlockSpec((rows, width), lambda g, core: (0, 0))),
            (right, pl.BlockSpec((rows, width), lambda g, core: (0, core[0] * 2 + g))),
        ],
        quarters(rows, width, part),
        "up_term",
        3.5,
    )


def qkv_out_term(first, packed, mixed, branch, core):
    rows, width = first.shape
    part = width // lax.axis_size("narrow")
    half = width // 2

    def body(core_ref, l_ref, r_ref, o_ref, b_ref, *outs):
        step = pl.program_id(0)
        last = core_ref[0] * 2 + step == 3

        def put(block, value):
            outs[block][...] = value[:half]
            outs[2 + block][...] = value[half:]

        @pl.when(last)
        def _():
            put(1, dot(o_ref[...], b_ref[...], (0, 0)).astype(low))

        @pl.when(jnp.logical_not(last))
        def _():
            value = dot(l_ref[...], r_ref[0], (0, 0)).astype(low)
            for block in range(2):

                @pl.when(step == block)
                def _():
                    put(block, value)

    flat = pl.BlockSpec((rows, width), lambda g, core: (0, 0))
    return picked(
        body,
        core,
        (2,),
        [
            (first, flat),
            (packed, pl.BlockSpec((1, rows, width), lambda g, core: (jnp.minimum(core[0] * 2 + g, 2), 0, 0))),
            (mixed, flat),
            (branch, flat),
        ],
        quarters(rows, width, part),
        "qkv_out_term",
        3.5,
    )


def down_term(left, right, core):
    rows, width = right.shape
    shares = lax.axis_size("narrow")
    part = left.shape[1] // (2 * shares)
    direct = part == width
    if not direct:
        left = left.reshape(rows, shares, 2, 2, part // 2)
        left = lax.dynamic_index_in_dim(left, core[0], 2, keepdims=False)
        left = left.reshape(rows, 2, shares // 2, 2, part // 2).swapaxes(2, 3).reshape(rows, 2 * width)
    half = width // 2

    def body(core_ref, l_ref, r_ref, *outs):
        value = dot(l_ref[...], r_ref[...], (0, 0)).astype(low)
        for owner in range(2):

            @pl.when(pl.program_id(0) == owner)
            def _():
                outs[2 * owner][...] = value[:half]
                outs[2 * owner + 1][...] = value[half:]

    return picked(
        body,
        core,
        (2,),
        [
            (left, pl.BlockSpec((rows, width), lambda g, core: (0, g * 2 + core[0] if direct else g))),
            (right, pl.BlockSpec((rows, width), lambda g, core: (0, 0))),
        ],
        quarters(rows, width, part // 2),
        "down_term",
        3.5,
    )


def join_term(middle, skip, right, core):
    rows, width = right.shape
    shares = lax.axis_size("narrow")
    part = width // shares
    half = width // 2
    if part != half:
        left = jnp.concatenate([middle, skip], axis=1).reshape(rows, shares, 2, 2, part // 2)
        left = lax.dynamic_index_in_dim(left, core[0], 2, keepdims=False)
        left = left.reshape(rows, 2, shares // 2, 2, part // 2).swapaxes(2, 3).reshape(rows, width)
        middle, skip = left[:, :half], left[:, half:]

    def body(core_ref, m_ref, s_ref, r_ref, *outs):
        for owner, left_ref in enumerate((m_ref, s_ref)):
            value = dot(left_ref[...], r_ref[...], (0, 0)).astype(low)
            outs[2 * owner][...] = value[: half // 2]
            outs[2 * owner + 1][...] = value[half // 2 :]

    side = pl.BlockSpec((rows, half), lambda g, core: (0, core[0] if part == half else 0))
    return picked(
        body,
        core,
        (1,),
        [(middle, side), (skip, side), (right, pl.BlockSpec((rows, width), lambda g, core: (0, 0)))],
        quarters(rows, width, part // 2),
        "join_term",
        2,
    )


def cross(bit, *pieces):
    kept, got = pieces[: len(pieces) // 2], pieces[len(pieces) // 2 :]
    rows, columns = kept[0].shape
    blocks = len(kept) // 2
    steps = 2 if rows % 32 == 0 else 1

    def body(bit_ref, *refs):
        sent_ref, left_ref = refs[-2:]

        def put(target, owner):
            for block in range(blocks):
                place = owner * blocks + block
                one, two = refs[place], refs[2 * blocks + place]
                target[block] = (one[...].astype(full) + two[...].astype(full)).astype(low)

        for mine in range(2):

            @pl.when(bit_ref[0] == mine)
            def _():
                put(sent_ref, 1 - mine)
                put(left_ref, mine)

    ins = [(piece, pl.BlockSpec((rows // steps, columns), lambda g, bit: (g, 0))) for piece in kept + got]
    out = ((blocks, rows, columns), low, pl.BlockSpec((blocks, rows // steps, columns), lambda g, bit: (0, g, 0)))
    return picked(body, bit, (steps,), ins, [out, out], "cross", 2)


def add_halve(bit, *pairs):
    lead, columns = pairs[0].shape[0], pairs[0].shape[-1]
    sizes = [pair.shape[2] for pair in pairs[::2]]
    total = sum(sizes)
    steps = 2 if len(sizes) == 1 and total % 32 == 0 and total >= 256 else 1

    def body(bit_ref, *refs):
        mine = bit_ref[0]
        for target, place in ((refs[-2], 1 - mine), (refs[-1], mine)):
            begin = 0
            for kept_ref, got_ref in zip(refs[:-2:2], refs[1:-2:2]):
                length = kept_ref.shape[2]
                for each in range(lead):
                    value = kept_ref[each, place].astype(full) + got_ref[each, place].astype(full)
                    target[each, begin : begin + length] = value.astype(low)
                begin += length

    ins = [
        (pair, pl.BlockSpec((lead, 2, pair.shape[2] // steps, columns), lambda g, bit: (0, 0, g, 0)))
        for pair in pairs
    ]
    out = (
        (lead, total, columns),
        low,
        pl.BlockSpec((lead, total // steps, columns), lambda g, bit: (0, g, 0)),
    )
    return picked(body, bit, (steps,), ins, [out, out], "add_halve", 2)


def add_into(target, place, count, one, two):
    rows, columns = one.shape[-2:]
    steps = 2 if rows % 32 == 0 else 1
    block = pl.BlockSpec((1, rows // steps, columns), lambda g: (0, g, 0))

    def body(one_ref, two_ref, *rest):
        rest[-1][...] = (one_ref[...].astype(full) + two_ref[...].astype(full)).astype(low)

    ins = [one.reshape(1, rows, columns), two.reshape(1, rows, columns)]
    return pl.pallas_call(
        body,
        grid=(steps,),
        in_specs=[block, block] + ([] if target is None else [ANY]),
        out_specs=pl.BlockSpec((1, rows // steps, columns), lambda g: (place, g, 0)),
        out_shape=jax.ShapeDtypeStruct((count, rows, columns), low),
        name="add_into",
        input_output_aliases={} if target is None else {2: 0},
        cost_estimate=cost(1.3),
    )(*ins, *([] if target is None else [target]))


def add(one, two):
    return (one.astype(full) + two.astype(full)).astype(low)


def pair_up(own, got, bit):
    rows, columns = own.shape

    def body(bit_ref, own_ref, got_ref, out_ref):
        mine = bit_ref[0]
        out_ref[mine] = own_ref[...]
        out_ref[1 - mine] = got_ref[...]

    flat = pl.BlockSpec((rows, columns), lambda g, bit: (0, 0))
    out = ((2, rows, columns), low, pl.BlockSpec((2, rows, columns), lambda g, bit: (0, 0, 0)))
    return picked(body, bit, (1,), [(own, flat), (got, flat)], [out], "pair_up", 1)[0]


def finish(kind, half, own, got, begin, length, core, layer, targets):
    pieces, _, columns = own.shape
    scale = 1.0 / lax.axis_size("wide")
    aliases = {place + 2: place for place in range(len(targets))}
    source = pl.BlockSpec((pieces, length, columns), lambda g, core: (0, begin // length, 0))
    ins = [(own, source), (got, source)] + [(target, ANY) for target in targets]
    rows = pieces * length

    def chosen(core_ref, which, own_ref, got_ref, place=None):
        sides = [own_ref, got_ref]
        if place is None:
            values = [side[...].reshape(pieces * length, columns) for side in sides]
        else:
            if pieces == 1:
                near = (0, pl.ds(place * (length // 2), length // 2))
            else:
                near = (pl.ds(place * (pieces // 2), pieces // 2),)
            values = [side[near].reshape(pieces * length // 2, columns) for side in sides]
        return jnp.where(core_ref[0] == which, values[0], values[1]).astype(full) * scale

    if kind in ("down", "join"):

        def body(core_ref, own_ref, got_ref, *rest):
            rest[-1][0] = chosen(core_ref, pl.program_id(0), own_ref, got_ref)

        place = layer if kind == "down" else 0
        shape = (2 if kind == "down" else 1, 2 * rows, columns)
        out = (shape, full, pl.BlockSpec((1, rows, columns), lambda g, core: (place, g, 0)))
        return picked(body, core, (2,), ins, [out], "finish_rows", 3, aliases)
    steps = 4 if half is None else 2
    rows = rows // 2 if half is None else rows

    def block(step):
        return step if half is None else 2 * step + half

    def values_of(core_ref, own_ref, got_ref):
        step = pl.program_id(0)
        if half is None:
            return chosen(core_ref, step // 2, own_ref, got_ref, step % 2)
        return chosen(core_ref, step, own_ref, got_ref)

    def body(core_ref, own_ref, got_ref, *rest):
        values = values_of(core_ref, own_ref, got_ref)
        if kind == "up":
            rest[-1][0] = values
            return
        if half == 0:
            rest[-1][0] = values
            return
        last = block(pl.program_id(0)) == 3

        @pl.when(jnp.logical_not(last))
        def _():
            rest[-2][0] = values

        @pl.when(last)
        def _():
            rest[-1][0] = values

    if kind == "up":
        outs = [((2, rows, 4 * columns), full, pl.BlockSpec((1, rows, columns), lambda g, core: (layer, 0, block(g))))]
        return picked(body, core, (steps,), ins, outs, "finish_columns", 3, aliases)

    def spot(step):
        return block(step if half == 0 else jnp.minimum(step, steps - 2))

    outs = [
        ((2, rows, 3 * columns), full, pl.BlockSpec((1, rows, columns), lambda g, core: (layer, 0, spot(g)))),
        ((2, rows, columns), full, pl.BlockSpec((1, rows, columns), lambda g, core: (layer, 0, 0))),
    ]
    if half == 0:
        kept = targets[1:]
        ins, outs, aliases = ins[:3] if targets else ins, outs[:1], {2: 0} if targets else {}
        return (picked(body, core, (steps,), ins, outs, "finish_qkv", 3, aliases)[0], *kept)
    return picked(body, core, (steps,), ins, outs, "finish_qkv_out", 3, aliases)


def small_gradients(total, me, width, shares, blocks):
    part = width // shares
    scale = 1.0 / lax.axis_size("wide")

    def body(me_ref, total_ref, gains_ref, shifts_ref, out_ref, up_ref, down_ref, join_ref):
        values = total_ref[...] * scale
        back = [values[0:8], values[8:16]]
        ahead = [values[16 : 20 + blocks], values[20 + blocks : 24 + 2 * blocks]]
        for place in range(shares):

            @pl.when(me_ref[0] == place)
            def _():
                columns = slice(place * part, place * part + part)
                for layer in range(2):
                    for row, target in ((0, gains_ref), (1, shifts_ref)):
                        target[layer, 0:1] = back[layer][row : row + 1, columns]
                        target[layer, 1:2] = ahead[layer][row + 1 : row + 2, columns]
                    out_ref[layer : layer + 1] = ahead[layer][3:4, columns]
                    down_ref[layer : layer + 1] = ahead[layer][0:1, columns]
                    begin = place * part * blocks
                    while begin < (place + 1) * part * blocks:
                        row, column = begin // width, begin % width
                        length = min(width - column, (place + 1) * part * blocks - begin)
                        at = begin - place * part * blocks
                        piece = ahead[layer][4 + row : 5 + row, column : column + length]
                        up_ref[layer : layer + 1, at : at + length] = piece
                        begin += length
                join_ref[...] = back[1][2:3, columns]

    shapes = [(2, 2, part), (2, 2, part), (2, part), (2, part * blocks), (2, part), (1, part)]
    outs = [(shape, full, pl.BlockSpec(shape, lambda g, me, n=len(shape): (0,) * n)) for shape in shapes]
    ins = [(total, pl.BlockSpec(total.shape, lambda g, me: (0, 0)))]
    return picked(body, me, (1,), ins, outs, "small_gradients", 1)


def after(value, *earlier):
    return lax.optimization_barrier((value,) + earlier)[0] if earlier else value


def swap(values, axis, mask):
    size = lax.axis_size(axis)
    return lax.ppermute(values, axis, [(source, source ^ mask) for source in range(size)])


def masks(axis):
    return [1 << bit for bit in range(lax.axis_size(axis).bit_length() - 1)]


class Order:
    def __init__(self):
        self.last = ()

    def run(self, function, *arrays):
        held = lax.optimization_barrier(tuple(arrays) + self.last)[: len(arrays)]
        out = function(*held)
        self.last = (jax.tree.leaves(out)[0],)
        return out

    def hold(self, *arrays):
        self.last += arrays


def place_bit(axis, mask):
    return ((lax.axis_index(axis) & mask) // mask).astype(jnp.int32).reshape(1)


class Term:
    def __init__(self, order, kind, layer, function, *arrays):
        self.order, self.kind, self.layer, self.half = order, kind, layer, None
        self.core = place_bit("wide", 1)
        sent = order.run(lambda *x: function(*x, 1 - self.core), *arrays)
        self.got = [swap(each, "wide", 1) for each in sent]
        self.columns = sent[0].shape[-1]
        self.keep = lambda: order.run(lambda *x: function(*x, self.core), *arrays)

    def stay(self):
        self.kept, self.keep = self.keep(), None

    def part(self, half):
        other = copy.copy(self)
        other.kept, other.got, other.half = self.kept[half::2], self.got[half::2], half
        return other

    def pass_narrow(self):
        stages = list(reversed(masks("narrow")))
        if isinstance(self.kept, (list, tuple)):
            bit = place_bit("narrow", stages[0])
            blocks = len(self.kept) // 2
            sent, self.kept = self.order.run(lambda *x: cross(bit, *x), *self.kept, *self.got)
            self.got = swap(sent, "narrow", stages.pop(0))
        else:
            blocks = 1
        for mask in stages:
            pairs = [(self.kept, self.got)]
            self.kept, self.got = halve(self.order, "narrow", mask, blocks, pairs, self.columns)

    def pass_first(self, mask):
        swapped = [self.kept[owner * 2 + block] for block in range(2) for owner in range(2)]
        brought = [self.got[owner * 2 + block] for block in range(2) for owner in range(2)]
        bit = place_bit("wide", mask)
        sent, self.kept = self.order.run(lambda *x: cross(bit, *x), *swapped, *brought)
        self.got = swap(sent, "wide", mask)

    def pass_wide(self, mask):
        pairs = list(zip(self.kept, self.got)) if isinstance(self.kept, (list, tuple)) else [(self.kept, self.got)]
        self.kept, self.got = halve(self.order, "wide", mask, 1, pairs, self.columns)

    def add_into(self, target, place, count):
        kept, got = [side.reshape(-1, self.columns) for side in (self.kept, self.got)]
        if target is None:
            return self.order.run(lambda one, two: add_into(None, place, count, one, two), kept, got)
        return self.order.run(lambda target, one, two: add_into(target, place, count, one, two), target, kept, got)

    def finish(self, done, own, got, begin, length):
        targets = done.get(self.kind, ())

        def last(own, got, core, *targets):
            return finish(self.kind, self.half, own, got, begin, length, core, self.layer, targets)

        done[self.kind] = self.order.run(last, own, got, self.core, *targets)


def halve(order, axis, mask, lead, pairs, columns):
    shaped = [array.reshape(lead, 2, -1, columns) for pair in pairs for array in pair]
    bit = place_bit(axis, mask)
    sent, kept = order.run(lambda *x: add_halve(bit, *x), *shaped)
    return kept, swap(sent, axis, mask)


class Reduce:
    def __init__(self, order, terms, passed=(), late=()):
        self.order, self.terms = order, terms
        rest = [mask for mask in masks("wide")[1:] if mask not in passed]
        self.down = [mask for mask in rest if mask not in late] + [mask for mask in rest if mask in late]
        self.up = list(reversed(passed))
        self.pieces, self.columns = 2 ** len(passed), terms[0].columns
        self.parts = [(term.kept, term.got) for term in terms]
        self.lengths, self.first = [each.size // self.columns for each, _ in self.parts], True
        self.joining, self.closed = None, False

    def step(self):
        if self.closed:
            return
        if self.down:
            mask = self.down.pop(0)
            rows = [kept.size // self.columns for kept, _ in self.parts]
            even = all(each % 32 == 0 for each in rows)
            if self.first and even:
                self.pieces, self.lengths = 2 * self.pieces, [each // 2 for each in rows]
            self.first = False
            if even:
                self.up.insert(0, mask)
                self.parts = [halve(self.order, "wide", mask, 1, self.parts, self.columns)]
            else:
                flat = [[side.reshape(-1, self.columns) for side in pair] for pair in self.parts]
                pair = [jnp.concatenate(sides) for sides in zip(*flat)]
                total = self.order.run(add, *pair)
                self.parts = [(total, swap(total, "wide", mask))]
            return
        kept, got = [array.reshape(-1, self.columns) for array in self.parts[0]]
        if self.joining is None:
            total = self.order.run(add, kept, got)
        else:
            bit = place_bit("wide", self.joining)
            total = self.order.run(lambda *x: pair_up(*x, bit), kept, got).reshape(-1, self.columns)
        if self.up:
            self.joining = self.up.pop(0)
            self.parts = [(total, swap(total, "wide", self.joining))]
        else:
            self.parts = [(total, swap(total, "wide", 1))]
            self.closed = True

    def finish(self, done):
        own, got = [array.reshape(self.pieces, -1, self.columns) for array in self.parts[0]]
        begin = 0
        for term, length in zip(self.terms, self.lengths):
            term.finish(done, own, got, begin, length)
            begin += length


def on_device(
    tokens,
    skip,
    flags,
    cotangent,
    norm_gains,
    norm_biases,
    qkv_weight,
    out_weight,
    out_bias,
    up_weight,
    up_bias,
    down_weight,
    down_bias,
    skip_weight,
    skip_bias,
):
    items, seq_rows, width = tokens.shape
    rows = items * seq_rows
    me = lax.axis_index("narrow")
    shares = lax.axis_size("narrow")
    spots = jnp.stack([me, lax.axis_index("wide")]).astype(jnp.int32)
    order = Order()

    def fetches(layer):
        return (
            Fetch([(qkv_weight, layer)], (1, 2)),
            Fetch([(out_weight, layer), (up_weight, layer)], (1, 2)),
            Fetch([(down_weight, layer)], (1, 4)),
        )

    fetch_qkv0, fetch_up0, fetch_down0 = fetches(0)
    fetch_qkv1, fetch_up1, fetch_down1 = fetches(1)
    fetch_join = Fetch([(skip_weight, None)], (1, 4))
    qkv0, qkv1 = [Weight(each, 0, width, spots) for each in (fetch_qkv0, fetch_qkv1)]
    out0, out1 = [Weight(each, 0, width, spots) for each in (fetch_up0, fetch_up1)]
    up0, up1 = [Weight(each, 1, width, spots) for each in (fetch_up0, fetch_up1)]
    down0, down1 = [Weight(each, 0, width, spots) for each in (fetch_down0, fetch_down1)]
    join = Weight(fetch_join, 0, width, spots)

    small = (norm_gains, norm_biases, out_bias, down_bias, skip_bias, up_bias)
    held = order.run(pack_small, *small)[None]
    for mask in masks("narrow"):
        held = jnp.concatenate([held, swap(held, "narrow", mask)])
    fetch_qkv0.fetch(*order.last)
    fetch_up0.fetch(held)
    fetch_down0.fetch(fetch_up0.sent)
    fetch_join.fetch(fetch_down0.sent)
    fetch_qkv1.fetch(fetch_join.sent)
    place = me.astype(jnp.int32).reshape(1)
    lines = order.run(lambda x: unpack_small(x, place, small, width), held)

    def line(row):
        return lines[row : row + 1]

    gains, shifts = [[line(2 * layer + each) for each in range(2)] for layer in range(2)], None
    shifts = [[line(4 + 2 * layer + each) for each in range(2)] for layer in range(2)]
    out_biases, down_biases, join_shift = [line(8), line(9)], [line(10), line(11)], line(12)
    blocks = up0.blocks
    up_biases = [lines[13 + layer * blocks : 13 + (layer + 1) * blocks].reshape(1, -1) for layer in range(2)]

    tokens_flat, skip_flat, cotangent_flat = [array.reshape(rows, width) for array in (tokens, skip, cotangent)]
    lengths = PATCHES + 1 + CAPTION * flags
    valid = lax.broadcasted_iota(jnp.int32, (items, seq_rows), 1) < lengths[:, None]
    keep = valid.reshape(rows, 1).astype(full)
    dz1 = jnp.where(keep > 0, cotangent_flat, 0)

    fetch_qkv0.share(1)
    fetch_qkv0.share(0)
    order.hold(*fetch_up0.got())
    fetch_up0.share(1)
    a0, packed0 = order.run(lambda *x: project_qkv(*x, qkv0), tokens_flat, gains[0][0], shifts[0][0])
    order.hold(*fetch_down0.got())
    fetch_down0.share(1, a0)
    fetch_up1.fetch(a0)
    fetch_down1.fetch(fetch_up1.sent)
    packed0 = packed0.reshape(3, items, seq_rows, width)
    mixed0, totals0 = order.run(lambda *x: attend(*x, items, seq_rows), packed0, lengths)
    fetch_up0.share(0, mixed0)
    fetch_down0.share(0, mixed0)
    order.hold(*fetch_join.got(), *fetch_qkv1.got())
    fetch_join.share(1, mixed0)
    fetch_qkv1.share(1, mixed0)
    mixed0 = mixed0.reshape(rows, width)
    m0, second0, hidden0, slope0, middle = order.run(
        lambda x, o, ob, g, s, ub, db: feed_forward(x, o, out0, ob, g, s, up0, ub, down0, db),
        tokens_flat, mixed0, out_biases[0], gains[0][1], shifts[0][1], up_biases[0], down_biases[0],
    )
    fetch_join.share(0, middle)
    fetch_qkv1.share(0, middle)
    order.hold(*fetch_up1.got(), *fetch_down1.got())
    fetch_up1.share(1, middle)
    fetch_down1.share(1, middle)
    entry, a1, packed1 = order.run(
        lambda m, s, jb, g, sh: join_qkv(m, s, join, jb, g, sh, qkv1),
        middle, skip_flat, join_shift, gains[1][0], shifts[1][0],
    )
    packed1 = packed1.reshape(3, items, seq_rows, width)
    mixed1, totals1 = order.run(lambda *x: attend(*x, items, seq_rows), packed1, lengths)
    fetch_up1.share(0, mixed1)
    fetch_down1.share(0, mixed1)
    mixed1 = mixed1.reshape(rows, width)
    m1, second1, hidden1, slope1, output = order.run(
        lambda x, o, ob, g, s, ub, db, k: feed_forward(x, o, out1, ob, g, s, up1, ub, down1, db, k),
        entry, mixed1, out_biases[1], gains[1][1], shifts[1][1], up_biases[1], down_biases[1], keep,
    )

    done = {}
    term_down1 = Term(order, "down", 1, down_term, hidden1, dz1)
    term_down1.stay()
    term_down1.pass_narrow()
    du, dm, db, do, sums1 = order.run(
        lambda y, z, s, m, g: feed_forward_back(y, z, s, down1, up1, m, g, out1),
        dz1, dz1, slope1, m1, gains[1][1],
    )
    term_up1 = Term(order, "up", 1, up_term, second1, du)
    term_up1.stay()
    term_up1.pass_narrow()
    total = term_down1.add_into(None, 0, 3)
    dpacked = order.run(
        lambda *x: attend_back(*x, items, seq_rows), packed1, do.reshape(items, seq_rows, width), totals1, lengths
    )
    flat_packed = dpacked.reshape(3, rows, width)
    term_qkv1 = Term(order, "qkv", 1, qkv_out_term, a1, flat_packed, mixed1, db)
    term_qkv1.stay()
    term_qkv1.pass_narrow()
    total = term_up1.add_into(total, 1, 3)
    dentry, dmiddle, dz0, skip_grad, sums3 = order.run(
        lambda gp, x, g, dm: project_back(gp, qkv1, x, g, dm, join), flat_packed, entry, gains[1][0], dm
    )
    term_join = Term(order, "join", 1, join_term, middle, skip_flat, dentry)
    term_join.stay()
    term_join.pass_narrow()
    term_down0 = Term(order, "down", 0, down_term, hidden0, dz0)
    term_down0.stay()
    total = term_qkv1.add_into(total, 2, 3)
    size = lax.axis_size("wide")
    groups = [[device + core for device in range(0, size, 2)] for core in range(2)]
    flat_total = total.reshape(-1, width)
    part = lax.psum_scatter(flat_total, "wide", axis_index_groups=groups, scatter_dimension=0, tiled=True)
    term_down0.pass_first(2)

    du, dm, db, do, sums0 = order.run(
        lambda y, z, s, m, g: feed_forward_back(y, z, s, down0, up0, m, g, out0),
        dmiddle, dz0, slope0, m0, gains[0][1],
    )
    term_join.pass_wide(2)
    term_up0 = Term(order, "up", 0, up_term, second0, du)
    term_up0.stay()
    term_down0.pass_narrow()
    term_up0.pass_narrow()
    dpacked = order.run(
        lambda *x: attend_back(*x, items, seq_rows), packed0, do.reshape(items, seq_rows, width), totals0, lengths
    )
    order.hold(term_down0.got, term_join.got)
    flat_packed = dpacked.reshape(3, rows, width)
    term_qkv0 = Term(order, "qkv", 0, qkv_out_term, a0, flat_packed, mixed0, db)
    term_qkv0.stay()
    one, two = term_qkv0.part(0), term_qkv0.part(1)
    one.pass_narrow()
    two.pass_narrow()
    first = Reduce(order, [term_down0, term_join], (2,))
    first.step()
    second = Reduce(order, [term_up0])
    second.step()
    tokens_grad, sums2 = order.run(
        lambda gp, x, g, dm: project_back(gp, qkv0, x, g, dm), flat_packed, tokens_flat, gains[0][0], dm
    )
    minor = jnp.concatenate([sums2, sums3, sums0, sums1])
    places = masks("wide")
    minor_stages = [("narrow", mask) for mask in masks("narrow")]
    minor_stages += [("wide", mask) for mask in places if mask != 2] + [("wide", mask) for mask in places if mask == 2]
    minor_got = swap(minor, *minor_stages[0])

    def minor_step():
        nonlocal minor, minor_got
        if minor_stages:
            minor_stages.pop(0)
            minor = order.run(lambda one, two: one + two, minor, minor_got)
            if minor_stages:
                minor_got = swap(minor, *minor_stages[0])

    third = Reduce(order, [one], late=(2,))
    third.step()
    first.step()
    second.step()
    order.hold(part)
    gathered = lax.all_gather(after(part, *order.last), "wide", axis_index_groups=groups, tiled=True)
    fourth = Reduce(order, [two])
    fourth.step()
    third.step()
    minor_step()
    first.step()
    fourth.step()
    second.step()
    minor_step()
    third.step()
    first.step()
    minor_step()
    fourth.step()
    second.step()
    third.step()
    minor_step()
    first.step()
    fourth.step()
    second.step()
    third.step()
    order.hold(gathered)
    other = swap(after(gathered, *order.last), "wide", 1)
    fourth.step()
    minor_step()
    second.step()
    first.step()
    own, got = gathered.reshape(1, -1, width), other.reshape(1, -1, width)
    for which, term in enumerate((term_down1, term_up1, term_qkv1)):
        term.finish(done, own, got, which * (own.shape[1] // 3), own.shape[1] // 3)
    third.step()
    fourth.step()
    first.finish(done)
    second.step()
    third.step()
    fourth.step()
    for each in (first, second, third, fourth):
        while not each.closed:
            each.step()
    while minor_stages:
        minor_step()
    second.finish(done)
    third.finish(done)
    fourth.finish(done)
    small = order.run(lambda x: small_gradients(x, place, width, shares, up1.blocks), minor)

    return (
        output.reshape(tokens.shape),
        tokens_grad.reshape(tokens.shape),
        skip_grad.reshape(tokens.shape),
        small[0],
        small[1],
        done["qkv"][0],
        done["qkv"][1],
        small[2],
        done["up"][0],
        small[3],
        done["down"][0],
        small[4],
        done["join"][0][0],
        small[5].reshape(-1),
    )


def solution(mesh):
    placed = (
        P(("wide", "narrow"), None, None),
        P(("wide", "narrow"), None, None),
        P(("wide", "narrow")),
        P(("wide", "narrow"), None, None),
        P(None, None, "narrow"),
        P(None, None, "narrow"),
        P(None, "narrow", None),
        P(None, "narrow", None),
        P(None, "narrow"),
        P(None, "narrow", None),
        P(None, "narrow"),
        P(None, "narrow", None),
        P(None, "narrow"),
        P("narrow", None),
        P("narrow"),
    )
    return jax.shard_map(
        on_device,
        mesh=mesh,
        in_specs=placed,
        out_specs=(
            P(("wide", "narrow"), None, None),
            P(("wide", "narrow"), None, None),
            P(("wide", "narrow"), None, None),
            P(None, None, "narrow"),
            P(None, None, "narrow"),
            P(None, "narrow", None),
            P(None, "narrow", None),
            P(None, "narrow"),
            P(None, "narrow", None),
            P(None, "narrow"),
            P(None, "narrow", None),
            P(None, "narrow"),
            P("narrow", None),
            P("narrow"),
        ),
        check_vma=False,
    )
```

```python
import copy
import math

import jax
import jax.numpy as jnp
from jax import lax
from jax.experimental import pallas as pl
from jax.experimental.pallas import tpu as pltpu
from jax.sharding import PartitionSpec as P

HEAD_DIM = 64
PATCHES = 256
CAPTION = 77
PAIR = 2 * HEAD_DIM


epsilon = 1e-05
masked_score = -1e30
low = jnp.bfloat16
full = jnp.float32
SPARE = 14
ANY = pl.BlockSpec(memory_space=pltpu.HBM)
SCALARS = pl.BlockSpec(memory_space=pltpu.SMEM)


def dot(left, right, contract=(1, 0)):
    dims = (((contract[0],), (contract[1],)), ((), ()))
    return lax.dot_general(left, right, dims, preferred_element_type=full)


def normalize(values):
    centred = values - jnp.mean(values, axis=-1, keepdims=True)
    factor = lax.rsqrt(jnp.mean(centred * centred, axis=-1, keepdims=True) + epsilon)
    return centred * factor, factor


def normalize_back(upstream, normed, factor):
    return factor * (
        upstream
        - jnp.mean(upstream, axis=-1, keepdims=True)
        - normed * jnp.mean(upstream * normed, axis=-1, keepdims=True)
    )


def column_sum(values):
    return jnp.sum(values.astype(full), axis=0, keepdims=True)


def whole(shape):
    return pl.BlockSpec(shape, lambda *grid: (0,) * len(shape))


def cost(micros):
    return pl.CostEstimate(flops=int(micros * 3 * 10**8), bytes_accessed=0, transcendentals=0)


def room(ins, outs, scratch, spare):
    total = spare * 2**20
    for shape, kind, spec in [(array.shape, array.dtype, spec) for array, spec in ins] + list(outs):
        if spec.block_shape is not None and spec.memory_space is None:
            total += 2 * math.prod(spec.block_shape) * jnp.dtype(kind).itemsize
    for piece in scratch:
        if piece.memory_space == pltpu.VMEM:
            total += math.prod(piece.shape) * jnp.dtype(piece.dtype).itemsize
    return total


def call(body, grid, ins, outs, name, micros, scratch=(), spare=6):
    return pl.pallas_call(
        body,
        grid=grid,
        in_specs=[spec for _, spec in ins],
        out_specs=[spec for _, _, spec in outs],
        out_shape=[jax.ShapeDtypeStruct(shape, kind) for shape, kind, _ in outs],
        scratch_shapes=list(scratch),
        name=name,
        cost_estimate=cost(micros),
        compiler_params=pltpu.CompilerParams(vmem_limit_bytes=room(ins, outs, scratch, spare)),
    )(*[array for array, _ in ins])


class Fetch:
    def __init__(self, arrays, sharing):
        self.arrays, self.sharing = arrays, list(sharing)
        self.rows = arrays[0][0].shape[-2]
        while self.rows % (16 << len(self.sharing)):
            self.sharing.pop()
        self.length = self.rows >> len(self.sharing)

    def quarter(self, place):
        return sum(((place // mask) & 1) << bit for bit, mask in enumerate(self.sharing))

    def cut(self, *earlier):
        found = []
        for array, layer in self.arrays:
            array = after(array, *earlier)
            lead = () if layer is None else (layer,)
            begin = self.quarter(lax.axis_index("wide")) * self.length
            sizes = (1,) * len(lead) + (self.length, array.shape[-1])
            found.append(lax.dynamic_slice(array, lead + (begin, 0), sizes).reshape(self.length, -1))
        self.sent = (jnp.concatenate(found, axis=1) if len(found) > 1 else found[0])[None]

    def fetch(self, *earlier):
        held = after(self.sent, *earlier)
        for mask in masks("narrow"):
            held = jnp.concatenate([held, swap(held, "narrow", mask)])
        self.pieces = {0: held[1:]}

    def share(self, which, *earlier):
        if which < len(self.sharing):
            mask = self.sharing[which]
            got = {key ^ (1 << which): swap(after(piece, *earlier), "wide", mask) for key, piece in self.pieces.items()}
            self.pieces.update(got)

    def got(self):
        return list(self.pieces.values())


class Weight:
    def __init__(self, fetched, which, width, spots):
        self.fetched, self.spots, self.width = fetched, spots, width
        self.array, self.layer = fetched.arrays[which]
        self.begin = sum(array.shape[-1] for array, _ in fetched.arrays[:which])
        self.rows, columns = self.array.shape[-2:]
        self.shares = lax.axis_size("narrow")
        self.blocks = columns // width
        self.total = self.rows * self.shares

    def arrays(self):
        return [self.array] + self.fetched.got()

    def scratch(self):
        copies = 1 + len(self.fetched.pieces) * (self.shares - 1)
        return [pltpu.VMEM((self.blocks, self.total, self.width), low), pltpu.SemaphoreType.DMA((self.blocks, copies))]

    def copies(self, spots, refs, held, signals, block):
        own, pieces = refs[0], refs[1:]
        me, length = spots[0], self.fetched.length
        own = own if self.layer is None else own.at[self.layer]
        columns = pl.ds(block * self.width, self.width)
        begin = pl.multiple_of(me * self.rows, 16)
        found = [(own.at[:, columns], begin, self.rows)]
        columns = pl.ds(self.begin + block * self.width, self.width)
        for key, piece in zip(self.fetched.pieces, pieces):
            for offset in range(1, self.shares):
                begin = (me ^ offset) * self.rows + (self.fetched.quarter(spots[1]) ^ key) * length
                found.append((piece.at[offset - 1, :, columns], pl.multiple_of(begin, 16), length))
        return [
            pltpu.make_async_copy(source, held.at[block, pl.ds(begin, length)], signals.at[block, place])
            for place, (source, begin, length) in enumerate(found)
        ]

    def wait(self, *refs, block=0):
        for copy in self.copies(*refs, block):
            copy.wait()


def weighted(body, weights, grid, ins, outs, name, micros, scratch=(), first=((0, 0),), spare=SPARE):
    spots = weights[0].spots
    operands = [(spots, SCALARS)]
    for weight in weights:
        operands += [(pltpu.with_memory_space_constraint(array, pltpu.HBM), ANY) for array in weight.arrays()]
    counts = [len(weight.arrays()) for weight in weights]
    extra = [piece for weight in weights for piece in weight.scratch()]

    def wrapped(*refs):
        spots_ref, rest = refs[0], list(refs[1:])
        sources = []
        for count in counts:
            sources.append(rest[:count])
            rest = rest[count:]
        spare = rest[len(rest) - len(extra) :]
        rest = rest[: len(rest) - len(extra)]
        handles = []
        for place, weight in enumerate(weights):
            held, signals = spare[2 * place : 2 * place + 2]
            refs_of = (spots_ref, sources[place], held, signals)
            handles.append((weight, refs_of, held))

        everything = [(place, block) for place, weight in enumerate(weights) for block in range(weight.blocks)]

        def begin(wanted):
            for place, block in wanted:
                weight, refs_of, _ = handles[place]
                for copy in weight.copies(*refs_of, block):
                    copy.start()

        @pl.when(pl.program_id(0) == 0)
        def _():
            begin(first)

        def ready(place, block=0, then=False):
            weight, refs_of, held = handles[place]
            weight.wait(*refs_of, block=block)
            if then:
                begin([each for each in everything if each not in first])

        body(ready, [held for _, _, held in handles], *rest)

    return call(wrapped, grid, operands + ins, outs, name, micros, list(scratch) + extra, spare)


def pack_small(*small):
    part = small[0].shape[-1]
    counts = [piece.size // part for piece in small]

    def body(*refs):
        row = 0
        for ref in refs[:-1]:
            values = ref[...].reshape(-1, ref.shape[-1])
            for each in range(values.shape[0]):
                for begin in range(0, values.shape[1], part):
                    refs[-1][row : row + 1] = values[each : each + 1, begin : begin + part].astype(full)
                    row += 1
        refs[-1][row:] = jnp.zeros((refs[-1].shape[0] - row, part), full)

    flat = [piece.reshape((1,) * (2 - piece.ndim) + piece.shape) for piece in small]
    rows = -(-sum(counts) // 16) * 16
    out = ((rows, part), full, whole((rows, part)))
    return call(body, (1,), [(piece, whole(piece.shape)) for piece in flat], [out], "pack_small", 1)[0].astype(low)


def unpack_small(parts, me, small, width):
    shares, _, part = parts.shape
    lines = [(piece.size // piece.shape[-1], piece.shape[-1] // part) for piece in small]
    total = sum(count * many for count, many in lines)
    rows = -(-total // 8) * 8

    def body(me_ref, parts_ref, out_ref):
        values = parts_ref[...].astype(full)
        for mine in range(shares):

            @pl.when(me_ref[0] == mine)
            def _():
                for owner in range(shares):
                    source, target = 0, 0
                    for count, many in lines:
                        for each in range(count):
                            for piece in range(many):
                                at = owner * many * part + piece * part
                                row, column = target + at // width, at % width
                                line = values[owner ^ mine, source : source + 1]
                                out_ref[row : row + 1, column : column + part] = line
                                source += 1
                            target += many
        if rows > total:
            out_ref[total:] = jnp.zeros((rows - total, width), full)

    ins = [(parts, pl.BlockSpec(parts.shape, lambda g, me: (0, 0, 0)))]
    out = ((rows, width), full, pl.BlockSpec((rows, width), lambda g, me: (0, 0)))
    return picked(body, me, (1,), ins, [out], "unpack_small", 1)[0]


def project_qkv(inputs, gain, shift, weight):
    rows, width = inputs.shape

    def body(ready, held, x_ref, gain_ref, shift_ref, a_ref, out_ref):
        step = pl.program_id(0)

        @pl.when(step == 0)
        def _():
            normed, _ = normalize(x_ref[...].astype(full))
            a_ref[...] = (normed * gain_ref[...] + shift_ref[...]).astype(low)
            ready(0, 0, then=True)

        @pl.when(step > 0)
        def _():
            ready(0, step)

        scale = jnp.where(step == 0, HEAD_DIM ** (-0.5), 1.0)
        out_ref[0] = (dot(a_ref[...], held[0][step]).astype(low).astype(full) * scale).astype(low)

    return weighted(
        body,
        [weight],
        (3,),
        [
            (inputs, whole((rows, width))),
            (gain, whole((1, width))),
            (shift, whole((1, width))),
        ],
        [
            ((rows, width), low, whole((rows, width))),
            ((3, rows, width), low, pl.BlockSpec((1, rows, width), lambda j: (j, 0, 0))),
        ],
        "project_qkv",
        7,
    )


def join_qkv(middle, skip, join_weight, join_shift, gain, shift, weight):
    rows, width = middle.shape

    def body(ready, held, m_ref, s_ref, jb_ref, gain_ref, shift_ref, e_ref, a_ref, out_ref):
        step = pl.program_id(0)

        @pl.when(step == 0)
        def _():
            ready(0, then=True)
            entry = dot(m_ref[...], held[0][0, :width]) + dot(s_ref[...], held[0][0, width:]) + jb_ref[...]
            e_ref[...] = entry
            normed, _ = normalize(entry)
            a_ref[...] = (normed * gain_ref[...] + shift_ref[...]).astype(low)

        ready(1, step)
        scale = jnp.where(step == 0, HEAD_DIM ** (-0.5), 1.0)
        out_ref[0] = (dot(a_ref[...], held[1][step]).astype(low).astype(full) * scale).astype(low)

    return weighted(
        body,
        [join_weight, weight],
        (3,),
        [
            (middle, whole((rows, width))),
            (skip, whole((rows, width))),
            (join_shift, whole((1, width))),
            (gain, whole((1, width))),
            (shift, whole((1, width))),
        ],
        [
            ((rows, width), full, whole((rows, width))),
            ((rows, width), low, whole((rows, width))),
            ((3, rows, width), low, pl.BlockSpec((1, rows, width), lambda j: (j, 0, 0))),
        ],
        "join_qkv",
        11,
        first=((0, 0), (1, 0)),
    )


def head_masks(seq_rows):
    lane = lax.broadcasted_iota(jnp.int32, (seq_rows, PAIR), 1)
    return [lane < HEAD_DIM, lane >= HEAD_DIM]


def pairs_of(width):
    pairs = width // PAIR
    return pairs, max(group for group in (1, 2, 3) if pairs % group == 0)


def attend(packed, lengths, items, seq_rows):
    width = packed.shape[-1]
    pairs, group = pairs_of(width)

    def body(length_ref, q_ref, k_ref, v_ref, out_ref, total_ref):
        counts = lax.broadcasted_iota(jnp.int32, (seq_rows, seq_rows), 1) < length_ref[pl.program_id(0)]
        for pair in range(group):
            columns = slice(pair * PAIR, (pair + 1) * PAIR)
            queries, keys, values = q_ref[0, 0, :, columns], k_ref[0, 0, :, columns], v_ref[0, 0, :, columns]
            mixed = jnp.zeros((seq_rows, PAIR), full)
            for head, lanes in enumerate(head_masks(seq_rows)):
                scores = dot(jnp.where(lanes, queries, 0), keys, (1, 1))
                scores = jnp.where(counts, scores, masked_score)
                largest = jnp.max(scores, axis=1, keepdims=True)
                weights = jnp.exp(scores - largest)
                total = jnp.sum(weights, axis=1, keepdims=True)
                mixed += dot(weights.astype(low), jnp.where(lanes, values, 0)) * (1.0 / total)
                total_ref[0, pair, head : head + 1] = (largest + jnp.log(total)).T
            out_ref[0, :, columns] = mixed.astype(low)

    def block(which):
        return pl.BlockSpec((1, 1, seq_rows, group * PAIR), lambda n, h: (which, n, 0, h))

    return call(
        body,
        (items, pairs // group),
        [(lengths, SCALARS), (packed, block(0)), (packed, block(1)), (packed, block(2))],
        [
            (
                (items, seq_rows, width),
                low,
                pl.BlockSpec((1, seq_rows, group * PAIR), lambda n, h: (n, 0, h)),
            ),
            (
                (items, pairs, 8, seq_rows),
                full,
                pl.BlockSpec((1, group, 8, seq_rows), lambda n, h: (n, h, 0, 0)),
            ),
        ],
        "attend",
        10,
        spare=14,
    )


def attend_back(packed, grad_mixed, totals, lengths, items, seq_rows):
    width = packed.shape[-1]
    pairs, group = pairs_of(width)
    sides = [slice(0, PATCHES), slice(PATCHES, seq_rows)]

    def body(length_ref, q_ref, k_ref, v_ref, g_ref, total_ref, out_ref):
        row = PATCHES + lax.broadcasted_iota(jnp.int32, (seq_rows - PATCHES, seq_rows), 0)
        counts = row < length_ref[pl.program_id(0)]
        for pair in range(group):
            columns = slice(pair * PAIR, (pair + 1) * PAIR)
            queries, keys, values = q_ref[0, 0, :, columns], k_ref[0, 0, :, columns], v_ref[0, 0, :, columns]
            upstream = g_ref[0, :, columns]
            grad_queries = jnp.zeros((PAIR, seq_rows), full)
            grad_keys, grad_values = [0.0, 0.0], [0.0, 0.0]
            for head, lanes in enumerate(head_masks(seq_rows)):
                own_queries = jnp.where(lanes, queries, 0)
                own_upstream = jnp.where(lanes, upstream, 0)
                own_keys = jnp.where(lanes, keys, 0)
                parts, centre = [], 0.0
                for side, rows in enumerate(sides):
                    scores = dot(keys[rows], own_queries, (1, 1))
                    if side:
                        scores = jnp.where(counts, scores, masked_score)
                    probs = jnp.exp(scores - total_ref[0, pair, head : head + 1])
                    grad_probs = dot(values[rows], own_upstream, (1, 1))
                    centre += jnp.sum(grad_probs * probs, axis=0, keepdims=True)
                    parts.append((probs, grad_probs))
                for side, (probs, grad_probs) in enumerate(parts):
                    grad_scores = (probs * (grad_probs - centre)).astype(low)
                    grad_values[side] += dot(probs.astype(low), own_upstream)
                    grad_keys[side] += dot(grad_scores, own_queries)
                    grad_queries += dot(own_keys[sides[side]], grad_scores, (0, 0))
            out_ref[0, 0, :, columns] = (grad_queries.T * HEAD_DIM ** (-0.5)).astype(low)
            for side, rows in enumerate(sides):
                out_ref[1, 0, rows, columns] = grad_keys[side].astype(low)
                out_ref[2, 0, rows, columns] = grad_values[side].astype(low)

    def block(which):
        return pl.BlockSpec((1, 1, seq_rows, group * PAIR), lambda n, h: (which, n, 0, h))

    return call(
        body,
        (items, pairs // group),
        [
            (lengths, SCALARS),
            (packed, block(0)),
            (packed, block(1)),
            (packed, block(2)),
            (grad_mixed, pl.BlockSpec((1, seq_rows, group * PAIR), lambda n, h: (n, 0, h))),
            (totals, pl.BlockSpec((1, group, 8, seq_rows), lambda n, h: (n, h, 0, 0))),
        ],
        [
            (
                (3, items, seq_rows, width),
                low,
                pl.BlockSpec((3, 1, seq_rows, group * PAIR), lambda n, h: (0, n, 0, h)),
            ),
        ],
        "attend_back",
        15,
        spare=14,
    )[0]


def gelu_parts(before):
    decay = jnp.exp(before * before * -0.5)
    inverse = pl.reciprocal(1.0 + (0.3275911 * 0.5**0.5) * jnp.abs(before), approx=False)
    series = 1.061405429 * 0.5
    for term in (-1.453152027, 1.421413741, -0.284496736, 0.254829592):
        series = series * inverse + term * 0.5
    below = series * inverse * decay
    share = jnp.where(before >= 0, 1.0 - below, below)
    return before * share, share + before * decay * 0.3989422804014327


def feed_forward(inputs, mixed, out_weight, out_bias, gain, shift, up_weight, up_bias, down_weight, down_bias, lengths=None):
    rows, width = inputs.shape
    steps = up_weight.blocks
    hidden = steps * width

    def body(ready, held, x_ref, o_ref, ob_ref, gain_ref, shift_ref, ub_ref, db_ref, *rest):
        m_ref, a_ref, g_ref, s_ref, y_ref, total = rest[-6:]
        step = pl.program_id(0)

        @pl.when(step == 0)
        def _():
            ready(0, then=True)
            middle = x_ref[...].astype(full) + dot(o_ref[...], held[0][0]) + ob_ref[...]
            m_ref[...] = middle
            normed, _ = normalize(middle)
            a_ref[...] = (normed * gain_ref[...] + shift_ref[...]).astype(low)
            total[...] = middle + db_ref[...]

        ready(1, step)
        before = dot(a_ref[...], held[1][step]) + ub_ref[...]
        value, slope = gelu_parts(before)
        g_ref[...] = value.astype(low)
        s_ref[...] = slope.astype(low)

        @pl.when(step == 0)
        def _():
            ready(2)

        total[...] += dot(g_ref[...], held[2][0, pl.ds(pl.multiple_of(step * width, width), width)])

        @pl.when(step == steps - 1)
        def _():
            if lengths is None:
                y_ref[...] = total[...].astype(low)
            else:
                length = rows // lengths.shape[0]
                row = lax.broadcasted_iota(jnp.int32, (length, width), 0)
                for item in range(lengths.shape[0]):
                    at = slice(item * length, (item + 1) * length)
                    y_ref[at] = jnp.where(row < rest[0][item], total[at], 0.0).astype(low)

    return weighted(
        body,
        [out_weight, up_weight, down_weight],
        (steps,),
        [
            (inputs, whole((rows, width))),
            (mixed, whole((rows, width))),
            (out_bias, whole((1, width))),
            (gain, whole((1, width))),
            (shift, whole((1, width))),
            (up_bias, pl.BlockSpec((1, width), lambda j: (0, j))),
            (down_bias, whole((1, width))),
        ]
        + ([] if lengths is None else [(lengths, SCALARS)]),
        [
            ((rows, width), full, whole((rows, width))),
            ((rows, width), low, whole((rows, width))),
            ((rows, hidden), low, pl.BlockSpec((rows, width), lambda j: (0, j))),
            ((rows, hidden), low, pl.BlockSpec((rows, width), lambda j: (0, j))),
            ((rows, width), low, whole((rows, width))),
        ],
        "feed_forward",
        23,
        scratch=[pltpu.VMEM((rows, width), full)],
        first=((0, 0), (1, 0)),
    )


def feed_forward_back(upstream, rounded, slope, down_weight, up_weight, middle, gain, out_weight):
    rows, width = upstream.shape
    steps = up_weight.blocks
    hidden = steps * width

    def body(ready, held, y_ref, dz_ref, s_ref, m_ref, gain_ref, du_ref, dm_ref, db_ref, do_ref, sums_ref, total):
        step = pl.program_id(0)

        @pl.when(step == 0)
        def _():
            sums_ref[0:1] = column_sum(dz_ref[...])
            total[...] = jnp.zeros_like(total)
            ready(0, then=True)

        down = held[0][0, pl.ds(pl.multiple_of(step * width, width), width)]
        grad = (dot(dz_ref[...], down, (1, 1)) * s_ref[...].astype(full)).astype(low)
        du_ref[...] = grad
        sums_ref[pl.ds(4 + step, 1)] = column_sum(grad)
        ready(1, step)
        total[...] += dot(grad, held[1][step], (1, 1))

        @pl.when(step == steps - 1)
        def _():
            grad_second = total[...]
            normed, factor = normalize(m_ref[...])
            sums_ref[1:2] = column_sum(grad_second * normed)
            sums_ref[2:3] = column_sum(grad_second)
            grad_middle = y_ref[...].astype(full) + normalize_back(grad_second * gain_ref[...], normed, factor)
            dm_ref[...] = grad_middle
            branch = grad_middle.astype(low)
            db_ref[...] = branch
            sums_ref[3:4] = column_sum(branch)
            ready(2)
            do_ref[...] = dot(branch, held[2][0], (1, 1)).astype(low)

    return weighted(
        body,
        [down_weight, up_weight, out_weight],
        (steps,),
        [
            (upstream, whole((rows, width))),
            (rounded, whole((rows, width))),
            (slope, pl.BlockSpec((rows, width), lambda j: (0, j))),
            (middle, whole((rows, width))),
            (gain, whole((1, width))),
        ],
        [
            ((rows, hidden), low, pl.BlockSpec((rows, width), lambda j: (0, j))),
            ((rows, width), full, whole((rows, width))),
            ((rows, width), low, whole((rows, width))),
            ((rows, width), low, whole((rows, width))),
            ((4 + steps, width), full, whole((4 + steps, width))),
        ],
        "feed_forward_back",
        21,
        scratch=[pltpu.VMEM((rows, width), full)],
        first=((0, 0), (1, 0)),
    )


def project_back(grad_packed, weight, inputs, gain, grad_middle, join_weight=None):
    rows, width = inputs.shape
    joined = join_weight is not None

    def body(ready, held, g_ref, x_ref, gain_ref, dm_ref, *rest):
        if joined:
            de_ref, dx_ref, dz_ref, skip_ref, sums_ref, total = rest
        else:
            dx_ref, sums_ref, total = rest
        step = pl.program_id(0)

        @pl.when(step == 0)
        def _():
            total[...] = jnp.zeros_like(total)
            ready(0, 0, then=True)

        @pl.when(step > 0)
        def _():
            ready(0, step)

        total[...] += dot(g_ref[0], held[0][step], (1, 1))

        @pl.when(step == 2)
        def _():
            grad_first = total[...]
            normed, factor = normalize(x_ref[...].astype(full))
            sums_ref[0:1] = column_sum(grad_first * normed)
            sums_ref[1:2] = column_sum(grad_first)
            grad = dm_ref[...] + normalize_back(grad_first * gain_ref[...], normed, factor)
            if joined:
                entry = grad.astype(low)
                de_ref[...] = entry
                sums_ref[2:3] = column_sum(entry)
                ready(1)
                grad = dot(entry, held[1][0, :width], (1, 1))
                dx_ref[...] = grad
                dz_ref[...] = grad.astype(low)
                skip_ref[...] = dot(entry, held[1][0, width:], (1, 1))
            else:
                dx_ref[...] = grad

    ins = [
        (grad_packed, pl.BlockSpec((1, rows, width), lambda j: (j, 0, 0))),
        (inputs, whole((rows, width))),
        (gain, whole((1, width))),
        (grad_middle, whole((rows, width))),
    ]
    outs = [((rows, width), full, whole((rows, width))), ((8, width), full, whole((8, width)))]
    if joined:
        rounded = ((rows, width), low, whole((rows, width)))
        outs = [rounded, outs[0], rounded, outs[0], outs[1]]
    return weighted(
        body,
        [weight] + ([join_weight] if joined else []),
        (3,),
        ins,
        outs,
        "project_back",
        13 if joined else 9,
        scratch=[pltpu.VMEM((rows, width), full)],
    )


def picked(body, which, grid, ins, outs, name, micros, aliases=None, spare=4):
    return pl.pallas_call(
        body,
        grid_spec=pltpu.PrefetchScalarGridSpec(
            num_scalar_prefetch=1,
            grid=grid,
            in_specs=[spec for _, spec in ins],
            out_specs=[spec for _, _, spec in outs],
        ),
        out_shape=[jax.ShapeDtypeStruct(shape, kind) for shape, kind, _ in outs],
        name=name,
        input_output_aliases={place + 1: out for place, out in (aliases or {}).items()},
        cost_estimate=cost(micros),
        compiler_params=pltpu.CompilerParams(vmem_limit_bytes=room(ins, outs, (), spare)),
    )(which, *[array for array, _ in ins])


def quarters(rows, width, narrow_rows):
    shape = (lax.axis_size("narrow") // 2 * narrow_rows, width)
    return [(shape, low, pl.BlockSpec(shape, lambda g, core: (0, 0)))] * 4


def up_term(left, right, core):
    rows, width = left.shape
    part = width // lax.axis_size("narrow")
    half = width // 2

    def body(core_ref, l_ref, r_ref, *outs):
        value = dot(l_ref[...], r_ref[...], (0, 0)).astype(low)
        for block in range(2):

            @pl.when(pl.program_id(0) == block)
            def _():
                outs[block][...] = value[:half]
                outs[2 + block][...] = value[half:]

    return picked(
        body,
        core,
        (2,),
        [
            (left, pl.BlockSpec((rows, width), lambda g, core: (0, 0))),
            (right, pl.BlockSpec((rows, width), lambda g, core: (0, core[0] * 2 + g))),
        ],
        quarters(rows, width, part),
        "up_term",
        3.5,
    )


def qkv_out_term(first, packed, mixed, branch, core):
    rows, width = first.shape
    part = width // lax.axis_size("narrow")
    half = width // 2

    def body(core_ref, l_ref, r_ref, o_ref, b_ref, *outs):
        step = pl.program_id(0)
        last = core_ref[0] * 2 + step == 3

        def put(block, value):
            outs[block][...] = value[:half]
            outs[2 + block][...] = value[half:]

        @pl.when(last)
        def _():
            put(1, dot(o_ref[...], b_ref[...], (0, 0)).astype(low))

        @pl.when(jnp.logical_not(last))
        def _():
            value = dot(l_ref[...], r_ref[0], (0, 0)).astype(low)
            for block in range(2):

                @pl.when(step == block)
                def _():
                    put(block, value)

    flat = pl.BlockSpec((rows, width), lambda g, core: (0, 0))
    return picked(
        body,
        core,
        (2,),
        [
            (first, flat),
            (packed, pl.BlockSpec((1, rows, width), lambda g, core: (jnp.minimum(core[0] * 2 + g, 2), 0, 0))),
            (mixed, flat),
            (branch, flat),
        ],
        quarters(rows, width, part),
        "qkv_out_term",
        3.5,
    )


def down_term(left, right, core):
    rows, width = right.shape
    shares = lax.axis_size("narrow")
    part = left.shape[1] // (2 * shares)
    direct = part == width
    if not direct:
        left = left.reshape(rows, shares, 2, 2, part // 2)
        left = lax.dynamic_index_in_dim(left, core[0], 2, keepdims=False)
        left = left.reshape(rows, 2, shares // 2, 2, part // 2).swapaxes(2, 3).reshape(rows, 2 * width)
    half = width // 2

    def body(core_ref, l_ref, r_ref, *outs):
        value = dot(l_ref[...], r_ref[...], (0, 0)).astype(low)
        for owner in range(2):

            @pl.when(pl.program_id(0) == owner)
            def _():
                outs[2 * owner][...] = value[:half]
                outs[2 * owner + 1][...] = value[half:]

    return picked(
        body,
        core,
        (2,),
        [
            (left, pl.BlockSpec((rows, width), lambda g, core: (0, g * 2 + core[0] if direct else g))),
            (right, pl.BlockSpec((rows, width), lambda g, core: (0, 0))),
        ],
        quarters(rows, width, part // 2),
        "down_term",
        3.5,
    )


def join_term(middle, skip, right, core):
    rows, width = right.shape
    shares = lax.axis_size("narrow")
    part = width // shares
    half = width // 2
    if part != half:
        left = jnp.concatenate([middle, skip], axis=1).reshape(rows, shares, 2, 2, part // 2)
        left = lax.dynamic_index_in_dim(left, core[0], 2, keepdims=False)
        left = left.reshape(rows, 2, shares // 2, 2, part // 2).swapaxes(2, 3).reshape(rows, width)
        middle, skip = left[:, :half], left[:, half:]

    def body(core_ref, m_ref, s_ref, r_ref, *outs):
        for owner, left_ref in enumerate((m_ref, s_ref)):
            value = dot(left_ref[...], r_ref[...], (0, 0)).astype(low)
            outs[2 * owner][...] = value[: half // 2]
            outs[2 * owner + 1][...] = value[half // 2 :]

    side = pl.BlockSpec((rows, half), lambda g, core: (0, core[0] if part == half else 0))
    return picked(
        body,
        core,
        (1,),
        [(middle, side), (skip, side), (right, pl.BlockSpec((rows, width), lambda g, core: (0, 0)))],
        quarters(rows, width, part // 2),
        "join_term",
        2,
    )


def cross(bit, *pieces):
    kept, got = pieces[: len(pieces) // 2], pieces[len(pieces) // 2 :]
    rows, columns = kept[0].shape
    blocks = len(kept) // 2
    steps = 2 if rows % 32 == 0 else 1

    def body(bit_ref, *refs):
        sent_ref, left_ref = refs[-2:]

        def put(target, owner):
            for block in range(blocks):
                place = owner * blocks + block
                one, two = refs[place], refs[2 * blocks + place]
                target[block] = (one[...].astype(full) + two[...].astype(full)).astype(low)

        for mine in range(2):

            @pl.when(bit_ref[0] == mine)
            def _():
                put(sent_ref, 1 - mine)
                put(left_ref, mine)

    ins = [(piece, pl.BlockSpec((rows // steps, columns), lambda g, bit: (g, 0))) for piece in kept + got]
    out = ((blocks, rows, columns), low, pl.BlockSpec((blocks, rows // steps, columns), lambda g, bit: (0, g, 0)))
    return picked(body, bit, (steps,), ins, [out, out], "cross", 2)


def add_halve(bit, *pairs):
    lead, columns = pairs[0].shape[0], pairs[0].shape[-1]
    sizes = [pair.shape[2] for pair in pairs[::2]]
    total = sum(sizes)
    steps = 2 if len(sizes) == 1 and total % 32 == 0 and total >= 256 else 1

    def body(bit_ref, *refs):
        mine = bit_ref[0]
        for target, place in ((refs[-2], 1 - mine), (refs[-1], mine)):
            begin = 0
            for kept_ref, got_ref in zip(refs[:-2:2], refs[1:-2:2]):
                length = kept_ref.shape[2]
                for each in range(lead):
                    value = kept_ref[each, place].astype(full) + got_ref[each, place].astype(full)
                    target[each, begin : begin + length] = value.astype(low)
                begin += length

    ins = [
        (pair, pl.BlockSpec((lead, 2, pair.shape[2] // steps, columns), lambda g, bit: (0, 0, g, 0)))
        for pair in pairs
    ]
    out = (
        (lead, total, columns),
        low,
        pl.BlockSpec((lead, total // steps, columns), lambda g, bit: (0, g, 0)),
    )
    return picked(body, bit, (steps,), ins, [out, out], "add_halve", 2)


def add_into(target, place, count, one, two):
    rows, columns = one.shape[-2:]
    steps = 2 if rows % 32 == 0 else 1
    block = pl.BlockSpec((1, rows // steps, columns), lambda g: (0, g, 0))

    def body(one_ref, two_ref, *rest):
        rest[-1][...] = (one_ref[...].astype(full) + two_ref[...].astype(full)).astype(low)

    ins = [one.reshape(1, rows, columns), two.reshape(1, rows, columns)]
    return pl.pallas_call(
        body,
        grid=(steps,),
        in_specs=[block, block] + ([] if target is None else [ANY]),
        out_specs=pl.BlockSpec((1, rows // steps, columns), lambda g: (place, g, 0)),
        out_shape=jax.ShapeDtypeStruct((count, rows, columns), low),
        name="add_into",
        input_output_aliases={} if target is None else {2: 0},
        cost_estimate=cost(1.3),
    )(*ins, *([] if target is None else [target]))


def add(one, two):
    return (one.astype(full) + two.astype(full)).astype(low)


def pair_up(own, got, bit):
    rows, columns = own.shape

    def body(bit_ref, own_ref, got_ref, out_ref):
        mine = bit_ref[0]
        out_ref[mine] = own_ref[...]
        out_ref[1 - mine] = got_ref[...]

    flat = pl.BlockSpec((rows, columns), lambda g, bit: (0, 0))
    out = ((2, rows, columns), low, pl.BlockSpec((2, rows, columns), lambda g, bit: (0, 0, 0)))
    return picked(body, bit, (1,), [(own, flat), (got, flat)], [out], "pair_up", 1)[0]


def finish(kind, half, own, got, begin, length, core, layer, targets):
    pieces, _, columns = own.shape
    scale = 1.0 / lax.axis_size("wide")
    aliases = {place + 2: place for place in range(len(targets))}
    source = pl.BlockSpec((pieces, length, columns), lambda g, core: (0, begin // length, 0))
    ins = [(own, source), (got, source)] + [(target, ANY) for target in targets]
    rows = pieces * length

    def chosen(core_ref, which, own_ref, got_ref, place=None):
        sides = [own_ref, got_ref]
        if place is None:
            values = [side[...].reshape(pieces * length, columns) for side in sides]
        else:
            if pieces == 1:
                near = (0, pl.ds(place * (length // 2), length // 2))
            else:
                near = (pl.ds(place * (pieces // 2), pieces // 2),)
            values = [side[near].reshape(pieces * length // 2, columns) for side in sides]
        return jnp.where(core_ref[0] == which, values[0], values[1]).astype(full) * scale

    if kind in ("down", "join"):

        def body(core_ref, own_ref, got_ref, *rest):
            rest[-1][0] = chosen(core_ref, pl.program_id(0), own_ref, got_ref)

        place = layer if kind == "down" else 0
        shape = (2 if kind == "down" else 1, 2 * rows, columns)
        out = (shape, full, pl.BlockSpec((1, rows, columns), lambda g, core: (place, g, 0)))
        return picked(body, core, (2,), ins, [out], "finish_rows", 3, aliases)
    steps = 4 if half is None else 2
    rows = rows // 2 if half is None else rows

    def block(step):
        return step if half is None else 2 * step + half

    def values_of(core_ref, own_ref, got_ref):
        step = pl.program_id(0)
        if half is None:
            return chosen(core_ref, step // 2, own_ref, got_ref, step % 2)
        return chosen(core_ref, step, own_ref, got_ref)

    def body(core_ref, own_ref, got_ref, *rest):
        values = values_of(core_ref, own_ref, got_ref)
        if kind == "up":
            rest[-1][0] = values
            return
        if half == 0:
            rest[-1][0] = values
            return
        last = block(pl.program_id(0)) == 3

        @pl.when(jnp.logical_not(last))
        def _():
            rest[-2][0] = values

        @pl.when(last)
        def _():
            rest[-1][0] = values

    if kind == "up":
        outs = [((2, rows, 4 * columns), full, pl.BlockSpec((1, rows, columns), lambda g, core: (layer, 0, block(g))))]
        return picked(body, core, (steps,), ins, outs, "finish_columns", 3, aliases)

    def spot(step):
        return block(step if half == 0 else jnp.minimum(step, steps - 2))

    outs = [
        ((2, rows, 3 * columns), full, pl.BlockSpec((1, rows, columns), lambda g, core: (layer, 0, spot(g)))),
        ((2, rows, columns), full, pl.BlockSpec((1, rows, columns), lambda g, core: (layer, 0, 0))),
    ]
    if half == 0:
        kept = targets[1:]
        ins, outs, aliases = ins[:3] if targets else ins, outs[:1], {2: 0} if targets else {}
        return (picked(body, core, (steps,), ins, outs, "finish_qkv", 3, aliases)[0], *kept)
    return picked(body, core, (steps,), ins, outs, "finish_qkv_out", 3, aliases)


def small_gradients(total, me, width, shares, blocks):
    part = width // shares
    scale = 1.0 / lax.axis_size("wide")

    def body(me_ref, total_ref, gains_ref, shifts_ref, out_ref, up_ref, down_ref, join_ref):
        values = total_ref[...] * scale
        back = [values[0:8], values[8:16]]
        ahead = [values[16 : 20 + blocks], values[20 + blocks : 24 + 2 * blocks]]
        for place in range(shares):

            @pl.when(me_ref[0] == place)
            def _():
                columns = slice(place * part, place * part + part)
                for layer in range(2):
                    for row, target in ((0, gains_ref), (1, shifts_ref)):
                        target[layer, 0:1] = back[layer][row : row + 1, columns]
                        target[layer, 1:2] = ahead[layer][row + 1 : row + 2, columns]
                    out_ref[layer : layer + 1] = ahead[layer][3:4, columns]
                    down_ref[layer : layer + 1] = ahead[layer][0:1, columns]
                    begin = place * part * blocks
                    while begin < (place + 1) * part * blocks:
                        row, column = begin // width, begin % width
                        length = min(width - column, (place + 1) * part * blocks - begin)
                        at = begin - place * part * blocks
                        piece = ahead[layer][4 + row : 5 + row, column : column + length]
                        up_ref[layer : layer + 1, at : at + length] = piece
                        begin += length
                join_ref[...] = back[1][2:3, columns]

    shapes = [(2, 2, part), (2, 2, part), (2, part), (2, part * blocks), (2, part), (1, part)]
    outs = [(shape, full, pl.BlockSpec(shape, lambda g, me, n=len(shape): (0,) * n)) for shape in shapes]
    ins = [(total, pl.BlockSpec(total.shape, lambda g, me: (0, 0)))]
    return picked(body, me, (1,), ins, outs, "small_gradients", 1)


def after(value, *earlier):
    return lax.optimization_barrier((value,) + earlier)[0] if earlier else value


def swap(values, axis, mask):
    size = lax.axis_size(axis)
    return lax.ppermute(values, axis, [(source, source ^ mask) for source in range(size)])


def masks(axis):
    return [1 << bit for bit in range(lax.axis_size(axis).bit_length() - 1)]


class Order:
    def __init__(self):
        self.last = ()

    def run(self, function, *arrays):
        held = lax.optimization_barrier(tuple(arrays) + self.last)[: len(arrays)]
        out = function(*held)
        self.last = (jax.tree.leaves(out)[0],)
        return out

    def mark(self, value):
        return self.run(lambda x: x + 1, value)

    def hold(self, *arrays):
        self.last += arrays


def place_bit(axis, mask):
    return ((lax.axis_index(axis) & mask) // mask).astype(jnp.int32).reshape(1)


class Term:
    def __init__(self, order, kind, layer, function, *arrays):
        self.order, self.kind, self.layer, self.half = order, kind, layer, None
        self.core = place_bit("wide", 1)
        sent = order.run(lambda *x: function(*x, 1 - self.core), *arrays)
        self.got = [swap(each, "wide", 1) for each in sent]
        self.columns = sent[0].shape[-1]
        self.keep = lambda: order.run(lambda *x: function(*x, self.core), *arrays)

    def stay(self):
        self.kept, self.keep = self.keep(), None

    def part(self, half):
        other = copy.copy(self)
        other.kept, other.got, other.half = self.kept[half::2], self.got[half::2], half
        return other

    def pass_narrow(self):
        stages = list(reversed(masks("narrow")))
        if isinstance(self.kept, (list, tuple)):
            bit = place_bit("narrow", stages[0])
            blocks = len(self.kept) // 2
            sent, self.kept = self.order.run(lambda *x: cross(bit, *x), *self.kept, *self.got)
            self.got = swap(sent, "narrow", stages.pop(0))
        else:
            blocks = 1
        for mask in stages:
            pairs = [(self.kept, self.got)]
            self.kept, self.got = halve(self.order, "narrow", mask, blocks, pairs, self.columns)

    def pass_first(self, mask):
        swapped = [self.kept[owner * 2 + block] for block in range(2) for owner in range(2)]
        brought = [self.got[owner * 2 + block] for block in range(2) for owner in range(2)]
        bit = place_bit("wide", mask)
        sent, self.kept = self.order.run(lambda *x: cross(bit, *x), *swapped, *brought)
        self.got = swap(sent, "wide", mask)

    def pass_wide(self, mask):
        pairs = list(zip(self.kept, self.got)) if isinstance(self.kept, (list, tuple)) else [(self.kept, self.got)]
        self.kept, self.got = halve(self.order, "wide", mask, 1, pairs, self.columns)

    def add_into(self, target, place, count):
        kept, got = [side.reshape(-1, self.columns) for side in (self.kept, self.got)]
        if target is None:
            return self.order.run(lambda one, two: add_into(None, place, count, one, two), kept, got)
        return self.order.run(lambda target, one, two: add_into(target, place, count, one, two), target, kept, got)

    def finish(self, done, own, got, begin, length):
        targets = done.get(self.kind, ())

        def last(own, got, core, *targets):
            return finish(self.kind, self.half, own, got, begin, length, core, self.layer, targets)

        done[self.kind] = self.order.run(last, own, got, self.core, *targets)


def halve(order, axis, mask, lead, pairs, columns):
    shaped = [array.reshape(lead, 2, -1, columns) for pair in pairs for array in pair]
    bit = place_bit(axis, mask)
    sent, kept = order.run(lambda *x: add_halve(bit, *x), *shaped)
    return kept, swap(sent, axis, mask)


class Reduce:
    def __init__(self, order, terms, passed=(), late=()):
        self.order, self.terms = order, terms
        rest = [mask for mask in masks("wide")[1:] if mask not in passed]
        self.down = [mask for mask in rest if mask not in late] + [mask for mask in rest if mask in late]
        self.up = list(reversed(passed))
        self.pieces, self.columns = 2 ** len(passed), terms[0].columns
        self.parts = [(term.kept, term.got) for term in terms]
        self.lengths, self.first = [each.size // self.columns for each, _ in self.parts], True
        self.joining, self.closed = None, False

    def step(self):
        if self.closed:
            return
        if self.down:
            mask = self.down.pop(0)
            rows = [kept.size // self.columns for kept, _ in self.parts]
            even = all(each % 32 == 0 for each in rows) and bool(self.down)
            if self.first and even:
                self.pieces, self.lengths = 2 * self.pieces, [each // 2 for each in rows]
            self.first = False
            if even:
                self.up.insert(0, mask)
                self.parts = [halve(self.order, "wide", mask, 1, self.parts, self.columns)]
            else:
                flat = [[side.reshape(-1, self.columns) for side in pair] for pair in self.parts]
                pair = [jnp.concatenate(sides) for sides in zip(*flat)]
                total = self.order.run(add, *pair)
                self.parts = [(total, swap(total, "wide", mask))]
            return
        kept, got = [array.reshape(-1, self.columns) for array in self.parts[0]]
        if self.joining is None:
            total = self.order.run(add, kept, got)
        else:
            bit = place_bit("wide", self.joining)
            total = self.order.run(lambda *x: pair_up(*x, bit), kept, got).reshape(-1, self.columns)
        if self.up:
            self.joining = self.up.pop(0)
            self.parts = [(total, swap(total, "wide", self.joining))]
        else:
            self.parts = [(total, swap(total, "wide", 1))]
            self.closed = True

    def finish(self, done):
        own, got = [array.reshape(self.pieces, -1, self.columns) for array in self.parts[0]]
        begin = 0
        for term, length in zip(self.terms, self.lengths):
            term.finish(done, own, got, begin, length)
            begin += length


def on_device(
    tokens,
    skip,
    flags,
    cotangent,
    norm_gains,
    norm_biases,
    qkv_weight,
    out_weight,
    out_bias,
    up_weight,
    up_bias,
    down_weight,
    down_bias,
    skip_weight,
    skip_bias,
):
    items, seq_rows, width = tokens.shape
    rows = items * seq_rows
    me = lax.axis_index("narrow")
    shares = lax.axis_size("narrow")
    spots = jnp.stack([me, lax.axis_index("wide")]).astype(jnp.int32)
    order = Order()

    def fetches(layer):
        return (
            Fetch([(qkv_weight, layer)], (1, 2)),
            Fetch([(out_weight, layer), (up_weight, layer)], (1, 2)),
            Fetch([(down_weight, layer)], (1, 4)),
        )

    fetch_qkv0, fetch_up0, fetch_down0 = fetches(0)
    fetch_qkv1, fetch_up1, fetch_down1 = fetches(1)
    fetch_join = Fetch([(skip_weight, None)], (1, 4))
    qkv0, qkv1 = [Weight(each, 0, width, spots) for each in (fetch_qkv0, fetch_qkv1)]
    out0, out1 = [Weight(each, 0, width, spots) for each in (fetch_up0, fetch_up1)]
    up0, up1 = [Weight(each, 1, width, spots) for each in (fetch_up0, fetch_up1)]
    down0, down1 = [Weight(each, 0, width, spots) for each in (fetch_down0, fetch_down1)]
    join = Weight(fetch_join, 0, width, spots)

    small = (norm_gains, norm_biases, out_bias, down_bias, skip_bias, up_bias)
    fetch_qkv0.cut()
    fetch_qkv0.fetch()
    held = order.run(pack_small, *[after(piece, fetch_qkv0.sent) for piece in small])[None]
    for mask in masks("narrow"):
        held = jnp.concatenate([held, swap(held, "narrow", mask)])
    last = order.last
    for each in (fetch_up0, fetch_down0, fetch_join, fetch_qkv1, fetch_up1, fetch_down1):
        each.cut(*last)
        last = (each.sent,)
    fetch_up0.fetch()
    fetch_down0.fetch(fetch_up0.sent)
    fetch_join.fetch(fetch_down0.sent)
    fetch_qkv1.fetch(fetch_join.sent)
    place = me.astype(jnp.int32).reshape(1)
    lines = order.run(lambda x: unpack_small(x, place, small, width), held)

    def line(row):
        return lines[row : row + 1]

    gains, shifts = [[line(2 * layer + each) for each in range(2)] for layer in range(2)], None
    shifts = [[line(4 + 2 * layer + each) for each in range(2)] for layer in range(2)]
    out_biases, down_biases, join_shift = [line(8), line(9)], [line(10), line(11)], line(12)
    blocks = up0.blocks
    up_biases = [lines[13 + layer * blocks : 13 + (layer + 1) * blocks].reshape(1, -1) for layer in range(2)]

    tokens_flat, skip_flat, cotangent_flat = [array.reshape(rows, width) for array in (tokens, skip, cotangent)]
    lengths = PATCHES + 1 + CAPTION * flags
    valid = lax.broadcasted_iota(jnp.int32, (items, seq_rows), 1) < lengths[:, None]
    dz1 = order.run(lambda x: jnp.where(valid.reshape(rows, 1), x, 0), after(cotangent_flat, fetch_down1.sent))

    fetch_qkv0.share(1)
    fetch_qkv0.share(0)
    order.hold(*fetch_up0.got())
    fetch_up0.share(1)
    a0, packed0 = order.run(lambda *x: project_qkv(*x, qkv0), tokens_flat, gains[0][0], shifts[0][0])
    order.hold(*fetch_down0.got())
    fetch_down0.share(1, a0)
    fetch_up1.fetch(a0)
    fetch_down1.fetch(a0)
    packed0 = packed0.reshape(3, items, seq_rows, width)
    mixed0, totals0 = order.run(lambda *x: attend(*x, items, seq_rows), packed0, lengths)
    order.hold(*fetch_join.got(), *fetch_qkv1.got())
    there = order.mark(spots)
    fetch_up0.share(0, there)
    fetch_down0.share(0, there)
    fetch_join.share(1, there)
    fetch_qkv1.share(1, there)
    mixed0 = mixed0.reshape(rows, width)
    m0, second0, hidden0, slope0, middle = order.run(
        lambda x, o, ob, g, s, ub, db: feed_forward(x, o, out0, ob, g, s, up0, ub, down0, db),
        tokens_flat, mixed0, out_biases[0], gains[0][1], shifts[0][1], up_biases[0], down_biases[0],
    )
    fetch_join.share(0, middle)
    fetch_qkv1.share(0, middle)
    order.hold(*fetch_up1.got(), *fetch_down1.got())
    fetch_up1.share(1, middle)
    fetch_down1.share(1, middle)
    entry, a1, packed1 = order.run(
        lambda m, s, jb, g, sh: join_qkv(m, s, join, jb, g, sh, qkv1),
        middle, skip_flat, join_shift, gains[1][0], shifts[1][0],
    )
    packed1 = packed1.reshape(3, items, seq_rows, width)
    mixed1, totals1 = order.run(lambda *x: attend(*x, items, seq_rows), packed1, lengths)
    fetch_up1.share(0, mixed1)
    fetch_down1.share(0, mixed1)
    mixed1 = mixed1.reshape(rows, width)
    m1, second1, hidden1, slope1, output = order.run(
        lambda x, o, ob, g, s, ub, db, k: feed_forward(x, o, out1, ob, g, s, up1, ub, down1, db, k),
        entry, mixed1, out_biases[1], gains[1][1], shifts[1][1], up_biases[1], down_biases[1], lengths,
    )

    done = {}
    term_down1 = Term(order, "down", 1, down_term, hidden1, dz1)
    term_down1.stay()
    term_down1.pass_narrow()
    du, dm, db, do, sums1 = order.run(
        lambda y, z, s, m, g: feed_forward_back(y, z, s, down1, up1, m, g, out1),
        dz1, dz1, slope1, m1, gains[1][1],
    )
    term_up1 = Term(order, "up", 1, up_term, second1, du)
    term_up1.stay()
    term_up1.pass_narrow()
    total = term_down1.add_into(None, 0, 3)
    dpacked = order.run(
        lambda *x: attend_back(*x, items, seq_rows), packed1, do.reshape(items, seq_rows, width), totals1, lengths
    )
    flat_packed = dpacked.reshape(3, rows, width)
    term_qkv1 = Term(order, "qkv", 1, qkv_out_term, a1, flat_packed, mixed1, db)
    term_qkv1.stay()
    term_qkv1.pass_narrow()
    total = term_up1.add_into(total, 1, 3)
    dentry, dmiddle, dz0, skip_grad, sums3 = order.run(
        lambda gp, x, g, dm: project_back(gp, qkv1, x, g, dm, join), flat_packed, entry, gains[1][0], dm
    )
    term_join = Term(order, "join", 1, join_term, middle, skip_flat, dentry)
    term_join.stay()
    term_join.pass_narrow()
    term_down0 = Term(order, "down", 0, down_term, hidden0, dz0)
    term_down0.stay()
    total = term_qkv1.add_into(total, 2, 3)
    size = lax.axis_size("wide")
    groups = [[device + core for device in range(0, size, 2)] for core in range(2)]
    flat_total = total.reshape(-1, width)
    part = lax.psum_scatter(flat_total, "wide", axis_index_groups=groups, scatter_dimension=0, tiled=True)
    term_down0.pass_first(2)

    du, dm, db, do, sums0 = order.run(
        lambda y, z, s, m, g: feed_forward_back(y, z, s, down0, up0, m, g, out0),
        dmiddle, dz0, slope0, m0, gains[0][1],
    )
    term_join.pass_wide(2)
    term_up0 = Term(order, "up", 0, up_term, second0, du)
    term_up0.stay()
    term_down0.pass_narrow()
    term_up0.pass_narrow()
    dpacked = order.run(
        lambda *x: attend_back(*x, items, seq_rows), packed0, do.reshape(items, seq_rows, width), totals0, lengths
    )
    order.hold(term_down0.got, term_join.got)
    flat_packed = dpacked.reshape(3, rows, width)
    term_qkv0 = Term(order, "qkv", 0, qkv_out_term, a0, flat_packed, mixed0, db)
    term_qkv0.stay()
    one, two = term_qkv0.part(0), term_qkv0.part(1)
    one.pass_narrow()
    two.pass_narrow()
    first = Reduce(order, [term_down0, term_join], (2,))
    first.step()
    second = Reduce(order, [term_up0])
    second.step()
    tokens_grad, sums2 = order.run(
        lambda gp, x, g, dm: project_back(gp, qkv0, x, g, dm), flat_packed, tokens_flat, gains[0][0], dm
    )
    minor = jnp.concatenate([sums2, sums3, sums0, sums1])
    places = masks("wide")
    minor_stages = [("narrow", mask) for mask in masks("narrow")]
    minor_stages += [("wide", mask) for mask in places if mask != 2] + [("wide", mask) for mask in places if mask == 2]
    minor_got = swap(minor, *minor_stages[0])

    def minor_step():
        nonlocal minor, minor_got
        if minor_stages:
            minor_stages.pop(0)
            minor = order.run(lambda one, two: one + two, minor, minor_got)
            if minor_stages:
                minor_got = swap(minor, *minor_stages[0])

    third = Reduce(order, [one])
    third.step()
    first.step()
    second.step()
    order.hold(part)
    gathered = lax.all_gather(after(part, *order.last), "wide", axis_index_groups=groups, tiled=True)
    fourth = Reduce(order, [two], late=(2,))
    fourth.step()
    minor_step()
    third.step()
    first.step()
    second.step()
    minor_step()
    fourth.step()
    minor_step()
    third.step()
    first.step()
    fourth.step()
    second.step()
    minor_step()
    first.step()
    third.step()
    fourth.step()
    order.hold(gathered)
    other = swap(after(gathered, *order.last), "wide", 1)
    first.finish(done)
    second.step()
    third.step()
    fourth.step()
    minor_step()
    own, got = gathered.reshape(1, -1, width), other.reshape(1, -1, width)
    for which, term in enumerate((term_down1, term_up1, term_qkv1)):
        term.finish(done, own, got, which * (own.shape[1] // 3), own.shape[1] // 3)
    fourth.step()
    second.step()
    third.step()
    for each in (first, second, third, fourth):
        while not each.closed:
            each.step()
    while minor_stages:
        minor_step()
    fourth.finish(done)
    second.finish(done)
    third.finish(done)
    small = order.run(lambda x: small_gradients(x, place, width, shares, up1.blocks), minor)

    return (
        output.reshape(tokens.shape),
        tokens_grad.reshape(tokens.shape),
        skip_grad.reshape(tokens.shape),
        small[0],
        small[1],
        done["qkv"][0],
        done["qkv"][1],
        small[2],
        done["up"][0],
        small[3],
        done["down"][0],
        small[4],
        done["join"][0][0],
        small[5].reshape(-1),
    )


def solution(mesh):
    placed = (
        P(("wide", "narrow"), None, None),
        P(("wide", "narrow"), None, None),
        P(("wide", "narrow")),
        P(("wide", "narrow"), None, None),
        P(None, None, "narrow"),
        P(None, None, "narrow"),
        P(None, "narrow", None),
        P(None, "narrow", None),
        P(None, "narrow"),
        P(None, "narrow", None),
        P(None, "narrow"),
        P(None, "narrow", None),
        P(None, "narrow"),
        P("narrow", None),
        P("narrow"),
    )
    return jax.shard_map(
        on_device,
        mesh=mesh,
        in_specs=placed,
        out_specs=(
            P(("wide", "narrow"), None, None),
            P(("wide", "narrow"), None, None),
            P(("wide", "narrow"), None, None),
            P(None, None, "narrow"),
            P(None, None, "narrow"),
            P(None, "narrow", None),
            P(None, "narrow", None),
            P(None, "narrow"),
            P(None, "narrow", None),
            P(None, "narrow"),
            P(None, "narrow", None),
            P(None, "narrow"),
            P("narrow", None),
            P("narrow"),
        ),
        check_vma=False,
    )
```

```python
import copy
import math

import jax
import jax.numpy as jnp
from jax import lax
from jax.experimental import pallas as pl
from jax.experimental.pallas import tpu as pltpu
from jax.sharding import PartitionSpec as P

HEAD_DIM = 64
PATCHES = 256
CAPTION = 77
PAIR = 2 * HEAD_DIM


epsilon = 1e-05
masked_score = -1e30
low = jnp.bfloat16
full = jnp.float32
SPARE = 14
ANY = pl.BlockSpec(memory_space=pltpu.HBM)
SCALARS = pl.BlockSpec(memory_space=pltpu.SMEM)


def dot(left, right, contract=(1, 0)):
    dims = (((contract[0],), (contract[1],)), ((), ()))
    return lax.dot_general(left, right, dims, preferred_element_type=full)


def normalize(values):
    centred = values - jnp.mean(values, axis=-1, keepdims=True)
    factor = lax.rsqrt(jnp.mean(centred * centred, axis=-1, keepdims=True) + epsilon)
    return centred * factor, factor


def normalize_back(upstream, normed, factor):
    return factor * (
        upstream
        - jnp.mean(upstream, axis=-1, keepdims=True)
        - normed * jnp.mean(upstream * normed, axis=-1, keepdims=True)
    )


def column_sum(values):
    return jnp.sum(values.astype(full), axis=0, keepdims=True)


def whole(shape):
    return pl.BlockSpec(shape, lambda *grid: (0,) * len(shape))


def cost(micros):
    return pl.CostEstimate(flops=int(micros * 3 * 10**8), bytes_accessed=0, transcendentals=0)


def room(ins, outs, scratch, spare):
    total = spare * 2**20
    for shape, kind, spec in [(array.shape, array.dtype, spec) for array, spec in ins] + list(outs):
        if spec.block_shape is not None and spec.memory_space is None:
            total += 2 * math.prod(spec.block_shape) * jnp.dtype(kind).itemsize
    for piece in scratch:
        if piece.memory_space == pltpu.VMEM:
            total += math.prod(piece.shape) * jnp.dtype(piece.dtype).itemsize
    return total


def call(body, grid, ins, outs, name, micros, scratch=(), spare=6):
    return pl.pallas_call(
        body,
        grid=grid,
        in_specs=[spec for _, spec in ins],
        out_specs=[spec for _, _, spec in outs],
        out_shape=[jax.ShapeDtypeStruct(shape, kind) for shape, kind, _ in outs],
        scratch_shapes=list(scratch),
        name=name,
        cost_estimate=cost(micros),
        compiler_params=pltpu.CompilerParams(vmem_limit_bytes=room(ins, outs, scratch, spare)),
    )(*[array for array, _ in ins])


class Fetch:
    def __init__(self, arrays, sharing):
        self.arrays, self.sharing = arrays, list(sharing)
        self.rows = arrays[0][0].shape[-2]
        while self.rows % (16 << len(self.sharing)):
            self.sharing.pop()
        self.length = self.rows >> len(self.sharing)

    def quarter(self, place):
        return sum(((place // mask) & 1) << bit for bit, mask in enumerate(self.sharing))

    def cut(self, *earlier):
        found = []
        for array, layer in self.arrays:
            array = after(array, *earlier)
            lead = () if layer is None else (layer,)
            begin = self.quarter(lax.axis_index("wide")) * self.length
            sizes = (1,) * len(lead) + (self.length, array.shape[-1])
            found.append(lax.dynamic_slice(array, lead + (begin, 0), sizes).reshape(self.length, -1))
        self.sent = (jnp.concatenate(found, axis=1) if len(found) > 1 else found[0])[None]

    def fetch(self, *earlier):
        held = after(self.sent, *earlier)
        for mask in masks("narrow"):
            held = jnp.concatenate([held, swap(held, "narrow", mask)])
        self.pieces = {0: held[1:]}

    def share(self, which, *earlier):
        if which < len(self.sharing):
            mask = self.sharing[which]
            got = {key ^ (1 << which): swap(after(piece, *earlier), "wide", mask) for key, piece in self.pieces.items()}
            self.pieces.update(got)

    def got(self):
        return list(self.pieces.values())


class Weight:
    def __init__(self, fetched, which, width, spots):
        self.fetched, self.spots, self.width = fetched, spots, width
        self.array, self.layer = fetched.arrays[which]
        self.begin = sum(array.shape[-1] for array, _ in fetched.arrays[:which])
        self.rows, columns = self.array.shape[-2:]
        self.shares = lax.axis_size("narrow")
        self.blocks = columns // width
        self.total = self.rows * self.shares

    def arrays(self):
        return [self.array] + self.fetched.got()

    def scratch(self):
        copies = 1 + len(self.fetched.pieces) * (self.shares - 1)
        return [pltpu.VMEM((self.blocks, self.total, self.width), low), pltpu.SemaphoreType.DMA((self.blocks, copies))]

    def copies(self, spots, refs, held, signals, block):
        own, pieces = refs[0], refs[1:]
        me, length = spots[0], self.fetched.length
        own = own if self.layer is None else own.at[self.layer]
        columns = pl.ds(block * self.width, self.width)
        begin = pl.multiple_of(me * self.rows, 16)
        found = [(own.at[:, columns], begin, self.rows)]
        columns = pl.ds(self.begin + block * self.width, self.width)
        for key, piece in zip(self.fetched.pieces, pieces):
            for offset in range(1, self.shares):
                begin = (me ^ offset) * self.rows + (self.fetched.quarter(spots[1]) ^ key) * length
                found.append((piece.at[offset - 1, :, columns], pl.multiple_of(begin, 16), length))
        return [
            pltpu.make_async_copy(source, held.at[block, pl.ds(begin, length)], signals.at[block, place])
            for place, (source, begin, length) in enumerate(found)
        ]

    def wait(self, *refs, block=0):
        for copy in self.copies(*refs, block):
            copy.wait()


def weighted(body, weights, grid, ins, outs, name, micros, scratch=(), first=((0, 0),), spare=SPARE):
    spots = weights[0].spots
    operands = [(spots, SCALARS)]
    for weight in weights:
        operands += [(pltpu.with_memory_space_constraint(array, pltpu.HBM), ANY) for array in weight.arrays()]
    counts = [len(weight.arrays()) for weight in weights]
    extra = [piece for weight in weights for piece in weight.scratch()]

    def wrapped(*refs):
        spots_ref, rest = refs[0], list(refs[1:])
        sources = []
        for count in counts:
            sources.append(rest[:count])
            rest = rest[count:]
        spare = rest[len(rest) - len(extra) :]
        rest = rest[: len(rest) - len(extra)]
        handles = []
        for place, weight in enumerate(weights):
            held, signals = spare[2 * place : 2 * place + 2]
            refs_of = (spots_ref, sources[place], held, signals)
            handles.append((weight, refs_of, held))

        everything = [(place, block) for place, weight in enumerate(weights) for block in range(weight.blocks)]

        def begin(wanted):
            for place, block in wanted:
                weight, refs_of, _ = handles[place]
                for copy in weight.copies(*refs_of, block):
                    copy.start()

        @pl.when(pl.program_id(0) == 0)
        def _():
            begin(first)

        def ready(place, block=0, then=False):
            weight, refs_of, held = handles[place]
            weight.wait(*refs_of, block=block)
            if then:
                begin([each for each in everything if each not in first])

        body(ready, [held for _, _, held in handles], *rest)

    return call(wrapped, grid, operands + ins, outs, name, micros, list(scratch) + extra, spare)


def pack_small(*small):
    part = small[0].shape[-1]
    counts = [piece.size // part for piece in small]

    def body(*refs):
        row = 0
        for ref in refs[:-1]:
            values = ref[...].reshape(-1, ref.shape[-1])
            for each in range(values.shape[0]):
                for begin in range(0, values.shape[1], part):
                    refs[-1][row : row + 1] = values[each : each + 1, begin : begin + part].astype(full)
                    row += 1
        refs[-1][row:] = jnp.zeros((refs[-1].shape[0] - row, part), full)

    flat = [piece.reshape((1,) * (2 - piece.ndim) + piece.shape) for piece in small]
    rows = -(-sum(counts) // 16) * 16
    out = ((rows, part), full, whole((rows, part)))
    return call(body, (1,), [(piece, whole(piece.shape)) for piece in flat], [out], "pack_small", 1)[0].astype(low)


def unpack_small(parts, me, small, width):
    shares, _, part = parts.shape
    lines = [(piece.size // piece.shape[-1], piece.shape[-1] // part) for piece in small]
    total = sum(count * many for count, many in lines)
    rows = -(-total // 8) * 8

    def body(me_ref, parts_ref, out_ref):
        values = parts_ref[...].astype(full)
        for mine in range(shares):

            @pl.when(me_ref[0] == mine)
            def _():
                for owner in range(shares):
                    source, target = 0, 0
                    for count, many in lines:
                        for each in range(count):
                            for piece in range(many):
                                at = owner * many * part + piece * part
                                row, column = target + at // width, at % width
                                line = values[owner ^ mine, source : source + 1]
                                out_ref[row : row + 1, column : column + part] = line
                                source += 1
                            target += many
        if rows > total:
            out_ref[total:] = jnp.zeros((rows - total, width), full)

    ins = [(parts, pl.BlockSpec(parts.shape, lambda g, me: (0, 0, 0)))]
    out = ((rows, width), full, pl.BlockSpec((rows, width), lambda g, me: (0, 0)))
    return picked(body, me, (1,), ins, [out], "unpack_small", 1)[0]


def project_qkv(inputs, gain, shift, weight):
    rows, width = inputs.shape

    def body(ready, held, x_ref, gain_ref, shift_ref, a_ref, out_ref):
        step = pl.program_id(0)

        @pl.when(step == 0)
        def _():
            normed, _ = normalize(x_ref[...].astype(full))
            a_ref[...] = (normed * gain_ref[...] + shift_ref[...]).astype(low)
            ready(0, 0, then=True)

        @pl.when(step > 0)
        def _():
            ready(0, step)

        scale = jnp.where(step == 0, HEAD_DIM ** (-0.5), 1.0)
        out_ref[0] = (dot(a_ref[...], held[0][step]).astype(low).astype(full) * scale).astype(low)

    return weighted(
        body,
        [weight],
        (3,),
        [
            (inputs, whole((rows, width))),
            (gain, whole((1, width))),
            (shift, whole((1, width))),
        ],
        [
            ((rows, width), low, whole((rows, width))),
            ((3, rows, width), low, pl.BlockSpec((1, rows, width), lambda j: (j, 0, 0))),
        ],
        "project_qkv",
        7,
    )


def join_qkv(middle, skip, join_weight, join_shift, gain, shift, weight):
    rows, width = middle.shape

    def body(ready, held, m_ref, s_ref, jb_ref, gain_ref, shift_ref, e_ref, a_ref, out_ref):
        step = pl.program_id(0)

        @pl.when(step == 0)
        def _():
            ready(0, then=True)
            entry = dot(m_ref[...], held[0][0, :width]) + dot(s_ref[...], held[0][0, width:]) + jb_ref[...]
            e_ref[...] = entry
            normed, _ = normalize(entry)
            a_ref[...] = (normed * gain_ref[...] + shift_ref[...]).astype(low)

        ready(1, step)
        scale = jnp.where(step == 0, HEAD_DIM ** (-0.5), 1.0)
        out_ref[0] = (dot(a_ref[...], held[1][step]).astype(low).astype(full) * scale).astype(low)

    return weighted(
        body,
        [join_weight, weight],
        (3,),
        [
            (middle, whole((rows, width))),
            (skip, whole((rows, width))),
            (join_shift, whole((1, width))),
            (gain, whole((1, width))),
            (shift, whole((1, width))),
        ],
        [
            ((rows, width), full, whole((rows, width))),
            ((rows, width), low, whole((rows, width))),
            ((3, rows, width), low, pl.BlockSpec((1, rows, width), lambda j: (j, 0, 0))),
        ],
        "join_qkv",
        11,
        first=((0, 0), (1, 0)),
    )


def head_masks(seq_rows):
    lane = lax.broadcasted_iota(jnp.int32, (seq_rows, PAIR), 1)
    return [lane < HEAD_DIM, lane >= HEAD_DIM]


def pairs_of(width):
    pairs = width // PAIR
    return pairs, max(group for group in (1, 2, 3) if pairs % group == 0)


def attend(packed, lengths, items, seq_rows):
    width = packed.shape[-1]
    pairs, group = pairs_of(width)

    def body(length_ref, q_ref, k_ref, v_ref, out_ref, total_ref):
        counts = lax.broadcasted_iota(jnp.int32, (seq_rows, seq_rows), 1) < length_ref[pl.program_id(0)]
        for pair in range(group):
            columns = slice(pair * PAIR, (pair + 1) * PAIR)
            queries, keys, values = q_ref[0, 0, :, columns], k_ref[0, 0, :, columns], v_ref[0, 0, :, columns]
            mixed = jnp.zeros((seq_rows, PAIR), full)
            for head, lanes in enumerate(head_masks(seq_rows)):
                scores = dot(jnp.where(lanes, queries, 0), keys, (1, 1))
                scores = jnp.where(counts, scores, masked_score)
                largest = jnp.max(scores, axis=1, keepdims=True)
                weights = jnp.exp(scores - largest)
                total = jnp.sum(weights, axis=1, keepdims=True)
                mixed += dot(weights.astype(low), jnp.where(lanes, values, 0)) * (1.0 / total)
                total_ref[0, pair, head : head + 1] = (largest + jnp.log(total)).T
            out_ref[0, :, columns] = mixed.astype(low)

    def block(which):
        return pl.BlockSpec((1, 1, seq_rows, group * PAIR), lambda n, h: (which, n, 0, h))

    return call(
        body,
        (items, pairs // group),
        [(lengths, SCALARS), (packed, block(0)), (packed, block(1)), (packed, block(2))],
        [
            (
                (items, seq_rows, width),
                low,
                pl.BlockSpec((1, seq_rows, group * PAIR), lambda n, h: (n, 0, h)),
            ),
            (
                (items, pairs, 8, seq_rows),
                full,
                pl.BlockSpec((1, group, 8, seq_rows), lambda n, h: (n, h, 0, 0)),
            ),
        ],
        "attend",
        10,
        spare=14,
    )


def attend_back(packed, grad_mixed, totals, lengths, items, seq_rows):
    width = packed.shape[-1]
    pairs, group = pairs_of(width)
    sides = [slice(0, PATCHES), slice(PATCHES, seq_rows)]

    def body(length_ref, q_ref, k_ref, v_ref, g_ref, total_ref, out_ref):
        row = PATCHES + lax.broadcasted_iota(jnp.int32, (seq_rows - PATCHES, seq_rows), 0)
        counts = row < length_ref[pl.program_id(0)]
        for pair in range(group):
            columns = slice(pair * PAIR, (pair + 1) * PAIR)
            queries, keys, values = q_ref[0, 0, :, columns], k_ref[0, 0, :, columns], v_ref[0, 0, :, columns]
            upstream = g_ref[0, :, columns]
            grad_queries = jnp.zeros((PAIR, seq_rows), full)
            grad_keys, grad_values = [0.0, 0.0], [0.0, 0.0]
            for head, lanes in enumerate(head_masks(seq_rows)):
                own_queries = jnp.where(lanes, queries, 0)
                own_upstream = jnp.where(lanes, upstream, 0)
                own_keys = jnp.where(lanes, keys, 0)
                parts, centre = [], 0.0
                for side, rows in enumerate(sides):
                    scores = dot(keys[rows], own_queries, (1, 1))
                    if side:
                        scores = jnp.where(counts, scores, masked_score)
                    probs = jnp.exp(scores - total_ref[0, pair, head : head + 1])
                    grad_probs = dot(values[rows], own_upstream, (1, 1))
                    centre += jnp.sum(grad_probs * probs, axis=0, keepdims=True)
                    parts.append((probs, grad_probs))
                for side, (probs, grad_probs) in enumerate(parts):
                    grad_scores = (probs * (grad_probs - centre)).astype(low)
                    grad_values[side] += dot(probs.astype(low), own_upstream)
                    grad_keys[side] += dot(grad_scores, own_queries)
                    grad_queries += dot(own_keys[sides[side]], grad_scores, (0, 0))
            out_ref[0, 0, :, columns] = (grad_queries.T * HEAD_DIM ** (-0.5)).astype(low)
            for side, rows in enumerate(sides):
                out_ref[1, 0, rows, columns] = grad_keys[side].astype(low)
                out_ref[2, 0, rows, columns] = grad_values[side].astype(low)

    def block(which):
        return pl.BlockSpec((1, 1, seq_rows, group * PAIR), lambda n, h: (which, n, 0, h))

    return call(
        body,
        (items, pairs // group),
        [
            (lengths, SCALARS),
            (packed, block(0)),
            (packed, block(1)),
            (packed, block(2)),
            (grad_mixed, pl.BlockSpec((1, seq_rows, group * PAIR), lambda n, h: (n, 0, h))),
            (totals, pl.BlockSpec((1, group, 8, seq_rows), lambda n, h: (n, h, 0, 0))),
        ],
        [
            (
                (3, items, seq_rows, width),
                low,
                pl.BlockSpec((3, 1, seq_rows, group * PAIR), lambda n, h: (0, n, 0, h)),
            ),
        ],
        "attend_back",
        15,
        spare=14,
    )[0]


def gelu_parts(before):
    decay = jnp.exp(before * before * -0.5)
    inverse = pl.reciprocal(1.0 + (0.3275911 * 0.5**0.5) * jnp.abs(before), approx=False)
    series = 1.061405429 * 0.5
    for term in (-1.453152027, 1.421413741, -0.284496736, 0.254829592):
        series = series * inverse + term * 0.5
    below = series * inverse * decay
    share = jnp.where(before >= 0, 1.0 - below, below)
    return before * share, share + before * decay * 0.3989422804014327


def feed_forward(inputs, mixed, out_weight, out_bias, gain, shift, up_weight, up_bias, down_weight, down_bias, lengths=None):
    rows, width = inputs.shape
    steps = up_weight.blocks
    hidden = steps * width

    def body(ready, held, x_ref, o_ref, ob_ref, gain_ref, shift_ref, ub_ref, db_ref, *rest):
        m_ref, a_ref, g_ref, s_ref, y_ref, total = rest[-6:]
        step = pl.program_id(0)

        @pl.when(step == 0)
        def _():
            ready(0, then=True)
            middle = x_ref[...].astype(full) + dot(o_ref[...], held[0][0]) + ob_ref[...]
            m_ref[...] = middle
            normed, _ = normalize(middle)
            a_ref[...] = (normed * gain_ref[...] + shift_ref[...]).astype(low)
            total[...] = middle + db_ref[...]

        ready(1, step)
        before = dot(a_ref[...], held[1][step]) + ub_ref[...]
        value, slope = gelu_parts(before)
        g_ref[...] = value.astype(low)
        s_ref[...] = slope.astype(low)

        @pl.when(step == 0)
        def _():
            ready(2)

        total[...] += dot(g_ref[...], held[2][0, pl.ds(pl.multiple_of(step * width, width), width)])

        @pl.when(step == steps - 1)
        def _():
            if lengths is None:
                y_ref[...] = total[...].astype(low)
            else:
                length = rows // lengths.shape[0]
                row = lax.broadcasted_iota(jnp.int32, (length, width), 0)
                for item in range(lengths.shape[0]):
                    at = slice(item * length, (item + 1) * length)
                    y_ref[at] = jnp.where(row < rest[0][item], total[at], 0.0).astype(low)

    return weighted(
        body,
        [out_weight, up_weight, down_weight],
        (steps,),
        [
            (inputs, whole((rows, width))),
            (mixed, whole((rows, width))),
            (out_bias, whole((1, width))),
            (gain, whole((1, width))),
            (shift, whole((1, width))),
            (up_bias, pl.BlockSpec((1, width), lambda j: (0, j))),
            (down_bias, whole((1, width))),
        ]
        + ([] if lengths is None else [(lengths, SCALARS)]),
        [
            ((rows, width), full, whole((rows, width))),
            ((rows, width), low, whole((rows, width))),
            ((rows, hidden), low, pl.BlockSpec((rows, width), lambda j: (0, j))),
            ((rows, hidden), low, pl.BlockSpec((rows, width), lambda j: (0, j))),
            ((rows, width), low, whole((rows, width))),
        ],
        "feed_forward",
        23,
        scratch=[pltpu.VMEM((rows, width), full)],
        first=((0, 0), (1, 0)),
    )


def feed_forward_back(upstream, rounded, slope, down_weight, up_weight, middle, gain, out_weight):
    rows, width = upstream.shape
    steps = up_weight.blocks
    hidden = steps * width

    def body(ready, held, y_ref, dz_ref, s_ref, m_ref, gain_ref, du_ref, dm_ref, db_ref, do_ref, sums_ref, total):
        step = pl.program_id(0)

        @pl.when(step == 0)
        def _():
            sums_ref[0:1] = column_sum(dz_ref[...])
            total[...] = jnp.zeros_like(total)
            ready(0, then=True)

        down = held[0][0, pl.ds(pl.multiple_of(step * width, width), width)]
        grad = (dot(dz_ref[...], down, (1, 1)) * s_ref[...].astype(full)).astype(low)
        du_ref[...] = grad
        sums_ref[pl.ds(4 + step, 1)] = column_sum(grad)
        ready(1, step)
        total[...] += dot(grad, held[1][step], (1, 1))

        @pl.when(step == steps - 1)
        def _():
            grad_second = total[...]
            normed, factor = normalize(m_ref[...])
            sums_ref[1:2] = column_sum(grad_second * normed)
            sums_ref[2:3] = column_sum(grad_second)
            grad_middle = y_ref[...].astype(full) + normalize_back(grad_second * gain_ref[...], normed, factor)
            dm_ref[...] = grad_middle
            branch = grad_middle.astype(low)
            db_ref[...] = branch
            sums_ref[3:4] = column_sum(branch)
            ready(2)
            do_ref[...] = dot(branch, held[2][0], (1, 1)).astype(low)

    return weighted(
        body,
        [down_weight, up_weight, out_weight],
        (steps,),
        [
            (upstream, whole((rows, width))),
            (rounded, whole((rows, width))),
            (slope, pl.BlockSpec((rows, width), lambda j: (0, j))),
            (middle, whole((rows, width))),
            (gain, whole((1, width))),
        ],
        [
            ((rows, hidden), low, pl.BlockSpec((rows, width), lambda j: (0, j))),
            ((rows, width), full, whole((rows, width))),
            ((rows, width), low, whole((rows, width))),
            ((rows, width), low, whole((rows, width))),
            ((4 + steps, width), full, whole((4 + steps, width))),
        ],
        "feed_forward_back",
        21,
        scratch=[pltpu.VMEM((rows, width), full)],
        first=((0, 0), (1, 0)),
    )


def project_back(grad_packed, weight, inputs, gain, grad_middle, join_weight=None):
    rows, width = inputs.shape
    joined = join_weight is not None

    def body(ready, held, g_ref, x_ref, gain_ref, dm_ref, *rest):
        if joined:
            de_ref, dx_ref, dz_ref, skip_ref, sums_ref, total = rest
        else:
            dx_ref, sums_ref, total = rest
        step = pl.program_id(0)

        @pl.when(step == 0)
        def _():
            total[...] = jnp.zeros_like(total)
            ready(0, 0, then=True)

        @pl.when(step > 0)
        def _():
            ready(0, step)

        total[...] += dot(g_ref[0], held[0][step], (1, 1))

        @pl.when(step == 2)
        def _():
            grad_first = total[...]
            normed, factor = normalize(x_ref[...].astype(full))
            sums_ref[0:1] = column_sum(grad_first * normed)
            sums_ref[1:2] = column_sum(grad_first)
            grad = dm_ref[...] + normalize_back(grad_first * gain_ref[...], normed, factor)
            if joined:
                entry = grad.astype(low)
                de_ref[...] = entry
                sums_ref[2:3] = column_sum(entry)
                ready(1)
                grad = dot(entry, held[1][0, :width], (1, 1))
                dx_ref[...] = grad
                dz_ref[...] = grad.astype(low)
                skip_ref[...] = dot(entry, held[1][0, width:], (1, 1))
            else:
                dx_ref[...] = grad

    ins = [
        (grad_packed, pl.BlockSpec((1, rows, width), lambda j: (j, 0, 0))),
        (inputs, whole((rows, width))),
        (gain, whole((1, width))),
        (grad_middle, whole((rows, width))),
    ]
    outs = [((rows, width), full, whole((rows, width))), ((8, width), full, whole((8, width)))]
    if joined:
        rounded = ((rows, width), low, whole((rows, width)))
        outs = [rounded, outs[0], rounded, outs[0], outs[1]]
    return weighted(
        body,
        [weight] + ([join_weight] if joined else []),
        (3,),
        ins,
        outs,
        "project_back",
        13 if joined else 9,
        scratch=[pltpu.VMEM((rows, width), full)],
    )


def picked(body, which, grid, ins, outs, name, micros, aliases=None, spare=4):
    return pl.pallas_call(
        body,
        grid_spec=pltpu.PrefetchScalarGridSpec(
            num_scalar_prefetch=1,
            grid=grid,
            in_specs=[spec for _, spec in ins],
            out_specs=[spec for _, _, spec in outs],
        ),
        out_shape=[jax.ShapeDtypeStruct(shape, kind) for shape, kind, _ in outs],
        name=name,
        input_output_aliases={place + 1: out for place, out in (aliases or {}).items()},
        cost_estimate=cost(micros),
        compiler_params=pltpu.CompilerParams(vmem_limit_bytes=room(ins, outs, (), spare)),
    )(which, *[array for array, _ in ins])


def quarters(rows, width, narrow_rows):
    shape = (lax.axis_size("narrow") // 2 * narrow_rows, width)
    return [(shape, low, pl.BlockSpec(shape, lambda g, core: (0, 0)))] * 4


def up_term(left, right, core):
    rows, width = left.shape
    part = width // lax.axis_size("narrow")
    half = width // 2

    def body(core_ref, l_ref, r_ref, *outs):
        value = dot(l_ref[...], r_ref[...], (0, 0)).astype(low)
        for block in range(2):

            @pl.when(pl.program_id(0) == block)
            def _():
                outs[block][...] = value[:half]
                outs[2 + block][...] = value[half:]

    return picked(
        body,
        core,
        (2,),
        [
            (left, pl.BlockSpec((rows, width), lambda g, core: (0, 0))),
            (right, pl.BlockSpec((rows, width), lambda g, core: (0, core[0] * 2 + g))),
        ],
        quarters(rows, width, part),
        "up_term",
        3.5,
    )


def qkv_out_term(first, packed, mixed, branch, core):
    rows, width = first.shape
    part = width // lax.axis_size("narrow")
    half = width // 2

    def body(core_ref, l_ref, r_ref, o_ref, b_ref, *outs):
        step = pl.program_id(0)
        last = core_ref[0] * 2 + step == 3

        def put(block, value):
            outs[block][...] = value[:half]
            outs[2 + block][...] = value[half:]

        @pl.when(last)
        def _():
            put(1, dot(o_ref[...], b_ref[...], (0, 0)).astype(low))

        @pl.when(jnp.logical_not(last))
        def _():
            value = dot(l_ref[...], r_ref[0], (0, 0)).astype(low)
            for block in range(2):

                @pl.when(step == block)
                def _():
                    put(block, value)

    flat = pl.BlockSpec((rows, width), lambda g, core: (0, 0))
    return picked(
        body,
        core,
        (2,),
        [
            (first, flat),
            (packed, pl.BlockSpec((1, rows, width), lambda g, core: (jnp.minimum(core[0] * 2 + g, 2), 0, 0))),
            (mixed, flat),
            (branch, flat),
        ],
        quarters(rows, width, part),
        "qkv_out_term",
        3.5,
    )


def down_term(left, right, core):
    rows, width = right.shape
    shares = lax.axis_size("narrow")
    part = left.shape[1] // (2 * shares)
    direct = part == width
    if not direct:
        left = left.reshape(rows, shares, 2, 2, part // 2)
        left = lax.dynamic_index_in_dim(left, core[0], 2, keepdims=False)
        left = left.reshape(rows, 2, shares // 2, 2, part // 2).swapaxes(2, 3).reshape(rows, 2 * width)
    half = width // 2

    def body(core_ref, l_ref, r_ref, *outs):
        value = dot(l_ref[...], r_ref[...], (0, 0)).astype(low)
        for owner in range(2):

            @pl.when(pl.program_id(0) == owner)
            def _():
                outs[2 * owner][...] = value[:half]
                outs[2 * owner + 1][...] = value[half:]

    return picked(
        body,
        core,
        (2,),
        [
            (left, pl.BlockSpec((rows, width), lambda g, core: (0, g * 2 + core[0] if direct else g))),
            (right, pl.BlockSpec((rows, width), lambda g, core: (0, 0))),
        ],
        quarters(rows, width, part // 2),
        "down_term",
        3.5,
    )


def join_term(middle, skip, right, core):
    rows, width = right.shape
    shares = lax.axis_size("narrow")
    part = width // shares
    half = width // 2
    if part != half:
        left = jnp.concatenate([middle, skip], axis=1).reshape(rows, shares, 2, 2, part // 2)
        left = lax.dynamic_index_in_dim(left, core[0], 2, keepdims=False)
        left = left.reshape(rows, 2, shares // 2, 2, part // 2).swapaxes(2, 3).reshape(rows, width)
        middle, skip = left[:, :half], left[:, half:]

    def body(core_ref, m_ref, s_ref, r_ref, *outs):
        for owner, left_ref in enumerate((m_ref, s_ref)):
            value = dot(left_ref[...], r_ref[...], (0, 0)).astype(low)
            outs[2 * owner][...] = value[: half // 2]
            outs[2 * owner + 1][...] = value[half // 2 :]

    side = pl.BlockSpec((rows, half), lambda g, core: (0, core[0] if part == half else 0))
    return picked(
        body,
        core,
        (1,),
        [(middle, side), (skip, side), (right, pl.BlockSpec((rows, width), lambda g, core: (0, 0)))],
        quarters(rows, width, part // 2),
        "join_term",
        2,
    )


def cross(bit, *pieces):
    kept, got = pieces[: len(pieces) // 2], pieces[len(pieces) // 2 :]
    rows, columns = kept[0].shape
    blocks = len(kept) // 2
    steps = 2 if rows % 32 == 0 else 1

    def body(bit_ref, *refs):
        sent_ref, left_ref = refs[-2:]

        def put(target, owner):
            for block in range(blocks):
                place = owner * blocks + block
                one, two = refs[place], refs[2 * blocks + place]
                target[block] = (one[...].astype(full) + two[...].astype(full)).astype(low)

        for mine in range(2):

            @pl.when(bit_ref[0] == mine)
            def _():
                put(sent_ref, 1 - mine)
                put(left_ref, mine)

    ins = [(piece, pl.BlockSpec((rows // steps, columns), lambda g, bit: (g, 0))) for piece in kept + got]
    out = ((blocks, rows, columns), low, pl.BlockSpec((blocks, rows // steps, columns), lambda g, bit: (0, g, 0)))
    return picked(body, bit, (steps,), ins, [out, out], "cross", 2)


def add_halve(bit, *pairs):
    lead, columns = pairs[0].shape[0], pairs[0].shape[-1]
    sizes = [pair.shape[2] for pair in pairs[::2]]
    total = sum(sizes)
    steps = 2 if len(sizes) == 1 and total % 32 == 0 and total >= 256 else 1

    def body(bit_ref, *refs):
        mine = bit_ref[0]
        for target, place in ((refs[-2], 1 - mine), (refs[-1], mine)):
            begin = 0
            for kept_ref, got_ref in zip(refs[:-2:2], refs[1:-2:2]):
                length = kept_ref.shape[2]
                for each in range(lead):
                    value = kept_ref[each, place].astype(full) + got_ref[each, place].astype(full)
                    target[each, begin : begin + length] = value.astype(low)
                begin += length

    ins = [
        (pair, pl.BlockSpec((lead, 2, pair.shape[2] // steps, columns), lambda g, bit: (0, 0, g, 0)))
        for pair in pairs
    ]
    out = (
        (lead, total, columns),
        low,
        pl.BlockSpec((lead, total // steps, columns), lambda g, bit: (0, g, 0)),
    )
    return picked(body, bit, (steps,), ins, [out, out], "add_halve", 2)


def add_into(target, place, count, one, two):
    rows, columns = one.shape[-2:]
    steps = 2 if rows % 32 == 0 else 1
    block = pl.BlockSpec((1, rows // steps, columns), lambda g: (0, g, 0))

    def body(one_ref, two_ref, *rest):
        rest[-1][...] = (one_ref[...].astype(full) + two_ref[...].astype(full)).astype(low)

    ins = [one.reshape(1, rows, columns), two.reshape(1, rows, columns)]
    return pl.pallas_call(
        body,
        grid=(steps,),
        in_specs=[block, block] + ([] if target is None else [ANY]),
        out_specs=pl.BlockSpec((1, rows // steps, columns), lambda g: (place, g, 0)),
        out_shape=jax.ShapeDtypeStruct((count, rows, columns), low),
        name="add_into",
        input_output_aliases={} if target is None else {2: 0},
        cost_estimate=cost(1.3),
    )(*ins, *([] if target is None else [target]))


def add(one, two):
    return (one.astype(full) + two.astype(full)).astype(low)


def pair_up(own, got, bit):
    rows, columns = own.shape

    def body(bit_ref, own_ref, got_ref, out_ref):
        mine = bit_ref[0]
        out_ref[mine] = own_ref[...]
        out_ref[1 - mine] = got_ref[...]

    flat = pl.BlockSpec((rows, columns), lambda g, bit: (0, 0))
    out = ((2, rows, columns), low, pl.BlockSpec((2, rows, columns), lambda g, bit: (0, 0, 0)))
    return picked(body, bit, (1,), [(own, flat), (got, flat)], [out], "pair_up", 1)[0]


def finish(kind, half, own, got, begin, length, core, layer, targets):
    pieces, _, columns = own.shape
    scale = 1.0 / lax.axis_size("wide")
    aliases = {place + 2: place for place in range(len(targets))}
    source = pl.BlockSpec((pieces, length, columns), lambda g, core: (0, begin // length, 0))
    ins = [(own, source), (got, source)] + [(target, ANY) for target in targets]
    rows = pieces * length

    def chosen(core_ref, which, own_ref, got_ref, place=None):
        sides = [own_ref, got_ref]
        if place is None:
            values = [side[...].reshape(pieces * length, columns) for side in sides]
        else:
            if pieces == 1:
                near = (0, pl.ds(place * (length // 2), length // 2))
            else:
                near = (pl.ds(place * (pieces // 2), pieces // 2),)
            values = [side[near].reshape(pieces * length // 2, columns) for side in sides]
        return jnp.where(core_ref[0] == which, values[0], values[1]).astype(full) * scale

    if kind in ("down", "join"):

        def body(core_ref, own_ref, got_ref, *rest):
            rest[-1][0] = chosen(core_ref, pl.program_id(0), own_ref, got_ref)

        place = layer if kind == "down" else 0
        shape = (2 if kind == "down" else 1, 2 * rows, columns)
        out = (shape, full, pl.BlockSpec((1, rows, columns), lambda g, core: (place, g, 0)))
        return picked(body, core, (2,), ins, [out], "finish_rows", 3, aliases)
    steps = 4 if half is None else 2
    rows = rows // 2 if half is None else rows

    def block(step):
        return step if half is None else 2 * step + half

    def values_of(core_ref, own_ref, got_ref):
        step = pl.program_id(0)
        if half is None:
            return chosen(core_ref, step // 2, own_ref, got_ref, step % 2)
        return chosen(core_ref, step, own_ref, got_ref)

    def body(core_ref, own_ref, got_ref, *rest):
        values = values_of(core_ref, own_ref, got_ref)
        if kind == "up":
            rest[-1][0] = values
            return
        if half == 0:
            rest[-1][0] = values
            return
        last = block(pl.program_id(0)) == 3

        @pl.when(jnp.logical_not(last))
        def _():
            rest[-2][0] = values

        @pl.when(last)
        def _():
            rest[-1][0] = values

    if kind == "up":
        outs = [((2, rows, 4 * columns), full, pl.BlockSpec((1, rows, columns), lambda g, core: (layer, 0, block(g))))]
        return picked(body, core, (steps,), ins, outs, "finish_columns", 3, aliases)

    def spot(step):
        return block(step if half == 0 else jnp.minimum(step, steps - 2))

    outs = [
        ((2, rows, 3 * columns), full, pl.BlockSpec((1, rows, columns), lambda g, core: (layer, 0, spot(g)))),
        ((2, rows, columns), full, pl.BlockSpec((1, rows, columns), lambda g, core: (layer, 0, 0))),
    ]
    if half == 0:
        kept = targets[1:]
        ins, outs, aliases = ins[:3] if targets else ins, outs[:1], {2: 0} if targets else {}
        return (picked(body, core, (steps,), ins, outs, "finish_qkv", 3, aliases)[0], *kept)
    return picked(body, core, (steps,), ins, outs, "finish_qkv_out", 3, aliases)


def small_gradients(total, me, width, shares, blocks):
    part = width // shares
    scale = 1.0 / lax.axis_size("wide")

    def body(me_ref, total_ref, gains_ref, shifts_ref, out_ref, up_ref, down_ref, join_ref):
        values = total_ref[...] * scale
        back = [values[0:8], values[8:16]]
        ahead = [values[16 : 20 + blocks], values[20 + blocks : 24 + 2 * blocks]]
        for place in range(shares):

            @pl.when(me_ref[0] == place)
            def _():
                columns = slice(place * part, place * part + part)
                for layer in range(2):
                    for row, target in ((0, gains_ref), (1, shifts_ref)):
                        target[layer, 0:1] = back[layer][row : row + 1, columns]
                        target[layer, 1:2] = ahead[layer][row + 1 : row + 2, columns]
                    out_ref[layer : layer + 1] = ahead[layer][3:4, columns]
                    down_ref[layer : layer + 1] = ahead[layer][0:1, columns]
                    begin = place * part * blocks
                    while begin < (place + 1) * part * blocks:
                        row, column = begin // width, begin % width
                        length = min(width - column, (place + 1) * part * blocks - begin)
                        at = begin - place * part * blocks
                        piece = ahead[layer][4 + row : 5 + row, column : column + length]
                        up_ref[layer : layer + 1, at : at + length] = piece
                        begin += length
                join_ref[...] = back[1][2:3, columns]

    shapes = [(2, 2, part), (2, 2, part), (2, part), (2, part * blocks), (2, part), (1, part)]
    outs = [(shape, full, pl.BlockSpec(shape, lambda g, me, n=len(shape): (0,) * n)) for shape in shapes]
    ins = [(total, pl.BlockSpec(total.shape, lambda g, me: (0, 0)))]
    return picked(body, me, (1,), ins, outs, "small_gradients", 1)


def after(value, *earlier):
    return lax.optimization_barrier((value,) + earlier)[0] if earlier else value


def swap(values, axis, mask):
    size = lax.axis_size(axis)
    return lax.ppermute(values, axis, [(source, source ^ mask) for source in range(size)])


def masks(axis):
    return [1 << bit for bit in range(lax.axis_size(axis).bit_length() - 1)]


class Order:
    def __init__(self):
        self.last = ()

    def run(self, function, *arrays):
        held = lax.optimization_barrier(tuple(arrays) + self.last)[: len(arrays)]
        out = function(*held)
        self.last = (jax.tree.leaves(out)[0],)
        return out

    def mark(self, value):
        return self.run(lambda x: x + 1, value)

    def hold(self, *arrays):
        self.last += arrays


def place_bit(axis, mask):
    return ((lax.axis_index(axis) & mask) // mask).astype(jnp.int32).reshape(1)


class Spread:
    def __init__(self, order, total):
        self.order = order
        self.count, rows, self.columns = total.shape
        self.masks = list(reversed(masks("wide")[1:]))
        places = 1 << len(self.masks)
        ranks = [sum(((place >> bit) & 1) << (len(self.masks) - 1 - bit) for bit in range(len(self.masks))) for place in range(places)]
        groups = [[2 * rank + core for rank in ranks] for core in range(2)]
        self.length = rows // places
        part = lax.psum_scatter(total, "wide", axis_index_groups=groups, scatter_dimension=1, tiled=True)
        self.part = part.reshape(-1, self.columns)
        self.mask, self.closed = None, False

    def step(self):
        if self.mask is not None:
            bit = place_bit("wide", self.mask)
            self.part = self.order.run(lambda *x: pair_up(*x, bit), self.part, self.got).reshape(-1, self.columns)
        if self.masks:
            self.mask = self.masks.pop(0)
            self.got = swap(self.part, "wide", self.mask)
        else:
            self.got, self.closed = swap(self.part, "wide", 1), True

    def finish(self, done, terms):
        while not self.closed:
            self.step()
        own, got = [side.reshape(-1, self.count * self.length, self.columns) for side in (self.part, self.got)]
        if self.length % 16:
            pieces = own.shape[0]
            own, got = [
                side.reshape(pieces, self.count, -1, self.columns).swapaxes(0, 1).reshape(1, -1, self.columns)
                for side in (own, got)
            ]
            self.length *= pieces
        for which, term in enumerate(terms):
            term.finish(done, own, got, which * self.length, self.length)


class Term:
    def __init__(self, order, kind, layer, function, *arrays):
        self.order, self.kind, self.layer, self.half = order, kind, layer, None
        self.core = place_bit("wide", 1)
        sent = order.run(lambda *x: function(*x, 1 - self.core), *arrays)
        self.got = [swap(each, "wide", 1) for each in sent]
        self.columns = sent[0].shape[-1]
        self.keep = lambda: order.run(lambda *x: function(*x, self.core), *arrays)

    def stay(self):
        self.kept, self.keep = self.keep(), None

    def part(self, half):
        other = copy.copy(self)
        other.kept, other.got, other.half = self.kept[half::2], self.got[half::2], half
        return other

    def pass_narrow(self):
        stages = list(reversed(masks("narrow")))
        if isinstance(self.kept, (list, tuple)):
            bit = place_bit("narrow", stages[0])
            blocks = len(self.kept) // 2
            sent, self.kept = self.order.run(lambda *x: cross(bit, *x), *self.kept, *self.got)
            self.got = swap(sent, "narrow", stages.pop(0))
        else:
            blocks = 1
        for mask in stages:
            pairs = [(self.kept, self.got)]
            self.kept, self.got = halve(self.order, "narrow", mask, blocks, pairs, self.columns)

    def pass_first(self, mask):
        swapped = [self.kept[owner * 2 + block] for block in range(2) for owner in range(2)]
        brought = [self.got[owner * 2 + block] for block in range(2) for owner in range(2)]
        bit = place_bit("wide", mask)
        sent, self.kept = self.order.run(lambda *x: cross(bit, *x), *swapped, *brought)
        self.got = swap(sent, "wide", mask)

    def pass_wide(self, mask):
        pairs = list(zip(self.kept, self.got)) if isinstance(self.kept, (list, tuple)) else [(self.kept, self.got)]
        self.kept, self.got = halve(self.order, "wide", mask, 1, pairs, self.columns)

    def add_into(self, target, place, count):
        kept, got = [side.reshape(-1, self.columns) for side in (self.kept, self.got)]
        if target is None:
            return self.order.run(lambda one, two: add_into(None, place, count, one, two), kept, got)
        return self.order.run(lambda target, one, two: add_into(target, place, count, one, two), target, kept, got)

    def finish(self, done, own, got, begin, length):
        targets = done.get(self.kind, ())

        def last(own, got, core, *targets):
            return finish(self.kind, self.half, own, got, begin, length, core, self.layer, targets)

        done[self.kind] = self.order.run(last, own, got, self.core, *targets)


def halve(order, axis, mask, lead, pairs, columns):
    shaped = [array.reshape(lead, 2, -1, columns) for pair in pairs for array in pair]
    bit = place_bit(axis, mask)
    sent, kept = order.run(lambda *x: add_halve(bit, *x), *shaped)
    return kept, swap(sent, axis, mask)


class Reduce:
    def __init__(self, order, terms, passed=(), late=()):
        self.order, self.terms = order, terms
        rest = [mask for mask in masks("wide")[1:] if mask not in passed]
        self.down = [mask for mask in rest if mask not in late] + [mask for mask in rest if mask in late]
        self.up = list(reversed(passed))
        self.pieces, self.columns = 2 ** len(passed), terms[0].columns
        self.parts = [(term.kept, term.got) for term in terms]
        self.lengths, self.first = [each.size // self.columns for each, _ in self.parts], True
        self.joining, self.closed = None, False

    def step(self):
        if self.closed:
            return
        if self.down:
            mask = self.down.pop(0)
            rows = [kept.size // self.columns for kept, _ in self.parts]
            even = all(each % 32 == 0 for each in rows) and bool(self.down)
            if self.first and even:
                self.pieces, self.lengths = 2 * self.pieces, [each // 2 for each in rows]
            self.first = False
            if even:
                self.up.insert(0, mask)
                self.parts = [halve(self.order, "wide", mask, 1, self.parts, self.columns)]
            else:
                flat = [[side.reshape(-1, self.columns) for side in pair] for pair in self.parts]
                pair = [jnp.concatenate(sides) for sides in zip(*flat)]
                total = self.order.run(add, *pair)
                self.parts = [(total, swap(total, "wide", mask))]
            return
        kept, got = [array.reshape(-1, self.columns) for array in self.parts[0]]
        if self.joining is None:
            total = self.order.run(add, kept, got)
        else:
            bit = place_bit("wide", self.joining)
            total = self.order.run(lambda *x: pair_up(*x, bit), kept, got).reshape(-1, self.columns)
        if self.up:
            self.joining = self.up.pop(0)
            self.parts = [(total, swap(total, "wide", self.joining))]
        else:
            self.parts = [(total, swap(total, "wide", 1))]
            self.closed = True

    def finish(self, done):
        own, got = [array.reshape(self.pieces, -1, self.columns) for array in self.parts[0]]
        begin = 0
        for term, length in zip(self.terms, self.lengths):
            term.finish(done, own, got, begin, length)
            begin += length


def on_device(
    tokens,
    skip,
    flags,
    cotangent,
    norm_gains,
    norm_biases,
    qkv_weight,
    out_weight,
    out_bias,
    up_weight,
    up_bias,
    down_weight,
    down_bias,
    skip_weight,
    skip_bias,
):
    items, seq_rows, width = tokens.shape
    rows = items * seq_rows
    me = lax.axis_index("narrow")
    shares = lax.axis_size("narrow")
    spots = jnp.stack([me, lax.axis_index("wide")]).astype(jnp.int32)
    order = Order()

    def fetches(layer):
        return (
            Fetch([(qkv_weight, layer)], (1, 2)),
            Fetch([(out_weight, layer), (up_weight, layer)], (1, 2)),
            Fetch([(down_weight, layer)], (1, 4)),
        )

    fetch_qkv0, fetch_up0, fetch_down0 = fetches(0)
    fetch_qkv1, fetch_up1, fetch_down1 = fetches(1)
    fetch_join = Fetch([(skip_weight, None)], (1, 4))
    qkv0, qkv1 = [Weight(each, 0, width, spots) for each in (fetch_qkv0, fetch_qkv1)]
    out0, out1 = [Weight(each, 0, width, spots) for each in (fetch_up0, fetch_up1)]
    up0, up1 = [Weight(each, 1, width, spots) for each in (fetch_up0, fetch_up1)]
    down0, down1 = [Weight(each, 0, width, spots) for each in (fetch_down0, fetch_down1)]
    join = Weight(fetch_join, 0, width, spots)

    small = (norm_gains, norm_biases, out_bias, down_bias, skip_bias, up_bias)
    fetch_qkv0.cut()
    fetch_qkv0.fetch()
    held = order.run(pack_small, *[after(piece, fetch_qkv0.sent) for piece in small])[None]
    for mask in masks("narrow"):
        held = jnp.concatenate([held, swap(held, "narrow", mask)])
    last = order.last
    for each in (fetch_up0, fetch_down0, fetch_join, fetch_qkv1, fetch_up1, fetch_down1):
        each.cut(*last)
        last = (each.sent,)
    fetch_up0.fetch()
    fetch_down0.fetch(fetch_up0.sent)
    fetch_join.fetch(fetch_down0.sent)
    fetch_qkv1.fetch(fetch_join.sent)
    place = me.astype(jnp.int32).reshape(1)
    lines = order.run(lambda x: unpack_small(x, place, small, width), held)

    def line(row):
        return lines[row : row + 1]

    gains, shifts = [[line(2 * layer + each) for each in range(2)] for layer in range(2)], None
    shifts = [[line(4 + 2 * layer + each) for each in range(2)] for layer in range(2)]
    out_biases, down_biases, join_shift = [line(8), line(9)], [line(10), line(11)], line(12)
    blocks = up0.blocks
    up_biases = [lines[13 + layer * blocks : 13 + (layer + 1) * blocks].reshape(1, -1) for layer in range(2)]

    tokens_flat, skip_flat, cotangent_flat = [array.reshape(rows, width) for array in (tokens, skip, cotangent)]
    lengths = PATCHES + 1 + CAPTION * flags
    valid = lax.broadcasted_iota(jnp.int32, (items, seq_rows), 1) < lengths[:, None]
    dz1 = order.run(lambda x: jnp.where(valid.reshape(rows, 1), x, 0), after(cotangent_flat, fetch_down1.sent))

    fetch_qkv0.share(1)
    fetch_qkv0.share(0)
    order.hold(*fetch_up0.got())
    fetch_up0.share(1)
    a0, packed0 = order.run(lambda *x: project_qkv(*x, qkv0), tokens_flat, gains[0][0], shifts[0][0])
    order.hold(*fetch_down0.got())
    fetch_down0.share(1, a0)
    fetch_up1.fetch(a0)
    fetch_down1.fetch(a0)
    packed0 = packed0.reshape(3, items, seq_rows, width)
    mixed0, totals0 = order.run(lambda *x: attend(*x, items, seq_rows), packed0, lengths)
    order.hold(*fetch_join.got(), *fetch_qkv1.got())
    there = order.mark(spots)
    fetch_up0.share(0, there)
    fetch_down0.share(0, there)
    fetch_join.share(1, there)
    fetch_qkv1.share(1, there)
    mixed0 = mixed0.reshape(rows, width)
    m0, second0, hidden0, slope0, middle = order.run(
        lambda x, o, ob, g, s, ub, db: feed_forward(x, o, out0, ob, g, s, up0, ub, down0, db),
        tokens_flat, mixed0, out_biases[0], gains[0][1], shifts[0][1], up_biases[0], down_biases[0],
    )
    fetch_join.share(0, middle)
    fetch_qkv1.share(0, middle)
    order.hold(*fetch_up1.got(), *fetch_down1.got())
    fetch_up1.share(1, middle)
    fetch_down1.share(1, middle)
    entry, a1, packed1 = order.run(
        lambda m, s, jb, g, sh: join_qkv(m, s, join, jb, g, sh, qkv1),
        middle, skip_flat, join_shift, gains[1][0], shifts[1][0],
    )
    packed1 = packed1.reshape(3, items, seq_rows, width)
    mixed1, totals1 = order.run(lambda *x: attend(*x, items, seq_rows), packed1, lengths)
    fetch_up1.share(0, mixed1)
    fetch_down1.share(0, mixed1)
    mixed1 = mixed1.reshape(rows, width)
    m1, second1, hidden1, slope1, output = order.run(
        lambda x, o, ob, g, s, ub, db, k: feed_forward(x, o, out1, ob, g, s, up1, ub, down1, db, k),
        entry, mixed1, out_biases[1], gains[1][1], shifts[1][1], up_biases[1], down_biases[1], lengths,
    )

    done = {}
    term_down1 = Term(order, "down", 1, down_term, hidden1, dz1)
    term_down1.stay()
    term_down1.pass_narrow()
    du, dm, db, do, sums1 = order.run(
        lambda y, z, s, m, g: feed_forward_back(y, z, s, down1, up1, m, g, out1),
        dz1, dz1, slope1, m1, gains[1][1],
    )
    term_up1 = Term(order, "up", 1, up_term, second1, du)
    term_up1.stay()
    term_up1.pass_narrow()
    total = term_down1.add_into(None, 0, 3)
    dpacked = order.run(
        lambda *x: attend_back(*x, items, seq_rows), packed1, do.reshape(items, seq_rows, width), totals1, lengths
    )
    flat_packed = dpacked.reshape(3, rows, width)
    term_qkv1 = Term(order, "qkv", 1, qkv_out_term, a1, flat_packed, mixed1, db)
    term_qkv1.stay()
    term_qkv1.pass_narrow()
    total = term_up1.add_into(total, 1, 3)
    dentry, dmiddle, dz0, skip_grad, sums3 = order.run(
        lambda gp, x, g, dm: project_back(gp, qkv1, x, g, dm, join), flat_packed, entry, gains[1][0], dm
    )
    term_join = Term(order, "join", 1, join_term, middle, skip_flat, dentry)
    term_join.stay()
    term_join.pass_narrow()
    term_down0 = Term(order, "down", 0, down_term, hidden0, dz0)
    term_down0.stay()
    total = term_qkv1.add_into(total, 2, 3)
    spread = Spread(order, total)
    term_down0.pass_first(2)

    du, dm, db, do, sums0 = order.run(
        lambda y, z, s, m, g: feed_forward_back(y, z, s, down0, up0, m, g, out0),
        dmiddle, dz0, slope0, m0, gains[0][1],
    )
    term_join.pass_wide(2)
    term_up0 = Term(order, "up", 0, up_term, second0, du)
    term_up0.stay()
    term_down0.pass_narrow()
    term_up0.pass_narrow()
    dpacked = order.run(
        lambda *x: attend_back(*x, items, seq_rows), packed0, do.reshape(items, seq_rows, width), totals0, lengths
    )
    order.hold(term_down0.got, term_join.got)
    flat_packed = dpacked.reshape(3, rows, width)
    term_qkv0 = Term(order, "qkv", 0, qkv_out_term, a0, flat_packed, mixed0, db)
    term_qkv0.stay()
    one, two = term_qkv0.part(0), term_qkv0.part(1)
    one.pass_narrow()
    two.pass_narrow()
    first = Reduce(order, [term_down0, term_join], (2,))
    first.step()
    second = Reduce(order, [term_up0])
    second.step()
    tokens_grad, sums2 = order.run(
        lambda gp, x, g, dm: project_back(gp, qkv0, x, g, dm), flat_packed, tokens_flat, gains[0][0], dm
    )
    minor = jnp.concatenate([sums2, sums3, sums0, sums1])
    places = masks("wide")
    minor_stages = [("narrow", mask) for mask in masks("narrow")]
    minor_stages += [("wide", mask) for mask in places if mask != 2] + [("wide", mask) for mask in places if mask == 2]
    minor_got = swap(minor, *minor_stages[0])

    def minor_step():
        nonlocal minor, minor_got
        if minor_stages:
            minor_stages.pop(0)
            minor = order.run(lambda one, two: one + two, minor, minor_got)
            if minor_stages:
                minor_got = swap(minor, *minor_stages[0])

    third = Reduce(order, [one])
    third.step()
    first.step()
    second.step()
    spread.step()
    fourth = Reduce(order, [two])
    fourth.step()
    minor_step()
    third.step()
    first.step()
    second.step()
    spread.step()
    fourth.step()
    minor_step()
    third.step()
    first.step()
    minor_step()
    spread.step()
    fourth.step()
    second.step()
    minor_step()
    first.step()
    third.step()
    fourth.step()
    second.step()
    spread.step()
    first.finish(done)
    third.step()
    fourth.step()
    minor_step()
    second.step()
    spread.finish(done, (term_down1, term_up1, term_qkv1))
    third.step()
    fourth.step()
    for each in (first, second, third, fourth):
        while not each.closed:
            each.step()
    while minor_stages:
        minor_step()
    second.finish(done)
    third.finish(done)
    fourth.finish(done)
    small = order.run(lambda x: small_gradients(x, place, width, shares, up1.blocks), minor)

    return (
        output.reshape(tokens.shape),
        tokens_grad.reshape(tokens.shape),
        skip_grad.reshape(tokens.shape),
        small[0],
        small[1],
        done["qkv"][0],
        done["qkv"][1],
        small[2],
        done["up"][0],
        small[3],
        done["down"][0],
        small[4],
        done["join"][0][0],
        small[5].reshape(-1),
    )


def solution(mesh):
    placed = (
        P(("wide", "narrow"), None, None),
        P(("wide", "narrow"), None, None),
        P(("wide", "narrow")),
        P(("wide", "narrow"), None, None),
        P(None, None, "narrow"),
        P(None, None, "narrow"),
        P(None, "narrow", None),
        P(None, "narrow", None),
        P(None, "narrow"),
        P(None, "narrow", None),
        P(None, "narrow"),
        P(None, "narrow", None),
        P(None, "narrow"),
        P("narrow", None),
        P("narrow"),
    )
    return jax.shard_map(
        on_device,
        mesh=mesh,
        in_specs=placed,
        out_specs=(
            P(("wide", "narrow"), None, None),
            P(("wide", "narrow"), None, None),
            P(("wide", "narrow"), None, None),
            P(None, None, "narrow"),
            P(None, None, "narrow"),
            P(None, "narrow", None),
            P(None, "narrow", None),
            P(None, "narrow"),
            P(None, "narrow", None),
            P(None, "narrow"),
            P(None, "narrow", None),
            P(None, "narrow"),
            P("narrow", None),
            P("narrow"),
        ),
        check_vma=False,
    )
```

```python
import copy
import math

import jax
import jax.numpy as jnp
from jax import lax
from jax.experimental import pallas as pl
from jax.experimental.pallas import tpu as pltpu
from jax.sharding import PartitionSpec as P

HEAD_DIM = 64
PATCHES = 256
CAPTION = 77
PAIR = 2 * HEAD_DIM


epsilon = 1e-05
masked_score = -1e30
low = jnp.bfloat16
full = jnp.float32
SPARE = 14
ANY = pl.BlockSpec(memory_space=pltpu.HBM)
SCALARS = pl.BlockSpec(memory_space=pltpu.SMEM)


def dot(left, right, contract=(1, 0)):
    dims = (((contract[0],), (contract[1],)), ((), ()))
    return lax.dot_general(left, right, dims, preferred_element_type=full)


def normalize(values):
    centred = values - jnp.mean(values, axis=-1, keepdims=True)
    factor = lax.rsqrt(jnp.mean(centred * centred, axis=-1, keepdims=True) + epsilon)
    return centred * factor, factor


def normalize_back(upstream, normed, factor):
    return factor * (
        upstream
        - jnp.mean(upstream, axis=-1, keepdims=True)
        - normed * jnp.mean(upstream * normed, axis=-1, keepdims=True)
    )


def column_sum(values):
    return jnp.sum(values.astype(full), axis=0, keepdims=True)


def whole(shape):
    return pl.BlockSpec(shape, lambda *grid: (0,) * len(shape))


def cost(micros):
    return pl.CostEstimate(flops=int(micros * 3 * 10**8), bytes_accessed=0, transcendentals=0)


def room(ins, outs, scratch, spare):
    total = spare * 2**20
    for shape, kind, spec in [(array.shape, array.dtype, spec) for array, spec in ins] + list(outs):
        if spec.block_shape is not None and spec.memory_space is None:
            total += 2 * math.prod(spec.block_shape) * jnp.dtype(kind).itemsize
    for piece in scratch:
        if piece.memory_space == pltpu.VMEM:
            total += math.prod(piece.shape) * jnp.dtype(piece.dtype).itemsize
    return total


def call(body, grid, ins, outs, name, micros, scratch=(), spare=6):
    return pl.pallas_call(
        body,
        grid=grid,
        in_specs=[spec for _, spec in ins],
        out_specs=[spec for _, _, spec in outs],
        out_shape=[jax.ShapeDtypeStruct(shape, kind) for shape, kind, _ in outs],
        scratch_shapes=list(scratch),
        name=name,
        cost_estimate=cost(micros),
        compiler_params=pltpu.CompilerParams(vmem_limit_bytes=room(ins, outs, scratch, spare)),
    )(*[array for array, _ in ins])


class Fetch:
    def __init__(self, arrays, sharing):
        self.arrays, self.sharing = arrays, list(sharing)
        self.rows = arrays[0][0].shape[-2]
        while self.rows % (16 << len(self.sharing)):
            self.sharing.pop()
        self.length = self.rows >> len(self.sharing)

    def quarter(self, place):
        return sum(((place // mask) & 1) << bit for bit, mask in enumerate(self.sharing))

    def cut(self, *earlier):
        found = []
        for array, layer in self.arrays:
            array = after(array, *earlier)
            lead = () if layer is None else (layer,)
            begin = self.quarter(lax.axis_index("wide")) * self.length
            sizes = (1,) * len(lead) + (self.length, array.shape[-1])
            found.append(lax.dynamic_slice(array, lead + (begin, 0), sizes).reshape(self.length, -1))
        self.sent = (jnp.concatenate(found, axis=1) if len(found) > 1 else found[0])[None]

    def fetch(self, *earlier):
        held = after(self.sent, *earlier)
        for mask in masks("narrow"):
            held = jnp.concatenate([held, swap(held, "narrow", mask)])
        self.pieces = {0: held[1:]}

    def share(self, which, *earlier):
        if which < len(self.sharing):
            mask = self.sharing[which]
            got = {key ^ (1 << which): swap(after(piece, *earlier), "wide", mask) for key, piece in self.pieces.items()}
            self.pieces.update(got)

    def got(self):
        return list(self.pieces.values())


class Weight:
    def __init__(self, fetched, which, width, spots):
        self.fetched, self.spots, self.width = fetched, spots, width
        self.array, self.layer = fetched.arrays[which]
        self.begin = sum(array.shape[-1] for array, _ in fetched.arrays[:which])
        self.rows, columns = self.array.shape[-2:]
        self.shares = lax.axis_size("narrow")
        self.blocks = columns // width
        self.total = self.rows * self.shares

    def arrays(self):
        return [self.array] + self.fetched.got()

    def scratch(self):
        copies = 1 + len(self.fetched.pieces) * (self.shares - 1)
        return [pltpu.VMEM((self.blocks, self.total, self.width), low), pltpu.SemaphoreType.DMA((self.blocks, copies))]

    def copies(self, spots, refs, held, signals, block):
        own, pieces = refs[0], refs[1:]
        me, length = spots[0], self.fetched.length
        own = own if self.layer is None else own.at[self.layer]
        columns = pl.ds(block * self.width, self.width)
        begin = pl.multiple_of(me * self.rows, 16)
        found = [(own.at[:, columns], begin, self.rows)]
        columns = pl.ds(self.begin + block * self.width, self.width)
        for key, piece in zip(self.fetched.pieces, pieces):
            for offset in range(1, self.shares):
                begin = (me ^ offset) * self.rows + (self.fetched.quarter(spots[1]) ^ key) * length
                found.append((piece.at[offset - 1, :, columns], pl.multiple_of(begin, 16), length))
        return [
            pltpu.make_async_copy(source, held.at[block, pl.ds(begin, length)], signals.at[block, place])
            for place, (source, begin, length) in enumerate(found)
        ]

    def wait(self, *refs, block=0):
        for copy in self.copies(*refs, block):
            copy.wait()


def weighted(body, weights, grid, ins, outs, name, micros, scratch=(), first=((0, 0),), spare=SPARE):
    spots = weights[0].spots
    operands = [(spots, SCALARS)]
    for weight in weights:
        operands += [(pltpu.with_memory_space_constraint(array, pltpu.HBM), ANY) for array in weight.arrays()]
    counts = [len(weight.arrays()) for weight in weights]
    extra = [piece for weight in weights for piece in weight.scratch()]

    def wrapped(*refs):
        spots_ref, rest = refs[0], list(refs[1:])
        sources = []
        for count in counts:
            sources.append(rest[:count])
            rest = rest[count:]
        spare = rest[len(rest) - len(extra) :]
        rest = rest[: len(rest) - len(extra)]
        handles = []
        for place, weight in enumerate(weights):
            held, signals = spare[2 * place : 2 * place + 2]
            refs_of = (spots_ref, sources[place], held, signals)
            handles.append((weight, refs_of, held))

        everything = [(place, block) for place, weight in enumerate(weights) for block in range(weight.blocks)]

        def begin(wanted):
            for place, block in wanted:
                weight, refs_of, _ = handles[place]
                for copy in weight.copies(*refs_of, block):
                    copy.start()

        @pl.when(pl.program_id(0) == 0)
        def _():
            begin(first)

        def ready(place, block=0, then=False):
            weight, refs_of, held = handles[place]
            weight.wait(*refs_of, block=block)
            if then:
                begin([each for each in everything if each not in first])

        body(ready, [held for _, _, held in handles], *rest)

    return call(wrapped, grid, operands + ins, outs, name, micros, list(scratch) + extra, spare)


def pack_small(*small):
    part = small[0].shape[-1]
    counts = [piece.size // part for piece in small]

    def body(*refs):
        row = 0
        for ref in refs[:-1]:
            values = ref[...].reshape(-1, ref.shape[-1])
            for each in range(values.shape[0]):
                for begin in range(0, values.shape[1], part):
                    refs[-1][row : row + 1] = values[each : each + 1, begin : begin + part].astype(full)
                    row += 1
        refs[-1][row:] = jnp.zeros((refs[-1].shape[0] - row, part), full)

    flat = [piece.reshape((1,) * (2 - piece.ndim) + piece.shape) for piece in small]
    rows = -(-sum(counts) // 16) * 16
    out = ((rows, part), full, whole((rows, part)))
    return call(body, (1,), [(piece, whole(piece.shape)) for piece in flat], [out], "pack_small", 1)[0].astype(low)


def unpack_small(parts, me, small, width):
    shares, _, part = parts.shape
    lines = [(piece.size // piece.shape[-1], piece.shape[-1] // part) for piece in small]
    total = sum(count * many for count, many in lines)
    rows = -(-total // 8) * 8

    def body(me_ref, parts_ref, out_ref):
        values = parts_ref[...].astype(full)
        for mine in range(shares):

            @pl.when(me_ref[0] == mine)
            def _():
                for owner in range(shares):
                    source, target = 0, 0
                    for count, many in lines:
                        for each in range(count):
                            for piece in range(many):
                                at = owner * many * part + piece * part
                                row, column = target + at // width, at % width
                                line = values[owner ^ mine, source : source + 1]
                                out_ref[row : row + 1, column : column + part] = line
                                source += 1
                            target += many
        if rows > total:
            out_ref[total:] = jnp.zeros((rows - total, width), full)

    ins = [(parts, pl.BlockSpec(parts.shape, lambda g, me: (0, 0, 0)))]
    out = ((rows, width), full, pl.BlockSpec((rows, width), lambda g, me: (0, 0)))
    return picked(body, me, (1,), ins, [out], "unpack_small", 1)[0]


def project_qkv(inputs, gain, shift, weight):
    rows, width = inputs.shape

    def body(ready, held, x_ref, gain_ref, shift_ref, a_ref, out_ref):
        step = pl.program_id(0)

        @pl.when(step == 0)
        def _():
            normed, _ = normalize(x_ref[...].astype(full))
            a_ref[...] = (normed * gain_ref[...] + shift_ref[...]).astype(low)
            ready(0, 0, then=True)

        @pl.when(step > 0)
        def _():
            ready(0, step)

        scale = jnp.where(step == 0, HEAD_DIM ** (-0.5), 1.0)
        out_ref[0] = (dot(a_ref[...], held[0][step]).astype(low).astype(full) * scale).astype(low)

    return weighted(
        body,
        [weight],
        (3,),
        [
            (inputs, whole((rows, width))),
            (gain, whole((1, width))),
            (shift, whole((1, width))),
        ],
        [
            ((rows, width), low, whole((rows, width))),
            ((3, rows, width), low, pl.BlockSpec((1, rows, width), lambda j: (j, 0, 0))),
        ],
        "project_qkv",
        7,
    )


def join_qkv(middle, skip, join_weight, join_shift, gain, shift, weight):
    rows, width = middle.shape

    def body(ready, held, m_ref, s_ref, jb_ref, gain_ref, shift_ref, e_ref, a_ref, out_ref):
        step = pl.program_id(0)

        @pl.when(step == 0)
        def _():
            ready(0, then=True)
            entry = dot(m_ref[...], held[0][0, :width]) + dot(s_ref[...], held[0][0, width:]) + jb_ref[...]
            e_ref[...] = entry
            normed, _ = normalize(entry)
            a_ref[...] = (normed * gain_ref[...] + shift_ref[...]).astype(low)

        ready(1, step)
        scale = jnp.where(step == 0, HEAD_DIM ** (-0.5), 1.0)
        out_ref[0] = (dot(a_ref[...], held[1][step]).astype(low).astype(full) * scale).astype(low)

    return weighted(
        body,
        [join_weight, weight],
        (3,),
        [
            (middle, whole((rows, width))),
            (skip, whole((rows, width))),
            (join_shift, whole((1, width))),
            (gain, whole((1, width))),
            (shift, whole((1, width))),
        ],
        [
            ((rows, width), full, whole((rows, width))),
            ((rows, width), low, whole((rows, width))),
            ((3, rows, width), low, pl.BlockSpec((1, rows, width), lambda j: (j, 0, 0))),
        ],
        "join_qkv",
        11,
        first=((0, 0), (1, 0)),
    )


def head_masks(seq_rows):
    lane = lax.broadcasted_iota(jnp.int32, (seq_rows, PAIR), 1)
    return [lane < HEAD_DIM, lane >= HEAD_DIM]


def pairs_of(width):
    pairs = width // PAIR
    return pairs, max(group for group in (1, 2, 3) if pairs % group == 0)


def attend(packed, lengths, items, seq_rows):
    width = packed.shape[-1]
    pairs, group = pairs_of(width)

    def body(length_ref, q_ref, k_ref, v_ref, out_ref, total_ref):
        counts = lax.broadcasted_iota(jnp.int32, (seq_rows, seq_rows), 1) < length_ref[pl.program_id(0)]
        for pair in range(group):
            columns = slice(pair * PAIR, (pair + 1) * PAIR)
            queries, keys, values = q_ref[0, 0, :, columns], k_ref[0, 0, :, columns], v_ref[0, 0, :, columns]
            mixed = jnp.zeros((seq_rows, PAIR), full)
            for head, lanes in enumerate(head_masks(seq_rows)):
                scores = dot(jnp.where(lanes, queries, 0), keys, (1, 1))
                scores = jnp.where(counts, scores, masked_score)
                largest = jnp.max(scores, axis=1, keepdims=True)
                weights = jnp.exp(scores - largest)
                total = jnp.sum(weights, axis=1, keepdims=True)
                mixed += dot(weights.astype(low), jnp.where(lanes, values, 0)) * (1.0 / total)
                total_ref[0, pair, head : head + 1] = (largest + jnp.log(total)).T
            out_ref[0, :, columns] = mixed.astype(low)

    def block(which):
        return pl.BlockSpec((1, 1, seq_rows, group * PAIR), lambda n, h: (which, n, 0, h))

    return call(
        body,
        (items, pairs // group),
        [(lengths, SCALARS), (packed, block(0)), (packed, block(1)), (packed, block(2))],
        [
            (
                (items, seq_rows, width),
                low,
                pl.BlockSpec((1, seq_rows, group * PAIR), lambda n, h: (n, 0, h)),
            ),
            (
                (items, pairs, 8, seq_rows),
                full,
                pl.BlockSpec((1, group, 8, seq_rows), lambda n, h: (n, h, 0, 0)),
            ),
        ],
        "attend",
        10,
        spare=14,
    )


def attend_back(packed, grad_mixed, totals, lengths, items, seq_rows):
    width = packed.shape[-1]
    pairs, group = pairs_of(width)
    sides = [slice(0, PATCHES), slice(PATCHES, seq_rows)]

    def body(length_ref, q_ref, k_ref, v_ref, g_ref, total_ref, out_ref):
        row = PATCHES + lax.broadcasted_iota(jnp.int32, (seq_rows - PATCHES, seq_rows), 0)
        counts = row < length_ref[pl.program_id(0)]
        for pair in range(group):
            columns = slice(pair * PAIR, (pair + 1) * PAIR)
            queries, keys, values = q_ref[0, 0, :, columns], k_ref[0, 0, :, columns], v_ref[0, 0, :, columns]
            upstream = g_ref[0, :, columns]
            grad_queries = jnp.zeros((PAIR, seq_rows), full)
            grad_keys, grad_values = [0.0, 0.0], [0.0, 0.0]
            for head, lanes in enumerate(head_masks(seq_rows)):
                own_queries = jnp.where(lanes, queries, 0)
                own_upstream = jnp.where(lanes, upstream, 0)
                own_keys = jnp.where(lanes, keys, 0)
                parts, centre = [], 0.0
                for side, rows in enumerate(sides):
                    scores = dot(keys[rows], own_queries, (1, 1))
                    if side:
                        scores = jnp.where(counts, scores, masked_score)
                    probs = jnp.exp(scores - total_ref[0, pair, head : head + 1])
                    grad_probs = dot(values[rows], own_upstream, (1, 1))
                    centre += jnp.sum(grad_probs * probs, axis=0, keepdims=True)
                    parts.append((probs, grad_probs))
                for side, (probs, grad_probs) in enumerate(parts):
                    grad_scores = (probs * (grad_probs - centre)).astype(low)
                    grad_values[side] += dot(probs.astype(low), own_upstream)
                    grad_keys[side] += dot(grad_scores, own_queries)
                    grad_queries += dot(own_keys[sides[side]], grad_scores, (0, 0))
            out_ref[0, 0, :, columns] = (grad_queries.T * HEAD_DIM ** (-0.5)).astype(low)
            for side, rows in enumerate(sides):
                out_ref[1, 0, rows, columns] = grad_keys[side].astype(low)
                out_ref[2, 0, rows, columns] = grad_values[side].astype(low)

    def block(which):
        return pl.BlockSpec((1, 1, seq_rows, group * PAIR), lambda n, h: (which, n, 0, h))

    return call(
        body,
        (items, pairs // group),
        [
            (lengths, SCALARS),
            (packed, block(0)),
            (packed, block(1)),
            (packed, block(2)),
            (grad_mixed, pl.BlockSpec((1, seq_rows, group * PAIR), lambda n, h: (n, 0, h))),
            (totals, pl.BlockSpec((1, group, 8, seq_rows), lambda n, h: (n, h, 0, 0))),
        ],
        [
            (
                (3, items, seq_rows, width),
                low,
                pl.BlockSpec((3, 1, seq_rows, group * PAIR), lambda n, h: (0, n, 0, h)),
            ),
        ],
        "attend_back",
        15,
        spare=14,
    )[0]


def gelu_parts(before):
    decay = jnp.exp(before * before * -0.5)
    inverse = pl.reciprocal(1.0 + (0.3275911 * 0.5**0.5) * jnp.abs(before), approx=False)
    series = 1.061405429 * 0.5
    for term in (-1.453152027, 1.421413741, -0.284496736, 0.254829592):
        series = series * inverse + term * 0.5
    below = series * inverse * decay
    share = jnp.where(before >= 0, 1.0 - below, below)
    return before * share, share + before * decay * 0.3989422804014327


def feed_forward(inputs, mixed, out_weight, out_bias, gain, shift, up_weight, up_bias, down_weight, down_bias, lengths=None):
    rows, width = inputs.shape
    steps = up_weight.blocks
    hidden = steps * width

    def body(ready, held, x_ref, o_ref, ob_ref, gain_ref, shift_ref, ub_ref, db_ref, *rest):
        m_ref, a_ref, g_ref, s_ref, y_ref, total = rest[-6:]
        step = pl.program_id(0)

        @pl.when(step == 0)
        def _():
            ready(0, then=True)
            middle = x_ref[...].astype(full) + dot(o_ref[...], held[0][0]) + ob_ref[...]
            m_ref[...] = middle
            normed, _ = normalize(middle)
            a_ref[...] = (normed * gain_ref[...] + shift_ref[...]).astype(low)
            total[...] = middle + db_ref[...]

        ready(1, step)
        before = dot(a_ref[...], held[1][step]) + ub_ref[...]
        value, slope = gelu_parts(before)
        g_ref[...] = value.astype(low)
        s_ref[...] = slope.astype(low)

        @pl.when(step == 0)
        def _():
            ready(2)

        total[...] += dot(g_ref[...], held[2][0, pl.ds(pl.multiple_of(step * width, width), width)])

        @pl.when(step == steps - 1)
        def _():
            if lengths is None:
                y_ref[...] = total[...].astype(low)
            else:
                length = rows // lengths.shape[0]
                row = lax.broadcasted_iota(jnp.int32, (length, width), 0)
                for item in range(lengths.shape[0]):
                    at = slice(item * length, (item + 1) * length)
                    y_ref[at] = jnp.where(row < rest[0][item], total[at], 0.0).astype(low)

    return weighted(
        body,
        [out_weight, up_weight, down_weight],
        (steps,),
        [
            (inputs, whole((rows, width))),
            (mixed, whole((rows, width))),
            (out_bias, whole((1, width))),
            (gain, whole((1, width))),
            (shift, whole((1, width))),
            (up_bias, pl.BlockSpec((1, width), lambda j: (0, j))),
            (down_bias, whole((1, width))),
        ]
        + ([] if lengths is None else [(lengths, SCALARS)]),
        [
            ((rows, width), full, whole((rows, width))),
            ((rows, width), low, whole((rows, width))),
            ((rows, hidden), low, pl.BlockSpec((rows, width), lambda j: (0, j))),
            ((rows, hidden), low, pl.BlockSpec((rows, width), lambda j: (0, j))),
            ((rows, width), low, whole((rows, width))),
        ],
        "feed_forward",
        23,
        scratch=[pltpu.VMEM((rows, width), full)],
        first=((0, 0), (1, 0)),
    )


def feed_forward_back(upstream, rounded, slope, down_weight, up_weight, middle, gain, out_weight):
    rows, width = upstream.shape
    steps = up_weight.blocks
    hidden = steps * width

    def body(ready, held, y_ref, dz_ref, s_ref, m_ref, gain_ref, du_ref, dm_ref, db_ref, do_ref, sums_ref, total):
        step = pl.program_id(0)

        @pl.when(step == 0)
        def _():
            sums_ref[0:1] = column_sum(dz_ref[...])
            total[...] = jnp.zeros_like(total)
            ready(0, then=True)

        down = held[0][0, pl.ds(pl.multiple_of(step * width, width), width)]
        grad = (dot(dz_ref[...], down, (1, 1)) * s_ref[...].astype(full)).astype(low)
        du_ref[...] = grad
        sums_ref[pl.ds(4 + step, 1)] = column_sum(grad)
        ready(1, step)
        total[...] += dot(grad, held[1][step], (1, 1))

        @pl.when(step == steps - 1)
        def _():
            grad_second = total[...]
            normed, factor = normalize(m_ref[...])
            sums_ref[1:2] = column_sum(grad_second * normed)
            sums_ref[2:3] = column_sum(grad_second)
            grad_middle = y_ref[...].astype(full) + normalize_back(grad_second * gain_ref[...], normed, factor)
            dm_ref[...] = grad_middle
            branch = grad_middle.astype(low)
            db_ref[...] = branch
            sums_ref[3:4] = column_sum(branch)
            ready(2)
            do_ref[...] = dot(branch, held[2][0], (1, 1)).astype(low)

    return weighted(
        body,
        [down_weight, up_weight, out_weight],
        (steps,),
        [
            (upstream, whole((rows, width))),
            (rounded, whole((rows, width))),
            (slope, pl.BlockSpec((rows, width), lambda j: (0, j))),
            (middle, whole((rows, width))),
            (gain, whole((1, width))),
        ],
        [
            ((rows, hidden), low, pl.BlockSpec((rows, width), lambda j: (0, j))),
            ((rows, width), full, whole((rows, width))),
            ((rows, width), low, whole((rows, width))),
            ((rows, width), low, whole((rows, width))),
            ((4 + steps, width), full, whole((4 + steps, width))),
        ],
        "feed_forward_back",
        21,
        scratch=[pltpu.VMEM((rows, width), full)],
        first=((0, 0), (1, 0)),
    )


def project_back(grad_packed, weight, inputs, gain, grad_middle, join_weight=None):
    rows, width = inputs.shape
    joined = join_weight is not None

    def body(ready, held, g_ref, x_ref, gain_ref, dm_ref, *rest):
        if joined:
            de_ref, dx_ref, dz_ref, skip_ref, sums_ref, total = rest
        else:
            dx_ref, sums_ref, total = rest
        step = pl.program_id(0)

        @pl.when(step == 0)
        def _():
            total[...] = jnp.zeros_like(total)
            ready(0, 0, then=True)

        @pl.when(step > 0)
        def _():
            ready(0, step)

        total[...] += dot(g_ref[0], held[0][step], (1, 1))

        @pl.when(step == 2)
        def _():
            grad_first = total[...]
            normed, factor = normalize(x_ref[...].astype(full))
            sums_ref[0:1] = column_sum(grad_first * normed)
            sums_ref[1:2] = column_sum(grad_first)
            grad = dm_ref[...] + normalize_back(grad_first * gain_ref[...], normed, factor)
            if joined:
                entry = grad.astype(low)
                de_ref[...] = entry
                sums_ref[2:3] = column_sum(entry)
                ready(1)
                grad = dot(entry, held[1][0, :width], (1, 1))
                dx_ref[...] = grad
                dz_ref[...] = grad.astype(low)
                skip_ref[...] = dot(entry, held[1][0, width:], (1, 1))
            else:
                dx_ref[...] = grad

    ins = [
        (grad_packed, pl.BlockSpec((1, rows, width), lambda j: (j, 0, 0))),
        (inputs, whole((rows, width))),
        (gain, whole((1, width))),
        (grad_middle, whole((rows, width))),
    ]
    outs = [((rows, width), full, whole((rows, width))), ((8, width), full, whole((8, width)))]
    if joined:
        rounded = ((rows, width), low, whole((rows, width)))
        outs = [rounded, outs[0], rounded, outs[0], outs[1]]
    return weighted(
        body,
        [weight] + ([join_weight] if joined else []),
        (3,),
        ins,
        outs,
        "project_back",
        13 if joined else 9,
        scratch=[pltpu.VMEM((rows, width), full)],
    )


def picked(body, which, grid, ins, outs, name, micros, aliases=None, spare=4):
    return pl.pallas_call(
        body,
        grid_spec=pltpu.PrefetchScalarGridSpec(
            num_scalar_prefetch=1,
            grid=grid,
            in_specs=[spec for _, spec in ins],
            out_specs=[spec for _, _, spec in outs],
        ),
        out_shape=[jax.ShapeDtypeStruct(shape, kind) for shape, kind, _ in outs],
        name=name,
        input_output_aliases={place + 1: out for place, out in (aliases or {}).items()},
        cost_estimate=cost(micros),
        compiler_params=pltpu.CompilerParams(vmem_limit_bytes=room(ins, outs, (), spare)),
    )(which, *[array for array, _ in ins])


def quarters(rows, width, narrow_rows):
    shape = (lax.axis_size("narrow") // 2 * narrow_rows, width)
    return [(shape, low, pl.BlockSpec(shape, lambda g, core: (0, 0)))] * 4


def up_term(left, right, core):
    rows, width = left.shape
    part = width // lax.axis_size("narrow")
    half = width // 2

    def body(core_ref, l_ref, r_ref, *outs):
        value = dot(l_ref[...], r_ref[...], (0, 0)).astype(low)
        for block in range(2):

            @pl.when(pl.program_id(0) == block)
            def _():
                outs[block][...] = value[:half]
                outs[2 + block][...] = value[half:]

    return picked(
        body,
        core,
        (2,),
        [
            (left, pl.BlockSpec((rows, width), lambda g, core: (0, 0))),
            (right, pl.BlockSpec((rows, width), lambda g, core: (0, core[0] * 2 + g))),
        ],
        quarters(rows, width, part),
        "up_term",
        3.5,
    )


def qkv_out_term(first, packed, mixed, branch, core):
    rows, width = first.shape
    part = width // lax.axis_size("narrow")
    half = width // 2

    def body(core_ref, l_ref, r_ref, o_ref, b_ref, *outs):
        step = pl.program_id(0)
        last = core_ref[0] * 2 + step == 3

        def put(block, value):
            outs[block][...] = value[:half]
            outs[2 + block][...] = value[half:]

        @pl.when(last)
        def _():
            put(1, dot(o_ref[...], b_ref[...], (0, 0)).astype(low))

        @pl.when(jnp.logical_not(last))
        def _():
            value = dot(l_ref[...], r_ref[0], (0, 0)).astype(low)
            for block in range(2):

                @pl.when(step == block)
                def _():
                    put(block, value)

    flat = pl.BlockSpec((rows, width), lambda g, core: (0, 0))
    return picked(
        body,
        core,
        (2,),
        [
            (first, flat),
            (packed, pl.BlockSpec((1, rows, width), lambda g, core: (jnp.minimum(core[0] * 2 + g, 2), 0, 0))),
            (mixed, flat),
            (branch, flat),
        ],
        quarters(rows, width, part),
        "qkv_out_term",
        3.5,
    )


def down_term(left, right, core):
    rows, width = right.shape
    shares = lax.axis_size("narrow")
    part = left.shape[1] // (2 * shares)
    direct = part == width
    if not direct:
        left = left.reshape(rows, shares, 2, 2, part // 2)
        left = lax.dynamic_index_in_dim(left, core[0], 2, keepdims=False)
        left = left.reshape(rows, 2, shares // 2, 2, part // 2).swapaxes(2, 3).reshape(rows, 2 * width)
    half = width // 2

    def body(core_ref, l_ref, r_ref, *outs):
        value = dot(l_ref[...], r_ref[...], (0, 0)).astype(low)
        for owner in range(2):

            @pl.when(pl.program_id(0) == owner)
            def _():
                outs[2 * owner][...] = value[:half]
                outs[2 * owner + 1][...] = value[half:]

    return picked(
        body,
        core,
        (2,),
        [
            (left, pl.BlockSpec((rows, width), lambda g, core: (0, g * 2 + core[0] if direct else g))),
            (right, pl.BlockSpec((rows, width), lambda g, core: (0, 0))),
        ],
        quarters(rows, width, part // 2),
        "down_term",
        3.5,
    )


def join_term(middle, skip, right, core):
    rows, width = right.shape
    shares = lax.axis_size("narrow")
    part = width // shares
    half = width // 2
    if part != half:
        left = jnp.concatenate([middle, skip], axis=1).reshape(rows, shares, 2, 2, part // 2)
        left = lax.dynamic_index_in_dim(left, core[0], 2, keepdims=False)
        left = left.reshape(rows, 2, shares // 2, 2, part // 2).swapaxes(2, 3).reshape(rows, width)
        middle, skip = left[:, :half], left[:, half:]

    def body(core_ref, m_ref, s_ref, r_ref, *outs):
        for owner, left_ref in enumerate((m_ref, s_ref)):
            value = dot(left_ref[...], r_ref[...], (0, 0)).astype(low)
            outs[2 * owner][...] = value[: half // 2]
            outs[2 * owner + 1][...] = value[half // 2 :]

    side = pl.BlockSpec((rows, half), lambda g, core: (0, core[0] if part == half else 0))
    return picked(
        body,
        core,
        (1,),
        [(middle, side), (skip, side), (right, pl.BlockSpec((rows, width), lambda g, core: (0, 0)))],
        quarters(rows, width, part // 2),
        "join_term",
        2,
    )


def cross(bit, *pieces):
    kept, got = pieces[: len(pieces) // 2], pieces[len(pieces) // 2 :]
    rows, columns = kept[0].shape
    blocks = len(kept) // 2
    steps = 2 if rows % 32 == 0 else 1

    def body(bit_ref, *refs):
        sent_ref, left_ref = refs[-2:]

        def put(target, owner):
            for block in range(blocks):
                place = owner * blocks + block
                one, two = refs[place], refs[2 * blocks + place]
                target[block] = (one[...].astype(full) + two[...].astype(full)).astype(low)

        for mine in range(2):

            @pl.when(bit_ref[0] == mine)
            def _():
                put(sent_ref, 1 - mine)
                put(left_ref, mine)

    ins = [(piece, pl.BlockSpec((rows // steps, columns), lambda g, bit: (g, 0))) for piece in kept + got]
    out = ((blocks, rows, columns), low, pl.BlockSpec((blocks, rows // steps, columns), lambda g, bit: (0, g, 0)))
    return picked(body, bit, (steps,), ins, [out, out], "cross", 2)


def add_halve(bit, *pairs):
    lead, columns = pairs[0].shape[0], pairs[0].shape[-1]
    sizes = [pair.shape[2] for pair in pairs[::2]]
    total = sum(sizes)
    steps = 2 if len(sizes) == 1 and total % 32 == 0 and total >= 256 else 1

    def body(bit_ref, *refs):
        mine = bit_ref[0]
        for target, place in ((refs[-2], 1 - mine), (refs[-1], mine)):
            begin = 0
            for kept_ref, got_ref in zip(refs[:-2:2], refs[1:-2:2]):
                length = kept_ref.shape[2]
                for each in range(lead):
                    value = kept_ref[each, place].astype(full) + got_ref[each, place].astype(full)
                    target[each, begin : begin + length] = value.astype(low)
                begin += length

    ins = [
        (pair, pl.BlockSpec((lead, 2, pair.shape[2] // steps, columns), lambda g, bit: (0, 0, g, 0)))
        for pair in pairs
    ]
    out = (
        (lead, total, columns),
        low,
        pl.BlockSpec((lead, total // steps, columns), lambda g, bit: (0, g, 0)),
    )
    return picked(body, bit, (steps,), ins, [out, out], "add_halve", 2)


def add_into(target, place, count, one, two):
    rows, columns = one.shape[-2:]
    steps = 2 if rows % 32 == 0 else 1
    block = pl.BlockSpec((1, rows // steps, columns), lambda g: (0, g, 0))

    def body(one_ref, two_ref, *rest):
        rest[-1][...] = (one_ref[...].astype(full) + two_ref[...].astype(full)).astype(low)

    ins = [one.reshape(1, rows, columns), two.reshape(1, rows, columns)]
    return pl.pallas_call(
        body,
        grid=(steps,),
        in_specs=[block, block] + ([] if target is None else [ANY]),
        out_specs=pl.BlockSpec((1, rows // steps, columns), lambda g: (place, g, 0)),
        out_shape=jax.ShapeDtypeStruct((count, rows, columns), low),
        name="add_into",
        input_output_aliases={} if target is None else {2: 0},
        cost_estimate=cost(1.3),
    )(*ins, *([] if target is None else [target]))


def add(one, two):
    return (one.astype(full) + two.astype(full)).astype(low)


def pair_up(own, got, bit):
    rows, columns = own.shape

    def body(bit_ref, own_ref, got_ref, out_ref):
        mine = bit_ref[0]
        out_ref[mine] = own_ref[...]
        out_ref[1 - mine] = got_ref[...]

    flat = pl.BlockSpec((rows, columns), lambda g, bit: (0, 0))
    out = ((2, rows, columns), low, pl.BlockSpec((2, rows, columns), lambda g, bit: (0, 0, 0)))
    return picked(body, bit, (1,), [(own, flat), (got, flat)], [out], "pair_up", 1)[0]


def finish(kind, half, own, got, begin, length, core, layer, targets, ranks=None):
    pieces, _, columns = own.shape
    scale = 1.0 / lax.axis_size("wide")
    aliases = {place + 2: place for place in range(len(targets))}
    source = pl.BlockSpec((pieces, length, columns), lambda g, core: (0, begin // length, 0))
    ins = [(own, source), (got, source)] + [(target, ANY) for target in targets]
    rows = pieces * length

    def chosen(core_ref, which, own_ref, got_ref, place=None):
        sides = [own_ref, got_ref]
        if ranks is not None:
            wanted = ranks if place is None else ranks[place * pieces // 2 : (place + 1) * pieces // 2]
            values = [jnp.concatenate([side[rank] for rank in wanted]) for side in sides]
        elif place is None:
            values = [side[...].reshape(pieces * length, columns) for side in sides]
        else:
            if pieces == 1:
                near = (0, pl.ds(place * (length // 2), length // 2))
            else:
                near = (pl.ds(place * (pieces // 2), pieces // 2),)
            values = [side[near].reshape(pieces * length // 2, columns) for side in sides]
        return jnp.where(core_ref[0] == which, values[0], values[1]).astype(full) * scale

    if kind in ("down", "join"):

        def body(core_ref, own_ref, got_ref, *rest):
            rest[-1][0] = chosen(core_ref, pl.program_id(0), own_ref, got_ref)

        place = layer if kind == "down" else 0
        shape = (2 if kind == "down" else 1, 2 * rows, columns)
        out = (shape, full, pl.BlockSpec((1, rows, columns), lambda g, core: (place, g, 0)))
        return picked(body, core, (2,), ins, [out], "finish_rows", 3, aliases)
    steps = 4 if half is None else 2
    rows = rows // 2 if half is None else rows

    def block(step):
        return step if half is None else 2 * step + half

    def values_of(core_ref, own_ref, got_ref):
        step = pl.program_id(0)
        if half is None and ranks is not None:
            both = [chosen(core_ref, step // 2, own_ref, got_ref, place) for place in range(2)]
            return jnp.where(step % 2 == 0, both[0], both[1])
        if half is None:
            return chosen(core_ref, step // 2, own_ref, got_ref, step % 2)
        return chosen(core_ref, step, own_ref, got_ref)

    def body(core_ref, own_ref, got_ref, *rest):
        values = values_of(core_ref, own_ref, got_ref)
        if kind == "up":
            rest[-1][0] = values
            return
        if half == 0:
            rest[-1][0] = values
            return
        last = block(pl.program_id(0)) == 3

        @pl.when(jnp.logical_not(last))
        def _():
            rest[-2][0] = values

        @pl.when(last)
        def _():
            rest[-1][0] = values

    if kind == "up":
        outs = [((2, rows, 4 * columns), full, pl.BlockSpec((1, rows, columns), lambda g, core: (layer, 0, block(g))))]
        return picked(body, core, (steps,), ins, outs, "finish_columns", 3, aliases)

    def spot(step):
        return block(step if half == 0 else jnp.minimum(step, steps - 2))

    outs = [
        ((2, rows, 3 * columns), full, pl.BlockSpec((1, rows, columns), lambda g, core: (layer, 0, spot(g)))),
        ((2, rows, columns), full, pl.BlockSpec((1, rows, columns), lambda g, core: (layer, 0, 0))),
    ]
    if half == 0:
        kept = targets[1:]
        ins, outs, aliases = ins[:3] if targets else ins, outs[:1], {2: 0} if targets else {}
        return (picked(body, core, (steps,), ins, outs, "finish_qkv", 3, aliases)[0], *kept)
    return picked(body, core, (steps,), ins, outs, "finish_qkv_out", 3, aliases)


def small_gradients(total, me, width, shares, blocks):
    part = width // shares
    scale = 1.0 / lax.axis_size("wide")

    def body(me_ref, total_ref, gains_ref, shifts_ref, out_ref, up_ref, down_ref, join_ref):
        values = total_ref[...] * scale
        back = [values[0:8], values[8:16]]
        ahead = [values[16 : 20 + blocks], values[20 + blocks : 24 + 2 * blocks]]
        for place in range(shares):

            @pl.when(me_ref[0] == place)
            def _():
                columns = slice(place * part, place * part + part)
                for layer in range(2):
                    for row, target in ((0, gains_ref), (1, shifts_ref)):
                        target[layer, 0:1] = back[layer][row : row + 1, columns]
                        target[layer, 1:2] = ahead[layer][row + 1 : row + 2, columns]
                    out_ref[layer : layer + 1] = ahead[layer][3:4, columns]
                    down_ref[layer : layer + 1] = ahead[layer][0:1, columns]
                    begin = place * part * blocks
                    while begin < (place + 1) * part * blocks:
                        row, column = begin // width, begin % width
                        length = min(width - column, (place + 1) * part * blocks - begin)
                        at = begin - place * part * blocks
                        piece = ahead[layer][4 + row : 5 + row, column : column + length]
                        up_ref[layer : layer + 1, at : at + length] = piece
                        begin += length
                join_ref[...] = back[1][2:3, columns]

    shapes = [(2, 2, part), (2, 2, part), (2, part), (2, part * blocks), (2, part), (1, part)]
    outs = [(shape, full, pl.BlockSpec(shape, lambda g, me, n=len(shape): (0,) * n)) for shape in shapes]
    ins = [(total, pl.BlockSpec(total.shape, lambda g, me: (0, 0)))]
    return picked(body, me, (1,), ins, outs, "small_gradients", 1)


def after(value, *earlier):
    return lax.optimization_barrier((value,) + earlier)[0] if earlier else value


def swap(values, axis, mask):
    size = lax.axis_size(axis)
    return lax.ppermute(values, axis, [(source, source ^ mask) for source in range(size)])


def masks(axis):
    return [1 << bit for bit in range(lax.axis_size(axis).bit_length() - 1)]


class Order:
    def __init__(self):
        self.last = ()

    def run(self, function, *arrays):
        held = lax.optimization_barrier(tuple(arrays) + self.last)[: len(arrays)]
        out = function(*held)
        self.last = (jax.tree.leaves(out)[0],)
        return out

    def mark(self, value):
        return self.run(lambda x: x + 1, value)

    def hold(self, *arrays):
        self.last += arrays


def place_bit(axis, mask):
    return ((lax.axis_index(axis) & mask) // mask).astype(jnp.int32).reshape(1)


class Spread:
    def __init__(self, order, total):
        self.order = order
        self.count, rows, self.columns = total.shape
        self.masks = list(reversed(masks("wide")[1:]))
        places = 1 << len(self.masks)
        last = len(self.masks) - 1
        self.ranks = [sum(((place >> bit) & 1) << (last - bit) for bit in range(last + 1)) for place in range(places)]
        groups = [[2 * place + core for place in range(places)] for core in range(2)]
        self.length = rows // places
        part = lax.psum_scatter(total, "wide", axis_index_groups=groups, scatter_dimension=1, tiled=True)
        self.part = part.reshape(-1, self.columns)
        self.mask, self.closed = None, False

    def step(self):
        if self.mask is not None:
            bit = place_bit("wide", self.mask)
            self.part = self.order.run(lambda *x: pair_up(*x, bit), self.part, self.got).reshape(-1, self.columns)
        if self.masks:
            self.mask = self.masks.pop(0)
            self.got = swap(self.part, "wide", self.mask)
        else:
            self.got, self.closed = swap(self.part, "wide", 1), True

    def finish(self, done, terms):
        while not self.closed:
            self.step()
        own, got = [side.reshape(-1, self.count * self.length, self.columns) for side in (self.part, self.got)]
        if self.length % 16:
            pieces = own.shape[0]
            own, got = [
                jnp.stack([side.reshape(pieces, self.count, -1, self.columns)[rank] for rank in self.ranks], axis=1)
                .reshape(1, -1, self.columns)
                for side in (own, got)
            ]
            self.length, self.ranks = self.length * pieces, None
        for which, term in enumerate(terms):
            term.finish(done, own, got, which * self.length, self.length, self.ranks)


class Term:
    def __init__(self, order, kind, layer, function, *arrays):
        self.order, self.kind, self.layer, self.half = order, kind, layer, None
        self.core = place_bit("wide", 1)
        sent = order.run(lambda *x: function(*x, 1 - self.core), *arrays)
        self.got = [swap(each, "wide", 1) for each in sent]
        self.columns = sent[0].shape[-1]
        self.keep = lambda: order.run(lambda *x: function(*x, self.core), *arrays)

    def stay(self):
        self.kept, self.keep = self.keep(), None

    def part(self, half):
        other = copy.copy(self)
        other.kept, other.got, other.half = self.kept[half::2], self.got[half::2], half
        return other

    def pass_narrow(self):
        stages = list(reversed(masks("narrow")))
        if isinstance(self.kept, (list, tuple)):
            bit = place_bit("narrow", stages[0])
            blocks = len(self.kept) // 2
            sent, self.kept = self.order.run(lambda *x: cross(bit, *x), *self.kept, *self.got)
            self.got = swap(sent, "narrow", stages.pop(0))
        else:
            blocks = 1
        for mask in stages:
            pairs = [(self.kept, self.got)]
            self.kept, self.got = halve(self.order, "narrow", mask, blocks, pairs, self.columns)

    def pass_first(self, mask):
        swapped = [self.kept[owner * 2 + block] for block in range(2) for owner in range(2)]
        brought = [self.got[owner * 2 + block] for block in range(2) for owner in range(2)]
        bit = place_bit("wide", mask)
        sent, self.kept = self.order.run(lambda *x: cross(bit, *x), *swapped, *brought)
        self.got = swap(sent, "wide", mask)

    def pass_wide(self, mask):
        pairs = list(zip(self.kept, self.got)) if isinstance(self.kept, (list, tuple)) else [(self.kept, self.got)]
        self.kept, self.got = halve(self.order, "wide", mask, 1, pairs, self.columns)

    def add_into(self, target, place, count):
        kept, got = [side.reshape(-1, self.columns) for side in (self.kept, self.got)]
        if target is None:
            return self.order.run(lambda one, two: add_into(None, place, count, one, two), kept, got)
        return self.order.run(lambda target, one, two: add_into(target, place, count, one, two), target, kept, got)

    def finish(self, done, own, got, begin, length, ranks=None):
        targets = done.get(self.kind, ())

        def last(own, got, core, *targets):
            return finish(self.kind, self.half, own, got, begin, length, core, self.layer, targets, ranks)

        done[self.kind] = self.order.run(last, own, got, self.core, *targets)


def halve(order, axis, mask, lead, pairs, columns):
    shaped = [array.reshape(lead, 2, -1, columns) for pair in pairs for array in pair]
    bit = place_bit(axis, mask)
    sent, kept = order.run(lambda *x: add_halve(bit, *x), *shaped)
    return kept, swap(sent, axis, mask)


class Reduce:
    def __init__(self, order, terms, passed=(), late=()):
        self.order, self.terms = order, terms
        rest = [mask for mask in masks("wide")[1:] if mask not in passed]
        self.down = [mask for mask in rest if mask not in late] + [mask for mask in rest if mask in late]
        self.up = list(reversed(passed))
        self.pieces, self.columns = 2 ** len(passed), terms[0].columns
        self.parts = [(term.kept, term.got) for term in terms]
        self.lengths, self.first = [each.size // self.columns for each, _ in self.parts], True
        self.joining, self.closed = None, False

    def step(self):
        if self.closed:
            return
        if self.down:
            mask = self.down.pop(0)
            rows = [kept.size // self.columns for kept, _ in self.parts]
            even = all(each % 32 == 0 for each in rows) and bool(self.down)
            if self.first and even:
                self.pieces, self.lengths = 2 * self.pieces, [each // 2 for each in rows]
            self.first = False
            if even:
                self.up.insert(0, mask)
                self.parts = [halve(self.order, "wide", mask, 1, self.parts, self.columns)]
            else:
                flat = [[side.reshape(-1, self.columns) for side in pair] for pair in self.parts]
                pair = [jnp.concatenate(sides) for sides in zip(*flat)]
                total = self.order.run(add, *pair)
                self.parts = [(total, swap(total, "wide", mask))]
            return
        kept, got = [array.reshape(-1, self.columns) for array in self.parts[0]]
        if self.joining is None:
            total = self.order.run(add, kept, got)
        else:
            bit = place_bit("wide", self.joining)
            total = self.order.run(lambda *x: pair_up(*x, bit), kept, got).reshape(-1, self.columns)
        if self.up:
            self.joining = self.up.pop(0)
            self.parts = [(total, swap(total, "wide", self.joining))]
        else:
            self.parts = [(total, swap(total, "wide", 1))]
            self.closed = True

    def finish(self, done):
        own, got = [array.reshape(self.pieces, -1, self.columns) for array in self.parts[0]]
        begin = 0
        for term, length in zip(self.terms, self.lengths):
            term.finish(done, own, got, begin, length)
            begin += length


def on_device(
    tokens,
    skip,
    flags,
    cotangent,
    norm_gains,
    norm_biases,
    qkv_weight,
    out_weight,
    out_bias,
    up_weight,
    up_bias,
    down_weight,
    down_bias,
    skip_weight,
    skip_bias,
):
    items, seq_rows, width = tokens.shape
    rows = items * seq_rows
    me = lax.axis_index("narrow")
    shares = lax.axis_size("narrow")
    spots = jnp.stack([me, lax.axis_index("wide")]).astype(jnp.int32)
    order = Order()

    def fetches(layer):
        return (
            Fetch([(qkv_weight, layer)], (1, 2)),
            Fetch([(out_weight, layer), (up_weight, layer)], (1, 2)),
            Fetch([(down_weight, layer)], (1, 4)),
        )

    fetch_qkv0, fetch_up0, fetch_down0 = fetches(0)
    fetch_qkv1, fetch_up1, fetch_down1 = fetches(1)
    fetch_join = Fetch([(skip_weight, None)], (1, 4))
    qkv0, qkv1 = [Weight(each, 0, width, spots) for each in (fetch_qkv0, fetch_qkv1)]
    out0, out1 = [Weight(each, 0, width, spots) for each in (fetch_up0, fetch_up1)]
    up0, up1 = [Weight(each, 1, width, spots) for each in (fetch_up0, fetch_up1)]
    down0, down1 = [Weight(each, 0, width, spots) for each in (fetch_down0, fetch_down1)]
    join = Weight(fetch_join, 0, width, spots)

    small = (norm_gains, norm_biases, out_bias, down_bias, skip_bias, up_bias)
    fetch_qkv0.cut()
    fetch_qkv0.fetch()
    held = order.run(pack_small, *[after(piece, fetch_qkv0.sent) for piece in small])[None]
    for mask in masks("narrow"):
        held = jnp.concatenate([held, swap(held, "narrow", mask)])
    last = order.last
    for each in (fetch_up0, fetch_down0, fetch_join, fetch_qkv1, fetch_up1, fetch_down1):
        each.cut(*last)
        last = (each.sent,)
    fetch_up0.fetch()
    fetch_down0.fetch(fetch_up0.sent)
    fetch_join.fetch(fetch_down0.sent)
    fetch_qkv1.fetch(fetch_join.sent)
    place = me.astype(jnp.int32).reshape(1)
    lines = order.run(lambda x: unpack_small(x, place, small, width), held)

    def line(row):
        return lines[row : row + 1]

    gains, shifts = [[line(2 * layer + each) for each in range(2)] for layer in range(2)], None
    shifts = [[line(4 + 2 * layer + each) for each in range(2)] for layer in range(2)]
    out_biases, down_biases, join_shift = [line(8), line(9)], [line(10), line(11)], line(12)
    blocks = up0.blocks
    up_biases = [lines[13 + layer * blocks : 13 + (layer + 1) * blocks].reshape(1, -1) for layer in range(2)]

    tokens_flat, skip_flat, cotangent_flat = [array.reshape(rows, width) for array in (tokens, skip, cotangent)]
    lengths = PATCHES + 1 + CAPTION * flags
    valid = lax.broadcasted_iota(jnp.int32, (items, seq_rows), 1) < lengths[:, None]
    dz1 = order.run(lambda x: jnp.where(valid.reshape(rows, 1), x, 0), after(cotangent_flat, fetch_down1.sent))

    fetch_qkv0.share(1)
    fetch_qkv0.share(0)
    order.hold(*fetch_up0.got())
    fetch_up0.share(1)
    a0, packed0 = order.run(lambda *x: project_qkv(*x, qkv0), tokens_flat, gains[0][0], shifts[0][0])
    order.hold(*fetch_down0.got())
    fetch_down0.share(1, a0)
    fetch_up1.fetch(a0)
    fetch_down1.fetch(a0)
    packed0 = packed0.reshape(3, items, seq_rows, width)
    mixed0, totals0 = order.run(lambda *x: attend(*x, items, seq_rows), packed0, lengths)
    order.hold(*fetch_join.got(), *fetch_qkv1.got())
    there = order.mark(spots)
    fetch_up0.share(0, there)
    fetch_down0.share(0, there)
    fetch_join.share(1, there)
    fetch_qkv1.share(1, there)
    mixed0 = mixed0.reshape(rows, width)
    m0, second0, hidden0, slope0, middle = order.run(
        lambda x, o, ob, g, s, ub, db: feed_forward(x, o, out0, ob, g, s, up0, ub, down0, db),
        tokens_flat, mixed0, out_biases[0], gains[0][1], shifts[0][1], up_biases[0], down_biases[0],
    )
    fetch_join.share(0, middle)
    fetch_qkv1.share(0, middle)
    order.hold(*fetch_up1.got(), *fetch_down1.got())
    fetch_up1.share(1, middle)
    fetch_down1.share(1, middle)
    entry, a1, packed1 = order.run(
        lambda m, s, jb, g, sh: join_qkv(m, s, join, jb, g, sh, qkv1),
        middle, skip_flat, join_shift, gains[1][0], shifts[1][0],
    )
    packed1 = packed1.reshape(3, items, seq_rows, width)
    mixed1, totals1 = order.run(lambda *x: attend(*x, items, seq_rows), packed1, lengths)
    fetch_up1.share(0, mixed1)
    fetch_down1.share(0, mixed1)
    mixed1 = mixed1.reshape(rows, width)
    m1, second1, hidden1, slope1, output = order.run(
        lambda x, o, ob, g, s, ub, db, k: feed_forward(x, o, out1, ob, g, s, up1, ub, down1, db, k),
        entry, mixed1, out_biases[1], gains[1][1], shifts[1][1], up_biases[1], down_biases[1], lengths,
    )

    done = {}
    term_down1 = Term(order, "down", 1, down_term, hidden1, dz1)
    term_down1.stay()
    term_down1.pass_narrow()
    du, dm, db, do, sums1 = order.run(
        lambda y, z, s, m, g: feed_forward_back(y, z, s, down1, up1, m, g, out1),
        dz1, dz1, slope1, m1, gains[1][1],
    )
    term_up1 = Term(order, "up", 1, up_term, second1, du)
    term_up1.stay()
    term_up1.pass_narrow()
    total = term_down1.add_into(None, 0, 3)
    dpacked = order.run(
        lambda *x: attend_back(*x, items, seq_rows), packed1, do.reshape(items, seq_rows, width), totals1, lengths
    )
    flat_packed = dpacked.reshape(3, rows, width)
    term_qkv1 = Term(order, "qkv", 1, qkv_out_term, a1, flat_packed, mixed1, db)
    term_qkv1.stay()
    term_qkv1.pass_narrow()
    total = term_up1.add_into(total, 1, 3)
    dentry, dmiddle, dz0, skip_grad, sums3 = order.run(
        lambda gp, x, g, dm: project_back(gp, qkv1, x, g, dm, join), flat_packed, entry, gains[1][0], dm
    )
    term_join = Term(order, "join", 1, join_term, middle, skip_flat, dentry)
    term_join.stay()
    term_join.pass_narrow()
    term_down0 = Term(order, "down", 0, down_term, hidden0, dz0)
    term_down0.stay()
    total = term_qkv1.add_into(total, 2, 3)
    spread = Spread(order, total)
    term_down0.pass_first(2)

    du, dm, db, do, sums0 = order.run(
        lambda y, z, s, m, g: feed_forward_back(y, z, s, down0, up0, m, g, out0),
        dmiddle, dz0, slope0, m0, gains[0][1],
    )
    term_join.pass_wide(2)
    term_up0 = Term(order, "up", 0, up_term, second0, du)
    term_up0.stay()
    term_down0.pass_narrow()
    term_up0.pass_narrow()
    dpacked = order.run(
        lambda *x: attend_back(*x, items, seq_rows), packed0, do.reshape(items, seq_rows, width), totals0, lengths
    )
    order.hold(term_down0.got, term_join.got)
    flat_packed = dpacked.reshape(3, rows, width)
    term_qkv0 = Term(order, "qkv", 0, qkv_out_term, a0, flat_packed, mixed0, db)
    term_qkv0.stay()
    one, two = term_qkv0.part(0), term_qkv0.part(1)
    one.pass_narrow()
    two.pass_narrow()
    first = Reduce(order, [term_down0, term_join], (2,))
    first.step()
    second = Reduce(order, [term_up0])
    second.step()
    tokens_grad, sums2 = order.run(
        lambda gp, x, g, dm: project_back(gp, qkv0, x, g, dm), flat_packed, tokens_flat, gains[0][0], dm
    )
    minor = jnp.concatenate([sums2, sums3, sums0, sums1])
    places = masks("wide")
    minor_stages = [("narrow", mask) for mask in masks("narrow")]
    minor_stages += [("wide", mask) for mask in places if mask != 2] + [("wide", mask) for mask in places if mask == 2]
    minor_got = swap(minor, *minor_stages[0])

    def minor_step():
        nonlocal minor, minor_got
        if minor_stages:
            minor_stages.pop(0)
            minor = order.run(lambda one, two: one + two, minor, minor_got)
            if minor_stages:
                minor_got = swap(minor, *minor_stages[0])

    third = Reduce(order, [one])
    third.step()
    first.step()
    second.step()
    spread.step()
    fourth = Reduce(order, [two])
    fourth.step()
    minor_step()
    third.step()
    first.step()
    second.step()
    spread.step()
    fourth.step()
    minor_step()
    third.step()
    first.step()
    minor_step()
    spread.step()
    fourth.step()
    second.step()
    minor_step()
    first.step()
    third.step()
    fourth.step()
    second.step()
    spread.step()
    first.finish(done)
    third.step()
    fourth.step()
    minor_step()
    second.step()
    spread.finish(done, (term_down1, term_up1, term_qkv1))
    third.step()
    fourth.step()
    for each in (first, second, third, fourth):
        while not each.closed:
            each.step()
    while minor_stages:
        minor_step()
    second.finish(done)
    third.finish(done)
    fourth.finish(done)
    small = order.run(lambda x: small_gradients(x, place, width, shares, up1.blocks), minor)

    return (
        output.reshape(tokens.shape),
        tokens_grad.reshape(tokens.shape),
        skip_grad.reshape(tokens.shape),
        small[0],
        small[1],
        done["qkv"][0],
        done["qkv"][1],
        small[2],
        done["up"][0],
        small[3],
        done["down"][0],
        small[4],
        done["join"][0][0],
        small[5].reshape(-1),
    )


def solution(mesh):
    placed = (
        P(("wide", "narrow"), None, None),
        P(("wide", "narrow"), None, None),
        P(("wide", "narrow")),
        P(("wide", "narrow"), None, None),
        P(None, None, "narrow"),
        P(None, None, "narrow"),
        P(None, "narrow", None),
        P(None, "narrow", None),
        P(None, "narrow"),
        P(None, "narrow", None),
        P(None, "narrow"),
        P(None, "narrow", None),
        P(None, "narrow"),
        P("narrow", None),
        P("narrow"),
    )
    return jax.shard_map(
        on_device,
        mesh=mesh,
        in_specs=placed,
        out_specs=(
            P(("wide", "narrow"), None, None),
            P(("wide", "narrow"), None, None),
            P(("wide", "narrow"), None, None),
            P(None, None, "narrow"),
            P(None, None, "narrow"),
            P(None, "narrow", None),
            P(None, "narrow", None),
            P(None, "narrow"),
            P(None, "narrow", None),
            P(None, "narrow"),
            P(None, "narrow", None),
            P(None, "narrow"),
            P("narrow", None),
            P("narrow"),
        ),
        check_vma=False,
    )
```

```python
import copy
import math

import jax
import jax.numpy as jnp
from jax import lax
from jax.experimental import pallas as pl
from jax.experimental.pallas import tpu as pltpu
from jax.sharding import PartitionSpec as P

HEAD_DIM = 64
PATCHES = 256
CAPTION = 77
PAIR = 2 * HEAD_DIM


epsilon = 1e-05
masked_score = -1e30
low = jnp.bfloat16
full = jnp.float32
SPARE = 14
ANY = pl.BlockSpec(memory_space=pltpu.HBM)
SCALARS = pl.BlockSpec(memory_space=pltpu.SMEM)


def dot(left, right, contract=(1, 0)):
    dims = (((contract[0],), (contract[1],)), ((), ()))
    return lax.dot_general(left, right, dims, preferred_element_type=full)


def normalize(values):
    centred = values - jnp.mean(values, axis=-1, keepdims=True)
    factor = lax.rsqrt(jnp.mean(centred * centred, axis=-1, keepdims=True) + epsilon)
    return centred * factor, factor


def normalize_back(upstream, normed, factor):
    return factor * (
        upstream
        - jnp.mean(upstream, axis=-1, keepdims=True)
        - normed * jnp.mean(upstream * normed, axis=-1, keepdims=True)
    )


def column_sum(values):
    return jnp.sum(values.astype(full), axis=0, keepdims=True)


def whole(shape):
    return pl.BlockSpec(shape, lambda *grid: (0,) * len(shape))


def cost(micros):
    return pl.CostEstimate(flops=int(micros * 3 * 10**8), bytes_accessed=0, transcendentals=0)


def room(ins, outs, scratch, spare):
    total = spare * 2**20
    for shape, kind, spec in [(array.shape, array.dtype, spec) for array, spec in ins] + list(outs):
        if spec.block_shape is not None and spec.memory_space is None:
            total += 2 * math.prod(spec.block_shape) * jnp.dtype(kind).itemsize
    for piece in scratch:
        if piece.memory_space == pltpu.VMEM:
            total += math.prod(piece.shape) * jnp.dtype(piece.dtype).itemsize
    return total


def call(body, grid, ins, outs, name, micros, scratch=(), spare=6):
    return pl.pallas_call(
        body,
        grid=grid,
        in_specs=[spec for _, spec in ins],
        out_specs=[spec for _, _, spec in outs],
        out_shape=[jax.ShapeDtypeStruct(shape, kind) for shape, kind, _ in outs],
        scratch_shapes=list(scratch),
        name=name,
        cost_estimate=cost(micros),
        compiler_params=pltpu.CompilerParams(vmem_limit_bytes=room(ins, outs, scratch, spare)),
    )(*[array for array, _ in ins])


class Fetch:
    def __init__(self, arrays, sharing):
        self.arrays, self.sharing = arrays, list(sharing)
        self.rows = arrays[0][0].shape[-2]
        while self.rows % (16 << len(self.sharing)):
            self.sharing.pop()
        self.length = self.rows >> len(self.sharing)

    def quarter(self, place):
        return sum(((place // mask) & 1) << bit for bit, mask in enumerate(self.sharing))

    def cut(self, *earlier):
        found = []
        for array, layer in self.arrays:
            array = after(array, *earlier)
            lead = () if layer is None else (layer,)
            begin = self.quarter(lax.axis_index("wide")) * self.length
            sizes = (1,) * len(lead) + (self.length, array.shape[-1])
            found.append(lax.dynamic_slice(array, lead + (begin, 0), sizes).reshape(self.length, -1))
        self.sent = (jnp.concatenate(found, axis=1) if len(found) > 1 else found[0])[None]

    def fetch(self, *earlier):
        held = after(self.sent, *earlier)
        for mask in masks("narrow"):
            held = jnp.concatenate([held, swap(held, "narrow", mask)])
        self.pieces = {0: held[1:]}

    def share(self, which, *earlier):
        if which < len(self.sharing):
            mask = self.sharing[which]
            got = {key ^ (1 << which): swap(after(piece, *earlier), "wide", mask) for key, piece in self.pieces.items()}
            self.pieces.update(got)

    def got(self):
        return list(self.pieces.values())


class Weight:
    def __init__(self, fetched, which, width, spots):
        self.fetched, self.spots, self.width = fetched, spots, width
        self.array, self.layer = fetched.arrays[which]
        self.begin = sum(array.shape[-1] for array, _ in fetched.arrays[:which])
        self.rows, columns = self.array.shape[-2:]
        self.shares = lax.axis_size("narrow")
        self.blocks = columns // width
        self.total = self.rows * self.shares

    def arrays(self):
        return [self.array] + self.fetched.got()

    def scratch(self):
        copies = 1 + len(self.fetched.pieces) * (self.shares - 1)
        return [pltpu.VMEM((self.blocks, self.total, self.width), low), pltpu.SemaphoreType.DMA((self.blocks, copies))]

    def copies(self, spots, refs, held, signals, block):
        own, pieces = refs[0], refs[1:]
        me, length = spots[0], self.fetched.length
        own = own if self.layer is None else own.at[self.layer]
        columns = pl.ds(block * self.width, self.width)
        begin = pl.multiple_of(me * self.rows, 16)
        found = [(own.at[:, columns], begin, self.rows)]
        columns = pl.ds(self.begin + block * self.width, self.width)
        for key, piece in zip(self.fetched.pieces, pieces):
            for offset in range(1, self.shares):
                begin = (me ^ offset) * self.rows + (self.fetched.quarter(spots[1]) ^ key) * length
                found.append((piece.at[offset - 1, :, columns], pl.multiple_of(begin, 16), length))
        return [
            pltpu.make_async_copy(source, held.at[block, pl.ds(begin, length)], signals.at[block, place])
            for place, (source, begin, length) in enumerate(found)
        ]

    def wait(self, *refs, block=0):
        for copy in self.copies(*refs, block):
            copy.wait()


def weighted(body, weights, grid, ins, outs, name, micros, scratch=(), first=((0, 0),), spare=SPARE):
    spots = weights[0].spots
    operands = [(spots, SCALARS)]
    for weight in weights:
        operands += [(pltpu.with_memory_space_constraint(array, pltpu.HBM), ANY) for array in weight.arrays()]
    counts = [len(weight.arrays()) for weight in weights]
    extra = [piece for weight in weights for piece in weight.scratch()]

    def wrapped(*refs):
        spots_ref, rest = refs[0], list(refs[1:])
        sources = []
        for count in counts:
            sources.append(rest[:count])
            rest = rest[count:]
        spare = rest[len(rest) - len(extra) :]
        rest = rest[: len(rest) - len(extra)]
        handles = []
        for place, weight in enumerate(weights):
            held, signals = spare[2 * place : 2 * place + 2]
            refs_of = (spots_ref, sources[place], held, signals)
            handles.append((weight, refs_of, held))

        everything = [(place, block) for place, weight in enumerate(weights) for block in range(weight.blocks)]

        def begin(wanted):
            for place, block in wanted:
                weight, refs_of, _ = handles[place]
                for copy in weight.copies(*refs_of, block):
                    copy.start()

        @pl.when(pl.program_id(0) == 0)
        def _():
            begin(first)

        def ready(place, block=0, then=False):
            weight, refs_of, held = handles[place]
            weight.wait(*refs_of, block=block)
            if then:
                begin([each for each in everything if each not in first])

        body(ready, [held for _, _, held in handles], *rest)

    return call(wrapped, grid, operands + ins, outs, name, micros, list(scratch) + extra, spare)


def pack_small(*small):
    part = small[0].shape[-1]
    counts = [piece.size // part for piece in small]

    def body(*refs):
        row = 0
        for ref in refs[:-1]:
            values = ref[...].reshape(-1, ref.shape[-1])
            for each in range(values.shape[0]):
                for begin in range(0, values.shape[1], part):
                    refs[-1][row : row + 1] = values[each : each + 1, begin : begin + part].astype(full)
                    row += 1
        refs[-1][row:] = jnp.zeros((refs[-1].shape[0] - row, part), full)

    flat = [piece.reshape((1,) * (2 - piece.ndim) + piece.shape) for piece in small]
    rows = -(-sum(counts) // 16) * 16
    out = ((rows, part), full, whole((rows, part)))
    return call(body, (1,), [(piece, whole(piece.shape)) for piece in flat], [out], "pack_small", 1)[0].astype(low)


def unpack_small(parts, me, small, width):
    shares, _, part = parts.shape
    lines = [(piece.size // piece.shape[-1], piece.shape[-1] // part) for piece in small]
    total = sum(count * many for count, many in lines)
    rows = -(-total // 8) * 8

    def body(me_ref, parts_ref, out_ref):
        values = parts_ref[...].astype(full)
        for mine in range(shares):

            @pl.when(me_ref[0] == mine)
            def _():
                for owner in range(shares):
                    source, target = 0, 0
                    for count, many in lines:
                        for each in range(count):
                            for piece in range(many):
                                at = owner * many * part + piece * part
                                row, column = target + at // width, at % width
                                line = values[owner ^ mine, source : source + 1]
                                out_ref[row : row + 1, column : column + part] = line
                                source += 1
                            target += many
        if rows > total:
            out_ref[total:] = jnp.zeros((rows - total, width), full)

    ins = [(parts, pl.BlockSpec(parts.shape, lambda g, me: (0, 0, 0)))]
    out = ((rows, width), full, pl.BlockSpec((rows, width), lambda g, me: (0, 0)))
    return picked(body, me, (1,), ins, [out], "unpack_small", 1)[0]


def project_qkv(inputs, gain, shift, weight):
    rows, width = inputs.shape

    def body(ready, held, x_ref, gain_ref, shift_ref, a_ref, out_ref):
        step = pl.program_id(0)

        @pl.when(step == 0)
        def _():
            normed, _ = normalize(x_ref[...].astype(full))
            a_ref[...] = (normed * gain_ref[...] + shift_ref[...]).astype(low)
            ready(0, 0, then=True)

        @pl.when(step > 0)
        def _():
            ready(0, step)

        scale = jnp.where(step == 0, HEAD_DIM ** (-0.5), 1.0)
        out_ref[0] = (dot(a_ref[...], held[0][step]).astype(low).astype(full) * scale).astype(low)

    return weighted(
        body,
        [weight],
        (3,),
        [
            (inputs, whole((rows, width))),
            (gain, whole((1, width))),
            (shift, whole((1, width))),
        ],
        [
            ((rows, width), low, whole((rows, width))),
            ((3, rows, width), low, pl.BlockSpec((1, rows, width), lambda j: (j, 0, 0))),
        ],
        "project_qkv",
        7,
    )


def join_qkv(middle, skip, join_weight, join_shift, gain, shift, weight):
    rows, width = middle.shape

    def body(ready, held, m_ref, s_ref, jb_ref, gain_ref, shift_ref, e_ref, a_ref, out_ref):
        step = pl.program_id(0)

        @pl.when(step == 0)
        def _():
            ready(0, then=True)
            entry = dot(m_ref[...], held[0][0, :width]) + dot(s_ref[...], held[0][0, width:]) + jb_ref[...]
            e_ref[...] = entry
            normed, _ = normalize(entry)
            a_ref[...] = (normed * gain_ref[...] + shift_ref[...]).astype(low)

        ready(1, step)
        scale = jnp.where(step == 0, HEAD_DIM ** (-0.5), 1.0)
        out_ref[0] = (dot(a_ref[...], held[1][step]).astype(low).astype(full) * scale).astype(low)

    return weighted(
        body,
        [join_weight, weight],
        (3,),
        [
            (middle, whole((rows, width))),
            (skip, whole((rows, width))),
            (join_shift, whole((1, width))),
            (gain, whole((1, width))),
            (shift, whole((1, width))),
        ],
        [
            ((rows, width), full, whole((rows, width))),
            ((rows, width), low, whole((rows, width))),
            ((3, rows, width), low, pl.BlockSpec((1, rows, width), lambda j: (j, 0, 0))),
        ],
        "join_qkv",
        11,
        first=((0, 0), (1, 0)),
    )


def head_masks(seq_rows):
    lane = lax.broadcasted_iota(jnp.int32, (seq_rows, PAIR), 1)
    return [lane < HEAD_DIM, lane >= HEAD_DIM]


def pairs_of(width):
    pairs = width // PAIR
    return pairs, max(group for group in (1, 2, 3) if pairs % group == 0)


def attend(packed, lengths, items, seq_rows):
    width = packed.shape[-1]
    pairs, group = pairs_of(width)

    def body(length_ref, q_ref, k_ref, v_ref, out_ref, total_ref):
        counts = lax.broadcasted_iota(jnp.int32, (seq_rows, seq_rows), 1) < length_ref[pl.program_id(0)]
        for pair in range(group):
            columns = slice(pair * PAIR, (pair + 1) * PAIR)
            queries, keys, values = q_ref[0, 0, :, columns], k_ref[0, 0, :, columns], v_ref[0, 0, :, columns]
            mixed = jnp.zeros((seq_rows, PAIR), full)
            for head, lanes in enumerate(head_masks(seq_rows)):
                scores = dot(jnp.where(lanes, queries, 0), keys, (1, 1))
                scores = jnp.where(counts, scores, masked_score)
                largest = jnp.max(scores, axis=1, keepdims=True)
                weights = jnp.exp(scores - largest)
                total = jnp.sum(weights, axis=1, keepdims=True)
                mixed += dot(weights.astype(low), jnp.where(lanes, values, 0)) * (1.0 / total)
                total_ref[0, pair, head : head + 1] = (largest + jnp.log(total)).T
            out_ref[0, :, columns] = mixed.astype(low)

    def block(which):
        return pl.BlockSpec((1, 1, seq_rows, group * PAIR), lambda n, h: (which, n, 0, h))

    return call(
        body,
        (items, pairs // group),
        [(lengths, SCALARS), (packed, block(0)), (packed, block(1)), (packed, block(2))],
        [
            (
                (items, seq_rows, width),
                low,
                pl.BlockSpec((1, seq_rows, group * PAIR), lambda n, h: (n, 0, h)),
            ),
            (
                (items, pairs, 8, seq_rows),
                full,
                pl.BlockSpec((1, group, 8, seq_rows), lambda n, h: (n, h, 0, 0)),
            ),
        ],
        "attend",
        10,
        spare=14,
    )


def attend_back(packed, grad_mixed, totals, lengths, items, seq_rows):
    width = packed.shape[-1]
    pairs, group = pairs_of(width)
    sides = [slice(0, PATCHES), slice(PATCHES, seq_rows)]

    def body(length_ref, q_ref, k_ref, v_ref, g_ref, total_ref, out_ref):
        row = PATCHES + lax.broadcasted_iota(jnp.int32, (seq_rows - PATCHES, seq_rows), 0)
        counts = row < length_ref[pl.program_id(0)]
        for pair in range(group):
            columns = slice(pair * PAIR, (pair + 1) * PAIR)
            queries, keys, values = q_ref[0, 0, :, columns], k_ref[0, 0, :, columns], v_ref[0, 0, :, columns]
            upstream = g_ref[0, :, columns]
            grad_queries = jnp.zeros((PAIR, seq_rows), full)
            grad_keys, grad_values = [0.0, 0.0], [0.0, 0.0]
            for head, lanes in enumerate(head_masks(seq_rows)):
                own_queries = jnp.where(lanes, queries, 0)
                own_upstream = jnp.where(lanes, upstream, 0)
                own_keys = jnp.where(lanes, keys, 0)
                parts, centre = [], 0.0
                for side, rows in enumerate(sides):
                    scores = dot(keys[rows], own_queries, (1, 1))
                    if side:
                        scores = jnp.where(counts, scores, masked_score)
                    probs = jnp.exp(scores - total_ref[0, pair, head : head + 1])
                    grad_probs = dot(values[rows], own_upstream, (1, 1))
                    centre += jnp.sum(grad_probs * probs, axis=0, keepdims=True)
                    parts.append((probs, grad_probs))
                for side, (probs, grad_probs) in enumerate(parts):
                    grad_scores = (probs * (grad_probs - centre)).astype(low)
                    grad_values[side] += dot(probs.astype(low), own_upstream)
                    grad_keys[side] += dot(grad_scores, own_queries)
                    grad_queries += dot(own_keys[sides[side]], grad_scores, (0, 0))
            out_ref[0, 0, :, columns] = (grad_queries.T * HEAD_DIM ** (-0.5)).astype(low)
            for side, rows in enumerate(sides):
                out_ref[1, 0, rows, columns] = grad_keys[side].astype(low)
                out_ref[2, 0, rows, columns] = grad_values[side].astype(low)

    def block(which):
        return pl.BlockSpec((1, 1, seq_rows, group * PAIR), lambda n, h: (which, n, 0, h))

    return call(
        body,
        (items, pairs // group),
        [
            (lengths, SCALARS),
            (packed, block(0)),
            (packed, block(1)),
            (packed, block(2)),
            (grad_mixed, pl.BlockSpec((1, seq_rows, group * PAIR), lambda n, h: (n, 0, h))),
            (totals, pl.BlockSpec((1, group, 8, seq_rows), lambda n, h: (n, h, 0, 0))),
        ],
        [
            (
                (3, items, seq_rows, width),
                low,
                pl.BlockSpec((3, 1, seq_rows, group * PAIR), lambda n, h: (0, n, 0, h)),
            ),
        ],
        "attend_back",
        15,
        spare=14,
    )[0]


def gelu_parts(before):
    decay = jnp.exp(before * before * -0.5)
    inverse = pl.reciprocal(1.0 + (0.3275911 * 0.5**0.5) * jnp.abs(before), approx=False)
    series = 1.061405429 * 0.5
    for term in (-1.453152027, 1.421413741, -0.284496736, 0.254829592):
        series = series * inverse + term * 0.5
    below = series * inverse * decay
    share = jnp.where(before >= 0, 1.0 - below, below)
    return before * share, share + before * decay * 0.3989422804014327


def feed_forward(inputs, mixed, out_weight, out_bias, gain, shift, up_weight, up_bias, down_weight, down_bias, lengths=None):
    rows, width = inputs.shape
    steps = up_weight.blocks
    hidden = steps * width

    def body(ready, held, x_ref, o_ref, ob_ref, gain_ref, shift_ref, ub_ref, db_ref, *rest):
        m_ref, a_ref, g_ref, s_ref, y_ref, total = rest[-6:]
        step = pl.program_id(0)

        @pl.when(step == 0)
        def _():
            ready(0, then=True)
            middle = x_ref[...].astype(full) + dot(o_ref[...], held[0][0]) + ob_ref[...]
            m_ref[...] = middle
            normed, _ = normalize(middle)
            a_ref[...] = (normed * gain_ref[...] + shift_ref[...]).astype(low)
            total[...] = middle + db_ref[...]

        ready(1, step)
        before = dot(a_ref[...], held[1][step]) + ub_ref[...]
        value, slope = gelu_parts(before)
        g_ref[...] = value.astype(low)
        s_ref[...] = slope.astype(low)

        @pl.when(step == 0)
        def _():
            ready(2)

        total[...] += dot(g_ref[...], held[2][0, pl.ds(pl.multiple_of(step * width, width), width)])

        @pl.when(step == steps - 1)
        def _():
            if lengths is None:
                y_ref[...] = total[...].astype(low)
            else:
                length = rows // lengths.shape[0]
                row = lax.broadcasted_iota(jnp.int32, (length, width), 0)
                for item in range(lengths.shape[0]):
                    at = slice(item * length, (item + 1) * length)
                    y_ref[at] = jnp.where(row < rest[0][item], total[at], 0.0).astype(low)

    return weighted(
        body,
        [out_weight, up_weight, down_weight],
        (steps,),
        [
            (inputs, whole((rows, width))),
            (mixed, whole((rows, width))),
            (out_bias, whole((1, width))),
            (gain, whole((1, width))),
            (shift, whole((1, width))),
            (up_bias, pl.BlockSpec((1, width), lambda j: (0, j))),
            (down_bias, whole((1, width))),
        ]
        + ([] if lengths is None else [(lengths, SCALARS)]),
        [
            ((rows, width), full, whole((rows, width))),
            ((rows, width), low, whole((rows, width))),
            ((rows, hidden), low, pl.BlockSpec((rows, width), lambda j: (0, j))),
            ((rows, hidden), low, pl.BlockSpec((rows, width), lambda j: (0, j))),
            ((rows, width), low, whole((rows, width))),
        ],
        "feed_forward",
        23,
        scratch=[pltpu.VMEM((rows, width), full)],
        first=((0, 0), (1, 0)),
    )


def feed_forward_back(upstream, rounded, slope, down_weight, up_weight, middle, gain, out_weight):
    rows, width = upstream.shape
    steps = up_weight.blocks
    hidden = steps * width

    def body(ready, held, y_ref, dz_ref, s_ref, m_ref, gain_ref, du_ref, dm_ref, db_ref, do_ref, sums_ref, total):
        step = pl.program_id(0)

        @pl.when(step == 0)
        def _():
            sums_ref[0:1] = column_sum(dz_ref[...])
            total[...] = jnp.zeros_like(total)
            ready(0, then=True)

        down = held[0][0, pl.ds(pl.multiple_of(step * width, width), width)]
        grad = (dot(dz_ref[...], down, (1, 1)) * s_ref[...].astype(full)).astype(low)
        du_ref[...] = grad
        sums_ref[pl.ds(4 + step, 1)] = column_sum(grad)
        ready(1, step)
        total[...] += dot(grad, held[1][step], (1, 1))

        @pl.when(step == steps - 1)
        def _():
            grad_second = total[...]
            normed, factor = normalize(m_ref[...])
            sums_ref[1:2] = column_sum(grad_second * normed)
            sums_ref[2:3] = column_sum(grad_second)
            grad_middle = y_ref[...].astype(full) + normalize_back(grad_second * gain_ref[...], normed, factor)
            dm_ref[...] = grad_middle
            branch = grad_middle.astype(low)
            db_ref[...] = branch
            sums_ref[3:4] = column_sum(branch)
            ready(2)
            do_ref[...] = dot(branch, held[2][0], (1, 1)).astype(low)

    return weighted(
        body,
        [down_weight, up_weight, out_weight],
        (steps,),
        [
            (upstream, whole((rows, width))),
            (rounded, whole((rows, width))),
            (slope, pl.BlockSpec((rows, width), lambda j: (0, j))),
            (middle, whole((rows, width))),
            (gain, whole((1, width))),
        ],
        [
            ((rows, hidden), low, pl.BlockSpec((rows, width), lambda j: (0, j))),
            ((rows, width), full, whole((rows, width))),
            ((rows, width), low, whole((rows, width))),
            ((rows, width), low, whole((rows, width))),
            ((4 + steps, width), full, whole((4 + steps, width))),
        ],
        "feed_forward_back",
        21,
        scratch=[pltpu.VMEM((rows, width), full)],
        first=((0, 0), (1, 0)),
    )


def project_back(grad_packed, weight, inputs, gain, grad_middle, join_weight=None):
    rows, width = inputs.shape
    joined = join_weight is not None

    def body(ready, held, g_ref, x_ref, gain_ref, dm_ref, *rest):
        if joined:
            de_ref, dx_ref, dz_ref, skip_ref, sums_ref, total = rest
        else:
            dx_ref, sums_ref, total = rest
        step = pl.program_id(0)

        @pl.when(step == 0)
        def _():
            total[...] = jnp.zeros_like(total)
            ready(0, 0, then=True)

        @pl.when(step > 0)
        def _():
            ready(0, step)

        total[...] += dot(g_ref[0], held[0][step], (1, 1))

        @pl.when(step == 2)
        def _():
            grad_first = total[...]
            normed, factor = normalize(x_ref[...].astype(full))
            sums_ref[0:1] = column_sum(grad_first * normed)
            sums_ref[1:2] = column_sum(grad_first)
            grad = dm_ref[...] + normalize_back(grad_first * gain_ref[...], normed, factor)
            if joined:
                entry = grad.astype(low)
                de_ref[...] = entry
                sums_ref[2:3] = column_sum(entry)
                ready(1)
                grad = dot(entry, held[1][0, :width], (1, 1))
                dx_ref[...] = grad
                dz_ref[...] = grad.astype(low)
                skip_ref[...] = dot(entry, held[1][0, width:], (1, 1))
            else:
                dx_ref[...] = grad

    ins = [
        (grad_packed, pl.BlockSpec((1, rows, width), lambda j: (j, 0, 0))),
        (inputs, whole((rows, width))),
        (gain, whole((1, width))),
        (grad_middle, whole((rows, width))),
    ]
    outs = [((rows, width), full, whole((rows, width))), ((8, width), full, whole((8, width)))]
    if joined:
        rounded = ((rows, width), low, whole((rows, width)))
        outs = [rounded, outs[0], rounded, outs[0], outs[1]]
    return weighted(
        body,
        [weight] + ([join_weight] if joined else []),
        (3,),
        ins,
        outs,
        "project_back",
        13 if joined else 9,
        scratch=[pltpu.VMEM((rows, width), full)],
    )


def picked(body, which, grid, ins, outs, name, micros, aliases=None, spare=4):
    return pl.pallas_call(
        body,
        grid_spec=pltpu.PrefetchScalarGridSpec(
            num_scalar_prefetch=1,
            grid=grid,
            in_specs=[spec for _, spec in ins],
            out_specs=[spec for _, _, spec in outs],
        ),
        out_shape=[jax.ShapeDtypeStruct(shape, kind) for shape, kind, _ in outs],
        name=name,
        input_output_aliases={place + 1: out for place, out in (aliases or {}).items()},
        cost_estimate=cost(micros),
        compiler_params=pltpu.CompilerParams(vmem_limit_bytes=room(ins, outs, (), spare)),
    )(which, *[array for array, _ in ins])


def quarters(rows, width, narrow_rows):
    shape = (lax.axis_size("narrow") // 2 * narrow_rows, width)
    return [(shape, low, pl.BlockSpec(shape, lambda g, core: (0, 0)))] * 4


def up_term(left, right, core):
    rows, width = left.shape
    part = width // lax.axis_size("narrow")
    half = width // 2

    def body(core_ref, l_ref, r_ref, *outs):
        value = dot(l_ref[...], r_ref[...], (0, 0)).astype(low)
        for block in range(2):

            @pl.when(pl.program_id(0) == block)
            def _():
                outs[block][...] = value[:half]
                outs[2 + block][...] = value[half:]

    return picked(
        body,
        core,
        (2,),
        [
            (left, pl.BlockSpec((rows, width), lambda g, core: (0, 0))),
            (right, pl.BlockSpec((rows, width), lambda g, core: (0, core[0] * 2 + g))),
        ],
        quarters(rows, width, part),
        "up_term",
        3.5,
    )


def qkv_out_term(first, packed, mixed, branch, core):
    rows, width = first.shape
    part = width // lax.axis_size("narrow")
    half = width // 2

    def body(core_ref, l_ref, r_ref, o_ref, b_ref, *outs):
        step = pl.program_id(0)
        last = core_ref[0] * 2 + step == 3

        def put(block, value):
            outs[block][...] = value[:half]
            outs[2 + block][...] = value[half:]

        @pl.when(last)
        def _():
            put(1, dot(o_ref[...], b_ref[...], (0, 0)).astype(low))

        @pl.when(jnp.logical_not(last))
        def _():
            value = dot(l_ref[...], r_ref[0], (0, 0)).astype(low)
            for block in range(2):

                @pl.when(step == block)
                def _():
                    put(block, value)

    flat = pl.BlockSpec((rows, width), lambda g, core: (0, 0))
    return picked(
        body,
        core,
        (2,),
        [
            (first, flat),
            (packed, pl.BlockSpec((1, rows, width), lambda g, core: (jnp.minimum(core[0] * 2 + g, 2), 0, 0))),
            (mixed, flat),
            (branch, flat),
        ],
        quarters(rows, width, part),
        "qkv_out_term",
        3.5,
    )


def down_term(left, right, core):
    rows, width = right.shape
    shares = lax.axis_size("narrow")
    part = left.shape[1] // (2 * shares)
    direct = part == width
    if not direct:
        left = left.reshape(rows, shares, 2, 2, part // 2)
        left = lax.dynamic_index_in_dim(left, core[0], 2, keepdims=False)
        left = left.reshape(rows, 2, shares // 2, 2, part // 2).swapaxes(2, 3).reshape(rows, 2 * width)
    half = width // 2

    def body(core_ref, l_ref, r_ref, *outs):
        value = dot(l_ref[...], r_ref[...], (0, 0)).astype(low)
        for owner in range(2):

            @pl.when(pl.program_id(0) == owner)
            def _():
                outs[2 * owner][...] = value[:half]
                outs[2 * owner + 1][...] = value[half:]

    return picked(
        body,
        core,
        (2,),
        [
            (left, pl.BlockSpec((rows, width), lambda g, core: (0, g * 2 + core[0] if direct else g))),
            (right, pl.BlockSpec((rows, width), lambda g, core: (0, 0))),
        ],
        quarters(rows, width, part // 2),
        "down_term",
        3.5,
    )


def join_term(middle, skip, right, core):
    rows, width = right.shape
    shares = lax.axis_size("narrow")
    part = width // shares
    half = width // 2
    if part != half:
        left = jnp.concatenate([middle, skip], axis=1).reshape(rows, shares, 2, 2, part // 2)
        left = lax.dynamic_index_in_dim(left, core[0], 2, keepdims=False)
        left = left.reshape(rows, 2, shares // 2, 2, part // 2).swapaxes(2, 3).reshape(rows, width)
        middle, skip = left[:, :half], left[:, half:]

    def body(core_ref, m_ref, s_ref, r_ref, *outs):
        for owner, left_ref in enumerate((m_ref, s_ref)):
            value = dot(left_ref[...], r_ref[...], (0, 0)).astype(low)
            outs[2 * owner][...] = value[: half // 2]
            outs[2 * owner + 1][...] = value[half // 2 :]

    side = pl.BlockSpec((rows, half), lambda g, core: (0, core[0] if part == half else 0))
    return picked(
        body,
        core,
        (1,),
        [(middle, side), (skip, side), (right, pl.BlockSpec((rows, width), lambda g, core: (0, 0)))],
        quarters(rows, width, part // 2),
        "join_term",
        2,
    )


def cross(bit, *pieces):
    kept, got = pieces[: len(pieces) // 2], pieces[len(pieces) // 2 :]
    rows, columns = kept[0].shape
    blocks = len(kept) // 2
    steps = 2 if rows % 32 == 0 else 1

    def body(bit_ref, *refs):
        sent_ref, left_ref = refs[-2:]

        def put(target, owner):
            for block in range(blocks):
                place = owner * blocks + block
                one, two = refs[place], refs[2 * blocks + place]
                target[block] = (one[...].astype(full) + two[...].astype(full)).astype(low)

        for mine in range(2):

            @pl.when(bit_ref[0] == mine)
            def _():
                put(sent_ref, 1 - mine)
                put(left_ref, mine)

    ins = [(piece, pl.BlockSpec((rows // steps, columns), lambda g, bit: (g, 0))) for piece in kept + got]
    out = ((blocks, rows, columns), low, pl.BlockSpec((blocks, rows // steps, columns), lambda g, bit: (0, g, 0)))
    return picked(body, bit, (steps,), ins, [out, out], "cross", 2)


def add_halve(bit, *pairs):
    lead, columns = pairs[0].shape[0], pairs[0].shape[-1]
    sizes = [pair.shape[2] for pair in pairs[::2]]
    total = sum(sizes)
    steps = 2 if len(sizes) == 1 and total % 32 == 0 and total >= 256 else 1

    def body(bit_ref, *refs):
        mine = bit_ref[0]
        for target, place in ((refs[-2], 1 - mine), (refs[-1], mine)):
            begin = 0
            for kept_ref, got_ref in zip(refs[:-2:2], refs[1:-2:2]):
                length = kept_ref.shape[2]
                for each in range(lead):
                    value = kept_ref[each, place].astype(full) + got_ref[each, place].astype(full)
                    target[each, begin : begin + length] = value.astype(low)
                begin += length

    ins = [
        (pair, pl.BlockSpec((lead, 2, pair.shape[2] // steps, columns), lambda g, bit: (0, 0, g, 0)))
        for pair in pairs
    ]
    out = (
        (lead, total, columns),
        low,
        pl.BlockSpec((lead, total // steps, columns), lambda g, bit: (0, g, 0)),
    )
    return picked(body, bit, (steps,), ins, [out, out], "add_halve", 2)


def add_into(target, place, count, one, two):
    rows, columns = one.shape[-2:]
    steps = 2 if rows % 32 == 0 else 1
    block = pl.BlockSpec((1, rows // steps, columns), lambda g: (0, g, 0))

    def body(one_ref, two_ref, *rest):
        rest[-1][...] = (one_ref[...].astype(full) + two_ref[...].astype(full)).astype(low)

    ins = [one.reshape(1, rows, columns), two.reshape(1, rows, columns)]
    return pl.pallas_call(
        body,
        grid=(steps,),
        in_specs=[block, block] + ([] if target is None else [ANY]),
        out_specs=pl.BlockSpec((1, rows // steps, columns), lambda g: (place, g, 0)),
        out_shape=jax.ShapeDtypeStruct((count, rows, columns), low),
        name="add_into",
        input_output_aliases={} if target is None else {2: 0},
        cost_estimate=cost(1.3),
    )(*ins, *([] if target is None else [target]))


def add(one, two):
    return (one.astype(full) + two.astype(full)).astype(low)


def pair_up(own, got, bit):
    rows, columns = own.shape

    def body(bit_ref, own_ref, got_ref, out_ref):
        mine = bit_ref[0]
        out_ref[mine] = own_ref[...]
        out_ref[1 - mine] = got_ref[...]

    flat = pl.BlockSpec((rows, columns), lambda g, bit: (0, 0))
    out = ((2, rows, columns), low, pl.BlockSpec((2, rows, columns), lambda g, bit: (0, 0, 0)))
    return picked(body, bit, (1,), [(own, flat), (got, flat)], [out], "pair_up", 1)[0]


def finish(kind, half, own, got, begin, length, core, layer, targets):
    pieces, _, columns = own.shape
    scale = 1.0 / lax.axis_size("wide")
    aliases = {place + 2: place for place in range(len(targets))}
    source = pl.BlockSpec((pieces, length, columns), lambda g, core: (0, begin // length, 0))
    ins = [(own, source), (got, source)] + [(target, ANY) for target in targets]
    rows = pieces * length

    def chosen(core_ref, which, own_ref, got_ref, place=None):
        sides = [own_ref, got_ref]
        if place is None:
            values = [side[...].reshape(pieces * length, columns) for side in sides]
        else:
            if pieces == 1:
                near = (0, pl.ds(place * (length // 2), length // 2))
            else:
                near = (pl.ds(place * (pieces // 2), pieces // 2),)
            values = [side[near].reshape(pieces * length // 2, columns) for side in sides]
        return jnp.where(core_ref[0] == which, values[0], values[1]).astype(full) * scale

    if kind in ("down", "join"):

        def body(core_ref, own_ref, got_ref, *rest):
            rest[-1][0] = chosen(core_ref, pl.program_id(0), own_ref, got_ref)

        place = layer if kind == "down" else 0
        shape = (2 if kind == "down" else 1, 2 * rows, columns)
        out = (shape, full, pl.BlockSpec((1, rows, columns), lambda g, core: (place, g, 0)))
        return picked(body, core, (2,), ins, [out], "finish_rows", 3, aliases)
    steps = 4 if half is None else 2
    rows = rows // 2 if half is None else rows

    def block(step):
        return step if half is None else 2 * step + half

    def values_of(core_ref, own_ref, got_ref):
        step = pl.program_id(0)
        if half is None:
            return chosen(core_ref, step // 2, own_ref, got_ref, step % 2)
        return chosen(core_ref, step, own_ref, got_ref)

    def body(core_ref, own_ref, got_ref, *rest):
        values = values_of(core_ref, own_ref, got_ref)
        if kind == "up":
            rest[-1][0] = values
            return
        if half == 0:
            rest[-1][0] = values
            return
        last = block(pl.program_id(0)) == 3

        @pl.when(jnp.logical_not(last))
        def _():
            rest[-2][0] = values

        @pl.when(last)
        def _():
            rest[-1][0] = values

    if kind == "up":
        outs = [((2, rows, 4 * columns), full, pl.BlockSpec((1, rows, columns), lambda g, core: (layer, 0, block(g))))]
        return picked(body, core, (steps,), ins, outs, "finish_columns", 3, aliases)

    def spot(step):
        return block(step if half == 0 else jnp.minimum(step, steps - 2))

    outs = [
        ((2, rows, 3 * columns), full, pl.BlockSpec((1, rows, columns), lambda g, core: (layer, 0, spot(g)))),
        ((2, rows, columns), full, pl.BlockSpec((1, rows, columns), lambda g, core: (layer, 0, 0))),
    ]
    if half == 0:
        kept = targets[1:]
        ins, outs, aliases = ins[:3] if targets else ins, outs[:1], {2: 0} if targets else {}
        return (picked(body, core, (steps,), ins, outs, "finish_qkv", 3, aliases)[0], *kept)
    return picked(body, core, (steps,), ins, outs, "finish_qkv_out", 3, aliases)


def small_gradients(total, me, width, shares, blocks):
    part = width // shares
    scale = 1.0 / lax.axis_size("wide")

    def body(me_ref, total_ref, gains_ref, shifts_ref, out_ref, up_ref, down_ref, join_ref):
        values = total_ref[...] * scale
        back = [values[0:8], values[8:16]]
        ahead = [values[16 : 20 + blocks], values[20 + blocks : 24 + 2 * blocks]]
        for place in range(shares):

            @pl.when(me_ref[0] == place)
            def _():
                columns = slice(place * part, place * part + part)
                for layer in range(2):
                    for row, target in ((0, gains_ref), (1, shifts_ref)):
                        target[layer, 0:1] = back[layer][row : row + 1, columns]
                        target[layer, 1:2] = ahead[layer][row + 1 : row + 2, columns]
                    out_ref[layer : layer + 1] = ahead[layer][3:4, columns]
                    down_ref[layer : layer + 1] = ahead[layer][0:1, columns]
                    begin = place * part * blocks
                    while begin < (place + 1) * part * blocks:
                        row, column = begin // width, begin % width
                        length = min(width - column, (place + 1) * part * blocks - begin)
                        at = begin - place * part * blocks
                        piece = ahead[layer][4 + row : 5 + row, column : column + length]
                        up_ref[layer : layer + 1, at : at + length] = piece
                        begin += length
                join_ref[...] = back[1][2:3, columns]

    shapes = [(2, 2, part), (2, 2, part), (2, part), (2, part * blocks), (2, part), (1, part)]
    outs = [(shape, full, pl.BlockSpec(shape, lambda g, me, n=len(shape): (0,) * n)) for shape in shapes]
    ins = [(total, pl.BlockSpec(total.shape, lambda g, me: (0, 0)))]
    return picked(body, me, (1,), ins, outs, "small_gradients", 1)


def after(value, *earlier):
    return lax.optimization_barrier((value,) + earlier)[0] if earlier else value


def swap(values, axis, mask):
    size = lax.axis_size(axis)
    return lax.ppermute(values, axis, [(source, source ^ mask) for source in range(size)])


def masks(axis):
    return [1 << bit for bit in range(lax.axis_size(axis).bit_length() - 1)]


class Order:
    def __init__(self):
        self.last = ()

    def run(self, function, *arrays):
        held = lax.optimization_barrier(tuple(arrays) + self.last)[: len(arrays)]
        out = function(*held)
        self.last = (jax.tree.leaves(out)[0],)
        return out

    def mark(self, value):
        return self.run(lambda x: x + 1, value)

    def hold(self, *arrays):
        self.last += arrays


def place_bit(axis, mask):
    return ((lax.axis_index(axis) & mask) // mask).astype(jnp.int32).reshape(1)


class Term:
    def __init__(self, order, kind, layer, function, *arrays):
        self.order, self.kind, self.layer, self.half = order, kind, layer, None
        self.core = place_bit("wide", 1)
        sent = order.run(lambda *x: function(*x, 1 - self.core), *arrays)
        self.got = [swap(each, "wide", 1) for each in sent]
        self.columns = sent[0].shape[-1]
        self.keep = lambda: order.run(lambda *x: function(*x, self.core), *arrays)

    def stay(self):
        self.kept, self.keep = self.keep(), None

    def part(self, half):
        other = copy.copy(self)
        other.kept, other.got, other.half = self.kept[half::2], self.got[half::2], half
        return other

    def pass_narrow(self):
        stages = list(reversed(masks("narrow")))
        if isinstance(self.kept, (list, tuple)):
            bit = place_bit("narrow", stages[0])
            blocks = len(self.kept) // 2
            sent, self.kept = self.order.run(lambda *x: cross(bit, *x), *self.kept, *self.got)
            self.got = swap(sent, "narrow", stages.pop(0))
        else:
            blocks = 1
        for mask in stages:
            pairs = [(self.kept, self.got)]
            self.kept, self.got = halve(self.order, "narrow", mask, blocks, pairs, self.columns)

    def pass_first(self, mask):
        swapped = [self.kept[owner * 2 + block] for block in range(2) for owner in range(2)]
        brought = [self.got[owner * 2 + block] for block in range(2) for owner in range(2)]
        bit = place_bit("wide", mask)
        sent, self.kept = self.order.run(lambda *x: cross(bit, *x), *swapped, *brought)
        self.got = swap(sent, "wide", mask)

    def pass_wide(self, mask):
        pairs = list(zip(self.kept, self.got)) if isinstance(self.kept, (list, tuple)) else [(self.kept, self.got)]
        self.kept, self.got = halve(self.order, "wide", mask, 1, pairs, self.columns)

    def add_into(self, target, place, count):
        kept, got = [side.reshape(-1, self.columns) for side in (self.kept, self.got)]
        if target is None:
            return self.order.run(lambda one, two: add_into(None, place, count, one, two), kept, got)
        return self.order.run(lambda target, one, two: add_into(target, place, count, one, two), target, kept, got)

    def finish(self, done, own, got, begin, length):
        targets = done.get(self.kind, ())

        def last(own, got, core, *targets):
            return finish(self.kind, self.half, own, got, begin, length, core, self.layer, targets)

        done[self.kind] = self.order.run(last, own, got, self.core, *targets)


def halve(order, axis, mask, lead, pairs, columns):
    shaped = [array.reshape(lead, 2, -1, columns) for pair in pairs for array in pair]
    bit = place_bit(axis, mask)
    sent, kept = order.run(lambda *x: add_halve(bit, *x), *shaped)
    return kept, swap(sent, axis, mask)


class Reduce:
    def __init__(self, order, terms, passed=(), late=()):
        self.order, self.terms = order, terms
        rest = [mask for mask in masks("wide")[1:] if mask not in passed]
        self.down = [mask for mask in rest if mask not in late] + [mask for mask in rest if mask in late]
        self.up = list(reversed(passed))
        self.pieces, self.columns = 2 ** len(passed), terms[0].columns
        self.parts = [(term.kept, term.got) for term in terms]
        self.lengths, self.first = [each.size // self.columns for each, _ in self.parts], True
        self.joining, self.closed = None, False

    def step(self):
        if self.closed:
            return
        if self.down:
            mask = self.down.pop(0)
            rows = [kept.size // self.columns for kept, _ in self.parts]
            even = all(each % 32 == 0 for each in rows) and bool(self.down)
            if self.first and even:
                self.pieces, self.lengths = 2 * self.pieces, [each // 2 for each in rows]
            self.first = False
            if even:
                self.up.insert(0, mask)
                self.parts = [halve(self.order, "wide", mask, 1, self.parts, self.columns)]
            else:
                flat = [[side.reshape(-1, self.columns) for side in pair] for pair in self.parts]
                pair = [jnp.concatenate(sides) for sides in zip(*flat)]
                total = self.order.run(add, *pair)
                self.parts = [(total, swap(total, "wide", mask))]
            return
        kept, got = [array.reshape(-1, self.columns) for array in self.parts[0]]
        if self.joining is None:
            total = self.order.run(add, kept, got)
        else:
            bit = place_bit("wide", self.joining)
            total = self.order.run(lambda *x: pair_up(*x, bit), kept, got).reshape(-1, self.columns)
        if self.up:
            self.joining = self.up.pop(0)
            self.parts = [(total, swap(total, "wide", self.joining))]
        else:
            self.parts = [(total, swap(total, "wide", 1))]
            self.closed = True

    def finish(self, done):
        own, got = [array.reshape(self.pieces, -1, self.columns) for array in self.parts[0]]
        begin = 0
        for term, length in zip(self.terms, self.lengths):
            term.finish(done, own, got, begin, length)
            begin += length


def on_device(
    tokens,
    skip,
    flags,
    cotangent,
    norm_gains,
    norm_biases,
    qkv_weight,
    out_weight,
    out_bias,
    up_weight,
    up_bias,
    down_weight,
    down_bias,
    skip_weight,
    skip_bias,
):
    items, seq_rows, width = tokens.shape
    rows = items * seq_rows
    me = lax.axis_index("narrow")
    shares = lax.axis_size("narrow")
    spots = jnp.stack([me, lax.axis_index("wide")]).astype(jnp.int32)
    order = Order()

    def fetches(layer):
        return (
            Fetch([(qkv_weight, layer)], (1, 2)),
            Fetch([(out_weight, layer), (up_weight, layer)], (1, 2)),
            Fetch([(down_weight, layer)], (1, 4)),
        )

    fetch_qkv0, fetch_up0, fetch_down0 = fetches(0)
    fetch_qkv1, fetch_up1, fetch_down1 = fetches(1)
    fetch_join = Fetch([(skip_weight, None)], (1, 4))
    qkv0, qkv1 = [Weight(each, 0, width, spots) for each in (fetch_qkv0, fetch_qkv1)]
    out0, out1 = [Weight(each, 0, width, spots) for each in (fetch_up0, fetch_up1)]
    up0, up1 = [Weight(each, 1, width, spots) for each in (fetch_up0, fetch_up1)]
    down0, down1 = [Weight(each, 0, width, spots) for each in (fetch_down0, fetch_down1)]
    join = Weight(fetch_join, 0, width, spots)

    small = (norm_gains, norm_biases, out_bias, down_bias, skip_bias, up_bias)
    fetch_qkv0.cut()
    fetch_qkv0.fetch()
    held = order.run(pack_small, *[after(piece, fetch_qkv0.sent) for piece in small])[None]
    for mask in masks("narrow"):
        held = jnp.concatenate([held, swap(held, "narrow", mask)])
    last = order.last
    for each in (fetch_up0, fetch_down0, fetch_join, fetch_qkv1, fetch_up1, fetch_down1):
        each.cut(*last)
        last = (each.sent,)
    fetch_up0.fetch()
    fetch_down0.fetch(fetch_up0.sent)
    fetch_join.fetch(fetch_down0.sent)
    fetch_qkv1.fetch(fetch_join.sent)
    place = me.astype(jnp.int32).reshape(1)
    lines = order.run(lambda x: unpack_small(x, place, small, width), held)

    def line(row):
        return lines[row : row + 1]

    gains, shifts = [[line(2 * layer + each) for each in range(2)] for layer in range(2)], None
    shifts = [[line(4 + 2 * layer + each) for each in range(2)] for layer in range(2)]
    out_biases, down_biases, join_shift = [line(8), line(9)], [line(10), line(11)], line(12)
    blocks = up0.blocks
    up_biases = [lines[13 + layer * blocks : 13 + (layer + 1) * blocks].reshape(1, -1) for layer in range(2)]

    tokens_flat, skip_flat, cotangent_flat = [array.reshape(rows, width) for array in (tokens, skip, cotangent)]
    lengths = PATCHES + 1 + CAPTION * flags
    valid = lax.broadcasted_iota(jnp.int32, (items, seq_rows), 1) < lengths[:, None]
    dz1 = order.run(lambda x: jnp.where(valid.reshape(rows, 1), x, 0), after(cotangent_flat, fetch_down1.sent))

    fetch_qkv0.share(1)
    fetch_qkv0.share(0)
    order.hold(*fetch_up0.got())
    fetch_up0.share(1)
    a0, packed0 = order.run(lambda *x: project_qkv(*x, qkv0), tokens_flat, gains[0][0], shifts[0][0])
    order.hold(*fetch_down0.got())
    fetch_down0.share(1, a0)
    fetch_up1.fetch(a0)
    fetch_down1.fetch(a0)
    packed0 = packed0.reshape(3, items, seq_rows, width)
    mixed0, totals0 = order.run(lambda *x: attend(*x, items, seq_rows), packed0, lengths)
    order.hold(*fetch_join.got(), *fetch_qkv1.got())
    there = order.mark(spots)
    fetch_up0.share(0, there)
    fetch_down0.share(0, there)
    fetch_join.share(1, there)
    fetch_qkv1.share(1, there)
    mixed0 = mixed0.reshape(rows, width)
    m0, second0, hidden0, slope0, middle = order.run(
        lambda x, o, ob, g, s, ub, db: feed_forward(x, o, out0, ob, g, s, up0, ub, down0, db),
        tokens_flat, mixed0, out_biases[0], gains[0][1], shifts[0][1], up_biases[0], down_biases[0],
    )
    fetch_join.share(0, middle)
    fetch_qkv1.share(0, middle)
    order.hold(*fetch_up1.got(), *fetch_down1.got())
    fetch_up1.share(1, middle)
    fetch_down1.share(1, middle)
    entry, a1, packed1 = order.run(
        lambda m, s, jb, g, sh: join_qkv(m, s, join, jb, g, sh, qkv1),
        middle, skip_flat, join_shift, gains[1][0], shifts[1][0],
    )
    packed1 = packed1.reshape(3, items, seq_rows, width)
    mixed1, totals1 = order.run(lambda *x: attend(*x, items, seq_rows), packed1, lengths)
    fetch_up1.share(0, mixed1)
    fetch_down1.share(0, mixed1)
    mixed1 = mixed1.reshape(rows, width)
    m1, second1, hidden1, slope1, output = order.run(
        lambda x, o, ob, g, s, ub, db, k: feed_forward(x, o, out1, ob, g, s, up1, ub, down1, db, k),
        entry, mixed1, out_biases[1], gains[1][1], shifts[1][1], up_biases[1], down_biases[1], lengths,
    )

    done = {}
    term_down1 = Term(order, "down", 1, down_term, hidden1, dz1)
    term_down1.stay()
    term_down1.pass_narrow()
    du, dm, db, do, sums1 = order.run(
        lambda y, z, s, m, g: feed_forward_back(y, z, s, down1, up1, m, g, out1),
        dz1, dz1, slope1, m1, gains[1][1],
    )
    term_up1 = Term(order, "up", 1, up_term, second1, du)
    term_up1.stay()
    term_up1.pass_narrow()
    total = term_down1.add_into(None, 0, 3)
    dpacked = order.run(
        lambda *x: attend_back(*x, items, seq_rows), packed1, do.reshape(items, seq_rows, width), totals1, lengths
    )
    flat_packed = dpacked.reshape(3, rows, width)
    term_qkv1 = Term(order, "qkv", 1, qkv_out_term, a1, flat_packed, mixed1, db)
    term_qkv1.stay()
    term_qkv1.pass_narrow()
    total = term_up1.add_into(total, 1, 3)
    dentry, dmiddle, dz0, skip_grad, sums3 = order.run(
        lambda gp, x, g, dm: project_back(gp, qkv1, x, g, dm, join), flat_packed, entry, gains[1][0], dm
    )
    term_join = Term(order, "join", 1, join_term, middle, skip_flat, dentry)
    term_join.stay()
    term_join.pass_narrow()
    term_down0 = Term(order, "down", 0, down_term, hidden0, dz0)
    term_down0.stay()
    total = term_qkv1.add_into(total, 2, 3)
    size = lax.axis_size("wide")
    groups = [[device + core for device in range(0, size, 2)] for core in range(2)]
    flat_total = total.reshape(-1, width)
    part = lax.psum_scatter(flat_total, "wide", axis_index_groups=groups, scatter_dimension=0, tiled=True)
    term_down0.pass_first(2)

    du, dm, db, do, sums0 = order.run(
        lambda y, z, s, m, g: feed_forward_back(y, z, s, down0, up0, m, g, out0),
        dmiddle, dz0, slope0, m0, gains[0][1],
    )
    term_join.pass_wide(2)
    term_up0 = Term(order, "up", 0, up_term, second0, du)
    term_up0.stay()
    term_down0.pass_narrow()
    term_up0.pass_narrow()
    dpacked = order.run(
        lambda *x: attend_back(*x, items, seq_rows), packed0, do.reshape(items, seq_rows, width), totals0, lengths
    )
    order.hold(term_down0.got, term_join.got)
    flat_packed = dpacked.reshape(3, rows, width)
    term_qkv0 = Term(order, "qkv", 0, qkv_out_term, a0, flat_packed, mixed0, db)
    term_qkv0.stay()
    one, two = term_qkv0.part(0), term_qkv0.part(1)
    one.pass_narrow()
    two.pass_narrow()
    first = Reduce(order, [term_down0, term_join], (2,))
    first.step()
    second = Reduce(order, [term_up0])
    second.step()
    tokens_grad, sums2 = order.run(
        lambda gp, x, g, dm: project_back(gp, qkv0, x, g, dm), flat_packed, tokens_flat, gains[0][0], dm
    )
    minor = jnp.concatenate([sums2, sums3, sums0, sums1])
    places = masks("wide")
    minor_stages = [("narrow", mask) for mask in masks("narrow")]
    minor_stages += [("wide", mask) for mask in places if mask != 2] + [("wide", mask) for mask in places if mask == 2]
    minor_got = swap(minor, *minor_stages[0])

    def minor_step():
        nonlocal minor, minor_got
        if minor_stages:
            minor_stages.pop(0)
            minor = order.run(lambda one, two: one + two, minor, minor_got)
            if minor_stages:
                minor_got = swap(minor, *minor_stages[0])

    third = Reduce(order, [one])
    third.step()
    first.step()
    second.step()
    fourth = Reduce(order, [two])
    fourth.step()
    minor_step()
    third.step()
    first.step()
    second.step()
    order.hold(part)
    gathered = lax.all_gather(after(part, *order.last), "wide", axis_index_groups=groups, tiled=True)
    fourth.step()
    third.step()
    first.step()
    minor_step()
    fourth.step()
    second.step()
    third.step()
    minor_step()
    first.step()
    fourth.step()
    second.step()
    minor_step()
    first.finish(done)
    third.step()
    fourth.step()
    minor_step()
    second.step()
    order.hold(gathered)
    other = swap(after(gathered, *order.last), "wide", 1)
    third.step()
    fourth.step()
    second.finish(done)
    own, got = gathered.reshape(1, -1, width), other.reshape(1, -1, width)
    for which, term in enumerate((term_down1, term_up1, term_qkv1)):
        term.finish(done, own, got, which * (own.shape[1] // 3), own.shape[1] // 3)
    for each in (first, second, third, fourth):
        while not each.closed:
            each.step()
    while minor_stages:
        minor_step()
    third.finish(done)
    fourth.finish(done)
    small = order.run(lambda x: small_gradients(x, place, width, shares, up1.blocks), minor)

    return (
        output.reshape(tokens.shape),
        tokens_grad.reshape(tokens.shape),
        skip_grad.reshape(tokens.shape),
        small[0],
        small[1],
        done["qkv"][0],
        done["qkv"][1],
        small[2],
        done["up"][0],
        small[3],
        done["down"][0],
        small[4],
        done["join"][0][0],
        small[5].reshape(-1),
    )


def solution(mesh):
    placed = (
        P(("wide", "narrow"), None, None),
        P(("wide", "narrow"), None, None),
        P(("wide", "narrow")),
        P(("wide", "narrow"), None, None),
        P(None, None, "narrow"),
        P(None, None, "narrow"),
        P(None, "narrow", None),
        P(None, "narrow", None),
        P(None, "narrow"),
        P(None, "narrow", None),
        P(None, "narrow"),
        P(None, "narrow", None),
        P(None, "narrow"),
        P("narrow", None),
        P("narrow"),
    )
    return jax.shard_map(
        on_device,
        mesh=mesh,
        in_specs=placed,
        out_specs=(
            P(("wide", "narrow"), None, None),
            P(("wide", "narrow"), None, None),
            P(("wide", "narrow"), None, None),
            P(None, None, "narrow"),
            P(None, None, "narrow"),
            P(None, "narrow", None),
            P(None, "narrow", None),
            P(None, "narrow"),
            P(None, "narrow", None),
            P(None, "narrow"),
            P(None, "narrow", None),
            P(None, "narrow"),
            P("narrow", None),
            P("narrow"),
        ),
        check_vma=False,
    )
```

```python
import copy
import math

import jax
import jax.numpy as jnp
from jax import lax
from jax.experimental import pallas as pl
from jax.experimental.pallas import tpu as pltpu
from jax.sharding import PartitionSpec as P

HEAD_DIM = 64
PATCHES = 256
CAPTION = 77
PAIR = 2 * HEAD_DIM


epsilon = 1e-05
masked_score = -1e30
low = jnp.bfloat16
full = jnp.float32
SPARE = 14
ANY = pl.BlockSpec(memory_space=pltpu.HBM)
SCALARS = pl.BlockSpec(memory_space=pltpu.SMEM)


def dot(left, right, contract=(1, 0)):
    dims = (((contract[0],), (contract[1],)), ((), ()))
    return lax.dot_general(left, right, dims, preferred_element_type=full)


def normalize(values):
    centred = values - jnp.mean(values, axis=-1, keepdims=True)
    factor = lax.rsqrt(jnp.mean(centred * centred, axis=-1, keepdims=True) + epsilon)
    return centred * factor, factor


def normalize_back(upstream, normed, factor):
    return factor * (
        upstream
        - jnp.mean(upstream, axis=-1, keepdims=True)
        - normed * jnp.mean(upstream * normed, axis=-1, keepdims=True)
    )


def column_sum(values):
    return jnp.sum(values.astype(full), axis=0, keepdims=True)


def whole(shape):
    return pl.BlockSpec(shape, lambda *grid: (0,) * len(shape))


def cost(micros):
    return pl.CostEstimate(flops=int(micros * 3 * 10**8), bytes_accessed=0, transcendentals=0)


def room(ins, outs, scratch, spare):
    total = spare * 2**20
    for shape, kind, spec in [(array.shape, array.dtype, spec) for array, spec in ins] + list(outs):
        if spec.block_shape is not None and spec.memory_space is None:
            total += 2 * math.prod(spec.block_shape) * jnp.dtype(kind).itemsize
    for piece in scratch:
        if piece.memory_space == pltpu.VMEM:
            total += math.prod(piece.shape) * jnp.dtype(piece.dtype).itemsize
    return total


def call(body, grid, ins, outs, name, micros, scratch=(), spare=6):
    return pl.pallas_call(
        body,
        grid=grid,
        in_specs=[spec for _, spec in ins],
        out_specs=[spec for _, _, spec in outs],
        out_shape=[jax.ShapeDtypeStruct(shape, kind) for shape, kind, _ in outs],
        scratch_shapes=list(scratch),
        name=name,
        cost_estimate=cost(micros),
        compiler_params=pltpu.CompilerParams(vmem_limit_bytes=room(ins, outs, scratch, spare)),
    )(*[array for array, _ in ins])


class Fetch:
    def __init__(self, arrays, sharing):
        self.arrays, self.sharing = arrays, list(sharing)
        self.rows = arrays[0][0].shape[-2]
        while self.rows % (16 << len(self.sharing)):
            self.sharing.pop()
        self.length = self.rows >> len(self.sharing)

    def quarter(self, place):
        return sum(((place // mask) & 1) << bit for bit, mask in enumerate(self.sharing))

    def cut(self, *earlier):
        found = []
        for array, layer in self.arrays:
            array = after(array, *earlier)
            lead = () if layer is None else (layer,)
            begin = self.quarter(lax.axis_index("wide")) * self.length
            sizes = (1,) * len(lead) + (self.length, array.shape[-1])
            found.append(lax.dynamic_slice(array, lead + (begin, 0), sizes).reshape(self.length, -1))
        self.sent = (jnp.concatenate(found, axis=1) if len(found) > 1 else found[0])[None]

    def fetch(self, *earlier):
        held = after(self.sent, *earlier)
        for mask in masks("narrow"):
            held = jnp.concatenate([held, swap(held, "narrow", mask)])
        self.pieces = {0: held[1:]}

    def share(self, which, *earlier):
        if which < len(self.sharing):
            mask = self.sharing[which]
            got = {key ^ (1 << which): swap(after(piece, *earlier), "wide", mask) for key, piece in self.pieces.items()}
            self.pieces.update(got)

    def got(self):
        return list(self.pieces.values())


class Weight:
    def __init__(self, fetched, which, width, spots):
        self.fetched, self.spots, self.width = fetched, spots, width
        self.array, self.layer = fetched.arrays[which]
        self.begin = sum(array.shape[-1] for array, _ in fetched.arrays[:which])
        self.rows, columns = self.array.shape[-2:]
        self.shares = lax.axis_size("narrow")
        self.blocks = columns // width
        self.total = self.rows * self.shares

    def arrays(self):
        return [self.array] + self.fetched.got()

    def scratch(self):
        copies = 1 + len(self.fetched.pieces) * (self.shares - 1)
        return [pltpu.VMEM((self.blocks, self.total, self.width), low), pltpu.SemaphoreType.DMA((self.blocks, copies))]

    def copies(self, spots, refs, held, signals, block):
        own, pieces = refs[0], refs[1:]
        me, length = spots[0], self.fetched.length
        own = own if self.layer is None else own.at[self.layer]
        columns = pl.ds(block * self.width, self.width)
        begin = pl.multiple_of(me * self.rows, 16)
        found = [(own.at[:, columns], begin, self.rows)]
        columns = pl.ds(self.begin + block * self.width, self.width)
        for key, piece in zip(self.fetched.pieces, pieces):
            for offset in range(1, self.shares):
                begin = (me ^ offset) * self.rows + (self.fetched.quarter(spots[1]) ^ key) * length
                found.append((piece.at[offset - 1, :, columns], pl.multiple_of(begin, 16), length))
        return [
            pltpu.make_async_copy(source, held.at[block, pl.ds(begin, length)], signals.at[block, place])
            for place, (source, begin, length) in enumerate(found)
        ]

    def wait(self, *refs, block=0):
        for copy in self.copies(*refs, block):
            copy.wait()


def weighted(body, weights, grid, ins, outs, name, micros, scratch=(), first=((0, 0),), spare=SPARE):
    spots = weights[0].spots
    operands = [(spots, SCALARS)]
    for weight in weights:
        operands += [(pltpu.with_memory_space_constraint(array, pltpu.HBM), ANY) for array in weight.arrays()]
    counts = [len(weight.arrays()) for weight in weights]
    extra = [piece for weight in weights for piece in weight.scratch()]

    def wrapped(*refs):
        spots_ref, rest = refs[0], list(refs[1:])
        sources = []
        for count in counts:
            sources.append(rest[:count])
            rest = rest[count:]
        spare = rest[len(rest) - len(extra) :]
        rest = rest[: len(rest) - len(extra)]
        handles = []
        for place, weight in enumerate(weights):
            held, signals = spare[2 * place : 2 * place + 2]
            refs_of = (spots_ref, sources[place], held, signals)
            handles.append((weight, refs_of, held))

        everything = [(place, block) for place, weight in enumerate(weights) for block in range(weight.blocks)]

        def begin(wanted):
            for place, block in wanted:
                weight, refs_of, _ = handles[place]
                for copy in weight.copies(*refs_of, block):
                    copy.start()

        @pl.when(pl.program_id(0) == 0)
        def _():
            begin(first)

        def ready(place, block=0, then=False):
            weight, refs_of, held = handles[place]
            weight.wait(*refs_of, block=block)
            if then:
                begin([each for each in everything if each not in first])

        body(ready, [held for _, _, held in handles], *rest)

    return call(wrapped, grid, operands + ins, outs, name, micros, list(scratch) + extra, spare)


def pack_small(*small):
    part = small[0].shape[-1]
    counts = [piece.size // part for piece in small]

    def body(*refs):
        row = 0
        for ref in refs[:-1]:
            values = ref[...].reshape(-1, ref.shape[-1])
            for each in range(values.shape[0]):
                for begin in range(0, values.shape[1], part):
                    refs[-1][row : row + 1] = values[each : each + 1, begin : begin + part].astype(full)
                    row += 1
        refs[-1][row:] = jnp.zeros((refs[-1].shape[0] - row, part), full)

    flat = [piece.reshape((1,) * (2 - piece.ndim) + piece.shape) for piece in small]
    rows = -(-sum(counts) // 16) * 16
    out = ((rows, part), full, whole((rows, part)))
    return call(body, (1,), [(piece, whole(piece.shape)) for piece in flat], [out], "pack_small", 1)[0].astype(low)


def unpack_small(parts, me, small, width):
    shares, _, part = parts.shape
    lines = [(piece.size // piece.shape[-1], piece.shape[-1] // part) for piece in small]
    total = sum(count * many for count, many in lines)
    rows = -(-total // 8) * 8

    def body(me_ref, parts_ref, out_ref):
        values = parts_ref[...].astype(full)
        for mine in range(shares):

            @pl.when(me_ref[0] == mine)
            def _():
                for owner in range(shares):
                    source, target = 0, 0
                    for count, many in lines:
                        for each in range(count):
                            for piece in range(many):
                                at = owner * many * part + piece * part
                                row, column = target + at // width, at % width
                                line = values[owner ^ mine, source : source + 1]
                                out_ref[row : row + 1, column : column + part] = line
                                source += 1
                            target += many
        if rows > total:
            out_ref[total:] = jnp.zeros((rows - total, width), full)

    ins = [(parts, pl.BlockSpec(parts.shape, lambda g, me: (0, 0, 0)))]
    out = ((rows, width), full, pl.BlockSpec((rows, width), lambda g, me: (0, 0)))
    return picked(body, me, (1,), ins, [out], "unpack_small", 1)[0]


def project_qkv(inputs, gain, shift, weight):
    rows, width = inputs.shape

    def body(ready, held, x_ref, gain_ref, shift_ref, a_ref, out_ref):
        step = pl.program_id(0)

        @pl.when(step == 0)
        def _():
            normed, _ = normalize(x_ref[...].astype(full))
            a_ref[...] = (normed * gain_ref[...] + shift_ref[...]).astype(low)
            ready(0, 0, then=True)

        @pl.when(step > 0)
        def _():
            ready(0, step)

        scale = jnp.where(step == 0, HEAD_DIM ** (-0.5), 1.0)
        out_ref[0] = (dot(a_ref[...], held[0][step]).astype(low).astype(full) * scale).astype(low)

    return weighted(
        body,
        [weight],
        (3,),
        [
            (inputs, whole((rows, width))),
            (gain, whole((1, width))),
            (shift, whole((1, width))),
        ],
        [
            ((rows, width), low, whole((rows, width))),
            ((3, rows, width), low, pl.BlockSpec((1, rows, width), lambda j: (j, 0, 0))),
        ],
        "project_qkv",
        7,
    )


def join_qkv(middle, skip, join_weight, join_shift, gain, shift, weight):
    rows, width = middle.shape

    def body(ready, held, m_ref, s_ref, jb_ref, gain_ref, shift_ref, e_ref, a_ref, out_ref):
        step = pl.program_id(0)

        @pl.when(step == 0)
        def _():
            ready(0, then=True)
            entry = dot(m_ref[...], held[0][0, :width]) + dot(s_ref[...], held[0][0, width:]) + jb_ref[...]
            e_ref[...] = entry
            normed, _ = normalize(entry)
            a_ref[...] = (normed * gain_ref[...] + shift_ref[...]).astype(low)

        ready(1, step)
        scale = jnp.where(step == 0, HEAD_DIM ** (-0.5), 1.0)
        out_ref[0] = (dot(a_ref[...], held[1][step]).astype(low).astype(full) * scale).astype(low)

    return weighted(
        body,
        [join_weight, weight],
        (3,),
        [
            (middle, whole((rows, width))),
            (skip, whole((rows, width))),
            (join_shift, whole((1, width))),
            (gain, whole((1, width))),
            (shift, whole((1, width))),
        ],
        [
            ((rows, width), full, whole((rows, width))),
            ((rows, width), low, whole((rows, width))),
            ((3, rows, width), low, pl.BlockSpec((1, rows, width), lambda j: (j, 0, 0))),
        ],
        "join_qkv",
        11,
        first=((0, 0), (1, 0)),
    )


def head_masks(seq_rows):
    lane = lax.broadcasted_iota(jnp.int32, (seq_rows, PAIR), 1)
    return [lane < HEAD_DIM, lane >= HEAD_DIM]


def pairs_of(width):
    pairs = width // PAIR
    return pairs, max(group for group in (1, 2, 3) if pairs % group == 0)


def attend(packed, lengths, items, seq_rows):
    width = packed.shape[-1]
    pairs, group = pairs_of(width)

    def body(length_ref, q_ref, k_ref, v_ref, out_ref, total_ref):
        counts = lax.broadcasted_iota(jnp.int32, (seq_rows, seq_rows), 1) < length_ref[pl.program_id(0)]
        for pair in range(group):
            columns = slice(pair * PAIR, (pair + 1) * PAIR)
            queries, keys, values = q_ref[0, 0, :, columns], k_ref[0, 0, :, columns], v_ref[0, 0, :, columns]
            mixed = jnp.zeros((seq_rows, PAIR), full)
            for head, lanes in enumerate(head_masks(seq_rows)):
                scores = dot(jnp.where(lanes, queries, 0), keys, (1, 1))
                scores = jnp.where(counts, scores, masked_score)
                largest = jnp.max(scores, axis=1, keepdims=True)
                weights = jnp.exp(scores - largest)
                total = jnp.sum(weights, axis=1, keepdims=True)
                mixed += dot(weights.astype(low), jnp.where(lanes, values, 0)) * (1.0 / total)
                total_ref[0, pair, head : head + 1] = (largest + jnp.log(total)).T
            out_ref[0, :, columns] = mixed.astype(low)

    def block(which):
        return pl.BlockSpec((1, 1, seq_rows, group * PAIR), lambda n, h: (which, n, 0, h))

    return call(
        body,
        (items, pairs // group),
        [(lengths, SCALARS), (packed, block(0)), (packed, block(1)), (packed, block(2))],
        [
            (
                (items, seq_rows, width),
                low,
                pl.BlockSpec((1, seq_rows, group * PAIR), lambda n, h: (n, 0, h)),
            ),
            (
                (items, pairs, 8, seq_rows),
                full,
                pl.BlockSpec((1, group, 8, seq_rows), lambda n, h: (n, h, 0, 0)),
            ),
        ],
        "attend",
        10,
        spare=14,
    )


def attend_back(packed, grad_mixed, totals, lengths, items, seq_rows):
    width = packed.shape[-1]
    pairs, group = pairs_of(width)
    sides = [slice(0, PATCHES), slice(PATCHES, seq_rows)]

    def body(length_ref, q_ref, k_ref, v_ref, g_ref, total_ref, out_ref):
        row = PATCHES + lax.broadcasted_iota(jnp.int32, (seq_rows - PATCHES, seq_rows), 0)
        counts = row < length_ref[pl.program_id(0)]
        for pair in range(group):
            columns = slice(pair * PAIR, (pair + 1) * PAIR)
            queries, keys, values = q_ref[0, 0, :, columns], k_ref[0, 0, :, columns], v_ref[0, 0, :, columns]
            upstream = g_ref[0, :, columns]
            grad_queries = jnp.zeros((PAIR, seq_rows), full)
            grad_keys, grad_values = [0.0, 0.0], [0.0, 0.0]
            for head, lanes in enumerate(head_masks(seq_rows)):
                own_queries = jnp.where(lanes, queries, 0)
                own_upstream = jnp.where(lanes, upstream, 0)
                own_keys = jnp.where(lanes, keys, 0)
                parts, centre = [], 0.0
                for side, rows in enumerate(sides):
                    scores = dot(keys[rows], own_queries, (1, 1))
                    if side:
                        scores = jnp.where(counts, scores, masked_score)
                    probs = jnp.exp(scores - total_ref[0, pair, head : head + 1])
                    grad_probs = dot(values[rows], own_upstream, (1, 1))
                    centre += jnp.sum(grad_probs * probs, axis=0, keepdims=True)
                    parts.append((probs, grad_probs))
                for side, (probs, grad_probs) in enumerate(parts):
                    grad_scores = (probs * (grad_probs - centre)).astype(low)
                    grad_values[side] += dot(probs.astype(low), own_upstream)
                    grad_keys[side] += dot(grad_scores, own_queries)
                    grad_queries += dot(own_keys[sides[side]], grad_scores, (0, 0))
            out_ref[0, 0, :, columns] = (grad_queries.T * HEAD_DIM ** (-0.5)).astype(low)
            for side, rows in enumerate(sides):
                out_ref[1, 0, rows, columns] = grad_keys[side].astype(low)
                out_ref[2, 0, rows, columns] = grad_values[side].astype(low)

    def block(which):
        return pl.BlockSpec((1, 1, seq_rows, group * PAIR), lambda n, h: (which, n, 0, h))

    return call(
        body,
        (items, pairs // group),
        [
            (lengths, SCALARS),
            (packed, block(0)),
            (packed, block(1)),
            (packed, block(2)),
            (grad_mixed, pl.BlockSpec((1, seq_rows, group * PAIR), lambda n, h: (n, 0, h))),
            (totals, pl.BlockSpec((1, group, 8, seq_rows), lambda n, h: (n, h, 0, 0))),
        ],
        [
            (
                (3, items, seq_rows, width),
                low,
                pl.BlockSpec((3, 1, seq_rows, group * PAIR), lambda n, h: (0, n, 0, h)),
            ),
        ],
        "attend_back",
        15,
        spare=14,
    )[0]


def gelu_parts(before):
    decay = jnp.exp(before * before * -0.5)
    inverse = pl.reciprocal(1.0 + (0.3275911 * 0.5**0.5) * jnp.abs(before), approx=False)
    series = 1.061405429 * 0.5
    for term in (-1.453152027, 1.421413741, -0.284496736, 0.254829592):
        series = series * inverse + term * 0.5
    below = series * inverse * decay
    share = jnp.where(before >= 0, 1.0 - below, below)
    return before * share, share + before * decay * 0.3989422804014327


def feed_forward(inputs, mixed, out_weight, out_bias, gain, shift, up_weight, up_bias, down_weight, down_bias, lengths=None):
    rows, width = inputs.shape
    steps = up_weight.blocks
    hidden = steps * width

    def body(ready, held, x_ref, o_ref, ob_ref, gain_ref, shift_ref, ub_ref, db_ref, *rest):
        m_ref, a_ref, g_ref, s_ref, y_ref, total = rest[-6:]
        step = pl.program_id(0)

        @pl.when(step == 0)
        def _():
            ready(0, then=True)
            middle = x_ref[...].astype(full) + dot(o_ref[...], held[0][0]) + ob_ref[...]
            m_ref[...] = middle
            normed, _ = normalize(middle)
            a_ref[...] = (normed * gain_ref[...] + shift_ref[...]).astype(low)
            total[...] = middle + db_ref[...]

        ready(1, step)
        before = dot(a_ref[...], held[1][step]) + ub_ref[...]
        value, slope = gelu_parts(before)
        g_ref[...] = value.astype(low)
        s_ref[...] = slope.astype(low)

        @pl.when(step == 0)
        def _():
            ready(2)

        total[...] += dot(g_ref[...], held[2][0, pl.ds(pl.multiple_of(step * width, width), width)])

        @pl.when(step == steps - 1)
        def _():
            if lengths is None:
                y_ref[...] = total[...].astype(low)
            else:
                length = rows // lengths.shape[0]
                row = lax.broadcasted_iota(jnp.int32, (length, width), 0)
                for item in range(lengths.shape[0]):
                    at = slice(item * length, (item + 1) * length)
                    y_ref[at] = jnp.where(row < rest[0][item], total[at], 0.0).astype(low)

    return weighted(
        body,
        [out_weight, up_weight, down_weight],
        (steps,),
        [
            (inputs, whole((rows, width))),
            (mixed, whole((rows, width))),
            (out_bias, whole((1, width))),
            (gain, whole((1, width))),
            (shift, whole((1, width))),
            (up_bias, pl.BlockSpec((1, width), lambda j: (0, j))),
            (down_bias, whole((1, width))),
        ]
        + ([] if lengths is None else [(lengths, SCALARS)]),
        [
            ((rows, width), full, whole((rows, width))),
            ((rows, width), low, whole((rows, width))),
            ((rows, hidden), low, pl.BlockSpec((rows, width), lambda j: (0, j))),
            ((rows, hidden), low, pl.BlockSpec((rows, width), lambda j: (0, j))),
            ((rows, width), low, whole((rows, width))),
        ],
        "feed_forward",
        23,
        scratch=[pltpu.VMEM((rows, width), full)],
        first=((0, 0), (1, 0)),
    )


def feed_forward_back(upstream, rounded, slope, down_weight, up_weight, middle, gain, out_weight):
    rows, width = upstream.shape
    steps = up_weight.blocks
    hidden = steps * width

    def body(ready, held, y_ref, dz_ref, s_ref, m_ref, gain_ref, du_ref, dm_ref, db_ref, do_ref, sums_ref, total):
        step = pl.program_id(0)

        @pl.when(step == 0)
        def _():
            sums_ref[0:1] = column_sum(dz_ref[...])
            total[...] = jnp.zeros_like(total)
            ready(0, then=True)

        down = held[0][0, pl.ds(pl.multiple_of(step * width, width), width)]
        grad = (dot(dz_ref[...], down, (1, 1)) * s_ref[...].astype(full)).astype(low)
        du_ref[...] = grad
        sums_ref[pl.ds(4 + step, 1)] = column_sum(grad)
        ready(1, step)
        total[...] += dot(grad, held[1][step], (1, 1))

        @pl.when(step == steps - 1)
        def _():
            grad_second = total[...]
            normed, factor = normalize(m_ref[...])
            sums_ref[1:2] = column_sum(grad_second * normed)
            sums_ref[2:3] = column_sum(grad_second)
            grad_middle = y_ref[...].astype(full) + normalize_back(grad_second * gain_ref[...], normed, factor)
            dm_ref[...] = grad_middle
            branch = grad_middle.astype(low)
            db_ref[...] = branch
            sums_ref[3:4] = column_sum(branch)
            ready(2)
            do_ref[...] = dot(branch, held[2][0], (1, 1)).astype(low)

    return weighted(
        body,
        [down_weight, up_weight, out_weight],
        (steps,),
        [
            (upstream, whole((rows, width))),
            (rounded, whole((rows, width))),
            (slope, pl.BlockSpec((rows, width), lambda j: (0, j))),
            (middle, whole((rows, width))),
            (gain, whole((1, width))),
        ],
        [
            ((rows, hidden), low, pl.BlockSpec((rows, width), lambda j: (0, j))),
            ((rows, width), full, whole((rows, width))),
            ((rows, width), low, whole((rows, width))),
            ((rows, width), low, whole((rows, width))),
            ((4 + steps, width), full, whole((4 + steps, width))),
        ],
        "feed_forward_back",
        21,
        scratch=[pltpu.VMEM((rows, width), full)],
        first=((0, 0), (1, 0)),
    )


def project_back(grad_packed, weight, inputs, gain, grad_middle, join_weight=None):
    rows, width = inputs.shape
    joined = join_weight is not None

    def body(ready, held, g_ref, x_ref, gain_ref, dm_ref, *rest):
        if joined:
            de_ref, dx_ref, dz_ref, skip_ref, sums_ref, total = rest
        else:
            dx_ref, sums_ref, total = rest
        step = pl.program_id(0)

        @pl.when(step == 0)
        def _():
            total[...] = jnp.zeros_like(total)
            ready(0, 0, then=True)

        @pl.when(step > 0)
        def _():
            ready(0, step)

        total[...] += dot(g_ref[0], held[0][step], (1, 1))

        @pl.when(step == 2)
        def _():
            grad_first = total[...]
            normed, factor = normalize(x_ref[...].astype(full))
            sums_ref[0:1] = column_sum(grad_first * normed)
            sums_ref[1:2] = column_sum(grad_first)
            grad = dm_ref[...] + normalize_back(grad_first * gain_ref[...], normed, factor)
            if joined:
                entry = grad.astype(low)
                de_ref[...] = entry
                sums_ref[2:3] = column_sum(entry)
                ready(1)
                grad = dot(entry, held[1][0, :width], (1, 1))
                dx_ref[...] = grad
                dz_ref[...] = grad.astype(low)
                skip_ref[...] = dot(entry, held[1][0, width:], (1, 1))
            else:
                dx_ref[...] = grad

    ins = [
        (grad_packed, pl.BlockSpec((1, rows, width), lambda j: (j, 0, 0))),
        (inputs, whole((rows, width))),
        (gain, whole((1, width))),
        (grad_middle, whole((rows, width))),
    ]
    outs = [((rows, width), full, whole((rows, width))), ((8, width), full, whole((8, width)))]
    if joined:
        rounded = ((rows, width), low, whole((rows, width)))
        outs = [rounded, outs[0], rounded, outs[0], outs[1]]
    return weighted(
        body,
        [weight] + ([join_weight] if joined else []),
        (3,),
        ins,
        outs,
        "project_back",
        13 if joined else 9,
        scratch=[pltpu.VMEM((rows, width), full)],
    )


def picked(body, which, grid, ins, outs, name, micros, aliases=None, spare=4):
    return pl.pallas_call(
        body,
        grid_spec=pltpu.PrefetchScalarGridSpec(
            num_scalar_prefetch=1,
            grid=grid,
            in_specs=[spec for _, spec in ins],
            out_specs=[spec for _, _, spec in outs],
        ),
        out_shape=[jax.ShapeDtypeStruct(shape, kind) for shape, kind, _ in outs],
        name=name,
        input_output_aliases={place + 1: out for place, out in (aliases or {}).items()},
        cost_estimate=cost(micros),
        compiler_params=pltpu.CompilerParams(vmem_limit_bytes=room(ins, outs, (), spare)),
    )(which, *[array for array, _ in ins])


def far(array):
    return pltpu.with_memory_space_constraint(array, pltpu.HBM)


def quarters(rows, width, narrow_rows):
    shape = (lax.axis_size("narrow") // 2 * narrow_rows, width)
    return [(shape, low, pl.BlockSpec(shape, lambda g, core: (0, 0)))] * 4


def up_term(left, right, core):
    rows, width = left.shape
    part = width // lax.axis_size("narrow")
    half = width // 2

    def body(core_ref, l_ref, r_ref, *outs):
        value = dot(l_ref[...], r_ref[...], (0, 0)).astype(low)
        for block in range(2):

            @pl.when(pl.program_id(0) == block)
            def _():
                outs[block][...] = value[:half]
                outs[2 + block][...] = value[half:]

    return picked(
        body,
        core,
        (2,),
        [
            (left, pl.BlockSpec((rows, width), lambda g, core: (0, 0))),
            (far(right), pl.BlockSpec((rows, width), lambda g, core: (0, core[0] * 2 + g))),
        ],
        quarters(rows, width, part),
        "up_term",
        3.5,
    )


def qkv_out_term(first, packed, mixed, branch, core):
    rows, width = first.shape
    part = width // lax.axis_size("narrow")
    half = width // 2

    def body(core_ref, l_ref, r_ref, o_ref, b_ref, *outs):
        step = pl.program_id(0)
        last = core_ref[0] * 2 + step == 3

        def put(block, value):
            outs[block][...] = value[:half]
            outs[2 + block][...] = value[half:]

        @pl.when(last)
        def _():
            put(1, dot(o_ref[...], b_ref[...], (0, 0)).astype(low))

        @pl.when(jnp.logical_not(last))
        def _():
            value = dot(l_ref[...], r_ref[0], (0, 0)).astype(low)
            for block in range(2):

                @pl.when(step == block)
                def _():
                    put(block, value)

    flat = pl.BlockSpec((rows, width), lambda g, core: (0, 0))
    return picked(
        body,
        core,
        (2,),
        [
            (first, flat),
            (packed, pl.BlockSpec((1, rows, width), lambda g, core: (jnp.minimum(core[0] * 2 + g, 2), 0, 0))),
            (mixed, flat),
            (branch, flat),
        ],
        quarters(rows, width, part),
        "qkv_out_term",
        3.5,
    )


def down_term(left, right, core):
    rows, width = right.shape
    shares = lax.axis_size("narrow")
    part = left.shape[1] // (2 * shares)
    direct = part == width
    if not direct:
        left = left.reshape(rows, shares, 2, 2, part // 2)
        left = lax.dynamic_index_in_dim(left, core[0], 2, keepdims=False)
        left = left.reshape(rows, 2, shares // 2, 2, part // 2).swapaxes(2, 3).reshape(rows, 2 * width)
    half = width // 2

    def body(core_ref, l_ref, r_ref, *outs):
        value = dot(l_ref[...], r_ref[...], (0, 0)).astype(low)
        for owner in range(2):

            @pl.when(pl.program_id(0) == owner)
            def _():
                outs[2 * owner][...] = value[:half]
                outs[2 * owner + 1][...] = value[half:]

    return picked(
        body,
        core,
        (2,),
        [
            (far(left), pl.BlockSpec((rows, width), lambda g, core: (0, g * 2 + core[0] if direct else g))),
            (right, pl.BlockSpec((rows, width), lambda g, core: (0, 0))),
        ],
        quarters(rows, width, part // 2),
        "down_term",
        3.5,
    )


def join_term(middle, skip, right, core):
    rows, width = right.shape
    shares = lax.axis_size("narrow")
    part = width // shares
    half = width // 2
    if part != half:
        left = jnp.concatenate([middle, skip], axis=1).reshape(rows, shares, 2, 2, part // 2)
        left = lax.dynamic_index_in_dim(left, core[0], 2, keepdims=False)
        left = left.reshape(rows, 2, shares // 2, 2, part // 2).swapaxes(2, 3).reshape(rows, width)
        middle, skip = left[:, :half], left[:, half:]

    def body(core_ref, m_ref, s_ref, r_ref, *outs):
        for owner, left_ref in enumerate((m_ref, s_ref)):
            value = dot(left_ref[...], r_ref[...], (0, 0)).astype(low)
            outs[2 * owner][...] = value[: half // 2]
            outs[2 * owner + 1][...] = value[half // 2 :]

    side = pl.BlockSpec((rows, half), lambda g, core: (0, core[0] if part == half else 0))
    return picked(
        body,
        core,
        (1,),
        [(middle, side), (skip, side), (right, pl.BlockSpec((rows, width), lambda g, core: (0, 0)))],
        quarters(rows, width, part // 2),
        "join_term",
        2,
    )


def cross(bit, *pieces):
    kept, got = pieces[: len(pieces) // 2], pieces[len(pieces) // 2 :]
    rows, columns = kept[0].shape
    blocks = len(kept) // 2
    steps = 2 if rows % 32 == 0 else 1

    def body(bit_ref, *refs):
        sent_ref, left_ref = refs[-2:]

        def put(target, owner):
            for block in range(blocks):
                place = owner * blocks + block
                one, two = refs[place], refs[2 * blocks + place]
                target[block] = (one[...].astype(full) + two[...].astype(full)).astype(low)

        for mine in range(2):

            @pl.when(bit_ref[0] == mine)
            def _():
                put(sent_ref, 1 - mine)
                put(left_ref, mine)

    ins = [(piece, pl.BlockSpec((rows // steps, columns), lambda g, bit: (g, 0))) for piece in kept + got]
    out = ((blocks, rows, columns), low, pl.BlockSpec((blocks, rows // steps, columns), lambda g, bit: (0, g, 0)))
    return picked(body, bit, (steps,), ins, [out, out], "cross", 2)


def add_halve(bit, *pairs):
    lead, columns = pairs[0].shape[0], pairs[0].shape[-1]
    sizes = [pair.shape[2] for pair in pairs[::2]]
    total = sum(sizes)
    steps = 2 if len(sizes) == 1 and total % 32 == 0 and total >= 256 else 1

    def body(bit_ref, *refs):
        mine = bit_ref[0]
        for target, place in ((refs[-2], 1 - mine), (refs[-1], mine)):
            begin = 0
            for kept_ref, got_ref in zip(refs[:-2:2], refs[1:-2:2]):
                length = kept_ref.shape[2]
                for each in range(lead):
                    value = kept_ref[each, place].astype(full) + got_ref[each, place].astype(full)
                    target[each, begin : begin + length] = value.astype(low)
                begin += length

    ins = [
        (pair, pl.BlockSpec((lead, 2, pair.shape[2] // steps, columns), lambda g, bit: (0, 0, g, 0)))
        for pair in pairs
    ]
    out = (
        (lead, total, columns),
        low,
        pl.BlockSpec((lead, total // steps, columns), lambda g, bit: (0, g, 0)),
    )
    return picked(body, bit, (steps,), ins, [out, out], "add_halve", 2)


def add_into(target, place, count, one, two):
    rows, columns = one.shape[-2:]
    steps = 2 if rows % 32 == 0 else 1
    block = pl.BlockSpec((1, rows // steps, columns), lambda g: (0, g, 0))

    def body(one_ref, two_ref, *rest):
        rest[-1][...] = (one_ref[...].astype(full) + two_ref[...].astype(full)).astype(low)

    ins = [one.reshape(1, rows, columns), two.reshape(1, rows, columns)]
    return pl.pallas_call(
        body,
        grid=(steps,),
        in_specs=[block, block] + ([] if target is None else [ANY]),
        out_specs=pl.BlockSpec((1, rows // steps, columns), lambda g: (place, g, 0)),
        out_shape=jax.ShapeDtypeStruct((count, rows, columns), low),
        name="add_into",
        input_output_aliases={} if target is None else {2: 0},
        cost_estimate=cost(1.3),
    )(*ins, *([] if target is None else [target]))


def add(one, two):
    return (one.astype(full) + two.astype(full)).astype(low)


def pair_up(own, got, bit):
    rows, columns = own.shape

    def body(bit_ref, own_ref, got_ref, out_ref):
        mine = bit_ref[0]
        out_ref[mine] = own_ref[...]
        out_ref[1 - mine] = got_ref[...]

    flat = pl.BlockSpec((rows, columns), lambda g, bit: (0, 0))
    out = ((2, rows, columns), low, pl.BlockSpec((2, rows, columns), lambda g, bit: (0, 0, 0)))
    return picked(body, bit, (1,), [(own, flat), (got, flat)], [out], "pair_up", 1)[0]


def finish(kind, half, own, got, begin, length, core, layer, targets):
    pieces, _, columns = own.shape
    scale = 1.0 / lax.axis_size("wide")
    aliases = {place + 2: place for place in range(len(targets))}
    source = pl.BlockSpec((pieces, length, columns), lambda g, core: (0, begin // length, 0))
    ins = [(own, source), (got, source)] + [(target, ANY) for target in targets]
    rows = pieces * length

    def chosen(core_ref, which, own_ref, got_ref, place=None):
        sides = [own_ref, got_ref]
        if place is None:
            values = [side[...].reshape(pieces * length, columns) for side in sides]
        else:
            if pieces == 1:
                near = (0, pl.ds(place * (length // 2), length // 2))
            else:
                near = (pl.ds(place * (pieces // 2), pieces // 2),)
            values = [side[near].reshape(pieces * length // 2, columns) for side in sides]
        return jnp.where(core_ref[0] == which, values[0], values[1]).astype(full) * scale

    if kind in ("down", "join"):

        def body(core_ref, own_ref, got_ref, *rest):
            rest[-1][0] = chosen(core_ref, pl.program_id(0), own_ref, got_ref)

        place = layer if kind == "down" else 0
        shape = (2 if kind == "down" else 1, 2 * rows, columns)
        out = (shape, full, pl.BlockSpec((1, rows, columns), lambda g, core: (place, g, 0)))
        return picked(body, core, (2,), ins, [out], "finish_rows", 3, aliases)
    steps = 4 if half is None else 2
    rows = rows // 2 if half is None else rows

    def block(step):
        return step if half is None else 2 * step + half

    def values_of(core_ref, own_ref, got_ref):
        step = pl.program_id(0)
        if half is None:
            return chosen(core_ref, step // 2, own_ref, got_ref, step % 2)
        return chosen(core_ref, step, own_ref, got_ref)

    def body(core_ref, own_ref, got_ref, *rest):
        values = values_of(core_ref, own_ref, got_ref)
        if kind == "up":
            rest[-1][0] = values
            return
        if half == 0:
            rest[-1][0] = values
            return
        last = block(pl.program_id(0)) == 3

        @pl.when(jnp.logical_not(last))
        def _():
            rest[-2][0] = values

        @pl.when(last)
        def _():
            rest[-1][0] = values

    if kind == "up":
        outs = [((2, rows, 4 * columns), full, pl.BlockSpec((1, rows, columns), lambda g, core: (layer, 0, block(g))))]
        return picked(body, core, (steps,), ins, outs, "finish_columns", 3, aliases)

    def spot(step):
        return block(step if half == 0 else jnp.minimum(step, steps - 2))

    outs = [
        ((2, rows, 3 * columns), full, pl.BlockSpec((1, rows, columns), lambda g, core: (layer, 0, spot(g)))),
        ((2, rows, columns), full, pl.BlockSpec((1, rows, columns), lambda g, core: (layer, 0, 0))),
    ]
    if half == 0:
        kept = targets[1:]
        ins, outs, aliases = ins[:3] if targets else ins, outs[:1], {2: 0} if targets else {}
        return (picked(body, core, (steps,), ins, outs, "finish_qkv", 3, aliases)[0], *kept)
    return picked(body, core, (steps,), ins, outs, "finish_qkv_out", 3, aliases)


def small_gradients(total, me, width, shares, blocks):
    part = width // shares
    scale = 1.0 / lax.axis_size("wide")

    def body(me_ref, total_ref, gains_ref, shifts_ref, out_ref, up_ref, down_ref, join_ref):
        values = total_ref[...] * scale
        back = [values[0:8], values[8:16]]
        ahead = [values[16 : 20 + blocks], values[20 + blocks : 24 + 2 * blocks]]
        for place in range(shares):

            @pl.when(me_ref[0] == place)
            def _():
                columns = slice(place * part, place * part + part)
                for layer in range(2):
                    for row, target in ((0, gains_ref), (1, shifts_ref)):
                        target[layer, 0:1] = back[layer][row : row + 1, columns]
                        target[layer, 1:2] = ahead[layer][row + 1 : row + 2, columns]
                    out_ref[layer : layer + 1] = ahead[layer][3:4, columns]
                    down_ref[layer : layer + 1] = ahead[layer][0:1, columns]
                    begin = place * part * blocks
                    while begin < (place + 1) * part * blocks:
                        row, column = begin // width, begin % width
                        length = min(width - column, (place + 1) * part * blocks - begin)
                        at = begin - place * part * blocks
                        piece = ahead[layer][4 + row : 5 + row, column : column + length]
                        up_ref[layer : layer + 1, at : at + length] = piece
                        begin += length
                join_ref[...] = back[1][2:3, columns]

    shapes = [(2, 2, part), (2, 2, part), (2, part), (2, part * blocks), (2, part), (1, part)]
    outs = [(shape, full, pl.BlockSpec(shape, lambda g, me, n=len(shape): (0,) * n)) for shape in shapes]
    ins = [(total, pl.BlockSpec(total.shape, lambda g, me: (0, 0)))]
    return picked(body, me, (1,), ins, outs, "small_gradients", 1)


def after(value, *earlier):
    return lax.optimization_barrier((value,) + earlier)[0] if earlier else value


def swap(values, axis, mask):
    size = lax.axis_size(axis)
    return lax.ppermute(values, axis, [(source, source ^ mask) for source in range(size)])


def masks(axis):
    return [1 << bit for bit in range(lax.axis_size(axis).bit_length() - 1)]


class Order:
    def __init__(self):
        self.last = ()

    def run(self, function, *arrays):
        held = lax.optimization_barrier(tuple(arrays) + self.last)[: len(arrays)]
        out = function(*held)
        self.last = (jax.tree.leaves(out)[0],)
        return out

    def mark(self, value):
        return self.run(lambda x: x + 1, value)

    def hold(self, *arrays):
        self.last += arrays


def place_bit(axis, mask):
    return ((lax.axis_index(axis) & mask) // mask).astype(jnp.int32).reshape(1)


class Term:
    def __init__(self, order, kind, layer, function, *arrays):
        self.order, self.kind, self.layer, self.half = order, kind, layer, None
        self.core = place_bit("wide", 1)
        sent = order.run(lambda *x: function(*x, 1 - self.core), *arrays)
        self.got = [swap(each, "wide", 1) for each in sent]
        self.columns = sent[0].shape[-1]
        self.keep = lambda: order.run(lambda *x: function(*x, self.core), *arrays)

    def stay(self):
        self.kept, self.keep = self.keep(), None

    def part(self, half):
        other = copy.copy(self)
        other.kept, other.got, other.half = self.kept[half::2], self.got[half::2], half
        return other

    def pass_narrow(self):
        stages = list(reversed(masks("narrow")))
        if isinstance(self.kept, (list, tuple)):
            bit = place_bit("narrow", stages[0])
            blocks = len(self.kept) // 2
            sent, self.kept = self.order.run(lambda *x: cross(bit, *x), *self.kept, *self.got)
            self.got = swap(sent, "narrow", stages.pop(0))
        else:
            blocks = 1
        for mask in stages:
            pairs = [(self.kept, self.got)]
            self.kept, self.got = halve(self.order, "narrow", mask, blocks, pairs, self.columns)

    def pass_first(self, mask):
        swapped = [self.kept[owner * 2 + block] for block in range(2) for owner in range(2)]
        brought = [self.got[owner * 2 + block] for block in range(2) for owner in range(2)]
        bit = place_bit("wide", mask)
        sent, self.kept = self.order.run(lambda *x: cross(bit, *x), *swapped, *brought)
        self.got = swap(sent, "wide", mask)

    def pass_wide(self, mask):
        pairs = list(zip(self.kept, self.got)) if isinstance(self.kept, (list, tuple)) else [(self.kept, self.got)]
        self.kept, self.got = halve(self.order, "wide", mask, 1, pairs, self.columns)

    def add_into(self, target, place, count):
        kept, got = [side.reshape(-1, self.columns) for side in (self.kept, self.got)]
        if target is None:
            return self.order.run(lambda one, two: add_into(None, place, count, one, two), kept, got)
        return self.order.run(lambda target, one, two: add_into(target, place, count, one, two), target, kept, got)

    def finish(self, done, own, got, begin, length):
        targets = done.get(self.kind, ())

        def last(own, got, core, *targets):
            return finish(self.kind, self.half, own, got, begin, length, core, self.layer, targets)

        done[self.kind] = self.order.run(last, own, got, self.core, *targets)


def halve(order, axis, mask, lead, pairs, columns):
    shaped = [array.reshape(lead, 2, -1, columns) for pair in pairs for array in pair]
    bit = place_bit(axis, mask)
    sent, kept = order.run(lambda *x: add_halve(bit, *x), *shaped)
    return kept, swap(sent, axis, mask)


class Reduce:
    def __init__(self, order, terms, passed=(), late=()):
        self.order, self.terms = order, terms
        rest = [mask for mask in masks("wide")[1:] if mask not in passed]
        self.down = [mask for mask in rest if mask not in late] + [mask for mask in rest if mask in late]
        self.up = list(reversed(passed))
        self.pieces, self.columns = 2 ** len(passed), terms[0].columns
        self.parts = [(term.kept, term.got) for term in terms]
        self.lengths, self.first = [each.size // self.columns for each, _ in self.parts], True
        self.joining, self.closed = None, False

    def step(self):
        if self.closed:
            return
        if self.down:
            mask = self.down.pop(0)
            rows = [kept.size // self.columns for kept, _ in self.parts]
            even = all(each % 32 == 0 for each in rows) and bool(self.down)
            if self.first and even:
                self.pieces, self.lengths = 2 * self.pieces, [each // 2 for each in rows]
            self.first = False
            if even:
                self.up.insert(0, mask)
                self.parts = [halve(self.order, "wide", mask, 1, self.parts, self.columns)]
            else:
                flat = [[side.reshape(-1, self.columns) for side in pair] for pair in self.parts]
                pair = [jnp.concatenate(sides) for sides in zip(*flat)]
                total = self.order.run(add, *pair)
                self.parts = [(total, swap(total, "wide", mask))]
            return
        kept, got = [array.reshape(-1, self.columns) for array in self.parts[0]]
        if self.joining is None:
            total = self.order.run(add, kept, got)
        else:
            bit = place_bit("wide", self.joining)
            total = self.order.run(lambda *x: pair_up(*x, bit), kept, got).reshape(-1, self.columns)
        if self.up:
            self.joining = self.up.pop(0)
            self.parts = [(total, swap(total, "wide", self.joining))]
        else:
            self.parts = [(total, swap(total, "wide", 1))]
            self.closed = True

    def finish(self, done):
        own, got = [array.reshape(self.pieces, -1, self.columns) for array in self.parts[0]]
        begin = 0
        for term, length in zip(self.terms, self.lengths):
            term.finish(done, own, got, begin, length)
            begin += length


def on_device(
    tokens,
    skip,
    flags,
    cotangent,
    norm_gains,
    norm_biases,
    qkv_weight,
    out_weight,
    out_bias,
    up_weight,
    up_bias,
    down_weight,
    down_bias,
    skip_weight,
    skip_bias,
):
    items, seq_rows, width = tokens.shape
    rows = items * seq_rows
    me = lax.axis_index("narrow")
    shares = lax.axis_size("narrow")
    spots = jnp.stack([me, lax.axis_index("wide")]).astype(jnp.int32)
    order = Order()

    def fetches(layer):
        return (
            Fetch([(qkv_weight, layer)], (1, 2)),
            Fetch([(out_weight, layer), (up_weight, layer)], (1, 2)),
            Fetch([(down_weight, layer)], (1, 4)),
        )

    fetch_qkv0, fetch_up0, fetch_down0 = fetches(0)
    fetch_qkv1, fetch_up1, fetch_down1 = fetches(1)
    fetch_join = Fetch([(skip_weight, None)], (1, 4))
    qkv0, qkv1 = [Weight(each, 0, width, spots) for each in (fetch_qkv0, fetch_qkv1)]
    out0, out1 = [Weight(each, 0, width, spots) for each in (fetch_up0, fetch_up1)]
    up0, up1 = [Weight(each, 1, width, spots) for each in (fetch_up0, fetch_up1)]
    down0, down1 = [Weight(each, 0, width, spots) for each in (fetch_down0, fetch_down1)]
    join = Weight(fetch_join, 0, width, spots)

    small = (norm_gains, norm_biases, out_bias, down_bias, skip_bias, up_bias)
    fetch_qkv0.cut()
    fetch_qkv0.fetch()
    held = order.run(pack_small, *[after(piece, fetch_qkv0.sent) for piece in small])[None]
    for mask in masks("narrow"):
        held = jnp.concatenate([held, swap(held, "narrow", mask)])
    last = order.last
    for each in (fetch_up0, fetch_down0, fetch_join, fetch_qkv1, fetch_up1, fetch_down1):
        each.cut(*last)
        last = (each.sent,)
    fetch_up0.fetch()
    fetch_down0.fetch(fetch_up0.sent)
    fetch_join.fetch(fetch_down0.sent)
    fetch_qkv1.fetch(fetch_join.sent)
    place = me.astype(jnp.int32).reshape(1)
    lines = order.run(lambda x: unpack_small(x, place, small, width), held)

    def line(row):
        return lines[row : row + 1]

    gains, shifts = [[line(2 * layer + each) for each in range(2)] for layer in range(2)], None
    shifts = [[line(4 + 2 * layer + each) for each in range(2)] for layer in range(2)]
    out_biases, down_biases, join_shift = [line(8), line(9)], [line(10), line(11)], line(12)
    blocks = up0.blocks
    up_biases = [lines[13 + layer * blocks : 13 + (layer + 1) * blocks].reshape(1, -1) for layer in range(2)]

    tokens_flat, skip_flat, cotangent_flat = [array.reshape(rows, width) for array in (tokens, skip, cotangent)]
    lengths = PATCHES + 1 + CAPTION * flags
    valid = lax.broadcasted_iota(jnp.int32, (items, seq_rows), 1) < lengths[:, None]
    dz1 = order.run(lambda x: jnp.where(valid.reshape(rows, 1), x, 0), after(cotangent_flat, fetch_down1.sent))

    fetch_qkv0.share(1)
    fetch_qkv0.share(0)
    order.hold(*fetch_up0.got())
    fetch_up0.share(1)
    a0, packed0 = order.run(lambda *x: project_qkv(*x, qkv0), tokens_flat, gains[0][0], shifts[0][0])
    order.hold(*fetch_down0.got())
    fetch_down0.share(1, a0)
    fetch_up1.fetch(a0)
    fetch_down1.fetch(a0)
    packed0 = packed0.reshape(3, items, seq_rows, width)
    mixed0, totals0 = order.run(lambda *x: attend(*x, items, seq_rows), packed0, lengths)
    order.hold(*fetch_join.got(), *fetch_qkv1.got())
    there = order.mark(spots)
    fetch_up0.share(0, there)
    fetch_down0.share(0, there)
    fetch_join.share(1, there)
    fetch_qkv1.share(1, there)
    mixed0 = mixed0.reshape(rows, width)
    m0, second0, hidden0, slope0, middle = order.run(
        lambda x, o, ob, g, s, ub, db: feed_forward(x, o, out0, ob, g, s, up0, ub, down0, db),
        tokens_flat, mixed0, out_biases[0], gains[0][1], shifts[0][1], up_biases[0], down_biases[0],
    )
    fetch_join.share(0, middle)
    fetch_qkv1.share(0, middle)
    order.hold(*fetch_up1.got(), *fetch_down1.got())
    fetch_up1.share(1, middle)
    fetch_down1.share(1, middle)
    entry, a1, packed1 = order.run(
        lambda m, s, jb, g, sh: join_qkv(m, s, join, jb, g, sh, qkv1),
        middle, skip_flat, join_shift, gains[1][0], shifts[1][0],
    )
    packed1 = packed1.reshape(3, items, seq_rows, width)
    mixed1, totals1 = order.run(lambda *x: attend(*x, items, seq_rows), packed1, lengths)
    fetch_up1.share(0, mixed1)
    fetch_down1.share(0, mixed1)
    mixed1 = mixed1.reshape(rows, width)
    m1, second1, hidden1, slope1, output = order.run(
        lambda x, o, ob, g, s, ub, db, k: feed_forward(x, o, out1, ob, g, s, up1, ub, down1, db, k),
        entry, mixed1, out_biases[1], gains[1][1], shifts[1][1], up_biases[1], down_biases[1], lengths,
    )

    done = {}
    term_down1 = Term(order, "down", 1, down_term, hidden1, dz1)
    term_down1.stay()
    term_down1.pass_narrow()
    du, dm, db, do, sums1 = order.run(
        lambda y, z, s, m, g: feed_forward_back(y, z, s, down1, up1, m, g, out1),
        dz1, dz1, slope1, m1, gains[1][1],
    )
    term_up1 = Term(order, "up", 1, up_term, second1, du)
    term_up1.stay()
    term_up1.pass_narrow()
    total = term_down1.add_into(None, 0, 3)
    dpacked = order.run(
        lambda *x: attend_back(*x, items, seq_rows), packed1, do.reshape(items, seq_rows, width), totals1, lengths
    )
    flat_packed = dpacked.reshape(3, rows, width)
    term_qkv1 = Term(order, "qkv", 1, qkv_out_term, a1, flat_packed, mixed1, db)
    term_qkv1.stay()
    term_qkv1.pass_narrow()
    total = term_up1.add_into(total, 1, 3)
    dentry, dmiddle, dz0, skip_grad, sums3 = order.run(
        lambda gp, x, g, dm: project_back(gp, qkv1, x, g, dm, join), flat_packed, entry, gains[1][0], dm
    )
    term_join = Term(order, "join", 1, join_term, middle, skip_flat, dentry)
    term_join.stay()
    term_join.pass_narrow()
    term_down0 = Term(order, "down", 0, down_term, hidden0, dz0)
    term_down0.stay()
    total = term_qkv1.add_into(total, 2, 3)
    size = lax.axis_size("wide")
    groups = [[device + core for device in range(0, size, 2)] for core in range(2)]
    flat_total = total.reshape(-1, width)
    part = lax.psum_scatter(flat_total, "wide", axis_index_groups=groups, scatter_dimension=0, tiled=True)
    term_down0.pass_first(2)

    du, dm, db, do, sums0 = order.run(
        lambda y, z, s, m, g: feed_forward_back(y, z, s, down0, up0, m, g, out0),
        dmiddle, dz0, slope0, m0, gains[0][1],
    )
    term_join.pass_wide(2)
    term_up0 = Term(order, "up", 0, up_term, second0, du)
    term_up0.stay()
    term_down0.pass_narrow()
    term_up0.pass_narrow()
    dpacked = order.run(
        lambda *x: attend_back(*x, items, seq_rows), packed0, do.reshape(items, seq_rows, width), totals0, lengths
    )
    order.hold(term_down0.got, term_join.got)
    flat_packed = dpacked.reshape(3, rows, width)
    term_qkv0 = Term(order, "qkv", 0, qkv_out_term, a0, flat_packed, mixed0, db)
    term_qkv0.stay()
    one, two = term_qkv0.part(0), term_qkv0.part(1)
    one.pass_narrow()
    two.pass_narrow()
    first = Reduce(order, [term_down0, term_join], (2,))
    first.step()
    second = Reduce(order, [term_up0])
    second.step()
    tokens_grad, sums2 = order.run(
        lambda gp, x, g, dm: project_back(gp, qkv0, x, g, dm), flat_packed, tokens_flat, gains[0][0], dm
    )
    minor = jnp.concatenate([sums2, sums3, sums0, sums1])
    places = masks("wide")
    minor_stages = [("narrow", mask) for mask in masks("narrow")]
    minor_stages += [("wide", mask) for mask in places if mask != 2] + [("wide", mask) for mask in places if mask == 2]
    minor_got = swap(minor, *minor_stages[0])

    def minor_step():
        nonlocal minor, minor_got
        if minor_stages:
            minor_stages.pop(0)
            minor = order.run(lambda one, two: one + two, minor, minor_got)
            if minor_stages:
                minor_got = swap(minor, *minor_stages[0])

    third = Reduce(order, [one])
    third.step()
    first.step()
    second.step()
    fourth = Reduce(order, [two])
    fourth.step()
    minor_step()
    third.step()
    first.step()
    second.step()
    order.hold(part)
    gathered = lax.all_gather(after(part, *order.last), "wide", axis_index_groups=groups, tiled=True)
    fourth.step()
    third.step()
    first.step()
    minor_step()
    fourth.step()
    second.step()
    third.step()
    minor_step()
    first.step()
    fourth.step()
    second.step()
    order.hold(gathered)
    other = swap(after(gathered, *order.last), "wide", 1)
    minor_step()
    first.finish(done)
    third.step()
    fourth.step()
    own, got = gathered.reshape(1, -1, width), other.reshape(1, -1, width)
    for which, term in enumerate((term_down1, term_up1, term_qkv1)):
        term.finish(done, own, got, which * (own.shape[1] // 3), own.shape[1] // 3)
    minor_step()
    second.step()
    third.step()
    second.finish(done)
    fourth.step()
    for each in (first, second, third, fourth):
        while not each.closed:
            each.step()
    while minor_stages:
        minor_step()
    third.finish(done)
    fourth.finish(done)
    small = order.run(lambda x: small_gradients(x, place, width, shares, up1.blocks), minor)

    return (
        output.reshape(tokens.shape),
        tokens_grad.reshape(tokens.shape),
        skip_grad.reshape(tokens.shape),
        small[0],
        small[1],
        done["qkv"][0],
        done["qkv"][1],
        small[2],
        done["up"][0],
        small[3],
        done["down"][0],
        small[4],
        done["join"][0][0],
        small[5].reshape(-1),
    )


def solution(mesh):
    placed = (
        P(("wide", "narrow"), None, None),
        P(("wide", "narrow"), None, None),
        P(("wide", "narrow")),
        P(("wide", "narrow"), None, None),
        P(None, None, "narrow"),
        P(None, None, "narrow"),
        P(None, "narrow", None),
        P(None, "narrow", None),
        P(None, "narrow"),
        P(None, "narrow", None),
        P(None, "narrow"),
        P(None, "narrow", None),
        P(None, "narrow"),
        P("narrow", None),
        P("narrow"),
    )
    return jax.shard_map(
        on_device,
        mesh=mesh,
        in_specs=placed,
        out_specs=(
            P(("wide", "narrow"), None, None),
            P(("wide", "narrow"), None, None),
            P(("wide", "narrow"), None, None),
            P(None, None, "narrow"),
            P(None, None, "narrow"),
            P(None, "narrow", None),
            P(None, "narrow", None),
            P(None, "narrow"),
            P(None, "narrow", None),
            P(None, "narrow"),
            P(None, "narrow", None),
            P(None, "narrow"),
            P("narrow", None),
            P("narrow"),
        ),
        check_vma=False,
    )
```

```python
import copy
import math

import jax
import jax.numpy as jnp
from jax import lax
from jax.experimental import pallas as pl
from jax.experimental.pallas import tpu as pltpu
from jax.sharding import PartitionSpec as P

HEAD_DIM = 64
PATCHES = 256
CAPTION = 77
PAIR = 2 * HEAD_DIM


epsilon = 1e-05
masked_score = -1e30
low = jnp.bfloat16
full = jnp.float32
SPARE = 14
ANY = pl.BlockSpec(memory_space=pltpu.HBM)
SCALARS = pl.BlockSpec(memory_space=pltpu.SMEM)


def dot(left, right, contract=(1, 0)):
    dims = (((contract[0],), (contract[1],)), ((), ()))
    return lax.dot_general(left, right, dims, preferred_element_type=full)


def normalize(values):
    centred = values - jnp.mean(values, axis=-1, keepdims=True)
    factor = lax.rsqrt(jnp.mean(centred * centred, axis=-1, keepdims=True) + epsilon)
    return centred * factor, factor


def normalize_back(upstream, normed, factor):
    return factor * (
        upstream
        - jnp.mean(upstream, axis=-1, keepdims=True)
        - normed * jnp.mean(upstream * normed, axis=-1, keepdims=True)
    )


def column_sum(values):
    return jnp.sum(values.astype(full), axis=0, keepdims=True)


def whole(shape):
    return pl.BlockSpec(shape, lambda *grid: (0,) * len(shape))


def cost(micros):
    return pl.CostEstimate(flops=int(micros * 3 * 10**8), bytes_accessed=0, transcendentals=0)


def room(ins, outs, scratch, spare):
    total = spare * 2**20
    for shape, kind, spec in [(array.shape, array.dtype, spec) for array, spec in ins] + list(outs):
        if spec.block_shape is not None and spec.memory_space is None:
            total += 2 * math.prod(spec.block_shape) * jnp.dtype(kind).itemsize
    for piece in scratch:
        if piece.memory_space == pltpu.VMEM:
            total += math.prod(piece.shape) * jnp.dtype(piece.dtype).itemsize
    return total


def call(body, grid, ins, outs, name, micros, scratch=(), spare=6):
    return pl.pallas_call(
        body,
        grid=grid,
        in_specs=[spec for _, spec in ins],
        out_specs=[spec for _, _, spec in outs],
        out_shape=[jax.ShapeDtypeStruct(shape, kind) for shape, kind, _ in outs],
        scratch_shapes=list(scratch),
        name=name,
        cost_estimate=cost(micros),
        compiler_params=pltpu.CompilerParams(vmem_limit_bytes=room(ins, outs, scratch, spare)),
    )(*[array for array, _ in ins])


class Fetch:
    def __init__(self, arrays, sharing):
        self.arrays, self.sharing = arrays, list(sharing)
        self.rows = arrays[0][0].shape[-2]
        while self.rows % (16 << len(self.sharing)):
            self.sharing.pop()
        self.length = self.rows >> len(self.sharing)

    def quarter(self, place):
        return sum(((place // mask) & 1) << bit for bit, mask in enumerate(self.sharing))

    def cut(self, *earlier):
        found = []
        for array, layer in self.arrays:
            array = after(array, *earlier)
            lead = () if layer is None else (layer,)
            begin = self.quarter(lax.axis_index("wide")) * self.length
            sizes = (1,) * len(lead) + (self.length, array.shape[-1])
            found.append(lax.dynamic_slice(array, lead + (begin, 0), sizes).reshape(self.length, -1))
        self.sent = (jnp.concatenate(found, axis=1) if len(found) > 1 else found[0])[None]

    def fetch(self, *earlier):
        held = after(self.sent, *earlier)
        for mask in masks("narrow"):
            held = jnp.concatenate([held, swap(held, "narrow", mask)])
        self.pieces = {0: held[1:]}

    def share(self, which, *earlier):
        if which < len(self.sharing):
            mask = self.sharing[which]
            got = {key ^ (1 << which): swap(after(piece, *earlier), "wide", mask) for key, piece in self.pieces.items()}
            self.pieces.update(got)

    def got(self):
        return list(self.pieces.values())


class Weight:
    def __init__(self, fetched, which, width, spots):
        self.fetched, self.spots, self.width = fetched, spots, width
        self.array, self.layer = fetched.arrays[which]
        self.begin = sum(array.shape[-1] for array, _ in fetched.arrays[:which])
        self.rows, columns = self.array.shape[-2:]
        self.shares = lax.axis_size("narrow")
        self.blocks = columns // width
        self.total = self.rows * self.shares

    def arrays(self):
        return [self.array] + self.fetched.got()

    def scratch(self):
        copies = 1 + len(self.fetched.pieces) * (self.shares - 1)
        return [pltpu.VMEM((self.blocks, self.total, self.width), low), pltpu.SemaphoreType.DMA((self.blocks, copies))]

    def copies(self, spots, refs, held, signals, block):
        own, pieces = refs[0], refs[1:]
        me, length = spots[0], self.fetched.length
        own = own if self.layer is None else own.at[self.layer]
        columns = pl.ds(block * self.width, self.width)
        begin = pl.multiple_of(me * self.rows, 16)
        found = [(own.at[:, columns], begin, self.rows)]
        columns = pl.ds(self.begin + block * self.width, self.width)
        for key, piece in zip(self.fetched.pieces, pieces):
            for offset in range(1, self.shares):
                begin = (me ^ offset) * self.rows + (self.fetched.quarter(spots[1]) ^ key) * length
                found.append((piece.at[offset - 1, :, columns], pl.multiple_of(begin, 16), length))
        return [
            pltpu.make_async_copy(source, held.at[block, pl.ds(begin, length)], signals.at[block, place])
            for place, (source, begin, length) in enumerate(found)
        ]

    def wait(self, *refs, block=0):
        for copy in self.copies(*refs, block):
            copy.wait()


def weighted(body, weights, grid, ins, outs, name, micros, scratch=(), first=((0, 0),), spare=SPARE):
    spots = weights[0].spots
    operands = [(spots, SCALARS)]
    for weight in weights:
        operands += [(pltpu.with_memory_space_constraint(array, pltpu.HBM), ANY) for array in weight.arrays()]
    counts = [len(weight.arrays()) for weight in weights]
    extra = [piece for weight in weights for piece in weight.scratch()]

    def wrapped(*refs):
        spots_ref, rest = refs[0], list(refs[1:])
        sources = []
        for count in counts:
            sources.append(rest[:count])
            rest = rest[count:]
        spare = rest[len(rest) - len(extra) :]
        rest = rest[: len(rest) - len(extra)]
        handles = []
        for place, weight in enumerate(weights):
            held, signals = spare[2 * place : 2 * place + 2]
            refs_of = (spots_ref, sources[place], held, signals)
            handles.append((weight, refs_of, held))

        everything = [(place, block) for place, weight in enumerate(weights) for block in range(weight.blocks)]

        def begin(wanted):
            for place, block in wanted:
                weight, refs_of, _ = handles[place]
                for copy in weight.copies(*refs_of, block):
                    copy.start()

        @pl.when(pl.program_id(0) == 0)
        def _():
            begin(first)

        def ready(place, block=0, then=False):
            weight, refs_of, held = handles[place]
            weight.wait(*refs_of, block=block)
            if then:
                begin([each for each in everything if each not in first])

        body(ready, [held for _, _, held in handles], *rest)

    return call(wrapped, grid, operands + ins, outs, name, micros, list(scratch) + extra, spare)


def pack_small(*small):
    part = small[0].shape[-1]
    counts = [piece.size // part for piece in small]

    def body(*refs):
        row = 0
        for ref in refs[:-1]:
            values = ref[...].reshape(-1, ref.shape[-1])
            for each in range(values.shape[0]):
                for begin in range(0, values.shape[1], part):
                    refs[-1][row : row + 1] = values[each : each + 1, begin : begin + part].astype(full)
                    row += 1
        refs[-1][row:] = jnp.zeros((refs[-1].shape[0] - row, part), full)

    flat = [piece.reshape((1,) * (2 - piece.ndim) + piece.shape) for piece in small]
    rows = -(-sum(counts) // 16) * 16
    out = ((rows, part), full, whole((rows, part)))
    return call(body, (1,), [(piece, whole(piece.shape)) for piece in flat], [out], "pack_small", 1)[0].astype(low)


def unpack_small(parts, me, small, width):
    shares, _, part = parts.shape
    lines = [(piece.size // piece.shape[-1], piece.shape[-1] // part) for piece in small]
    total = sum(count * many for count, many in lines)
    rows = -(-total // 8) * 8

    def body(me_ref, parts_ref, out_ref):
        values = parts_ref[...].astype(full)
        for mine in range(shares):

            @pl.when(me_ref[0] == mine)
            def _():
                for owner in range(shares):
                    source, target = 0, 0
                    for count, many in lines:
                        for each in range(count):
                            for piece in range(many):
                                at = owner * many * part + piece * part
                                row, column = target + at // width, at % width
                                line = values[owner ^ mine, source : source + 1]
                                out_ref[row : row + 1, column : column + part] = line
                                source += 1
                            target += many
        if rows > total:
            out_ref[total:] = jnp.zeros((rows - total, width), full)

    ins = [(parts, pl.BlockSpec(parts.shape, lambda g, me: (0, 0, 0)))]
    out = ((rows, width), full, pl.BlockSpec((rows, width), lambda g, me: (0, 0)))
    return picked(body, me, (1,), ins, [out], "unpack_small", 1)[0]


def project_qkv(inputs, gain, shift, weight):
    rows, width = inputs.shape

    def body(ready, held, x_ref, gain_ref, shift_ref, a_ref, out_ref):
        step = pl.program_id(0)

        @pl.when(step == 0)
        def _():
            normed, _ = normalize(x_ref[...].astype(full))
            a_ref[...] = (normed * gain_ref[...] + shift_ref[...]).astype(low)
            ready(0, 0, then=True)

        @pl.when(step > 0)
        def _():
            ready(0, step)

        scale = jnp.where(step == 0, HEAD_DIM ** (-0.5), 1.0)
        out_ref[0] = (dot(a_ref[...], held[0][step]).astype(low).astype(full) * scale).astype(low)

    return weighted(
        body,
        [weight],
        (3,),
        [
            (inputs, whole((rows, width))),
            (gain, whole((1, width))),
            (shift, whole((1, width))),
        ],
        [
            ((rows, width), low, whole((rows, width))),
            ((3, rows, width), low, pl.BlockSpec((1, rows, width), lambda j: (j, 0, 0))),
        ],
        "project_qkv",
        7,
    )


def join_qkv(middle, skip, join_weight, join_shift, gain, shift, weight):
    rows, width = middle.shape

    def body(ready, held, m_ref, s_ref, jb_ref, gain_ref, shift_ref, e_ref, a_ref, out_ref):
        step = pl.program_id(0)

        @pl.when(step == 0)
        def _():
            ready(0, then=True)
            entry = dot(m_ref[...], held[0][0, :width]) + dot(s_ref[...], held[0][0, width:]) + jb_ref[...]
            e_ref[...] = entry
            normed, _ = normalize(entry)
            a_ref[...] = (normed * gain_ref[...] + shift_ref[...]).astype(low)

        ready(1, step)
        scale = jnp.where(step == 0, HEAD_DIM ** (-0.5), 1.0)
        out_ref[0] = (dot(a_ref[...], held[1][step]).astype(low).astype(full) * scale).astype(low)

    return weighted(
        body,
        [join_weight, weight],
        (3,),
        [
            (middle, whole((rows, width))),
            (skip, whole((rows, width))),
            (join_shift, whole((1, width))),
            (gain, whole((1, width))),
            (shift, whole((1, width))),
        ],
        [
            ((rows, width), full, whole((rows, width))),
            ((rows, width), low, whole((rows, width))),
            ((3, rows, width), low, pl.BlockSpec((1, rows, width), lambda j: (j, 0, 0))),
        ],
        "join_qkv",
        11,
        first=((0, 0), (1, 0)),
    )


def head_masks(seq_rows):
    lane = lax.broadcasted_iota(jnp.int32, (seq_rows, PAIR), 1)
    return [lane < HEAD_DIM, lane >= HEAD_DIM]


def pairs_of(width):
    pairs = width // PAIR
    return pairs, max(group for group in (1, 2, 3) if pairs % group == 0)


def attend(packed, lengths, items, seq_rows):
    width = packed.shape[-1]
    pairs, group = pairs_of(width)

    def body(length_ref, q_ref, k_ref, v_ref, out_ref, total_ref):
        counts = lax.broadcasted_iota(jnp.int32, (seq_rows, seq_rows), 1) < length_ref[pl.program_id(0)]
        for pair in range(group):
            columns = slice(pair * PAIR, (pair + 1) * PAIR)
            queries, keys, values = q_ref[0, 0, :, columns], k_ref[0, 0, :, columns], v_ref[0, 0, :, columns]
            mixed = jnp.zeros((seq_rows, PAIR), full)
            for head, lanes in enumerate(head_masks(seq_rows)):
                scores = dot(jnp.where(lanes, queries, 0), keys, (1, 1))
                scores = jnp.where(counts, scores, masked_score)
                largest = jnp.max(scores, axis=1, keepdims=True)
                weights = jnp.exp(scores - largest)
                total = jnp.sum(weights, axis=1, keepdims=True)
                mixed += dot(weights.astype(low), jnp.where(lanes, values, 0)) * (1.0 / total)
                total_ref[0, pair, head : head + 1] = (largest + jnp.log(total)).T
            out_ref[0, :, columns] = mixed.astype(low)

    def block(which):
        return pl.BlockSpec((1, 1, seq_rows, group * PAIR), lambda n, h: (which, n, 0, h))

    return call(
        body,
        (items, pairs // group),
        [(lengths, SCALARS), (packed, block(0)), (packed, block(1)), (packed, block(2))],
        [
            (
                (items, seq_rows, width),
                low,
                pl.BlockSpec((1, seq_rows, group * PAIR), lambda n, h: (n, 0, h)),
            ),
            (
                (items, pairs, 8, seq_rows),
                full,
                pl.BlockSpec((1, group, 8, seq_rows), lambda n, h: (n, h, 0, 0)),
            ),
        ],
        "attend",
        10,
        spare=14,
    )


def attend_back(packed, grad_mixed, totals, lengths, items, seq_rows):
    width = packed.shape[-1]
    pairs, group = pairs_of(width)
    sides = [slice(0, PATCHES), slice(PATCHES, seq_rows)]

    def body(length_ref, q_ref, k_ref, v_ref, g_ref, total_ref, out_ref):
        row = PATCHES + lax.broadcasted_iota(jnp.int32, (seq_rows - PATCHES, seq_rows), 0)
        counts = row < length_ref[pl.program_id(0)]
        for pair in range(group):
            columns = slice(pair * PAIR, (pair + 1) * PAIR)
            queries, keys, values = q_ref[0, 0, :, columns], k_ref[0, 0, :, columns], v_ref[0, 0, :, columns]
            upstream = g_ref[0, :, columns]
            grad_queries = jnp.zeros((PAIR, seq_rows), full)
            grad_keys, grad_values = [0.0, 0.0], [0.0, 0.0]
            for head, lanes in enumerate(head_masks(seq_rows)):
                own_queries = jnp.where(lanes, queries, 0)
                own_upstream = jnp.where(lanes, upstream, 0)
                own_keys = jnp.where(lanes, keys, 0)
                parts, centre = [], 0.0
                for side, rows in enumerate(sides):
                    scores = dot(keys[rows], own_queries, (1, 1))
                    if side:
                        scores = jnp.where(counts, scores, masked_score)
                    probs = jnp.exp(scores - total_ref[0, pair, head : head + 1])
                    grad_probs = dot(values[rows], own_upstream, (1, 1))
                    centre += jnp.sum(grad_probs * probs, axis=0, keepdims=True)
                    parts.append((probs, grad_probs))
                for side, (probs, grad_probs) in enumerate(parts):
                    grad_scores = (probs * (grad_probs - centre)).astype(low)
                    grad_values[side] += dot(probs.astype(low), own_upstream)
                    grad_keys[side] += dot(grad_scores, own_queries)
                    grad_queries += dot(own_keys[sides[side]], grad_scores, (0, 0))
            out_ref[0, 0, :, columns] = (grad_queries.T * HEAD_DIM ** (-0.5)).astype(low)
            for side, rows in enumerate(sides):
                out_ref[1, 0, rows, columns] = grad_keys[side].astype(low)
                out_ref[2, 0, rows, columns] = grad_values[side].astype(low)

    def block(which):
        return pl.BlockSpec((1, 1, seq_rows, group * PAIR), lambda n, h: (which, n, 0, h))

    return call(
        body,
        (items, pairs // group),
        [
            (lengths, SCALARS),
            (packed, block(0)),
            (packed, block(1)),
            (packed, block(2)),
            (grad_mixed, pl.BlockSpec((1, seq_rows, group * PAIR), lambda n, h: (n, 0, h))),
            (totals, pl.BlockSpec((1, group, 8, seq_rows), lambda n, h: (n, h, 0, 0))),
        ],
        [
            (
                (3, items, seq_rows, width),
                low,
                pl.BlockSpec((3, 1, seq_rows, group * PAIR), lambda n, h: (0, n, 0, h)),
            ),
        ],
        "attend_back",
        15,
        spare=14,
    )[0]


def gelu_parts(before):
    decay = jnp.exp(before * before * -0.5)
    inverse = pl.reciprocal(1.0 + (0.3275911 * 0.5**0.5) * jnp.abs(before), approx=False)
    series = 1.061405429 * 0.5
    for term in (-1.453152027, 1.421413741, -0.284496736, 0.254829592):
        series = series * inverse + term * 0.5
    below = series * inverse * decay
    share = jnp.where(before >= 0, 1.0 - below, below)
    return before * share, share + before * decay * 0.3989422804014327


def feed_forward(inputs, mixed, out_weight, out_bias, gain, shift, up_weight, up_bias, down_weight, down_bias, lengths=None):
    rows, width = inputs.shape
    steps = up_weight.blocks
    hidden = steps * width

    def body(ready, held, x_ref, o_ref, ob_ref, gain_ref, shift_ref, ub_ref, db_ref, *rest):
        m_ref, a_ref, g_ref, s_ref, y_ref, total = rest[-6:]
        step = pl.program_id(0)

        @pl.when(step == 0)
        def _():
            ready(0, then=True)
            middle = x_ref[...].astype(full) + dot(o_ref[...], held[0][0]) + ob_ref[...]
            m_ref[...] = middle
            normed, _ = normalize(middle)
            a_ref[...] = (normed * gain_ref[...] + shift_ref[...]).astype(low)
            total[...] = middle + db_ref[...]

        ready(1, step)
        before = dot(a_ref[...], held[1][step]) + ub_ref[...]
        value, slope = gelu_parts(before)
        g_ref[...] = value.astype(low)
        s_ref[...] = slope.astype(low)

        @pl.when(step == 0)
        def _():
            ready(2)

        total[...] += dot(g_ref[...], held[2][0, pl.ds(pl.multiple_of(step * width, width), width)])

        @pl.when(step == steps - 1)
        def _():
            if lengths is None:
                y_ref[...] = total[...].astype(low)
            else:
                length = rows // lengths.shape[0]
                row = lax.broadcasted_iota(jnp.int32, (length, width), 0)
                for item in range(lengths.shape[0]):
                    at = slice(item * length, (item + 1) * length)
                    y_ref[at] = jnp.where(row < rest[0][item], total[at], 0.0).astype(low)

    return weighted(
        body,
        [out_weight, up_weight, down_weight],
        (steps,),
        [
            (inputs, whole((rows, width))),
            (mixed, whole((rows, width))),
            (out_bias, whole((1, width))),
            (gain, whole((1, width))),
            (shift, whole((1, width))),
            (up_bias, pl.BlockSpec((1, width), lambda j: (0, j))),
            (down_bias, whole((1, width))),
        ]
        + ([] if lengths is None else [(lengths, SCALARS)]),
        [
            ((rows, width), full, whole((rows, width))),
            ((rows, width), low, whole((rows, width))),
            ((rows, hidden), low, pl.BlockSpec((rows, width), lambda j: (0, j))),
            ((rows, hidden), low, pl.BlockSpec((rows, width), lambda j: (0, j))),
            ((rows, width), low, whole((rows, width))),
        ],
        "feed_forward",
        23,
        scratch=[pltpu.VMEM((rows, width), full)],
        first=((0, 0), (1, 0)),
    )


def feed_forward_back(upstream, rounded, slope, down_weight, up_weight, middle, gain, out_weight):
    rows, width = upstream.shape
    steps = up_weight.blocks
    hidden = steps * width

    def body(ready, held, y_ref, dz_ref, s_ref, m_ref, gain_ref, du_ref, dm_ref, db_ref, do_ref, sums_ref, total):
        step = pl.program_id(0)

        @pl.when(step == 0)
        def _():
            sums_ref[0:1] = column_sum(dz_ref[...])
            total[...] = jnp.zeros_like(total)
            ready(0, then=True)

        down = held[0][0, pl.ds(pl.multiple_of(step * width, width), width)]
        grad = (dot(dz_ref[...], down, (1, 1)) * s_ref[...].astype(full)).astype(low)
        du_ref[...] = grad
        sums_ref[pl.ds(4 + step, 1)] = column_sum(grad)
        ready(1, step)
        total[...] += dot(grad, held[1][step], (1, 1))

        @pl.when(step == steps - 1)
        def _():
            grad_second = total[...]
            normed, factor = normalize(m_ref[...])
            sums_ref[1:2] = column_sum(grad_second * normed)
            sums_ref[2:3] = column_sum(grad_second)
            grad_middle = y_ref[...].astype(full) + normalize_back(grad_second * gain_ref[...], normed, factor)
            dm_ref[...] = grad_middle
            branch = grad_middle.astype(low)
            db_ref[...] = branch
            sums_ref[3:4] = column_sum(branch)
            ready(2)
            do_ref[...] = dot(branch, held[2][0], (1, 1)).astype(low)

    return weighted(
        body,
        [down_weight, up_weight, out_weight],
        (steps,),
        [
            (upstream, whole((rows, width))),
            (rounded, whole((rows, width))),
            (slope, pl.BlockSpec((rows, width), lambda j: (0, j))),
            (middle, whole((rows, width))),
            (gain, whole((1, width))),
        ],
        [
            ((rows, hidden), low, pl.BlockSpec((rows, width), lambda j: (0, j))),
            ((rows, width), full, whole((rows, width))),
            ((rows, width), low, whole((rows, width))),
            ((rows, width), low, whole((rows, width))),
            ((4 + steps, width), full, whole((4 + steps, width))),
        ],
        "feed_forward_back",
        21,
        scratch=[pltpu.VMEM((rows, width), full)],
        first=((0, 0), (1, 0)),
    )


def project_back(grad_packed, weight, inputs, gain, grad_middle, join_weight=None):
    rows, width = inputs.shape
    joined = join_weight is not None

    def body(ready, held, g_ref, x_ref, gain_ref, dm_ref, *rest):
        if joined:
            de_ref, dx_ref, dz_ref, skip_ref, sums_ref, total = rest
        else:
            dx_ref, sums_ref, total = rest
        step = pl.program_id(0)

        @pl.when(step == 0)
        def _():
            total[...] = jnp.zeros_like(total)
            ready(0, 0, then=True)

        @pl.when(step > 0)
        def _():
            ready(0, step)

        total[...] += dot(g_ref[0], held[0][step], (1, 1))

        @pl.when(step == 2)
        def _():
            grad_first = total[...]
            normed, factor = normalize(x_ref[...].astype(full))
            sums_ref[0:1] = column_sum(grad_first * normed)
            sums_ref[1:2] = column_sum(grad_first)
            grad = dm_ref[...] + normalize_back(grad_first * gain_ref[...], normed, factor)
            if joined:
                entry = grad.astype(low)
                de_ref[...] = entry
                sums_ref[2:3] = column_sum(entry)
                ready(1)
                grad = dot(entry, held[1][0, :width], (1, 1))
                dx_ref[...] = grad
                dz_ref[...] = grad.astype(low)
                skip_ref[...] = dot(entry, held[1][0, width:], (1, 1))
            else:
                dx_ref[...] = grad

    ins = [
        (grad_packed, pl.BlockSpec((1, rows, width), lambda j: (j, 0, 0))),
        (inputs, whole((rows, width))),
        (gain, whole((1, width))),
        (grad_middle, whole((rows, width))),
    ]
    outs = [((rows, width), full, whole((rows, width))), ((8, width), full, whole((8, width)))]
    if joined:
        rounded = ((rows, width), low, whole((rows, width)))
        outs = [rounded, outs[0], rounded, outs[0], outs[1]]
    return weighted(
        body,
        [weight] + ([join_weight] if joined else []),
        (3,),
        ins,
        outs,
        "project_back",
        13 if joined else 9,
        scratch=[pltpu.VMEM((rows, width), full)],
    )


def picked(body, which, grid, ins, outs, name, micros, aliases=None, spare=4):
    return pl.pallas_call(
        body,
        grid_spec=pltpu.PrefetchScalarGridSpec(
            num_scalar_prefetch=1,
            grid=grid,
            in_specs=[spec for _, spec in ins],
            out_specs=[spec for _, _, spec in outs],
        ),
        out_shape=[jax.ShapeDtypeStruct(shape, kind) for shape, kind, _ in outs],
        name=name,
        input_output_aliases={place + 1: out for place, out in (aliases or {}).items()},
        cost_estimate=cost(micros),
        compiler_params=pltpu.CompilerParams(vmem_limit_bytes=room(ins, outs, (), spare)),
    )(which, *[array for array, _ in ins])


def far(array):
    return pltpu.with_memory_space_constraint(array, pltpu.HBM)


def quarters(rows, width, narrow_rows):
    shape = (lax.axis_size("narrow") // 2 * narrow_rows, width)
    return [(shape, low, pl.BlockSpec(shape, lambda g, core: (0, 0)))] * 4


def up_term(left, right, core):
    rows, width = left.shape
    part = width // lax.axis_size("narrow")
    half = width // 2

    def body(core_ref, l_ref, r_ref, *outs):
        value = dot(l_ref[...], r_ref[...], (0, 0)).astype(low)
        for block in range(2):

            @pl.when(pl.program_id(0) == block)
            def _():
                outs[block][...] = value[:half]
                outs[2 + block][...] = value[half:]

    return picked(
        body,
        core,
        (2,),
        [
            (left, pl.BlockSpec((rows, width), lambda g, core: (0, 0))),
            (far(right), pl.BlockSpec((rows, width), lambda g, core: (0, core[0] * 2 + g))),
        ],
        quarters(rows, width, part),
        "up_term",
        3.5,
    )


def qkv_out_term(first, packed, mixed, branch, core):
    rows, width = first.shape
    part = width // lax.axis_size("narrow")
    half = width // 2

    def body(core_ref, l_ref, r_ref, o_ref, b_ref, *outs):
        step = pl.program_id(0)
        last = core_ref[0] * 2 + step == 3

        def put(block, value):
            outs[block][...] = value[:half]
            outs[2 + block][...] = value[half:]

        @pl.when(last)
        def _():
            put(1, dot(o_ref[...], b_ref[...], (0, 0)).astype(low))

        @pl.when(jnp.logical_not(last))
        def _():
            value = dot(l_ref[...], r_ref[0], (0, 0)).astype(low)
            for block in range(2):

                @pl.when(step == block)
                def _():
                    put(block, value)

    flat = pl.BlockSpec((rows, width), lambda g, core: (0, 0))
    return picked(
        body,
        core,
        (2,),
        [
            (first, flat),
            (packed, pl.BlockSpec((1, rows, width), lambda g, core: (jnp.minimum(core[0] * 2 + g, 2), 0, 0))),
            (mixed, flat),
            (branch, flat),
        ],
        quarters(rows, width, part),
        "qkv_out_term",
        3.5,
    )


def down_term(left, right, core):
    rows, width = right.shape
    shares = lax.axis_size("narrow")
    part = left.shape[1] // (2 * shares)
    direct = part == width
    if not direct:
        left = left.reshape(rows, shares, 2, 2, part // 2)
        left = lax.dynamic_index_in_dim(left, core[0], 2, keepdims=False)
        left = left.reshape(rows, 2, shares // 2, 2, part // 2).swapaxes(2, 3).reshape(rows, 2 * width)
    half = width // 2

    def body(core_ref, l_ref, r_ref, *outs):
        value = dot(l_ref[...], r_ref[...], (0, 0)).astype(low)
        for owner in range(2):

            @pl.when(pl.program_id(0) == owner)
            def _():
                outs[2 * owner][...] = value[:half]
                outs[2 * owner + 1][...] = value[half:]

    return picked(
        body,
        core,
        (2,),
        [
            (left, pl.BlockSpec((rows, width), lambda g, core: (0, g * 2 + core[0] if direct else g))),
            (right, pl.BlockSpec((rows, width), lambda g, core: (0, 0))),
        ],
        quarters(rows, width, part // 2),
        "down_term",
        3.5,
    )


def join_term(middle, skip, right, core):
    rows, width = right.shape
    shares = lax.axis_size("narrow")
    part = width // shares
    half = width // 2
    if part != half:
        left = jnp.concatenate([middle, skip], axis=1).reshape(rows, shares, 2, 2, part // 2)
        left = lax.dynamic_index_in_dim(left, core[0], 2, keepdims=False)
        left = left.reshape(rows, 2, shares // 2, 2, part // 2).swapaxes(2, 3).reshape(rows, width)
        middle, skip = left[:, :half], left[:, half:]

    def body(core_ref, m_ref, s_ref, r_ref, *outs):
        for owner, left_ref in enumerate((m_ref, s_ref)):
            value = dot(left_ref[...], r_ref[...], (0, 0)).astype(low)
            outs[2 * owner][...] = value[: half // 2]
            outs[2 * owner + 1][...] = value[half // 2 :]

    side = pl.BlockSpec((rows, half), lambda g, core: (0, core[0] if part == half else 0))
    return picked(
        body,
        core,
        (1,),
        [(middle, side), (skip, side), (right, pl.BlockSpec((rows, width), lambda g, core: (0, 0)))],
        quarters(rows, width, part // 2),
        "join_term",
        2,
    )


def cross(bit, *pieces):
    kept, got = pieces[: len(pieces) // 2], pieces[len(pieces) // 2 :]
    rows, columns = kept[0].shape
    blocks = len(kept) // 2
    steps = 2 if rows % 32 == 0 else 1

    def body(bit_ref, *refs):
        sent_ref, left_ref = refs[-2:]

        def put(target, owner):
            for block in range(blocks):
                place = owner * blocks + block
                one, two = refs[place], refs[2 * blocks + place]
                target[block] = (one[...].astype(full) + two[...].astype(full)).astype(low)

        for mine in range(2):

            @pl.when(bit_ref[0] == mine)
            def _():
                put(sent_ref, 1 - mine)
                put(left_ref, mine)

    ins = [(piece, pl.BlockSpec((rows // steps, columns), lambda g, bit: (g, 0))) for piece in kept + got]
    out = ((blocks, rows, columns), low, pl.BlockSpec((blocks, rows // steps, columns), lambda g, bit: (0, g, 0)))
    return picked(body, bit, (steps,), ins, [out, out], "cross", 2)


def add_halve(bit, *pairs):
    lead, columns = pairs[0].shape[0], pairs[0].shape[-1]
    sizes = [pair.shape[2] for pair in pairs[::2]]
    total = sum(sizes)
    steps = 2 if len(sizes) == 1 and total % 32 == 0 and total >= 256 else 1

    def body(bit_ref, *refs):
        mine = bit_ref[0]
        for target, place in ((refs[-2], 1 - mine), (refs[-1], mine)):
            begin = 0
            for kept_ref, got_ref in zip(refs[:-2:2], refs[1:-2:2]):
                length = kept_ref.shape[2]
                for each in range(lead):
                    value = kept_ref[each, place].astype(full) + got_ref[each, place].astype(full)
                    target[each, begin : begin + length] = value.astype(low)
                begin += length

    ins = [
        (pair, pl.BlockSpec((lead, 2, pair.shape[2] // steps, columns), lambda g, bit: (0, 0, g, 0)))
        for pair in pairs
    ]
    out = (
        (lead, total, columns),
        low,
        pl.BlockSpec((lead, total // steps, columns), lambda g, bit: (0, g, 0)),
    )
    return picked(body, bit, (steps,), ins, [out, out], "add_halve", 2)


def add_into(target, place, count, one, two):
    rows, columns = one.shape[-2:]
    steps = 2 if rows % 32 == 0 else 1
    block = pl.BlockSpec((1, rows // steps, columns), lambda g: (0, g, 0))

    def body(one_ref, two_ref, *rest):
        rest[-1][...] = (one_ref[...].astype(full) + two_ref[...].astype(full)).astype(low)

    ins = [one.reshape(1, rows, columns), two.reshape(1, rows, columns)]
    return pl.pallas_call(
        body,
        grid=(steps,),
        in_specs=[block, block] + ([] if target is None else [ANY]),
        out_specs=pl.BlockSpec((1, rows // steps, columns), lambda g: (place, g, 0)),
        out_shape=jax.ShapeDtypeStruct((count, rows, columns), low),
        name="add_into",
        input_output_aliases={} if target is None else {2: 0},
        cost_estimate=cost(1.3),
    )(*ins, *([] if target is None else [target]))


def add(one, two):
    return (one.astype(full) + two.astype(full)).astype(low)


def pair_up(own, got, bit):
    rows, columns = own.shape

    def body(bit_ref, own_ref, got_ref, out_ref):
        mine = bit_ref[0]
        out_ref[mine] = own_ref[...]
        out_ref[1 - mine] = got_ref[...]

    flat = pl.BlockSpec((rows, columns), lambda g, bit: (0, 0))
    out = ((2, rows, columns), low, pl.BlockSpec((2, rows, columns), lambda g, bit: (0, 0, 0)))
    return picked(body, bit, (1,), [(own, flat), (got, flat)], [out], "pair_up", 1)[0]


def finish(kind, half, own, got, begin, length, core, layer, targets):
    pieces, _, columns = own.shape
    scale = 1.0 / lax.axis_size("wide")
    aliases = {place + 2: place for place in range(len(targets))}
    source = pl.BlockSpec((pieces, length, columns), lambda g, core: (0, begin // length, 0))
    ins = [(own, source), (got, source)] + [(target, ANY) for target in targets]
    rows = pieces * length

    def chosen(core_ref, which, own_ref, got_ref, place=None):
        sides = [own_ref, got_ref]
        if place is None:
            values = [side[...].reshape(pieces * length, columns) for side in sides]
        else:
            if pieces == 1:
                near = (0, pl.ds(place * (length // 2), length // 2))
            else:
                near = (pl.ds(place * (pieces // 2), pieces // 2),)
            values = [side[near].reshape(pieces * length // 2, columns) for side in sides]
        return jnp.where(core_ref[0] == which, values[0], values[1]).astype(full) * scale

    if kind in ("down", "join"):

        def body(core_ref, own_ref, got_ref, *rest):
            rest[-1][0] = chosen(core_ref, pl.program_id(0), own_ref, got_ref)

        place = layer if kind == "down" else 0
        shape = (2 if kind == "down" else 1, 2 * rows, columns)
        out = (shape, full, pl.BlockSpec((1, rows, columns), lambda g, core: (place, g, 0)))
        return picked(body, core, (2,), ins, [out], "finish_rows", 0, aliases)
    steps = 4 if half is None else 2
    rows = rows // 2 if half is None else rows

    def block(step):
        return step if half is None else 2 * step + half

    def values_of(core_ref, own_ref, got_ref):
        step = pl.program_id(0)
        if half is None:
            return chosen(core_ref, step // 2, own_ref, got_ref, step % 2)
        return chosen(core_ref, step, own_ref, got_ref)

    def body(core_ref, own_ref, got_ref, *rest):
        values = values_of(core_ref, own_ref, got_ref)
        if kind == "up":
            rest[-1][0] = values
            return
        if half == 0:
            rest[-1][0] = values
            return
        last = block(pl.program_id(0)) == 3

        @pl.when(jnp.logical_not(last))
        def _():
            rest[-2][0] = values

        @pl.when(last)
        def _():
            rest[-1][0] = values

    if kind == "up":
        outs = [((2, rows, 4 * columns), full, pl.BlockSpec((1, rows, columns), lambda g, core: (layer, 0, block(g))))]
        return picked(body, core, (steps,), ins, outs, "finish_columns", 0, aliases)

    def spot(step):
        return block(step if half == 0 else jnp.minimum(step, steps - 2))

    outs = [
        ((2, rows, 3 * columns), full, pl.BlockSpec((1, rows, columns), lambda g, core: (layer, 0, spot(g)))),
        ((2, rows, columns), full, pl.BlockSpec((1, rows, columns), lambda g, core: (layer, 0, 0))),
    ]
    if half == 0:
        kept = targets[1:]
        ins, outs, aliases = ins[:3] if targets else ins, outs[:1], {2: 0} if targets else {}
        return (picked(body, core, (steps,), ins, outs, "finish_qkv", 0, aliases)[0], *kept)
    return picked(body, core, (steps,), ins, outs, "finish_qkv_out", 0, aliases)


def small_gradients(total, me, width, shares, blocks):
    part = width // shares
    scale = 1.0 / lax.axis_size("wide")

    def body(me_ref, total_ref, gains_ref, shifts_ref, out_ref, up_ref, down_ref, join_ref):
        values = total_ref[...] * scale
        back = [values[0:8], values[8:16]]
        ahead = [values[16 : 20 + blocks], values[20 + blocks : 24 + 2 * blocks]]
        for place in range(shares):

            @pl.when(me_ref[0] == place)
            def _():
                columns = slice(place * part, place * part + part)
                for layer in range(2):
                    for row, target in ((0, gains_ref), (1, shifts_ref)):
                        target[layer, 0:1] = back[layer][row : row + 1, columns]
                        target[layer, 1:2] = ahead[layer][row + 1 : row + 2, columns]
                    out_ref[layer : layer + 1] = ahead[layer][3:4, columns]
                    down_ref[layer : layer + 1] = ahead[layer][0:1, columns]
                    begin = place * part * blocks
                    while begin < (place + 1) * part * blocks:
                        row, column = begin // width, begin % width
                        length = min(width - column, (place + 1) * part * blocks - begin)
                        at = begin - place * part * blocks
                        piece = ahead[layer][4 + row : 5 + row, column : column + length]
                        up_ref[layer : layer + 1, at : at + length] = piece
                        begin += length
                join_ref[...] = back[1][2:3, columns]

    shapes = [(2, 2, part), (2, 2, part), (2, part), (2, part * blocks), (2, part), (1, part)]
    outs = [(shape, full, pl.BlockSpec(shape, lambda g, me, n=len(shape): (0,) * n)) for shape in shapes]
    ins = [(total, pl.BlockSpec(total.shape, lambda g, me: (0, 0)))]
    return picked(body, me, (1,), ins, outs, "small_gradients", 1)


def after(value, *earlier):
    return lax.optimization_barrier((value,) + earlier)[0] if earlier else value


def swap(values, axis, mask):
    size = lax.axis_size(axis)
    return lax.ppermute(values, axis, [(source, source ^ mask) for source in range(size)])


def masks(axis):
    return [1 << bit for bit in range(lax.axis_size(axis).bit_length() - 1)]


class Order:
    def __init__(self):
        self.last = ()

    def run(self, function, *arrays):
        held = lax.optimization_barrier(tuple(arrays) + self.last)[: len(arrays)]
        out = function(*held)
        self.last = (jax.tree.leaves(out)[0],)
        return out

    def mark(self, value):
        return self.run(lambda x: x + 1, value)

    def hold(self, *arrays):
        self.last += arrays


def place_bit(axis, mask):
    return ((lax.axis_index(axis) & mask) // mask).astype(jnp.int32).reshape(1)


class Term:
    def __init__(self, order, kind, layer, function, *arrays):
        self.order, self.kind, self.layer, self.half = order, kind, layer, None
        self.core = place_bit("wide", 1)
        sent = order.run(lambda *x: function(*x, 1 - self.core), *arrays)
        self.got = [swap(each, "wide", 1) for each in sent]
        self.columns = sent[0].shape[-1]
        self.keep = lambda: order.run(lambda *x: function(*x, self.core), *arrays)

    def stay(self):
        self.kept, self.keep = self.keep(), None

    def part(self, half):
        other = copy.copy(self)
        other.kept, other.got, other.half = self.kept[half::2], self.got[half::2], half
        return other

    def pass_narrow(self):
        stages = list(reversed(masks("narrow")))
        if isinstance(self.kept, (list, tuple)):
            bit = place_bit("narrow", stages[0])
            blocks = len(self.kept) // 2
            sent, self.kept = self.order.run(lambda *x: cross(bit, *x), *self.kept, *self.got)
            self.got = swap(sent, "narrow", stages.pop(0))
        else:
            blocks = 1
        for mask in stages:
            pairs = [(self.kept, self.got)]
            self.kept, self.got = halve(self.order, "narrow", mask, blocks, pairs, self.columns)

    def pass_first(self, mask):
        swapped = [self.kept[owner * 2 + block] for block in range(2) for owner in range(2)]
        brought = [self.got[owner * 2 + block] for block in range(2) for owner in range(2)]
        bit = place_bit("wide", mask)
        sent, self.kept = self.order.run(lambda *x: cross(bit, *x), *swapped, *brought)
        self.got = swap(sent, "wide", mask)

    def pass_wide(self, mask):
        pairs = list(zip(self.kept, self.got)) if isinstance(self.kept, (list, tuple)) else [(self.kept, self.got)]
        self.kept, self.got = halve(self.order, "wide", mask, 1, pairs, self.columns)

    def add_into(self, target, place, count):
        kept, got = [side.reshape(-1, self.columns) for side in (self.kept, self.got)]
        if target is None:
            return self.order.run(lambda one, two: add_into(None, place, count, one, two), kept, got)
        return self.order.run(lambda target, one, two: add_into(target, place, count, one, two), target, kept, got)

    def finish(self, done, own, got, begin, length):
        targets = done.get(self.kind, ())

        def last(own, got, core, *targets):
            return finish(self.kind, self.half, own, got, begin, length, core, self.layer, targets)

        done[self.kind] = self.order.run(last, own, got, self.core, *targets)


def halve(order, axis, mask, lead, pairs, columns):
    shaped = [array.reshape(lead, 2, -1, columns) for pair in pairs for array in pair]
    bit = place_bit(axis, mask)
    sent, kept = order.run(lambda *x: add_halve(bit, *x), *shaped)
    return kept, swap(sent, axis, mask)


class Reduce:
    def __init__(self, order, terms, passed=(), late=()):
        self.order, self.terms = order, terms
        rest = [mask for mask in masks("wide")[1:] if mask not in passed]
        self.down = [mask for mask in rest if mask not in late] + [mask for mask in rest if mask in late]
        self.up = list(reversed(passed))
        self.pieces, self.columns = 2 ** len(passed), terms[0].columns
        self.parts = [(term.kept, term.got) for term in terms]
        self.lengths, self.first = [each.size // self.columns for each, _ in self.parts], True
        self.joining, self.closed = None, False

    def step(self):
        if self.closed:
            return
        if self.down:
            mask = self.down.pop(0)
            rows = [kept.size // self.columns for kept, _ in self.parts]
            even = all(each % 32 == 0 for each in rows) and bool(self.down)
            if self.first and even:
                self.pieces, self.lengths = 2 * self.pieces, [each // 2 for each in rows]
            self.first = False
            if even:
                self.up.insert(0, mask)
                self.parts = [halve(self.order, "wide", mask, 1, self.parts, self.columns)]
            else:
                flat = [[side.reshape(-1, self.columns) for side in pair] for pair in self.parts]
                pair = [jnp.concatenate(sides) for sides in zip(*flat)]
                total = self.order.run(add, *pair)
                self.parts = [(total, swap(total, "wide", mask))]
            return
        kept, got = [array.reshape(-1, self.columns) for array in self.parts[0]]
        if self.joining is None:
            total = self.order.run(add, kept, got)
        else:
            bit = place_bit("wide", self.joining)
            total = self.order.run(lambda *x: pair_up(*x, bit), kept, got).reshape(-1, self.columns)
        if self.up:
            self.joining = self.up.pop(0)
            self.parts = [(total, swap(total, "wide", self.joining))]
        else:
            self.parts = [(total, swap(total, "wide", 1))]
            self.closed = True

    def finish(self, done):
        own, got = [array.reshape(self.pieces, -1, self.columns) for array in self.parts[0]]
        begin = 0
        for term, length in zip(self.terms, self.lengths):
            term.finish(done, own, got, begin, length)
            begin += length


def on_device(
    tokens,
    skip,
    flags,
    cotangent,
    norm_gains,
    norm_biases,
    qkv_weight,
    out_weight,
    out_bias,
    up_weight,
    up_bias,
    down_weight,
    down_bias,
    skip_weight,
    skip_bias,
):
    items, seq_rows, width = tokens.shape
    rows = items * seq_rows
    me = lax.axis_index("narrow")
    shares = lax.axis_size("narrow")
    spots = jnp.stack([me, lax.axis_index("wide")]).astype(jnp.int32)
    order = Order()

    def fetches(layer):
        return (
            Fetch([(qkv_weight, layer)], (1, 2)),
            Fetch([(out_weight, layer), (up_weight, layer)], (1, 2)),
            Fetch([(down_weight, layer)], (1, 4)),
        )

    fetch_qkv0, fetch_up0, fetch_down0 = fetches(0)
    fetch_qkv1, fetch_up1, fetch_down1 = fetches(1)
    fetch_join = Fetch([(skip_weight, None)], (1, 4))
    qkv0, qkv1 = [Weight(each, 0, width, spots) for each in (fetch_qkv0, fetch_qkv1)]
    out0, out1 = [Weight(each, 0, width, spots) for each in (fetch_up0, fetch_up1)]
    up0, up1 = [Weight(each, 1, width, spots) for each in (fetch_up0, fetch_up1)]
    down0, down1 = [Weight(each, 0, width, spots) for each in (fetch_down0, fetch_down1)]
    join = Weight(fetch_join, 0, width, spots)

    small = (norm_gains, norm_biases, out_bias, down_bias, skip_bias, up_bias)
    fetch_qkv0.cut()
    fetch_qkv0.fetch()
    held = order.run(pack_small, *[after(piece, fetch_qkv0.sent) for piece in small])[None]
    for mask in masks("narrow"):
        held = jnp.concatenate([held, swap(held, "narrow", mask)])
    last = order.last
    for each in (fetch_up0, fetch_down0, fetch_join, fetch_qkv1, fetch_up1, fetch_down1):
        each.cut(*last)
        last = (each.sent,)
    fetch_up0.fetch()
    fetch_down0.fetch(fetch_up0.sent)
    fetch_join.fetch(fetch_down0.sent)
    fetch_qkv1.fetch(fetch_join.sent)
    place = me.astype(jnp.int32).reshape(1)
    lines = order.run(lambda x: unpack_small(x, place, small, width), held)

    def line(row):
        return lines[row : row + 1]

    gains, shifts = [[line(2 * layer + each) for each in range(2)] for layer in range(2)], None
    shifts = [[line(4 + 2 * layer + each) for each in range(2)] for layer in range(2)]
    out_biases, down_biases, join_shift = [line(8), line(9)], [line(10), line(11)], line(12)
    blocks = up0.blocks
    up_biases = [lines[13 + layer * blocks : 13 + (layer + 1) * blocks].reshape(1, -1) for layer in range(2)]

    tokens_flat, skip_flat, cotangent_flat = [array.reshape(rows, width) for array in (tokens, skip, cotangent)]
    lengths = PATCHES + 1 + CAPTION * flags
    valid = lax.broadcasted_iota(jnp.int32, (items, seq_rows), 1) < lengths[:, None]
    dz1 = order.run(lambda x: jnp.where(valid.reshape(rows, 1), x, 0), after(cotangent_flat, fetch_down1.sent))

    fetch_qkv0.share(1)
    fetch_qkv0.share(0)
    order.hold(*fetch_up0.got())
    fetch_up0.share(1)
    a0, packed0 = order.run(lambda *x: project_qkv(*x, qkv0), tokens_flat, gains[0][0], shifts[0][0])
    order.hold(*fetch_down0.got())
    fetch_down0.share(1, a0)
    fetch_up1.fetch(a0)
    fetch_down1.fetch(a0)
    packed0 = packed0.reshape(3, items, seq_rows, width)
    mixed0, totals0 = order.run(lambda *x: attend(*x, items, seq_rows), packed0, lengths)
    order.hold(*fetch_join.got(), *fetch_qkv1.got())
    there = order.mark(spots)
    fetch_up0.share(0, there)
    fetch_down0.share(0, there)
    fetch_join.share(1, there)
    fetch_qkv1.share(1, there)
    mixed0 = mixed0.reshape(rows, width)
    m0, second0, hidden0, slope0, middle = order.run(
        lambda x, o, ob, g, s, ub, db: feed_forward(x, o, out0, ob, g, s, up0, ub, down0, db),
        tokens_flat, mixed0, out_biases[0], gains[0][1], shifts[0][1], up_biases[0], down_biases[0],
    )
    fetch_join.share(0, middle)
    fetch_qkv1.share(0, middle)
    order.hold(*fetch_up1.got(), *fetch_down1.got())
    fetch_up1.share(1, middle)
    fetch_down1.share(1, middle)
    entry, a1, packed1 = order.run(
        lambda m, s, jb, g, sh: join_qkv(m, s, join, jb, g, sh, qkv1),
        middle, skip_flat, join_shift, gains[1][0], shifts[1][0],
    )
    packed1 = packed1.reshape(3, items, seq_rows, width)
    mixed1, totals1 = order.run(lambda *x: attend(*x, items, seq_rows), packed1, lengths)
    fetch_up1.share(0, mixed1)
    fetch_down1.share(0, mixed1)
    mixed1 = mixed1.reshape(rows, width)
    m1, second1, hidden1, slope1, output = order.run(
        lambda x, o, ob, g, s, ub, db, k: feed_forward(x, o, out1, ob, g, s, up1, ub, down1, db, k),
        entry, mixed1, out_biases[1], gains[1][1], shifts[1][1], up_biases[1], down_biases[1], lengths,
    )

    done = {}
    term_down1 = Term(order, "down", 1, down_term, hidden1, dz1)
    term_down1.stay()
    term_down1.pass_narrow()
    du, dm, db, do, sums1 = order.run(
        lambda y, z, s, m, g: feed_forward_back(y, z, s, down1, up1, m, g, out1),
        dz1, dz1, slope1, m1, gains[1][1],
    )
    term_up1 = Term(order, "up", 1, up_term, second1, du)
    term_up1.stay()
    term_up1.pass_narrow()
    total = term_down1.add_into(None, 0, 3)
    dpacked = order.run(
        lambda *x: attend_back(*x, items, seq_rows), packed1, do.reshape(items, seq_rows, width), totals1, lengths
    )
    flat_packed = dpacked.reshape(3, rows, width)
    term_qkv1 = Term(order, "qkv", 1, qkv_out_term, a1, flat_packed, mixed1, db)
    term_qkv1.stay()
    term_qkv1.pass_narrow()
    total = term_up1.add_into(total, 1, 3)
    dentry, dmiddle, dz0, skip_grad, sums3 = order.run(
        lambda gp, x, g, dm: project_back(gp, qkv1, x, g, dm, join), flat_packed, entry, gains[1][0], dm
    )
    term_join = Term(order, "join", 1, join_term, middle, skip_flat, dentry)
    term_join.stay()
    term_join.pass_narrow()
    term_down0 = Term(order, "down", 0, down_term, hidden0, dz0)
    term_down0.stay()
    total = term_qkv1.add_into(total, 2, 3)
    size = lax.axis_size("wide")
    groups = [[device + core for device in range(0, size, 2)] for core in range(2)]
    flat_total = total.reshape(-1, width)
    part = lax.psum_scatter(flat_total, "wide", axis_index_groups=groups, scatter_dimension=0, tiled=True)
    term_down0.pass_first(2)

    du, dm, db, do, sums0 = order.run(
        lambda y, z, s, m, g: feed_forward_back(y, z, s, down0, up0, m, g, out0),
        dmiddle, dz0, slope0, m0, gains[0][1],
    )
    term_join.pass_wide(2)
    term_up0 = Term(order, "up", 0, up_term, second0, du)
    term_up0.stay()
    term_down0.pass_narrow()
    term_up0.pass_narrow()
    dpacked = order.run(
        lambda *x: attend_back(*x, items, seq_rows), packed0, do.reshape(items, seq_rows, width), totals0, lengths
    )
    order.hold(term_down0.got, term_join.got)
    flat_packed = dpacked.reshape(3, rows, width)
    term_qkv0 = Term(order, "qkv", 0, qkv_out_term, a0, flat_packed, mixed0, db)
    term_qkv0.stay()
    one, two = term_qkv0.part(0), term_qkv0.part(1)
    one.pass_narrow()
    two.pass_narrow()
    first = Reduce(order, [term_down0, term_join], (2,))
    first.step()
    second = Reduce(order, [term_up0])
    second.step()
    tokens_grad, sums2 = order.run(
        lambda gp, x, g, dm: project_back(gp, qkv0, x, g, dm), flat_packed, tokens_flat, gains[0][0], dm
    )
    minor = jnp.concatenate([sums2, sums3, sums0, sums1])
    places = masks("wide")
    minor_stages = [("narrow", mask) for mask in masks("narrow")]
    minor_stages += [("wide", mask) for mask in places if mask != 2] + [("wide", mask) for mask in places if mask == 2]
    minor_got = swap(minor, *minor_stages[0])

    def minor_step():
        nonlocal minor, minor_got
        if minor_stages:
            minor_stages.pop(0)
            minor = order.run(lambda one, two: one + two, minor, minor_got)
            if minor_stages:
                minor_got = swap(minor, *minor_stages[0])

    third = Reduce(order, [one])
    third.step()
    first.step()
    second.step()
    fourth = Reduce(order, [two])
    fourth.step()
    minor_step()
    third.step()
    first.step()
    second.step()
    order.hold(part)
    gathered = lax.all_gather(after(part, *order.last), "wide", axis_index_groups=groups, tiled=True)
    fourth.step()
    third.step()
    first.step()
    minor_step()
    fourth.step()
    second.step()
    third.step()
    minor_step()
    first.step()
    fourth.step()
    second.step()
    order.hold(gathered)
    other = swap(after(gathered, *order.last), "wide", 1)
    minor_step()
    first.finish(done)
    third.step()
    fourth.step()
    own, got = gathered.reshape(1, -1, width), other.reshape(1, -1, width)
    for which, term in enumerate((term_down1, term_up1, term_qkv1)):
        term.finish(done, own, got, which * (own.shape[1] // 3), own.shape[1] // 3)
    minor_step()
    second.step()
    third.step()
    second.finish(done)
    fourth.step()
    for each in (first, second, third, fourth):
        while not each.closed:
            each.step()
    while minor_stages:
        minor_step()
    third.finish(done)
    fourth.finish(done)
    small = order.run(lambda x: small_gradients(x, place, width, shares, up1.blocks), minor)

    return (
        output.reshape(tokens.shape),
        tokens_grad.reshape(tokens.shape),
        skip_grad.reshape(tokens.shape),
        small[0],
        small[1],
        done["qkv"][0],
        done["qkv"][1],
        small[2],
        done["up"][0],
        small[3],
        done["down"][0],
        small[4],
        done["join"][0][0],
        small[5].reshape(-1),
    )


def solution(mesh):
    placed = (
        P(("wide", "narrow"), None, None),
        P(("wide", "narrow"), None, None),
        P(("wide", "narrow")),
        P(("wide", "narrow"), None, None),
        P(None, None, "narrow"),
        P(None, None, "narrow"),
        P(None, "narrow", None),
        P(None, "narrow", None),
        P(None, "narrow"),
        P(None, "narrow", None),
        P(None, "narrow"),
        P(None, "narrow", None),
        P(None, "narrow"),
        P("narrow", None),
        P("narrow"),
    )
    return jax.shard_map(
        on_device,
        mesh=mesh,
        in_specs=placed,
        out_specs=(
            P(("wide", "narrow"), None, None),
            P(("wide", "narrow"), None, None),
            P(("wide", "narrow"), None, None),
            P(None, None, "narrow"),
            P(None, None, "narrow"),
            P(None, "narrow", None),
            P(None, "narrow", None),
            P(None, "narrow"),
            P(None, "narrow", None),
            P(None, "narrow"),
            P(None, "narrow", None),
            P(None, "narrow"),
            P("narrow", None),
            P("narrow"),
        ),
        check_vma=False,
    )
```
